32 devices in a mesh: section: 2 (over core), batch: 4 (over y, x), rows: 4 (over z).
Axes of the slice: x: 2, y: 2, z: 4, core: 2. Of those that a mesh axis runs over, the one named last changes fastest.
Arguments:
- inputs: float32 [4, 4, 256, 64, 256], P(None, 'batch', 'rows'), may hold values from -6 to 6
- cotangent: float32 [4, 4, 256, 64, 256], P(None, 'batch', 'rows'), may hold values from -6 to 6
- region_id: int32 [4, 4, 256, 256], P(None, 'batch', 'rows'), may hold values from 0 to 8, as said below
- spectral_w: float32 [2, 64, 64, 64, 128], P('section', 'rows'), may hold values from -1 to 1
- conv_w: float32 [2, 64, 64], P('section'), may hold values from -0.75 to 0.75
- bias_vector: float32 [2, 64], P('section'), may hold values from -3 to 3
Outputs:
- boundary: float32 [2, 4, 4, 256, 64, 256], P('section', None, 'batch', 'rows')
- spectral_grad: float32 [2, 64, 64, 64, 128], P('section', 'rows')
- conv_grad: float32 [2, 64, 64], P('section')
- bias_grad: float32 [2, 64], P('section')
- layer_rms: float32 [2, 2, 8], P('section')
The draws below stay inside these ranges and needn't reach their ends.
Inputs may be any that keep to these rules, and one draw needn't show every extreme that they name: `region_id`: 0 marks land, 1 to 8 the subregion of a sea pixel; the first column of every grid is sea and holds every subregion.
All inputs are finite; a program needn't handle non-finite values.
Results may differ from the reference program's by a relative error of at most 0.0003.
Values sent between devices are 32-bit elements; how exact they have to be, the bound alone decides.
A program may use at most 832 MiB of HBM per device.

```python
import jax
import jax.numpy as jnp
from jax import lax

C = 64
KX = 64
KY = 64
H = 256
W = 256
R = 8
MB = 4
GRIDS = 4


def draw_region_id(key, part):
    key = jax.random.fold_in(key, 11)
    shift_key, land_key = jax.random.split(key)
    shifts = jax.random.randint(shift_key, (MB, GRIDS, 1, W), 0, H)
    row_index = jnp.arange(H, dtype=jnp.int32)[None, None, :, None]
    band = 1 + (row_index + shifts) % H * R // H
    land = jax.random.randint(land_key, (MB, GRIDS, H, W), 0, 4) == 0
    column = jnp.arange(W, dtype=jnp.int32)[None, None, None, :]
    land = jnp.logical_and(land, column != 0)
    return jnp.where(land, 0, band).astype(jnp.int32)


def block_levels(own_key, extent, pieces, smallest, high):
    level = 1.0
    for dim, parts in pieces:
        draws = jax.random.uniform(jax.random.fold_in(jax.random.fold_in(own_key, 6), dim), (parts,), jnp.float32, smallest / len(pieces), high / len(pieces))
        level = level * jnp.repeat(jnp.exp(draws), extent[dim] // parts).reshape((-1,) + (1,) * (len(extent) - 1 - dim))
    return level


def scatter_about(key, dims, spread, most, pieces=(), kind=jnp.bfloat16):
    factor_of = block_levels(key, dims, pieces, -0.22, 0.18) if pieces else 1.0
    drawn = jax.random.normal(key, dims, jnp.float32) * spread * factor_of
    return jnp.minimum(jnp.maximum(drawn, -most), most).astype(kind)


def setup_inputs(seed: int = 0) -> dict:
    key_list = jax.random.split(jax.random.key(seed), 7)
    inputs = scatter_about(key_list[0], (MB, GRIDS, H, C, W), 1.0, 6.0, ((1, 4), (2, 4)), jnp.float32)
    cotangent = scatter_about(key_list[1], (MB, GRIDS, H, C, W), 1.0, 6.0, ((1, 4), (2, 4)), jnp.float32)
    region_id = draw_region_id(jax.random.fold_in(key_list[6], 71), 0)
    spectral_w = scatter_about(key_list[3], (2, KX, C, C, 2 * KY), (8 * C * KX * KY // (H * W)) ** -0.5, 1.0, ((0, 2), (1, 4)), jnp.float32)
    conv_w = scatter_about(key_list[4], (2, C, C), C ** -0.5, 0.75, ((0, 2),), jnp.float32)
    bias_vector = scatter_about(key_list[5], (2, C), 0.5, 3.0, ((0, 2),), jnp.float32)
    return {"inputs": inputs, "cotangent": cotangent, "region_id": region_id, "spectral_w": spectral_w, "conv_w": conv_w, "bias_vector": bias_vector}


precise = lax.Precision.HIGHEST

def mode_product(left, right):
    return jnp.einsum('xik,xiok->xok', left, right, precision=precise)

def fourier_layer(field_in, spectral_layer, conv_layer, bias_layer):
    spectrum = jnp.fft.rfft2(field_in, axes=(0, 2), norm='ortho')
    retained = jnp.concatenate([spectrum[:KX // 2], spectrum[H - KX // 2:]], 0)[:, :, :KY]
    real_part = jnp.real(retained)
    imag_part = jnp.imag(retained)
    weight_real = spectral_layer[..., :KY]
    weight_imag = spectral_layer[..., KY:]
    mixed_real = mode_product(real_part, weight_real) - mode_product(imag_part, weight_imag)
    mixed_imag = mode_product(real_part, weight_imag) + mode_product(imag_part, weight_real)
    mixed = lax.complex(mixed_real, mixed_imag)
    mixed = jnp.pad(mixed, ((0, 0), (0, 0), (0, W // 2 + 1 - KY)))
    zero_rows = jnp.zeros((H - KX, C, W // 2 + 1), mixed.dtype)
    padded = jnp.concatenate([mixed[:KX // 2], zero_rows, mixed[KX // 2:]], 0)
    spectral_part = jnp.fft.irfft2(padded, s=(H, W), axes=(0, 2), norm='ortho')
    pointwise = jnp.einsum('hcw,co->how', field_in, conv_layer, precision=precise)
    pre_act = spectral_part + pointwise + bias_layer[None, :, None]
    branch = jax.nn.gelu(pre_act, approximate=False)
    return (field_in + branch, branch)

def region_sums(output, branch, zone):
    region_ids = jnp.arange(1, R + 1, dtype=jnp.int32)
    member = (zone[:, :, None] == region_ids[None, None, :]).astype(output.dtype)
    energy = jnp.stack([lax.optimization_barrier(jnp.sum(output * output, axis=1)), lax.optimization_barrier(jnp.sum(branch * branch, axis=1))])
    return jnp.einsum('shw,hwj->sj', energy, member, precision=precise)

def reference(inputs, cotangent, region_id, spectral_w, conv_w, bias_vector):

    def forward(field_all, spectral_all, conv_all, bias_all):
        flat_inputs = field_all.reshape((MB * GRIDS, H, C, W))
        flat_zones = region_id.reshape((MB * GRIDS, H, W))

        def one_grid(grid_pair):
            current, zone = grid_pair
            layer_stats = []
            for layer_index in range(2):
                current, branch = fourier_layer(current, spectral_all[layer_index], conv_all[layer_index], bias_all[layer_index])
                layer_stats.append(region_sums(current, branch, zone))
            return (current, jnp.stack(layer_stats))
        outputs, grid_stats = lax.map(jax.checkpoint(one_grid), (flat_inputs, flat_zones))
        return (outputs.reshape(field_all.shape), lax.optimization_barrier(jnp.sum(grid_stats, axis=0)))
    outputs, pullback, totals = jax.vjp(forward, inputs, spectral_w, conv_w, bias_vector, has_aux=True)
    grad_inputs, grad_spectral, grad_conv, grad_bias = pullback(cotangent)
    region_ids = jnp.arange(1, R + 1, dtype=jnp.int32)
    counts = lax.optimization_barrier(jnp.sum((region_id[..., None] == region_ids).astype(inputs.dtype), axis=(0, 1, 2, 3)))
    layer_rms = jnp.sqrt(totals / (C * counts)[None, None, :] + 1e-06)
    boundary = jnp.stack([grad_inputs, outputs])
    return (boundary, grad_spectral, grad_conv, grad_bias, layer_rms)
```

```python
import functools
import math

import jax
import jax.numpy as jnp
import numpy as np
from jax import lax
from jax.experimental import pallas as pl
from jax.experimental.pallas import tpu as pltpu
from jax.sharding import PartitionSpec as P

R = 8
G = 8
F32 = jnp.float32
BF16 = jnp.bfloat16
VMEM_LIMIT = 56 * 1024 * 1024


def split(value):
    high = value.astype(BF16)
    return high, (value - high.astype(F32)).astype(BF16)


def dot(left, right, dims=(((1,), (0,)), ((), ()))):
    return lax.dot_general(left, right, dims, preferred_element_type=F32)


def dot3(left, right):
    return dot(left[0], right[0]) + (dot(left[1], right[0]) + dot(left[0], right[1]))


def np_split(value):
    high = value.astype(np.float32).astype(BF16)
    return high, (value - high.astype(np.float64)).astype(np.float32).astype(BF16)


def col_tables(width, half):
    phase = 2.0 * math.pi / width * (np.outer(np.arange(width), np.arange(half)) % width)
    cosine, sine = np.cos(phase) / math.sqrt(width), np.sin(phase) / math.sqrt(width)
    plain = np.concatenate([cosine, -sine, -sine, -cosine], 1)
    doubled = plain * np.tile(np.where(np.arange(half) == 0, 1.0, 2.0), 4)[None, :]
    return plain, doubled


def row_tables(height, mode_rows, first_row, rows_dev):
    position = jnp.arange(mode_rows, dtype=jnp.int32)
    frequency = jnp.where(position < mode_rows // 2, position, height - mode_rows + position)
    row = first_row + jnp.arange(rows_dev, dtype=jnp.int32)
    phase = 2.0 * math.pi / height * (frequency[:, None] * row[None, :] % height).astype(F32)
    small = jnp.concatenate([jnp.cos(phase), jnp.sin(phase)], 1) / math.sqrt(height)
    high = lax.reduce_precision(small, 8, 7)
    parts = (high.astype(BF16), (small - high).astype(BF16))
    spread_x = np.kron(np.eye(mode_rows), np.ones((G, 1))).astype(np.float32)
    spread_r = np.kron(np.eye(2 * rows_dev), np.ones((1, G))).astype(np.float32)
    rows, cols = mode_rows * G, 2 * rows_dev * G
    same = (np.arange(rows)[:, None] % G) == (np.arange(cols)[None, :] % G)

    def widen(part):
        wide = dot(dot(spread_x.astype(BF16), part).astype(BF16), spread_r.astype(BF16))
        return jnp.where(same, wide, 0.0).astype(BF16)

    def widen_t(part):
        wide = dot(dot(spread_r.T.astype(BF16), part.T).astype(BF16), spread_x.T.astype(BF16))
        return jnp.where(same.T, wide, 0.0).astype(BF16)

    return [widen(p) for p in parts], [widen_t(p) for p in parts]


def to_modes(groups, table, kron):
    sides = []
    for group in groups:
        spectra = dot3(split(group), table)
        lanes = spectra.shape[1] // 2
        sides.append(jnp.concatenate([spectra[:, :lanes], spectra[:, lanes:]], 0))
    return dot3(kron, split(jnp.concatenate(sides, 1)))


def from_modes(groups, table, kron_t):
    lanes = groups[0].shape[1]
    mixed = dot3(kron_t, split(jnp.concatenate(groups, 1)))
    half = mixed.shape[0] // 2
    out = []
    for index in range(2):
        side = mixed[:, index * lanes:(index + 1) * lanes]
        out.append(dot3(split(jnp.concatenate([side[:half], side[half:]], 1)), table))
    return out


def gelu_parts(z):
    size = jnp.abs(z)
    gauss = jnp.exp(-0.5 * z * z)
    t = 1.0 / (1.0 + (0.3275911 / math.sqrt(2.0)) * size)
    poly = t * (0.254829592 + t * (-0.284496736 + t * (1.421413741 + t * (-1.453152027 + t * 1.061405429))))
    tail = 0.5 * poly * gauss
    phi = jnp.where(z >= 0, 1.0 - tail, tail)
    return z * phi, phi + z * (gauss * (1.0 / math.sqrt(2.0 * math.pi)))


def load_groups(ref):
    rows, _, width = ref.shape
    return [ref[:, i * G:(i + 1) * G, :].reshape(rows * G, width) for i in range(2)]


def store_groups(ref, groups):
    rows, _, width = ref.shape
    for i in range(2):
        ref[:, i * G:(i + 1) * G, :] = groups[i].reshape(rows, G, width)


def store_modes(ref, modes):
    rows, _, lanes = ref.shape
    for i in range(2):
        ref[:, i * G:(i + 1) * G, :] = modes[:, i * lanes:(i + 1) * lanes].reshape(rows, G, lanes)


def head_kernel(m_ref, a_ref, th, tl, kh, kl, p_ref):
    store_modes(p_ref, to_modes(load_groups(a_ref), (th[...], tl[...]), (kh[...], kl[...])))


def region_stats(step, last, out, branch, rid_ref, stat_ref, eo, eb):
    rows, _, width = eo.shape

    @pl.when(step == 0)
    def _():
        eo[...] = jnp.zeros_like(eo)
        eb[...] = jnp.zeros_like(eb)

    eo[...] += (out[0] * out[0] + out[1] * out[1]).reshape(rows, G, width)
    eb[...] += (branch[0] * branch[0] + branch[1] * branch[1]).reshape(rows, G, width)

    @pl.when(step == last)
    def _():
        rid = rid_ref[...]
        energies = (jnp.sum(eo[...], axis=1), jnp.sum(eb[...], axis=1), jnp.ones((rows, width), F32))
        for kind in range(3):
            for region in range(R):
                line = jnp.sum(jnp.where(rid == region + 1, energies[kind], 0.0), axis=0, keepdims=True)
                total = line[:, :128]
                for piece in range(1, width // 128):
                    total = total + line[:, piece * 128:(piece + 1) * 128]
                stat_ref[kind, region:region + 1, :] = total


def middle_kernel(last, m_ref, y_ref, zc_ref, a_ref, rid_ref, ith, itl, kth, ktl, th, tl, kh, kl,
                  o_ref, dg_ref, p_ref, stat_ref, eo, eb):
    spectral = from_modes(load_groups(y_ref), (ith[...], itl[...]), (kth[...], ktl[...]))
    zc, a = load_groups(zc_ref), load_groups(a_ref)
    out, branch, slope = [], [], []
    for i in range(2):
        value, grad = gelu_parts(spectral[i] + zc[i])
        branch.append(value)
        slope.append(grad)
        out.append(a[i] + value)
    store_groups(o_ref, out)
    store_groups(dg_ref, slope)
    region_stats(pl.program_id(0), last, out, branch, rid_ref, stat_ref, eo, eb)
    store_modes(p_ref, to_modes(out, (th[...], tl[...]), (kh[...], kl[...])))


def turn_kernel(last, m_ref, y_ref, zc_ref, a_ref, cot_ref, rid_ref, ith, itl, kth, ktl, th, tl, kh, kl,
                o_ref, gz_ref, p_ref, stat_ref, eo, eb):
    spectral = from_modes(load_groups(y_ref), (ith[...], itl[...]), (kth[...], ktl[...]))
    zc, a, cot = load_groups(zc_ref), load_groups(a_ref), load_groups(cot_ref)
    out, branch, gz = [], [], []
    for i in range(2):
        value, grad = gelu_parts(spectral[i] + zc[i])
        branch.append(value)
        out.append(a[i] + value)
        gz.append(cot[i] * grad)
    store_groups(o_ref, out)
    store_groups(gz_ref, gz)
    region_stats(pl.program_id(0), last, out, branch, rid_ref, stat_ref, eo, eb)
    store_modes(p_ref, to_modes(gz, (th[...], tl[...]), (kh[...], kl[...])))


def back_kernel(y_ref, h_ref, dg_ref, ith, itl, kth, ktl, th, tl, kh, kl, ga_ref, gz_ref, p_ref):
    spectral = from_modes(load_groups(y_ref), (ith[...], itl[...]), (kth[...], ktl[...]))
    h, dg = load_groups(h_ref), load_groups(dg_ref)
    ga = [spectral[i] + h[i] for i in range(2)]
    gz = [ga[i] * dg[i] for i in range(2)]
    store_groups(ga_ref, ga)
    store_groups(gz_ref, gz)
    store_modes(p_ref, to_modes(gz, (th[...], tl[...]), (kh[...], kl[...])))


def tail_kernel(y_ref, h_ref, ith, itl, kth, ktl, ga_ref):
    spectral = from_modes(load_groups(y_ref), (ith[...], itl[...]), (kth[...], ktl[...]))
    h = load_groups(h_ref)
    store_groups(ga_ref, [spectral[i] + h[i] for i in range(2)])


def conv_kernel(m_ref, a_ref, wh, wl, bias_ref, z_ref):
    rows, channels, width = a_ref.shape
    block = wh.shape[0] // channels
    weight = (wh[...], wl[...])
    for start in range(0, rows, block):
        piece = a_ref[start:start + block].reshape(block * channels, width)
        out = dot3(weight, split(piece)).reshape(block, channels, width)
        z_ref[start:start + block] = out + bias_ref[...][None]


def grad_kernel(m_ref, gz_ref, a_ref, g_ref, wh, wl, h_ref, cg_ref, bg_ref):
    rows, channels, width = a_ref.shape
    block = wh.shape[0] // channels
    weight = (wh[...], wl[...])

    @pl.when(pl.program_id(0) == 0)
    def _():
        cg_ref[...] = jnp.zeros_like(cg_ref)
        bg_ref[...] = jnp.zeros_like(bg_ref)

    grad = jnp.zeros((2 * channels, 2 * channels), F32)
    bias = jnp.zeros((channels, width), F32)
    for start in range(0, rows, block):
        gz = gz_ref[start:start + block]
        parts = split(gz.reshape(block * channels, width))
        h_ref[start:start + block] = g_ref[start:start + block] + dot3(weight, parts).reshape(block, channels, width)
        a_parts = split(a_ref[start:start + block].reshape(block * channels, width))
        for row in range(block):
            rows_of = slice(row * channels, (row + 1) * channels)
            left = jnp.concatenate([p[rows_of] for p in a_parts], 0)
            right = jnp.concatenate([p[rows_of] for p in parts], 0)
            grad = grad + dot(left, right, (((1,), (1,)), ((), ())))
            bias = bias + gz[row]
    cg_ref[...] += grad
    bg_ref[...] += bias


def swap_halves(value):
    return pltpu.roll(value, value.shape[-1] // 2, value.ndim - 1)


def left_lanes(shape):
    return lax.broadcasted_iota(jnp.int32, shape, len(shape) - 1) < shape[-1] // 2


def weight_stream(own, base, local_ref, far_ref, wbuf, sem):
    step, count = pl.program_id(0), pl.num_programs(0)

    def begin(at, slot):
        @pl.when(own)
        def _():
            pltpu.make_async_copy(local_ref.at[0, base + at], wbuf.at[slot], sem.at[slot]).start()

        @pl.when(jnp.logical_not(own))
        def _():
            pltpu.make_async_copy(far_ref.at[at], wbuf.at[slot], sem.at[slot]).start()

    @pl.when(step == 0)
    def _():
        begin(0, 0)

    @pl.when(step + 1 < count)
    def _():
        begin(step + 1, (step + 1) % 2)

    pltpu.make_async_copy(far_ref.at[step], wbuf.at[step % 2], sem.at[step % 2]).wait()
    return wbuf.at[step % 2]


def mix_kernel(m_ref, f_ref, local_ref, far_ref, y_ref, wbuf, f2, sem):
    weight = weight_stream(m_ref[0] == 1, m_ref[1], local_ref, far_ref, wbuf, sem)
    grids, channels, lanes = f_ref.shape
    f2[...] = swap_halves(f_ref[...])

    def body(i, acc):
        w = weight[i]
        out = []
        for g in range(grids):
            out.append(acc[2 * g] + f_ref[g, pl.ds(i, 1), :] * w)
            out.append(acc[2 * g + 1] + f2[g, pl.ds(i, 1), :] * w)
        return tuple(out)

    acc = lax.fori_loop(0, channels, body, tuple(jnp.zeros(weight.shape[1:], F32) for _ in range(2 * grids)),
                        unroll=8)
    left = left_lanes(weight.shape[1:])
    for g in range(grids):
        a, b = acc[2 * g], acc[2 * g + 1]
        y_ref[g] = jnp.where(left, a - swap_halves(a), b + swap_halves(b))


def mix_t_kernel(m_ref, d_ref, local_ref, far_ref, y_ref, wbuf, a1, a2, sem):
    weight = weight_stream(m_ref[0] == 1, m_ref[1], local_ref, far_ref, wbuf, sem)
    grids, channels, lanes = d_ref.shape
    d1 = [d_ref[g] for g in range(grids)]
    d2 = [swap_halves(d) for d in d1]

    def body(i, carry):
        w = weight[i]
        for g in range(grids):
            a1[g, pl.ds(i, 1), :] = jnp.sum(w * d1[g], axis=0, keepdims=True)
            a2[g, pl.ds(i, 1), :] = jnp.sum(w * d2[g], axis=0, keepdims=True)
        return carry

    lax.fori_loop(0, channels, body, 0, unroll=4)
    left = left_lanes((channels, lanes))
    for g in range(grids):
        a, b = a1[g], a2[g]
        y_ref[g] = jnp.where(left, a + swap_halves(a), swap_halves(b) - b)


def weight_grad_kernel(f_ref, d_ref, w_ref, fa, fb, d2):
    count, channels, lanes = f_ref.shape
    block = w_ref.shape[0]
    step = pl.program_id(1)

    @pl.when(step == 0)
    def _():
        f = f_ref[...]
        other = swap_halves(f)
        left = left_lanes(f.shape)
        fa[...] = jnp.where(left, f, other)
        fb[...] = jnp.where(left, other, -f)
        d2[...] = swap_halves(d_ref[...])

    def body(quad, carry):
        at = quad * 4
        acc = [jnp.zeros((channels, lanes), F32) for _ in range(4)]
        for g in range(count):
            d, e = d_ref[g], d2[g]
            for q in range(4):
                i = step * block + at + q
                acc[q] = acc[q] + (fa[g, pl.ds(i, 1), :] * d + fb[g, pl.ds(i, 1), :] * e)
        for q in range(4):
            w_ref[at + q] = acc[q]
        return carry

    lax.fori_loop(0, block // 4, body, 0)


def whole(array):
    return pl.BlockSpec(array.shape, lambda *_: (0,) * array.ndim)


def params(**kw):
    return pltpu.CompilerParams(vmem_limit_bytes=VMEM_LIMIT, **kw)


def local(inputs, cotangent, region_id, spectral_w, conv_w, bias_vector):
    micro_count, _, rows_dev, channels, width = inputs.shape
    lanes = spectral_w.shape[-1]
    half = lanes // 2
    kx_dev = spectral_w.shape[1]
    row_devices, sections = lax.axis_size("rows"), lax.axis_size("section")
    mode_rows, height = kx_dev * row_devices, rows_dev * row_devices
    section = lax.axis_index("section")
    per_core = micro_count // sections
    kx_half = kx_dev // sections
    other_core = [(0, 1), (1, 0)]

    plain, doubled = col_tables(width, half)
    t_plain, t_doubled = np_split(plain), np_split(doubled)
    it_plain, it_doubled = np_split(plain.T), np_split(doubled.T)
    kron, kron_t = row_tables(height, mode_rows, lax.axis_index("rows") * rows_dev, rows_dev)

    chunk = 2 * G
    chunks = channels // chunk
    field = pl.BlockSpec((rows_dev, chunk, width), lambda c, *_: (0, c, 0))
    modes = pl.BlockSpec((mode_rows, chunk, lanes), lambda c, *_: (0, c, 0))
    from_all = pl.BlockSpec((None, None, rows_dev, chunk, width), lambda c, m: (m[0], 0, 0, c, 0))
    rid_all = pl.BlockSpec((None, None, rows_dev, width), lambda c, m: (m[0], 0, 0, 0))
    field_shape = jax.ShapeDtypeStruct((rows_dev, channels, width), F32)
    modes_shape = jax.ShapeDtypeStruct((mode_rows, channels, lanes), F32)
    stat_shape = jax.ShapeDtypeStruct((3, R, 128), F32)
    stat = pl.BlockSpec((3, R, 128), lambda *_: (0, 0, 0))
    energy = pltpu.VMEM((rows_dev, G, width), F32)

    def call(body, prefetch, args, specs, out_shape, out_specs, scratch=(), grid=(chunks,)):
        grid_spec = pltpu.PrefetchScalarGridSpec(
            num_scalar_prefetch=len(prefetch), grid=grid, in_specs=specs, out_specs=out_specs,
            scratch_shapes=list(scratch))
        return pl.pallas_call(body, grid_spec=grid_spec, out_shape=out_shape, compiler_params=params())(
            *prefetch, *args)

    def tables(*groups):
        flat = [t for group in groups for t in group]
        return flat, [whole(t) for t in flat]

    row_block = min(16, rows_dev)
    conv_rows = 256 // channels
    conv_both = lax.all_gather(conv_w, "section", axis=0, tiled=True)
    bias_both = lax.all_gather(bias_vector, "section", axis=0, tiled=True)

    def conv_parts(matrix):
        wide = jnp.kron(jnp.eye(conv_rows, dtype=F32), matrix)
        high = lax.reduce_precision(wide, 8, 7)
        return high.astype(BF16), (wide - high).astype(BF16)

    conv_fwd = [conv_parts(conv_both[l].T) for l in range(2)]
    conv_bwd = [conv_parts(conv_both[l]) for l in range(2)]
    row_field = pl.BlockSpec((row_block, channels, width), lambda r, *_: (r, 0, 0))
    row_all = pl.BlockSpec((None, None, row_block, channels, width), lambda r, m: (m[0], 0, r, 0, 0))

    def conv(layer, micro, field_in, from_inputs):
        flat, specs = tables(conv_fwd[layer])
        bias = jnp.broadcast_to(bias_both[layer][:, None], (channels, width))
        return call(conv_kernel, (micro,), [field_in, *flat, bias],
                    [row_all if from_inputs else row_field, *specs, whole(bias)],
                    field_shape, row_field, grid=(rows_dev // row_block,))

    def grads(layer, micro, gz, a, a_all, g, g_all):
        flat, specs = tables(conv_bwd[layer])
        return call(grad_kernel, (micro,), [gz, a, g, *flat],
                    [row_field, row_all if a_all else row_field, row_all if g_all else row_field, *specs],
                    [field_shape, jax.ShapeDtypeStruct((2 * channels, 2 * channels), F32),
                     jax.ShapeDtypeStruct((channels, width), F32)],
                    [row_field, pl.BlockSpec((2 * channels, 2 * channels), lambda *_: (0, 0)),
                     pl.BlockSpec((channels, width), lambda *_: (0, 0))],
                    grid=(rows_dev // row_block,))

    def swap_cores(value):
        return lax.ppermute(value, "section", other_core)

    def reduce_modes(partial_modes):
        mine = lax.psum_scatter(partial_modes, "rows", scatter_dimension=0, tiled=True)
        keep = lax.dynamic_slice_in_dim(mine, section * kx_half, kx_half, 0)
        give = lax.dynamic_slice_in_dim(mine, (1 - section) * kx_half, kx_half, 0)
        return jnp.stack([keep, swap_cores(give)])

    def gather_modes(mixed):
        back = swap_cores(mixed[1])
        first = section == 0
        shard = jnp.concatenate([jnp.where(first, mixed[0], back), jnp.where(first, back, mixed[0])], 0)
        return lax.all_gather(shard, "rows", axis=0, tiled=True)

    far_weights = swap_cores(lax.dynamic_slice_in_dim(spectral_w[0], (1 - section) * kx_half, kx_half, 0))

    def mixing(body, layer, pair):
        flag = jnp.stack([(section == layer).astype(jnp.int32), section * kx_half])
        block = pl.BlockSpec((2, None, channels, lanes), lambda x, m: (0, x, 0, 0))
        forward = body is mix_kernel
        small = pltpu.VMEM((2, channels, lanes), F32)
        return call(body, (flag,), [pair, spectral_w, far_weights],
                    [block, pl.BlockSpec(memory_space=pl.ANY), pl.BlockSpec(memory_space=pl.ANY)],
                    jax.ShapeDtypeStruct(pair.shape, F32), block,
                    [pltpu.VMEM((2, channels, channels, lanes), F32), small]
                    + ([] if forward else [small]) + [pltpu.SemaphoreType.DMA((2,))], grid=(kx_half,))

    def gather_batch(pairs):
        joined = jnp.concatenate(pairs, 0)
        return lax.all_gather(joined, "batch", axis=0, tiled=True)

    def weight_grad(f_all, d_all):
        count = f_all.shape[0]
        block = 16
        spec = pl.BlockSpec((count, None, channels, lanes), lambda x, i: (0, x, 0, 0))
        big = pltpu.VMEM((count, channels, lanes), F32)
        return pl.pallas_call(
            weight_grad_kernel, grid=(kx_half, channels // block), in_specs=[spec, spec],
            out_specs=pl.BlockSpec((None, block, channels, lanes), lambda x, i: (x, i, 0, 0)),
            out_shape=jax.ShapeDtypeStruct((kx_half, channels, channels, lanes), F32),
            scratch_shapes=[big, big, big], compiler_params=params())(f_all, d_all)

    micro = [jnp.reshape(section * per_core + j, (1,)).astype(jnp.int32) for j in range(per_core)]
    streams = range(per_core)

    flat, specs = tables(t_plain, kron)
    partials = [call(head_kernel, (micro[j],), [inputs, *flat], [from_all, *specs], modes_shape, modes)
                for j in streams]
    f0 = [reduce_modes(p) for p in partials]
    zc0 = [conv(0, micro[j], inputs, True) for j in streams]
    y0 = [gather_modes(mixing(mix_kernel, 0, f)) for f in f0]
    flat, specs = tables(it_doubled, kron_t, t_plain, kron)
    a1, dg0, partials, stats0 = zip(*[
        call(functools.partial(middle_kernel, chunks - 1), (micro[j],),
             [y0[j], zc0[j], inputs, region_id, *flat], [modes, field, from_all, rid_all, *specs],
             [field_shape, field_shape, modes_shape, stat_shape], [field, field, modes, stat], [energy, energy])
        for j in streams])
    f1 = [reduce_modes(p) for p in partials]
    zc1 = [conv(1, micro[j], a1[j], False) for j in streams]
    y1 = [gather_modes(mixing(mix_kernel, 1, f)) for f in f1]
    flat, specs = tables(it_doubled, kron_t, t_doubled, kron)
    out1, gz1, partials, stats1 = zip(*[
        call(functools.partial(turn_kernel, chunks - 1), (micro[j],),
             [y1[j], zc1[j], a1[j], cotangent, region_id, *flat], [modes, field, field, from_all, rid_all, *specs],
             [field_shape, field_shape, modes_shape, stat_shape], [field, field, modes, stat], [energy, energy])
        for j in streams])
    d1 = [reduce_modes(p) for p in partials]
    h1, cg1, bg1 = zip(*[grads(1, micro[j], gz1[j], a1[j], False, cotangent, True) for j in streams])
    e1 = [gather_modes(mixing(mix_t_kernel, 1, d)) for d in d1]
    flat, specs = tables(it_plain, kron_t, t_doubled, kron)
    ga1, gz0, partials = zip(*[
        call(back_kernel, (), [e1[j], h1[j], dg0[j], *flat], [modes, field, field, *specs],
             [field_shape, field_shape, modes_shape], [field, field, modes]) for j in streams])
    d0 = [reduce_modes(p) for p in partials]
    h0, cg0, bg0 = zip(*[grads(0, micro[j], gz0[j], inputs, True, ga1[j], False) for j in streams])
    wg1 = weight_grad(gather_batch(f1), gather_batch(d1))
    e0 = [gather_modes(mixing(mix_t_kernel, 0, d)) for d in d0]
    flat, specs = tables(it_plain, kron_t)
    ga0 = [call(tail_kernel, (), [e0[j], h0[j], *flat], [modes, field, *specs], field_shape, field) for j in streams]
    wg0 = weight_grad(gather_batch(f0), gather_batch(d0))

    def lower(value):
        return (value[:channels, :channels] + value[channels:, channels:]
                + value[:channels, channels:] + value[channels:, :channels])

    conv_local = jnp.stack([lower(sum(cg0)), lower(sum(cg1))])
    bias_local = jnp.stack([jnp.sum(sum(bg0), -1), jnp.sum(sum(bg1), -1)])
    stat_local = jnp.stack([jnp.sum(sum(stats0), -1), jnp.sum(sum(stats1), -1)])
    conv_sum, bias_sum, stat_sum = lax.psum((conv_local, bias_local, stat_local), ("section", "batch", "rows"))
    own_stat = lax.dynamic_index_in_dim(stat_sum, section, 0, False)
    layer_rms = jnp.sqrt(own_stat[:2] / (channels * own_stat[2])[None, :] + 1e-06)[None]

    first = section == 0
    mine = jnp.where(first, jnp.stack(ga0), jnp.stack(out1))
    theirs = swap_cores(jnp.where(first, jnp.stack(out1), jnp.stack(ga0)))
    boundary = jnp.concatenate([jnp.where(first, mine, theirs), jnp.where(first, theirs, mine)], 0)[None, :, None]
    mine = jnp.where(first, wg0, wg1)
    theirs = swap_cores(jnp.where(first, wg1, wg0))
    spectral_grad = jnp.concatenate([jnp.where(first, mine, theirs), jnp.where(first, theirs, mine)], 0)[None]
    own = lambda value: lax.dynamic_slice_in_dim(value, section, 1, 0)
    return boundary, spectral_grad, own(conv_sum), own(bias_sum), layer_rms


def solution(mesh):
    placed = (
        P(None, "batch", "rows", None, None),
        P(None, "batch", "rows", None, None),
        P(None, "batch", "rows", None),
        P("section", "rows", None, None, None),
        P("section", None, None),
        P("section", None),
    )
    return jax.shard_map(
        local,
        mesh=mesh,
        in_specs=placed,
        out_specs=(
            P("section", None, "batch", "rows", None, None),
            P("section", "rows", None, None, None),
            P("section", None, None),
            P("section", None),
            P("section", None, None),
        ),
        check_vma=False,
    )
```

```python
import functools
import math

import jax
import jax.numpy as jnp
import numpy as np
from jax import lax
from jax.experimental import pallas as pl
from jax.experimental.pallas import tpu as pltpu
from jax.sharding import PartitionSpec as P

R = 8
G = 8
F32 = jnp.float32
BF16 = jnp.bfloat16
VMEM_LIMIT = 56 * 1024 * 1024


def split(value):
    high = value.astype(BF16)
    return high, (value - high.astype(F32)).astype(BF16)


def dot(left, right, dims=(((1,), (0,)), ((), ()))):
    return lax.dot_general(left, right, dims, preferred_element_type=F32)


def dot3(left, right):
    return dot(left[0], right[0]) + (dot(left[1], right[0]) + dot(left[0], right[1]))


def np_split(value):
    high = value.astype(np.float32).astype(BF16)
    return high, (value - high.astype(np.float64)).astype(np.float32).astype(BF16)


def col_tables(width, half):
    phase = 2.0 * math.pi / width * (np.outer(np.arange(width), np.arange(half)) % width)
    cosine, sine = np.cos(phase) / math.sqrt(width), np.sin(phase) / math.sqrt(width)
    plain = np.concatenate([cosine, -sine, -sine, -cosine], 1)
    doubled = plain * np.tile(np.where(np.arange(half) == 0, 1.0, 2.0), 4)[None, :]
    return plain, doubled


def row_tables(height, mode_rows, first_row, rows_dev):
    position = jnp.arange(mode_rows, dtype=jnp.int32)
    frequency = jnp.where(position < mode_rows // 2, position, height - mode_rows + position)
    row = first_row + jnp.arange(rows_dev, dtype=jnp.int32)
    phase = 2.0 * math.pi / height * (frequency[:, None] * row[None, :] % height).astype(F32)
    small = jnp.concatenate([jnp.cos(phase), jnp.sin(phase)], 1) / math.sqrt(height)
    rounded = lax.reduce_precision(small, 8, 7)
    high, low = rounded.astype(BF16), (small - rounded).astype(BF16)
    forward = jnp.concatenate([jnp.concatenate([high, high], 1), jnp.concatenate([low, jnp.zeros_like(low)], 1)], 0)
    inverse = jnp.concatenate([high.T, high.T, low.T], 1)
    return forward, inverse


def to_modes(value, table, kron, spread, p_ref):
    mode_rows, count, lanes = p_ref.shape
    rows = value.shape[0] // count
    high, low = split(value)
    spectra = dot(jnp.concatenate([high, low, high], 1), table)
    for i in range(2):
        spread[i] = spectra[:, i * lanes:(i + 1) * lanes]
    out = p_ref.reshape(mode_rows * count, lanes)
    for first in range(0, count, 2):
        sides = []
        for c in (first, first + 1):
            pick = pl.ds(c, rows, stride=count)
            sides.append(jnp.concatenate([spread[i, pick, :] for i in range(2)], 0))
        high, low = split(jnp.concatenate(sides, 1))
        both = dot(kron, jnp.concatenate([high, low], 0))
        result = both[:mode_rows] + both[mode_rows:]
        for i in range(2):
            out[pl.ds(first + i, mode_rows, stride=count), :] = result[:, i * lanes:(i + 1) * lanes]


def from_modes(y_ref, table, kron, spread):
    mode_rows, count, lanes = y_ref.shape
    rows, pieces = spread.shape[1] // count, spread.shape[0]
    modes = y_ref.reshape(mode_rows * count, lanes)
    sides = []
    for first in range(0, count, 2):
        pair = [modes[pl.ds(c, mode_rows, stride=count), :] for c in (first, first + 1)]
        high, low = split(jnp.concatenate(pair, 1))
        both = dot(kron, jnp.concatenate([high, low, high], 0))
        for i in range(2):
            side = both[:, i * lanes:(i + 1) * lanes]
            sides.append(jnp.concatenate([side[:rows], side[rows:]], 1))
    high, low = split(jnp.concatenate(sides, 0))
    out = dot(jnp.concatenate([high, low, high], 1), table)
    for c in range(count):
        for i in range(pieces):
            spread[i, pl.ds(c, rows, stride=count), :] = out[c * rows:(c + 1) * rows, i * 128:(i + 1) * 128]
    return jnp.concatenate([spread[i] for i in range(pieces)], 1)


def gelu_parts(z):
    size = jnp.abs(z)
    gauss = jnp.exp(-0.5 * z * z)
    t = 1.0 / (1.0 + (0.3275911 / math.sqrt(2.0)) * size)
    poly = t * (0.254829592 + t * (-0.284496736 + t * (1.421413741 + t * (-1.453152027 + t * 1.061405429))))
    tail = 0.5 * poly * gauss
    phi = jnp.where(z >= 0, 1.0 - tail, tail)
    return z * phi, phi + z * (gauss * (1.0 / math.sqrt(2.0 * math.pi)))


def flat(ref):
    rows, count, width = ref.shape
    return ref[...].reshape(rows * count, width)


def put(ref, value):
    ref[...] = value.reshape(ref.shape)


def head_kernel(m_ref, a_ref, table, kron, p_ref, spread):
    to_modes(flat(a_ref), table[...], kron[...], spread, p_ref)


def region_stats(step, last, out, branch, rid_ref, stat_ref, eo, eb):
    rows, _, width = eo.shape

    @pl.when(step == 0)
    def _():
        eo[...] = jnp.zeros_like(eo)
        eb[...] = jnp.zeros_like(eb)

    for value, total in ((out, eo), (branch, eb)):
        square = (value * value).reshape(rows, -1, width)
        for at in range(0, square.shape[1], G):
            total[...] += square[:, at:at + G]

    @pl.when(step == last)
    def _():
        rid = rid_ref[...]
        energies = (jnp.sum(eo[...], axis=1), jnp.sum(eb[...], axis=1), jnp.ones((rows, width), F32))
        for kind in range(3):
            for region in range(R):
                line = jnp.sum(jnp.where(rid == region + 1, energies[kind], 0.0), axis=0, keepdims=True)
                total = line[:, :128]
                for piece in range(1, width // 128):
                    total = total + line[:, piece * 128:(piece + 1) * 128]
                stat_ref[kind, region:region + 1, :] = total


def middle_kernel(last, m_ref, y_ref, zc_ref, a_ref, rid_ref, itable, ikron, table, kron,
                  o_ref, dg_ref, p_ref, stat_ref, spread, eo, eb):
    z = from_modes(y_ref, itable[...], ikron[...], spread) + flat(zc_ref)
    branch, slope = gelu_parts(z)
    put(dg_ref, slope)
    out = flat(a_ref) + branch
    put(o_ref, out)
    region_stats(pl.program_id(0), last, out, branch, rid_ref, stat_ref, eo, eb)
    to_modes(flat(o_ref), table[...], kron[...], spread, p_ref)


def turn_kernel(last, m_ref, y_ref, zc_ref, a_ref, cot_ref, rid_ref, itable, ikron, table, kron,
                o_ref, gz_ref, p_ref, stat_ref, spread, eo, eb):
    z = from_modes(y_ref, itable[...], ikron[...], spread) + flat(zc_ref)
    branch, slope = gelu_parts(z)
    put(gz_ref, flat(cot_ref) * slope)
    out = flat(a_ref) + branch
    put(o_ref, out)
    region_stats(pl.program_id(0), last, out, branch, rid_ref, stat_ref, eo, eb)
    to_modes(flat(gz_ref), table[...], kron[...], spread, p_ref)


def back_kernel(y_ref, h_ref, dg_ref, itable, ikron, table, kron, ga_ref, gz_ref, p_ref, spread):
    ga = from_modes(y_ref, itable[...], ikron[...], spread) + flat(h_ref)
    put(ga_ref, ga)
    put(gz_ref, ga * flat(dg_ref))
    to_modes(flat(gz_ref), table[...], kron[...], spread, p_ref)


def tail_kernel(y_ref, h_ref, itable, ikron, ga_ref, spread):
    put(ga_ref, from_modes(y_ref, itable[...], ikron[...], spread) + flat(h_ref))


def conv_kernel(m_ref, a_ref, wh, wl, bias_ref, z_ref):
    rows, channels, width = a_ref.shape
    block = wh.shape[0] // channels
    weight = (wh[...], wl[...])
    for start in range(0, rows, block):
        piece = a_ref[start:start + block].reshape(block * channels, width)
        out = dot3(weight, split(piece)).reshape(block, channels, width)
        z_ref[start:start + block] = out + bias_ref[...][None]


def grad_kernel(m_ref, gz_ref, a_ref, g_ref, wh, wl, h_ref, cg_ref, bg_ref):
    rows, channels, width = a_ref.shape
    block = wh.shape[0] // channels
    weight = (wh[...], wl[...])

    @pl.when(pl.program_id(0) == 0)
    def _():
        cg_ref[...] = jnp.zeros_like(cg_ref)
        bg_ref[...] = jnp.zeros_like(bg_ref)

    grad = jnp.zeros((2 * channels, 2 * channels), F32)
    bias = jnp.zeros((channels, width), F32)
    for start in range(0, rows, block):
        gz = gz_ref[start:start + block]
        parts = split(gz.reshape(block * channels, width))
        h_ref[start:start + block] = g_ref[start:start + block] + dot3(weight, parts).reshape(block, channels, width)
        a_parts = split(a_ref[start:start + block].reshape(block * channels, width))
        for row in range(block):
            rows_of = slice(row * channels, (row + 1) * channels)
            left = jnp.concatenate([p[rows_of] for p in a_parts], 0)
            right = jnp.concatenate([p[rows_of] for p in parts], 0)
            grad = grad + dot(left, right, (((1,), (1,)), ((), ())))
            bias = bias + gz[row]
    cg_ref[...] += grad
    bg_ref[...] += bias


def swap_halves(value):
    return pltpu.roll(value, value.shape[-1] // 2, value.ndim - 1)


def left_lanes(shape):
    return lax.broadcasted_iota(jnp.int32, shape, len(shape) - 1) < shape[-1] // 2


def weight_stream(own, base, local_ref, far_ref, wbuf, sem):
    step, count = pl.program_id(0), pl.num_programs(0)

    def begin(at, slot):
        @pl.when(own)
        def _():
            pltpu.make_async_copy(local_ref.at[0, base + at], wbuf.at[slot], sem.at[slot]).start()

        @pl.when(jnp.logical_not(own))
        def _():
            pltpu.make_async_copy(far_ref.at[at], wbuf.at[slot], sem.at[slot]).start()

    @pl.when(step == 0)
    def _():
        begin(0, 0)

    @pl.when(step + 1 < count)
    def _():
        begin(step + 1, (step + 1) % 2)

    pltpu.make_async_copy(far_ref.at[step], wbuf.at[step % 2], sem.at[step % 2]).wait()
    return wbuf.at[step % 2]


def mix_kernel(m_ref, f_ref, local_ref, far_ref, y_ref, wbuf, f2, sem):
    weight = weight_stream(m_ref[0] == 1, m_ref[1], local_ref, far_ref, wbuf, sem)
    grids, channels, lanes = f_ref.shape
    f2[...] = swap_halves(f_ref[...])

    def body(block, acc):
        at = pl.multiple_of(block * G, G)
        acc = list(acc)
        tiles = [(f_ref[g, pl.ds(at, G), :], f2[g, pl.ds(at, G), :]) for g in range(grids)]
        for u in range(G):
            w = weight[at + u]
            for g in range(grids):
                for side in range(2):
                    acc[2 * g + side] = acc[2 * g + side] + tiles[g][side][u:u + 1] * w
        return tuple(acc)

    acc = lax.fori_loop(0, channels // G, body, tuple(jnp.zeros(weight.shape[1:], F32) for _ in range(2 * grids)))
    left = left_lanes(weight.shape[1:])
    for g in range(grids):
        a, b = acc[2 * g], acc[2 * g + 1]
        y_ref[g] = jnp.where(left, a - swap_halves(a), b + swap_halves(b))


def mix_t_kernel(m_ref, d_ref, local_ref, far_ref, y_ref, wbuf, a1, a2, sem):
    weight = weight_stream(m_ref[0] == 1, m_ref[1], local_ref, far_ref, wbuf, sem)
    grids, channels, lanes = d_ref.shape
    d1 = [d_ref[g] for g in range(grids)]
    d2 = [swap_halves(d) for d in d1]

    def body(block, carry):
        at = pl.multiple_of(block * G, G)
        rows = [[] for _ in range(2 * grids)]
        for u in range(G):
            w = weight[at + u]
            for g in range(grids):
                rows[2 * g].append(jnp.sum(w * d1[g], axis=0, keepdims=True))
                rows[2 * g + 1].append(jnp.sum(w * d2[g], axis=0, keepdims=True))
        for g in range(grids):
            a1[g, pl.ds(at, G), :] = jnp.concatenate(rows[2 * g], 0)
            a2[g, pl.ds(at, G), :] = jnp.concatenate(rows[2 * g + 1], 0)
        return carry

    lax.fori_loop(0, channels // G, body, 0)
    left = left_lanes((channels, lanes))
    for g in range(grids):
        a, b = a1[g], a2[g]
        y_ref[g] = jnp.where(left, a + swap_halves(a), swap_halves(b) - b)


def weight_grad_kernel(f_ref, d_ref, w_ref, fa, fb, d2):
    count, channels, lanes = f_ref.shape
    block = w_ref.shape[0]
    step = pl.program_id(1)

    @pl.when(step == 0)
    def _():
        f = f_ref[...]
        other = swap_halves(f)
        left = left_lanes(f.shape)
        fa[...] = jnp.where(left, f, other)
        fb[...] = jnp.where(left, other, -f)
        d2[...] = swap_halves(d_ref[...])

    def body(octet, carry):
        at = pl.multiple_of(octet * G, G)
        rows = pl.ds(pl.multiple_of(step * block + at, G), G)
        for first in range(0, G, 4):
            acc = [jnp.zeros((channels, lanes), F32) for _ in range(4)]
            for g in range(count):
                d, e = d_ref[g], d2[g]
                ta, tb = fa[g, rows, :], fb[g, rows, :]
                for q in range(4):
                    u = first + q
                    acc[q] = acc[q] + (ta[u:u + 1] * d + tb[u:u + 1] * e)
            for q in range(4):
                w_ref[at + first + q] = acc[q]
        return carry

    lax.fori_loop(0, block // G, body, 0)


def place_kernel(o_here, o_far, g_here, g_far, w1_here, w1_far, w0_here, w0_far, field_ref, weight_ref, sem):
    section = lax.axis_index("section")
    count, half = g_here.shape[0], w0_here.shape[0]

    def run(copies):
        moves = [pltpu.make_async_copy(src, dst, sem.at[i]) for i, (src, dst) in enumerate(copies)]
        for move in moves:
            move.start()
        for move in moves:
            move.wait()

    @pl.when(section == 0)
    def _():
        run([(g_here, field_ref.at[pl.ds(0, count)]), (g_far, field_ref.at[pl.ds(count, count)]),
             (w0_here, weight_ref.at[pl.ds(0, half)]), (w0_far, weight_ref.at[pl.ds(half, half)])])

    @pl.when(section != 0)
    def _():
        run([(o_far, field_ref.at[pl.ds(0, count)]), (o_here, field_ref.at[pl.ds(count, count)]),
             (w1_far, weight_ref.at[pl.ds(0, half)]), (w1_here, weight_ref.at[pl.ds(half, half)])])


def whole(array):
    return pl.BlockSpec(array.shape, lambda *_: (0,) * array.ndim)


def params(**kw):
    return pltpu.CompilerParams(vmem_limit_bytes=VMEM_LIMIT, **kw)


def local(inputs, cotangent, region_id, spectral_w, conv_w, bias_vector):
    micro_count, _, rows_dev, channels, width = inputs.shape
    lanes = spectral_w.shape[-1]
    half = lanes // 2
    kx_dev = spectral_w.shape[1]
    row_devices, sections = lax.axis_size("rows"), lax.axis_size("section")
    mode_rows, height = kx_dev * row_devices, rows_dev * row_devices
    section = lax.axis_index("section")
    per_core = micro_count // sections
    kx_half = kx_dev // sections
    other_core = [(0, 1), (1, 0)]

    plain, doubled = col_tables(width, half)
    def stacked(array):
        high, low = np_split(array)
        return np.concatenate([high, high, low], 0)

    t_plain, t_doubled, it_plain, it_doubled = [stacked(t) for t in (plain, doubled, plain.T, doubled.T)]
    kron, ikron = row_tables(height, mode_rows, lax.axis_index("rows") * rows_dev, rows_dev)

    chunk = 2 * G
    chunks = channels // chunk
    field = pl.BlockSpec((rows_dev, chunk, width), lambda c, *_: (0, c, 0))
    modes = pl.BlockSpec((mode_rows, chunk, lanes), lambda c, *_: (0, c, 0))
    from_all = pl.BlockSpec((None, None, rows_dev, chunk, width), lambda c, m: (m[0], 0, 0, c, 0))
    rid_all = pl.BlockSpec((None, None, rows_dev, width), lambda c, m: (m[0], 0, 0, 0))
    field_shape = jax.ShapeDtypeStruct((rows_dev, channels, width), F32)
    modes_shape = jax.ShapeDtypeStruct((mode_rows, channels, lanes), F32)
    stat_shape = jax.ShapeDtypeStruct((3, R, 128), F32)
    stat = pl.BlockSpec((3, R, 128), lambda *_: (0, 0, 0))
    energy = pltpu.VMEM((rows_dev, G, width), F32)
    spread = pltpu.VMEM((width // 128, rows_dev * chunk, 128), F32)

    def call(body, prefetch, args, specs, out_shape, out_specs, scratch=(), grid=(chunks,)):
        grid_spec = pltpu.PrefetchScalarGridSpec(
            num_scalar_prefetch=len(prefetch), grid=grid, in_specs=specs, out_specs=out_specs,
            scratch_shapes=list(scratch))
        return pl.pallas_call(body, grid_spec=grid_spec, out_shape=out_shape, compiler_params=params())(
            *prefetch, *args)

    def tables(*arrays):
        return arrays, [whole(t) for t in arrays]

    row_block = min(16, rows_dev)
    conv_rows = 256 // channels
    conv_both = lax.all_gather(conv_w, "section", axis=0, tiled=True)
    bias_both = lax.all_gather(bias_vector, "section", axis=0, tiled=True)

    def conv_parts(matrix):
        wide = jnp.kron(jnp.eye(conv_rows, dtype=F32), matrix)
        high = lax.reduce_precision(wide, 8, 7)
        return high.astype(BF16), (wide - high).astype(BF16)

    conv_fwd = [conv_parts(conv_both[l].T) for l in range(2)]
    conv_bwd = [conv_parts(conv_both[l]) for l in range(2)]
    row_field = pl.BlockSpec((row_block, channels, width), lambda r, *_: (r, 0, 0))
    row_all = pl.BlockSpec((None, None, row_block, channels, width), lambda r, m: (m[0], 0, r, 0, 0))

    def conv(layer, micro, field_in, from_inputs):
        consts, specs = tables(*conv_fwd[layer])
        bias = jnp.broadcast_to(bias_both[layer][:, None], (channels, width))
        return call(conv_kernel, (micro,), [field_in, *consts, bias],
                    [row_all if from_inputs else row_field, *specs, whole(bias)],
                    field_shape, row_field, grid=(rows_dev // row_block,))

    def grads(layer, micro, gz, a, a_all, g, g_all):
        consts, specs = tables(*conv_bwd[layer])
        return call(grad_kernel, (micro,), [gz, a, g, *consts],
                    [row_field, row_all if a_all else row_field, row_all if g_all else row_field, *specs],
                    [field_shape, jax.ShapeDtypeStruct((2 * channels, 2 * channels), F32),
                     jax.ShapeDtypeStruct((channels, width), F32)],
                    [row_field, pl.BlockSpec((2 * channels, 2 * channels), lambda *_: (0, 0)),
                     pl.BlockSpec((channels, width), lambda *_: (0, 0))],
                    grid=(rows_dev // row_block,))

    def swap_cores(value):
        return lax.ppermute(value, "section", other_core)

    def reduce_modes(partial_modes):
        mine = lax.psum_scatter(partial_modes, "rows", scatter_dimension=0, tiled=True)
        keep = lax.dynamic_slice_in_dim(mine, section * kx_half, kx_half, 0)
        give = lax.dynamic_slice_in_dim(mine, (1 - section) * kx_half, kx_half, 0)
        return jnp.stack([keep, swap_cores(give)])

    def gather_modes(mixed):
        back = swap_cores(mixed[1])
        first = section == 0
        shard = jnp.concatenate([jnp.where(first, mixed[0], back), jnp.where(first, back, mixed[0])], 0)
        return lax.all_gather(shard, "rows", axis=0, tiled=True)

    far_weights = swap_cores(lax.dynamic_slice_in_dim(spectral_w[0], (1 - section) * kx_half, kx_half, 0))

    def mixing(body, layer, pair):
        flag = jnp.stack([(section == layer).astype(jnp.int32), section * kx_half])
        block = pl.BlockSpec((2, None, channels, lanes), lambda x, m: (0, x, 0, 0))
        forward = body is mix_kernel
        small = pltpu.VMEM((2, channels, lanes), F32)
        return call(body, (flag,), [pair, spectral_w, far_weights],
                    [block, pl.BlockSpec(memory_space=pl.ANY), pl.BlockSpec(memory_space=pl.ANY)],
                    jax.ShapeDtypeStruct(pair.shape, F32), block,
                    [pltpu.VMEM((2, channels, channels, lanes), F32), small]
                    + ([] if forward else [small]) + [pltpu.SemaphoreType.DMA((2,))], grid=(kx_half,))

    def gather_batch(pairs):
        joined = jnp.concatenate(pairs, 0)
        return lax.all_gather(joined, "batch", axis=0, tiled=True)

    def weight_grad(f_all, d_all):
        count = f_all.shape[0]
        block = 16
        spec = pl.BlockSpec((count, None, channels, lanes), lambda x, i: (0, x, 0, 0))
        big = pltpu.VMEM((count, channels, lanes), F32)
        return pl.pallas_call(
            weight_grad_kernel, grid=(kx_half, channels // block), in_specs=[spec, spec],
            out_specs=pl.BlockSpec((None, block, channels, lanes), lambda x, i: (x, i, 0, 0)),
            out_shape=jax.ShapeDtypeStruct((kx_half, channels, channels, lanes), F32),
            scratch_shapes=[big, big, big], compiler_params=params())(f_all, d_all)

    micro = [jnp.reshape(section * per_core + j, (1,)).astype(jnp.int32) for j in range(per_core)]
    streams = range(per_core)

    consts, specs = tables(t_plain, kron)
    partials = [call(head_kernel, (micro[j],), [inputs, *consts], [from_all, *specs], modes_shape, modes, [spread])
                for j in streams]
    f0 = [reduce_modes(p) for p in partials]
    zc0 = [conv(0, micro[j], inputs, True) for j in streams]
    y0 = [gather_modes(mixing(mix_kernel, 0, f)) for f in f0]
    consts, specs = tables(it_doubled, ikron, t_plain, kron)
    a1, dg0, partials, stats0 = zip(*[
        call(functools.partial(middle_kernel, chunks - 1), (micro[j],),
             [y0[j], zc0[j], inputs, region_id, *consts], [modes, field, from_all, rid_all, *specs],
             [field_shape, field_shape, modes_shape, stat_shape], [field, field, modes, stat], [spread, energy, energy])
        for j in streams])
    f1 = [reduce_modes(p) for p in partials]
    zc1 = [conv(1, micro[j], a1[j], False) for j in streams]
    y1 = [gather_modes(mixing(mix_kernel, 1, f)) for f in f1]
    consts, specs = tables(it_doubled, ikron, t_doubled, kron)
    out1, gz1, partials, stats1 = zip(*[
        call(functools.partial(turn_kernel, chunks - 1), (micro[j],),
             [y1[j], zc1[j], a1[j], cotangent, region_id, *consts], [modes, field, field, from_all, rid_all, *specs],
             [field_shape, field_shape, modes_shape, stat_shape], [field, field, modes, stat], [spread, energy, energy])
        for j in streams])
    d1 = [reduce_modes(p) for p in partials]
    h1, cg1, bg1 = zip(*[grads(1, micro[j], gz1[j], a1[j], False, cotangent, True) for j in streams])
    e1 = [gather_modes(mixing(mix_t_kernel, 1, d)) for d in d1]
    consts, specs = tables(it_plain, ikron, t_doubled, kron)
    ga1, gz0, partials = zip(*[
        call(back_kernel, (), [e1[j], h1[j], dg0[j], *consts], [modes, field, field, *specs],
             [field_shape, field_shape, modes_shape], [field, field, modes], [spread]) for j in streams])
    d0 = [reduce_modes(p) for p in partials]
    h0, cg0, bg0 = zip(*[grads(0, micro[j], gz0[j], inputs, True, ga1[j], False) for j in streams])
    wg1 = weight_grad(gather_batch(f1), gather_batch(d1))
    e0 = [gather_modes(mixing(mix_t_kernel, 0, d)) for d in d0]
    consts, specs = tables(it_plain, ikron)
    ga0 = [call(tail_kernel, (), [e0[j], h0[j], *consts], [modes, field, *specs], field_shape, field, [spread])
           for j in streams]
    wg0 = weight_grad(gather_batch(f0), gather_batch(d0))

    def lower(value):
        return (value[:channels, :channels] + value[channels:, channels:]
                + value[:channels, channels:] + value[channels:, :channels])

    conv_local = jnp.stack([lower(sum(cg0)), lower(sum(cg1))])
    bias_local = jnp.stack([jnp.sum(sum(bg0), -1), jnp.sum(sum(bg1), -1)])
    stat_local = jnp.stack([jnp.sum(sum(stats0), -1), jnp.sum(sum(stats1), -1)])
    conv_sum, bias_sum, stat_sum = lax.psum((conv_local, bias_local, stat_local), ("section", "batch", "rows"))
    own_stat = lax.dynamic_index_in_dim(stat_sum, section, 0, False)
    layer_rms = jnp.sqrt(own_stat[:2] / (channels * own_stat[2])[None, :] + 1e-06)[None]

    down, up = [(1, 0)], [(0, 1)]
    outs, gas = jnp.stack(out1), jnp.stack(ga0)
    placed = [outs, lax.ppermute(outs, "section", up), gas, lax.ppermute(gas, "section", down),
              wg1, lax.ppermute(wg1, "section", up), wg0, lax.ppermute(wg0, "section", down)]
    hbm = pl.BlockSpec(memory_space=pl.ANY)
    boundary, spectral_grad = pl.pallas_call(
        place_kernel, in_specs=[hbm] * 8, out_specs=[hbm] * 2,
        out_shape=[jax.ShapeDtypeStruct((micro_count, rows_dev, channels, width), F32),
                   jax.ShapeDtypeStruct((kx_dev, channels, channels, lanes), F32)],
        scratch_shapes=[pltpu.SemaphoreType.DMA((4,))], compiler_params=params())(*placed)
    boundary, spectral_grad = boundary[None, :, None], spectral_grad[None]
    own = lambda value: lax.dynamic_slice_in_dim(value, section, 1, 0)
    return boundary, spectral_grad, own(conv_sum), own(bias_sum), layer_rms


def solution(mesh):
    placed = (
        P(None, "batch", "rows", None, None),
        P(None, "batch", "rows", None, None),
        P(None, "batch", "rows", None),
        P("section", "rows", None, None, None),
        P("section", None, None),
        P("section", None),
    )
    return jax.shard_map(
        local,
        mesh=mesh,
        in_specs=placed,
        out_specs=(
            P("section", None, "batch", "rows", None, None),
            P("section", "rows", None, None, None),
            P("section", None, None),
            P("section", None),
            P("section", None, None),
        ),
        check_vma=False,
    )
```

```python
import functools
import math

import jax
import jax.numpy as jnp
import numpy as np
from jax import lax
from jax.experimental import pallas as pl
from jax.experimental.pallas import tpu as pltpu
from jax.sharding import PartitionSpec as P

R = 8
G = 8
F32 = jnp.float32
BF16 = jnp.bfloat16
VMEM_LIMIT = 56 * 1024 * 1024
MESH = pl.DeviceIdType.MESH


def split(value):
    high = value.astype(BF16)
    return high, (value - high.astype(F32)).astype(BF16)


def dot(left, right, dims=(((1,), (0,)), ((), ()))):
    return lax.dot_general(left, right, dims, preferred_element_type=F32)


def dot3(left, right):
    return dot(left[0], right[0]) + (dot(left[1], right[0]) + dot(left[0], right[1]))


def np_split(value):
    high = value.astype(np.float32).astype(BF16)
    return high, (value - high.astype(np.float64)).astype(np.float32).astype(BF16)


def col_tables(width, half):
    phase = 2.0 * math.pi / width * (np.outer(np.arange(width), np.arange(half)) % width)
    cosine, sine = np.cos(phase) / math.sqrt(width), np.sin(phase) / math.sqrt(width)
    plain = np.concatenate([cosine, -sine, -sine, -cosine], 1)
    doubled = plain * np.tile(np.where(np.arange(half) == 0, 1.0, 2.0), 4)[None, :]
    return plain, doubled


def row_tables(height, mode_rows, first_row, rows_dev):
    position = jnp.arange(mode_rows, dtype=jnp.int32)
    frequency = jnp.where(position < mode_rows // 2, position, height - mode_rows + position)
    row = first_row + jnp.arange(rows_dev, dtype=jnp.int32)
    phase = 2.0 * math.pi / height * (frequency[:, None] * row[None, :] % height).astype(F32)
    small = jnp.concatenate([jnp.cos(phase), jnp.sin(phase)], 1) / math.sqrt(height)
    rounded = lax.reduce_precision(small, 8, 7)
    high, low = rounded.astype(BF16), (small - rounded).astype(BF16)
    forward = jnp.concatenate([jnp.concatenate([high, high], 1), jnp.concatenate([low, jnp.zeros_like(low)], 1)], 0)
    inverse = jnp.concatenate([high.T, high.T, low.T], 1)
    return forward, inverse


def to_modes(value, table, kron, spread, p_ref):
    mode_rows, count, lanes = p_ref.shape
    rows = value.shape[0] // count
    high, low = split(value)
    spectra = dot(jnp.concatenate([high, low, high], 1), table)
    for i in range(2):
        spread[i] = spectra[:, i * lanes:(i + 1) * lanes]
    out = p_ref.reshape(mode_rows * count, lanes)
    for first in range(0, count, 2):
        sides = []
        for c in (first, first + 1):
            pick = pl.ds(c, rows, stride=count)
            sides.append(jnp.concatenate([spread[i, pick, :] for i in range(2)], 0))
        high, low = split(jnp.concatenate(sides, 1))
        both = dot(kron, jnp.concatenate([high, low], 0))
        result = both[:mode_rows] + both[mode_rows:]
        for i in range(2):
            out[pl.ds(first + i, mode_rows, stride=count), :] = result[:, i * lanes:(i + 1) * lanes]


def from_modes(y_ref, table, kron, spread):
    mode_rows, count, lanes = y_ref.shape
    rows, pieces = spread.shape[1] // count, spread.shape[0]
    modes = y_ref.reshape(mode_rows * count, lanes)
    sides = []
    for first in range(0, count, 2):
        pair = [modes[pl.ds(c, mode_rows, stride=count), :] for c in (first, first + 1)]
        high, low = split(jnp.concatenate(pair, 1))
        both = dot(kron, jnp.concatenate([high, low, high], 0))
        for i in range(2):
            side = both[:, i * lanes:(i + 1) * lanes]
            sides.append(jnp.concatenate([side[:rows], side[rows:]], 1))
    high, low = split(jnp.concatenate(sides, 0))
    out = dot(jnp.concatenate([high, low, high], 1), table)
    for c in range(count):
        for i in range(pieces):
            spread[i, pl.ds(c, rows, stride=count), :] = out[c * rows:(c + 1) * rows, i * 128:(i + 1) * 128]
    return jnp.concatenate([spread[i] for i in range(pieces)], 1)


def gelu_parts(z):
    size = jnp.abs(z)
    gauss = jnp.exp(-0.5 * z * z)
    t = 1.0 / (1.0 + (0.3275911 / math.sqrt(2.0)) * size)
    poly = t * (0.254829592 + t * (-0.284496736 + t * (1.421413741 + t * (-1.453152027 + t * 1.061405429))))
    tail = 0.5 * poly * gauss
    phi = jnp.where(z >= 0, 1.0 - tail, tail)
    return z * phi, phi + z * (gauss * (1.0 / math.sqrt(2.0 * math.pi)))


def flat(ref):
    rows, count, width = ref.shape
    return ref[...].reshape(rows * count, width)


def put(ref, value):
    ref[...] = value.reshape(ref.shape)


def place_and_peers():
    section, z = lax.axis_index("section"), lax.axis_index("rows")
    return section, z, lax.axis_size("rows")


def greet(section, z, n, lines):
    barrier = pltpu.get_barrier_semaphore()
    pl.semaphore_signal(barrier, inc=1, device_id={"section": 1 - section}, device_id_type=MESH)
    if not lines:
        pl.semaphore_wait(barrier, 1)
        return

    @pl.when(z > 0)
    def _():
        pl.semaphore_signal(barrier, inc=1, device_id={"rows": z - 1}, device_id_type=MESH)

    @pl.when(z < n - 1)
    def _():
        pl.semaphore_signal(barrier, inc=1, device_id={"rows": z + 1}, device_id_type=MESH)

    pl.semaphore_wait(barrier, 1 + (z > 0).astype(jnp.int32) + (z < n - 1).astype(jnp.int32))


def to_core(src, dst, sems, section):
    return pltpu.make_async_remote_copy(src_ref=src, dst_ref=dst, send_sem=sems[0], recv_sem=sems[1],
                                        device_id={"section": 1 - section}, device_id_type=MESH)


class Gather:
    def __init__(self, section, z, n, y, full, load, cross, send, recv):
        self.section, self.z, self.n = section, z, n
        self.full, self.send, self.recv = full, send, recv
        self.chunks = full.shape[0]
        self.here = pltpu.make_async_copy(y.at[0], full.at[:, z, section], load)
        self.cross = to_core(y.at[1], full.at[:, z, section], (cross.at[0], cross.at[1]), section)

    def hop(self, way, q, hop, source):
        piece = self.full.at[q, source]
        target = self.z + 1 if way == 0 else self.z - 1
        return pltpu.make_async_remote_copy(
            src_ref=piece, dst_ref=piece, send_sem=self.send.at[way, q, hop], recv_sem=self.recv.at[way, q, hop],
            device_id={"rows": target}, device_id_type=MESH)

    def sends(self, way):
        return self.z < self.n - 1 if way == 0 else self.z > 0

    def source(self, way, hop):
        return self.z - hop if way == 0 else self.z + hop

    def known(self, way, hop):
        at = self.source(way, hop)
        return at >= 0 if way == 0 else at < self.n

    def begin(self):
        self.here.start()
        self.cross.start()

    def launch(self):
        self.here.wait()
        self.cross.wait_recv()
        for q in range(self.chunks):
            for way in range(2):
                @pl.when(self.sends(way))
                def _():
                    self.hop(way, q, 0, self.z).start()

    def step(self, q, hop):
        for way in range(2):
            source = self.source(way, hop + 1)

            @pl.when(self.known(way, hop + 1))
            def _():
                self.hop(way, q, hop, source).wait_recv()

                @pl.when(self.sends(way))
                def _():
                    self.hop(way, q, hop + 1, source).start()

    def prologue(self):
        for tick in range(self.n - 2):
            for hop in range(tick + 1):
                if tick - hop < self.chunks:
                    self.step(tick - hop, hop)

    def complete(self, q):
        for hop in range(self.n - 1):
            at = q + self.n - 2 - hop

            @pl.when(at < self.chunks)
            def _():
                self.step(at, hop)

    def finish(self):
        self.cross.wait_send()

        def body(q, carry):
            for way in range(2):
                for hop in range(self.n - 1):
                    @pl.when(jnp.logical_and(self.sends(way), self.known(way, hop)))
                    def _():
                        self.hop(way, q, hop, self.source(way, hop)).wait_send()
            return carry

        lax.fori_loop(0, self.chunks, body, 0)


def fetch(src, dst, sem, parts=4):
    step = dst.shape[0] // parts
    for i in range(parts):
        pltpu.make_async_copy(src.at[pl.ds(i * step, step)], dst.at[pl.ds(i * step, step)], sem).start()


def arrived(dst, sem):
    pltpu.make_async_copy(dst, dst, sem).wait()


def conv_rows(weight, bias, a, out):
    rows, channels, width = a.shape
    block = weight.shape[0] // channels

    def body(i, carry):
        at = pl.ds(i * block, block)
        high, low = split(a[at].reshape(block * channels, width))
        result = dot(weight[...], jnp.concatenate([high, high, low], 0)).reshape(block, channels, width)
        out[at] = result + bias[...][None] if bias is not None else out[at] + result
        return carry

    lax.fori_loop(0, rows // block, body, 0)


def grad_rows(a, gz, cg_ref, bg_ref):
    rows, channels, width = a.shape

    def body(r, carry):
        grad, bias = carry
        g = gz[r]
        left = jnp.concatenate(split(a[r]), 0)
        right = jnp.concatenate(split(g), 0)
        return grad + dot(left, right, (((1,), (1,)), ((), ()))), bias + g

    grad, bias = lax.fori_loop(0, rows, body, (jnp.zeros((2 * channels, 2 * channels), F32),
                                               jnp.zeros((channels, width), F32)))
    cg_ref[...] = grad
    bg_ref[...] = bias


def chunk_of(ref, q, count):
    rows, _, width = ref.shape
    return ref[:, pl.ds(pl.multiple_of(q * count, count), count), :].reshape(rows * count, width)


def chunk_at(ref, q, count):
    return ref.at[:, pl.ds(pl.multiple_of(q * count, count), count), :]


class Modes:
    def __init__(self, section, buffer, p_out, local, cross):
        self.section, self.buffer, self.p_out, self.local, self.cross = section, buffer, p_out, local, cross

    def view(self, q):
        n, halves, kx, count, lanes = self.buffer.shape[1:]
        return self.buffer.at[q].reshape(n * halves * kx, count, lanes)

    def copies(self, q):
        s = self.section
        return (pltpu.make_async_copy(self.buffer.at[q, :, s], self.p_out.at[:, 0, q], self.local.at[q]),
                to_core(self.buffer.at[q, :, 1 - s], self.p_out.at[:, 1, q],
                        (self.cross.at[0, q], self.cross.at[1, q]), s))

    def start(self, q):
        for copy in self.copies(q):
            copy.start()

    def wait(self, q):
        for copy in self.copies(q):
            copy.wait()


class Bound:
    def __init__(self, section, owner, micro, other, source, bound, local, cross):
        self.section, self.owner, self.micro, self.other = section, owner, micro, other
        self.source, self.bound, self.local, self.cross = source, bound, local, cross

    def copies(self, q, count, micro):
        src, dst = chunk_at(self.source, q, count), chunk_at(self.bound.at[micro], q, count)
        return (pltpu.make_async_copy(src, dst, self.local.at[q]),
                to_core(src, dst, (self.cross.at[0, q], self.cross.at[1, q]), self.section))

    def start(self, q, count):
        here, there = self.copies(q, count, self.micro)

        @pl.when(self.section == self.owner)
        def _():
            here.start()

        @pl.when(self.section != self.owner)
        def _():
            there.start()

    def wait(self, q, count):
        here, there = self.copies(q, count, self.micro)
        come = self.copies(q, count, self.other)[1]

        @pl.when(self.section == self.owner)
        def _():
            here.wait()
            come.wait_recv()

        @pl.when(self.section != self.owner)
        def _():
            there.wait_send()


def add_squares(value, total):
    rows, _, width = total.shape
    square = (value * value).reshape(rows, -1, width)
    for at in range(0, square.shape[1], G):
        total[...] += square[:, at:at + G]


def region_sums(rid_ref, eo, eb, stat_ref):
    rows, _, width = eo.shape
    rid = rid_ref[...]
    energies = (jnp.sum(eo[...], axis=1), jnp.sum(eb[...], axis=1), jnp.ones((rows, width), F32))
    for kind in range(3):
        for region in range(R):
            line = jnp.sum(jnp.where(rid == region + 1, energies[kind], 0.0), axis=0, keepdims=True)
            total = line[:, :128]
            for piece in range(1, width // 128):
                total = total + line[:, piece * 128:(piece + 1) * 128]
            stat_ref[kind, region:region + 1, :] = total


def head_kernel(per_core, count, a_in, w_in, table, kron, p0, p1, far, a_buf, w_buf, p_buf, spread,
                a_sem, w_sem, w_cross, p_local, p_cross):
    section, z, n = place_and_peers()
    p_outs = (p0, p1)
    chunks, half = p_buf.shape[1], far.shape[0]
    blocks = [(j, q) for j in range(per_core) for q in range(chunks)]

    def field(k):
        j, q = blocks[k]
        src = chunk_at(a_in.at[section * per_core + j, 0], q, count)
        return pltpu.make_async_copy(src, a_buf.at[k % 2], a_sem.at[k % 2])

    def weight_in(x):
        return pltpu.make_async_copy(w_in.at[0, (1 - section) * half + x], w_buf.at[x % 2], w_sem.at[x % 2])

    def weight_out(x):
        return to_core(w_buf.at[x % 2], far.at[x], (w_cross.at[0, x], w_cross.at[1, x]), section)

    field(0).start()
    weight_in(0).start()
    if half > 1:
        weight_in(1).start()
    greet(section, z, n, False)
    for k, (j, q) in enumerate(blocks):
        if k + 1 < len(blocks):
            field(k + 1).start()
        if k < half:
            weight_in(k).wait()
            weight_out(k).start()
        field(k).wait()
        modes = Modes(section, p_buf.at[j], p_outs[j], p_local.at[j], p_cross.at[j])
        to_modes(flat(a_buf.at[k % 2]), table[...], kron[...], spread, modes.view(q))
        modes.start(q)
        if k + 2 < half:
            weight_out(k).wait_send()
            weight_in(k + 2).start()
    for x in range(half):
        if x + 2 >= half:
            weight_out(x).wait_send()
        weight_out(x).wait_recv()
    for j, q in blocks:
        Modes(section, p_buf.at[j], p_outs[j], p_local.at[j], p_cross.at[j]).wait(q)


def middle_kernel(j, per_core, y, a_in, rid_in, itable, ikron, table, kron, weight, bias,
                  p_out, o_out, dg_out, stat_ref,
                  full, p_buf, spread, a, z_buf, rid, eo, eb,
                  load, cross, send, recv, p_local, p_cross, a_sem, rid_sem, out_sem):
    section, z, n = place_and_peers()
    micro = section * per_core + j
    fetch(a_in.at[micro, 0], a, a_sem)
    rid_copy = pltpu.make_async_copy(rid_in.at[micro, 0], rid, rid_sem)
    rid_copy.start()
    greet(section, z, n, True)
    gather = Gather(section, z, n, y, full, load, cross, send, recv)
    gather.begin()
    gather.launch()
    eo[...] = jnp.zeros_like(eo)
    eb[...] = jnp.zeros_like(eb)
    arrived(a, a_sem)
    conv_rows(weight, bias, a, z_buf)
    gather.prologue()
    modes = Modes(section, p_buf, p_out, p_local, p_cross)
    chunks, count = full.shape[0], full.shape[4]

    def outs(q):
        return (pltpu.make_async_copy(chunk_at(a, q, count), chunk_at(o_out, q, count), out_sem.at[0, q]),
                pltpu.make_async_copy(chunk_at(z_buf, q, count), chunk_at(dg_out, q, count), out_sem.at[1, q]))

    def body(q, carry):
        gather.complete(q)
        pre = from_modes(full.at[q].reshape(-1, count, full.shape[5]), itable[...], ikron[...], spread)
        branch, slope = gelu_parts(pre + chunk_of(z_buf, q, count))
        put(chunk_at(z_buf, q, count), slope)
        add_squares(branch, eb)
        out = chunk_of(a, q, count) + branch
        put(chunk_at(a, q, count), out)
        add_squares(out, eo)
        for copy in outs(q):
            copy.start()
        to_modes(chunk_of(a, q, count), table[...], kron[...], spread, modes.view(q))
        modes.start(q)
        return carry

    lax.fori_loop(0, chunks, body, 0)
    rid_copy.wait()
    region_sums(rid, eo, eb, stat_ref)

    def close(q, carry):
        for copy in outs(q):
            copy.wait()
        modes.wait(q)
        return carry

    lax.fori_loop(0, chunks, close, 0)
    gather.finish()


def turn_kernel(j, per_core, aliased, y, a_in, cot_in, rid_in, itable, ikron, table, kron, weight, bias, *refs):
    refs = refs[1:] if aliased else refs
    (p_out, bound, gz_out, stat_ref, full, p_buf, spread, a, z_buf, cot, rid, eo, eb,
     load, cross, send, recv, p_local, p_cross, a_sem, c_sem, rid_sem, out_sem, b_local, b_cross) = refs
    section, z, n = place_and_peers()
    micro = section * per_core + j
    fetch(a_in, a, a_sem)
    fetch(cot_in.at[micro, 0], cot, c_sem)
    rid_copy = pltpu.make_async_copy(rid_in.at[micro, 0], rid, rid_sem)
    rid_copy.start()
    greet(section, z, n, True)
    gather = Gather(section, z, n, y, full, load, cross, send, recv)
    gather.begin()
    gather.launch()
    eo[...] = jnp.zeros_like(eo)
    eb[...] = jnp.zeros_like(eb)
    arrived(a, a_sem)
    conv_rows(weight, bias, a, z_buf)
    arrived(cot, c_sem)
    gather.prologue()
    modes = Modes(section, p_buf, p_out, p_local, p_cross)
    result = Bound(section, 1, micro, (1 - section) * per_core + j, a, bound, b_local, b_cross)
    chunks, count = full.shape[0], full.shape[4]

    def gz_copy(q):
        return pltpu.make_async_copy(chunk_at(cot, q, count), chunk_at(gz_out, q, count), out_sem.at[q])

    def body(q, carry):
        gather.complete(q)
        pre = from_modes(full.at[q].reshape(-1, count, full.shape[5]), itable[...], ikron[...], spread)
        branch, slope = gelu_parts(pre + chunk_of(z_buf, q, count))
        put(chunk_at(cot, q, count), chunk_of(cot, q, count) * slope)
        gz_copy(q).start()
        add_squares(branch, eb)
        out = chunk_of(a, q, count) + branch
        put(chunk_at(a, q, count), out)
        result.start(q, count)
        add_squares(out, eo)
        to_modes(chunk_of(cot, q, count), table[...], kron[...], spread, modes.view(q))
        modes.start(q)
        return carry

    lax.fori_loop(0, chunks, body, 0)
    rid_copy.wait()
    region_sums(rid, eo, eb, stat_ref)

    def close(q, carry):
        gz_copy(q).wait()
        result.wait(q, count)
        modes.wait(q)
        return carry

    lax.fori_loop(0, chunks, close, 0)
    gather.finish()


def back_kernel(j, per_core, y, gz_in, a_in, g_in, dg_in, itable, ikron, table, kron, weight,
                p_out, ga_out, gz_out, cg_ref, bg_ref,
                full, p_buf, spread, gz, a, h, dg,
                load, cross, send, recv, p_local, p_cross, gz_sem, a_sem, h_sem, dg_sem, out_sem):
    section, z, n = place_and_peers()
    micro = section * per_core + j
    fetch(gz_in, gz, gz_sem)
    fetch(g_in.at[micro, 0], h, h_sem)
    fetch(a_in, a, a_sem)
    fetch(dg_in, dg, dg_sem)
    greet(section, z, n, True)
    gather = Gather(section, z, n, y, full, load, cross, send, recv)
    gather.begin()
    gather.launch()
    arrived(gz, gz_sem)
    arrived(h, h_sem)
    conv_rows(weight, None, gz, h)
    arrived(a, a_sem)
    gather.prologue()
    grad_rows(a, gz, cg_ref, bg_ref)
    arrived(dg, dg_sem)
    modes = Modes(section, p_buf, p_out, p_local, p_cross)
    chunks, count = full.shape[0], full.shape[4]

    def outs(q):
        return (pltpu.make_async_copy(chunk_at(h, q, count), chunk_at(ga_out, q, count), out_sem.at[0, q]),
                pltpu.make_async_copy(chunk_at(dg, q, count), chunk_at(gz_out, q, count), out_sem.at[1, q]))

    def body(q, carry):
        gather.complete(q)
        pre = from_modes(full.at[q].reshape(-1, count, full.shape[5]), itable[...], ikron[...], spread)
        ga = pre + chunk_of(h, q, count)
        put(chunk_at(h, q, count), ga)
        put(chunk_at(dg, q, count), ga * chunk_of(dg, q, count))
        for copy in outs(q):
            copy.start()
        to_modes(chunk_of(dg, q, count), table[...], kron[...], spread, modes.view(q))
        modes.start(q)
        return carry

    lax.fori_loop(0, chunks, body, 0)

    def close(q, carry):
        for copy in outs(q):
            copy.wait()
        modes.wait(q)
        return carry

    lax.fori_loop(0, chunks, close, 0)
    gather.finish()


def tail_kernel(j, per_core, y, gz_in, a_in, g_in, itable, ikron, weight, bound_in,
                bound, cg_ref, bg_ref, full, spread, gz, a, h,
                load, cross, send, recv, gz_sem, a_sem, h_sem, b_local, b_cross):
    section, z, n = place_and_peers()
    micro = section * per_core + j
    fetch(gz_in, gz, gz_sem)
    fetch(g_in, h, h_sem)
    fetch(a_in.at[micro, 0], a, a_sem)
    greet(section, z, n, True)
    gather = Gather(section, z, n, y, full, load, cross, send, recv)
    gather.begin()
    gather.launch()
    arrived(gz, gz_sem)
    arrived(h, h_sem)
    conv_rows(weight, None, gz, h)
    arrived(a, a_sem)
    gather.prologue()
    grad_rows(a, gz, cg_ref, bg_ref)
    result = Bound(section, 0, micro, (1 - section) * per_core + j, h, bound, b_local, b_cross)
    chunks, count = full.shape[0], full.shape[4]

    def body(q, carry):
        gather.complete(q)
        pre = from_modes(full.at[q].reshape(-1, count, full.shape[5]), itable[...], ikron[...], spread)
        put(chunk_at(h, q, count), pre + chunk_of(h, q, count))
        result.start(q, count)
        return carry

    lax.fori_loop(0, chunks, body, 0)

    def close(q, carry):
        result.wait(q, count)
        return carry

    lax.fori_loop(0, chunks, close, 0)
    gather.finish()


def swap_halves(value):
    return pltpu.roll(value, value.shape[-1] // 2, value.ndim - 1)


def left_lanes(shape):
    return lax.broadcasted_iota(jnp.int32, shape, len(shape) - 1) < shape[-1] // 2


SLOTS = 4


def weight_stream(own, base, local_ref, far_ref, wbuf, sem):
    step, count = pl.program_id(0), pl.num_programs(0)

    def begin(at):
        slot = lax.rem(at, SLOTS)

        @pl.when(own)
        def _():
            fetch(local_ref.at[0, base + at], wbuf.at[slot], sem.at[slot])

        @pl.when(jnp.logical_not(own))
        def _():
            fetch(far_ref.at[at], wbuf.at[slot], sem.at[slot])

    @pl.when(step == 0)
    def _():
        for at in range(SLOTS - 1):
            @pl.when(at < count)
            def _():
                begin(at)

    @pl.when(step + SLOTS - 1 < count)
    def _():
        begin(step + SLOTS - 1)

    slot = lax.rem(step, SLOTS)
    arrived(wbuf.at[slot], sem.at[slot])
    return wbuf.at[slot]


def pieces(array):
    return [array[at:at + G] for at in range(0, array.shape[0], G)]


def spread_row(tile, row):
    return jnp.broadcast_to(tile[row:row + 1], tile.shape)


def mix_kernel(m_ref, f_ref, local_ref, far_ref, y_ref, wbuf, f1, f2, sem):
    weight = weight_stream(m_ref[0] == 1, m_ref[1], local_ref, far_ref, wbuf, sem)
    grids, channels, lanes = f1.shape
    f1[...] = f_ref[...].reshape(f1.shape)
    f2[...] = swap_halves(f1[...])
    groups = channels // G

    def body(block, acc):
        at = pl.multiple_of(block * G, G)
        acc = list(acc)
        tiles = [f[g, pl.ds(at, G), :] for g in range(grids) for f in (f1, f2)]
        for u in range(G):
            rows = [spread_row(tile, u) for tile in tiles]
            for o in range(groups):
                w = weight[at + u, o * G:(o + 1) * G, :]
                for k, row in enumerate(rows):
                    acc[k * groups + o] = acc[k * groups + o] + row * w
        return tuple(acc)

    acc = lax.fori_loop(0, groups, body, tuple(jnp.zeros((G, lanes), F32) for _ in range(2 * grids * groups)))
    left = left_lanes((channels, lanes))
    for g in range(grids):
        a, b = [jnp.concatenate(acc[k * groups:(k + 1) * groups], 0) for k in (2 * g, 2 * g + 1)]
        y_ref[g] = jnp.where(left, a - swap_halves(a), b + swap_halves(b)).reshape(y_ref.shape[1:])


def mix_t_kernel(m_ref, d_ref, local_ref, far_ref, y_ref, wbuf, a1, a2, sem):
    weight = weight_stream(m_ref[0] == 1, m_ref[1], local_ref, far_ref, wbuf, sem)
    grids, channels, lanes = a1.shape
    d = d_ref[...].reshape(a1.shape)
    d1 = [pieces(d[g]) for g in range(grids)]
    d2 = [pieces(swap_halves(d[g])) for g in range(grids)]
    groups = channels // G

    def body(block, carry):
        at = pl.multiple_of(block * G, G)
        rows = [[] for _ in range(2 * grids)]
        for u in range(G):
            total = [None] * (2 * grids)
            for o in range(groups):
                w = weight[at + u, o * G:(o + 1) * G, :]
                for g in range(grids):
                    for side, source in enumerate((d1, d2)):
                        term = w * source[g][o]
                        k = 2 * g + side
                        total[k] = term if total[k] is None else total[k] + term
            for k in range(2 * grids):
                rows[k].append(jnp.sum(total[k], axis=0, keepdims=True))
        for g in range(grids):
            a1[g, pl.ds(at, G), :] = jnp.concatenate(rows[2 * g], 0)
            a2[g, pl.ds(at, G), :] = jnp.concatenate(rows[2 * g + 1], 0)
        return carry

    lax.fori_loop(0, groups, body, 0)
    left = left_lanes((channels, lanes))
    for g in range(grids):
        a, b = a1[g], a2[g]
        y_ref[g] = jnp.where(left, a + swap_halves(a), swap_halves(b) - b).reshape(y_ref.shape[1:])


def grad_tables(f_ref, d_ref, fa, fb, d1, d2):
    f = f_ref[...].reshape(fa.shape)
    other = swap_halves(f)
    left = left_lanes(f.shape)
    fa[...] = jnp.where(left, f, other)
    fb[...] = jnp.where(left, other, -f)
    d1[...] = d_ref[...].reshape(d1.shape)
    d2[...] = swap_halves(d1[...])


def grad_block(first_row, fa, fb, d1, d2, out):
    count, channels, lanes = fa.shape
    groups = channels // G
    wide = 4

    def body(octet, carry):
        at = pl.multiple_of(octet * G, G)
        rows = pl.ds(pl.multiple_of(first_row + at, G), G)
        for first in range(0, G, wide):
            acc = [[None] * groups for _ in range(wide)]
            for g in range(count):
                ta, tb = fa[g, rows, :], fb[g, rows, :]
                pairs = [(spread_row(ta, first + u), spread_row(tb, first + u)) for u in range(wide)]
                for o in range(groups):
                    x, y = d1[g, o * G:(o + 1) * G, :], d2[g, o * G:(o + 1) * G, :]
                    for u in range(wide):
                        term = pairs[u][0] * x + pairs[u][1] * y
                        acc[u][o] = term if acc[u][o] is None else acc[u][o] + term
            for u in range(wide):
                for o in range(groups):
                    out[at + first + u, o * G:(o + 1) * G, :] = acc[u][o]
        return carry

    lax.fori_loop(0, out.shape[0] // G, body, 0)


def far_grad_kernel(f0, f1, g0, g1, far, fbuf, gbuf, out, fa, fb, d1, d2, in_sem, send, recv):
    section, z, n = place_and_peers()
    half, channels = far.shape[0], far.shape[1]
    block = out.shape[1]
    blocks = channels // block

    def load(x, slot):
        @pl.when(section == 0)
        def _():
            pltpu.make_async_copy(f1.at[:, :, x], fbuf.at[slot], in_sem.at[0, slot]).start()
            pltpu.make_async_copy(g1.at[:, :, x], gbuf.at[slot], in_sem.at[1, slot]).start()

        @pl.when(section != 0)
        def _():
            pltpu.make_async_copy(f0.at[:, :, x], fbuf.at[slot], in_sem.at[0, slot]).start()
            pltpu.make_async_copy(g0.at[:, :, x], gbuf.at[slot], in_sem.at[1, slot]).start()

    def move(k, slot):
        x, i = k // blocks, k % blocks
        return to_core(out.at[slot], far.at[x, pl.ds(i * block, block)], (send.at[k], recv.at[k]), section)

    load(0, 0)
    greet(section, z, n, False)

    def body(x, carry):
        slot = lax.rem(x, 2)

        @pl.when(x + 1 < half)
        def _():
            load(x + 1, 1 - slot)

        pltpu.make_async_copy(fbuf.at[slot], fbuf.at[slot], in_sem.at[0, slot]).wait()
        pltpu.make_async_copy(gbuf.at[slot], gbuf.at[slot], in_sem.at[1, slot]).wait()
        grad_tables(fbuf.at[slot], gbuf.at[slot], fa, fb, d1, d2)

        def inner(i, carry):
            k = x * blocks + i

            @pl.when(k >= 2)
            def _():
                move(k - 2, lax.rem(k, 2)).wait_send()

            grad_block(i * block, fa, fb, d1, d2, out.at[lax.rem(k, 2)])
            move(k, lax.rem(k, 2)).start()
            return carry

        return lax.fori_loop(0, blocks, inner, carry)

    lax.fori_loop(0, half, body, 0)
    total = half * blocks
    for k in (total - 2, total - 1):
        move(k, k % 2).wait_send()

    def close(k, carry):
        move(k, 0).wait_recv()
        return carry

    lax.fori_loop(0, total, close, 0)


def own_grad_kernel(m_ref, f0, f1, g0, g1, far_ref, w_ref, fa, fb, d1, d2, fbuf, gbuf, in_sem):
    x, i, kind = pl.program_id(0), pl.program_id(1), pl.program_id(2)
    half, block = pl.num_programs(0), w_ref.shape[0]
    first = m_ref[0] == 0

    def load(at, slot):
        @pl.when(first)
        def _():
            pltpu.make_async_copy(f0.at[:, :, at], fbuf.at[slot], in_sem.at[0, slot]).start()
            pltpu.make_async_copy(g0.at[:, :, at], gbuf.at[slot], in_sem.at[1, slot]).start()

        @pl.when(jnp.logical_not(first))
        def _():
            pltpu.make_async_copy(f1.at[:, :, at], fbuf.at[slot], in_sem.at[0, slot]).start()
            pltpu.make_async_copy(g1.at[:, :, at], gbuf.at[slot], in_sem.at[1, slot]).start()

    @pl.when(jnp.logical_and(i == 0, kind == 0))
    def _():
        slot = lax.rem(x, 2)

        @pl.when(x == 0)
        def _():
            load(0, 0)

        @pl.when(x + 1 < half)
        def _():
            load(x + 1, 1 - slot)

        pltpu.make_async_copy(fbuf.at[slot], fbuf.at[slot], in_sem.at[0, slot]).wait()
        pltpu.make_async_copy(gbuf.at[slot], gbuf.at[slot], in_sem.at[1, slot]).wait()
        grad_tables(fbuf.at[slot], gbuf.at[slot], fa, fb, d1, d2)

    @pl.when(kind == 0)
    def _():
        grad_block(i * block, fa, fb, d1, d2, w_ref)

    @pl.when(kind == 1)
    def _():
        w_ref[...] = far_ref[...]


def whole(array):
    return pl.BlockSpec(array.shape, lambda *_: (0,) * array.ndim)


def params(**kw):
    return pltpu.CompilerParams(vmem_limit_bytes=VMEM_LIMIT, **kw)


def local(inputs, cotangent, region_id, spectral_w, conv_w, bias_vector):
    micro_count, _, rows_dev, channels, width = inputs.shape
    lanes = spectral_w.shape[-1]
    half = lanes // 2
    kx_dev = spectral_w.shape[1]
    row_devices, sections = lax.axis_size("rows"), lax.axis_size("section")
    mode_rows, height = kx_dev * row_devices, rows_dev * row_devices
    section = lax.axis_index("section")
    per_core = micro_count // sections
    kx_half = kx_dev // sections

    plain, doubled = col_tables(width, half)

    def stacked(array):
        high, low = np_split(array)
        return np.concatenate([high, high, low], 0)

    t_plain, t_doubled, it_plain, it_doubled = [stacked(t) for t in (plain, doubled, plain.T, doubled.T)]
    kron, ikron = row_tables(height, mode_rows, lax.axis_index("rows") * rows_dev, rows_dev)

    count = 2 * G
    chunks = channels // count
    hbm, vmem = pl.BlockSpec(memory_space=pl.ANY), pl.BlockSpec(memory_space=pltpu.VMEM)
    field_shape = jax.ShapeDtypeStruct((rows_dev, channels, width), F32)
    p_shape = jax.ShapeDtypeStruct((row_devices, sections, chunks, kx_half, count, lanes), F32)
    pair_shape = jax.ShapeDtypeStruct(p_shape.shape[1:], F32)
    stat_shape = jax.ShapeDtypeStruct((3, R, 128), F32)
    cg_shape = jax.ShapeDtypeStruct((2 * channels, 2 * channels), F32)
    bg_shape = jax.ShapeDtypeStruct((channels, width), F32)
    bound_shape = jax.ShapeDtypeStruct((micro_count, rows_dev, channels, width), F32)
    dma = pltpu.SemaphoreType.DMA
    field_buf = pltpu.VMEM((rows_dev, channels, width), F32)
    full_buf = pltpu.VMEM((chunks, row_devices, sections, kx_half, count, lanes), F32)
    spread = pltpu.VMEM((width // 128, rows_dev * count, 128), F32)
    energy = pltpu.VMEM((rows_dev, G, width), F32)
    rid_buf = pltpu.VMEM((rows_dev, width), jnp.int32)
    gather_sems = [dma, dma((2,)), dma((2, chunks, row_devices)), dma((2, chunks, row_devices))]
    modes_sems = [dma((chunks,)), dma((2, chunks))]

    def call(body, ident, args, specs, out_shape, out_specs, scratch, cost=40, aliases=None):
        return pl.pallas_call(
            body, in_specs=specs, out_specs=out_specs, out_shape=out_shape, scratch_shapes=scratch,
            input_output_aliases=aliases or {},
            cost_estimate=pl.CostEstimate(flops=0, bytes_accessed=cost * 3_000_000, transcendentals=0),
            compiler_params=params(collective_id=ident, has_side_effects=True))(*args)

    conv_rows_at_once = 256 // channels
    conv_both = lax.all_gather(conv_w, "section", axis=0, tiled=True)
    bias_both = lax.all_gather(bias_vector, "section", axis=0, tiled=True)

    def conv_parts(matrix):
        wide = jnp.kron(jnp.eye(conv_rows_at_once, dtype=F32), matrix)
        rounded = lax.reduce_precision(wide, 8, 7)
        high, low = rounded.astype(BF16), (wide - rounded).astype(BF16)
        return jnp.concatenate([high, low, high], 1)

    conv_fwd = [conv_parts(conv_both[l].T) for l in range(2)]
    conv_bwd = [conv_parts(conv_both[l]) for l in range(2)]
    bias_wide = [jnp.broadcast_to(bias_both[l][:, None], (channels, width)) for l in range(2)]

    def reduce_modes(partial_modes):
        return lax.psum_scatter(partial_modes, "rows", scatter_dimension=0, tiled=False)

    def mixing(body, layer, pair):
        flag = jnp.stack([(section == layer).astype(jnp.int32), section * kx_half])
        block = pl.BlockSpec((sections, chunks, None, count, lanes), lambda x, m: (0, 0, x, 0, 0))
        small = pltpu.VMEM((sections, channels, lanes), F32)
        grid_spec = pltpu.PrefetchScalarGridSpec(
            num_scalar_prefetch=1, grid=(kx_half,), in_specs=[block, hbm, hbm], out_specs=block,
            scratch_shapes=[pltpu.VMEM((SLOTS, channels, channels, lanes), F32), small, small, dma((SLOTS,))])
        return pl.pallas_call(
            body, grid_spec=grid_spec, out_shape=pair_shape, compiler_params=params(),
            cost_estimate=pl.CostEstimate(flops=0, bytes_accessed=25_000_000, transcendentals=0))(
                flag, pair, spectral_w, far_weights)

    def gather_batch(pairs):
        joined = jnp.concatenate(pairs, 0)
        return lax.all_gather(joined, "batch", axis=0, tiled=True)

    streams = range(per_core)

    whole_p = pltpu.VMEM((per_core,) + full_buf.shape, F32)
    *partials, far_weights = call(
        functools.partial(head_kernel, per_core, count), 0, [inputs, spectral_w, t_plain, kron],
        [hbm, hbm, vmem, vmem], [p_shape] * per_core + [jax.ShapeDtypeStruct((kx_half,) + spectral_w.shape[2:], F32)],
        [hbm] * (per_core + 1),
        [pltpu.VMEM((2, rows_dev, count, width), F32), pltpu.VMEM((2,) + spectral_w.shape[2:], F32), whole_p, spread,
         dma((2,)), dma((2,)), dma((2, kx_half)), dma((per_core, chunks)), dma((per_core, 2, chunks))])
    f0 = [reduce_modes(p) for p in partials]
    y0 = [mixing(mix_kernel, 0, f) for f in f0]
    a1, dg0, partials, stats0 = [None] * per_core, [None] * per_core, [None] * per_core, [None] * per_core
    f1, y1 = [None] * per_core, [None] * per_core
    for j in streams:
        partials[j], a1[j], dg0[j], stats0[j] = call(
            functools.partial(middle_kernel, j, per_core), 1 + j,
            [y0[j], inputs, region_id, it_doubled, ikron, t_plain, kron, conv_fwd[0], bias_wide[0]],
            [hbm] * 3 + [vmem] * 6, [p_shape, field_shape, field_shape, stat_shape], [hbm, hbm, hbm, vmem],
            [full_buf, full_buf, spread, field_buf, field_buf, rid_buf, energy, energy]
            + gather_sems + modes_sems + [dma, dma, dma((2, chunks))])
        f1[j] = reduce_modes(partials[j])
    y1 = [mixing(mix_kernel, 1, f) for f in f1]
    gz1, stats1, d1 = [None] * per_core, [None] * per_core, [None] * per_core
    bound = None
    for j in streams:
        aliased = bound is not None
        partials[j], bound, gz1[j], stats1[j] = call(
            functools.partial(turn_kernel, j, per_core, aliased), 3 + j,
            [y1[j], a1[j], cotangent, region_id, it_doubled, ikron, t_doubled, kron, conv_fwd[1], bias_wide[1]]
            + [bound] * aliased,
            [hbm] * 4 + [vmem] * 6 + [hbm] * aliased, [p_shape, bound_shape, field_shape, stat_shape],
            [hbm, hbm, hbm, vmem],
            [full_buf, full_buf, spread, field_buf, field_buf, field_buf, rid_buf, energy, energy]
            + gather_sems + modes_sems + [dma, dma, dma, dma((chunks,)), dma((chunks,)), dma((2, chunks))],
            aliases={10: 1} if aliased else None)
        d1[j] = reduce_modes(partials[j])
    e1 = [mixing(mix_t_kernel, 1, d) for d in d1]
    ga1, gz0, cg1, bg1, d0 = [[None] * per_core for _ in range(5)]
    for j in streams:
        partials[j], ga1[j], gz0[j], cg1[j], bg1[j] = call(
            functools.partial(back_kernel, j, per_core), 5 + j,
            [e1[j], gz1[j], a1[j], cotangent, dg0[j], it_plain, ikron, t_doubled, kron, conv_bwd[1]],
            [hbm] * 5 + [vmem] * 5, [p_shape, field_shape, field_shape, cg_shape, bg_shape],
            [hbm, hbm, hbm, vmem, vmem],
            [full_buf, full_buf, spread] + [field_buf] * 4 + gather_sems + modes_sems
            + [dma, dma, dma, dma, dma((2, chunks))])
        d0[j] = reduce_modes(partials[j])
    e0 = [mixing(mix_t_kernel, 0, d) for d in d0]
    cg0, bg0 = [None] * per_core, [None] * per_core
    for j in streams:
        bound, cg0[j], bg0[j] = call(
            functools.partial(tail_kernel, j, per_core), 7 + j,
            [e0[j], gz0[j], inputs, ga1[j], it_plain, ikron, conv_bwd[0], bound],
            [hbm] * 4 + [vmem] * 3 + [hbm], [bound_shape, cg_shape, bg_shape], [hbm, vmem, vmem],
            [full_buf, spread] + [field_buf] * 3 + gather_sems
            + [dma, dma, dma, dma((chunks,)), dma((2, chunks))], aliases={7: 0})

    f_all, d_all = [gather_batch(f) for f in (f0, f1)], [gather_batch(d) for d in (d0, d1)]
    grids = f_all[0].shape[0]
    block = 16
    blocks = channels // block
    in_buf = pltpu.VMEM((2, grids, chunks, count, lanes), F32)
    big = pltpu.VMEM((grids, channels, lanes), F32)
    far_shape = jax.ShapeDtypeStruct((kx_half, channels, channels, lanes), F32)
    far_grad = call(far_grad_kernel, 9, [*f_all, *d_all], [hbm] * 4, far_shape, hbm,
                    [in_buf, in_buf, pltpu.VMEM((2, block, channels, lanes), F32), big, big, big, big,
                     dma((2, 2)), dma((kx_half * blocks,)), dma((kx_half * blocks,))])
    grid_spec = pltpu.PrefetchScalarGridSpec(
        num_scalar_prefetch=1, grid=(kx_half, blocks, 2),
        in_specs=[hbm] * 4 + [pl.BlockSpec((None, block, channels, lanes), lambda x, i, k, m: (x, i, 0, 0))],
        out_specs=pl.BlockSpec(
            (None, block, channels, lanes),
            lambda x, i, k, m: (jnp.where(k == 0, m[0], 1 - m[0]) * kx_half + x, i, 0, 0)),
        scratch_shapes=[big, big, big, big, in_buf, in_buf, dma((2, 2))])
    spectral_grad = pl.pallas_call(
        own_grad_kernel, grid_spec=grid_spec, out_shape=jax.ShapeDtypeStruct(spectral_w.shape[1:], F32),
        cost_estimate=pl.CostEstimate(flops=0, bytes_accessed=100_000_000, transcendentals=0),
        compiler_params=params())(jnp.reshape(section, (1,)).astype(jnp.int32), *f_all, *d_all, far_grad)[None]

    def lower(value):
        return (value[:channels, :channels] + value[channels:, channels:]
                + value[:channels, channels:] + value[channels:, :channels])

    conv_local = jnp.stack([lower(sum(cg0)), lower(sum(cg1))])
    bias_local = jnp.stack([jnp.sum(sum(bg0), -1), jnp.sum(sum(bg1), -1)])
    stat_local = jnp.stack([jnp.sum(sum(stats0), -1), jnp.sum(sum(stats1), -1)])
    conv_sum, bias_sum, stat_sum = lax.psum((conv_local, bias_local, stat_local), ("section", "batch", "rows"))
    own_stat = lax.dynamic_index_in_dim(stat_sum, section, 0, False)
    layer_rms = jnp.sqrt(own_stat[:2] / (channels * own_stat[2])[None, :] + 1e-06)[None]
    own = lambda value: lax.dynamic_slice_in_dim(value, section, 1, 0)
    return bound[None, :, None], spectral_grad, own(conv_sum), own(bias_sum), layer_rms


def solution(mesh):
    placed = (
        P(None, "batch", "rows", None, None),
        P(None, "batch", "rows", None, None),
        P(None, "batch", "rows", None),
        P("section", "rows", None, None, None),
        P("section", None, None),
        P("section", None),
    )
    return jax.shard_map(
        local,
        mesh=mesh,
        in_specs=placed,
        out_specs=(
            P("section", None, "batch", "rows", None, None),
            P("section", "rows", None, None, None),
            P("section", None, None),
            P("section", None),
            P("section", None, None),
        ),
        check_vma=False,
    )
```

```python
import functools
import math
import types

import jax
import jax.numpy as jnp
import numpy as np
from jax import lax
from jax.experimental import pallas as pl
from jax.experimental.pallas import tpu as pltpu
from jax.sharding import PartitionSpec as P

R = 8
G = 8
F32 = jnp.float32
BF16 = jnp.bfloat16
VMEM_LIMIT = 56 * 1024 * 1024
MESH = pl.DeviceIdType.MESH


def split(value):
    high = value.astype(BF16)
    return high, (value - high.astype(F32)).astype(BF16)


def dot(left, right, dims=(((1,), (0,)), ((), ()))):
    return lax.dot_general(left, right, dims, preferred_element_type=F32)


def dot3(left, right):
    return dot(left[0], right[0]) + (dot(left[1], right[0]) + dot(left[0], right[1]))


def np_split(value):
    high = value.astype(np.float32).astype(BF16)
    return high, (value - high.astype(np.float64)).astype(np.float32).astype(BF16)


def col_tables(width, half):
    phase = 2.0 * math.pi / width * (np.outer(np.arange(width), np.arange(half)) % width)
    cosine, sine = np.cos(phase) / math.sqrt(width), np.sin(phase) / math.sqrt(width)
    plain = np.concatenate([cosine, -sine, -sine, -cosine], 1)
    doubled = plain * np.tile(np.where(np.arange(half) == 0, 1.0, 2.0), 4)[None, :]
    return plain, doubled


def row_tables(height, mode_rows, first_row, rows_dev):
    position = jnp.arange(mode_rows, dtype=jnp.int32)
    frequency = jnp.where(position < mode_rows // 2, position, height - mode_rows + position)
    row = first_row + jnp.arange(rows_dev, dtype=jnp.int32)
    phase = 2.0 * math.pi / height * (frequency[:, None] * row[None, :] % height).astype(F32)
    small = jnp.concatenate([jnp.cos(phase), jnp.sin(phase)], 1) / math.sqrt(height)
    rounded = lax.reduce_precision(small, 8, 7)
    high, low = rounded.astype(BF16), (small - rounded).astype(BF16)
    forward = jnp.concatenate([jnp.concatenate([high, high], 1), jnp.concatenate([low, jnp.zeros_like(low)], 1)], 0)
    inverse = jnp.concatenate([high.T, high.T, low.T], 1)
    return forward, inverse


def to_modes(value, table, kron, spread, p_ref):
    mode_rows, count, lanes = p_ref.shape
    rows = value.shape[0] // count
    high, low = split(value)
    spectra = dot(jnp.concatenate([high, low, high], 1), table)
    for i in range(2):
        spread[i] = spectra[:, i * lanes:(i + 1) * lanes]
    out = p_ref.reshape(mode_rows * count, lanes)
    for first in range(0, count, 2):
        sides = []
        for c in (first, first + 1):
            pick = pl.ds(c, rows, stride=count)
            sides.append(jnp.concatenate([spread[i, pick, :] for i in range(2)], 0))
        high, low = split(jnp.concatenate(sides, 1))
        both = dot(kron, jnp.concatenate([high, low], 0))
        result = both[:mode_rows] + both[mode_rows:]
        for i in range(2):
            out[pl.ds(first + i, mode_rows, stride=count), :] = result[:, i * lanes:(i + 1) * lanes]


def from_modes(y_ref, table, kron, spread):
    mode_rows, count, lanes = y_ref.shape
    rows, pieces = spread.shape[1] // count, spread.shape[0]
    modes = y_ref.reshape(mode_rows * count, lanes)
    sides = []
    for first in range(0, count, 2):
        pair = [modes[pl.ds(c, mode_rows, stride=count), :] for c in (first, first + 1)]
        high, low = split(jnp.concatenate(pair, 1))
        both = dot(kron, jnp.concatenate([high, low, high], 0))
        for i in range(2):
            side = both[:, i * lanes:(i + 1) * lanes]
            sides.append(jnp.concatenate([side[:rows], side[rows:]], 1))
    high, low = split(jnp.concatenate(sides, 0))
    out = dot(jnp.concatenate([high, low, high], 1), table)
    for c in range(count):
        for i in range(pieces):
            spread[i, pl.ds(c, rows, stride=count), :] = out[c * rows:(c + 1) * rows, i * 128:(i + 1) * 128]
    return jnp.concatenate([spread[i] for i in range(pieces)], 1)


def gelu_parts(z):
    size = jnp.abs(z)
    gauss = jnp.exp(-0.5 * z * z)
    t = 1.0 / (1.0 + (0.3275911 / math.sqrt(2.0)) * size)
    poly = t * (0.254829592 + t * (-0.284496736 + t * (1.421413741 + t * (-1.453152027 + t * 1.061405429))))
    tail = 0.5 * poly * gauss
    phi = jnp.where(z >= 0, 1.0 - tail, tail)
    return z * phi, phi + z * (gauss * (1.0 / math.sqrt(2.0 * math.pi)))


def flat(ref):
    rows, count, width = ref.shape
    return ref[...].reshape(rows * count, width)


def put(ref, value):
    ref[...] = value.reshape(ref.shape)


def place_and_peers():
    section, z = lax.axis_index("section"), lax.axis_index("rows")
    return section, z, lax.axis_size("rows")


def greet(section, z, n, lines):
    barrier = pltpu.get_barrier_semaphore()
    pl.semaphore_signal(barrier, inc=1, device_id={"section": 1 - section}, device_id_type=MESH)
    if not lines:
        pl.semaphore_wait(barrier, 1)
        return

    @pl.when(z > 0)
    def _():
        pl.semaphore_signal(barrier, inc=1, device_id={"rows": z - 1}, device_id_type=MESH)

    @pl.when(z < n - 1)
    def _():
        pl.semaphore_signal(barrier, inc=1, device_id={"rows": z + 1}, device_id_type=MESH)

    pl.semaphore_wait(barrier, 1 + (z > 0).astype(jnp.int32) + (z < n - 1).astype(jnp.int32))


def to_core(src, dst, sems, section):
    return pltpu.make_async_remote_copy(src_ref=src, dst_ref=dst, send_sem=sems[0], recv_sem=sems[1],
                                        device_id={"section": 1 - section}, device_id_type=MESH)


def guard(condition, body):
    if isinstance(condition, (bool, np.bool_)):
        if condition:
            body()
    else:
        pl.when(condition)(body)


class Line:
    def __init__(self, section, z, n, chunks, send, recv):
        self.section, self.z, self.n, self.chunks = section, z, n, chunks
        self.send, self.recv = send, recv

    def move(self, way, q, hop, src, dst):
        return pltpu.make_async_remote_copy(
            src_ref=src, dst_ref=dst, send_sem=self.send.at[way, q, hop], recv_sem=self.recv.at[way, q, hop],
            device_id={"rows": self.z + 1 if way == 0 else self.z - 1}, device_id_type=MESH)

    def sends(self, way):
        return self.z < self.n - 1 if way == 0 else self.z > 0

    def hears(self, way):
        return self.z > 0 if way == 0 else self.z < self.n - 1


class Gather(Line):
    def __init__(self, section, z, n, y, full, load, cross, send, recv):
        super().__init__(section, z, n, full.shape[0], send, recv)
        self.full = full
        self.here = pltpu.make_async_copy(y.at[0], full.at[:, z, section], load)
        self.cross = to_core(y.at[1], full.at[:, z, section], (cross.at[0], cross.at[1]), section)

    def hop(self, way, q, hop):
        piece = self.full.at[q, self.source(way, hop)]
        return self.move(way, q, hop, piece, piece)

    def source(self, way, hop):
        return self.z - hop if way == 0 else self.z + hop

    def known(self, way, hop):
        at = self.source(way, hop)
        return at >= 0 if way == 0 else at < self.n

    def begin(self):
        self.here.start()
        self.cross.start()

    def ready(self):
        self.here.wait()
        self.cross.wait_recv()

    def own(self, q):
        for way in range(2):
            @pl.when(self.sends(way))
            def _():
                self.hop(way, q, 0).start()

    def step(self, q, hop):
        for way in range(2):
            @pl.when(self.known(way, hop + 1))
            def _():
                piece = self.full.at[q, self.source(way, hop + 1)]
                self.move(way, q, hop, piece, piece).wait_recv()

                @pl.when(self.sends(way))
                def _():
                    self.hop(way, q, hop + 1).start()

    def tick(self, t):
        if isinstance(t, int) and t == 0:
            self.own(0)
        guard(t + 1 < self.chunks, lambda: self.own(t + 1))
        for hop in range(self.n - 1):
            q = t - hop - 1
            if isinstance(q, int):
                valid = 0 <= q < self.chunks
            else:
                valid = q < self.chunks
            guard(valid, functools.partial(self.step, q, hop))

    def finish(self):
        self.cross.wait_send()

        def body(q, carry):
            for way in range(2):
                for hop in range(self.n - 1):
                    @pl.when(jnp.logical_and(self.sends(way), self.known(way, hop)))
                    def _():
                        self.hop(way, q, hop).wait_send()
            return carry

        lax.fori_loop(0, self.chunks, body, 0)


class Reduce(Line):
    def __init__(self, section, z, n, part, come, f_out, f_sem, send, recv):
        super().__init__(section, z, n, part.shape[1], send, recv)
        self.part, self.come, self.f_out, self.f_sem = part, come, f_out, f_sem

    def owner(self, way, hop):
        return self.z + self.n - hop if way == 0 else self.z - self.n + hop

    def valid(self, way, hop):
        return self.z <= hop - 1 if way == 0 else self.z >= self.n - hop

    def sent(self, way, q, hop):
        return self.move(way, q, hop, self.part.at[self.owner(way, hop), q], self.come.at[way, q, hop])

    def heard(self, way, q, hop):
        come = self.come.at[way, q, hop]
        self.move(way, q, hop, come, come).wait_recv()

    def step(self, q, hop):
        for way in range(2):
            @pl.when(self.valid(way, hop))
            def _():
                if hop > 1:
                    @pl.when(self.hears(way))
                    def _():
                        self.heard(way, q, hop - 1)
                        owner = self.owner(way, hop)
                        self.part[owner, q] = self.part[owner, q] + self.come[way, q, hop - 1]

                self.sent(way, q, hop).start()

    def result(self, q):
        return pltpu.make_async_copy(self.part.at[self.z, q], self.f_out.at[q], self.f_sem.at[q])

    def final(self, q):
        for way in range(2):
            @pl.when(self.hears(way))
            def _():
                self.heard(way, q, self.n - 1)
                self.part[self.z, q] = self.part[self.z, q] + self.come[way, q, self.n - 1]

        self.result(q).start()

    def tick(self, t):
        for hop in range(1, self.n + 1):
            q = t - hop + 1
            if isinstance(q, int):
                valid = 0 <= q < self.chunks
            else:
                valid = q < self.chunks
            guard(valid, functools.partial(self.step, q, hop) if hop < self.n else functools.partial(self.final, q))

    def finish(self):
        def body(q, carry):
            self.result(q).wait()
            for way in range(2):
                for hop in range(1, self.n):
                    @pl.when(self.valid(way, hop))
                    def _():
                        self.sent(way, q, hop).wait_send()
            return carry

        lax.fori_loop(0, self.chunks, body, 0)


def fetch(src, dst, sem, parts=4):
    step = dst.shape[0] // parts
    for i in range(parts):
        pltpu.make_async_copy(src.at[pl.ds(i * step, step)], dst.at[pl.ds(i * step, step)], sem).start()


def arrived(dst, sem):
    pltpu.make_async_copy(dst, dst, sem).wait()


def portions(total, count):
    return [(i * total // count, (i + 1) * total // count) for i in range(count)]


def conv_rows(weight, bias, a, out, first, last):
    channels, width = a.shape[1:]
    block = weight.shape[0] // channels

    def body(i, carry):
        at = pl.ds(i * block, block)
        high, low = split(a[at].reshape(block * channels, width))
        result = dot(weight[...], jnp.concatenate([high, high, low], 0)).reshape(block, channels, width)
        out[at] = result + bias[...][None] if bias is not None else out[at] + result
        return carry

    lax.fori_loop(first, last, body, 0)


def grad_rows(a, gz, cg_ref, bg_ref, first, last):
    channels, width = a.shape[1:]

    def body(r, carry):
        grad, bias = carry
        g = gz[r]
        left = jnp.concatenate(split(a[r]), 0)
        right = jnp.concatenate(split(g), 0)
        return grad + dot(left, right, (((1,), (1,)), ((), ()))), bias + g

    zero = (jnp.zeros(cg_ref.shape, F32), jnp.zeros(bg_ref.shape, F32))
    grad, bias = lax.fori_loop(first, last, body, zero if first == 0 else (cg_ref[...], bg_ref[...]))
    cg_ref[...] = grad
    bg_ref[...] = bias


def chunk_of(ref, q, count):
    rows, _, width = ref.shape
    return ref[:, pl.ds(pl.multiple_of(q * count, count), count), :].reshape(rows * count, width)


def chunk_at(ref, q, count):
    return ref.at[:, pl.ds(pl.multiple_of(q * count, count), count), :]


class Modes:
    def __init__(self, section, buffer, p_out, local, cross):
        self.section, self.buffer, self.p_out, self.local, self.cross = section, buffer, p_out, local, cross

    def view(self, q):
        n, halves, kx, count, lanes = self.buffer.shape[1:]
        return self.buffer.at[q].reshape(n * halves * kx, count, lanes)

    def copies(self, q):
        s = self.section
        return (pltpu.make_async_copy(self.buffer.at[q, :, s], self.p_out.at[:, q, 0], self.local.at[q]),
                to_core(self.buffer.at[q, :, 1 - s], self.p_out.at[:, q, 1],
                        (self.cross.at[0, q], self.cross.at[1, q]), s))

    def start(self, q):
        for copy in self.copies(q):
            copy.start()

    def wait(self, q):
        for copy in self.copies(q):
            copy.wait()


class Bound:
    def __init__(self, section, owner, micro, other, source, bound, local, cross):
        self.section, self.owner, self.micro, self.other = section, owner, micro, other
        self.source, self.bound, self.local, self.cross = source, bound, local, cross

    def copies(self, q, count, micro):
        src, dst = chunk_at(self.source, q, count), chunk_at(self.bound.at[micro], q, count)
        return (pltpu.make_async_copy(src, dst, self.local.at[q]),
                to_core(src, dst, (self.cross.at[0, q], self.cross.at[1, q]), self.section))

    def start(self, q, count):
        here, there = self.copies(q, count, self.micro)

        @pl.when(self.section == self.owner)
        def _():
            here.start()

        @pl.when(self.section != self.owner)
        def _():
            there.start()

    def wait(self, q, count):
        here, there = self.copies(q, count, self.micro)
        come = self.copies(q, count, self.other)[1]

        @pl.when(self.section == self.owner)
        def _():
            here.wait()
            come.wait_recv()

        @pl.when(self.section != self.owner)
        def _():
            there.wait_send()


def add_squares(value, total):
    rows, _, width = total.shape
    square = (value * value).reshape(rows, -1, width)
    for at in range(0, square.shape[1], G):
        total[...] += square[:, at:at + G]


def region_sums(rid_ref, eo, eb, stat_ref):
    rows, _, width = eo.shape
    rid = rid_ref[...]
    energies = (jnp.sum(eo[...], axis=1), jnp.sum(eb[...], axis=1), jnp.ones((rows, width), F32))
    for kind in range(3):
        for region in range(R):
            line = jnp.sum(jnp.where(rid == region + 1, energies[kind], 0.0), axis=0, keepdims=True)
            total = line[:, :128]
            for piece in range(1, width // 128):
                total = total + line[:, piece * 128:(piece + 1) * 128]
            stat_ref[kind, region:region + 1, :] = total


def start_kernel(per_core, r):
    section, z, n = place_and_peers()
    chunks, count, half = r.p_buf.shape[1], r.p_buf.shape[5], r.far.shape[0]
    blocks = [(j, q) for j in range(per_core) for q in range(chunks)]
    reduce = Reduce(section, z, n, r.part, r.come, r.f_out, r.f_sem, r.red_send, r.red_recv)
    outs = [r.part] + [getattr(r, f"p{j}") for j in range(1, per_core)]
    modes = [Modes(section, r.p_buf.at[j], outs[j], r.p_local.at[j], r.p_cross.at[j]) for j in range(per_core)]

    def field(k):
        j, q = blocks[k]
        src = chunk_at(r.inputs.at[section * per_core + j, 0], q, count)
        return pltpu.make_async_copy(src, r.a_buf.at[k % 2], r.a_sem.at[k % 2])

    def weight_in(x):
        return pltpu.make_async_copy(r.weights.at[0, (1 - section) * half + x], r.w_buf.at[x % 2], r.w_sem.at[x % 2])

    def weight_out(x):
        return to_core(r.w_buf.at[x % 2], r.far.at[x], (r.w_cross.at[0, x], r.w_cross.at[1, x]), section)

    def lend(x):
        if x < half:
            weight_in(x).wait()
            weight_out(x).start()
        if 1 <= x <= half:
            weight_out(x - 1).wait_send()
            if x + 1 < half:
                weight_in(x + 1).start()

    field(0).start()
    for x in range(min(2, half)):
        weight_in(x).start()
    greet(section, z, n, True)
    for k, (j, q) in enumerate(blocks):
        if k + 1 < len(blocks):
            field(k + 1).start()
        field(k).wait()
        to_modes(flat(r.a_buf.at[k % 2]), r.table[...], r.kron[...], r.spread, modes[j].view(q))
        modes[j].start(q)
        lend(k)
        if k >= 1:
            if k <= chunks:
                modes[0].wait(k - 1)
            reduce.tick(k - 1)
    for k in range(len(blocks), half + 1):
        lend(k)
    for t in range(len(blocks) - 1, chunks + n - 1):
        reduce.tick(t)
    for x in range(half):
        weight_out(x).wait_recv()
    for j, q in blocks[chunks:]:
        modes[j].wait(q)
    reduce.finish()


def stage_kernel(kind, j, per_core, r):
    section, z, n = place_and_peers()
    micro, other = section * per_core + j, (1 - section) * per_core + j
    forward, last = kind in ("middle", "turn"), kind == "tail"
    chunks, count, lanes = r.full.shape[0], r.full.shape[4], r.full.shape[5]
    gather = Gather(section, z, n, r.y, r.full, r.load, r.cross, r.send, r.recv)
    reduce = None
    if hasattr(r, "part"):
        reduce = Reduce(section, z, n, r.part, r.come, r.f_out, r.f_sem, r.red_send, r.red_recv)
        fetch(r.p_in, r.part, r.part_sem)
    if forward:
        fetch(r.a_in.at[micro, 0] if kind == "middle" else r.a_in, r.a, r.a_sem)
        if kind == "turn":
            fetch(r.cot_in.at[micro, 0], r.cot, r.c_sem)
        rid_copy = pltpu.make_async_copy(r.rid_in.at[micro, 0], r.rid, r.rid_sem)
        rid_copy.start()
    else:
        fetch(r.gz_in, r.gz, r.gz_sem)
        fetch(r.g_in if last else r.g_in.at[micro, 0], r.h, r.h_sem)
        fetch(r.a_in.at[micro, 0] if last else r.a_in, r.a, r.a_sem)
        if not last:
            fetch(r.dg_in, r.dg, r.dg_sem)
    greet(section, z, n, True)
    gather.begin()
    if reduce is not None:
        arrived(r.part, r.part_sem)
        reduce.tick(0)
    gather.ready()
    gather.tick(0)
    if forward:
        r.eo[...] = jnp.zeros_like(r.eo)
        r.eb[...] = jnp.zeros_like(r.eb)
        arrived(r.a, r.a_sem)
    else:
        arrived(r.gz, r.gz_sem)
        arrived(r.h, r.h_sem)

    rows, channels = r.a.shape[:2]
    conv_blocks = rows // (r.weight.shape[0] // channels)
    if forward:
        work = [functools.partial(conv_rows, r.weight, r.bias, r.a, r.z_buf, *span)
                for span in portions(conv_blocks, n - 1)]
    else:
        work = [functools.partial(conv_rows, r.weight, None, r.gz, r.h, 0, conv_blocks)]
        spans = portions(rows, n - 2)
        work += [functools.partial(grad_rows, r.a, r.gz, r.cg, r.bg, *span) for span in spans]
    for t in range(n - 1):
        if t > 0:
            if reduce is not None:
                reduce.tick(t)
            gather.tick(t)
        if not forward and t == 1:
            arrived(r.a, r.a_sem)
        work[t]()
    if kind == "turn":
        arrived(r.cot, r.c_sem)
    if kind == "back":
        arrived(r.dg, r.dg_sem)

    if not last:
        modes = Modes(section, r.p_buf, r.p_out, r.p_local, r.p_cross)
    if kind == "turn":
        bound = Bound(section, 1, micro, other, r.a, r.bound, r.b_local, r.b_cross)
    if last:
        bound = Bound(section, 0, micro, other, r.h, r.bound, r.b_local, r.b_cross)

    def saves(q):
        pairs = {"middle": lambda: [(r.a, r.a_out), (r.z_buf, r.dg_out)], "turn": lambda: [(r.cot, r.gz_out)],
                 "back": lambda: [(r.h, r.ga_out), (r.dg, r.gz_out)], "tail": lambda: []}[kind]()
        return [pltpu.make_async_copy(chunk_at(src, q, count), chunk_at(dst, q, count), r.out_sem.at[i, q])
                for i, (src, dst) in enumerate(pairs)]

    def body(q, carry):
        if reduce is not None:
            reduce.tick(q + n - 1)
        gather.tick(q + n - 1)
        spectral = from_modes(r.full.at[q].reshape(-1, count, lanes), r.itable[...], r.ikron[...], r.spread)
        if forward:
            branch, slope = gelu_parts(spectral + chunk_of(r.z_buf, q, count))
            if kind == "turn":
                put(chunk_at(r.cot, q, count), chunk_of(r.cot, q, count) * slope)
            else:
                put(chunk_at(r.z_buf, q, count), slope)
            add_squares(branch, r.eb)
            out = chunk_of(r.a, q, count) + branch
            put(chunk_at(r.a, q, count), out)
            add_squares(out, r.eo)
            source = r.cot if kind == "turn" else r.a
        else:
            ga = spectral + chunk_of(r.h, q, count)
            put(chunk_at(r.h, q, count), ga)
            if not last:
                put(chunk_at(r.dg, q, count), ga * chunk_of(r.dg, q, count))
                source = r.dg
        for copy in saves(q):
            copy.start()
        if kind in ("turn", "tail"):
            bound.start(q, count)
        if not last:
            to_modes(chunk_of(source, q, count), r.table[...], r.kron[...], r.spread, modes.view(q))
            modes.start(q)
        return carry

    lax.fori_loop(0, chunks, body, 0)
    if forward:
        rid_copy.wait()
        region_sums(r.rid, r.eo, r.eb, r.stat)

    def close(q, carry):
        for copy in saves(q):
            copy.wait()
        if kind in ("turn", "tail"):
            bound.wait(q, count)
        if not last:
            modes.wait(q)
        return carry

    lax.fori_loop(0, chunks, close, 0)
    gather.finish()
    if reduce is not None:
        reduce.finish()


def swap_halves(value):
    return pltpu.roll(value, value.shape[-1] // 2, value.ndim - 1)


def left_lanes(shape):
    return lax.broadcasted_iota(jnp.int32, shape, len(shape) - 1) < shape[-1] // 2


SLOTS = 4


def weight_stream(own, base, local_ref, far_ref, wbuf, sem):
    step, count = pl.program_id(0), pl.num_programs(0)

    def begin(at):
        slot = lax.rem(at, SLOTS)

        @pl.when(own)
        def _():
            fetch(local_ref.at[0, base + at], wbuf.at[slot], sem.at[slot])

        @pl.when(jnp.logical_not(own))
        def _():
            fetch(far_ref.at[at], wbuf.at[slot], sem.at[slot])

    @pl.when(step == 0)
    def _():
        for at in range(SLOTS - 1):
            @pl.when(at < count)
            def _():
                begin(at)

    @pl.when(step + SLOTS - 1 < count)
    def _():
        begin(step + SLOTS - 1)

    slot = lax.rem(step, SLOTS)
    arrived(wbuf.at[slot], sem.at[slot])
    return wbuf.at[slot]


def pieces(array):
    return [array[at:at + G] for at in range(0, array.shape[0], G)]


def spread_row(tile, row):
    return jnp.broadcast_to(tile[row:row + 1], tile.shape)


def mix_kernel(m_ref, f_ref, local_ref, far_ref, y_ref, wbuf, f1, f2, sem):
    weight = weight_stream(m_ref[0] == 1, m_ref[1], local_ref, far_ref, wbuf, sem)
    grids, channels, lanes = f1.shape
    for g in range(grids):
        f1[g] = f_ref[:, g].reshape(channels, lanes)
    f2[...] = swap_halves(f1[...])
    groups = channels // G

    def body(block, acc):
        at = pl.multiple_of(block * G, G)
        acc = list(acc)
        tiles = [f[g, pl.ds(at, G), :] for g in range(grids) for f in (f1, f2)]
        for u in range(G):
            rows = [spread_row(tile, u) for tile in tiles]
            for o in range(groups):
                w = weight[at + u, o * G:(o + 1) * G, :]
                for k, row in enumerate(rows):
                    acc[k * groups + o] = acc[k * groups + o] + row * w
        return tuple(acc)

    acc = lax.fori_loop(0, groups, body, tuple(jnp.zeros((G, lanes), F32) for _ in range(2 * grids * groups)))
    left = left_lanes((channels, lanes))
    for g in range(grids):
        a, b = [jnp.concatenate(acc[k * groups:(k + 1) * groups], 0) for k in (2 * g, 2 * g + 1)]
        y_ref[g] = jnp.where(left, a - swap_halves(a), b + swap_halves(b)).reshape(y_ref.shape[1:])


def mix_t_kernel(m_ref, d_ref, local_ref, far_ref, y_ref, wbuf, a1, a2, sem):
    weight = weight_stream(m_ref[0] == 1, m_ref[1], local_ref, far_ref, wbuf, sem)
    grids, channels, lanes = a1.shape
    d = [d_ref[:, g].reshape(channels, lanes) for g in range(grids)]
    d1 = [pieces(d[g]) for g in range(grids)]
    d2 = [pieces(swap_halves(d[g])) for g in range(grids)]
    groups = channels // G

    def body(block, carry):
        at = pl.multiple_of(block * G, G)
        rows = [[] for _ in range(2 * grids)]
        for u in range(G):
            total = [None] * (2 * grids)
            for o in range(groups):
                w = weight[at + u, o * G:(o + 1) * G, :]
                for g in range(grids):
                    for side, source in enumerate((d1, d2)):
                        term = w * source[g][o]
                        k = 2 * g + side
                        total[k] = term if total[k] is None else total[k] + term
            for k in range(2 * grids):
                rows[k].append(jnp.sum(total[k], axis=0, keepdims=True))
        for g in range(grids):
            a1[g, pl.ds(at, G), :] = jnp.concatenate(rows[2 * g], 0)
            a2[g, pl.ds(at, G), :] = jnp.concatenate(rows[2 * g + 1], 0)
        return carry

    lax.fori_loop(0, groups, body, 0)
    left = left_lanes((channels, lanes))
    for g in range(grids):
        a, b = a1[g], a2[g]
        y_ref[g] = jnp.where(left, a + swap_halves(a), swap_halves(b) - b).reshape(y_ref.shape[1:])


def grad_tables(f_ref, d_ref, fa, fb, d1, d2):
    channels, lanes = fa.shape[1:]
    left = left_lanes((channels, lanes))
    at = 0
    for stream in range(f_ref.shape[0]):
        for member in range(f_ref.shape[1]):
            for g in range(f_ref.shape[3]):
                f = f_ref[stream, member, :, g].reshape(channels, lanes)
                other = swap_halves(f)
                fa[at] = jnp.where(left, f, other)
                fb[at] = jnp.where(left, other, -f)
                d = d_ref[stream, member, :, g].reshape(channels, lanes)
                d1[at] = d
                d2[at] = swap_halves(d)
                at += 1


def grad_block(first_row, fa, fb, d1, d2, out):
    count, channels, lanes = fa.shape
    groups = channels // G
    wide = 4

    def body(octet, carry):
        at = pl.multiple_of(octet * G, G)
        rows = pl.ds(pl.multiple_of(first_row + at, G), G)
        for first in range(0, G, wide):
            acc = [[None] * groups for _ in range(wide)]
            for g in range(count):
                ta, tb = fa[g, rows, :], fb[g, rows, :]
                pairs = [(spread_row(ta, first + u), spread_row(tb, first + u)) for u in range(wide)]
                for o in range(groups):
                    x, y = d1[g, o * G:(o + 1) * G, :], d2[g, o * G:(o + 1) * G, :]
                    for u in range(wide):
                        term = pairs[u][0] * x + pairs[u][1] * y
                        acc[u][o] = term if acc[u][o] is None else acc[u][o] + term
            for u in range(wide):
                for o in range(groups):
                    out[at + first + u, o * G:(o + 1) * G, :] = acc[u][o]
        return carry

    lax.fori_loop(0, out.shape[0] // G, body, 0)


class GradInput:
    def __init__(self, first, f, g, fbuf, gbuf, sem):
        self.first, self.f, self.g, self.fbuf, self.gbuf, self.sem = first, f, g, fbuf, gbuf, sem

    def load(self, x, slot):
        for layer, condition in enumerate((self.first, jnp.logical_not(self.first))):
            @pl.when(condition)
            def _():
                for j in range(len(self.f[layer])):
                    pltpu.make_async_copy(self.f[layer][j].at[:, :, :, x], self.fbuf.at[slot, j],
                                          self.sem.at[0, slot]).start()
                    pltpu.make_async_copy(self.g[layer][j].at[:, :, :, x], self.gbuf.at[slot, j],
                                          self.sem.at[1, slot]).start()

    def next(self, x, count):
        slot = lax.rem(x, 2)

        @pl.when(x + 1 < count)
        def _():
            self.load(x + 1, 1 - slot)

        arrived(self.fbuf.at[slot], self.sem.at[0, slot])
        arrived(self.gbuf.at[slot], self.sem.at[1, slot])
        return self.fbuf.at[slot], self.gbuf.at[slot]


def grad_input(r, first, per_core):
    f = [[getattr(r, f"f{layer}{j}") for j in range(per_core)] for layer in range(2)]
    g = [[getattr(r, f"g{layer}{j}") for j in range(per_core)] for layer in range(2)]
    return GradInput(first, f, g, r.fbuf, r.gbuf, r.in_sem)


def far_grad_kernel(per_core, r):
    section, z, n = place_and_peers()
    half, channels = r.far.shape[0], r.far.shape[1]
    block = r.out.shape[1]
    blocks = channels // block
    source = grad_input(r, section != 0, per_core)

    def move(k, slot):
        x, i = k // blocks, k % blocks
        return to_core(r.out.at[slot], r.far.at[x, pl.ds(i * block, block)], (r.send.at[k], r.recv.at[k]), section)

    source.load(0, 0)
    greet(section, z, n, False)

    def body(x, carry):
        grad_tables(*source.next(x, half), r.fa, r.fb, r.d1, r.d2)

        def inner(i, carry):
            k = x * blocks + i

            @pl.when(k >= 2)
            def _():
                move(k - 2, lax.rem(k, 2)).wait_send()

            grad_block(i * block, r.fa, r.fb, r.d1, r.d2, r.out.at[lax.rem(k, 2)])
            move(k, lax.rem(k, 2)).start()
            return carry

        return lax.fori_loop(0, blocks, inner, carry)

    lax.fori_loop(0, half, body, 0)
    total = half * blocks
    for k in (total - 2, total - 1):
        move(k, k % 2).wait_send()

    def close(k, carry):
        move(k, 0).wait_recv()
        return carry

    lax.fori_loop(0, total, close, 0)


def own_grad_kernel(names, per_core, m_ref, *refs):
    r = types.SimpleNamespace(**dict(zip(names, refs)))
    x, i, kind = pl.program_id(0), pl.program_id(1), pl.program_id(2)
    source = grad_input(r, m_ref[0] == 0, per_core)

    @pl.when(jnp.logical_and(i == 0, kind == 0))
    def _():
        @pl.when(x == 0)
        def _():
            source.load(0, 0)

        grad_tables(*source.next(x, pl.num_programs(0)), r.fa, r.fb, r.d1, r.d2)

    @pl.when(kind == 0)
    def _():
        grad_block(i * r.out.shape[0], r.fa, r.fb, r.d1, r.d2, r.out)

    @pl.when(kind == 1)
    def _():
        r.out[...] = r.far[...]


def whole(array):
    return pl.BlockSpec(array.shape, lambda *_: (0,) * array.ndim)


def params(**kw):
    return pltpu.CompilerParams(vmem_limit_bytes=VMEM_LIMIT, **kw)


def local(inputs, cotangent, region_id, spectral_w, conv_w, bias_vector):
    micro_count, _, rows_dev, channels, width = inputs.shape
    lanes = spectral_w.shape[-1]
    half = lanes // 2
    kx_dev = spectral_w.shape[1]
    row_devices, sections = lax.axis_size("rows"), lax.axis_size("section")
    mode_rows, height = kx_dev * row_devices, rows_dev * row_devices
    section = lax.axis_index("section")
    per_core = micro_count // sections
    kx_half = kx_dev // sections

    plain, doubled = col_tables(width, half)

    def stacked(array):
        high, low = np_split(array)
        return np.concatenate([high, high, low], 0)

    t_plain, t_doubled, it_plain, it_doubled = [stacked(t) for t in (plain, doubled, plain.T, doubled.T)]
    kron, ikron = row_tables(height, mode_rows, lax.axis_index("rows") * rows_dev, rows_dev)

    count = 2 * G
    chunks = channels // count
    hbm, vmem = pl.BlockSpec(memory_space=pl.ANY), pl.BlockSpec(memory_space=pltpu.VMEM)
    field_shape = jax.ShapeDtypeStruct((rows_dev, channels, width), F32)
    part_dims = (row_devices, chunks, sections, kx_half, count, lanes)
    p_shape, f_shape = jax.ShapeDtypeStruct(part_dims, F32), jax.ShapeDtypeStruct(part_dims[1:], F32)
    y_shape = jax.ShapeDtypeStruct((sections, chunks, kx_half, count, lanes), F32)
    stat_shape = jax.ShapeDtypeStruct((3, R, 128), F32)
    cg_shape = jax.ShapeDtypeStruct((2 * channels, 2 * channels), F32)
    bg_shape = jax.ShapeDtypeStruct((channels, width), F32)
    bound_shape = jax.ShapeDtypeStruct((micro_count, rows_dev, channels, width), F32)
    dma = pltpu.SemaphoreType.DMA
    field_buf = pltpu.VMEM((rows_dev, channels, width), F32)
    full_dims = (chunks, row_devices, sections, kx_half, count, lanes)
    spread = pltpu.VMEM((width // 128, rows_dev * count, 128), F32)
    energy = pltpu.VMEM((rows_dev, G, width), F32)
    line_sems = dma((2, chunks, row_devices))
    reduce_scratch = dict(part=pltpu.VMEM(part_dims, F32), come=pltpu.VMEM((2, chunks) + (row_devices,) + part_dims[2:], F32),
                          f_sem=dma((chunks,)), red_send=line_sems, red_recv=line_sems, part_sem=dma)

    def run(body, ident, ins, outs, scratch, cost=50, aliases=None):
        names = [*ins, *outs, *scratch]
        spec = lambda entry: vmem if isinstance(entry, tuple) else hbm
        plain = lambda entry: entry[0] if isinstance(entry, tuple) else entry
        kernel = lambda *refs: body(types.SimpleNamespace(**dict(zip(names, refs))))
        positions = {list(ins).index(k): list(outs).index(v) for k, v in (aliases or {}).items()}
        result = pl.pallas_call(
            kernel, in_specs=[spec(e) for e in ins.values()], out_specs=[spec(e) for e in outs.values()],
            out_shape=[plain(e) for e in outs.values()], scratch_shapes=list(scratch.values()),
            input_output_aliases=positions,
            cost_estimate=pl.CostEstimate(flops=0, bytes_accessed=cost * 3_000_000, transcendentals=0),
            compiler_params=params(collective_id=ident, has_side_effects=True))(*[plain(e) for e in ins.values()])
        return types.SimpleNamespace(**dict(zip(outs, result)))

    conv_rows_at_once = 256 // channels
    conv_both = lax.all_gather(conv_w, "section", axis=0, tiled=True)
    bias_both = lax.all_gather(bias_vector, "section", axis=0, tiled=True)

    def conv_parts(matrix):
        wide = jnp.kron(jnp.eye(conv_rows_at_once, dtype=F32), matrix)
        rounded = lax.reduce_precision(wide, 8, 7)
        high, low = rounded.astype(BF16), (wide - rounded).astype(BF16)
        return jnp.concatenate([high, low, high], 1)

    conv_fwd = [conv_parts(conv_both[l].T) for l in range(2)]
    conv_bwd = [conv_parts(conv_both[l]) for l in range(2)]
    bias_wide = [jnp.broadcast_to(bias_both[l][:, None], (channels, width)) for l in range(2)]

    def mixing(body, layer, pair):
        flag = jnp.stack([(section == layer).astype(jnp.int32), section * kx_half])
        f_block = pl.BlockSpec((chunks, sections, None, count, lanes), lambda x, m: (0, 0, x, 0, 0))
        y_block = pl.BlockSpec((sections, chunks, None, count, lanes), lambda x, m: (0, 0, x, 0, 0))
        small = pltpu.VMEM((sections, channels, lanes), F32)
        grid_spec = pltpu.PrefetchScalarGridSpec(
            num_scalar_prefetch=1, grid=(kx_half,), in_specs=[f_block, hbm, hbm], out_specs=y_block,
            scratch_shapes=[pltpu.VMEM((SLOTS, channels, channels, lanes), F32), small, small, dma((SLOTS,))])
        return pl.pallas_call(
            body, grid_spec=grid_spec, out_shape=y_shape, compiler_params=params(),
            cost_estimate=pl.CostEstimate(flops=0, bytes_accessed=30_000_000, transcendentals=0))(
                flag, pair, spectral_w, far_weights)

    streams = range(per_core)
    start = run(
        functools.partial(start_kernel, per_core), 0,
        dict(inputs=inputs, weights=spectral_w, table=(t_plain,), kron=(kron,)),
        dict(f_out=f_shape, far=jax.ShapeDtypeStruct((kx_half,) + spectral_w.shape[2:], F32),
             **{f"p{j}": p_shape for j in streams[1:]}),
        dict(a_buf=pltpu.VMEM((2, rows_dev, count, width), F32), w_buf=pltpu.VMEM((2,) + spectral_w.shape[2:], F32),
             p_buf=pltpu.VMEM((per_core,) + full_dims, F32), spread=spread, a_sem=dma((2,)), w_sem=dma((2,)),
             w_cross=dma((2, kx_half)), p_local=dma((per_core, chunks)), p_cross=dma((per_core, 2, chunks)),
             **reduce_scratch))
    far_weights = start.far

    kinds = ["middle", "turn", "back", "tail"]
    mixes = [(mix_kernel, 0), (mix_kernel, 1), (mix_t_kernel, 1), (mix_t_kernel, 0)]
    sums = [[None] * per_core for _ in kinds]
    sums[0][0] = start.f_out
    parts = [getattr(start, f"p{j}", None) for j in streams]
    kept = [types.SimpleNamespace() for _ in streams]
    bound, calls = None, 0
    for phase, kind in enumerate(kinds):
        for j in streams:
            y = mixing(*mixes[phase], sums[phase][j])
            keep = kept[j]
            ins, outs = dict(y=y), {}
            scratch = dict(full=pltpu.VMEM(full_dims, F32), spread=spread, load=dma, cross=dma((2,)),
                           send=line_sems, recv=line_sems, a=field_buf, a_sem=dma)
            aliases = {}
            if kind == "middle":
                ins.update(a_in=inputs, rid_in=region_id, weight=(conv_fwd[0],), bias=(bias_wide[0],))
                outs.update(a_out=field_shape, dg_out=field_shape, stat=(stat_shape,))
            elif kind == "turn":
                ins.update(a_in=keep.a1, rid_in=region_id, cot_in=cotangent, weight=(conv_fwd[1],), bias=(bias_wide[1],))
                outs.update(gz_out=field_shape, stat=(stat_shape,), bound=bound_shape)
                scratch.update(cot=field_buf, c_sem=dma)
            elif kind == "back":
                ins.update(a_in=keep.a1, gz_in=keep.gz1, g_in=cotangent, dg_in=keep.dg0, weight=(conv_bwd[1],))
                outs.update(ga_out=field_shape, gz_out=field_shape, cg=(cg_shape,), bg=(bg_shape,))
                scratch.update(dg=field_buf, dg_sem=dma)
            else:
                ins.update(a_in=inputs, gz_in=keep.gz0, g_in=keep.ga1, weight=(conv_bwd[0],))
                outs.update(cg=(cg_shape,), bg=(bg_shape,), bound=bound_shape)
            if kind in ("middle", "turn"):
                scratch.update(z_buf=field_buf, rid=pltpu.VMEM((rows_dev, width), jnp.int32), rid_sem=dma,
                               eo=energy, eb=energy)
            else:
                scratch.update(gz=field_buf, h=field_buf, gz_sem=dma, h_sem=dma)
            ins.update(itable=(it_doubled if kind in ("middle", "turn") else it_plain,), ikron=(ikron,))
            if kind != "tail":
                ins.update(table=(t_plain if kind == "middle" else t_doubled,), kron=(kron,))
                outs.update(p_out=p_shape)
                scratch.update(p_buf=pltpu.VMEM(full_dims, F32), p_local=dma((chunks,)), p_cross=dma((2, chunks)),
                               out_sem=dma((2, chunks)))
            if kind in ("turn", "tail"):
                scratch.update(b_local=dma((chunks,)), b_cross=dma((2, chunks)))
                if bound is not None:
                    ins.update(bound_in=bound)
                    aliases = dict(bound_in="bound")
            follow = (j + 1) % per_core
            follow_phase = phase + (1 if follow == 0 else 0)
            if follow_phase < len(kinds):
                ins.update(p_in=parts[follow])
                outs.update(f_out=f_shape)
                scratch.update(reduce_scratch)
            done = run(functools.partial(stage_kernel, kind, j, per_core), 1 + calls, ins, outs, scratch, aliases=aliases)
            calls += 1
            if kind != "tail":
                parts[j] = done.p_out
            if follow_phase < len(kinds):
                sums[follow_phase][follow] = done.f_out
            if kind in ("turn", "tail"):
                bound = done.bound
            if kind == "middle":
                keep.a1, keep.dg0, keep.stat0 = done.a_out, done.dg_out, done.stat
            elif kind == "turn":
                keep.gz1, keep.stat1 = done.gz_out, done.stat
            elif kind == "back":
                keep.ga1, keep.gz0, keep.cg1, keep.bg1 = done.ga_out, done.gz_out, done.cg, done.bg
            else:
                keep.cg0, keep.bg0 = done.cg, done.bg
    stats0, stats1, cg0, cg1, bg0, bg1 = [[getattr(k, name) for k in kept]
                                          for name in ("stat0", "stat1", "cg0", "cg1", "bg0", "bg1")]

    gathered = {}
    for name, phase in (("f0", 0), ("f1", 1), ("g1", 2), ("g0", 3)):
        for j in streams:
            gathered[f"{name}{j}"] = lax.all_gather(sums[phase][j], "batch", axis=0)
    members = lax.axis_size("batch")
    grids = per_core * members * sections
    block = 16
    blocks = channels // block
    in_buf = pltpu.VMEM((2, per_core, members, chunks, sections, count, lanes), F32)
    big = pltpu.VMEM((grids, channels, lanes), F32)
    grad_scratch = dict(fbuf=in_buf, gbuf=in_buf, in_sem=dma((2, 2)), fa=big, fb=big, d1=big, d2=big)
    far_shape = jax.ShapeDtypeStruct((kx_half, channels, channels, lanes), F32)
    far_grad = run(functools.partial(far_grad_kernel, per_core), 1 + calls, gathered, dict(far=far_shape),
                   dict(out=pltpu.VMEM((2, block, channels, lanes), F32), send=dma((kx_half * blocks,)),
                        recv=dma((kx_half * blocks,)), **grad_scratch)).far

    def far_block(x, i, k, m):
        at = jnp.maximum(x * blocks + i + k - 1, 0)
        return (at // blocks, at % blocks, 0, 0)

    grid_spec = pltpu.PrefetchScalarGridSpec(
        num_scalar_prefetch=1, grid=(kx_half, blocks, 2),
        in_specs=[hbm] * len(gathered) + [pl.BlockSpec((None, block, channels, lanes), far_block)],
        out_specs=pl.BlockSpec(
            (None, block, channels, lanes),
            lambda x, i, k, m: (jnp.where(k == 0, m[0], 1 - m[0]) * kx_half + x, i, 0, 0)),
        scratch_shapes=list(grad_scratch.values()))
    spectral_grad = pl.pallas_call(
        functools.partial(own_grad_kernel, [*gathered, "far", "out", *grad_scratch], per_core),
        grid_spec=grid_spec, out_shape=jax.ShapeDtypeStruct(spectral_w.shape[1:], F32),
        cost_estimate=pl.CostEstimate(flops=0, bytes_accessed=150_000_000, transcendentals=0),
        compiler_params=params())(jnp.reshape(section, (1,)).astype(jnp.int32), *gathered.values(), far_grad)[None]

    def lower(value):
        return (value[:channels, :channels] + value[channels:, channels:]
                + value[:channels, channels:] + value[channels:, :channels])

    conv_local = jnp.stack([lower(sum(cg0)), lower(sum(cg1))])
    bias_local = jnp.stack([jnp.sum(sum(bg0), -1), jnp.sum(sum(bg1), -1)])
    stat_local = jnp.stack([jnp.sum(sum(stats0), -1), jnp.sum(sum(stats1), -1)])
    conv_sum, bias_sum, stat_sum = lax.psum((conv_local, bias_local, stat_local), ("section", "batch", "rows"))
    own_stat = lax.dynamic_index_in_dim(stat_sum, section, 0, False)
    layer_rms = jnp.sqrt(own_stat[:2] / (channels * own_stat[2])[None, :] + 1e-06)[None]
    own = lambda value: lax.dynamic_slice_in_dim(value, section, 1, 0)
    return bound[None, :, None], spectral_grad, own(conv_sum), own(bias_sum), layer_rms


def solution(mesh):
    placed = (
        P(None, "batch", "rows", None, None),
        P(None, "batch", "rows", None, None),
        P(None, "batch", "rows", None),
        P("section", "rows", None, None, None),
        P("section", None, None),
        P("section", None),
    )
    return jax.shard_map(
        local,
        mesh=mesh,
        in_specs=placed,
        out_specs=(
            P("section", None, "batch", "rows", None, None),
            P("section", "rows", None, None, None),
            P("section", None, None),
            P("section", None),
            P("section", None, None),
        ),
        check_vma=False,
    )
```

```python
import functools
import math
import types

import jax
import jax.numpy as jnp
import numpy as np
from jax import lax
from jax.experimental import pallas as pl
from jax.experimental.pallas import tpu as pltpu
from jax.sharding import PartitionSpec as P

R = 8
G = 8
F32 = jnp.float32
BF16 = jnp.bfloat16
VMEM_LIMIT = 56 * 1024 * 1024
MESH = pl.DeviceIdType.MESH


def split(value):
    high = value.astype(BF16)
    return high, (value - high.astype(F32)).astype(BF16)


def dot(left, right, dims=(((1,), (0,)), ((), ()))):
    return lax.dot_general(left, right, dims, preferred_element_type=F32)


def dot3(left, right):
    return dot(left[0], right[0]) + (dot(left[1], right[0]) + dot(left[0], right[1]))


def np_split(value):
    high = value.astype(np.float32).astype(BF16)
    return high, (value - high.astype(np.float64)).astype(np.float32).astype(BF16)


def col_tables(width, half):
    phase = 2.0 * math.pi / width * (np.outer(np.arange(width), np.arange(half)) % width)
    cosine, sine = np.cos(phase) / math.sqrt(width), np.sin(phase) / math.sqrt(width)
    plain = np.concatenate([cosine, -sine, -sine, -cosine], 1)
    doubled = plain * np.tile(np.where(np.arange(half) == 0, 1.0, 2.0), 4)[None, :]
    return plain, doubled


def row_tables(height, mode_rows, first_row, rows_dev):
    position = jnp.arange(mode_rows, dtype=jnp.int32)
    frequency = jnp.where(position < mode_rows // 2, position, height - mode_rows + position)
    row = first_row + jnp.arange(rows_dev, dtype=jnp.int32)
    phase = 2.0 * math.pi / height * (frequency[:, None] * row[None, :] % height).astype(F32)
    small = jnp.concatenate([jnp.cos(phase), jnp.sin(phase)], 1) / math.sqrt(height)
    rounded = lax.reduce_precision(small, 8, 7)
    high, low = rounded.astype(BF16), (small - rounded).astype(BF16)
    forward = jnp.concatenate([jnp.concatenate([high, high], 1), jnp.concatenate([low, jnp.zeros_like(low)], 1)], 0)
    inverse = jnp.concatenate([high.T, high.T, low.T], 1)
    return forward, inverse


def to_modes(value, table, kron, spread, p_ref):
    mode_rows, count, lanes = p_ref.shape
    rows = value.shape[0] // count
    high, low = split(value)
    spectra = dot(jnp.concatenate([high, low, high], 1), table)
    for i in range(2):
        spread[i] = spectra[:, i * lanes:(i + 1) * lanes]
    out = p_ref.reshape(mode_rows * count, lanes)
    for first in range(0, count, 2):
        sides = []
        for c in (first, first + 1):
            pick = pl.ds(c, rows, stride=count)
            sides.append(jnp.concatenate([spread[i, pick, :] for i in range(2)], 0))
        high, low = split(jnp.concatenate(sides, 1))
        both = dot(kron, jnp.concatenate([high, low], 0))
        result = both[:mode_rows] + both[mode_rows:]
        for i in range(2):
            out[pl.ds(first + i, mode_rows, stride=count), :] = result[:, i * lanes:(i + 1) * lanes]


def from_modes(y_ref, table, kron, spread):
    mode_rows, count, lanes = y_ref.shape
    rows, pieces = spread.shape[1] // count, spread.shape[0]
    modes = y_ref.reshape(mode_rows * count, lanes)
    sides = []
    for first in range(0, count, 2):
        pair = [modes[pl.ds(c, mode_rows, stride=count), :] for c in (first, first + 1)]
        high, low = split(jnp.concatenate(pair, 1))
        both = dot(kron, jnp.concatenate([high, low, high], 0))
        for i in range(2):
            side = both[:, i * lanes:(i + 1) * lanes]
            sides.append(jnp.concatenate([side[:rows], side[rows:]], 1))
    high, low = split(jnp.concatenate(sides, 0))
    out = dot(jnp.concatenate([high, low, high], 1), table)
    for c in range(count):
        for i in range(pieces):
            spread[i, pl.ds(c, rows, stride=count), :] = out[c * rows:(c + 1) * rows, i * 128:(i + 1) * 128]
    return jnp.concatenate([spread[i] for i in range(pieces)], 1)


def gelu_parts(z):
    size = jnp.abs(z)
    gauss = jnp.exp(-0.5 * z * z)
    t = 1.0 / (1.0 + (0.3275911 / math.sqrt(2.0)) * size)
    poly = t * (0.254829592 + t * (-0.284496736 + t * (1.421413741 + t * (-1.453152027 + t * 1.061405429))))
    tail = 0.5 * poly * gauss
    phi = jnp.where(z >= 0, 1.0 - tail, tail)
    return z * phi, phi + z * (gauss * (1.0 / math.sqrt(2.0 * math.pi)))


def flat(ref):
    rows, count, width = ref.shape
    return ref[...].reshape(rows * count, width)


def put(ref, value):
    ref[...] = value.reshape(ref.shape)


def place_and_peers():
    section, z = lax.axis_index("section"), lax.axis_index("rows")
    return section, z, lax.axis_size("rows")


def greet(section, z, n, lines):
    barrier = pltpu.get_barrier_semaphore()
    pl.semaphore_signal(barrier, inc=1, device_id={"section": 1 - section}, device_id_type=MESH)
    if not lines:
        pl.semaphore_wait(barrier, 1)
        return

    @pl.when(z > 0)
    def _():
        pl.semaphore_signal(barrier, inc=1, device_id={"rows": z - 1}, device_id_type=MESH)

    @pl.when(z < n - 1)
    def _():
        pl.semaphore_signal(barrier, inc=1, device_id={"rows": z + 1}, device_id_type=MESH)

    pl.semaphore_wait(barrier, 1 + (z > 0).astype(jnp.int32) + (z < n - 1).astype(jnp.int32))


def to_core(src, dst, sems, section):
    return pltpu.make_async_remote_copy(src_ref=src, dst_ref=dst, send_sem=sems[0], recv_sem=sems[1],
                                        device_id={"section": 1 - section}, device_id_type=MESH)


def guard(condition, body):
    if isinstance(condition, (bool, np.bool_)):
        if condition:
            body()
    else:
        pl.when(condition)(body)


class Line:
    def __init__(self, section, z, n, chunks, send, recv):
        self.section, self.z, self.n, self.chunks = section, z, n, chunks
        self.send, self.recv = send, recv

    def move(self, way, q, hop, src, dst):
        return pltpu.make_async_remote_copy(
            src_ref=src, dst_ref=dst, send_sem=self.send.at[way, q, hop], recv_sem=self.recv.at[way, q, hop],
            device_id={"rows": self.z + 1 if way == 0 else self.z - 1}, device_id_type=MESH)

    def sends(self, way):
        return self.z < self.n - 1 if way == 0 else self.z > 0

    def hears(self, way):
        return self.z > 0 if way == 0 else self.z < self.n - 1


class Gather(Line):
    def __init__(self, section, z, n, y, full, load, cross, send, recv):
        super().__init__(section, z, n, full.shape[0], send, recv)
        self.full = full
        self.here = pltpu.make_async_copy(y.at[0], full.at[:, z, section], load)
        self.cross = to_core(y.at[1], full.at[:, z, section], (cross.at[0], cross.at[1]), section)

    def hop(self, way, q, hop):
        piece = self.full.at[q, self.source(way, hop)]
        return self.move(way, q, hop, piece, piece)

    def source(self, way, hop):
        return self.z - hop if way == 0 else self.z + hop

    def known(self, way, hop):
        at = self.source(way, hop)
        return at >= 0 if way == 0 else at < self.n

    def begin(self):
        self.here.start()
        self.cross.start()

    def ready(self):
        self.here.wait()
        self.cross.wait_recv()

    def own(self, q):
        for way in range(2):
            @pl.when(self.sends(way))
            def _():
                self.hop(way, q, 0).start()

    def step(self, q, hop):
        for way in range(2):
            @pl.when(self.known(way, hop + 1))
            def _():
                piece = self.full.at[q, self.source(way, hop + 1)]
                self.move(way, q, hop, piece, piece).wait_recv()

                @pl.when(self.sends(way))
                def _():
                    self.hop(way, q, hop + 1).start()

    def tick(self, t):
        if isinstance(t, int) and t == 0:
            self.own(0)
        guard(t + 1 < self.chunks, lambda: self.own(t + 1))
        for hop in range(self.n - 1):
            q = t - hop - 1
            if isinstance(q, int):
                valid = 0 <= q < self.chunks
            else:
                valid = q < self.chunks
            guard(valid, functools.partial(self.step, q, hop))

    def finish(self):
        self.cross.wait_send()

        def body(q, carry):
            for way in range(2):
                for hop in range(self.n - 1):
                    @pl.when(jnp.logical_and(self.sends(way), self.known(way, hop)))
                    def _():
                        self.hop(way, q, hop).wait_send()
            return carry

        lax.fori_loop(0, self.chunks, body, 0)


class Reduce(Line):
    def __init__(self, section, z, n, part, come, f_out, f_sem, send, recv):
        super().__init__(section, z, n, part.shape[1], send, recv)
        self.part, self.come, self.f_out, self.f_sem = part, come, f_out, f_sem

    def owner(self, way, hop):
        return self.z + self.n - hop if way == 0 else self.z - self.n + hop

    def valid(self, way, hop):
        return self.z <= hop - 1 if way == 0 else self.z >= self.n - hop

    def sent(self, way, q, hop):
        return self.move(way, q, hop, self.part.at[self.owner(way, hop), q], self.come.at[way, q, hop])

    def heard(self, way, q, hop):
        come = self.come.at[way, q, hop]
        self.move(way, q, hop, come, come).wait_recv()

    def step(self, q, hop):
        for way in range(2):
            @pl.when(self.valid(way, hop))
            def _():
                if hop > 1:
                    @pl.when(self.hears(way))
                    def _():
                        self.heard(way, q, hop - 1)
                        owner = self.owner(way, hop)
                        self.part[owner, q] = self.part[owner, q] + self.come[way, q, hop - 1]

                self.sent(way, q, hop).start()

    def result(self, q):
        return pltpu.make_async_copy(self.part.at[self.z, q], self.f_out.at[q], self.f_sem.at[q])

    def final(self, q):
        for way in range(2):
            @pl.when(self.hears(way))
            def _():
                self.heard(way, q, self.n - 1)
                self.part[self.z, q] = self.part[self.z, q] + self.come[way, q, self.n - 1]

        self.result(q).start()

    def tick(self, t):
        for hop in range(1, self.n + 1):
            q = t - hop + 1
            if isinstance(q, int):
                valid = 0 <= q < self.chunks
            else:
                valid = q < self.chunks
            guard(valid, functools.partial(self.step, q, hop) if hop < self.n else functools.partial(self.final, q))

    def finish(self):
        def body(q, carry):
            self.result(q).wait()
            for way in range(2):
                for hop in range(1, self.n):
                    @pl.when(self.valid(way, hop))
                    def _():
                        self.sent(way, q, hop).wait_send()
            return carry

        lax.fori_loop(0, self.chunks, body, 0)


def fetch(src, dst, sem, parts=4):
    step = dst.shape[0] // parts
    for i in range(parts):
        pltpu.make_async_copy(src.at[pl.ds(i * step, step)], dst.at[pl.ds(i * step, step)], sem).start()


def arrived(dst, sem):
    pltpu.make_async_copy(dst, dst, sem).wait()


def portions(total, count):
    return [(i * total // count, (i + 1) * total // count) for i in range(count)]


def conv_rows(weight, bias, a, out, first, last):
    channels, width = a.shape[1:]
    block = weight.shape[0] // channels

    def body(i, carry):
        at = pl.ds(i * block, block)
        high, low = split(a[at].reshape(block * channels, width))
        result = dot(weight[...], jnp.concatenate([high, high, low], 0)).reshape(block, channels, width)
        out[at] = result + bias[...][None] if bias is not None else out[at] + result
        return carry

    lax.fori_loop(first, last, body, 0)


def grad_rows(a, gz, cg_ref, bg_ref, first, last):
    channels, width = a.shape[1:]

    def body(r, carry):
        grad, bias = carry
        g = gz[r]
        left = jnp.concatenate(split(a[r]), 0)
        right = jnp.concatenate(split(g), 0)
        return grad + dot(left, right, (((1,), (1,)), ((), ()))), bias + g

    zero = (jnp.zeros(cg_ref.shape, F32), jnp.zeros(bg_ref.shape, F32))
    grad, bias = lax.fori_loop(first, last, body, zero if first == 0 else (cg_ref[...], bg_ref[...]))
    cg_ref[...] = grad
    bg_ref[...] = bias


def chunk_of(ref, q, count):
    rows, _, width = ref.shape
    return ref[:, pl.ds(pl.multiple_of(q * count, count), count), :].reshape(rows * count, width)


def chunk_at(ref, q, count):
    return ref.at[:, pl.ds(pl.multiple_of(q * count, count), count), :]


class Modes:
    def __init__(self, section, buffer, p_out, local, cross):
        self.section, self.buffer, self.p_out, self.local, self.cross = section, buffer, p_out, local, cross

    def view(self, q):
        n, halves, kx, count, lanes = self.buffer.shape[1:]
        return self.buffer.at[q].reshape(n * halves * kx, count, lanes)

    def copies(self, q):
        s = self.section
        return (pltpu.make_async_copy(self.buffer.at[q, :, s], self.p_out.at[:, q, 0], self.local.at[q]),
                to_core(self.buffer.at[q, :, 1 - s], self.p_out.at[:, q, 1],
                        (self.cross.at[0, q], self.cross.at[1, q]), s))

    def start(self, q):
        for copy in self.copies(q):
            copy.start()

    def wait(self, q):
        for copy in self.copies(q):
            copy.wait()


class Bound:
    def __init__(self, section, owner, micro, other, source, bound, local, cross):
        self.section, self.owner, self.micro, self.other = section, owner, micro, other
        self.source, self.bound, self.local, self.cross = source, bound, local, cross

    def copies(self, q, count, micro):
        src, dst = chunk_at(self.source, q, count), chunk_at(self.bound.at[micro], q, count)
        return (pltpu.make_async_copy(src, dst, self.local.at[q]),
                to_core(src, dst, (self.cross.at[0, q], self.cross.at[1, q]), self.section))

    def start(self, q, count):
        here, there = self.copies(q, count, self.micro)

        @pl.when(self.section == self.owner)
        def _():
            here.start()

        @pl.when(self.section != self.owner)
        def _():
            there.start()

    def wait(self, q, count):
        here, there = self.copies(q, count, self.micro)
        come = self.copies(q, count, self.other)[1]

        @pl.when(self.section == self.owner)
        def _():
            here.wait()
            come.wait_recv()

        @pl.when(self.section != self.owner)
        def _():
            there.wait_send()


def add_squares(value, total):
    rows, _, width = total.shape
    square = (value * value).reshape(rows, -1, width)
    for at in range(0, square.shape[1], G):
        total[...] += square[:, at:at + G]


def region_sums(rid_ref, eo, eb, stat_ref):
    rows, _, width = eo.shape
    rid = rid_ref[...]
    energies = (jnp.sum(eo[...], axis=1), jnp.sum(eb[...], axis=1), jnp.ones((rows, width), F32))
    for kind in range(3):
        for region in range(R):
            line = jnp.sum(jnp.where(rid == region + 1, energies[kind], 0.0), axis=0, keepdims=True)
            total = line[:, :128]
            for piece in range(1, width // 128):
                total = total + line[:, piece * 128:(piece + 1) * 128]
            stat_ref[kind, region:region + 1, :] = total


def start_kernel(per_core, r):
    section, z, n = place_and_peers()
    chunks, count, half = r.p_buf.shape[1], r.p_buf.shape[5], r.far.shape[0]
    blocks = [(j, q) for j in range(per_core) for q in range(chunks)]
    reduce = Reduce(section, z, n, r.part, r.come, r.f_out, r.f_sem, r.red_send, r.red_recv)
    outs = [r.part] + [getattr(r, f"p{j}") for j in range(1, per_core)]
    modes = [Modes(section, r.p_buf.at[j], outs[j], r.p_local.at[j], r.p_cross.at[j]) for j in range(per_core)]

    def field(k):
        j, q = blocks[k]
        src = chunk_at(r.inputs.at[section * per_core + j, 0], q, count)
        return pltpu.make_async_copy(src, r.a_buf.at[k % 2], r.a_sem.at[k % 2])

    def weight_in(x):
        return pltpu.make_async_copy(r.weights.at[0, (1 - section) * half + x], r.w_buf.at[x % 2], r.w_sem.at[x % 2])

    def weight_out(x):
        return to_core(r.w_buf.at[x % 2], r.far.at[x], (r.w_cross.at[0, x], r.w_cross.at[1, x]), section)

    def lend(x):
        if x < half:
            weight_in(x).wait()
            weight_out(x).start()
        if 1 <= x <= half:
            weight_out(x - 1).wait_send()
            if x + 1 < half:
                weight_in(x + 1).start()

    field(0).start()
    for x in range(min(2, half)):
        weight_in(x).start()
    greet(section, z, n, True)
    for k, (j, q) in enumerate(blocks):
        if k + 1 < len(blocks):
            field(k + 1).start()
        field(k).wait()
        to_modes(flat(r.a_buf.at[k % 2]), r.table[...], r.kron[...], r.spread, modes[j].view(q))
        modes[j].start(q)
        lend(k)
        if k >= 1:
            if k <= chunks:
                modes[0].wait(k - 1)
            reduce.tick(k - 1)
    for k in range(len(blocks), half + 1):
        lend(k)
    for t in range(len(blocks) - 1, chunks + n - 1):
        reduce.tick(t)
    for x in range(half):
        weight_out(x).wait_recv()
    for j, q in blocks[chunks:]:
        modes[j].wait(q)
    reduce.finish()


def stage_kernel(kind, j, per_core, r):
    section, z, n = place_and_peers()
    micro, other = section * per_core + j, (1 - section) * per_core + j
    forward, last = kind in ("middle", "turn"), kind == "tail"
    chunks, count, lanes = r.full.shape[0], r.full.shape[4], r.full.shape[5]
    gather = Gather(section, z, n, r.y, r.full, r.load, r.cross, r.send, r.recv)
    reduce = None
    if hasattr(r, "part"):
        reduce = Reduce(section, z, n, r.part, r.come, r.f_out, r.f_sem, r.red_send, r.red_recv)
        fetch(r.p_in, r.part, r.part_sem)
    if forward:
        fetch(r.a_in.at[micro, 0] if kind == "middle" else r.a_in, r.a, r.a_sem)
        if kind == "turn":
            fetch(r.cot_in.at[micro, 0], r.cot, r.c_sem)
        rid_copy = pltpu.make_async_copy(r.rid_in.at[micro, 0], r.rid, r.rid_sem)
        rid_copy.start()
    else:
        fetch(r.gz_in, r.gz, r.gz_sem)
        fetch(r.g_in if last else r.g_in.at[micro, 0], r.h, r.h_sem)
        fetch(r.a_in.at[micro, 0] if last else r.a_in, r.a, r.a_sem)
        if not last:
            fetch(r.dg_in, r.dg, r.dg_sem)
    greet(section, z, n, True)
    gather.begin()
    if reduce is not None:
        arrived(r.part, r.part_sem)
        reduce.tick(0)
    gather.ready()
    gather.tick(0)
    if forward:
        r.eo[...] = jnp.zeros_like(r.eo)
        r.eb[...] = jnp.zeros_like(r.eb)
        arrived(r.a, r.a_sem)
    else:
        arrived(r.gz, r.gz_sem)
        arrived(r.h, r.h_sem)

    rows, channels = r.a.shape[:2]
    conv_blocks = rows // (r.weight.shape[0] // channels)
    if forward:
        work = [functools.partial(conv_rows, r.weight, r.bias, r.a, r.z_buf, *span)
                for span in portions(conv_blocks, n - 1)]
    else:
        work = [functools.partial(conv_rows, r.weight, None, r.gz, r.h, 0, conv_blocks)]
        spans = portions(rows, n - 2)
        work += [functools.partial(grad_rows, r.a, r.gz, r.cg, r.bg, *span) for span in spans]
    for t in range(n - 1):
        if t > 0:
            if reduce is not None:
                reduce.tick(t)
            gather.tick(t)
        if not forward and t == 1:
            arrived(r.a, r.a_sem)
        work[t]()
    if kind == "turn":
        arrived(r.cot, r.c_sem)
    if kind == "back":
        arrived(r.dg, r.dg_sem)

    if not last:
        modes = Modes(section, r.p_buf, r.p_out, r.p_local, r.p_cross)
    if kind == "turn":
        bound = Bound(section, 1, micro, other, r.a, r.bound, r.b_local, r.b_cross)
    if last:
        bound = Bound(section, 0, micro, other, r.h, r.bound, r.b_local, r.b_cross)

    def saves(q):
        pairs = {"middle": lambda: [(r.a, r.a_out), (r.z_buf, r.dg_out)], "turn": lambda: [(r.cot, r.gz_out)],
                 "back": lambda: [(r.h, r.ga_out), (r.dg, r.gz_out)], "tail": lambda: []}[kind]()
        return [pltpu.make_async_copy(chunk_at(src, q, count), chunk_at(dst, q, count), r.out_sem.at[i, q])
                for i, (src, dst) in enumerate(pairs)]

    def body(q, carry):
        if reduce is not None:
            reduce.tick(q + n - 1)
        gather.tick(q + n - 1)
        spectral = from_modes(r.full.at[q].reshape(-1, count, lanes), r.itable[...], r.ikron[...], r.spread)
        if forward:
            branch, slope = gelu_parts(spectral + chunk_of(r.z_buf, q, count))
            if kind == "turn":
                put(chunk_at(r.cot, q, count), chunk_of(r.cot, q, count) * slope)
            else:
                put(chunk_at(r.z_buf, q, count), slope)
            add_squares(branch, r.eb)
            out = chunk_of(r.a, q, count) + branch
            put(chunk_at(r.a, q, count), out)
            add_squares(out, r.eo)
            source = r.cot if kind == "turn" else r.a
        else:
            ga = spectral + chunk_of(r.h, q, count)
            put(chunk_at(r.h, q, count), ga)
            if not last:
                put(chunk_at(r.dg, q, count), ga * chunk_of(r.dg, q, count))
                source = r.dg
        for copy in saves(q):
            copy.start()
        if kind in ("turn", "tail"):
            bound.start(q, count)
        if not last:
            to_modes(chunk_of(source, q, count), r.table[...], r.kron[...], r.spread, modes.view(q))
            modes.start(q)
        return carry

    lax.fori_loop(0, chunks, body, 0)
    if forward:
        rid_copy.wait()
        region_sums(r.rid, r.eo, r.eb, r.stat)

    def close(q, carry):
        for copy in saves(q):
            copy.wait()
        if kind in ("turn", "tail"):
            bound.wait(q, count)
        if not last:
            modes.wait(q)
        return carry

    lax.fori_loop(0, chunks, close, 0)
    gather.finish()
    if reduce is not None:
        reduce.finish()


def swap_halves(value):
    return pltpu.roll(value, value.shape[-1] // 2, value.ndim - 1)


def left_lanes(shape):
    return lax.broadcasted_iota(jnp.int32, shape, len(shape) - 1) < shape[-1] // 2


SLOTS = 4


def weight_stream(own, base, local_ref, far_ref, wbuf, sem):
    step, count = pl.program_id(0), pl.num_programs(0)

    def begin(at):
        slot = lax.rem(at, SLOTS)

        @pl.when(own)
        def _():
            fetch(local_ref.at[0, base + at], wbuf.at[slot], sem.at[slot])

        @pl.when(jnp.logical_not(own))
        def _():
            fetch(far_ref.at[at], wbuf.at[slot], sem.at[slot])

    @pl.when(step == 0)
    def _():
        for at in range(SLOTS - 1):
            @pl.when(at < count)
            def _():
                begin(at)

    @pl.when(step + SLOTS - 1 < count)
    def _():
        begin(step + SLOTS - 1)

    slot = lax.rem(step, SLOTS)
    arrived(wbuf.at[slot], sem.at[slot])
    return wbuf.at[slot]


def pieces(array):
    return [array[at:at + G] for at in range(0, array.shape[0], G)]


def spread_row(tile, row):
    return jnp.broadcast_to(tile[row:row + 1], tile.shape)


def mix_kernel(m_ref, f_ref, local_ref, far_ref, y_ref, wbuf, f1, f2, sem):
    weight = weight_stream(m_ref[0] == 1, m_ref[1], local_ref, far_ref, wbuf, sem)
    grids, channels, lanes = f1.shape
    for g in range(grids):
        f1[g] = f_ref[:, g].reshape(channels, lanes)
    f2[...] = swap_halves(f1[...])
    groups = channels // G

    def body(block, acc):
        at = pl.multiple_of(block * G, G)
        acc = list(acc)
        tiles = [f[g, pl.ds(at, G), :] for g in range(grids) for f in (f1, f2)]
        for u in range(G):
            rows = [spread_row(tile, u) for tile in tiles]
            for o in range(groups):
                w = weight[at + u, o * G:(o + 1) * G, :]
                for k, row in enumerate(rows):
                    acc[k * groups + o] = acc[k * groups + o] + row * w
        return tuple(acc)

    acc = lax.fori_loop(0, groups, body, tuple(jnp.zeros((G, lanes), F32) for _ in range(2 * grids * groups)))
    left = left_lanes((channels, lanes))
    for g in range(grids):
        a, b = [jnp.concatenate(acc[k * groups:(k + 1) * groups], 0) for k in (2 * g, 2 * g + 1)]
        y_ref[g] = jnp.where(left, a - swap_halves(a), b + swap_halves(b)).reshape(y_ref.shape[1:])


def mix_t_kernel(m_ref, d_ref, local_ref, far_ref, y_ref, wbuf, a1, a2, sem):
    weight = weight_stream(m_ref[0] == 1, m_ref[1], local_ref, far_ref, wbuf, sem)
    grids, channels, lanes = a1.shape
    d = [d_ref[:, g].reshape(channels, lanes) for g in range(grids)]
    d1 = [pieces(d[g]) for g in range(grids)]
    d2 = [pieces(swap_halves(d[g])) for g in range(grids)]
    groups = channels // G

    def body(block, carry):
        at = pl.multiple_of(block * G, G)
        rows = [[] for _ in range(2 * grids)]
        for u in range(G):
            total = [None] * (2 * grids)
            for o in range(groups):
                w = weight[at + u, o * G:(o + 1) * G, :]
                for g in range(grids):
                    for side, source in enumerate((d1, d2)):
                        term = w * source[g][o]
                        k = 2 * g + side
                        total[k] = term if total[k] is None else total[k] + term
            for k in range(2 * grids):
                rows[k].append(jnp.sum(total[k], axis=0, keepdims=True))
        for g in range(grids):
            a1[g, pl.ds(at, G), :] = jnp.concatenate(rows[2 * g], 0)
            a2[g, pl.ds(at, G), :] = jnp.concatenate(rows[2 * g + 1], 0)
        return carry

    lax.fori_loop(0, groups, body, 0)
    left = left_lanes((channels, lanes))
    for g in range(grids):
        a, b = a1[g], a2[g]
        y_ref[g] = jnp.where(left, a + swap_halves(a), swap_halves(b) - b).reshape(y_ref.shape[1:])


def grad_tables(f_ref, d_ref, f1, fs, d1, ds):
    channels, lanes = f1.shape[1:]
    left = left_lanes((channels // 2, lanes))
    at = 0
    for stream in range(f_ref.shape[0]):
        for member in range(f_ref.shape[1]):
            for g in range(f_ref.shape[3]):
                f = f_ref[stream, member, :, g].reshape(channels, lanes)
                f1[at] = f
                less = f - swap_halves(f)
                fs[at] = jnp.where(left, less[:channels // 2], -less[channels // 2:])
                d = d_ref[stream, member, :, g].reshape(channels, lanes)
                d1[at] = d
                ds[at] = d + swap_halves(d)
                at += 1


def grad_block(first_row, f1, fs, d1, ds, out):
    count, channels, lanes = f1.shape
    groups, middle = channels // G, channels // 2
    left = left_lanes((G, lanes))

    def body(octet, carry):
        at = pl.multiple_of(octet * G, G)
        low = pl.multiple_of(first_row + at, G)
        rows = (pl.ds(low, G), pl.ds(pl.multiple_of(middle + low, G), G))
        for first in range(0, G, 2):
            acc = [[None] * groups for _ in range(6)]
            for g in range(count):
                tiles = (f1[g, rows[0], :], f1[g, rows[1], :], fs[g, rows[0], :])
                factors = [spread_row(tile, first + u) for u in range(2) for tile in tiles]
                for o in range(groups):
                    d, e = d1[g, o * G:(o + 1) * G, :], ds[g, o * G:(o + 1) * G, :]
                    for k, factor in enumerate(factors):
                        term = factor * (e if k % 3 == 2 else d)
                        acc[k][o] = term if acc[k][o] is None else acc[k][o] + term
            for u in range(2):
                for o in range(groups):
                    p = acc[3 * u + 2][o]
                    for side in range(2):
                        m = acc[3 * u + side][o]
                        n = swap_halves(m)
                        third = swap_halves(p) if side == 0 else p
                        out[side, at + first + u, o * G:(o + 1) * G, :] = jnp.where(left, m + n, m - n + third)
        return carry

    lax.fori_loop(0, out.shape[1] // G, body, 0)


class GradInput:
    def __init__(self, first, f, g, fbuf, gbuf, sem):
        self.first, self.f, self.g, self.fbuf, self.gbuf, self.sem = first, f, g, fbuf, gbuf, sem

    def load(self, x, slot):
        for layer, condition in enumerate((self.first, jnp.logical_not(self.first))):
            @pl.when(condition)
            def _():
                for j in range(len(self.f[layer])):
                    pltpu.make_async_copy(self.f[layer][j].at[:, :, :, x], self.fbuf.at[slot, j],
                                          self.sem.at[0, slot]).start()
                    pltpu.make_async_copy(self.g[layer][j].at[:, :, :, x], self.gbuf.at[slot, j],
                                          self.sem.at[1, slot]).start()

    def next(self, x, count):
        slot = lax.rem(x, 2)

        @pl.when(x + 1 < count)
        def _():
            self.load(x + 1, 1 - slot)

        arrived(self.fbuf.at[slot], self.sem.at[0, slot])
        arrived(self.gbuf.at[slot], self.sem.at[1, slot])
        return self.fbuf.at[slot], self.gbuf.at[slot]


def grad_input(r, first, per_core):
    f = [[getattr(r, f"f{layer}{j}") for j in range(per_core)] for layer in range(2)]
    g = [[getattr(r, f"g{layer}{j}") for j in range(per_core)] for layer in range(2)]
    return GradInput(first, f, g, r.fbuf, r.gbuf, r.in_sem)


def far_grad_kernel(per_core, r):
    section, z, n = place_and_peers()
    half = r.far.shape[0]
    block = r.out.shape[2]
    blocks = r.far.shape[2] // block
    source = grad_input(r, section != 0, per_core)

    def move(k, slot):
        x, i = k // blocks, k % blocks
        return to_core(r.out.at[slot], r.far.at[x, :, pl.ds(i * block, block)], (r.send.at[k], r.recv.at[k]), section)

    source.load(0, 0)
    greet(section, z, n, False)

    def body(x, carry):
        grad_tables(*source.next(x, half), r.f1, r.fs, r.d1, r.ds)

        def inner(i, carry):
            k = x * blocks + i

            @pl.when(k >= 2)
            def _():
                move(k - 2, lax.rem(k, 2)).wait_send()

            grad_block(i * block, r.f1, r.fs, r.d1, r.ds, r.out.at[lax.rem(k, 2)])
            move(k, lax.rem(k, 2)).start()
            return carry

        return lax.fori_loop(0, blocks, inner, carry)

    lax.fori_loop(0, half, body, 0)
    total = half * blocks
    for k in (total - 2, total - 1):
        move(k, k % 2).wait_send()

    def close(k, carry):
        move(k, 0).wait_recv()
        return carry

    lax.fori_loop(0, total, close, 0)


def own_grad_kernel(names, per_core, m_ref, *refs):
    r = types.SimpleNamespace(**dict(zip(names, refs)))
    x, i = pl.program_id(0), pl.program_id(1)
    source = grad_input(r, m_ref[0] == 0, per_core)

    @pl.when(i == 0)
    def _():
        @pl.when(x == 0)
        def _():
            source.load(0, 0)

        grad_tables(*source.next(x, pl.num_programs(0)), r.f1, r.fs, r.d1, r.ds)

    r.bound_out[...] = r.bound_in[...]
    r.out[1 - m_ref[0]] = r.far[...]
    grad_block(i * r.out.shape[2], r.f1, r.fs, r.d1, r.ds, r.out.at[m_ref[0]])


def whole(array):
    return pl.BlockSpec(array.shape, lambda *_: (0,) * array.ndim)


def params(**kw):
    return pltpu.CompilerParams(vmem_limit_bytes=VMEM_LIMIT, **kw)


def local(inputs, cotangent, region_id, spectral_w, conv_w, bias_vector):
    micro_count, _, rows_dev, channels, width = inputs.shape
    lanes = spectral_w.shape[-1]
    half = lanes // 2
    kx_dev = spectral_w.shape[1]
    row_devices, sections = lax.axis_size("rows"), lax.axis_size("section")
    mode_rows, height = kx_dev * row_devices, rows_dev * row_devices
    section = lax.axis_index("section")
    per_core = micro_count // sections
    kx_half = kx_dev // sections

    plain, doubled = col_tables(width, half)

    def stacked(array):
        high, low = np_split(array)
        return np.concatenate([high, high, low], 0)

    t_plain, t_doubled, it_plain, it_doubled = [stacked(t) for t in (plain, doubled, plain.T, doubled.T)]
    kron, ikron = row_tables(height, mode_rows, lax.axis_index("rows") * rows_dev, rows_dev)

    count = 2 * G
    chunks = channels // count
    hbm, vmem = pl.BlockSpec(memory_space=pl.ANY), pl.BlockSpec(memory_space=pltpu.VMEM)
    field_shape = jax.ShapeDtypeStruct((rows_dev, channels, width), F32)
    part_dims = (row_devices, chunks, sections, kx_half, count, lanes)
    p_shape, f_shape = jax.ShapeDtypeStruct(part_dims, F32), jax.ShapeDtypeStruct(part_dims[1:], F32)
    y_shape = jax.ShapeDtypeStruct((sections, chunks, kx_half, count, lanes), F32)
    stat_shape = jax.ShapeDtypeStruct((3, R, 128), F32)
    cg_shape = jax.ShapeDtypeStruct((2 * channels, 2 * channels), F32)
    bg_shape = jax.ShapeDtypeStruct((channels, width), F32)
    bound_shape = jax.ShapeDtypeStruct((micro_count, rows_dev, channels, width), F32)
    dma = pltpu.SemaphoreType.DMA
    field_buf = pltpu.VMEM((rows_dev, channels, width), F32)
    full_dims = (chunks, row_devices, sections, kx_half, count, lanes)
    spread = pltpu.VMEM((width // 128, rows_dev * count, 128), F32)
    energy = pltpu.VMEM((rows_dev, G, width), F32)
    line_sems = dma((2, chunks, row_devices))
    reduce_scratch = dict(part=pltpu.VMEM(part_dims, F32), come=pltpu.VMEM((2, chunks) + (row_devices,) + part_dims[2:], F32),
                          f_sem=dma((chunks,)), red_send=line_sems, red_recv=line_sems, part_sem=dma)

    def run(body, ident, ins, outs, scratch, cost=50, aliases=None):
        names = [*ins, *outs, *scratch]
        spec = lambda entry: vmem if isinstance(entry, tuple) else hbm
        plain = lambda entry: entry[0] if isinstance(entry, tuple) else entry
        kernel = lambda *refs: body(types.SimpleNamespace(**dict(zip(names, refs))))
        positions = {list(ins).index(k): list(outs).index(v) for k, v in (aliases or {}).items()}
        result = pl.pallas_call(
            kernel, in_specs=[spec(e) for e in ins.values()], out_specs=[spec(e) for e in outs.values()],
            out_shape=[plain(e) for e in outs.values()], scratch_shapes=list(scratch.values()),
            input_output_aliases=positions,
            cost_estimate=pl.CostEstimate(flops=0, bytes_accessed=cost * 3_000_000, transcendentals=0),
            compiler_params=params(collective_id=ident, has_side_effects=True))(*[plain(e) for e in ins.values()])
        return types.SimpleNamespace(**dict(zip(outs, result)))

    conv_rows_at_once = 256 // channels
    conv_both = lax.all_gather(conv_w, "section", axis=0, tiled=True)
    bias_both = lax.all_gather(bias_vector, "section", axis=0, tiled=True)

    def conv_parts(matrix):
        wide = jnp.kron(jnp.eye(conv_rows_at_once, dtype=F32), matrix)
        rounded = lax.reduce_precision(wide, 8, 7)
        high, low = rounded.astype(BF16), (wide - rounded).astype(BF16)
        return jnp.concatenate([high, low, high], 1)

    conv_fwd = [conv_parts(conv_both[l].T) for l in range(2)]
    conv_bwd = [conv_parts(conv_both[l]) for l in range(2)]
    bias_wide = [jnp.broadcast_to(bias_both[l][:, None], (channels, width)) for l in range(2)]

    def mixing(body, layer, pair):
        flag = jnp.stack([(section == layer).astype(jnp.int32), section * kx_half])
        f_block = pl.BlockSpec((chunks, sections, None, count, lanes), lambda x, m: (0, 0, x, 0, 0))
        y_block = pl.BlockSpec((sections, chunks, None, count, lanes), lambda x, m: (0, 0, x, 0, 0))
        small = pltpu.VMEM((sections, channels, lanes), F32)
        grid_spec = pltpu.PrefetchScalarGridSpec(
            num_scalar_prefetch=1, grid=(kx_half,), in_specs=[f_block, hbm, hbm], out_specs=y_block,
            scratch_shapes=[pltpu.VMEM((SLOTS, channels, channels, lanes), F32), small, small, dma((SLOTS,))])
        return pl.pallas_call(
            body, grid_spec=grid_spec, out_shape=y_shape, compiler_params=params(),
            cost_estimate=pl.CostEstimate(flops=0, bytes_accessed=30_000_000, transcendentals=0))(
                flag, pair, spectral_w, far_weights)

    streams = range(per_core)
    start = run(
        functools.partial(start_kernel, per_core), 0,
        dict(inputs=inputs, weights=spectral_w, table=(t_plain,), kron=(kron,)),
        dict(f_out=f_shape, far=jax.ShapeDtypeStruct((kx_half,) + spectral_w.shape[2:], F32),
             **{f"p{j}": p_shape for j in streams[1:]}),
        dict(a_buf=pltpu.VMEM((2, rows_dev, count, width), F32), w_buf=pltpu.VMEM((2,) + spectral_w.shape[2:], F32),
             p_buf=pltpu.VMEM((per_core,) + full_dims, F32), spread=spread, a_sem=dma((2,)), w_sem=dma((2,)),
             w_cross=dma((2, kx_half)), p_local=dma((per_core, chunks)), p_cross=dma((per_core, 2, chunks)),
             **reduce_scratch))
    far_weights = start.far

    kinds = ["middle", "turn", "back", "tail"]
    mixes = [(mix_kernel, 0), (mix_kernel, 1), (mix_t_kernel, 1), (mix_t_kernel, 0)]
    names = ["f0", "f1", "g1", "g0"]
    sums = [[None] * per_core for _ in kinds]
    sums[0][0] = start.f_out
    gathered, waiting = {}, [None, ("f00", lax.all_gather(start.f_out, "batch", axis=0))]
    parts = [getattr(start, f"p{j}", None) for j in streams]
    kept = [types.SimpleNamespace() for _ in streams]
    bound, calls = None, 0
    for phase, kind in enumerate(kinds):
        for j in streams:
            y = mixing(*mixes[phase], sums[phase][j])
            keep = kept[j]
            ins, outs = dict(y=y), {}
            scratch = dict(full=pltpu.VMEM(full_dims, F32), spread=spread, load=dma, cross=dma((2,)),
                           send=line_sems, recv=line_sems, a=field_buf, a_sem=dma)
            aliases = {}
            if kind == "middle":
                ins.update(a_in=inputs, rid_in=region_id, weight=(conv_fwd[0],), bias=(bias_wide[0],))
                outs.update(a_out=field_shape, dg_out=field_shape, stat=(stat_shape,))
            elif kind == "turn":
                ins.update(a_in=keep.a1, rid_in=region_id, cot_in=cotangent, weight=(conv_fwd[1],), bias=(bias_wide[1],))
                outs.update(gz_out=field_shape, stat=(stat_shape,), bound=bound_shape)
                scratch.update(cot=field_buf, c_sem=dma)
            elif kind == "back":
                ins.update(a_in=keep.a1, gz_in=keep.gz1, g_in=cotangent, dg_in=keep.dg0, weight=(conv_bwd[1],))
                outs.update(ga_out=field_shape, gz_out=field_shape, cg=(cg_shape,), bg=(bg_shape,))
                scratch.update(dg=field_buf, dg_sem=dma)
            else:
                ins.update(a_in=inputs, gz_in=keep.gz0, g_in=keep.ga1, weight=(conv_bwd[0],))
                outs.update(cg=(cg_shape,), bg=(bg_shape,), bound=bound_shape)
            if kind in ("middle", "turn"):
                scratch.update(z_buf=field_buf, rid=pltpu.VMEM((rows_dev, width), jnp.int32), rid_sem=dma,
                               eo=energy, eb=energy)
            else:
                scratch.update(gz=field_buf, h=field_buf, gz_sem=dma, h_sem=dma)
            ins.update(itable=(it_doubled if kind in ("middle", "turn") else it_plain,), ikron=(ikron,))
            if kind != "tail":
                ins.update(table=(t_plain if kind == "middle" else t_doubled,), kron=(kron,))
                outs.update(p_out=p_shape)
                scratch.update(p_buf=pltpu.VMEM(full_dims, F32), p_local=dma((chunks,)), p_cross=dma((2, chunks)),
                               out_sem=dma((2, chunks)))
            if kind in ("turn", "tail"):
                scratch.update(b_local=dma((chunks,)), b_cross=dma((2, chunks)))
                if bound is not None:
                    ins.update(bound_in=bound)
                    aliases = dict(bound_in="bound")
            follow = (j + 1) % per_core
            follow_phase = phase + (1 if follow == 0 else 0)
            if follow_phase < len(kinds):
                ins.update(p_in=parts[follow])
                outs.update(f_out=f_shape)
                scratch.update(reduce_scratch)
            early = waiting.pop(0)
            if early is not None:
                ins.update(held=early[1])
                gathered[early[0]] = early[1]
            done = run(functools.partial(stage_kernel, kind, j, per_core), 1 + calls, ins, outs, scratch, aliases=aliases)
            calls += 1
            if kind != "tail":
                parts[j] = done.p_out
            if follow_phase < len(kinds):
                sums[follow_phase][follow] = done.f_out
                waiting.append((f"{names[follow_phase]}{follow}", lax.all_gather(done.f_out, "batch", axis=0)))
            if kind in ("turn", "tail"):
                bound = done.bound
            if kind == "middle":
                keep.a1, keep.dg0, keep.stat0 = done.a_out, done.dg_out, done.stat
            elif kind == "turn":
                keep.gz1, keep.stat1 = done.gz_out, done.stat
            elif kind == "back":
                keep.ga1, keep.gz0, keep.cg1, keep.bg1 = done.ga_out, done.gz_out, done.cg, done.bg
            else:
                keep.cg0, keep.bg0 = done.cg, done.bg
    stats0, stats1, cg0, cg1, bg0, bg1 = [[getattr(k, name) for k in kept]
                                          for name in ("stat0", "stat1", "cg0", "cg1", "bg0", "bg1")]

    gathered.update(waiting)
    members = lax.axis_size("batch")
    grids = per_core * members * sections
    block = G
    blocks = channels // 2 // block
    in_buf = pltpu.VMEM((2, per_core, members, chunks, sections, count, lanes), F32)
    big, small = pltpu.VMEM((grids, channels, lanes), F32), pltpu.VMEM((grids, channels // 2, lanes), F32)
    grad_scratch = dict(fbuf=in_buf, gbuf=in_buf, in_sem=dma((2, 2)), f1=big, fs=small, d1=big, ds=big)
    row_dims = (2, channels // 2, channels, lanes)
    far_grad = run(functools.partial(far_grad_kernel, per_core), 1 + calls, gathered,
                   dict(far=jax.ShapeDtypeStruct((kx_half,) + row_dims, F32)),
                   dict(out=pltpu.VMEM((2, 2, block, channels, lanes), F32), send=dma((kx_half * blocks,)),
                        recv=dma((kx_half * blocks,)), **grad_scratch)).far
    bound_rows = bound.reshape(micro_count * rows_dev, channels, width)
    bound_block = pl.BlockSpec((bound_rows.shape[0] // (kx_half * blocks), channels, width),
                               lambda x, i, m: (x * blocks + i, 0, 0))
    grid_spec = pltpu.PrefetchScalarGridSpec(
        num_scalar_prefetch=1, grid=(kx_half, blocks),
        in_specs=[hbm] * len(gathered)
        + [pl.BlockSpec((None, 2, block, channels, lanes), lambda x, i, m: (x, 0, i, 0, 0)), bound_block],
        out_specs=[pl.BlockSpec((2, None, 2, block, channels, lanes), lambda x, i, m: (0, x, 0, i, 0, 0)), bound_block],
        scratch_shapes=list(grad_scratch.values()))
    spectral_grad, boundary = pl.pallas_call(
        functools.partial(own_grad_kernel, [*gathered, "far", "bound_in", "out", "bound_out", *grad_scratch], per_core),
        grid_spec=grid_spec, out_shape=[jax.ShapeDtypeStruct((2, kx_half) + row_dims, F32),
                                        jax.ShapeDtypeStruct(bound_rows.shape, F32)],
        cost_estimate=pl.CostEstimate(flops=0, bytes_accessed=150_000_000, transcendentals=0),
        compiler_params=params())(
            jnp.reshape(section, (1,)).astype(jnp.int32), *gathered.values(), far_grad, bound_rows)
    spectral_grad = spectral_grad.reshape(spectral_w.shape)
    boundary = boundary.reshape((1, micro_count, 1) + inputs.shape[2:])

    def lower(value):
        return (value[:channels, :channels] + value[channels:, channels:]
                + value[:channels, channels:] + value[channels:, :channels])

    conv_local = jnp.stack([lower(sum(cg0)), lower(sum(cg1))])
    bias_local = jnp.stack([jnp.sum(sum(bg0), -1), jnp.sum(sum(bg1), -1)])
    stat_local = jnp.stack([jnp.sum(sum(stats0), -1), jnp.sum(sum(stats1), -1)])
    shapes = [v.shape for v in (conv_local, bias_local, stat_local)]
    flat_sums = jnp.concatenate([v.reshape(-1) for v in (conv_local, bias_local, stat_local)])
    length = flat_sums.shape[0]
    flat_sums = jnp.pad(flat_sums, (0, -length % 1024)).reshape(-1, 128)
    flat_sums = jnp.sum(lax.all_gather(flat_sums, ("section", "batch", "rows"), axis=0), 0).reshape(-1)
    ends = np.cumsum([0] + [math.prod(shape) for shape in shapes])
    conv_sum, bias_sum, stat_sum = [flat_sums[ends[i]:ends[i + 1]].reshape(shapes[i]) for i in range(3)]
    own_stat = lax.dynamic_index_in_dim(stat_sum, section, 0, False)
    layer_rms = jnp.sqrt(own_stat[:2] / (channels * own_stat[2])[None, :] + 1e-06)[None]
    own = lambda value: lax.dynamic_slice_in_dim(value, section, 1, 0)
    return boundary, spectral_grad, own(conv_sum), own(bias_sum), layer_rms


def solution(mesh):
    placed = (
        P(None, "batch", "rows", None, None),
        P(None, "batch", "rows", None, None),
        P(None, "batch", "rows", None),
        P("section", "rows", None, None, None),
        P("section", None, None),
        P("section", None),
    )
    return jax.shard_map(
        local,
        mesh=mesh,
        in_specs=placed,
        out_specs=(
            P("section", None, "batch", "rows", None, None),
            P("section", "rows", None, None, None),
            P("section", None, None),
            P("section", None),
            P("section", None, None),
        ),
        check_vma=False,
    )
```

```python
import functools
import math
import types

import jax
import jax.numpy as jnp
import numpy as np
from jax import lax
from jax.experimental import pallas as pl
from jax.experimental.pallas import tpu as pltpu
from jax.sharding import PartitionSpec as P

R = 8
G = 8
AHEAD = 2
F32 = jnp.float32
BF16 = jnp.bfloat16
VMEM_LIMIT = 56 * 1024 * 1024
MESH = pl.DeviceIdType.MESH


def split(value):
    high = value.astype(BF16)
    return high, (value - high.astype(F32)).astype(BF16)


def dot(left, right, dims=(((1,), (0,)), ((), ()))):
    return lax.dot_general(left, right, dims, preferred_element_type=F32)


def dot3(left, right):
    return dot(left[0], right[0]) + (dot(left[1], right[0]) + dot(left[0], right[1]))


def np_split(value):
    high = value.astype(np.float32).astype(BF16)
    return high, (value - high.astype(np.float64)).astype(np.float32).astype(BF16)


def col_tables(width, half):
    phase = 2.0 * math.pi / width * (np.outer(np.arange(width), np.arange(half)) % width)
    cosine, sine = np.cos(phase) / math.sqrt(width), np.sin(phase) / math.sqrt(width)
    plain = np.concatenate([cosine, -sine, -sine, -cosine], 1)
    doubled = plain * np.tile(np.where(np.arange(half) == 0, 1.0, 2.0), 4)[None, :]
    return plain, doubled


def row_tables(height, mode_rows, first_row, rows_dev):
    position = jnp.arange(mode_rows, dtype=jnp.int32)
    frequency = jnp.where(position < mode_rows // 2, position, height - mode_rows + position)
    row = first_row + jnp.arange(rows_dev, dtype=jnp.int32)
    phase = 2.0 * math.pi / height * (frequency[:, None] * row[None, :] % height).astype(F32)
    small = jnp.concatenate([jnp.cos(phase), jnp.sin(phase)], 1) / math.sqrt(height)
    rounded = lax.reduce_precision(small, 8, 7)
    high, low = rounded.astype(BF16), (small - rounded).astype(BF16)
    forward = jnp.concatenate([jnp.concatenate([high, high], 1), jnp.concatenate([low, jnp.zeros_like(low)], 1)], 0)
    inverse = jnp.concatenate([high.T, high.T, low.T], 1)
    return forward, inverse


def to_modes(value, table, kron, spread, p_ref):
    mode_rows, count, lanes = p_ref.shape
    rows = value.shape[0] // count
    high, low = split(value)
    spectra = dot(jnp.concatenate([high, low, high], 1), table)
    for i in range(2):
        spread[i] = spectra[:, i * lanes:(i + 1) * lanes]
    out = p_ref.reshape(mode_rows * count, lanes)
    for first in range(0, count, 2):
        sides = []
        for c in (first, first + 1):
            pick = pl.ds(c, rows, stride=count)
            sides.append(jnp.concatenate([spread[i, pick, :] for i in range(2)], 0))
        high, low = split(jnp.concatenate(sides, 1))
        both = dot(kron, jnp.concatenate([high, low], 0))
        result = both[:mode_rows] + both[mode_rows:]
        for i in range(2):
            out[pl.ds(first + i, mode_rows, stride=count), :] = result[:, i * lanes:(i + 1) * lanes]


def from_modes(y_ref, table, kron, spread):
    mode_rows, count, lanes = y_ref.shape
    rows, pieces = spread.shape[1] // count, spread.shape[0]
    modes = y_ref.reshape(mode_rows * count, lanes)
    sides = []
    for first in range(0, count, 2):
        pair = [modes[pl.ds(c, mode_rows, stride=count), :] for c in (first, first + 1)]
        high, low = split(jnp.concatenate(pair, 1))
        both = dot(kron, jnp.concatenate([high, low, high], 0))
        for i in range(2):
            side = both[:, i * lanes:(i + 1) * lanes]
            sides.append(jnp.concatenate([side[:rows], side[rows:]], 1))
    high, low = split(jnp.concatenate(sides, 0))
    out = dot(jnp.concatenate([high, low, high], 1), table)
    for c in range(count):
        for i in range(pieces):
            spread[i, pl.ds(c, rows, stride=count), :] = out[c * rows:(c + 1) * rows, i * 128:(i + 1) * 128]
    return jnp.concatenate([spread[i] for i in range(pieces)], 1)


def gelu_parts(z):
    size = jnp.abs(z)
    gauss = jnp.exp(-0.5 * z * z)
    t = 1.0 / (1.0 + (0.3275911 / math.sqrt(2.0)) * size)
    poly = t * (0.254829592 + t * (-0.284496736 + t * (1.421413741 + t * (-1.453152027 + t * 1.061405429))))
    tail = 0.5 * poly * gauss
    phi = jnp.where(z >= 0, 1.0 - tail, tail)
    return z * phi, phi + z * (gauss * (1.0 / math.sqrt(2.0 * math.pi)))


def flat(ref):
    rows, count, width = ref.shape
    return ref[...].reshape(rows * count, width)


def put(ref, value):
    ref[...] = value.reshape(ref.shape)


def place_and_peers():
    section, z = lax.axis_index("section"), lax.axis_index("rows")
    return section, z, lax.axis_size("rows")


def greet(section, z, n, lines):
    barrier = pltpu.get_barrier_semaphore()
    pl.semaphore_signal(barrier, inc=1, device_id={"section": 1 - section}, device_id_type=MESH)
    if not lines:
        pl.semaphore_wait(barrier, 1)
        return

    @pl.when(z > 0)
    def _():
        pl.semaphore_signal(barrier, inc=1, device_id={"rows": z - 1}, device_id_type=MESH)

    @pl.when(z < n - 1)
    def _():
        pl.semaphore_signal(barrier, inc=1, device_id={"rows": z + 1}, device_id_type=MESH)

    pl.semaphore_wait(barrier, 1 + (z > 0).astype(jnp.int32) + (z < n - 1).astype(jnp.int32))


def to_core(src, dst, sems, section):
    return pltpu.make_async_remote_copy(src_ref=src, dst_ref=dst, send_sem=sems[0], recv_sem=sems[1],
                                        device_id={"section": 1 - section}, device_id_type=MESH)


def guard(condition, body):
    if isinstance(condition, (bool, np.bool_)):
        if condition:
            body()
    else:
        pl.when(condition)(body)


class Line:
    def __init__(self, section, z, n, chunks, send, recv):
        self.section, self.z, self.n, self.chunks = section, z, n, chunks
        self.send, self.recv = send, recv

    def move(self, way, q, hop, src, dst):
        return pltpu.make_async_remote_copy(
            src_ref=src, dst_ref=dst, send_sem=self.send.at[way, q, hop], recv_sem=self.recv.at[way, q, hop],
            device_id={"rows": self.z + 1 if way == 0 else self.z - 1}, device_id_type=MESH)

    def sends(self, way):
        return self.z < self.n - 1 if way == 0 else self.z > 0

    def hears(self, way):
        return self.z > 0 if way == 0 else self.z < self.n - 1


class Gather(Line):
    def __init__(self, section, z, n, y, full, load, cross, send, recv):
        super().__init__(section, z, n, full.shape[0], send, recv)
        self.full = full
        self.here = pltpu.make_async_copy(y.at[0], full.at[:, z, section], load)
        self.cross = to_core(y.at[1], full.at[:, z, section], (cross.at[0], cross.at[1]), section)

    def hop(self, way, q, hop):
        piece = self.full.at[q, self.source(way, hop)]
        return self.move(way, q, hop, piece, piece)

    def source(self, way, hop):
        return self.z - hop if way == 0 else self.z + hop

    def known(self, way, hop):
        at = self.source(way, hop)
        return at >= 0 if way == 0 else at < self.n

    def begin(self):
        self.here.start()
        self.cross.start()

    def ready(self):
        self.here.wait()
        self.cross.wait_recv()

    def own(self, q):
        for way in range(2):
            @pl.when(self.sends(way))
            def _():
                self.hop(way, q, 0).start()

    def step(self, q, hop):
        for way in range(2):
            @pl.when(self.known(way, hop + 1))
            def _():
                piece = self.full.at[q, self.source(way, hop + 1)]
                self.move(way, q, hop, piece, piece).wait_recv()

                @pl.when(self.sends(way))
                def _():
                    self.hop(way, q, hop + 1).start()

    def tick(self, t):
        if isinstance(t, int) and t == 0:
            for q in range(min(AHEAD, self.chunks)):
                self.own(q)
        guard(t + AHEAD < self.chunks, lambda: self.own(t + AHEAD))
        for hop in range(self.n - 1):
            q = t - hop - 1
            if isinstance(q, int):
                valid = 0 <= q < self.chunks
            else:
                valid = q < self.chunks
            guard(valid, functools.partial(self.step, q, hop))

    def finish(self):
        self.cross.wait_send()

        def body(q, carry):
            for way in range(2):
                for hop in range(self.n - 1):
                    @pl.when(jnp.logical_and(self.sends(way), self.known(way, hop)))
                    def _():
                        self.hop(way, q, hop).wait_send()
            return carry

        lax.fori_loop(0, self.chunks, body, 0)


class Reduce(Line):
    def __init__(self, section, z, n, part, come, f_out, f_sem, send, recv, ahead):
        super().__init__(section, z, n, part.shape[1], send, recv)
        self.ahead = ahead
        self.part, self.come, self.f_out, self.f_sem = part, come, f_out, f_sem

    def owner(self, way, hop):
        return self.z + self.n - hop if way == 0 else self.z - self.n + hop

    def valid(self, way, hop):
        return self.z <= hop - 1 if way == 0 else self.z >= self.n - hop

    def sent(self, way, q, hop):
        return self.move(way, q, hop, self.part.at[self.owner(way, hop), q], self.come.at[way, q, hop])

    def heard(self, way, q, hop):
        come = self.come.at[way, q, hop]
        self.move(way, q, hop, come, come).wait_recv()

    def first(self, t):
        for hop in range(1, self.n):
            q = t - hop + 1

            def send():
                for way in range(2):
                    @pl.when(jnp.logical_and(self.valid(way, hop), jnp.logical_not(self.hears(way))))
                    def _():
                        self.sent(way, q, hop).start()

            guard(0 <= q < self.chunks if isinstance(q, int) else q < self.chunks, send)

    def step(self, q, hop):
        for way in range(2):
            @pl.when(jnp.logical_and(self.valid(way, hop), self.hears(way)))
            def _():
                self.heard(way, q, hop - 1)
                owner = self.owner(way, hop)
                self.part[owner, q] = self.part[owner, q] + self.come[way, q, hop - 1]
                self.sent(way, q, hop).start()

    def result(self, q):
        return pltpu.make_async_copy(self.part.at[self.z, q], self.f_out.at[q], self.f_sem.at[q])

    def final(self, q):
        for way in range(2):
            @pl.when(self.hears(way))
            def _():
                self.heard(way, q, self.n - 1)
                self.part[self.z, q] = self.part[self.z, q] + self.come[way, q, self.n - 1]

        self.result(q).start()

    def tick(self, t):
        if isinstance(t, int) and t == 0:
            for early in range(self.ahead):
                self.first(early)
        self.first(t + self.ahead)
        for hop in range(2, self.n + 1):
            q = t - hop + 1
            if isinstance(q, int):
                valid = 0 <= q < self.chunks
            else:
                valid = q < self.chunks
            guard(valid, functools.partial(self.step, q, hop) if hop < self.n else functools.partial(self.final, q))

    def finish(self):
        def body(q, carry):
            self.result(q).wait()
            for way in range(2):
                for hop in range(1, self.n):
                    @pl.when(self.valid(way, hop))
                    def _():
                        self.sent(way, q, hop).wait_send()
            return carry

        lax.fori_loop(0, self.chunks, body, 0)


def fetch(src, dst, sem, parts=4):
    step = dst.shape[0] // parts
    for i in range(parts):
        pltpu.make_async_copy(src.at[pl.ds(i * step, step)], dst.at[pl.ds(i * step, step)], sem).start()


def arrived(dst, sem):
    pltpu.make_async_copy(dst, dst, sem).wait()


def portions(total, count):
    return [(i * total // count, (i + 1) * total // count) for i in range(count)]


def conv_rows(weight, bias, a, out, first, last):
    channels, width = a.shape[1:]
    block = weight.shape[0] // channels

    def body(i, carry):
        at = pl.ds(i * block, block)
        high, low = split(a[at].reshape(block * channels, width))
        result = dot(weight[...], jnp.concatenate([high, high, low], 0)).reshape(block, channels, width)
        out[at] = result + bias[...][None] if bias is not None else out[at] + result
        return carry

    lax.fori_loop(first, last, body, 0)


def grad_rows(a, gz, cg_ref, bg_ref, first, last):
    channels, width = a.shape[1:]

    def body(r, carry):
        grad, bias = carry
        g = gz[r]
        left = jnp.concatenate(split(a[r]), 0)
        right = jnp.concatenate(split(g), 0)
        return grad + dot(left, right, (((1,), (1,)), ((), ()))), bias + g

    zero = (jnp.zeros(cg_ref.shape, F32), jnp.zeros(bg_ref.shape, F32))
    grad, bias = lax.fori_loop(first, last, body, zero if first == 0 else (cg_ref[...], bg_ref[...]))
    cg_ref[...] = grad
    bg_ref[...] = bias


def chunk_of(ref, q, count):
    rows, _, width = ref.shape
    return ref[:, pl.ds(pl.multiple_of(q * count, count), count), :].reshape(rows * count, width)


def chunk_at(ref, q, count):
    return ref.at[:, pl.ds(pl.multiple_of(q * count, count), count), :]


class Modes:
    def __init__(self, section, buffer, p_out, local, cross):
        self.section, self.buffer, self.p_out, self.local, self.cross = section, buffer, p_out, local, cross

    def view(self, q):
        n, halves, kx, count, lanes = self.buffer.shape[1:]
        return self.buffer.at[q].reshape(n * halves * kx, count, lanes)

    def copies(self, q):
        s = self.section
        return (pltpu.make_async_copy(self.buffer.at[q, :, s], self.p_out.at[:, q, 0], self.local.at[q]),
                to_core(self.buffer.at[q, :, 1 - s], self.p_out.at[:, q, 1],
                        (self.cross.at[0, q], self.cross.at[1, q]), s))

    def start(self, q):
        for copy in self.copies(q):
            copy.start()

    def wait(self, q):
        for copy in self.copies(q):
            copy.wait()


class Bound:
    def __init__(self, section, owner, micro, other, source, bound, local, cross):
        self.section, self.owner, self.micro, self.other = section, owner, micro, other
        self.source, self.bound, self.local, self.cross = source, bound, local, cross

    def copies(self, q, count, micro):
        src, dst = chunk_at(self.source, q, count), chunk_at(self.bound.at[micro], q, count)
        return (pltpu.make_async_copy(src, dst, self.local.at[q]),
                to_core(src, dst, (self.cross.at[0, q], self.cross.at[1, q]), self.section))

    def start(self, q, count):
        here, there = self.copies(q, count, self.micro)

        @pl.when(self.section == self.owner)
        def _():
            here.start()

        @pl.when(self.section != self.owner)
        def _():
            there.start()

    def wait(self, q, count):
        here, there = self.copies(q, count, self.micro)
        come = self.copies(q, count, self.other)[1]

        @pl.when(self.section == self.owner)
        def _():
            here.wait()
            come.wait_recv()

        @pl.when(self.section != self.owner)
        def _():
            there.wait_send()


def add_squares(value, total):
    rows, _, width = total.shape
    square = (value * value).reshape(rows, -1, width)
    for at in range(0, square.shape[1], G):
        total[...] += square[:, at:at + G]


def region_sums(rid_ref, eo, eb, stat_ref):
    rows, _, width = eo.shape
    rid = rid_ref[...]
    energies = (jnp.sum(eo[...], axis=1), jnp.sum(eb[...], axis=1), jnp.ones((rows, width), F32))
    for kind in range(3):
        for region in range(R):
            line = jnp.sum(jnp.where(rid == region + 1, energies[kind], 0.0), axis=0, keepdims=True)
            total = line[:, :128]
            for piece in range(1, width // 128):
                total = total + line[:, piece * 128:(piece + 1) * 128]
            stat_ref[kind, region:region + 1, :] = total


def start_kernel(per_core, r):
    section, z, n = place_and_peers()
    chunks, count, half = r.p_buf.shape[1], r.p_buf.shape[5], r.far.shape[0]
    blocks = [(j, q) for j in range(per_core) for q in range(chunks)]
    reduce = Reduce(section, z, n, r.part, r.come, r.f_out, r.f_sem, r.red_send, r.red_recv, 0)
    outs = [r.part] + [getattr(r, f"p{j}") for j in range(1, per_core)]
    modes = [Modes(section, r.p_buf.at[j], outs[j], r.p_local.at[j], r.p_cross.at[j]) for j in range(per_core)]

    def field(k):
        j, q = blocks[k]
        src = chunk_at(r.inputs.at[section * per_core + j, 0], q, count)
        return pltpu.make_async_copy(src, r.a_buf.at[k % 2], r.a_sem.at[k % 2])

    def weight_in(x):
        return pltpu.make_async_copy(r.weights.at[0, (1 - section) * half + x], r.w_buf.at[x % 2], r.w_sem.at[x % 2])

    def weight_out(x):
        return to_core(r.w_buf.at[x % 2], r.far.at[x], (r.w_cross.at[0, x], r.w_cross.at[1, x]), section)

    def lend(x):
        if x < half:
            weight_in(x).wait()
            weight_out(x).start()
        if 1 <= x <= half:
            weight_out(x - 1).wait_send()
            if x + 1 < half:
                weight_in(x + 1).start()

    field(0).start()
    for x in range(min(2, half)):
        weight_in(x).start()
    greet(section, z, n, True)
    for k, (j, q) in enumerate(blocks):
        if k + 1 < len(blocks):
            field(k + 1).start()
        field(k).wait()
        to_modes(flat(r.a_buf.at[k % 2]), r.table[...], r.kron[...], r.spread, modes[j].view(q))
        modes[j].start(q)
        lend(k)
        if k >= 1:
            if k <= chunks:
                modes[0].wait(k - 1)
            reduce.tick(k - 1)
    for k in range(len(blocks), half + 1):
        lend(k)
    for t in range(len(blocks) - 1, chunks + n - 1):
        reduce.tick(t)
    for x in range(half):
        weight_out(x).wait_recv()
    for j, q in blocks[chunks:]:
        modes[j].wait(q)
    reduce.finish()


def stage_kernel(kind, j, per_core, layer, flip, r):
    section, z, n = place_and_peers()
    micro, other = section * per_core + j, (1 - section) * per_core + j
    forward, last = kind in ("middle", "turn"), kind == "tail"
    chunks, count, lanes = r.full.shape[0], r.full.shape[4], r.full.shape[5]
    gather = Gather(section, z, n, r.y, r.full, r.load, r.cross, r.send, r.recv)
    reduce = None
    if hasattr(r, "part"):
        reduce = Reduce(section, z, n, r.part, r.come, r.f_out, r.f_sem, r.red_send, r.red_recv, AHEAD)
        fetch(r.p_in, r.part, r.part_sem)
    if forward:
        fetch(r.a_in.at[micro, 0] if kind == "middle" else r.a_in, r.a, r.a_sem)
        if kind == "turn":
            fetch(r.cot_in.at[micro, 0], r.cot, r.c_sem)
        rid_copy = pltpu.make_async_copy(r.rid_in.at[micro, 0], r.rid, r.rid_sem)
        rid_copy.start()
    else:
        fetch(r.gz_in, r.gz, r.gz_sem)
        fetch(r.g_in if last else r.g_in.at[micro, 0], r.h, r.h_sem)
        fetch(r.a_in.at[micro, 0] if last else r.a_in, r.a, r.a_sem)
        if not last:
            fetch(r.dg_in, r.dg, r.dg_sem)
    greet(section, z, n, True)
    gather.begin()
    if reduce is not None:
        arrived(r.part, r.part_sem)
        reduce.tick(0)
    gather.ready()
    gather.tick(0)
    if reduce is not None:
        mix = Mix(section, z, layer, flip, r)
        mix.prime()
    if forward:
        r.eo[...] = jnp.zeros_like(r.eo)
        r.eb[...] = jnp.zeros_like(r.eb)
        arrived(r.a, r.a_sem)
    else:
        arrived(r.gz, r.gz_sem)
        arrived(r.h, r.h_sem)

    rows, channels = r.a.shape[:2]
    conv_blocks = rows // (r.weight.shape[0] // channels)
    if forward:
        work = [functools.partial(conv_rows, r.weight, r.bias, r.a, r.z_buf, *span)
                for span in portions(conv_blocks, n - 1)]
    else:
        work = [functools.partial(conv_rows, r.weight, None, r.gz, r.h, 0, conv_blocks)]
        spans = portions(rows, n - 2)
        work += [functools.partial(grad_rows, r.a, r.gz, r.cg, r.bg, *span) for span in spans]
    for t in range(n - 1):
        if t > 0:
            if reduce is not None:
                reduce.tick(t)
            gather.tick(t)
        if not forward and t == 1:
            arrived(r.a, r.a_sem)
        work[t]()
    if kind == "turn":
        arrived(r.cot, r.c_sem)
    if kind == "back":
        arrived(r.dg, r.dg_sem)

    if not last:
        modes = Modes(section, r.p_buf, r.p_out, r.p_local, r.p_cross)
    if kind == "turn":
        bound = Bound(section, 1, micro, other, r.a, r.bound, r.b_local, r.b_cross)
    if last:
        bound = Bound(section, 0, micro, other, r.h, r.bound, r.b_local, r.b_cross)

    def saves(q):
        pairs = {"middle": lambda: [(r.a, r.a_out), (r.z_buf, r.dg_out)], "turn": lambda: [(r.cot, r.gz_out)],
                 "back": lambda: [(r.h, r.ga_out), (r.dg, r.gz_out)], "tail": lambda: []}[kind]()
        return [pltpu.make_async_copy(chunk_at(src, q, count), chunk_at(dst, q, count), r.out_sem.at[i, q])
                for i, (src, dst) in enumerate(pairs)]

    def body(q, carry):
        if reduce is not None:
            reduce.tick(q + n - 1)
        gather.tick(q + n - 1)
        spectral = from_modes(r.full.at[q].reshape(-1, count, lanes), r.itable[...], r.ikron[...], r.spread)
        if forward:
            branch, slope = gelu_parts(spectral + chunk_of(r.z_buf, q, count))
            if kind == "turn":
                put(chunk_at(r.cot, q, count), chunk_of(r.cot, q, count) * slope)
            else:
                put(chunk_at(r.z_buf, q, count), slope)
            add_squares(branch, r.eb)
            out = chunk_of(r.a, q, count) + branch
            put(chunk_at(r.a, q, count), out)
            add_squares(out, r.eo)
            source = r.cot if kind == "turn" else r.a
        else:
            ga = spectral + chunk_of(r.h, q, count)
            put(chunk_at(r.h, q, count), ga)
            if not last:
                put(chunk_at(r.dg, q, count), ga * chunk_of(r.dg, q, count))
                source = r.dg
        for copy in saves(q):
            copy.start()
        if kind in ("turn", "tail"):
            bound.start(q, count)
        if not last:
            to_modes(chunk_of(source, q, count), r.table[...], r.kron[...], r.spread, modes.view(q))
            modes.start(q)
        if reduce is not None:
            mix.chunk(q)
        return carry

    lax.fori_loop(0, chunks, body, 0)
    if reduce is not None:
        mix.finish()
    if forward:
        rid_copy.wait()
        region_sums(r.rid, r.eo, r.eb, r.stat)

    def close(q, carry):
        for copy in saves(q):
            copy.wait()
        if kind in ("turn", "tail"):
            bound.wait(q, count)
        if not last:
            modes.wait(q)
        return carry

    lax.fori_loop(0, chunks, close, 0)
    gather.finish()
    if reduce is not None:
        reduce.finish()


def swap_halves(value):
    return pltpu.roll(value, value.shape[-1] // 2, value.ndim - 1)


def left_lanes(shape):
    return lax.broadcasted_iota(jnp.int32, shape, len(shape) - 1) < shape[-1] // 2


SLOTS = 4


def weight_stream(own, base, local_ref, far_ref, wbuf, sem):
    step, count = pl.program_id(0), pl.num_programs(0)

    def begin(at):
        slot = lax.rem(at, SLOTS)

        @pl.when(own)
        def _():
            fetch(local_ref.at[0, base + at], wbuf.at[slot], sem.at[slot])

        @pl.when(jnp.logical_not(own))
        def _():
            fetch(far_ref.at[at], wbuf.at[slot], sem.at[slot])

    @pl.when(step == 0)
    def _():
        for at in range(SLOTS - 1):
            @pl.when(at < count)
            def _():
                begin(at)

    @pl.when(step + SLOTS - 1 < count)
    def _():
        begin(step + SLOTS - 1)

    slot = lax.rem(step, SLOTS)
    arrived(wbuf.at[slot], sem.at[slot])
    return wbuf.at[slot]


def pieces(array):
    return [array[at:at + G] for at in range(0, array.shape[0], G)]


def spread_row(ref, row):
    return ref[pl.ds(row, G, stride=0), :]


def mix_kernel(m_ref, f_ref, local_ref, far_ref, y_ref, wbuf, f1, f2, sem):
    weight = weight_stream(m_ref[0] == 1, m_ref[1], local_ref, far_ref, wbuf, sem)
    grids, channels, lanes = f1.shape
    for g in range(grids):
        f1[g] = f_ref[:, g].reshape(channels, lanes)
    f2[...] = swap_halves(f1[...])
    groups = channels // G

    def body(block, acc):
        at = pl.multiple_of(block * G, G)
        acc = list(acc)
        for u in range(G):
            rows = [spread_row(f.at[g], at + u) for g in range(grids) for f in (f1, f2)]
            for o in range(groups):
                w = weight[at + u, o * G:(o + 1) * G, :]
                for k, row in enumerate(rows):
                    acc[k * groups + o] = acc[k * groups + o] + row * w
        return tuple(acc)

    acc = lax.fori_loop(0, groups, body, tuple(jnp.zeros((G, lanes), F32) for _ in range(2 * grids * groups)))
    left = left_lanes((channels, lanes))
    for g in range(grids):
        a, b = [jnp.concatenate(acc[k * groups:(k + 1) * groups], 0) for k in (2 * g, 2 * g + 1)]
        y_ref[g] = jnp.where(left, a - swap_halves(a), b + swap_halves(b)).reshape(y_ref.shape[1:])


def mix_t_kernel(m_ref, d_ref, local_ref, far_ref, y_ref, wbuf, a1, a2, sem):
    weight = weight_stream(m_ref[0] == 1, m_ref[1], local_ref, far_ref, wbuf, sem)
    grids, channels, lanes = a1.shape
    d = [d_ref[:, g].reshape(channels, lanes) for g in range(grids)]
    d1 = [pieces(d[g]) for g in range(grids)]
    d2 = [pieces(swap_halves(d[g])) for g in range(grids)]
    groups = channels // G

    def body(block, carry):
        at = pl.multiple_of(block * G, G)
        rows = [[] for _ in range(2 * grids)]
        for u in range(G):
            total = [None] * (2 * grids)
            for o in range(groups):
                w = weight[at + u, o * G:(o + 1) * G, :]
                for g in range(grids):
                    for side, source in enumerate((d1, d2)):
                        term = w * source[g][o]
                        k = 2 * g + side
                        total[k] = term if total[k] is None else total[k] + term
            for k in range(2 * grids):
                rows[k].append(jnp.sum(total[k], axis=0, keepdims=True))
        for g in range(grids):
            a1[g, pl.ds(at, G), :] = jnp.concatenate(rows[2 * g], 0)
            a2[g, pl.ds(at, G), :] = jnp.concatenate(rows[2 * g + 1], 0)
        return carry

    lax.fori_loop(0, groups, body, 0)
    left = left_lanes((channels, lanes))
    for g in range(grids):
        a, b = a1[g], a2[g]
        y_ref[g] = jnp.where(left, a + swap_halves(a), swap_halves(b) - b).reshape(y_ref.shape[1:])


class Mix:
    def __init__(self, section, z, layer, flip, r):
        self.section, self.z, self.layer, self.flip, self.r = section, z, layer, flip, r
        self.chunks, self.grids, self.half, self.count, self.lanes = r.part.shape[1:]
        self.channels, self.slots = r.weights.shape[2], r.wbuf.shape[0]

    def begin(self, block):
        q, x = block // self.half, block % self.half
        slot = lax.rem(block, self.slots)
        part = pl.ds(q * self.count, self.count)

        def load(rows):
            pltpu.make_async_copy(rows.at[:, part] if self.flip else rows.at[part], self.r.wbuf.at[slot],
                                  self.r.wsem.at[slot]).start()

        @pl.when(self.section == self.layer)
        def _():
            load(self.r.weights.at[0, self.section * self.half + x])

        @pl.when(self.section != self.layer)
        def _():
            load(self.r.far.at[x])

    def prime(self):
        for block in range(min(self.slots, self.chunks * self.half)):
            self.begin(jnp.int32(block))
        self.r.macc[...] = jnp.zeros_like(self.r.macc)

    def chunk(self, q):
        def body(x, carry):
            block = q * self.half + x
            slot = lax.rem(block, self.slots)
            weight = self.r.wbuf.at[slot]
            arrived(weight, self.r.wsem.at[slot])
            sources = [self.r.part.at[self.z, q, g, x] for g in range(self.grids)]
            for g in range(self.grids):
                self.r.msrc[2 * g] = sources[g][...]
                self.r.msrc[2 * g + 1] = swap_halves(sources[g][...])
            (self.transposed if self.flip else self.forward)(x, weight)

            @pl.when(block + self.slots < self.chunks * self.half)
            def _():
                self.begin(block + self.slots)

            return carry

        lax.fori_loop(0, self.half, body, 0)

    def forward(self, x, weight):
        sides, groups = 2 * self.grids, self.channels // G
        total = self.r.macc.at[x]
        keys = [(k, o) for k in range(sides) for o in range(groups)]

        def body(octet, acc):
            acc = dict(zip(keys, acc))
            for u in range(G):
                i = octet * G + u
                rows = [spread_row(self.r.msrc.at[k], i) for k in range(sides)]
                for o in range(groups):
                    w = weight[i, o * G:(o + 1) * G, :]
                    for k in range(sides):
                        acc[k, o] = acc[k, o] + rows[k] * w
            return tuple(acc[key] for key in keys)

        acc = lax.fori_loop(0, self.count // G, body, tuple(total[k, o * G:(o + 1) * G, :] for k, o in keys))
        for key, value in zip(keys, acc):
            total[key[0], key[1] * G:(key[1] + 1) * G, :] = value

    def transposed(self, x, weight):
        sides, groups = 2 * self.grids, self.count // G
        total = self.r.macc.at[x]
        rows = [pieces(self.r.msrc[k]) for k in range(sides)]

        def body(octet, carry):
            for u in range(G):
                i = octet * G + u
                tile = pl.ds(pl.multiple_of(i * G, G), G)
                w = [weight[i, o * G:(o + 1) * G, :] for o in range(groups)]
                for k in range(sides):
                    term = w[0] * rows[k][0]
                    for o in range(1, groups):
                        term = term + w[o] * rows[k][o]
                    total[k, tile, :] = total[k, tile, :] + term
            return carry

        lax.fori_loop(0, self.channels // G, body, 0)

    def finish(self):
        left = left_lanes((self.channels, self.lanes))

        def body(x, carry):
            for g in range(self.grids):
                a, b = [self.r.macc[x, 2 * g + side] for side in range(2)]
                if self.flip:
                    a, b = [jnp.sum(v.reshape(self.channels, G, self.lanes), axis=1) for v in (a, b)]
                    result = jnp.where(left, a + swap_halves(a), swap_halves(b) - b)
                else:
                    result = jnp.where(left, a - swap_halves(a), b + swap_halves(b))
                self.r.y_out[g, :, x] = result.reshape(self.chunks, self.count, self.lanes)
            return carry

        lax.fori_loop(0, self.half, body, 0)


def grad_tables(f_ref, d_ref, f1, fs, d1, ds):
    channels, lanes = f1.shape[1:]
    left = left_lanes((channels // 2, lanes))
    at = 0
    for stream in range(f_ref.shape[0]):
        for member in range(f_ref.shape[1]):
            for g in range(f_ref.shape[3]):
                f = f_ref[stream, member, :, g].reshape(channels, lanes)
                f1[at] = f
                less = f - swap_halves(f)
                fs[at] = jnp.where(left, less[:channels // 2], -less[channels // 2:])
                d = d_ref[stream, member, :, g].reshape(channels, lanes)
                d1[at] = d
                ds[at] = d + swap_halves(d)
                at += 1


def grad_block(first_row, f1, fs, d1, ds, out):
    count, channels, lanes = f1.shape
    groups, middle = channels // G, channels // 2
    left = left_lanes((G, lanes))

    def body(octet, carry):
        at = pl.multiple_of(octet * G, G)
        low = first_row + at
        for first in range(0, G, 2):
            acc = [[None] * groups for _ in range(6)]
            for g in range(count):
                factors = [spread_row(ref, row) for u in range(first, first + 2)
                           for ref, row in ((f1.at[g], low + u), (f1.at[g], middle + low + u), (fs.at[g], low + u))]
                for o in range(groups):
                    d, e = d1[g, o * G:(o + 1) * G, :], ds[g, o * G:(o + 1) * G, :]
                    for k, factor in enumerate(factors):
                        term = factor * (e if k % 3 == 2 else d)
                        acc[k][o] = term if acc[k][o] is None else acc[k][o] + term
            for u in range(2):
                for o in range(groups):
                    p = acc[3 * u + 2][o]
                    for side in range(2):
                        m = acc[3 * u + side][o]
                        n = swap_halves(m)
                        third = swap_halves(p) if side == 0 else p
                        out[side, at + first + u, o * G:(o + 1) * G, :] = jnp.where(left, m + n, m - n + third)
        return carry

    lax.fori_loop(0, out.shape[1] // G, body, 0)


class GradInput:
    def __init__(self, first, f, g, fbuf, gbuf, sem):
        self.first, self.f, self.g, self.fbuf, self.gbuf, self.sem = first, f, g, fbuf, gbuf, sem

    def load(self, x, slot):
        for layer, condition in enumerate((self.first, jnp.logical_not(self.first))):
            @pl.when(condition)
            def _():
                for j in range(len(self.f[layer])):
                    pltpu.make_async_copy(self.f[layer][j].at[:, :, :, x], self.fbuf.at[slot, j],
                                          self.sem.at[0, slot]).start()
                    pltpu.make_async_copy(self.g[layer][j].at[:, :, :, x], self.gbuf.at[slot, j],
                                          self.sem.at[1, slot]).start()

    def next(self, x, count):
        slot = lax.rem(x, 2)

        @pl.when(x + 1 < count)
        def _():
            self.load(x + 1, 1 - slot)

        arrived(self.fbuf.at[slot], self.sem.at[0, slot])
        arrived(self.gbuf.at[slot], self.sem.at[1, slot])
        return self.fbuf.at[slot], self.gbuf.at[slot]


def grad_input(r, first, per_core):
    f = [[getattr(r, f"f{layer}{j}") for j in range(per_core)] for layer in range(2)]
    g = [[getattr(r, f"g{layer}{j}") for j in range(per_core)] for layer in range(2)]
    return GradInput(first, f, g, r.fbuf, r.gbuf, r.in_sem)


def far_grad_kernel(per_core, r):
    section, z, n = place_and_peers()
    half = r.far.shape[0]
    block = r.out.shape[2]
    blocks = r.far.shape[2] // block
    source = grad_input(r, section != 0, per_core)

    def move(k, slot):
        x, i = k // blocks, k % blocks
        return to_core(r.out.at[slot], r.far.at[x, :, pl.ds(i * block, block)], (r.send.at[k], r.recv.at[k]), section)

    source.load(0, 0)
    greet(section, z, n, False)

    def body(x, carry):
        grad_tables(*source.next(x, half), r.f1, r.fs, r.d1, r.ds)

        def inner(i, carry):
            k = x * blocks + i

            @pl.when(k >= 2)
            def _():
                move(k - 2, lax.rem(k, 2)).wait_send()

            grad_block(i * block, r.f1, r.fs, r.d1, r.ds, r.out.at[lax.rem(k, 2)])
            move(k, lax.rem(k, 2)).start()
            return carry

        return lax.fori_loop(0, blocks, inner, carry)

    lax.fori_loop(0, half, body, 0)
    total = half * blocks
    for k in (total - 2, total - 1):
        move(k, k % 2).wait_send()

    def close(k, carry):
        move(k, 0).wait_recv()
        return carry

    lax.fori_loop(0, total, close, 0)


def own_grad_kernel(names, per_core, m_ref, *refs):
    r = types.SimpleNamespace(**dict(zip(names, refs)))
    x, i = pl.program_id(0), pl.program_id(1)
    source = grad_input(r, m_ref[0] == 0, per_core)

    @pl.when(i == 0)
    def _():
        @pl.when(x == 0)
        def _():
            source.load(0, 0)

        grad_tables(*source.next(x, pl.num_programs(0)), r.f1, r.fs, r.d1, r.ds)

    r.bound_out[...] = r.bound_in[...]
    r.out[1 - m_ref[0]] = r.far[...]
    grad_block(i * r.out.shape[2], r.f1, r.fs, r.d1, r.ds, r.out.at[m_ref[0]])


def whole(array):
    return pl.BlockSpec(array.shape, lambda *_: (0,) * array.ndim)


def params(**kw):
    return pltpu.CompilerParams(vmem_limit_bytes=VMEM_LIMIT, **kw)


def local(inputs, cotangent, region_id, spectral_w, conv_w, bias_vector):
    micro_count, _, rows_dev, channels, width = inputs.shape
    lanes = spectral_w.shape[-1]
    half = lanes // 2
    kx_dev = spectral_w.shape[1]
    row_devices, sections = lax.axis_size("rows"), lax.axis_size("section")
    mode_rows, height = kx_dev * row_devices, rows_dev * row_devices
    section = lax.axis_index("section")
    per_core = micro_count // sections
    kx_half = kx_dev // sections

    plain, doubled = col_tables(width, half)

    def stacked(array):
        high, low = np_split(array)
        return np.concatenate([high, high, low], 0)

    t_plain, t_doubled, it_plain, it_doubled = [stacked(t) for t in (plain, doubled, plain.T, doubled.T)]
    kron, ikron = row_tables(height, mode_rows, lax.axis_index("rows") * rows_dev, rows_dev)

    count = 2 * G
    chunks = channels // count
    hbm, vmem = pl.BlockSpec(memory_space=pl.ANY), pl.BlockSpec(memory_space=pltpu.VMEM)
    field_shape = jax.ShapeDtypeStruct((rows_dev, channels, width), F32)
    part_dims = (row_devices, chunks, sections, kx_half, count, lanes)
    p_shape, f_shape = jax.ShapeDtypeStruct(part_dims, F32), jax.ShapeDtypeStruct(part_dims[1:], F32)
    y_shape = jax.ShapeDtypeStruct((sections, chunks, kx_half, count, lanes), F32)
    stat_shape = jax.ShapeDtypeStruct((3, R, 128), F32)
    cg_shape = jax.ShapeDtypeStruct((2 * channels, 2 * channels), F32)
    bg_shape = jax.ShapeDtypeStruct((channels, width), F32)
    bound_shape = jax.ShapeDtypeStruct((micro_count, rows_dev, channels, width), F32)
    dma = pltpu.SemaphoreType.DMA
    field_buf = pltpu.VMEM((rows_dev, channels, width), F32)
    full_dims = (chunks, row_devices, sections, kx_half, count, lanes)
    spread = pltpu.VMEM((width // 128, rows_dev * count, 128), F32)
    energy = pltpu.VMEM((rows_dev, G, width), F32)
    line_sems = dma((2, chunks, row_devices))
    reduce_scratch = dict(part=pltpu.VMEM(part_dims, F32), come=pltpu.VMEM((2, chunks) + (row_devices,) + part_dims[2:], F32),
                          f_sem=dma((chunks,)), red_send=line_sems, red_recv=line_sems, part_sem=dma)

    def run(body, ident, ins, outs, scratch, cost=50, aliases=None):
        names = [*ins, *outs, *scratch]
        spec = lambda entry: vmem if isinstance(entry, tuple) else hbm
        plain = lambda entry: entry[0] if isinstance(entry, tuple) else entry
        kernel = lambda *refs: body(types.SimpleNamespace(**dict(zip(names, refs))))
        positions = {list(ins).index(k): list(outs).index(v) for k, v in (aliases or {}).items()}
        result = pl.pallas_call(
            kernel, in_specs=[spec(e) for e in ins.values()], out_specs=[spec(e) for e in outs.values()],
            out_shape=[plain(e) for e in outs.values()], scratch_shapes=list(scratch.values()),
            input_output_aliases=positions,
            cost_estimate=pl.CostEstimate(flops=0, bytes_accessed=cost * 3_000_000, transcendentals=0),
            compiler_params=params(collective_id=ident, has_side_effects=True))(*[plain(e) for e in ins.values()])
        return types.SimpleNamespace(**dict(zip(outs, result)))

    conv_rows_at_once = 256 // channels
    conv_both = lax.all_gather(conv_w, "section", axis=0, tiled=True)
    bias_both = lax.all_gather(bias_vector, "section", axis=0, tiled=True)

    def conv_parts(matrix):
        wide = jnp.kron(jnp.eye(conv_rows_at_once, dtype=F32), matrix)
        rounded = lax.reduce_precision(wide, 8, 7)
        high, low = rounded.astype(BF16), (wide - rounded).astype(BF16)
        return jnp.concatenate([high, low, high], 1)

    conv_fwd = [conv_parts(conv_both[l].T) for l in range(2)]
    conv_bwd = [conv_parts(conv_both[l]) for l in range(2)]
    bias_wide = [jnp.broadcast_to(bias_both[l][:, None], (channels, width)) for l in range(2)]

    def mixing(body, layer, pair):
        flag = jnp.stack([(section == layer).astype(jnp.int32), section * kx_half])
        f_block = pl.BlockSpec((chunks, sections, None, count, lanes), lambda x, m: (0, 0, x, 0, 0))
        y_block = pl.BlockSpec((sections, chunks, None, count, lanes), lambda x, m: (0, 0, x, 0, 0))
        small = pltpu.VMEM((sections, channels, lanes), F32)
        grid_spec = pltpu.PrefetchScalarGridSpec(
            num_scalar_prefetch=1, grid=(kx_half,), in_specs=[f_block, hbm, hbm], out_specs=y_block,
            scratch_shapes=[pltpu.VMEM((SLOTS, channels, channels, lanes), F32), small, small, dma((SLOTS,))])
        return pl.pallas_call(
            body, grid_spec=grid_spec, out_shape=y_shape, compiler_params=params(),
            cost_estimate=pl.CostEstimate(flops=0, bytes_accessed=30_000_000, transcendentals=0))(
                flag, pair, spectral_w, far_weights)

    streams = range(per_core)
    start = run(
        functools.partial(start_kernel, per_core), 0,
        dict(inputs=inputs, weights=spectral_w, table=(t_plain,), kron=(kron,)),
        dict(f_out=f_shape, far=jax.ShapeDtypeStruct((kx_half,) + spectral_w.shape[2:], F32),
             **{f"p{j}": p_shape for j in streams[1:]}),
        dict(a_buf=pltpu.VMEM((2, rows_dev, count, width), F32), w_buf=pltpu.VMEM((2,) + spectral_w.shape[2:], F32),
             p_buf=pltpu.VMEM((per_core,) + full_dims, F32), spread=spread, a_sem=dma((2,)), w_sem=dma((2,)),
             w_cross=dma((2, kx_half)), p_local=dma((per_core, chunks)), p_cross=dma((per_core, 2, chunks)),
             **reduce_scratch))
    far_weights = start.far

    kinds = ["middle", "turn", "back", "tail"]
    mixes = [(mix_kernel, 0), (mix_kernel, 1), (mix_t_kernel, 1), (mix_t_kernel, 0)]
    names = ["f0", "f1", "g1", "g0"]
    sums = [[None] * per_core for _ in kinds]
    sums[0][0] = start.f_out
    gathered, waiting = {}, [None, ("f00", lax.all_gather(start.f_out, "batch", axis=0))]
    parts = [getattr(start, f"p{j}", None) for j in streams]
    kept = [types.SimpleNamespace() for _ in streams]
    bound, calls, y = None, 0, None
    for phase, kind in enumerate(kinds):
        for j in streams:
            y = mixing(*mixes[0], start.f_out) if y is None else y
            keep = kept[j]
            ins, outs = dict(y=y), {}
            scratch = dict(full=pltpu.VMEM(full_dims, F32), spread=spread, load=dma, cross=dma((2,)),
                           send=line_sems, recv=line_sems, a=field_buf, a_sem=dma)
            aliases = {}
            if kind == "middle":
                ins.update(a_in=inputs, rid_in=region_id, weight=(conv_fwd[0],), bias=(bias_wide[0],))
                outs.update(a_out=field_shape, dg_out=field_shape, stat=(stat_shape,))
            elif kind == "turn":
                ins.update(a_in=keep.a1, rid_in=region_id, cot_in=cotangent, weight=(conv_fwd[1],), bias=(bias_wide[1],))
                outs.update(gz_out=field_shape, stat=(stat_shape,), bound=bound_shape)
                scratch.update(cot=field_buf, c_sem=dma)
            elif kind == "back":
                ins.update(a_in=keep.a1, gz_in=keep.gz1, g_in=cotangent, dg_in=keep.dg0, weight=(conv_bwd[1],))
                outs.update(ga_out=field_shape, gz_out=field_shape, cg=(cg_shape,), bg=(bg_shape,))
                scratch.update(dg=field_buf, dg_sem=dma)
            else:
                ins.update(a_in=inputs, gz_in=keep.gz0, g_in=keep.ga1, weight=(conv_bwd[0],))
                outs.update(cg=(cg_shape,), bg=(bg_shape,), bound=bound_shape)
            if kind in ("middle", "turn"):
                scratch.update(z_buf=field_buf, rid=pltpu.VMEM((rows_dev, width), jnp.int32), rid_sem=dma,
                               eo=energy, eb=energy)
            else:
                scratch.update(gz=field_buf, h=field_buf, gz_sem=dma, h_sem=dma)
            ins.update(itable=(it_doubled if kind in ("middle", "turn") else it_plain,), ikron=(ikron,))
            if kind != "tail":
                ins.update(table=(t_plain if kind == "middle" else t_doubled,), kron=(kron,))
                outs.update(p_out=p_shape)
                scratch.update(p_buf=pltpu.VMEM(full_dims, F32), p_local=dma((chunks,)), p_cross=dma((2, chunks)),
                               out_sem=dma((2, chunks)))
            if kind in ("turn", "tail"):
                scratch.update(b_local=dma((chunks,)), b_cross=dma((2, chunks)))
                if bound is not None:
                    ins.update(bound_in=bound)
                    aliases = dict(bound_in="bound")
            follow = (j + 1) % per_core
            follow_phase = phase + (1 if follow == 0 else 0)
            if follow_phase < len(kinds):
                body, layer = mixes[follow_phase]
                flip = body is mix_t_kernel
                ins.update(p_in=parts[follow], weights=spectral_w, far=far_weights)
                outs.update(f_out=f_shape, y_out=(y_shape,))
                blocks_at = (channels, count) if flip else (count, channels)
                scratch.update(reduce_scratch, wbuf=pltpu.VMEM((8,) + blocks_at + (lanes,), F32), wsem=dma((8,)),
                               macc=pltpu.VMEM((kx_half, 2 * sections, channels * (G if flip else 1), lanes), F32),
                               msrc=pltpu.VMEM((2 * sections, count, lanes), F32))
            early = waiting.pop(0)
            if early is not None:
                ins.update(held=early[1])
                gathered[early[0]] = early[1]
            done = run(functools.partial(stage_kernel, kind, j, per_core, layer, flip), 1 + calls, ins, outs, scratch, aliases=aliases)
            calls += 1
            if kind != "tail":
                parts[j] = done.p_out
            if follow_phase < len(kinds):
                sums[follow_phase][follow], y = done.f_out, done.y_out
                waiting.append((f"{names[follow_phase]}{follow}", lax.all_gather(done.f_out, "batch", axis=0)))
            if kind in ("turn", "tail"):
                bound = done.bound
            if kind == "middle":
                keep.a1, keep.dg0, keep.stat0 = done.a_out, done.dg_out, done.stat
            elif kind == "turn":
                keep.gz1, keep.stat1 = done.gz_out, done.stat
            elif kind == "back":
                keep.ga1, keep.gz0, keep.cg1, keep.bg1 = done.ga_out, done.gz_out, done.cg, done.bg
            else:
                keep.cg0, keep.bg0 = done.cg, done.bg
    stats0, stats1, cg0, cg1, bg0, bg1 = [[getattr(k, name) for k in kept]
                                          for name in ("stat0", "stat1", "cg0", "cg1", "bg0", "bg1")]

    gathered.update(waiting)
    members = lax.axis_size("batch")
    grids = per_core * members * sections
    block = G
    blocks = channels // 2 // block
    in_buf = pltpu.VMEM((2, per_core, members, chunks, sections, count, lanes), F32)
    big, small = pltpu.VMEM((grids, channels, lanes), F32), pltpu.VMEM((grids, channels // 2, lanes), F32)
    grad_scratch = dict(fbuf=in_buf, gbuf=in_buf, in_sem=dma((2, 2)), f1=big, fs=small, d1=big, ds=big)
    row_dims = (2, channels // 2, channels, lanes)
    far_grad = run(functools.partial(far_grad_kernel, per_core), 1 + calls, gathered,
                   dict(far=jax.ShapeDtypeStruct((kx_half,) + row_dims, F32)),
                   dict(out=pltpu.VMEM((2, 2, block, channels, lanes), F32), send=dma((kx_half * blocks,)),
                        recv=dma((kx_half * blocks,)), **grad_scratch)).far
    bound_rows = bound.reshape(micro_count * rows_dev, channels, width)
    bound_block = pl.BlockSpec((bound_rows.shape[0] // (kx_half * blocks), channels, width),
                               lambda x, i, m: (x * blocks + i, 0, 0))
    grid_spec = pltpu.PrefetchScalarGridSpec(
        num_scalar_prefetch=1, grid=(kx_half, blocks),
        in_specs=[hbm] * len(gathered)
        + [pl.BlockSpec((None, 2, block, channels, lanes), lambda x, i, m: (x, 0, i, 0, 0)), bound_block],
        out_specs=[pl.BlockSpec((2, None, 2, block, channels, lanes), lambda x, i, m: (0, x, 0, i, 0, 0)), bound_block],
        scratch_shapes=list(grad_scratch.values()))
    spectral_grad, boundary = pl.pallas_call(
        functools.partial(own_grad_kernel, [*gathered, "far", "bound_in", "out", "bound_out", *grad_scratch], per_core),
        grid_spec=grid_spec, out_shape=[jax.ShapeDtypeStruct((2, kx_half) + row_dims, F32),
                                        jax.ShapeDtypeStruct(bound_rows.shape, F32)],
        cost_estimate=pl.CostEstimate(flops=0, bytes_accessed=150_000_000, transcendentals=0),
        compiler_params=params())(
            jnp.reshape(section, (1,)).astype(jnp.int32), *gathered.values(), far_grad, bound_rows)
    spectral_grad = spectral_grad.reshape(spectral_w.shape)
    boundary = boundary.reshape((1, micro_count, 1) + inputs.shape[2:])

    def lower(value):
        return (value[:channels, :channels] + value[channels:, channels:]
                + value[:channels, channels:] + value[channels:, :channels])

    conv_local = jnp.stack([lower(sum(cg0)), lower(sum(cg1))])
    bias_local = jnp.stack([jnp.sum(sum(bg0), -1), jnp.sum(sum(bg1), -1)])
    stat_local = jnp.stack([jnp.sum(sum(stats0), -1), jnp.sum(sum(stats1), -1)])
    shapes = [v.shape for v in (conv_local, bias_local, stat_local)]
    flat_sums = jnp.concatenate([v.reshape(-1) for v in (conv_local, bias_local, stat_local)])
    length = flat_sums.shape[0]
    flat_sums = jnp.pad(flat_sums, (0, -length % 1024)).reshape(-1, 128)
    flat_sums = jnp.sum(lax.all_gather(flat_sums, ("section", "batch", "rows"), axis=0), 0).reshape(-1)
    ends = np.cumsum([0] + [math.prod(shape) for shape in shapes])
    conv_sum, bias_sum, stat_sum = [flat_sums[ends[i]:ends[i + 1]].reshape(shapes[i]) for i in range(3)]
    own_stat = lax.dynamic_index_in_dim(stat_sum, section, 0, False)
    layer_rms = jnp.sqrt(own_stat[:2] / (channels * own_stat[2])[None, :] + 1e-06)[None]
    own = lambda value: lax.dynamic_slice_in_dim(value, section, 1, 0)
    return boundary, spectral_grad, own(conv_sum), own(bias_sum), layer_rms


def solution(mesh):
    placed = (
        P(None, "batch", "rows", None, None),
        P(None, "batch", "rows", None, None),
        P(None, "batch", "rows", None),
        P("section", "rows", None, None, None),
        P("section", None, None),
        P("section", None),
    )
    return jax.shard_map(
        local,
        mesh=mesh,
        in_specs=placed,
        out_specs=(
            P("section", None, "batch", "rows", None, None),
            P("section", "rows", None, None, None),
            P("section", None, None),
            P("section", None),
            P("section", None, None),
        ),
        check_vma=False,
    )
```

```python
import functools
import math
import types

import jax
import jax.numpy as jnp
import numpy as np
from jax import lax
from jax.experimental import pallas as pl
from jax.experimental.pallas import tpu as pltpu
from jax.sharding import PartitionSpec as P

R = 8
G = 8
AHEAD = 2
F32 = jnp.float32
BF16 = jnp.bfloat16
VMEM_LIMIT = 56 * 1024 * 1024
MESH = pl.DeviceIdType.MESH


def split(value):
    high = value.astype(BF16)
    return high, (value - high.astype(F32)).astype(BF16)


def dot(left, right, dims=(((1,), (0,)), ((), ()))):
    return lax.dot_general(left, right, dims, preferred_element_type=F32)


def dot3(left, right):
    return dot(left[0], right[0]) + (dot(left[1], right[0]) + dot(left[0], right[1]))


def np_split(value):
    high = value.astype(np.float32).astype(BF16)
    return high, (value - high.astype(np.float64)).astype(np.float32).astype(BF16)


def col_tables(width, half):
    phase = 2.0 * math.pi / width * (np.outer(np.arange(width), np.arange(half)) % width)
    cosine, sine = np.cos(phase) / math.sqrt(width), np.sin(phase) / math.sqrt(width)
    plain = np.concatenate([cosine, -sine, -sine, -cosine], 1)
    doubled = plain * np.tile(np.where(np.arange(half) == 0, 1.0, 2.0), 4)[None, :]
    return plain, doubled


def row_tables(height, mode_rows, first_row, rows_dev):
    position = jnp.arange(mode_rows, dtype=jnp.int32)
    frequency = jnp.where(position < mode_rows // 2, position, height - mode_rows + position)
    row = first_row + jnp.arange(rows_dev, dtype=jnp.int32)
    phase = 2.0 * math.pi / height * (frequency[:, None] * row[None, :] % height).astype(F32)
    small = jnp.concatenate([jnp.cos(phase), jnp.sin(phase)], 1) / math.sqrt(height)
    rounded = lax.reduce_precision(small, 8, 7)
    high, low = rounded.astype(BF16), (small - rounded).astype(BF16)
    forward = jnp.concatenate([jnp.concatenate([high, high], 1), jnp.concatenate([low, jnp.zeros_like(low)], 1)], 0)
    inverse = jnp.concatenate([high.T, high.T, low.T], 1)
    return forward, inverse


def to_modes(value, table, kron, spread, p_ref):
    mode_rows, count, lanes = p_ref.shape
    rows = value.shape[0] // count
    high, low = split(value)
    spectra = dot(jnp.concatenate([high, low, high], 1), table)
    for i in range(2):
        spread[i] = spectra[:, i * lanes:(i + 1) * lanes]
    out = p_ref.reshape(mode_rows * count, lanes)
    for first in range(0, count, 2):
        sides = []
        for c in (first, first + 1):
            pick = pl.ds(c, rows, stride=count)
            sides.append(jnp.concatenate([spread[i, pick, :] for i in range(2)], 0))
        high, low = split(jnp.concatenate(sides, 1))
        both = dot(kron, jnp.concatenate([high, low], 0))
        result = both[:mode_rows] + both[mode_rows:]
        for i in range(2):
            out[pl.ds(first + i, mode_rows, stride=count), :] = result[:, i * lanes:(i + 1) * lanes]


def from_modes(y_ref, table, kron, spread):
    mode_rows, count, lanes = y_ref.shape
    rows, pieces = spread.shape[1] // count, spread.shape[0]
    modes = y_ref.reshape(mode_rows * count, lanes)
    sides = []
    for first in range(0, count, 2):
        pair = [modes[pl.ds(c, mode_rows, stride=count), :] for c in (first, first + 1)]
        high, low = split(jnp.concatenate(pair, 1))
        both = dot(kron, jnp.concatenate([high, low, high], 0))
        for i in range(2):
            side = both[:, i * lanes:(i + 1) * lanes]
            sides.append(jnp.concatenate([side[:rows], side[rows:]], 1))
    high, low = split(jnp.concatenate(sides, 0))
    out = dot(jnp.concatenate([high, low, high], 1), table)
    for c in range(count):
        for i in range(pieces):
            spread[i, pl.ds(c, rows, stride=count), :] = out[c * rows:(c + 1) * rows, i * 128:(i + 1) * 128]
    return jnp.concatenate([spread[i] for i in range(pieces)], 1)


def gelu_parts(z):
    size = jnp.abs(z)
    gauss = jnp.exp(-0.5 * z * z)
    base = 1.0 + (0.3275911 / math.sqrt(2.0)) * size
    t = pl.reciprocal(base, approx=True)
    t = t * (2.0 - base * t)
    poly = t * (0.254829592 + t * (-0.284496736 + t * (1.421413741 + t * (-1.453152027 + t * 1.061405429))))
    tail = 0.5 * poly * gauss
    phi = jnp.where(z >= 0, 1.0 - tail, tail)
    return z * phi, phi + z * (gauss * (1.0 / math.sqrt(2.0 * math.pi)))


def flat(ref):
    rows, count, width = ref.shape
    return ref[...].reshape(rows * count, width)


def put(ref, value):
    ref[...] = value.reshape(ref.shape)


def place_and_peers():
    section, z = lax.axis_index("section"), lax.axis_index("rows")
    return section, z, lax.axis_size("rows")


def greet(section, z, n, lines):
    barrier = pltpu.get_barrier_semaphore()
    pl.semaphore_signal(barrier, inc=1, device_id={"section": 1 - section}, device_id_type=MESH)
    if not lines:
        pl.semaphore_wait(barrier, 1)
        return

    @pl.when(z > 0)
    def _():
        pl.semaphore_signal(barrier, inc=1, device_id={"rows": z - 1}, device_id_type=MESH)

    @pl.when(z < n - 1)
    def _():
        pl.semaphore_signal(barrier, inc=1, device_id={"rows": z + 1}, device_id_type=MESH)

    pl.semaphore_wait(barrier, 1 + (z > 0).astype(jnp.int32) + (z < n - 1).astype(jnp.int32))


def to_core(src, dst, sems, section):
    return pltpu.make_async_remote_copy(src_ref=src, dst_ref=dst, send_sem=sems[0], recv_sem=sems[1],
                                        device_id={"section": 1 - section}, device_id_type=MESH)


def guard(condition, body):
    if isinstance(condition, (bool, np.bool_)):
        if condition:
            body()
    else:
        pl.when(condition)(body)


class Line:
    def __init__(self, section, z, n, chunks, send, recv):
        self.section, self.z, self.n, self.chunks = section, z, n, chunks
        self.send, self.recv = send, recv

    def move(self, way, q, hop, src, dst):
        return pltpu.make_async_remote_copy(
            src_ref=src, dst_ref=dst, send_sem=self.send.at[way, q, hop], recv_sem=self.recv.at[way, q, hop],
            device_id={"rows": self.z + 1 if way == 0 else self.z - 1}, device_id_type=MESH)

    def sends(self, way):
        return self.z < self.n - 1 if way == 0 else self.z > 0

    def hears(self, way):
        return self.z > 0 if way == 0 else self.z < self.n - 1


class Gather(Line):
    def __init__(self, section, z, n, y, full, load, cross, send, recv):
        super().__init__(section, z, n, full.shape[0], send, recv)
        self.full = full
        self.here = pltpu.make_async_copy(y.at[0], full.at[:, z, section], load)
        self.cross = to_core(y.at[1], full.at[:, z, section], (cross.at[0], cross.at[1]), section)

    def hop(self, way, q, hop):
        piece = self.full.at[q, self.source(way, hop)]
        return self.move(way, q, hop, piece, piece)

    def source(self, way, hop):
        return self.z - hop if way == 0 else self.z + hop

    def known(self, way, hop):
        at = self.source(way, hop)
        return at >= 0 if way == 0 else at < self.n

    def begin(self):
        self.here.start()
        self.cross.start()

    def ready(self):
        self.here.wait()
        self.cross.wait_recv()

    def own(self, q):
        for way in range(2):
            @pl.when(self.sends(way))
            def _():
                self.hop(way, q, 0).start()

    def step(self, q, hop):
        for way in range(2):
            @pl.when(self.known(way, hop + 1))
            def _():
                piece = self.full.at[q, self.source(way, hop + 1)]
                self.move(way, q, hop, piece, piece).wait_recv()

                @pl.when(self.sends(way))
                def _():
                    self.hop(way, q, hop + 1).start()

    def tick(self, t):
        if isinstance(t, int) and t == 0:
            for q in range(min(AHEAD, self.chunks)):
                self.own(q)
        guard(t + AHEAD < self.chunks, lambda: self.own(t + AHEAD))
        for hop in range(self.n - 1):
            q = t - hop - 1
            if isinstance(q, int):
                valid = 0 <= q < self.chunks
            else:
                valid = q < self.chunks
            guard(valid, functools.partial(self.step, q, hop))

    def finish(self):
        self.cross.wait_send()

        def body(q, carry):
            for way in range(2):
                for hop in range(self.n - 1):
                    @pl.when(jnp.logical_and(self.sends(way), self.known(way, hop)))
                    def _():
                        self.hop(way, q, hop).wait_send()
            return carry

        lax.fori_loop(0, self.chunks, body, 0)


class Reduce(Line):
    def __init__(self, section, z, n, part, come, f_out, f_sem, send, recv, ahead):
        super().__init__(section, z, n, part.shape[1], send, recv)
        self.ahead = ahead
        self.part, self.come, self.f_out, self.f_sem = part, come, f_out, f_sem

    def owner(self, way, hop):
        return self.z + self.n - hop if way == 0 else self.z - self.n + hop

    def valid(self, way, hop):
        return self.z <= hop - 1 if way == 0 else self.z >= self.n - hop

    def sent(self, way, q, hop):
        return self.move(way, q, hop, self.part.at[self.owner(way, hop), q], self.come.at[way, q, hop])

    def heard(self, way, q, hop):
        come = self.come.at[way, q, hop]
        self.move(way, q, hop, come, come).wait_recv()

    def first(self, t):
        for hop in range(1, self.n):
            q = t - hop + 1

            def send():
                for way in range(2):
                    @pl.when(jnp.logical_and(self.valid(way, hop), jnp.logical_not(self.hears(way))))
                    def _():
                        self.sent(way, q, hop).start()

            guard(0 <= q < self.chunks if isinstance(q, int) else q < self.chunks, send)

    def step(self, q, hop):
        for way in range(2):
            @pl.when(jnp.logical_and(self.valid(way, hop), self.hears(way)))
            def _():
                self.heard(way, q, hop - 1)
                owner = self.owner(way, hop)
                self.part[owner, q] = self.part[owner, q] + self.come[way, q, hop - 1]
                self.sent(way, q, hop).start()

    def result(self, q):
        return pltpu.make_async_copy(self.part.at[self.z, q], self.f_out.at[q], self.f_sem.at[q])

    def final(self, q):
        for way in range(2):
            @pl.when(self.hears(way))
            def _():
                self.heard(way, q, self.n - 1)
                self.part[self.z, q] = self.part[self.z, q] + self.come[way, q, self.n - 1]

        self.result(q).start()

    def tick(self, t):
        if isinstance(t, int) and t == 0:
            for early in range(self.ahead):
                self.first(early)
        self.first(t + self.ahead)
        for hop in range(2, self.n + 1):
            q = t - hop + 1
            if isinstance(q, int):
                valid = 0 <= q < self.chunks
            else:
                valid = q < self.chunks
            guard(valid, functools.partial(self.step, q, hop) if hop < self.n else functools.partial(self.final, q))

    def finish(self):
        def body(q, carry):
            self.result(q).wait()
            for way in range(2):
                for hop in range(1, self.n):
                    @pl.when(self.valid(way, hop))
                    def _():
                        self.sent(way, q, hop).wait_send()
            return carry

        lax.fori_loop(0, self.chunks, body, 0)


def fetch(src, dst, sem, parts=4):
    step = dst.shape[0] // parts
    for i in range(parts):
        pltpu.make_async_copy(src.at[pl.ds(i * step, step)], dst.at[pl.ds(i * step, step)], sem).start()


def arrived(dst, sem):
    pltpu.make_async_copy(dst, dst, sem).wait()


def portions(total, count):
    return [(i * total // count, (i + 1) * total // count) for i in range(count)]


def conv_rows(weight, bias, a, out, first, last):
    channels, width = a.shape[1:]
    block = weight.shape[0] // channels

    def body(i, carry):
        at = pl.ds(i * block, block)
        high, low = split(a[at].reshape(block * channels, width))
        result = dot(weight[...], jnp.concatenate([high, high, low], 0)).reshape(block, channels, width)
        out[at] = result + bias[...][None] if bias is not None else out[at] + result
        return carry

    lax.fori_loop(first, last, body, 0)


def grad_rows(a, gz, cg_ref, bg_ref, first, last):
    channels, width = a.shape[1:]

    def body(r, carry):
        grad, bias = carry
        g = gz[r]
        left = jnp.concatenate(split(a[r]), 0)
        right = jnp.concatenate(split(g), 0)
        return grad + dot(left, right, (((1,), (1,)), ((), ()))), bias + g

    zero = (jnp.zeros(cg_ref.shape, F32), jnp.zeros(bg_ref.shape, F32))
    grad, bias = lax.fori_loop(first, last, body, zero if first == 0 else (cg_ref[...], bg_ref[...]))
    cg_ref[...] = grad
    bg_ref[...] = bias


def chunk_of(ref, q, count):
    rows, _, width = ref.shape
    return ref[:, pl.ds(pl.multiple_of(q * count, count), count), :].reshape(rows * count, width)


def chunk_at(ref, q, count):
    return ref.at[:, pl.ds(pl.multiple_of(q * count, count), count), :]


class Modes:
    def __init__(self, section, buffer, p_out, local, cross):
        self.section, self.buffer, self.p_out, self.local, self.cross = section, buffer, p_out, local, cross

    def view(self, q):
        n, halves, kx, count, lanes = self.buffer.shape[1:]
        return self.buffer.at[q].reshape(n * halves * kx, count, lanes)

    def copies(self, q):
        s = self.section
        return (pltpu.make_async_copy(self.buffer.at[q, :, s], self.p_out.at[:, q, 0], self.local.at[q]),
                to_core(self.buffer.at[q, :, 1 - s], self.p_out.at[:, q, 1],
                        (self.cross.at[0, q], self.cross.at[1, q]), s))

    def start(self, q):
        for copy in self.copies(q):
            copy.start()

    def wait(self, q):
        for copy in self.copies(q):
            copy.wait()


class Bound:
    def __init__(self, section, owner, micro, other, source, bound, local, cross):
        self.section, self.owner, self.micro, self.other = section, owner, micro, other
        self.source, self.bound, self.local, self.cross = source, bound, local, cross

    def copies(self, q, count, micro):
        src, dst = chunk_at(self.source, q, count), chunk_at(self.bound.at[micro], q, count)
        return (pltpu.make_async_copy(src, dst, self.local.at[q]),
                to_core(src, dst, (self.cross.at[0, q], self.cross.at[1, q]), self.section))

    def start(self, q, count):
        here, there = self.copies(q, count, self.micro)

        @pl.when(self.section == self.owner)
        def _():
            here.start()

        @pl.when(self.section != self.owner)
        def _():
            there.start()

    def wait(self, q, count):
        here, there = self.copies(q, count, self.micro)
        come = self.copies(q, count, self.other)[1]

        @pl.when(self.section == self.owner)
        def _():
            here.wait()
            come.wait_recv()

        @pl.when(self.section != self.owner)
        def _():
            there.wait_send()


def add_squares(value, total):
    rows, _, width = total.shape
    square = (value * value).reshape(rows, -1, width)
    for at in range(0, square.shape[1], G):
        total[...] += square[:, at:at + G]


def region_sums(rid_ref, eo, eb, stat_ref):
    rows, _, width = eo.shape
    rid = rid_ref[...]
    energies = (jnp.sum(eo[...], axis=1), jnp.sum(eb[...], axis=1), jnp.ones((rows, width), F32))
    for kind in range(3):
        for region in range(R):
            line = jnp.sum(jnp.where(rid == region + 1, energies[kind], 0.0), axis=0, keepdims=True)
            total = line[:, :128]
            for piece in range(1, width // 128):
                total = total + line[:, piece * 128:(piece + 1) * 128]
            stat_ref[kind, region:region + 1, :] = total


def start_kernel(per_core, r):
    section, z, n = place_and_peers()
    chunks, count, half = r.p_buf.shape[1], r.p_buf.shape[5], r.far.shape[0]
    blocks = [(j, q) for j in range(per_core) for q in range(chunks)]
    reduce = Reduce(section, z, n, r.part, r.come, r.f_out, r.f_sem, r.red_send, r.red_recv, 0)
    outs = [r.part] + [getattr(r, f"p{j}") for j in range(1, per_core)]
    modes = [Modes(section, r.p_buf.at[j], outs[j], r.p_local.at[j], r.p_cross.at[j]) for j in range(per_core)]

    def field(k):
        j, q = blocks[k]
        src = chunk_at(r.inputs.at[section * per_core + j, 0], q, count)
        return pltpu.make_async_copy(src, r.a_buf.at[k % 2], r.a_sem.at[k % 2])

    def weight_in(x):
        return pltpu.make_async_copy(r.weights.at[0, (1 - section) * half + x], r.w_buf.at[x % 2], r.w_sem.at[x % 2])

    def weight_out(x):
        return to_core(r.w_buf.at[x % 2], r.far.at[x], (r.w_cross.at[0, x], r.w_cross.at[1, x]), section)

    def lend(x):
        if x < half:
            weight_in(x).wait()
            weight_out(x).start()
        if 1 <= x <= half:
            weight_out(x - 1).wait_send()
            if x + 1 < half:
                weight_in(x + 1).start()

    field(0).start()
    for x in range(min(2, half)):
        weight_in(x).start()
    greet(section, z, n, True)
    for k, (j, q) in enumerate(blocks):
        if k + 1 < len(blocks):
            field(k + 1).start()
        field(k).wait()
        to_modes(flat(r.a_buf.at[k % 2]), r.table[...], r.kron[...], r.spread, modes[j].view(q))
        modes[j].start(q)
        lend(k)
        if k >= 1:
            if k <= chunks:
                modes[0].wait(k - 1)
            reduce.tick(k - 1)
    for k in range(len(blocks), half + 1):
        lend(k)
    for t in range(len(blocks) - 1, chunks + n - 1):
        reduce.tick(t)
    for x in range(half):
        weight_out(x).wait_recv()
    for j, q in blocks[chunks:]:
        modes[j].wait(q)
    reduce.finish()


def stage_kernel(kind, j, per_core, layer, flip, r):
    section, z, n = place_and_peers()
    micro, other = section * per_core + j, (1 - section) * per_core + j
    forward, last = kind in ("middle", "turn"), kind == "tail"
    chunks, count, lanes = r.full.shape[0], r.full.shape[4], r.full.shape[5]
    gather = Gather(section, z, n, r.y, r.full, r.load, r.cross, r.send, r.recv)
    reduce = None
    if hasattr(r, "part"):
        reduce = Reduce(section, z, n, r.part, r.come, r.f_out, r.f_sem, r.red_send, r.red_recv, AHEAD)
        fetch(r.p_in, r.part, r.part_sem)
    if forward:
        fetch(r.a_in.at[micro, 0] if kind == "middle" else r.a_in, r.a, r.a_sem)
        if kind == "turn":
            fetch(r.cot_in.at[micro, 0], r.cot, r.c_sem)
        rid_copy = pltpu.make_async_copy(r.rid_in.at[micro, 0], r.rid, r.rid_sem)
        rid_copy.start()
    else:
        fetch(r.gz_in, r.gz, r.gz_sem)
        fetch(r.g_in if last else r.g_in.at[micro, 0], r.h, r.h_sem)
        fetch(r.a_in.at[micro, 0] if last else r.a_in, r.a, r.a_sem)
        if not last:
            fetch(r.dg_in, r.dg, r.dg_sem)
    greet(section, z, n, True)
    gather.begin()
    if reduce is not None:
        arrived(r.part, r.part_sem)
        reduce.tick(0)
    gather.ready()
    gather.tick(0)
    if reduce is not None:
        mix = Mix(section, z, layer, flip, r)
        mix.prime()
    if forward:
        r.eo[...] = jnp.zeros_like(r.eo)
        r.eb[...] = jnp.zeros_like(r.eb)
        arrived(r.a, r.a_sem)
    else:
        arrived(r.gz, r.gz_sem)
        arrived(r.h, r.h_sem)

    rows, channels = r.a.shape[:2]
    conv_blocks = rows // (r.weight.shape[0] // channels)
    if forward:
        work = [functools.partial(conv_rows, r.weight, r.bias, r.a, r.z_buf, *span)
                for span in portions(conv_blocks, n - 1)]
    else:
        work = [functools.partial(conv_rows, r.weight, None, r.gz, r.h, 0, conv_blocks)]
        spans = portions(rows, n - 2)
        work += [functools.partial(grad_rows, r.a, r.gz, r.cg, r.bg, *span) for span in spans]
    for t in range(n - 1):
        if t > 0:
            if reduce is not None:
                reduce.tick(t)
            gather.tick(t)
        if not forward and t == 1:
            arrived(r.a, r.a_sem)
        work[t]()
    if kind == "turn":
        arrived(r.cot, r.c_sem)
    if kind == "back":
        arrived(r.dg, r.dg_sem)

    if not last:
        modes = Modes(section, r.p_buf, r.p_out, r.p_local, r.p_cross)
    if kind == "turn":
        bound = Bound(section, 1, micro, other, r.a, r.bound, r.b_local, r.b_cross)
    if last:
        bound = Bound(section, 0, micro, other, r.h, r.bound, r.b_local, r.b_cross)

    def saves(q):
        pairs = {"middle": lambda: [(r.a, r.a_out), (r.z_buf, r.dg_out)], "turn": lambda: [(r.cot, r.gz_out)],
                 "back": lambda: [(r.h, r.ga_out), (r.dg, r.gz_out)], "tail": lambda: []}[kind]()
        return [pltpu.make_async_copy(chunk_at(src, q, count), chunk_at(dst, q, count), r.out_sem.at[i, q])
                for i, (src, dst) in enumerate(pairs)]

    def body(q, carry):
        if reduce is not None:
            reduce.tick(q + n - 1)
        gather.tick(q + n - 1)
        spectral = from_modes(r.full.at[q].reshape(-1, count, lanes), r.itable[...], r.ikron[...], r.spread)
        if forward:
            branch, slope = gelu_parts(spectral + chunk_of(r.z_buf, q, count))
            if kind == "turn":
                put(chunk_at(r.cot, q, count), chunk_of(r.cot, q, count) * slope)
            else:
                put(chunk_at(r.z_buf, q, count), slope)
            add_squares(branch, r.eb)
            out = chunk_of(r.a, q, count) + branch
            put(chunk_at(r.a, q, count), out)
            add_squares(out, r.eo)
            source = r.cot if kind == "turn" else r.a
        else:
            ga = spectral + chunk_of(r.h, q, count)
            put(chunk_at(r.h, q, count), ga)
            if not last:
                put(chunk_at(r.dg, q, count), ga * chunk_of(r.dg, q, count))
                source = r.dg
        for copy in saves(q):
            copy.start()
        if kind in ("turn", "tail"):
            bound.start(q, count)
        if not last:
            to_modes(chunk_of(source, q, count), r.table[...], r.kron[...], r.spread, modes.view(q))
            modes.start(q)
        if reduce is not None:
            mix.chunk(q)
        return carry

    lax.fori_loop(0, chunks, body, 0)
    if reduce is not None:
        mix.finish()
    if forward:
        rid_copy.wait()
        region_sums(r.rid, r.eo, r.eb, r.stat)

    def close(q, carry):
        for copy in saves(q):
            copy.wait()
        if kind in ("turn", "tail"):
            bound.wait(q, count)
        if not last:
            modes.wait(q)
        return carry

    lax.fori_loop(0, chunks, close, 0)
    gather.finish()
    if reduce is not None:
        reduce.finish()


def swap_halves(value):
    return pltpu.roll(value, value.shape[-1] // 2, value.ndim - 1)


def left_lanes(shape):
    return lax.broadcasted_iota(jnp.int32, shape, len(shape) - 1) < shape[-1] // 2


SLOTS = 4


def weight_stream(own, base, local_ref, far_ref, wbuf, sem):
    step, count = pl.program_id(0), pl.num_programs(0)

    def begin(at):
        slot = lax.rem(at, SLOTS)

        @pl.when(own)
        def _():
            fetch(local_ref.at[0, base + at], wbuf.at[slot], sem.at[slot])

        @pl.when(jnp.logical_not(own))
        def _():
            fetch(far_ref.at[at], wbuf.at[slot], sem.at[slot])

    @pl.when(step == 0)
    def _():
        for at in range(SLOTS - 1):
            @pl.when(at < count)
            def _():
                begin(at)

    @pl.when(step + SLOTS - 1 < count)
    def _():
        begin(step + SLOTS - 1)

    slot = lax.rem(step, SLOTS)
    arrived(wbuf.at[slot], sem.at[slot])
    return wbuf.at[slot]


def pieces(array):
    return [array[at:at + G] for at in range(0, array.shape[0], G)]


def spread_row(ref, row):
    return ref[pl.ds(row, G, stride=0), :]


def mix_kernel(m_ref, f_ref, local_ref, far_ref, y_ref, wbuf, f1, f2, sem):
    weight = weight_stream(m_ref[0] == 1, m_ref[1], local_ref, far_ref, wbuf, sem)
    grids, channels, lanes = f1.shape
    for g in range(grids):
        f1[g] = f_ref[:, g].reshape(channels, lanes)
    f2[...] = swap_halves(f1[...])
    groups = channels // G

    def body(block, acc):
        at = pl.multiple_of(block * G, G)
        acc = list(acc)
        for u in range(G):
            rows = [spread_row(f.at[g], at + u) for g in range(grids) for f in (f1, f2)]
            for o in range(groups):
                w = weight[at + u, o * G:(o + 1) * G, :]
                for k, row in enumerate(rows):
                    acc[k * groups + o] = acc[k * groups + o] + row * w
        return tuple(acc)

    acc = lax.fori_loop(0, groups, body, tuple(jnp.zeros((G, lanes), F32) for _ in range(2 * grids * groups)))
    left = left_lanes((channels, lanes))
    for g in range(grids):
        a, b = [jnp.concatenate(acc[k * groups:(k + 1) * groups], 0) for k in (2 * g, 2 * g + 1)]
        y_ref[g] = jnp.where(left, a - swap_halves(a), b + swap_halves(b)).reshape(y_ref.shape[1:])


def mix_t_kernel(m_ref, d_ref, local_ref, far_ref, y_ref, wbuf, a1, a2, sem):
    weight = weight_stream(m_ref[0] == 1, m_ref[1], local_ref, far_ref, wbuf, sem)
    grids, channels, lanes = a1.shape
    d = [d_ref[:, g].reshape(channels, lanes) for g in range(grids)]
    d1 = [pieces(d[g]) for g in range(grids)]
    d2 = [pieces(swap_halves(d[g])) for g in range(grids)]
    groups = channels // G

    def body(block, carry):
        at = pl.multiple_of(block * G, G)
        rows = [[] for _ in range(2 * grids)]
        for u in range(G):
            total = [None] * (2 * grids)
            for o in range(groups):
                w = weight[at + u, o * G:(o + 1) * G, :]
                for g in range(grids):
                    for side, source in enumerate((d1, d2)):
                        term = w * source[g][o]
                        k = 2 * g + side
                        total[k] = term if total[k] is None else total[k] + term
            for k in range(2 * grids):
                rows[k].append(jnp.sum(total[k], axis=0, keepdims=True))
        for g in range(grids):
            a1[g, pl.ds(at, G), :] = jnp.concatenate(rows[2 * g], 0)
            a2[g, pl.ds(at, G), :] = jnp.concatenate(rows[2 * g + 1], 0)
        return carry

    lax.fori_loop(0, groups, body, 0)
    left = left_lanes((channels, lanes))
    for g in range(grids):
        a, b = a1[g], a2[g]
        y_ref[g] = jnp.where(left, a + swap_halves(a), swap_halves(b) - b).reshape(y_ref.shape[1:])


class Mix:
    def __init__(self, section, z, layer, flip, r):
        self.section, self.z, self.layer, self.flip, self.r = section, z, layer, flip, r
        self.grids, self.half, _, self.lanes = r.part.shape[2:]
        self.channels, self.slots, self.count = r.weights.shape[2], r.wbuf.shape[0], r.msrc.shape[1]
        self.together = self.count // r.part.shape[4]
        self.blocks = self.channels // self.count * self.half

    def begin(self, block):
        q, x = block // self.half, block % self.half
        slot = lax.rem(block, self.slots)
        part = pl.ds(q * self.count, self.count)

        def load(rows):
            pltpu.make_async_copy(rows.at[:, part] if self.flip else rows.at[part], self.r.wbuf.at[slot],
                                  self.r.wsem.at[slot]).start()

        @pl.when(self.section == self.layer)
        def _():
            load(self.r.weights.at[0, self.section * self.half + x])

        @pl.when(self.section != self.layer)
        def _():
            load(self.r.far.at[x])

    def prime(self):
        for block in range(min(self.slots, self.blocks)):
            self.begin(jnp.int32(block))
        self.r.macc[...] = jnp.zeros_like(self.r.macc)

    def chunk(self, q):
        @pl.when(lax.rem(q, self.together) == self.together - 1)
        def _():
            self.take(q // self.together)

    def take(self, q):
        def body(x, carry):
            block = q * self.half + x
            slot = lax.rem(block, self.slots)
            weight = self.r.wbuf.at[slot]
            arrived(weight, self.r.wsem.at[slot])
            for g in range(self.grids):
                value = jnp.concatenate([self.r.part[self.z, q * self.together + i, g, x]
                                         for i in range(self.together)], 0)
                self.r.msrc[2 * g] = value
                self.r.msrc[2 * g + 1] = swap_halves(value)
            (self.transposed if self.flip else self.forward)(x, weight)

            @pl.when(block + self.slots < self.blocks)
            def _():
                self.begin(block + self.slots)

            return carry

        lax.fori_loop(0, self.half, body, 0)

    def forward(self, x, weight):
        sides, groups = 2 * self.grids, self.channels // G
        total = self.r.macc.at[x]
        keys = [(k, o) for k in range(sides) for o in range(groups)]

        def body(octet, acc):
            acc = dict(zip(keys, acc))
            for u in range(G):
                i = octet * G + u
                rows = [spread_row(self.r.msrc.at[k], i) for k in range(sides)]
                for o in range(groups):
                    w = weight[i, o * G:(o + 1) * G, :]
                    for k in range(sides):
                        acc[k, o] = acc[k, o] + rows[k] * w
            return tuple(acc[key] for key in keys)

        acc = lax.fori_loop(0, self.count // G, body, tuple(total[k, o * G:(o + 1) * G, :] for k, o in keys))
        for key, value in zip(keys, acc):
            total[key[0], key[1] * G:(key[1] + 1) * G, :] = value

    def transposed(self, x, weight):
        sides, groups = 2 * self.grids, self.count // G
        total = self.r.macc.at[x]
        rows = [pieces(self.r.msrc[k]) for k in range(sides)]

        def body(octet, carry):
            for u in range(G):
                i = octet * G + u
                tile = pl.ds(pl.multiple_of(i * G, G), G)
                w = [weight[i, o * G:(o + 1) * G, :] for o in range(groups)]
                for k in range(sides):
                    term = w[0] * rows[k][0]
                    for o in range(1, groups):
                        term = term + w[o] * rows[k][o]
                    total[k, tile, :] = total[k, tile, :] + term
            return carry

        lax.fori_loop(0, self.channels // G, body, 0)

    def finish(self):
        left = left_lanes((self.channels, self.lanes))

        def body(x, carry):
            for g in range(self.grids):
                a, b = [self.r.macc[x, 2 * g + side] for side in range(2)]
                if self.flip:
                    a, b = [jnp.sum(v.reshape(self.channels, G, self.lanes), axis=1) for v in (a, b)]
                    result = jnp.where(left, a + swap_halves(a), swap_halves(b) - b)
                else:
                    result = jnp.where(left, a - swap_halves(a), b + swap_halves(b))
                self.r.y_out[g, :, x] = result.reshape(-1, self.r.part.shape[4], self.lanes)
            return carry

        lax.fori_loop(0, self.half, body, 0)


def grad_tables(f_ref, d_ref, f1, fs, d1, ds):
    channels, lanes = f1.shape[1:]
    left = left_lanes((channels // 2, lanes))
    at = 0
    for stream in range(f_ref.shape[0]):
        for member in range(f_ref.shape[1]):
            for g in range(f_ref.shape[3]):
                f = f_ref[stream, member, :, g].reshape(channels, lanes)
                f1[at] = f
                less = f - swap_halves(f)
                fs[at] = jnp.where(left, less[:channels // 2], -less[channels // 2:])
                d = d_ref[stream, member, :, g].reshape(channels, lanes)
                d1[at] = d
                ds[at] = d + swap_halves(d)
                at += 1


def grad_block(first_row, f1, fs, d1, ds, out):
    count, channels, lanes = f1.shape
    groups, middle = channels // G, channels // 2
    left = left_lanes((G, lanes))

    def body(octet, carry):
        at = pl.multiple_of(octet * G, G)
        low = first_row + at
        for first in range(0, G, 2):
            acc = [[None] * groups for _ in range(6)]
            for g in range(count):
                factors = [spread_row(ref, row) for u in range(first, first + 2)
                           for ref, row in ((f1.at[g], low + u), (f1.at[g], middle + low + u), (fs.at[g], low + u))]
                for o in range(groups):
                    d, e = d1[g, o * G:(o + 1) * G, :], ds[g, o * G:(o + 1) * G, :]
                    for k, factor in enumerate(factors):
                        term = factor * (e if k % 3 == 2 else d)
                        acc[k][o] = term if acc[k][o] is None else acc[k][o] + term
            for u in range(2):
                for o in range(groups):
                    p = acc[3 * u + 2][o]
                    for side in range(2):
                        m = acc[3 * u + side][o]
                        n = swap_halves(m)
                        third = swap_halves(p) if side == 0 else p
                        out[side, at + first + u, o * G:(o + 1) * G, :] = jnp.where(left, m + n, m - n + third)
        return carry

    lax.fori_loop(0, out.shape[1] // G, body, 0)


class GradInput:
    def __init__(self, first, f, g, fbuf, gbuf, sem):
        self.first, self.f, self.g, self.fbuf, self.gbuf, self.sem = first, f, g, fbuf, gbuf, sem

    def load(self, x, slot):
        for layer, condition in enumerate((self.first, jnp.logical_not(self.first))):
            @pl.when(condition)
            def _():
                for j in range(len(self.f[layer])):
                    pltpu.make_async_copy(self.f[layer][j].at[:, :, :, x], self.fbuf.at[slot, j],
                                          self.sem.at[0, slot]).start()
                    pltpu.make_async_copy(self.g[layer][j].at[:, :, :, x], self.gbuf.at[slot, j],
                                          self.sem.at[1, slot]).start()

    def next(self, x, count):
        slot = lax.rem(x, 2)

        @pl.when(x + 1 < count)
        def _():
            self.load(x + 1, 1 - slot)

        arrived(self.fbuf.at[slot], self.sem.at[0, slot])
        arrived(self.gbuf.at[slot], self.sem.at[1, slot])
        return self.fbuf.at[slot], self.gbuf.at[slot]


def grad_input(r, first, per_core):
    f = [[getattr(r, f"f{layer}{j}") for j in range(per_core)] for layer in range(2)]
    g = [[getattr(r, f"g{layer}{j}") for j in range(per_core)] for layer in range(2)]
    return GradInput(first, f, g, r.fbuf, r.gbuf, r.in_sem)


def far_grad_kernel(per_core, r):
    section, z, n = place_and_peers()
    half = r.far.shape[0]
    block = r.out.shape[2]
    blocks = r.far.shape[2] // block
    source = grad_input(r, section != 0, per_core)

    def move(k, slot):
        x, i = k // blocks, k % blocks
        return to_core(r.out.at[slot], r.far.at[x, :, pl.ds(i * block, block)], (r.send.at[k], r.recv.at[k]), section)

    source.load(0, 0)
    greet(section, z, n, False)

    def body(x, carry):
        grad_tables(*source.next(x, half), r.f1, r.fs, r.d1, r.ds)

        def inner(i, carry):
            k = x * blocks + i

            @pl.when(k >= 2)
            def _():
                move(k - 2, lax.rem(k, 2)).wait_send()

            grad_block(i * block, r.f1, r.fs, r.d1, r.ds, r.out.at[lax.rem(k, 2)])
            move(k, lax.rem(k, 2)).start()
            return carry

        return lax.fori_loop(0, blocks, inner, carry)

    lax.fori_loop(0, half, body, 0)
    total = half * blocks
    for k in (total - 2, total - 1):
        move(k, k % 2).wait_send()

    def close(k, carry):
        move(k, 0).wait_recv()
        return carry

    lax.fori_loop(0, total, close, 0)


def own_grad_kernel(names, per_core, m_ref, *refs):
    r = types.SimpleNamespace(**dict(zip(names, refs)))
    x, i = pl.program_id(0), pl.program_id(1)
    source = grad_input(r, m_ref[0] == 0, per_core)

    @pl.when(i == 0)
    def _():
        @pl.when(x == 0)
        def _():
            source.load(0, 0)

        grad_tables(*source.next(x, pl.num_programs(0)), r.f1, r.fs, r.d1, r.ds)

    r.bound_out[...] = r.bound_in[...]
    r.out[1 - m_ref[0]] = r.far[...]
    grad_block(i * r.out.shape[2], r.f1, r.fs, r.d1, r.ds, r.out.at[m_ref[0]])


def whole(array):
    return pl.BlockSpec(array.shape, lambda *_: (0,) * array.ndim)


def params(**kw):
    return pltpu.CompilerParams(vmem_limit_bytes=VMEM_LIMIT, **kw)


def local(inputs, cotangent, region_id, spectral_w, conv_w, bias_vector):
    micro_count, _, rows_dev, channels, width = inputs.shape
    lanes = spectral_w.shape[-1]
    half = lanes // 2
    kx_dev = spectral_w.shape[1]
    row_devices, sections = lax.axis_size("rows"), lax.axis_size("section")
    mode_rows, height = kx_dev * row_devices, rows_dev * row_devices
    section = lax.axis_index("section")
    per_core = micro_count // sections
    kx_half = kx_dev // sections

    plain, doubled = col_tables(width, half)

    def stacked(array):
        high, low = np_split(array)
        return np.concatenate([high, high, low], 0)

    t_plain, t_doubled, it_plain, it_doubled = [stacked(t) for t in (plain, doubled, plain.T, doubled.T)]
    kron, ikron = row_tables(height, mode_rows, lax.axis_index("rows") * rows_dev, rows_dev)

    count = G
    chunks = channels // count
    hbm, vmem = pl.BlockSpec(memory_space=pl.ANY), pl.BlockSpec(memory_space=pltpu.VMEM)
    field_shape = jax.ShapeDtypeStruct((rows_dev, channels, width), F32)
    part_dims = (row_devices, chunks, sections, kx_half, count, lanes)
    p_shape, f_shape = jax.ShapeDtypeStruct(part_dims, F32), jax.ShapeDtypeStruct(part_dims[1:], F32)
    y_shape = jax.ShapeDtypeStruct((sections, chunks, kx_half, count, lanes), F32)
    stat_shape = jax.ShapeDtypeStruct((3, R, 128), F32)
    cg_shape = jax.ShapeDtypeStruct((2 * channels, 2 * channels), F32)
    bg_shape = jax.ShapeDtypeStruct((channels, width), F32)
    bound_shape = jax.ShapeDtypeStruct((micro_count, rows_dev, channels, width), F32)
    dma = pltpu.SemaphoreType.DMA
    field_buf = pltpu.VMEM((rows_dev, channels, width), F32)
    full_dims = (chunks, row_devices, sections, kx_half, count, lanes)
    spread = pltpu.VMEM((width // 128, rows_dev * count, 128), F32)
    energy = pltpu.VMEM((rows_dev, G, width), F32)
    line_sems = dma((2, chunks, row_devices))
    reduce_scratch = dict(part=pltpu.VMEM(part_dims, F32), come=pltpu.VMEM((2, chunks) + (row_devices,) + part_dims[2:], F32),
                          f_sem=dma((chunks,)), red_send=line_sems, red_recv=line_sems, part_sem=dma)

    def run(body, ident, ins, outs, scratch, cost=50, aliases=None):
        names = [*ins, *outs, *scratch]
        spec = lambda entry: vmem if isinstance(entry, tuple) else hbm
        plain = lambda entry: entry[0] if isinstance(entry, tuple) else entry
        kernel = lambda *refs: body(types.SimpleNamespace(**dict(zip(names, refs))))
        positions = {list(ins).index(k): list(outs).index(v) for k, v in (aliases or {}).items()}
        result = pl.pallas_call(
            kernel, in_specs=[spec(e) for e in ins.values()], out_specs=[spec(e) for e in outs.values()],
            out_shape=[plain(e) for e in outs.values()], scratch_shapes=list(scratch.values()),
            input_output_aliases=positions,
            cost_estimate=pl.CostEstimate(flops=0, bytes_accessed=cost * 3_000_000, transcendentals=0),
            compiler_params=params(collective_id=ident, has_side_effects=True))(*[plain(e) for e in ins.values()])
        return types.SimpleNamespace(**dict(zip(outs, result)))

    conv_rows_at_once = 256 // channels
    conv_both = lax.all_gather(conv_w, "section", axis=0, tiled=True)
    bias_both = lax.all_gather(bias_vector, "section", axis=0, tiled=True)

    def conv_parts(matrix):
        wide = jnp.kron(jnp.eye(conv_rows_at_once, dtype=F32), matrix)
        rounded = lax.reduce_precision(wide, 8, 7)
        high, low = rounded.astype(BF16), (wide - rounded).astype(BF16)
        return jnp.concatenate([high, low, high], 1)

    conv_fwd = [conv_parts(conv_both[l].T) for l in range(2)]
    conv_bwd = [conv_parts(conv_both[l]) for l in range(2)]
    bias_wide = [jnp.broadcast_to(bias_both[l][:, None], (channels, width)) for l in range(2)]

    def mixing(body, layer, pair):
        flag = jnp.stack([(section == layer).astype(jnp.int32), section * kx_half])
        f_block = pl.BlockSpec((chunks, sections, None, count, lanes), lambda x, m: (0, 0, x, 0, 0))
        y_block = pl.BlockSpec((sections, chunks, None, count, lanes), lambda x, m: (0, 0, x, 0, 0))
        small = pltpu.VMEM((sections, channels, lanes), F32)
        grid_spec = pltpu.PrefetchScalarGridSpec(
            num_scalar_prefetch=1, grid=(kx_half,), in_specs=[f_block, hbm, hbm], out_specs=y_block,
            scratch_shapes=[pltpu.VMEM((SLOTS, channels, channels, lanes), F32), small, small, dma((SLOTS,))])
        return pl.pallas_call(
            body, grid_spec=grid_spec, out_shape=y_shape, compiler_params=params(),
            cost_estimate=pl.CostEstimate(flops=0, bytes_accessed=30_000_000, transcendentals=0))(
                flag, pair, spectral_w, far_weights)

    streams = range(per_core)
    start = run(
        functools.partial(start_kernel, per_core), 0,
        dict(inputs=inputs, weights=spectral_w, table=(t_plain,), kron=(kron,)),
        dict(f_out=f_shape, far=jax.ShapeDtypeStruct((kx_half,) + spectral_w.shape[2:], F32),
             **{f"p{j}": p_shape for j in streams[1:]}),
        dict(a_buf=pltpu.VMEM((2, rows_dev, count, width), F32), w_buf=pltpu.VMEM((2,) + spectral_w.shape[2:], F32),
             p_buf=pltpu.VMEM((per_core,) + full_dims, F32), spread=spread, a_sem=dma((2,)), w_sem=dma((2,)),
             w_cross=dma((2, kx_half)), p_local=dma((per_core, chunks)), p_cross=dma((per_core, 2, chunks)),
             **reduce_scratch))
    far_weights = start.far

    kinds = ["middle", "turn", "back", "tail"]
    mixes = [(mix_kernel, 0), (mix_kernel, 1), (mix_t_kernel, 1), (mix_t_kernel, 0)]
    names = ["f0", "f1", "g1", "g0"]
    sums = [[None] * per_core for _ in kinds]
    sums[0][0] = start.f_out
    gathered, waiting = {}, [None, ("f00", lax.all_gather(start.f_out, "batch", axis=0))]
    parts = [getattr(start, f"p{j}", None) for j in streams]
    kept = [types.SimpleNamespace() for _ in streams]
    bound, calls, y = None, 0, None
    for phase, kind in enumerate(kinds):
        for j in streams:
            y = mixing(*mixes[0], start.f_out) if y is None else y
            keep = kept[j]
            ins, outs = dict(y=y), {}
            scratch = dict(full=pltpu.VMEM(full_dims, F32), spread=spread, load=dma, cross=dma((2,)),
                           send=line_sems, recv=line_sems, a=field_buf, a_sem=dma)
            aliases = {}
            if kind == "middle":
                ins.update(a_in=inputs, rid_in=region_id, weight=(conv_fwd[0],), bias=(bias_wide[0],))
                outs.update(a_out=field_shape, dg_out=field_shape, stat=(stat_shape,))
            elif kind == "turn":
                ins.update(a_in=keep.a1, rid_in=region_id, cot_in=cotangent, weight=(conv_fwd[1],), bias=(bias_wide[1],))
                outs.update(gz_out=field_shape, stat=(stat_shape,), bound=bound_shape)
                scratch.update(cot=field_buf, c_sem=dma)
            elif kind == "back":
                ins.update(a_in=keep.a1, gz_in=keep.gz1, g_in=cotangent, dg_in=keep.dg0, weight=(conv_bwd[1],))
                outs.update(ga_out=field_shape, gz_out=field_shape, cg=(cg_shape,), bg=(bg_shape,))
                scratch.update(dg=field_buf, dg_sem=dma)
            else:
                ins.update(a_in=inputs, gz_in=keep.gz0, g_in=keep.ga1, weight=(conv_bwd[0],))
                outs.update(cg=(cg_shape,), bg=(bg_shape,), bound=bound_shape)
            if kind in ("middle", "turn"):
                scratch.update(z_buf=field_buf, rid=pltpu.VMEM((rows_dev, width), jnp.int32), rid_sem=dma,
                               eo=energy, eb=energy)
            else:
                scratch.update(gz=field_buf, h=field_buf, gz_sem=dma, h_sem=dma)
            ins.update(itable=(it_doubled if kind in ("middle", "turn") else it_plain,), ikron=(ikron,))
            if kind != "tail":
                ins.update(table=(t_plain if kind == "middle" else t_doubled,), kron=(kron,))
                outs.update(p_out=p_shape)
                scratch.update(p_buf=pltpu.VMEM(full_dims, F32), p_local=dma((chunks,)), p_cross=dma((2, chunks)),
                               out_sem=dma((2, chunks)))
            if kind in ("turn", "tail"):
                scratch.update(b_local=dma((chunks,)), b_cross=dma((2, chunks)))
                if bound is not None:
                    ins.update(bound_in=bound)
                    aliases = dict(bound_in="bound")
            follow = (j + 1) % per_core
            follow_phase = phase + (1 if follow == 0 else 0)
            if follow_phase < len(kinds):
                body, layer = mixes[follow_phase]
                flip = body is mix_t_kernel
                ins.update(p_in=parts[follow], weights=spectral_w, far=far_weights)
                outs.update(f_out=f_shape, y_out=(y_shape,))
                mixed = 2 * G
                blocks_at = (channels, mixed) if flip else (mixed, channels)
                scratch.update(reduce_scratch, wbuf=pltpu.VMEM((8,) + blocks_at + (lanes,), F32), wsem=dma((8,)),
                               macc=pltpu.VMEM((kx_half, 2 * sections, channels * (G if flip else 1), lanes), F32),
                               msrc=pltpu.VMEM((2 * sections, mixed, lanes), F32))
            early = waiting.pop(0)
            if early is not None:
                ins.update(held=early[1])
                gathered[early[0]] = early[1]
            done = run(functools.partial(stage_kernel, kind, j, per_core, layer, flip), 1 + calls, ins, outs, scratch, aliases=aliases)
            calls += 1
            if kind != "tail":
                parts[j] = done.p_out
            if follow_phase < len(kinds):
                sums[follow_phase][follow], y = done.f_out, done.y_out
                waiting.append((f"{names[follow_phase]}{follow}", lax.all_gather(done.f_out, "batch", axis=0)))
            if kind in ("turn", "tail"):
                bound = done.bound
            if kind == "middle":
                keep.a1, keep.dg0, keep.stat0 = done.a_out, done.dg_out, done.stat
            elif kind == "turn":
                keep.gz1, keep.stat1 = done.gz_out, done.stat
            elif kind == "back":
                keep.ga1, keep.gz0, keep.cg1, keep.bg1 = done.ga_out, done.gz_out, done.cg, done.bg
            else:
                keep.cg0, keep.bg0 = done.cg, done.bg
    stats0, stats1, cg0, cg1, bg0, bg1 = [[getattr(k, name) for k in kept]
                                          for name in ("stat0", "stat1", "cg0", "cg1", "bg0", "bg1")]

    gathered.update(waiting)
    members = lax.axis_size("batch")
    grids = per_core * members * sections
    block = G
    blocks = channels // 2 // block
    in_buf = pltpu.VMEM((2, per_core, members, chunks, sections, count, lanes), F32)
    big, small = pltpu.VMEM((grids, channels, lanes), F32), pltpu.VMEM((grids, channels // 2, lanes), F32)
    grad_scratch = dict(fbuf=in_buf, gbuf=in_buf, in_sem=dma((2, 2)), f1=big, fs=small, d1=big, ds=big)
    row_dims = (2, channels // 2, channels, lanes)
    far_grad = run(functools.partial(far_grad_kernel, per_core), 1 + calls, gathered,
                   dict(far=jax.ShapeDtypeStruct((kx_half,) + row_dims, F32)),
                   dict(out=pltpu.VMEM((2, 2, block, channels, lanes), F32), send=dma((kx_half * blocks,)),
                        recv=dma((kx_half * blocks,)), **grad_scratch)).far
    bound_rows = bound.reshape(micro_count * rows_dev, channels, width)
    bound_block = pl.BlockSpec((bound_rows.shape[0] // (kx_half * blocks), channels, width),
                               lambda x, i, m: (x * blocks + i, 0, 0))
    grid_spec = pltpu.PrefetchScalarGridSpec(
        num_scalar_prefetch=1, grid=(kx_half, blocks),
        in_specs=[hbm] * len(gathered)
        + [pl.BlockSpec((None, 2, block, channels, lanes), lambda x, i, m: (x, 0, i, 0, 0)), bound_block],
        out_specs=[pl.BlockSpec((2, None, 2, block, channels, lanes), lambda x, i, m: (0, x, 0, i, 0, 0)), bound_block],
        scratch_shapes=list(grad_scratch.values()))
    spectral_grad, boundary = pl.pallas_call(
        functools.partial(own_grad_kernel, [*gathered, "far", "bound_in", "out", "bound_out", *grad_scratch], per_core),
        grid_spec=grid_spec, out_shape=[jax.ShapeDtypeStruct((2, kx_half) + row_dims, F32),
                                        jax.ShapeDtypeStruct(bound_rows.shape, F32)],
        cost_estimate=pl.CostEstimate(flops=0, bytes_accessed=150_000_000, transcendentals=0),
        compiler_params=params())(
            jnp.reshape(section, (1,)).astype(jnp.int32), *gathered.values(), far_grad, bound_rows)
    spectral_grad = spectral_grad.reshape(spectral_w.shape)
    boundary = boundary.reshape((1, micro_count, 1) + inputs.shape[2:])

    def lower(value):
        return (value[:channels, :channels] + value[channels:, channels:]
                + value[:channels, channels:] + value[channels:, :channels])

    conv_local = jnp.stack([lower(sum(cg0)), lower(sum(cg1))])
    bias_local = jnp.stack([jnp.sum(sum(bg0), -1), jnp.sum(sum(bg1), -1)])
    stat_local = jnp.stack([jnp.sum(sum(stats0), -1), jnp.sum(sum(stats1), -1)])
    shapes = [v.shape for v in (conv_local, bias_local, stat_local)]
    flat_sums = jnp.concatenate([v.reshape(-1) for v in (conv_local, bias_local, stat_local)])
    length = flat_sums.shape[0]
    flat_sums = jnp.pad(flat_sums, (0, -length % 1024)).reshape(-1, 128)
    flat_sums = jnp.sum(lax.all_gather(flat_sums, ("section", "batch", "rows"), axis=0), 0).reshape(-1)
    ends = np.cumsum([0] + [math.prod(shape) for shape in shapes])
    conv_sum, bias_sum, stat_sum = [flat_sums[ends[i]:ends[i + 1]].reshape(shapes[i]) for i in range(3)]
    own_stat = lax.dynamic_index_in_dim(stat_sum, section, 0, False)
    layer_rms = jnp.sqrt(own_stat[:2] / (channels * own_stat[2])[None, :] + 1e-06)[None]
    own = lambda value: lax.dynamic_slice_in_dim(value, section, 1, 0)
    return boundary, spectral_grad, own(conv_sum), own(bias_sum), layer_rms


def solution(mesh):
    placed = (
        P(None, "batch", "rows", None, None),
        P(None, "batch", "rows", None, None),
        P(None, "batch", "rows", None),
        P("section", "rows", None, None, None),
        P("section", None, None),
        P("section", None),
    )
    return jax.shard_map(
        local,
        mesh=mesh,
        in_specs=placed,
        out_specs=(
            P("section", None, "batch", "rows", None, None),
            P("section", "rows", None, None, None),
            P("section", None, None),
            P("section", None),
            P("section", None, None),
        ),
        check_vma=False,
    )
```

```python
import functools
import math
import types

import jax
import jax.numpy as jnp
import numpy as np
from jax import lax
from jax.experimental import pallas as pl
from jax.experimental.pallas import tpu as pltpu
from jax.sharding import PartitionSpec as P

R = 8
G = 8
AHEAD = 2
F32 = jnp.float32
BF16 = jnp.bfloat16
VMEM_LIMIT = 62 * 1024 * 1024
MESH = pl.DeviceIdType.MESH


def split(value):
    high = value.astype(BF16)
    return high, (value - high.astype(F32)).astype(BF16)


def dot(left, right, dims=(((1,), (0,)), ((), ()))):
    return lax.dot_general(left, right, dims, preferred_element_type=F32)


def dot3(left, right):
    return dot(left[0], right[0]) + (dot(left[1], right[0]) + dot(left[0], right[1]))


def np_split(value):
    high = value.astype(np.float32).astype(BF16)
    return high, (value - high.astype(np.float64)).astype(np.float32).astype(BF16)


def col_tables(width, half):
    phase = 2.0 * math.pi / width * (np.outer(np.arange(width), np.arange(half)) % width)
    cosine, sine = np.cos(phase) / math.sqrt(width), np.sin(phase) / math.sqrt(width)
    plain = np.concatenate([cosine, -sine, -sine, -cosine], 1)
    doubled = plain * np.tile(np.where(np.arange(half) == 0, 1.0, 2.0), 4)[None, :]
    return plain, doubled


def row_tables(height, mode_rows, first_row, rows_dev):
    position = jnp.arange(mode_rows, dtype=jnp.int32)
    frequency = jnp.where(position < mode_rows // 2, position, height - mode_rows + position)
    row = first_row + jnp.arange(rows_dev, dtype=jnp.int32)
    phase = 2.0 * math.pi / height * (frequency[:, None] * row[None, :] % height).astype(F32)
    small = jnp.concatenate([jnp.cos(phase), jnp.sin(phase)], 1) / math.sqrt(height)
    rounded = lax.reduce_precision(small, 8, 7)
    high, low = rounded.astype(BF16), (small - rounded).astype(BF16)
    forward = jnp.concatenate([jnp.concatenate([high, high], 1), jnp.concatenate([low, jnp.zeros_like(low)], 1)], 0)
    inverse = jnp.concatenate([high.T, high.T, low.T], 1)
    return forward, inverse


def to_modes(value, table, kron, spread, p_ref):
    mode_rows, count, lanes = p_ref.shape
    rows = value.shape[0] // count
    high, low = split(value)
    spectra = dot(jnp.concatenate([high, low, high], 1), table)
    for i in range(2):
        spread[i] = spectra[:, i * lanes:(i + 1) * lanes]
    out = p_ref.reshape(mode_rows * count, lanes)
    for first in range(0, count, 2):
        sides = []
        for c in (first, first + 1):
            pick = pl.ds(c, rows, stride=count)
            sides.append(jnp.concatenate([spread[i, pick, :] for i in range(2)], 0))
        high, low = split(jnp.concatenate(sides, 1))
        both = dot(kron, jnp.concatenate([high, low], 0))
        result = both[:mode_rows] + both[mode_rows:]
        for i in range(2):
            out[pl.ds(first + i, mode_rows, stride=count), :] = result[:, i * lanes:(i + 1) * lanes]


def from_modes(y_ref, table, kron, spread):
    mode_rows, count, lanes = y_ref.shape
    rows, pieces = spread.shape[1] // count, spread.shape[0]
    modes = y_ref.reshape(mode_rows * count, lanes)
    sides = []
    for first in range(0, count, 2):
        pair = [modes[pl.ds(c, mode_rows, stride=count), :] for c in (first, first + 1)]
        high, low = split(jnp.concatenate(pair, 1))
        both = dot(kron, jnp.concatenate([high, low, high], 0))
        for i in range(2):
            side = both[:, i * lanes:(i + 1) * lanes]
            sides.append(jnp.concatenate([side[:rows], side[rows:]], 1))
    high, low = split(jnp.concatenate(sides, 0))
    out = dot(jnp.concatenate([high, low, high], 1), table)
    for c in range(count):
        for i in range(pieces):
            spread[i, pl.ds(c, rows, stride=count), :] = out[c * rows:(c + 1) * rows, i * 128:(i + 1) * 128]
    return jnp.concatenate([spread[i] for i in range(pieces)], 1)


def gelu_parts(z):
    size = jnp.abs(z)
    gauss = jnp.exp(-0.5 * z * z)
    base = 1.0 + (0.3275911 / math.sqrt(2.0)) * size
    t = pl.reciprocal(base, approx=True)
    t = t * (2.0 - base * t)
    poly = t * (0.254829592 + t * (-0.284496736 + t * (1.421413741 + t * (-1.453152027 + t * 1.061405429))))
    tail = 0.5 * poly * gauss
    phi = jnp.where(z >= 0, 1.0 - tail, tail)
    return z * phi, phi + z * (gauss * (1.0 / math.sqrt(2.0 * math.pi)))


def flat(ref):
    rows, count, width = ref.shape
    return ref[...].reshape(rows * count, width)


def put(ref, value):
    ref[...] = value.reshape(ref.shape)


def place_and_peers():
    section, z = lax.axis_index("section"), lax.axis_index("rows")
    return section, z, lax.axis_size("rows")


def greet(section, z, n, lines, members=0):
    barrier = pltpu.get_barrier_semaphore()
    pl.semaphore_signal(barrier, inc=1, device_id={"section": 1 - section}, device_id_type=MESH)
    if not lines:
        pl.semaphore_wait(barrier, 1)
        return

    @pl.when(z > 0)
    def _():
        pl.semaphore_signal(barrier, inc=1, device_id={"rows": z - 1}, device_id_type=MESH)

    @pl.when(z < n - 1)
    def _():
        pl.semaphore_signal(barrier, inc=1, device_id={"rows": z + 1}, device_id_type=MESH)

    for away in range(1, members):
        pl.semaphore_signal(barrier, inc=1, device_id={"batch": lax.rem(lax.axis_index("batch") + away, members)},
                            device_id_type=MESH)

    others = 1 + max(members - 1, 0)
    pl.semaphore_wait(barrier, others + (z > 0).astype(jnp.int32) + (z < n - 1).astype(jnp.int32))


def to_core(src, dst, sems, section):
    return pltpu.make_async_remote_copy(src_ref=src, dst_ref=dst, send_sem=sems[0], recv_sem=sems[1],
                                        device_id={"section": 1 - section}, device_id_type=MESH)


def guard(condition, body):
    if isinstance(condition, (bool, np.bool_)):
        if condition:
            body()
    else:
        pl.when(condition)(body)


class Line:
    def __init__(self, section, z, n, chunks, send, recv):
        self.section, self.z, self.n, self.chunks = section, z, n, chunks
        self.send, self.recv = send, recv

    def move(self, way, q, hop, src, dst):
        return pltpu.make_async_remote_copy(
            src_ref=src, dst_ref=dst, send_sem=self.send.at[way, q, hop], recv_sem=self.recv.at[way, q, hop],
            device_id={"rows": self.z + 1 if way == 0 else self.z - 1}, device_id_type=MESH)

    def sends(self, way):
        return self.z < self.n - 1 if way == 0 else self.z > 0

    def hears(self, way):
        return self.z > 0 if way == 0 else self.z < self.n - 1


def within(value, count):
    return jnp.logical_and(value >= 0, value < count)


class Gather(Line):
    def __init__(self, section, z, n, r, parity):
        super().__init__(section, z, n, r.full.shape[1], r.send.at[parity], r.recv.at[parity])
        self.full, self.give_from = r.full.at[parity], r.y_give.at[parity]
        self.cross = r.y_cross.at[parity]

    def swap(self, q):
        return to_core(self.give_from.at[q], self.full.at[q, self.z, self.section],
                       (self.cross.at[0, q], self.cross.at[1, q]), self.section)

    def give(self, q):
        self.swap(q).start()

    def hop(self, way, q, hop):
        piece = self.full.at[q, self.source(way, hop)]
        return self.move(way, q, hop, piece, piece)

    def source(self, way, hop):
        return self.z - hop if way == 0 else self.z + hop

    def known(self, way, hop):
        at = self.source(way, hop)
        return at >= 0 if way == 0 else at < self.n

    def own(self, q):
        self.swap(q).wait_recv()
        for way in range(2):
            @pl.when(self.sends(way))
            def _():
                self.hop(way, q, 0).start()

    def step(self, q, hop):
        for way in range(2):
            @pl.when(self.known(way, hop + 1))
            def _():
                piece = self.full.at[q, self.source(way, hop + 1)]
                self.move(way, q, hop, piece, piece).wait_recv()

                @pl.when(self.sends(way))
                def _():
                    self.hop(way, q, hop + 1).start()

    def begin(self):
        for q in range(min(AHEAD, self.chunks)):
            self.own(q)

    def tick(self, t):
        @pl.when(t + AHEAD < self.chunks)
        def _():
            self.own(t + AHEAD)

        for hop in range(self.n - 1):
            q = t - hop - 1
            pl.when(within(q, self.chunks))(functools.partial(self.step, q, hop))

    def finish(self):
        def body(q, carry):
            self.swap(q).wait_send()
            for way in range(2):
                for hop in range(self.n - 1):
                    @pl.when(jnp.logical_and(self.sends(way), self.known(way, hop)))
                    def _():
                        self.hop(way, q, hop).wait_send()
            return carry

        lax.fori_loop(0, self.chunks, body, 0)


class Sum(Line):
    def __init__(self, section, z, n, r, parity, admit):
        super().__init__(section, z, n, r.part.shape[2], r.red_send.at[parity], r.red_recv.at[parity])
        self.part, self.come, self.keep, self.admit = r.part.at[parity], r.come.at[parity], r.keep.at[parity], admit

    def owner(self, way, hop):
        return self.z + self.n - hop if way == 0 else self.z - self.n + hop

    def valid(self, way, hop):
        return self.z <= hop - 1 if way == 0 else self.z >= self.n - hop

    def sent(self, way, q, hop):
        return self.move(way, q, hop, self.part.at[self.owner(way, hop), q], self.come.at[way, q, hop - 1])

    def heard(self, way, q, hop):
        come = self.come.at[way, q, hop - 1]
        self.move(way, q, hop, come, come).wait_recv()

    def first(self, q):
        self.admit(q)
        for way in range(2):
            @pl.when(jnp.logical_not(self.hears(way)))
            def _():
                for hop in range(1, self.n):
                    @pl.when(self.valid(way, hop))
                    def _():
                        self.sent(way, q, hop).start()

    def step(self, q, hop):
        for way in range(2):
            @pl.when(jnp.logical_and(self.valid(way, hop), self.hears(way)))
            def _():
                self.heard(way, q, hop - 1)
                owner = self.owner(way, hop)
                self.part[owner, q] = self.part[owner, q] + self.come[way, q, hop - 2]
                self.sent(way, q, hop).start()

    def final(self, q):
        for way in range(2):
            @pl.when(self.hears(way))
            def _():
                self.heard(way, q, self.n - 1)
                self.part[self.z, q] = self.part[self.z, q] + self.come[way, q, self.n - 2]

        self.keep[q] = self.part[self.z, q]

    def tick(self, t):
        pl.when(within(t, self.chunks))(functools.partial(self.first, t))
        for hop in range(2, self.n + 1):
            q = t - hop + 1
            pl.when(within(q, self.chunks))(
                functools.partial(self.step, q, hop) if hop < self.n else functools.partial(self.final, q))

    def finish(self):
        def body(q, carry):
            for way in range(2):
                for hop in range(1, self.n):
                    @pl.when(self.valid(way, hop))
                    def _():
                        self.sent(way, q, hop).wait_send()
            return carry

        lax.fori_loop(0, self.chunks, body, 0)


class Reduce(Line):
    def __init__(self, section, z, n, part, come, f_out, f_sem, send, recv, ahead):
        super().__init__(section, z, n, part.shape[1], send, recv)
        self.ahead = ahead
        self.part, self.come, self.f_out, self.f_sem = part, come, f_out, f_sem

    def owner(self, way, hop):
        return self.z + self.n - hop if way == 0 else self.z - self.n + hop

    def valid(self, way, hop):
        return self.z <= hop - 1 if way == 0 else self.z >= self.n - hop

    def sent(self, way, q, hop):
        return self.move(way, q, hop, self.part.at[self.owner(way, hop), q], self.come.at[way, q, hop])

    def heard(self, way, q, hop):
        come = self.come.at[way, q, hop]
        self.move(way, q, hop, come, come).wait_recv()

    def first(self, t):
        for hop in range(1, self.n):
            q = t - hop + 1

            def send():
                for way in range(2):
                    @pl.when(jnp.logical_and(self.valid(way, hop), jnp.logical_not(self.hears(way))))
                    def _():
                        self.sent(way, q, hop).start()

            guard(0 <= q < self.chunks if isinstance(q, int) else q < self.chunks, send)

    def step(self, q, hop):
        for way in range(2):
            @pl.when(jnp.logical_and(self.valid(way, hop), self.hears(way)))
            def _():
                self.heard(way, q, hop - 1)
                owner = self.owner(way, hop)
                self.part[owner, q] = self.part[owner, q] + self.come[way, q, hop - 1]
                self.sent(way, q, hop).start()

    def result(self, q):
        return pltpu.make_async_copy(self.part.at[self.z, q], self.f_out.at[q], self.f_sem.at[q])

    def final(self, q):
        for way in range(2):
            @pl.when(self.hears(way))
            def _():
                self.heard(way, q, self.n - 1)
                self.part[self.z, q] = self.part[self.z, q] + self.come[way, q, self.n - 1]

        self.result(q).start()

    def tick(self, t):
        if isinstance(t, int) and t == 0:
            for early in range(self.ahead):
                self.first(early)
        self.first(t + self.ahead)
        for hop in range(2, self.n + 1):
            q = t - hop + 1
            if isinstance(q, int):
                valid = 0 <= q < self.chunks
            else:
                valid = q < self.chunks
            guard(valid, functools.partial(self.step, q, hop) if hop < self.n else functools.partial(self.final, q))

    def finish(self):
        def body(q, carry):
            self.result(q).wait()
            for way in range(2):
                for hop in range(1, self.n):
                    @pl.when(self.valid(way, hop))
                    def _():
                        self.sent(way, q, hop).wait_send()
            return carry

        lax.fori_loop(0, self.chunks, body, 0)


def fetch(src, dst, sem, parts=4):
    step = dst.shape[0] // parts
    for i in range(parts):
        pltpu.make_async_copy(src.at[pl.ds(i * step, step)], dst.at[pl.ds(i * step, step)], sem).start()


def arrived(dst, sem):
    pltpu.make_async_copy(dst, dst, sem).wait()


def portions(total, count):
    return [(i * total // count, (i + 1) * total // count) for i in range(count)]


def conv_rows(weight, bias, a, out, first, last):
    channels, width = a.shape[1:]
    block = weight.shape[0] // channels

    def body(i, carry):
        at = pl.ds(i * block, block)
        high, low = split(a[at].reshape(block * channels, width))
        result = dot(weight[...], jnp.concatenate([high, high, low], 0)).reshape(block, channels, width)
        out[at] = result + bias[...][None] if bias is not None else out[at] + result
        return carry

    lax.fori_loop(first, last, body, 0)


def grad_rows(a, gz, cg_ref, bg_ref, first, last):
    channels, width = a.shape[1:]

    def body(r, carry):
        grad, bias = carry
        g = gz[r]
        left = jnp.concatenate(split(a[r]), 0)
        right = jnp.concatenate(split(g), 0)
        return grad + dot(left, right, (((1,), (1,)), ((), ()))), bias + g

    grad, bias = lax.fori_loop(first, last, body, (cg_ref[...], bg_ref[...]))
    cg_ref[...] = grad
    bg_ref[...] = bias


def chunk_of(ref, q, count):
    rows, _, width = ref.shape
    return ref[:, pl.ds(pl.multiple_of(q * count, count), count), :].reshape(rows * count, width)


def chunk_at(ref, q, count):
    return ref.at[:, pl.ds(pl.multiple_of(q * count, count), count), :]


class Modes:
    def __init__(self, section, buffer, p_out, local, cross):
        self.section, self.buffer, self.p_out, self.local, self.cross = section, buffer, p_out, local, cross

    def view(self, q):
        n, halves, kx, count, lanes = self.buffer.shape[1:]
        return self.buffer.at[q].reshape(n * halves * kx, count, lanes)

    def copies(self, q):
        s = self.section
        return (pltpu.make_async_copy(self.buffer.at[q, :, s], self.p_out.at[:, q, 0], self.local.at[q]),
                to_core(self.buffer.at[q, :, 1 - s], self.p_out.at[:, q, 1],
                        (self.cross.at[0, q], self.cross.at[1, q]), s))

    def start(self, q):
        for copy in self.copies(q):
            copy.start()

    def wait(self, q):
        for copy in self.copies(q):
            copy.wait()


class Bound:
    def __init__(self, section, owner, micro, other, source, bound, local, cross):
        self.section, self.owner, self.micro, self.other = section, owner, micro, other
        self.source, self.bound, self.local, self.cross = source, bound, local, cross

    def copies(self, q, count, micro):
        src, dst = chunk_at(self.source, q, count), chunk_at(self.bound.at[micro], q, count)
        return (pltpu.make_async_copy(src, dst, self.local.at[q]),
                to_core(src, dst, (self.cross.at[0, q], self.cross.at[1, q]), self.section))

    def start(self, q, count):
        here, there = self.copies(q, count, self.micro)

        @pl.when(self.section == self.owner)
        def _():
            here.start()

        @pl.when(self.section != self.owner)
        def _():
            there.start()

    def wait(self, q, count):
        here, there = self.copies(q, count, self.micro)
        come = self.copies(q, count, self.other)[1]

        @pl.when(self.section == self.owner)
        def _():
            here.wait()
            come.wait_recv()

        @pl.when(self.section != self.owner)
        def _():
            there.wait_send()


def add_squares(value, total):
    rows, _, width = total.shape
    square = (value * value).reshape(rows, -1, width)
    for at in range(0, square.shape[1], G):
        total[...] += square[:, at:at + G]


def region_sums(rid_ref, eo, eb, stat_ref):
    rows, _, width = eo.shape
    rid = rid_ref[...]
    energies = (jnp.sum(eo[...], axis=1), jnp.sum(eb[...], axis=1), jnp.ones((rows, width), F32))
    for kind in range(3):
        for region in range(R):
            line = jnp.sum(jnp.where(rid == region + 1, energies[kind], 0.0), axis=0, keepdims=True)
            total = line[:, :128]
            for piece in range(1, width // 128):
                total = total + line[:, piece * 128:(piece + 1) * 128]
            stat_ref[kind, region:region + 1, :] = total


def start_kernel(per_core, r):
    section, z, n = place_and_peers()
    chunks, count, half = r.p_buf.shape[1], r.p_buf.shape[5], r.far.shape[0]
    blocks = [(j, q) for j in range(per_core) for q in range(chunks)]
    reduce = Reduce(section, z, n, r.part, r.come, r.f_out, r.f_sem, r.red_send, r.red_recv, 0)
    outs = [r.part] + [getattr(r, f"p{j}") for j in range(1, per_core)]
    modes = [Modes(section, r.p_buf.at[j], outs[j], r.p_local.at[j], r.p_cross.at[j]) for j in range(per_core)]

    def field(k):
        j, q = blocks[k]
        src = chunk_at(r.inputs.at[section * per_core + j, 0], q, count)
        return pltpu.make_async_copy(src, r.a_buf.at[k % 2], r.a_sem.at[k % 2])

    def weight_in(x):
        return pltpu.make_async_copy(r.weights.at[0, (1 - section) * half + x], r.w_buf.at[x % 2], r.w_sem.at[x % 2])

    def weight_out(x):
        return to_core(r.w_buf.at[x % 2], r.far.at[x], (r.w_cross.at[0, x], r.w_cross.at[1, x]), section)

    def lend(x):
        if x < half:
            weight_in(x).wait()
            weight_out(x).start()
        if 1 <= x <= half:
            weight_out(x - 1).wait_send()
            if x + 1 < half:
                weight_in(x + 1).start()

    field(0).start()
    for x in range(min(2, half)):
        weight_in(x).start()
    greet(section, z, n, True)
    for k, (j, q) in enumerate(blocks):
        if k + 1 < len(blocks):
            field(k + 1).start()
        field(k).wait()
        to_modes(flat(r.a_buf.at[k % 2]), r.table[...], r.kron[...], r.spread, modes[j].view(q))
        modes[j].start(q)
        lend(k)
        if k >= 1:
            if k <= chunks:
                modes[0].wait(k - 1)
            reduce.tick(k - 1)
    for k in range(len(blocks), half + 1):
        lend(k)
    for t in range(len(blocks) - 1, chunks + n - 1):
        reduce.tick(t)
    for x in range(half):
        weight_out(x).wait_recv()
    for j, q in blocks[chunks:]:
        modes[j].wait(q)
    reduce.finish()


class Share:
    def __init__(self, r, index, parity):
        self.r, self.index, self.parity = r, index, parity
        self.me, self.members = lax.axis_index("batch"), lax.axis_size("batch")

    def copies(self):
        source, target = self.r.keep.at[self.parity], getattr(self.r, f"shared{self.index}").at[self.me]
        yield pltpu.make_async_copy(source, target, self.r.s_local.at[self.parity])
        for away in range(1, self.members):
            yield pltpu.make_async_remote_copy(
                src_ref=source, dst_ref=target, send_sem=self.r.s_send.at[self.parity, away],
                recv_sem=self.r.s_recv.at[self.index, away],
                device_id={"batch": lax.rem(self.me + away, self.members)}, device_id_type=MESH)

    def start(self):
        for copy in self.copies():
            copy.start()

    def wait_send(self):
        for i, copy in enumerate(self.copies()):
            if i == 0:
                copy.wait()
            else:
                copy.wait_send()

    def wait_recv(self):
        for i, copy in enumerate(self.copies()):
            if i > 0:
                copy.wait_recv()


class Stage:
    def __init__(self, k, kind, j, per_core, places, section, z, n, r):
        self.k, self.kind, self.j, self.r, self.section, self.n = k, kind, j, r, section, n
        self.parity = k % 2
        self.micro, self.other = section * per_core + j, (1 - section) * per_core + j
        self.forward, self.last = kind in ("middle", "turn"), kind == "tail"
        self.buffers = {name: r.fields.at[i] for name, i in places.items()}
        self.sems = {name: r.field_sem.at[i] for name, i in places.items()}
        self.gather = Gather(section, z, n, r, self.parity)
        self.count, self.lanes = r.full.shape[5], r.full.shape[6]
        self.chunks = r.full.shape[1]
        plain = lambda name: getattr(r, f"{name}{j}")
        if kind == "middle":
            self.loads = dict(a=r.inputs.at[self.micro, 0])
            self.saves = dict(a=plain("a1_"), z=plain("dg0_"))
        elif kind == "turn":
            self.loads = dict(a=plain("a1_"), cot=r.cotangent.at[self.micro, 0])
            self.saves = dict(cot=plain("gz1_"))
        elif kind == "back":
            self.loads = dict(gz=plain("gz1_"), h=r.cotangent.at[self.micro, 0], a=plain("a1_"), dg=plain("dg0_"))
            self.saves = dict(h=plain("ga1_"), dg=plain("gz0_"))
        else:
            self.loads = dict(gz=plain("gz0_"), h=plain("ga1_"), a=r.inputs.at[self.micro, 0])
            self.saves = {}
        layer = 0 if kind in ("middle", "tail") else 1
        self.weight = getattr(r, f"conv_{'f' if self.forward else 'b'}{layer}")
        self.bias = getattr(r, f"bias{layer}")
        self.table = r.t_plain if kind == "middle" else r.t_doubled
        self.itable = r.it_doubled if self.forward else r.it_plain
        if not self.last:
            self.modes = Modes(section, r.p_buf, r.part.at[self.parity], r.p_local, r.p_cross.at[self.parity])
        if kind in ("turn", "tail"):
            self.bound = Bound(section, 1 if kind == "turn" else 0, self.micro, self.other,
                               self.buffers["a" if kind == "turn" else "h"], r.bound,
                               r.b_local.at[self.parity], r.b_cross.at[self.parity])

    def prefetch(self):
        for name, src in self.loads.items():
            fetch(src, self.buffers[name], self.sems[name])
        if self.forward:
            self.rid_copy().start()

    def rid_copy(self):
        return pltpu.make_async_copy(self.r.region.at[self.micro, 0], self.r.rid.at[self.parity],
                                     self.r.rid_sem.at[self.parity])

    def got(self, name):
        arrived(self.buffers[name], self.sems[name])

    def open(self):
        r, b = self.r, self.buffers
        if self.forward:
            r.eo[...] = jnp.zeros_like(r.eo)
            r.eb[...] = jnp.zeros_like(r.eb)
            self.got("a")
        else:
            for name in ("gz", "h", "a"):
                self.got(name)
            at = self.k - self.r.first_back
            r.cg[at] = jnp.zeros_like(r.cg[at])
            r.bg[at] = jnp.zeros_like(r.bg[at])

    def before(self, i):
        r, b = self.r, self.buffers
        a = b["a"]
        rows, channels = a.shape[:2]
        blocks, parts = rows // (self.weight.shape[0] // channels), self.n - 1
        span = (i * blocks // parts, (i + 1) * blocks // parts)
        if self.forward:
            conv_rows(self.weight, self.bias, a, b["z"], *span)
        else:
            conv_rows(self.weight, None, b["gz"], b["h"], *span)
            at = self.k - r.first_back
            grad_rows(a, b["gz"], r.cg.at[at], r.bg.at[at], i * rows // parts, (i + 1) * rows // parts)

    def outs(self, q):
        return [pltpu.make_async_copy(chunk_at(self.buffers[name], q, self.count), chunk_at(dst, q, self.count),
                                      self.r.out_sem.at[self.parity, i, q])
                for i, (name, dst) in enumerate(self.saves.items())]

    def late(self):
        for name in ("cot", "dg"):
            if name in self.loads:
                self.got(name)

    def chunk(self, q):
        r, b, count = self.r, self.buffers, self.count
        spectral = from_modes(self.gather.full.at[q].reshape(-1, count, self.lanes), self.itable[...], r.ikron[...],
                              r.spread)
        if self.forward:
            branch, slope = gelu_parts(spectral + chunk_of(b["z"], q, count))
            if self.kind == "turn":
                put(chunk_at(b["cot"], q, count), chunk_of(b["cot"], q, count) * slope)
            else:
                put(chunk_at(b["z"], q, count), slope)
            add_squares(branch, r.eb)
            out = chunk_of(b["a"], q, count) + branch
            put(chunk_at(b["a"], q, count), out)
            add_squares(out, r.eo)
            source = b["cot" if self.kind == "turn" else "a"]
        else:
            ga = spectral + chunk_of(b["h"], q, count)
            put(chunk_at(b["h"], q, count), ga)
            if not self.last:
                put(chunk_at(b["dg"], q, count), ga * chunk_of(b["dg"], q, count))
                source = b["dg"]
        for copy in self.outs(q):
            copy.start()
        if self.kind in ("turn", "tail"):
            self.bound.start(q, count)
        if not self.last:
            to_modes(chunk_of(source, q, count), self.table[...], r.kron[...], r.spread, self.modes.view(q))

            pl.when(q == self.chunks - 1)(self.gather.finish)
            self.modes.start(q)

    def end(self):
        if self.forward:
            self.rid_copy().wait()
            region_sums(self.r.rid.at[self.parity], self.r.eo, self.r.eb, self.r.stat.at[self.k])
        if self.last:
            self.gather.finish()

    def close(self):
        def body(q, carry):
            for copy in self.outs(q):
                copy.wait()
            if self.kind in ("turn", "tail"):
                self.bound.wait(q, self.count)
            return carry

        lax.fori_loop(0, self.chunks, body, 0)


def stages_kernel(per_core, kinds, places, mixes, r):
    section, z, n = place_and_peers()
    chunks = r.full.shape[1]
    r.first_back = 2 * per_core
    stages = [Stage(k, kind, j, per_core, places[k], section, z, n, r)
              for k, (kind, j) in enumerate((kind, j) for kind in kinds for j in range(per_core))]
    ticks = chunks + n - 1
    stages[0].prefetch()
    first = [pltpu.make_async_copy(r.p_in, r.part.at[1], r.first_sem.at[0]),
             pltpu.make_async_copy(r.y_in.at[0], r.full.at[0, :, z, section], r.first_sem.at[1]),
             pltpu.make_async_copy(r.y_in.at[1], r.y_give.at[0], r.first_sem.at[2])]
    for copy in first:
        copy.start()
    greet(section, z, n, True, lax.axis_size("batch"))
    for copy in first:
        copy.wait()
    for q in range(chunks):
        stages[0].gather.give(q)
    shares = []
    sums = Sum(section, z, n, r, 1, lambda q: None)
    for k, stage in enumerate(stages):
        gather = stage.gather
        now = None if stage.last else Sum(section, z, n, r, stage.parity, stage.modes.wait)
        mix = None
        if sums is not None:
            mix = Mix(section, z, *mixes[(k + 1) // per_core], sums, stages[k + 1].gather, r)
            share = Share(r, k, 1 - stage.parity)
            if k >= 2:
                shares[k - 2].wait_send()
            shares.append(share)
            mix.prime()
        lead = 0 if k == 0 else chunks - 1
        ready = n - 1 - lead
        gather.begin()
        stage.open()

        def early(i, carry):
            if sums is not None:
                sums.tick(i + lead)
            gather.tick(i)
            stage.before(i)
            if mix is not None and not mix.flip:
                pl.when(within(i - ready, chunks))(lambda: mix.chunk(i - ready))
            return carry

        lax.fori_loop(0, n - 1, early, 0)
        if k > 0:
            stages[k - 1].close()
        if k + 1 < len(stages):
            stages[k + 1].prefetch()
        stage.late()

        def later(q, carry):
            i = q + n - 1
            if sums is not None:
                sums.tick(i + lead)
            if now is not None:
                now.tick(i - n)
            gather.tick(i)
            stage.chunk(q)
            if mix is not None:
                if mix.flip:
                    pl.when(q == 0)(sums.finish)
                    mix.chunk(q)
                else:
                    pl.when(within(i - ready, chunks))(lambda: mix.chunk(i - ready))
            return carry

        lax.fori_loop(0, chunks, later, 0)
        if mix is not None:
            if not mix.flip:
                sums.finish()
            mix.finish()
            share.start()
        stage.end()
        sums = now
    stages[-1].close()
    for share in shares[-2:]:
        share.wait_send()
    for share in shares:
        share.wait_recv()


def swap_halves(value):
    return pltpu.roll(value, value.shape[-1] // 2, value.ndim - 1)


def left_lanes(shape):
    return lax.broadcasted_iota(jnp.int32, shape, len(shape) - 1) < shape[-1] // 2


SLOTS = 4


def weight_stream(own, base, local_ref, far_ref, wbuf, sem):
    step, count = pl.program_id(0), pl.num_programs(0)

    def begin(at):
        slot = lax.rem(at, SLOTS)

        @pl.when(own)
        def _():
            fetch(local_ref.at[0, base + at], wbuf.at[slot], sem.at[slot])

        @pl.when(jnp.logical_not(own))
        def _():
            fetch(far_ref.at[at], wbuf.at[slot], sem.at[slot])

    @pl.when(step == 0)
    def _():
        for at in range(SLOTS - 1):
            @pl.when(at < count)
            def _():
                begin(at)

    @pl.when(step + SLOTS - 1 < count)
    def _():
        begin(step + SLOTS - 1)

    slot = lax.rem(step, SLOTS)
    arrived(wbuf.at[slot], sem.at[slot])
    return wbuf.at[slot]


def pieces(array):
    return [array[at:at + G] for at in range(0, array.shape[0], G)]


def spread_row(ref, row):
    return ref[pl.ds(row, G, stride=0), :]


def mix_kernel(m_ref, f_ref, local_ref, far_ref, y_ref, wbuf, f1, f2, sem):
    weight = weight_stream(m_ref[0] == 1, m_ref[1], local_ref, far_ref, wbuf, sem)
    grids, channels, lanes = f1.shape
    for g in range(grids):
        f1[g] = f_ref[:, g].reshape(channels, lanes)
    f2[...] = swap_halves(f1[...])
    groups = channels // G

    def body(block, acc):
        at = pl.multiple_of(block * G, G)
        acc = list(acc)
        for u in range(G):
            rows = [spread_row(f.at[g], at + u) for g in range(grids) for f in (f1, f2)]
            for o in range(groups):
                w = weight[at + u, o * G:(o + 1) * G, :]
                for k, row in enumerate(rows):
                    acc[k * groups + o] = acc[k * groups + o] + row * w
        return tuple(acc)

    acc = lax.fori_loop(0, groups, body, tuple(jnp.zeros((G, lanes), F32) for _ in range(2 * grids * groups)))
    left = left_lanes((channels, lanes))
    for g in range(grids):
        a, b = [jnp.concatenate(acc[k * groups:(k + 1) * groups], 0) for k in (2 * g, 2 * g + 1)]
        y_ref[g] = jnp.where(left, a - swap_halves(a), b + swap_halves(b)).reshape(y_ref.shape[1:])


def mix_t_kernel(m_ref, d_ref, local_ref, far_ref, y_ref, wbuf, a1, a2, sem):
    weight = weight_stream(m_ref[0] == 1, m_ref[1], local_ref, far_ref, wbuf, sem)
    grids, channels, lanes = a1.shape
    d = [d_ref[:, g].reshape(channels, lanes) for g in range(grids)]
    d1 = [pieces(d[g]) for g in range(grids)]
    d2 = [pieces(swap_halves(d[g])) for g in range(grids)]
    groups = channels // G

    def body(block, carry):
        at = pl.multiple_of(block * G, G)
        rows = [[] for _ in range(2 * grids)]
        for u in range(G):
            total = [None] * (2 * grids)
            for o in range(groups):
                w = weight[at + u, o * G:(o + 1) * G, :]
                for g in range(grids):
                    for side, source in enumerate((d1, d2)):
                        term = w * source[g][o]
                        k = 2 * g + side
                        total[k] = term if total[k] is None else total[k] + term
            for k in range(2 * grids):
                rows[k].append(jnp.sum(total[k], axis=0, keepdims=True))
        for g in range(grids):
            a1[g, pl.ds(at, G), :] = jnp.concatenate(rows[2 * g], 0)
            a2[g, pl.ds(at, G), :] = jnp.concatenate(rows[2 * g + 1], 0)
        return carry

    lax.fori_loop(0, groups, body, 0)
    left = left_lanes((channels, lanes))
    for g in range(grids):
        a, b = a1[g], a2[g]
        y_ref[g] = jnp.where(left, a + swap_halves(a), swap_halves(b) - b).reshape(y_ref.shape[1:])


class Mix:
    def __init__(self, section, z, layer, flip, sums, gather, r):
        self.section, self.z, self.layer, self.flip, self.r = section, z, layer, flip, r
        self.sums, self.gather = sums, gather
        self.chunks, self.grids, self.half, self.count, self.lanes = sums.part.shape[1:]
        self.channels, self.slots = r.weights.shape[2], r.wbuf.shape[0]
        self.blocks = self.chunks * self.half

    def begin(self, block):
        q, x = block // self.half, block % self.half
        slot = lax.rem(block, self.slots)
        rows = pl.ds(q * self.count, self.count)

        @pl.when(self.section == self.layer)
        def _():
            pltpu.make_async_copy(self.r.weights.at[0, self.section * self.half + x, rows], self.r.wbuf.at[slot],
                                  self.r.wsem.at[slot]).start()

        @pl.when(self.section != self.layer)
        def _():
            pltpu.make_async_copy(self.r.far.at[x, rows], self.r.wbuf.at[slot], self.r.wsem.at[slot]).start()

    def prime(self):
        for block in range(min(self.slots, self.blocks)):
            self.begin(jnp.int32(block))
        if not self.flip:
            self.r.macc[...] = jnp.zeros_like(self.r.macc)

    def chunk(self, q):
        def body(x, carry):
            block = q * self.half + x
            slot = lax.rem(block, self.slots)
            weight = self.r.wbuf.at[slot]
            arrived(weight, self.r.wsem.at[slot])
            (self.transposed if self.flip else self.forward)(q, x, weight)

            @pl.when(block + self.slots < self.blocks)
            def _():
                self.begin(block + self.slots)

            return carry

        lax.fori_loop(0, self.half, body, 0)
        if self.flip:
            self.gather.give(q)

    def forward(self, q, x, weight):
        sides, groups = 2 * self.grids, self.channels // G
        total, source = self.r.macc.at[x], self.r.msrc
        for g in range(self.grids):
            value = self.sums.part[self.z, q, g, x]
            source[2 * g, :self.count] = value
            source[2 * g + 1, :self.count] = swap_halves(value)
        keys = [(k, o) for k in range(sides) for o in range(groups)]

        def body(octet, acc):
            acc = dict(zip(keys, acc))
            for u in range(G):
                i = octet * G + u
                rows = [spread_row(source.at[k], i) for k in range(sides)]
                for o in range(groups):
                    w = weight[i, o * G:(o + 1) * G, :]
                    for k in range(sides):
                        acc[k, o] = acc[k, o] + rows[k] * w
            return tuple(acc[key] for key in keys)

        acc = lax.fori_loop(0, self.count // G, body, tuple(total[k, o * G:(o + 1) * G, :] for k, o in keys))
        for key, value in zip(keys, acc):
            total[key[0], key[1] * G:(key[1] + 1) * G, :] = value

    def transposed(self, q, x, weight):
        sides, groups = 2 * self.grids, self.channels // G
        source = self.r.msrc
        for g in range(self.grids):
            value = jnp.concatenate([self.sums.part[self.z, at, g, x] for at in range(self.chunks)], 0)
            source[2 * g] = value
            source[2 * g + 1] = swap_halves(value)
        rows = [pieces(source[k]) for k in range(sides)]
        out = [[] for _ in range(sides)]
        for i in range(self.count):
            total = [None] * sides
            for o in range(groups):
                w = weight[i, o * G:(o + 1) * G, :]
                for k in range(sides):
                    term = w * rows[k][o]
                    total[k] = term if total[k] is None else total[k] + term
            for k in range(sides):
                out[k].append(jnp.sum(total[k], axis=0, keepdims=True))
        left = left_lanes((self.count, self.lanes))
        for g in range(self.grids):
            a, b = [jnp.concatenate(out[2 * g + side], 0) for side in range(2)]
            self.put(g, q, x, jnp.where(left, a + swap_halves(a), swap_halves(b) - b))

    def put(self, g, q, x, value):
        if g == 0:
            self.gather.full[q, self.z, self.section, x] = value
        else:
            self.gather.give_from[q, x] = value

    def finish(self):
        if self.flip:
            return
        left = left_lanes((self.channels, self.lanes))

        def body(x, carry):
            for g in range(self.grids):
                a, b = [self.r.macc[x, 2 * g + side] for side in range(2)]
                result = jnp.where(left, a - swap_halves(a), b + swap_halves(b))
                for q in range(self.chunks):
                    self.put(g, q, x, result[q * self.count:(q + 1) * self.count])
            return carry

        lax.fori_loop(0, self.half, body, 0)
        for q in range(self.chunks):
            self.gather.give(q)


def grad_tables(f_ref, d_ref, f1, fs, d1, ds):
    channels, lanes = f1.shape[1:]
    left = left_lanes((channels // 2, lanes))
    at = 0
    for stream in range(f_ref.shape[0]):
        for member in range(f_ref.shape[1]):
            for g in range(f_ref.shape[3]):
                f = f_ref[stream, member, :, g].reshape(channels, lanes)
                f1[at] = f
                less = f - swap_halves(f)
                fs[at] = jnp.where(left, less[:channels // 2], -less[channels // 2:])
                d = d_ref[stream, member, :, g].reshape(channels, lanes)
                d1[at] = d
                ds[at] = d + swap_halves(d)
                at += 1


def grad_block(first_row, f1, fs, d1, ds, out):
    count, channels, lanes = f1.shape
    groups, middle = channels // G, channels // 2
    left = left_lanes((G, lanes))

    def body(octet, carry):
        at = pl.multiple_of(octet * G, G)
        low = first_row + at
        for first in range(0, G, 2):
            acc = [[None] * groups for _ in range(6)]
            for g in range(count):
                factors = [spread_row(ref, row) for u in range(first, first + 2)
                           for ref, row in ((f1.at[g], low + u), (f1.at[g], middle + low + u), (fs.at[g], low + u))]
                for o in range(groups):
                    d, e = d1[g, o * G:(o + 1) * G, :], ds[g, o * G:(o + 1) * G, :]
                    for k, factor in enumerate(factors):
                        term = factor * (e if k % 3 == 2 else d)
                        acc[k][o] = term if acc[k][o] is None else acc[k][o] + term
            for u in range(2):
                for o in range(groups):
                    p = acc[3 * u + 2][o]
                    for side in range(2):
                        m = acc[3 * u + side][o]
                        n = swap_halves(m)
                        third = swap_halves(p) if side == 0 else p
                        out[side, at + first + u, o * G:(o + 1) * G, :] = jnp.where(left, m + n, m - n + third)
        return carry

    lax.fori_loop(0, out.shape[1] // G, body, 0)


class GradInput:
    def __init__(self, first, f, g, fbuf, gbuf, sem):
        self.first, self.f, self.g, self.fbuf, self.gbuf, self.sem = first, f, g, fbuf, gbuf, sem

    def load(self, x, slot):
        for layer, condition in enumerate((self.first, jnp.logical_not(self.first))):
            @pl.when(condition)
            def _():
                for j in range(len(self.f[layer])):
                    pltpu.make_async_copy(self.f[layer][j].at[:, :, :, x], self.fbuf.at[slot, j],
                                          self.sem.at[0, slot]).start()
                    pltpu.make_async_copy(self.g[layer][j].at[:, :, :, x], self.gbuf.at[slot, j],
                                          self.sem.at[1, slot]).start()

    def next(self, x, count):
        slot = lax.rem(x, 2)

        @pl.when(x + 1 < count)
        def _():
            self.load(x + 1, 1 - slot)

        arrived(self.fbuf.at[slot], self.sem.at[0, slot])
        arrived(self.gbuf.at[slot], self.sem.at[1, slot])
        return self.fbuf.at[slot], self.gbuf.at[slot]


def grad_input(r, first, per_core):
    f = [[getattr(r, f"f{layer}{j}") for j in range(per_core)] for layer in range(2)]
    g = [[getattr(r, f"g{layer}{j}") for j in range(per_core)] for layer in range(2)]
    return GradInput(first, f, g, r.fbuf, r.gbuf, r.in_sem)


def far_grad_kernel(per_core, r):
    section, z, n = place_and_peers()
    half = r.far.shape[0]
    block = r.out.shape[2]
    blocks = r.far.shape[2] // block
    source = grad_input(r, section != 0, per_core)

    def move(k, slot):
        x, i = k // blocks, k % blocks
        return to_core(r.out.at[slot], r.far.at[x, :, pl.ds(i * block, block)], (r.send.at[k], r.recv.at[k]), section)

    source.load(0, 0)
    greet(section, z, n, False)

    def body(x, carry):
        grad_tables(*source.next(x, half), r.f1, r.fs, r.d1, r.ds)

        def inner(i, carry):
            k = x * blocks + i

            @pl.when(k >= 2)
            def _():
                move(k - 2, lax.rem(k, 2)).wait_send()

            grad_block(i * block, r.f1, r.fs, r.d1, r.ds, r.out.at[lax.rem(k, 2)])
            move(k, lax.rem(k, 2)).start()
            return carry

        return lax.fori_loop(0, blocks, inner, carry)

    lax.fori_loop(0, half, body, 0)
    total = half * blocks
    for k in (total - 2, total - 1):
        move(k, k % 2).wait_send()

    def close(k, carry):
        move(k, 0).wait_recv()
        return carry

    lax.fori_loop(0, total, close, 0)


def own_grad_kernel(names, per_core, m_ref, *refs):
    r = types.SimpleNamespace(**dict(zip(names, refs)))
    x, i = pl.program_id(0), pl.program_id(1)
    source = grad_input(r, m_ref[0] == 0, per_core)

    @pl.when(i == 0)
    def _():
        @pl.when(x == 0)
        def _():
            source.load(0, 0)

        grad_tables(*source.next(x, pl.num_programs(0)), r.f1, r.fs, r.d1, r.ds)

    r.bound_out[...] = r.bound_in[...]
    r.out[1 - m_ref[0]] = r.far[...]
    grad_block(i * r.out.shape[2], r.f1, r.fs, r.d1, r.ds, r.out.at[m_ref[0]])


def whole(array):
    return pl.BlockSpec(array.shape, lambda *_: (0,) * array.ndim)


def params(**kw):
    return pltpu.CompilerParams(vmem_limit_bytes=VMEM_LIMIT, **kw)


def local(inputs, cotangent, region_id, spectral_w, conv_w, bias_vector):
    micro_count, _, rows_dev, channels, width = inputs.shape
    lanes = spectral_w.shape[-1]
    half = lanes // 2
    kx_dev = spectral_w.shape[1]
    row_devices, sections = lax.axis_size("rows"), lax.axis_size("section")
    mode_rows, height = kx_dev * row_devices, rows_dev * row_devices
    section = lax.axis_index("section")
    per_core = micro_count // sections
    kx_half = kx_dev // sections

    plain, doubled = col_tables(width, half)

    def stacked(array):
        high, low = np_split(array)
        return np.concatenate([high, high, low], 0)

    t_plain, t_doubled, it_plain, it_doubled = [stacked(t) for t in (plain, doubled, plain.T, doubled.T)]
    kron, ikron = row_tables(height, mode_rows, lax.axis_index("rows") * rows_dev, rows_dev)

    count = 2 * G
    chunks = channels // count
    hbm, vmem = pl.BlockSpec(memory_space=pl.ANY), pl.BlockSpec(memory_space=pltpu.VMEM)
    field_shape = jax.ShapeDtypeStruct((rows_dev, channels, width), F32)
    part_dims = (row_devices, chunks, sections, kx_half, count, lanes)
    p_shape, f_shape = jax.ShapeDtypeStruct(part_dims, F32), jax.ShapeDtypeStruct(part_dims[1:], F32)
    y_shape = jax.ShapeDtypeStruct((sections, chunks, kx_half, count, lanes), F32)
    stat_shape = jax.ShapeDtypeStruct((3, R, 128), F32)
    cg_shape = jax.ShapeDtypeStruct((2 * channels, 2 * channels), F32)
    bg_shape = jax.ShapeDtypeStruct((channels, width), F32)
    bound_shape = jax.ShapeDtypeStruct((micro_count, rows_dev, channels, width), F32)
    dma = pltpu.SemaphoreType.DMA
    field_buf = pltpu.VMEM((rows_dev, channels, width), F32)
    full_dims = (chunks, row_devices, sections, kx_half, count, lanes)
    spread = pltpu.VMEM((width // 128, rows_dev * count, 128), F32)
    energy = pltpu.VMEM((rows_dev, G, width), F32)
    line_sems = dma((2, chunks, row_devices))
    start_scratch = dict(part=pltpu.VMEM(part_dims, F32), come=pltpu.VMEM((2, chunks, row_devices) + part_dims[2:], F32),
                         f_sem=dma((chunks,)), red_send=line_sems, red_recv=line_sems)

    def run(body, ident, ins, outs, scratch, cost=50, aliases=None):
        names = [*ins, *outs, *scratch]
        spec = lambda entry: vmem if isinstance(entry, tuple) else hbm
        plain = lambda entry: entry[0] if isinstance(entry, tuple) else entry
        kernel = lambda *refs: body(types.SimpleNamespace(**dict(zip(names, refs))))
        positions = {list(ins).index(k): list(outs).index(v) for k, v in (aliases or {}).items()}
        result = pl.pallas_call(
            kernel, in_specs=[spec(e) for e in ins.values()], out_specs=[spec(e) for e in outs.values()],
            out_shape=[plain(e) for e in outs.values()], scratch_shapes=list(scratch.values()),
            input_output_aliases=positions,
            cost_estimate=pl.CostEstimate(flops=0, bytes_accessed=cost * 3_000_000, transcendentals=0),
            compiler_params=params(collective_id=ident, has_side_effects=True))(*[plain(e) for e in ins.values()])
        return types.SimpleNamespace(**dict(zip(outs, result)))

    conv_rows_at_once = 256 // channels
    conv_both = lax.all_gather(conv_w, "section", axis=0, tiled=True)
    bias_both = lax.all_gather(bias_vector, "section", axis=0, tiled=True)

    def conv_parts(matrix):
        wide = jnp.kron(jnp.eye(conv_rows_at_once, dtype=F32), matrix)
        rounded = lax.reduce_precision(wide, 8, 7)
        high, low = rounded.astype(BF16), (wide - rounded).astype(BF16)
        return jnp.concatenate([high, low, high], 1)

    conv_fwd = [conv_parts(conv_both[l].T) for l in range(2)]
    conv_bwd = [conv_parts(conv_both[l]) for l in range(2)]
    bias_wide = [jnp.broadcast_to(bias_both[l][:, None], (channels, width)) for l in range(2)]

    def mixing(body, layer, pair):
        flag = jnp.stack([(section == layer).astype(jnp.int32), section * kx_half])
        f_block = pl.BlockSpec((chunks, sections, None, count, lanes), lambda x, m: (0, 0, x, 0, 0))
        y_block = pl.BlockSpec((sections, chunks, None, count, lanes), lambda x, m: (0, 0, x, 0, 0))
        small = pltpu.VMEM((sections, channels, lanes), F32)
        grid_spec = pltpu.PrefetchScalarGridSpec(
            num_scalar_prefetch=1, grid=(kx_half,), in_specs=[f_block, hbm, hbm], out_specs=y_block,
            scratch_shapes=[pltpu.VMEM((SLOTS, channels, channels, lanes), F32), small, small, dma((SLOTS,))])
        return pl.pallas_call(
            body, grid_spec=grid_spec, out_shape=y_shape, compiler_params=params(),
            cost_estimate=pl.CostEstimate(flops=0, bytes_accessed=30_000_000, transcendentals=0))(
                flag, pair, spectral_w, far_weights)

    streams = range(per_core)
    start = run(
        functools.partial(start_kernel, per_core), 0,
        dict(inputs=inputs, weights=spectral_w, table=(t_plain,), kron=(kron,)),
        dict(f_out=f_shape, far=jax.ShapeDtypeStruct((kx_half,) + spectral_w.shape[2:], F32),
             **{f"p{j}": p_shape for j in streams[1:]}),
        dict(a_buf=pltpu.VMEM((2, rows_dev, count, width), F32), w_buf=pltpu.VMEM((2,) + spectral_w.shape[2:], F32),
             p_buf=pltpu.VMEM((per_core,) + full_dims, F32), spread=spread, a_sem=dma((2,)), w_sem=dma((2,)),
             w_cross=dma((2, kx_half)), p_local=dma((per_core, chunks)), p_cross=dma((per_core, 2, chunks)),
             **start_scratch))
    far_weights = start.far

    members = lax.axis_size("batch")
    kinds = ["middle", "turn", "back", "tail"]
    mixes = [(0, False), (1, False), (1, True), (0, True)]
    names = ["f01", "f10", "f11", "g10", "g11", "g00", "g01"]
    places = [dict(a=0, z=1), dict(a=2, z=3), dict(a=4, z=5, cot=6), dict(a=0, z=1, cot=2),
              dict(gz=3, a=4, h=5, dg=6), dict(gz=0, a=1, h=2, dg=3), dict(gz=4, a=5, h=6), dict(gz=0, a=1, h=2)]
    y = mixing(mix_kernel, 0, start.f_out)
    both = (2,)
    ins = dict(inputs=inputs, cotangent=cotangent, region=region_id, weights=spectral_w, far=far_weights,
               p_in=start.p1, y_in=y, t_plain=(t_plain,), t_doubled=(t_doubled,), it_plain=(it_plain,),
               it_doubled=(it_doubled,), kron=(kron,), ikron=(ikron,),
               **{f"conv_f{l}": (conv_fwd[l],) for l in range(2)}, **{f"conv_b{l}": (conv_bwd[l],) for l in range(2)},
               **{f"bias{l}": (bias_wide[l],) for l in range(2)})
    outs = dict(bound=bound_shape, stat=(jax.ShapeDtypeStruct((2 * per_core,) + stat_shape.shape, F32),),
                cg=(jax.ShapeDtypeStruct((2 * per_core,) + cg_shape.shape, F32),),
                bg=(jax.ShapeDtypeStruct((2 * per_core,) + bg_shape.shape, F32),),
                **{f"{name}{j}": field_shape for name in ("a1_", "dg0_", "gz1_", "ga1_", "gz0_") for j in streams},
                **{f"shared{i}": jax.ShapeDtypeStruct((members,) + f_shape.shape, F32) for i in range(len(names))})
    scratch = dict(
        fields=pltpu.VMEM((7,) + field_shape.shape, F32), full=pltpu.VMEM(both + full_dims, F32),
        part=pltpu.VMEM(both + part_dims, F32),
        come=pltpu.VMEM(both + (2, chunks, row_devices - 1) + part_dims[2:], F32),
        keep=pltpu.VMEM(both + f_shape.shape, F32), y_give=pltpu.VMEM(both + y_shape.shape[1:], F32),
        p_buf=pltpu.VMEM(full_dims, F32), spread=spread, eo=energy, eb=energy,
        rid=pltpu.VMEM((2, rows_dev, width), jnp.int32),
        wbuf=pltpu.VMEM((6, count, channels, lanes), F32), macc=pltpu.VMEM((kx_half, 2 * sections, channels, lanes), F32),
        msrc=pltpu.VMEM((2 * sections, channels, lanes), F32),
        field_sem=dma((7,)), rid_sem=dma(both), out_sem=dma((2, 2, chunks)), wsem=dma((6,)), first_sem=dma((3,)),
        send=dma(both + (2, chunks, row_devices)), recv=dma(both + (2, chunks, row_devices)),
        red_send=dma(both + (2, chunks, row_devices)), red_recv=dma(both + (2, chunks, row_devices)),
        y_cross=dma((2, 2, chunks)), p_local=dma((chunks,)), p_cross=dma((2, 2, chunks)),
        b_local=dma((2, chunks)), b_cross=dma((2, 2, chunks)),
        s_local=dma(both), s_send=dma((2, members)), s_recv=dma((len(names), members)))
    gathered = {"f00": lax.all_gather(start.f_out, "batch", axis=0)}
    done = run(functools.partial(stages_kernel, per_core, kinds, places, mixes), 1, ins, outs, scratch, cost=400)
    gathered.update({name: getattr(done, f"shared{i}") for i, name in enumerate(names)})
    bound, calls = done.bound, 1

    grids = per_core * members * sections
    block = G
    blocks = channels // 2 // block
    in_buf = pltpu.VMEM((2, per_core, members, chunks, sections, count, lanes), F32)
    big, small = pltpu.VMEM((grids, channels, lanes), F32), pltpu.VMEM((grids, channels // 2, lanes), F32)
    grad_scratch = dict(fbuf=in_buf, gbuf=in_buf, in_sem=dma((2, 2)), f1=big, fs=small, d1=big, ds=big)
    row_dims = (2, channels // 2, channels, lanes)
    far_grad = run(functools.partial(far_grad_kernel, per_core), 1 + calls, gathered,
                   dict(far=jax.ShapeDtypeStruct((kx_half,) + row_dims, F32)),
                   dict(out=pltpu.VMEM((2, 2, block, channels, lanes), F32), send=dma((kx_half * blocks,)),
                        recv=dma((kx_half * blocks,)), **grad_scratch)).far
    bound_rows = bound.reshape(micro_count * rows_dev, channels, width)
    bound_block = pl.BlockSpec((bound_rows.shape[0] // (kx_half * blocks), channels, width),
                               lambda x, i, m: (x * blocks + i, 0, 0))
    grid_spec = pltpu.PrefetchScalarGridSpec(
        num_scalar_prefetch=1, grid=(kx_half, blocks),
        in_specs=[hbm] * len(gathered)
        + [pl.BlockSpec((None, 2, block, channels, lanes), lambda x, i, m: (x, 0, i, 0, 0)), bound_block],
        out_specs=[pl.BlockSpec((2, None, 2, block, channels, lanes), lambda x, i, m: (0, x, 0, i, 0, 0)), bound_block],
        scratch_shapes=list(grad_scratch.values()))
    spectral_grad, boundary = pl.pallas_call(
        functools.partial(own_grad_kernel, [*gathered, "far", "bound_in", "out", "bound_out", *grad_scratch], per_core),
        grid_spec=grid_spec, out_shape=[jax.ShapeDtypeStruct((2, kx_half) + row_dims, F32),
                                        jax.ShapeDtypeStruct(bound_rows.shape, F32)],
        cost_estimate=pl.CostEstimate(flops=0, bytes_accessed=150_000_000, transcendentals=0),
        compiler_params=params())(
            jnp.reshape(section, (1,)).astype(jnp.int32), *gathered.values(), far_grad, bound_rows)
    spectral_grad = spectral_grad.reshape(spectral_w.shape)
    boundary = boundary.reshape((1, micro_count, 1) + inputs.shape[2:])

    def lower(value):
        return (value[:channels, :channels] + value[channels:, channels:]
                + value[:channels, channels:] + value[channels:, :channels])

    pair = lambda value: jnp.sum(value.reshape((2, per_core) + value.shape[1:]), 1)
    conv_local = jnp.stack([lower(value) for value in pair(done.cg)[::-1]])
    bias_local = jnp.sum(pair(done.bg)[::-1], -1)
    stat_local = jnp.sum(pair(done.stat), -1)
    shapes = [v.shape for v in (conv_local, bias_local, stat_local)]
    flat_sums = jnp.concatenate([v.reshape(-1) for v in (conv_local, bias_local, stat_local)])
    length = flat_sums.shape[0]
    flat_sums = jnp.pad(flat_sums, (0, -length % 1024)).reshape(-1, 128)
    flat_sums = jnp.sum(lax.all_gather(flat_sums, ("section", "batch", "rows"), axis=0), 0).reshape(-1)
    ends = np.cumsum([0] + [math.prod(shape) for shape in shapes])
    conv_sum, bias_sum, stat_sum = [flat_sums[ends[i]:ends[i + 1]].reshape(shapes[i]) for i in range(3)]
    own_stat = lax.dynamic_index_in_dim(stat_sum, section, 0, False)
    layer_rms = jnp.sqrt(own_stat[:2] / (channels * own_stat[2])[None, :] + 1e-06)[None]
    own = lambda value: lax.dynamic_slice_in_dim(value, section, 1, 0)
    return boundary, spectral_grad, own(conv_sum), own(bias_sum), layer_rms


def solution(mesh):
    placed = (
        P(None, "batch", "rows", None, None),
        P(None, "batch", "rows", None, None),
        P(None, "batch", "rows", None),
        P("section", "rows", None, None, None),
        P("section", None, None),
        P("section", None),
    )
    return jax.shard_map(
        local,
        mesh=mesh,
        in_specs=placed,
        out_specs=(
            P("section", None, "batch", "rows", None, None),
            P("section", "rows", None, None, None),
            P("section", None, None),
            P("section", None),
            P("section", None, None),
        ),
        check_vma=False,
    )
```

```python
import functools
import math
import types

import jax
import jax.numpy as jnp
import numpy as np
from jax import lax
from jax.experimental import pallas as pl
from jax.experimental.pallas import tpu as pltpu
from jax.sharding import PartitionSpec as P

R = 8
G = 8
AHEAD = 2
F32 = jnp.float32
BF16 = jnp.bfloat16
VMEM_LIMIT = 62 * 1024 * 1024
MESH = pl.DeviceIdType.MESH


def split(value):
    high = value.astype(BF16)
    return high, (value - high.astype(F32)).astype(BF16)


def dot(left, right, dims=(((1,), (0,)), ((), ()))):
    return lax.dot_general(left, right, dims, preferred_element_type=F32)


def dot3(left, right):
    return dot(left[0], right[0]) + (dot(left[1], right[0]) + dot(left[0], right[1]))


def np_split(value):
    high = value.astype(np.float32).astype(BF16)
    return high, (value - high.astype(np.float64)).astype(np.float32).astype(BF16)


def col_tables(width, half):
    phase = 2.0 * math.pi / width * (np.outer(np.arange(width), np.arange(half)) % width)
    cosine, sine = np.cos(phase) / math.sqrt(width), np.sin(phase) / math.sqrt(width)
    plain = np.concatenate([cosine, -sine, -sine, -cosine], 1)
    doubled = plain * np.tile(np.where(np.arange(half) == 0, 1.0, 2.0), 4)[None, :]
    return plain, doubled


def row_tables(height, mode_rows, first_row, rows_dev):
    position = jnp.arange(mode_rows, dtype=jnp.int32)
    frequency = jnp.where(position < mode_rows // 2, position, height - mode_rows + position)
    row = first_row + jnp.arange(rows_dev, dtype=jnp.int32)
    phase = 2.0 * math.pi / height * (frequency[:, None] * row[None, :] % height).astype(F32)
    small = jnp.concatenate([jnp.cos(phase), jnp.sin(phase)], 1) / math.sqrt(height)
    rounded = lax.reduce_precision(small, 8, 7)
    high, low = rounded.astype(BF16), (small - rounded).astype(BF16)
    forward = jnp.concatenate([jnp.concatenate([high, high], 1), jnp.concatenate([low, jnp.zeros_like(low)], 1)], 0)
    inverse = jnp.concatenate([high.T, high.T, low.T], 1)
    return forward, inverse


def to_modes(value, table, kron, spread, p_ref):
    mode_rows, count, lanes = p_ref.shape
    rows = value.shape[0] // count
    high, low = split(value)
    spectra = dot(jnp.concatenate([high, low, high], 1), table)
    for i in range(2):
        spread[i] = spectra[:, i * lanes:(i + 1) * lanes]
    out = p_ref.reshape(mode_rows * count, lanes)
    for first in range(0, count, 2):
        sides = []
        for c in (first, first + 1):
            pick = pl.ds(c, rows, stride=count)
            sides.append(jnp.concatenate([spread[i, pick, :] for i in range(2)], 0))
        high, low = split(jnp.concatenate(sides, 1))
        both = dot(kron, jnp.concatenate([high, low], 0))
        result = both[:mode_rows] + both[mode_rows:]
        for i in range(2):
            out[pl.ds(first + i, mode_rows, stride=count), :] = result[:, i * lanes:(i + 1) * lanes]


def from_modes(y_ref, table, kron, spread):
    mode_rows, count, lanes = y_ref.shape
    rows, pieces = spread.shape[1] // count, spread.shape[0]
    modes = y_ref.reshape(mode_rows * count, lanes)
    sides = []
    for first in range(0, count, 2):
        pair = [modes[pl.ds(c, mode_rows, stride=count), :] for c in (first, first + 1)]
        high, low = split(jnp.concatenate(pair, 1))
        both = dot(kron, jnp.concatenate([high, low, high], 0))
        for i in range(2):
            side = both[:, i * lanes:(i + 1) * lanes]
            sides.append(jnp.concatenate([side[:rows], side[rows:]], 1))
    high, low = split(jnp.concatenate(sides, 0))
    out = dot(jnp.concatenate([high, low, high], 1), table)
    for c in range(count):
        for i in range(pieces):
            spread[i, pl.ds(c, rows, stride=count), :] = out[c * rows:(c + 1) * rows, i * 128:(i + 1) * 128]
    return jnp.concatenate([spread[i] for i in range(pieces)], 1)


def gelu_parts(z):
    size = jnp.abs(z)
    gauss = jnp.exp(-0.5 * z * z)
    base = 1.0 + (0.3275911 / math.sqrt(2.0)) * size
    t = pl.reciprocal(base, approx=True)
    t = t * (2.0 - base * t)
    poly = t * (0.254829592 + t * (-0.284496736 + t * (1.421413741 + t * (-1.453152027 + t * 1.061405429))))
    tail = 0.5 * poly * gauss
    phi = jnp.where(z >= 0, 1.0 - tail, tail)
    return z * phi, phi + z * (gauss * (1.0 / math.sqrt(2.0 * math.pi)))


def flat(ref):
    rows, count, width = ref.shape
    return ref[...].reshape(rows * count, width)


def put(ref, value):
    ref[...] = value.reshape(ref.shape)


def place_and_peers():
    section, z = lax.axis_index("section"), lax.axis_index("rows")
    return section, z, lax.axis_size("rows")


def greet(section, z, n, lines, members=0):
    barrier = pltpu.get_barrier_semaphore()
    pl.semaphore_signal(barrier, inc=1, device_id={"section": 1 - section}, device_id_type=MESH)
    if not lines:
        pl.semaphore_wait(barrier, 1)
        return

    @pl.when(z > 0)
    def _():
        pl.semaphore_signal(barrier, inc=1, device_id={"rows": z - 1}, device_id_type=MESH)

    @pl.when(z < n - 1)
    def _():
        pl.semaphore_signal(barrier, inc=1, device_id={"rows": z + 1}, device_id_type=MESH)

    for away in range(1, members):
        pl.semaphore_signal(barrier, inc=1, device_id={"batch": lax.rem(lax.axis_index("batch") + away, members)},
                            device_id_type=MESH)

    others = 1 + max(members - 1, 0)
    pl.semaphore_wait(barrier, others + (z > 0).astype(jnp.int32) + (z < n - 1).astype(jnp.int32))


def to_core(src, dst, sems, section):
    return pltpu.make_async_remote_copy(src_ref=src, dst_ref=dst, send_sem=sems[0], recv_sem=sems[1],
                                        device_id={"section": 1 - section}, device_id_type=MESH)


def guard(condition, body):
    if isinstance(condition, (bool, np.bool_)):
        if condition:
            body()
    else:
        pl.when(condition)(body)


class Line:
    def __init__(self, section, z, n, chunks, send, recv):
        self.section, self.z, self.n, self.chunks = section, z, n, chunks
        self.send, self.recv = send, recv

    def move(self, way, q, hop, src, dst):
        return pltpu.make_async_remote_copy(
            src_ref=src, dst_ref=dst, send_sem=self.send.at[way, q, hop], recv_sem=self.recv.at[way, q, hop],
            device_id={"rows": self.z + 1 if way == 0 else self.z - 1}, device_id_type=MESH)

    def sends(self, way):
        return self.z < self.n - 1 if way == 0 else self.z > 0

    def hears(self, way):
        return self.z > 0 if way == 0 else self.z < self.n - 1


def within(value, count):
    return jnp.logical_and(value >= 0, value < count)


class Gather(Line):
    def __init__(self, section, z, n, r, parity):
        super().__init__(section, z, n, r.full.shape[1], r.send.at[parity], r.recv.at[parity])
        self.full, self.give_from = r.full.at[parity], r.y_give.at[parity]
        self.cross = r.y_cross.at[parity]

    def swap(self, q):
        return to_core(self.give_from.at[q], self.full.at[q, self.z, self.section],
                       (self.cross.at[0, q], self.cross.at[1, q]), self.section)

    def give(self, q):
        self.swap(q).start()

    def hop(self, way, q, hop):
        piece = self.full.at[q, self.source(way, hop)]
        return self.move(way, q, hop, piece, piece)

    def source(self, way, hop):
        return self.z - hop if way == 0 else self.z + hop

    def known(self, way, hop):
        at = self.source(way, hop)
        return at >= 0 if way == 0 else at < self.n

    def own(self, q):
        self.swap(q).wait_recv()
        for way in range(2):
            @pl.when(self.sends(way))
            def _():
                self.hop(way, q, 0).start()

    def step(self, q, hop):
        for way in range(2):
            @pl.when(self.known(way, hop + 1))
            def _():
                piece = self.full.at[q, self.source(way, hop + 1)]
                self.move(way, q, hop, piece, piece).wait_recv()

                @pl.when(self.sends(way))
                def _():
                    self.hop(way, q, hop + 1).start()

    def begin(self):
        for q in range(min(AHEAD, self.chunks)):
            self.own(q)

    def tick(self, t):
        @pl.when(t + AHEAD < self.chunks)
        def _():
            self.own(t + AHEAD)

        for hop in range(self.n - 1):
            q = t - hop - 1
            pl.when(within(q, self.chunks))(functools.partial(self.step, q, hop))

    def finish(self):
        def body(q, carry):
            self.swap(q).wait_send()
            for way in range(2):
                for hop in range(self.n - 1):
                    @pl.when(jnp.logical_and(self.sends(way), self.known(way, hop)))
                    def _():
                        self.hop(way, q, hop).wait_send()
            return carry

        lax.fori_loop(0, self.chunks, body, 0)


class Sum(Line):
    def __init__(self, section, z, n, r, parity, admit):
        super().__init__(section, z, n, r.part.shape[2], r.red_send.at[parity], r.red_recv.at[parity])
        self.part, self.come, self.keep, self.admit = r.part.at[parity], r.come.at[parity], r.keep.at[parity], admit

    def owner(self, way, hop):
        return self.z + self.n - hop if way == 0 else self.z - self.n + hop

    def valid(self, way, hop):
        return self.z <= hop - 1 if way == 0 else self.z >= self.n - hop

    def sent(self, way, q, hop):
        return self.move(way, q, hop, self.part.at[self.owner(way, hop), q], self.come.at[way, q, hop - 1])

    def heard(self, way, q, hop):
        come = self.come.at[way, q, hop - 1]
        self.move(way, q, hop, come, come).wait_recv()

    def first(self, q):
        self.admit(q)
        for way in range(2):
            @pl.when(jnp.logical_not(self.hears(way)))
            def _():
                for hop in range(1, self.n):
                    @pl.when(self.valid(way, hop))
                    def _():
                        self.sent(way, q, hop).start()

    def step(self, q, hop):
        for way in range(2):
            @pl.when(jnp.logical_and(self.valid(way, hop), self.hears(way)))
            def _():
                self.heard(way, q, hop - 1)
                owner = self.owner(way, hop)
                self.part[owner, q] = self.part[owner, q] + self.come[way, q, hop - 2]
                self.sent(way, q, hop).start()

    def final(self, q):
        for way in range(2):
            @pl.when(self.hears(way))
            def _():
                self.heard(way, q, self.n - 1)
                self.part[self.z, q] = self.part[self.z, q] + self.come[way, q, self.n - 2]

        self.keep[q] = self.part[self.z, q]

    def tick(self, t):
        pl.when(within(t, self.chunks))(functools.partial(self.first, t))
        for hop in range(2, self.n + 1):
            q = t - hop + 1
            pl.when(within(q, self.chunks))(
                functools.partial(self.step, q, hop) if hop < self.n else functools.partial(self.final, q))

    def finish(self):
        def body(q, carry):
            for way in range(2):
                for hop in range(1, self.n):
                    @pl.when(self.valid(way, hop))
                    def _():
                        self.sent(way, q, hop).wait_send()
            return carry

        lax.fori_loop(0, self.chunks, body, 0)


class Reduce(Line):
    def __init__(self, section, z, n, part, come, f_out, f_sem, send, recv, ahead):
        super().__init__(section, z, n, part.shape[1], send, recv)
        self.ahead = ahead
        self.part, self.come, self.f_out, self.f_sem = part, come, f_out, f_sem

    def owner(self, way, hop):
        return self.z + self.n - hop if way == 0 else self.z - self.n + hop

    def valid(self, way, hop):
        return self.z <= hop - 1 if way == 0 else self.z >= self.n - hop

    def sent(self, way, q, hop):
        return self.move(way, q, hop, self.part.at[self.owner(way, hop), q], self.come.at[way, q, hop])

    def heard(self, way, q, hop):
        come = self.come.at[way, q, hop]
        self.move(way, q, hop, come, come).wait_recv()

    def first(self, t):
        for hop in range(1, self.n):
            q = t - hop + 1

            def send():
                for way in range(2):
                    @pl.when(jnp.logical_and(self.valid(way, hop), jnp.logical_not(self.hears(way))))
                    def _():
                        self.sent(way, q, hop).start()

            guard(0 <= q < self.chunks if isinstance(q, int) else q < self.chunks, send)

    def step(self, q, hop):
        for way in range(2):
            @pl.when(jnp.logical_and(self.valid(way, hop), self.hears(way)))
            def _():
                self.heard(way, q, hop - 1)
                owner = self.owner(way, hop)
                self.part[owner, q] = self.part[owner, q] + self.come[way, q, hop - 1]
                self.sent(way, q, hop).start()

    def result(self, q):
        return pltpu.make_async_copy(self.part.at[self.z, q], self.f_out.at[q], self.f_sem.at[q])

    def final(self, q):
        for way in range(2):
            @pl.when(self.hears(way))
            def _():
                self.heard(way, q, self.n - 1)
                self.part[self.z, q] = self.part[self.z, q] + self.come[way, q, self.n - 1]

        self.result(q).start()

    def tick(self, t):
        if isinstance(t, int) and t == 0:
            for early in range(self.ahead):
                self.first(early)
        self.first(t + self.ahead)
        for hop in range(2, self.n + 1):
            q = t - hop + 1
            if isinstance(q, int):
                valid = 0 <= q < self.chunks
            else:
                valid = q < self.chunks
            guard(valid, functools.partial(self.step, q, hop) if hop < self.n else functools.partial(self.final, q))

    def finish(self):
        def body(q, carry):
            self.result(q).wait()
            for way in range(2):
                for hop in range(1, self.n):
                    @pl.when(self.valid(way, hop))
                    def _():
                        self.sent(way, q, hop).wait_send()
            return carry

        lax.fori_loop(0, self.chunks, body, 0)


def fetch(src, dst, sem, parts=4):
    step = dst.shape[0] // parts
    for i in range(parts):
        pltpu.make_async_copy(src.at[pl.ds(i * step, step)], dst.at[pl.ds(i * step, step)], sem).start()


def arrived(dst, sem):
    pltpu.make_async_copy(dst, dst, sem).wait()


def portions(total, count):
    return [(i * total // count, (i + 1) * total // count) for i in range(count)]


def conv_rows(weight, bias, a, out, first, last):
    channels, width = a.shape[1:]
    block = weight.shape[0] // channels

    def body(i, carry):
        at = pl.ds(i * block, block)
        high, low = split(a[at].reshape(block * channels, width))
        result = dot(weight[...], jnp.concatenate([high, high, low], 0)).reshape(block, channels, width)
        out[at] = result + bias[...][None] if bias is not None else out[at] + result
        return carry

    lax.fori_loop(first, last, body, 0)


def grad_rows(a, gz, cg_ref, bg_ref, first, last):
    channels, width = a.shape[1:]

    def body(r, carry):
        grad, bias = carry
        g = gz[r]
        left = jnp.concatenate(split(a[r]), 0)
        right = jnp.concatenate(split(g), 0)
        return grad + dot(left, right, (((1,), (1,)), ((), ()))), bias + g

    grad, bias = lax.fori_loop(first, last, body, (cg_ref[...], bg_ref[...]))
    cg_ref[...] = grad
    bg_ref[...] = bias


def chunk_of(ref, q, count):
    rows, _, width = ref.shape
    return ref[:, pl.ds(pl.multiple_of(q * count, count), count), :].reshape(rows * count, width)


def chunk_at(ref, q, count):
    return ref.at[:, pl.ds(pl.multiple_of(q * count, count), count), :]


class Modes:
    def __init__(self, section, buffer, p_out, local, cross):
        self.section, self.buffer, self.p_out, self.local, self.cross = section, buffer, p_out, local, cross

    def view(self, q):
        n, halves, kx, count, lanes = self.buffer.shape[1:]
        return self.buffer.at[q].reshape(n * halves * kx, count, lanes)

    def copies(self, q):
        s = self.section
        return (pltpu.make_async_copy(self.buffer.at[q, :, s], self.p_out.at[:, q, 0], self.local.at[q]),
                to_core(self.buffer.at[q, :, 1 - s], self.p_out.at[:, q, 1],
                        (self.cross.at[0, q], self.cross.at[1, q]), s))

    def start(self, q):
        for copy in self.copies(q):
            copy.start()

    def wait(self, q):
        for copy in self.copies(q):
            copy.wait()


class Bound:
    def __init__(self, section, owner, micro, other, source, bound, local, cross):
        self.section, self.owner, self.micro, self.other = section, owner, micro, other
        self.source, self.bound, self.local, self.cross = source, bound, local, cross

    def copies(self, q, count, micro):
        src, dst = chunk_at(self.source, q, count), chunk_at(self.bound.at[micro], q, count)
        return (pltpu.make_async_copy(src, dst, self.local.at[q]),
                to_core(src, dst, (self.cross.at[0, q], self.cross.at[1, q]), self.section))

    def start(self, q, count):
        here, there = self.copies(q, count, self.micro)

        @pl.when(self.section == self.owner)
        def _():
            here.start()

        @pl.when(self.section != self.owner)
        def _():
            there.start()

    def wait(self, q, count):
        here, there = self.copies(q, count, self.micro)
        come = self.copies(q, count, self.other)[1]

        @pl.when(self.section == self.owner)
        def _():
            here.wait()
            come.wait_recv()

        @pl.when(self.section != self.owner)
        def _():
            there.wait_send()


def add_squares(value, total):
    rows, _, width = total.shape
    square = (value * value).reshape(rows, -1, width)
    for at in range(0, square.shape[1], G):
        total[...] += square[:, at:at + G]


def region_sums(rid_ref, eo, eb, stat_ref):
    rows, _, width = eo.shape
    rid = rid_ref[...]
    energies = (jnp.sum(eo[...], axis=1), jnp.sum(eb[...], axis=1), jnp.ones((rows, width), F32))
    for kind in range(3):
        for region in range(R):
            line = jnp.sum(jnp.where(rid == region + 1, energies[kind], 0.0), axis=0, keepdims=True)
            total = line[:, :128]
            for piece in range(1, width // 128):
                total = total + line[:, piece * 128:(piece + 1) * 128]
            stat_ref[kind, region:region + 1, :] = total


def start_kernel(per_core, r):
    section, z, n = place_and_peers()
    chunks, count, half = r.p_buf.shape[1], r.p_buf.shape[5], r.far.shape[0]
    blocks = [(j, q) for j in range(per_core) for q in range(chunks)]
    reduce = Reduce(section, z, n, r.part, r.come, r.f_out, r.f_sem, r.red_send, r.red_recv, 0)
    outs = [r.part] + [getattr(r, f"p{j}") for j in range(1, per_core)]
    modes = [Modes(section, r.p_buf.at[j], outs[j], r.p_local.at[j], r.p_cross.at[j]) for j in range(per_core)]

    def field(k):
        j, q = blocks[k]
        src = chunk_at(r.inputs.at[section * per_core + j, 0], q, count)
        return pltpu.make_async_copy(src, r.a_buf.at[k % 2], r.a_sem.at[k % 2])

    def weight_in(x):
        return pltpu.make_async_copy(r.weights.at[0, (1 - section) * half + x], r.w_buf.at[x % 2], r.w_sem.at[x % 2])

    def weight_out(x):
        return to_core(r.w_buf.at[x % 2], r.far.at[x], (r.w_cross.at[0, x], r.w_cross.at[1, x]), section)

    def lend(x):
        if x < half:
            weight_in(x).wait()
            weight_out(x).start()
        if 1 <= x <= half:
            weight_out(x - 1).wait_send()
            if x + 1 < half:
                weight_in(x + 1).start()

    field(0).start()
    for x in range(min(2, half)):
        weight_in(x).start()
    greet(section, z, n, True)
    for k, (j, q) in enumerate(blocks):
        if k + 1 < len(blocks):
            field(k + 1).start()
        field(k).wait()
        to_modes(flat(r.a_buf.at[k % 2]), r.table[...], r.kron[...], r.spread, modes[j].view(q))
        modes[j].start(q)
        lend(k)
        if k >= 1:
            if k <= chunks:
                modes[0].wait(k - 1)
            reduce.tick(k - 1)
    for k in range(len(blocks), half + 1):
        lend(k)
    for t in range(len(blocks) - 1, chunks + n - 1):
        reduce.tick(t)
    for x in range(half):
        weight_out(x).wait_recv()
    for j, q in blocks[chunks:]:
        modes[j].wait(q)
    reduce.finish()


class Share:
    def __init__(self, r, index, parity):
        self.r, self.index, self.parity = r, index, parity
        self.me, self.members = lax.axis_index("batch"), lax.axis_size("batch")

    def copies(self):
        source, target = self.r.keep.at[self.parity], getattr(self.r, f"shared{self.index}").at[self.me]
        yield pltpu.make_async_copy(source, target, self.r.s_local.at[self.parity])
        for away in range(1, self.members):
            yield pltpu.make_async_remote_copy(
                src_ref=source, dst_ref=target, send_sem=self.r.s_send.at[self.parity, away],
                recv_sem=self.r.s_recv.at[self.index, away],
                device_id={"batch": lax.rem(self.me + away, self.members)}, device_id_type=MESH)

    def start(self):
        for copy in self.copies():
            copy.start()

    def wait_send(self):
        for i, copy in enumerate(self.copies()):
            if i == 0:
                copy.wait()
            else:
                copy.wait_send()

    def wait_recv(self):
        for i, copy in enumerate(self.copies()):
            if i > 0:
                copy.wait_recv()


class Stage:
    def __init__(self, k, kind, j, per_core, places, section, z, n, r):
        self.k, self.kind, self.j, self.r, self.section, self.n = k, kind, j, r, section, n
        self.parity = k % 2
        self.micro, self.other = section * per_core + j, (1 - section) * per_core + j
        self.forward, self.last = kind in ("middle", "turn"), kind == "tail"
        self.buffers = {name: r.fields.at[i] for name, i in places.items()}
        self.sems = {name: r.field_sem.at[i] for name, i in places.items()}
        self.gather = Gather(section, z, n, r, self.parity)
        self.count, self.lanes = r.full.shape[5], r.full.shape[6]
        self.chunks = r.full.shape[1]
        plain = lambda name: getattr(r, f"{name}{j}")
        if kind == "middle":
            self.loads = dict(a=r.inputs.at[self.micro, 0])
            self.saves = dict(a=plain("a1_"), z=plain("dg0_"))
        elif kind == "turn":
            self.loads = dict(a=plain("a1_"), cot=r.cotangent.at[self.micro, 0])
            self.saves = dict(cot=plain("gz1_"))
        elif kind == "back":
            self.loads = dict(gz=plain("gz1_"), h=r.cotangent.at[self.micro, 0], a=plain("a1_"), dg=plain("dg0_"))
            self.saves = dict(h=plain("ga1_"), dg=plain("gz0_"))
        else:
            self.loads = dict(gz=plain("gz0_"), h=plain("ga1_"), a=r.inputs.at[self.micro, 0])
            self.saves = {}
        layer = 0 if kind in ("middle", "tail") else 1
        self.weight = getattr(r, f"conv_{'f' if self.forward else 'b'}{layer}")
        self.bias = getattr(r, f"bias{layer}")
        self.table = r.t_plain if kind == "middle" else r.t_doubled
        self.itable = r.it_doubled if self.forward else r.it_plain
        if not self.last:
            self.modes = Modes(section, r.p_buf, r.part.at[self.parity], r.p_local, r.p_cross.at[self.parity])
        if kind in ("turn", "tail"):
            self.bound = Bound(section, 1 if kind == "turn" else 0, self.micro, self.other,
                               self.buffers["a" if kind == "turn" else "h"], r.bound,
                               r.b_local.at[self.parity], r.b_cross.at[self.parity])

    def prefetch(self):
        for name, src in self.loads.items():
            fetch(src, self.buffers[name], self.sems[name])
        if self.forward:
            self.rid_copy().start()

    def rid_copy(self):
        return pltpu.make_async_copy(self.r.region.at[self.micro, 0], self.r.rid.at[self.parity],
                                     self.r.rid_sem.at[self.parity])

    def got(self, name):
        arrived(self.buffers[name], self.sems[name])

    def open(self):
        r, b = self.r, self.buffers
        if self.forward:
            r.eo[...] = jnp.zeros_like(r.eo)
            r.eb[...] = jnp.zeros_like(r.eb)
            self.got("a")
        else:
            for name in ("gz", "h", "a"):
                self.got(name)
            at = self.k - self.r.first_back
            r.cg[at] = jnp.zeros_like(r.cg[at])
            r.bg[at] = jnp.zeros_like(r.bg[at])

    def before(self, i):
        r, b = self.r, self.buffers
        a = b["a"]
        rows, channels = a.shape[:2]
        blocks, parts = rows // (self.weight.shape[0] // channels), self.n - 1
        span = (i * blocks // parts, (i + 1) * blocks // parts)
        if self.forward:
            conv_rows(self.weight, self.bias, a, b["z"], *span)
        else:
            conv_rows(self.weight, None, b["gz"], b["h"], *span)
            at = self.k - r.first_back
            grad_rows(a, b["gz"], r.cg.at[at], r.bg.at[at], i * rows // parts, (i + 1) * rows // parts)

    def outs(self, q):
        return [pltpu.make_async_copy(chunk_at(self.buffers[name], q, self.count), chunk_at(dst, q, self.count),
                                      self.r.out_sem.at[self.parity, i, q])
                for i, (name, dst) in enumerate(self.saves.items())]

    def late(self):
        for name in ("cot", "dg"):
            if name in self.loads:
                self.got(name)

    def chunk(self, q):
        r, b, count = self.r, self.buffers, self.count
        spectral = from_modes(self.gather.full.at[q].reshape(-1, count, self.lanes), self.itable[...], r.ikron[...],
                              r.spread)
        if self.forward:
            branch, slope = gelu_parts(spectral + chunk_of(b["z"], q, count))
            if self.kind == "turn":
                put(chunk_at(b["cot"], q, count), chunk_of(b["cot"], q, count) * slope)
            else:
                put(chunk_at(b["z"], q, count), slope)
            add_squares(branch, r.eb)
            out = chunk_of(b["a"], q, count) + branch
            put(chunk_at(b["a"], q, count), out)
            add_squares(out, r.eo)
            source = b["cot" if self.kind == "turn" else "a"]
        else:
            ga = spectral + chunk_of(b["h"], q, count)
            put(chunk_at(b["h"], q, count), ga)
            if not self.last:
                put(chunk_at(b["dg"], q, count), ga * chunk_of(b["dg"], q, count))
                source = b["dg"]
        for copy in self.outs(q):
            copy.start()
        if self.kind in ("turn", "tail"):
            self.bound.start(q, count)
        if not self.last:
            to_modes(chunk_of(source, q, count), self.table[...], r.kron[...], r.spread, self.modes.view(q))

            pl.when(q == self.chunks - 1)(self.gather.finish)
            self.modes.start(q)

    def end(self):
        if self.forward:
            self.rid_copy().wait()
            region_sums(self.r.rid.at[self.parity], self.r.eo, self.r.eb, self.r.stat.at[self.k])
        if self.last:
            self.gather.finish()

    def close(self):
        def body(q, carry):
            for copy in self.outs(q):
                copy.wait()
            if self.kind in ("turn", "tail"):
                self.bound.wait(q, self.count)
            return carry

        lax.fori_loop(0, self.chunks, body, 0)


def stages_kernel(per_core, kinds, places, mixes, r):
    section, z, n = place_and_peers()
    chunks = r.full.shape[1]
    r.first_back = 2 * per_core
    stages = [Stage(k, kind, j, per_core, places[k], section, z, n, r)
              for k, (kind, j) in enumerate((kind, j) for kind in kinds for j in range(per_core))]
    ticks = chunks + n - 1
    stages[0].prefetch()
    first = [pltpu.make_async_copy(r.p_in, r.part.at[1], r.first_sem.at[0]),
             pltpu.make_async_copy(r.y_in.at[0], r.full.at[0, :, z, section], r.first_sem.at[1]),
             pltpu.make_async_copy(r.y_in.at[1], r.y_give.at[0], r.first_sem.at[2]),
             pltpu.make_async_copy(r.f_in, r.keep.at[0], r.first_sem.at[3])]
    for copy in first:
        copy.start()
    greet(section, z, n, True, lax.axis_size("batch"))
    for copy in first:
        copy.wait()
    for q in range(chunks):
        stages[0].gather.give(q)
    shares = [Share(r, 0, 0)]
    shares[0].start()
    sums = Sum(section, z, n, r, 1, lambda q: None)
    for k, stage in enumerate(stages):
        gather = stage.gather
        now = None if stage.last else Sum(section, z, n, r, stage.parity, stage.modes.wait)
        mix = None
        if sums is not None:
            mix = Mix(section, z, *mixes[(k + 1) // per_core], sums, stages[k + 1].gather, r)
            share = Share(r, k + 1, 1 - stage.parity)
            if k >= 1:
                shares[k - 1].wait_send()
            shares.append(share)
            mix.prime()
        lead = 0 if k == 0 else chunks - 1
        ready = n - 1 - lead
        gather.begin()
        stage.open()

        def early(i, carry):
            if sums is not None:
                sums.tick(i + lead)
            gather.tick(i)
            stage.before(i)
            if mix is not None and not mix.flip:
                pl.when(within(i - ready, chunks))(lambda: mix.chunk(i - ready))
            return carry

        lax.fori_loop(0, n - 1, early, 0)
        if k > 0:
            stages[k - 1].close()
        if k + 1 < len(stages):
            stages[k + 1].prefetch()
        stage.late()

        def later(q, carry):
            i = q + n - 1
            if sums is not None:
                sums.tick(i + lead)
            if now is not None:
                now.tick(i - n)
            gather.tick(i)
            stage.chunk(q)
            if mix is not None:
                if mix.flip:
                    pl.when(q == 0)(sums.finish)
                    mix.chunk(q)
                else:
                    pl.when(within(i - ready, chunks))(lambda: mix.chunk(i - ready))
            return carry

        lax.fori_loop(0, chunks, later, 0)
        if mix is not None:
            if not mix.flip:
                sums.finish()
            mix.finish()
            share.start()
        stage.end()
        sums = now
    stages[-1].close()
    for share in shares[-2:]:
        share.wait_send()
    for share in shares:
        share.wait_recv()


def swap_halves(value):
    return pltpu.roll(value, value.shape[-1] // 2, value.ndim - 1)


def left_lanes(shape):
    return lax.broadcasted_iota(jnp.int32, shape, len(shape) - 1) < shape[-1] // 2


SLOTS = 4


def weight_stream(own, base, local_ref, far_ref, wbuf, sem):
    step, count = pl.program_id(0), pl.num_programs(0)

    def begin(at):
        slot = lax.rem(at, SLOTS)

        @pl.when(own)
        def _():
            fetch(local_ref.at[0, base + at], wbuf.at[slot], sem.at[slot])

        @pl.when(jnp.logical_not(own))
        def _():
            fetch(far_ref.at[at], wbuf.at[slot], sem.at[slot])

    @pl.when(step == 0)
    def _():
        for at in range(SLOTS - 1):
            @pl.when(at < count)
            def _():
                begin(at)

    @pl.when(step + SLOTS - 1 < count)
    def _():
        begin(step + SLOTS - 1)

    slot = lax.rem(step, SLOTS)
    arrived(wbuf.at[slot], sem.at[slot])
    return wbuf.at[slot]


def pieces(array):
    return [array[at:at + G] for at in range(0, array.shape[0], G)]


def spread_row(ref, row):
    return ref[pl.ds(row, G, stride=0), :]


def mix_kernel(m_ref, f_ref, local_ref, far_ref, y_ref, wbuf, f1, f2, sem):
    weight = weight_stream(m_ref[0] == 1, m_ref[1], local_ref, far_ref, wbuf, sem)
    grids, channels, lanes = f1.shape
    for g in range(grids):
        f1[g] = f_ref[:, g].reshape(channels, lanes)
    f2[...] = swap_halves(f1[...])
    groups = channels // G

    def body(block, acc):
        at = pl.multiple_of(block * G, G)
        acc = list(acc)
        for u in range(G):
            rows = [spread_row(f.at[g], at + u) for g in range(grids) for f in (f1, f2)]
            for o in range(groups):
                w = weight[at + u, o * G:(o + 1) * G, :]
                for k, row in enumerate(rows):
                    acc[k * groups + o] = acc[k * groups + o] + row * w
        return tuple(acc)

    acc = lax.fori_loop(0, groups, body, tuple(jnp.zeros((G, lanes), F32) for _ in range(2 * grids * groups)))
    left = left_lanes((channels, lanes))
    for g in range(grids):
        a, b = [jnp.concatenate(acc[k * groups:(k + 1) * groups], 0) for k in (2 * g, 2 * g + 1)]
        y_ref[g] = jnp.where(left, a - swap_halves(a), b + swap_halves(b)).reshape(y_ref.shape[1:])


def mix_t_kernel(m_ref, d_ref, local_ref, far_ref, y_ref, wbuf, a1, a2, sem):
    weight = weight_stream(m_ref[0] == 1, m_ref[1], local_ref, far_ref, wbuf, sem)
    grids, channels, lanes = a1.shape
    d = [d_ref[:, g].reshape(channels, lanes) for g in range(grids)]
    d1 = [pieces(d[g]) for g in range(grids)]
    d2 = [pieces(swap_halves(d[g])) for g in range(grids)]
    groups = channels // G

    def body(block, carry):
        at = pl.multiple_of(block * G, G)
        rows = [[] for _ in range(2 * grids)]
        for u in range(G):
            total = [None] * (2 * grids)
            for o in range(groups):
                w = weight[at + u, o * G:(o + 1) * G, :]
                for g in range(grids):
                    for side, source in enumerate((d1, d2)):
                        term = w * source[g][o]
                        k = 2 * g + side
                        total[k] = term if total[k] is None else total[k] + term
            for k in range(2 * grids):
                rows[k].append(jnp.sum(total[k], axis=0, keepdims=True))
        for g in range(grids):
            a1[g, pl.ds(at, G), :] = jnp.concatenate(rows[2 * g], 0)
            a2[g, pl.ds(at, G), :] = jnp.concatenate(rows[2 * g + 1], 0)
        return carry

    lax.fori_loop(0, groups, body, 0)
    left = left_lanes((channels, lanes))
    for g in range(grids):
        a, b = a1[g], a2[g]
        y_ref[g] = jnp.where(left, a + swap_halves(a), swap_halves(b) - b).reshape(y_ref.shape[1:])


class Mix:
    def __init__(self, section, z, layer, flip, sums, gather, r):
        self.section, self.z, self.layer, self.flip, self.r = section, z, layer, flip, r
        self.sums, self.gather = sums, gather
        self.chunks, self.grids, self.half, self.count, self.lanes = sums.part.shape[1:]
        self.channels, self.slots = r.weights.shape[2], r.wbuf.shape[0]
        self.blocks = self.chunks * self.half

    def begin(self, block):
        q, x = block // self.half, block % self.half
        slot = lax.rem(block, self.slots)
        rows = pl.ds(q * self.count, self.count)

        @pl.when(self.section == self.layer)
        def _():
            pltpu.make_async_copy(self.r.weights.at[0, self.section * self.half + x, rows], self.r.wbuf.at[slot],
                                  self.r.wsem.at[slot]).start()

        @pl.when(self.section != self.layer)
        def _():
            pltpu.make_async_copy(self.r.far.at[x, rows], self.r.wbuf.at[slot], self.r.wsem.at[slot]).start()

    def prime(self):
        for block in range(min(self.slots, self.blocks)):
            self.begin(jnp.int32(block))
        if not self.flip:
            self.r.macc[...] = jnp.zeros_like(self.r.macc)

    def chunk(self, q):
        def body(x, carry):
            block = q * self.half + x
            slot = lax.rem(block, self.slots)
            weight = self.r.wbuf.at[slot]
            arrived(weight, self.r.wsem.at[slot])
            (self.transposed if self.flip else self.forward)(q, x, weight)

            @pl.when(block + self.slots < self.blocks)
            def _():
                self.begin(block + self.slots)

            return carry

        lax.fori_loop(0, self.half, body, 0)
        if self.flip:
            self.gather.give(q)

    def forward(self, q, x, weight):
        sides, groups = 2 * self.grids, self.channels // G
        total, source = self.r.macc.at[x], self.r.msrc
        for g in range(self.grids):
            value = self.sums.part[self.z, q, g, x]
            source[2 * g, :self.count] = value
            source[2 * g + 1, :self.count] = swap_halves(value)
        keys = [(k, o) for k in range(sides) for o in range(groups)]

        def body(octet, acc):
            acc = dict(zip(keys, acc))
            for u in range(G):
                i = octet * G + u
                rows = [spread_row(source.at[k], i) for k in range(sides)]
                for o in range(groups):
                    w = weight[i, o * G:(o + 1) * G, :]
                    for k in range(sides):
                        acc[k, o] = acc[k, o] + rows[k] * w
            return tuple(acc[key] for key in keys)

        acc = lax.fori_loop(0, self.count // G, body, tuple(total[k, o * G:(o + 1) * G, :] for k, o in keys))
        for key, value in zip(keys, acc):
            total[key[0], key[1] * G:(key[1] + 1) * G, :] = value

    def transposed(self, q, x, weight):
        sides, groups = 2 * self.grids, self.channels // G
        source = self.r.msrc
        for g in range(self.grids):
            value = jnp.concatenate([self.sums.part[self.z, at, g, x] for at in range(self.chunks)], 0)
            source[2 * g] = value
            source[2 * g + 1] = swap_halves(value)
        rows = [pieces(source[k]) for k in range(sides)]
        out = [[] for _ in range(sides)]
        for i in range(self.count):
            total = [None] * sides
            for o in range(groups):
                w = weight[i, o * G:(o + 1) * G, :]
                for k in range(sides):
                    term = w * rows[k][o]
                    total[k] = term if total[k] is None else total[k] + term
            for k in range(sides):
                out[k].append(jnp.sum(total[k], axis=0, keepdims=True))
        left = left_lanes((self.count, self.lanes))
        for g in range(self.grids):
            a, b = [jnp.concatenate(out[2 * g + side], 0) for side in range(2)]
            self.put(g, q, x, jnp.where(left, a + swap_halves(a), swap_halves(b) - b))

    def put(self, g, q, x, value):
        if g == 0:
            self.gather.full[q, self.z, self.section, x] = value
        else:
            self.gather.give_from[q, x] = value

    def finish(self):
        if self.flip:
            return
        left = left_lanes((self.channels, self.lanes))

        def body(x, carry):
            for g in range(self.grids):
                a, b = [self.r.macc[x, 2 * g + side] for side in range(2)]
                result = jnp.where(left, a - swap_halves(a), b + swap_halves(b))
                for q in range(self.chunks):
                    self.put(g, q, x, result[q * self.count:(q + 1) * self.count])
            return carry

        lax.fori_loop(0, self.half, body, 0)
        for q in range(self.chunks):
            self.gather.give(q)


def grad_tables(f_ref, d_ref, f1, fs, d1, ds):
    channels, lanes = f1.shape[1:]
    left = left_lanes((channels // 2, lanes))
    at = 0
    for stream in range(f_ref.shape[0]):
        for member in range(f_ref.shape[1]):
            for g in range(f_ref.shape[3]):
                f = f_ref[stream, member, :, g].reshape(channels, lanes)
                f1[at] = f
                less = f - swap_halves(f)
                fs[at] = jnp.where(left, less[:channels // 2], -less[channels // 2:])
                d = d_ref[stream, member, :, g].reshape(channels, lanes)
                d1[at] = d
                ds[at] = d + swap_halves(d)
                at += 1


def grad_block(first_row, f1, fs, d1, ds, out):
    count, channels, lanes = f1.shape
    groups, middle = channels // G, channels // 2
    left = left_lanes((G, lanes))

    def body(u, carry):
        rows = ((f1, first_row + u), (f1, middle + first_row + u), (fs, first_row + u))

        def grid(g, acc):
            factors = [spread_row(ref.at[g], row) for ref, row in rows]
            out = []
            for o in range(groups):
                d, e = d1[g, o * G:(o + 1) * G, :], ds[g, o * G:(o + 1) * G, :]
                out += [acc[3 * o] + factors[0] * d, acc[3 * o + 1] + factors[1] * d, acc[3 * o + 2] + factors[2] * e]
            return tuple(out)

        acc = lax.fori_loop(0, count, grid, (jnp.zeros((G, lanes), F32),) * (3 * groups), unroll=4)
        for o in range(groups):
            p = acc[3 * o + 2]
            for side in range(2):
                m = acc[3 * o + side]
                n = swap_halves(m)
                third = swap_halves(p) if side == 0 else p
                out[side, u, o * G:(o + 1) * G, :] = jnp.where(left, m + n, m - n + third)
        return carry

    lax.fori_loop(0, out.shape[1], body, 0)


class GradInput:
    def __init__(self, first, f, g, fbuf, gbuf, sem):
        self.first, self.f, self.g, self.fbuf, self.gbuf, self.sem = first, f, g, fbuf, gbuf, sem

    def load(self, x, slot):
        for layer, condition in enumerate((self.first, jnp.logical_not(self.first))):
            @pl.when(condition)
            def _():
                for j in range(len(self.f[layer])):
                    pltpu.make_async_copy(self.f[layer][j].at[:, :, :, x], self.fbuf.at[slot, j],
                                          self.sem.at[0, slot]).start()
                    pltpu.make_async_copy(self.g[layer][j].at[:, :, :, x], self.gbuf.at[slot, j],
                                          self.sem.at[1, slot]).start()

    def next(self, x, count):
        slot = lax.rem(x, 2)

        @pl.when(x + 1 < count)
        def _():
            self.load(x + 1, 1 - slot)

        arrived(self.fbuf.at[slot], self.sem.at[0, slot])
        arrived(self.gbuf.at[slot], self.sem.at[1, slot])
        return self.fbuf.at[slot], self.gbuf.at[slot]


def grad_input(r, first, per_core):
    f = [[getattr(r, f"f{layer}{j}") for j in range(per_core)] for layer in range(2)]
    g = [[getattr(r, f"g{layer}{j}") for j in range(per_core)] for layer in range(2)]
    return GradInput(first, f, g, r.fbuf, r.gbuf, r.in_sem)


def far_grad_kernel(per_core, r):
    section, z, n = place_and_peers()
    half = r.far.shape[0]
    block = r.out.shape[2]
    blocks = r.far.shape[2] // block
    source = grad_input(r, section != 0, per_core)

    def move(k, slot):
        x, i = k // blocks, k % blocks
        return to_core(r.out.at[slot], r.far.at[x, :, pl.ds(i * block, block)], (r.send.at[k], r.recv.at[k]), section)

    source.load(0, 0)
    greet(section, z, n, False)

    def body(x, carry):
        grad_tables(*source.next(x, half), r.f1, r.fs, r.d1, r.ds)

        def inner(i, carry):
            k = x * blocks + i

            @pl.when(k >= 2)
            def _():
                move(k - 2, lax.rem(k, 2)).wait_send()

            grad_block(i * block, r.f1, r.fs, r.d1, r.ds, r.out.at[lax.rem(k, 2)])
            move(k, lax.rem(k, 2)).start()
            return carry

        return lax.fori_loop(0, blocks, inner, carry)

    lax.fori_loop(0, half, body, 0)
    total = half * blocks
    for k in (total - 2, total - 1):
        move(k, k % 2).wait_send()

    def close(k, carry):
        move(k, 0).wait_recv()
        return carry

    lax.fori_loop(0, total, close, 0)


def own_grad_kernel(names, per_core, m_ref, *refs):
    r = types.SimpleNamespace(**dict(zip(names, refs)))
    x, i = pl.program_id(0), pl.program_id(1)
    source = grad_input(r, m_ref[0] == 0, per_core)

    @pl.when(i == 0)
    def _():
        @pl.when(x == 0)
        def _():
            source.load(0, 0)

        grad_tables(*source.next(x, pl.num_programs(0)), r.f1, r.fs, r.d1, r.ds)

    r.bound_out[...] = r.bound_in[...]
    r.out[1 - m_ref[0]] = r.far[...]
    grad_block(i * r.out.shape[2], r.f1, r.fs, r.d1, r.ds, r.out.at[m_ref[0]])


def whole(array):
    return pl.BlockSpec(array.shape, lambda *_: (0,) * array.ndim)


def params(**kw):
    return pltpu.CompilerParams(vmem_limit_bytes=VMEM_LIMIT, **kw)


def local(inputs, cotangent, region_id, spectral_w, conv_w, bias_vector):
    micro_count, _, rows_dev, channels, width = inputs.shape
    lanes = spectral_w.shape[-1]
    half = lanes // 2
    kx_dev = spectral_w.shape[1]
    row_devices, sections = lax.axis_size("rows"), lax.axis_size("section")
    mode_rows, height = kx_dev * row_devices, rows_dev * row_devices
    section = lax.axis_index("section")
    per_core = micro_count // sections
    kx_half = kx_dev // sections

    plain, doubled = col_tables(width, half)

    def stacked(array):
        high, low = np_split(array)
        return np.concatenate([high, high, low], 0)

    t_plain, t_doubled, it_plain, it_doubled = [stacked(t) for t in (plain, doubled, plain.T, doubled.T)]
    kron, ikron = row_tables(height, mode_rows, lax.axis_index("rows") * rows_dev, rows_dev)

    count = 2 * G
    chunks = channels // count
    hbm, vmem = pl.BlockSpec(memory_space=pl.ANY), pl.BlockSpec(memory_space=pltpu.VMEM)
    field_shape = jax.ShapeDtypeStruct((rows_dev, channels, width), F32)
    part_dims = (row_devices, chunks, sections, kx_half, count, lanes)
    p_shape, f_shape = jax.ShapeDtypeStruct(part_dims, F32), jax.ShapeDtypeStruct(part_dims[1:], F32)
    y_shape = jax.ShapeDtypeStruct((sections, chunks, kx_half, count, lanes), F32)
    stat_shape = jax.ShapeDtypeStruct((3, R, 128), F32)
    cg_shape = jax.ShapeDtypeStruct((2 * channels, 2 * channels), F32)
    bg_shape = jax.ShapeDtypeStruct((channels, width), F32)
    bound_shape = jax.ShapeDtypeStruct((micro_count, rows_dev, channels, width), F32)
    dma = pltpu.SemaphoreType.DMA
    field_buf = pltpu.VMEM((rows_dev, channels, width), F32)
    full_dims = (chunks, row_devices, sections, kx_half, count, lanes)
    spread = pltpu.VMEM((width // 128, rows_dev * count, 128), F32)
    energy = pltpu.VMEM((rows_dev, G, width), F32)
    line_sems = dma((2, chunks, row_devices))
    start_scratch = dict(part=pltpu.VMEM(part_dims, F32), come=pltpu.VMEM((2, chunks, row_devices) + part_dims[2:], F32),
                         f_sem=dma((chunks,)), red_send=line_sems, red_recv=line_sems)

    def run(body, ident, ins, outs, scratch, cost=50, aliases=None):
        names = [*ins, *outs, *scratch]
        spec = lambda entry: vmem if isinstance(entry, tuple) else hbm
        plain = lambda entry: entry[0] if isinstance(entry, tuple) else entry
        kernel = lambda *refs: body(types.SimpleNamespace(**dict(zip(names, refs))))
        positions = {list(ins).index(k): list(outs).index(v) for k, v in (aliases or {}).items()}
        result = pl.pallas_call(
            kernel, in_specs=[spec(e) for e in ins.values()], out_specs=[spec(e) for e in outs.values()],
            out_shape=[plain(e) for e in outs.values()], scratch_shapes=list(scratch.values()),
            input_output_aliases=positions,
            cost_estimate=pl.CostEstimate(flops=0, bytes_accessed=cost * 3_000_000, transcendentals=0),
            compiler_params=params(collective_id=ident, has_side_effects=True))(*[plain(e) for e in ins.values()])
        return types.SimpleNamespace(**dict(zip(outs, result)))

    conv_rows_at_once = 256 // channels
    both_layers = lax.all_gather(jnp.concatenate([conv_w, bias_vector[:, None]], 1), "section", axis=0, tiled=True)
    conv_both, bias_both = both_layers[:, :channels], both_layers[:, channels]

    def conv_parts(matrix):
        wide = jnp.kron(jnp.eye(conv_rows_at_once, dtype=F32), matrix)
        rounded = lax.reduce_precision(wide, 8, 7)
        high, low = rounded.astype(BF16), (wide - rounded).astype(BF16)
        return jnp.concatenate([high, low, high], 1)

    conv_fwd = [conv_parts(conv_both[l].T) for l in range(2)]
    conv_bwd = [conv_parts(conv_both[l]) for l in range(2)]
    bias_wide = [jnp.broadcast_to(bias_both[l][:, None], (channels, width)) for l in range(2)]

    def mixing(body, layer, pair):
        flag = jnp.stack([(section == layer).astype(jnp.int32), section * kx_half])
        f_block = pl.BlockSpec((chunks, sections, None, count, lanes), lambda x, m: (0, 0, x, 0, 0))
        y_block = pl.BlockSpec((sections, chunks, None, count, lanes), lambda x, m: (0, 0, x, 0, 0))
        small = pltpu.VMEM((sections, channels, lanes), F32)
        grid_spec = pltpu.PrefetchScalarGridSpec(
            num_scalar_prefetch=1, grid=(kx_half,), in_specs=[f_block, hbm, hbm], out_specs=y_block,
            scratch_shapes=[pltpu.VMEM((SLOTS, channels, channels, lanes), F32), small, small, dma((SLOTS,))])
        return pl.pallas_call(
            body, grid_spec=grid_spec, out_shape=y_shape, compiler_params=params(),
            cost_estimate=pl.CostEstimate(flops=0, bytes_accessed=30_000_000, transcendentals=0))(
                flag, pair, spectral_w, far_weights)

    streams = range(per_core)
    start = run(
        functools.partial(start_kernel, per_core), 0,
        dict(inputs=inputs, weights=spectral_w, table=(t_plain,), kron=(kron,)),
        dict(f_out=f_shape, far=jax.ShapeDtypeStruct((kx_half,) + spectral_w.shape[2:], F32),
             **{f"p{j}": p_shape for j in streams[1:]}),
        dict(a_buf=pltpu.VMEM((2, rows_dev, count, width), F32), w_buf=pltpu.VMEM((2,) + spectral_w.shape[2:], F32),
             p_buf=pltpu.VMEM((per_core,) + full_dims, F32), spread=spread, a_sem=dma((2,)), w_sem=dma((2,)),
             w_cross=dma((2, kx_half)), p_local=dma((per_core, chunks)), p_cross=dma((per_core, 2, chunks)),
             **start_scratch))
    far_weights = start.far

    members = lax.axis_size("batch")
    kinds = ["middle", "turn", "back", "tail"]
    mixes = [(0, False), (1, False), (1, True), (0, True)]
    names = ["f00", "f01", "f10", "f11", "g10", "g11", "g00", "g01"]
    places = [dict(a=0, z=1), dict(a=2, z=3), dict(a=4, z=5, cot=6), dict(a=0, z=1, cot=2),
              dict(gz=3, a=4, h=5, dg=6), dict(gz=0, a=1, h=2, dg=3), dict(gz=4, a=5, h=6), dict(gz=0, a=1, h=2)]
    y = mixing(mix_kernel, 0, start.f_out)
    both = (2,)
    ins = dict(inputs=inputs, cotangent=cotangent, region=region_id, weights=spectral_w, far=far_weights,
               p_in=start.p1, f_in=start.f_out, y_in=y, t_plain=(t_plain,), t_doubled=(t_doubled,), it_plain=(it_plain,),
               it_doubled=(it_doubled,), kron=(kron,), ikron=(ikron,),
               **{f"conv_f{l}": (conv_fwd[l],) for l in range(2)}, **{f"conv_b{l}": (conv_bwd[l],) for l in range(2)},
               **{f"bias{l}": (bias_wide[l],) for l in range(2)})
    outs = dict(bound=bound_shape, stat=(jax.ShapeDtypeStruct((2 * per_core,) + stat_shape.shape, F32),),
                cg=(jax.ShapeDtypeStruct((2 * per_core,) + cg_shape.shape, F32),),
                bg=(jax.ShapeDtypeStruct((2 * per_core,) + bg_shape.shape, F32),),
                **{f"{name}{j}": field_shape for name in ("a1_", "dg0_", "gz1_", "ga1_", "gz0_") for j in streams},
                **{f"shared{i}": jax.ShapeDtypeStruct((members,) + f_shape.shape, F32) for i in range(len(names))})
    scratch = dict(
        fields=pltpu.VMEM((7,) + field_shape.shape, F32), full=pltpu.VMEM(both + full_dims, F32),
        part=pltpu.VMEM(both + part_dims, F32),
        come=pltpu.VMEM(both + (2, chunks, row_devices - 1) + part_dims[2:], F32),
        keep=pltpu.VMEM(both + f_shape.shape, F32), y_give=pltpu.VMEM(both + y_shape.shape[1:], F32),
        p_buf=pltpu.VMEM(full_dims, F32), spread=spread, eo=energy, eb=energy,
        rid=pltpu.VMEM((2, rows_dev, width), jnp.int32),
        wbuf=pltpu.VMEM((6, count, channels, lanes), F32), macc=pltpu.VMEM((kx_half, 2 * sections, channels, lanes), F32),
        msrc=pltpu.VMEM((2 * sections, channels, lanes), F32),
        field_sem=dma((7,)), rid_sem=dma(both), out_sem=dma((2, 2, chunks)), wsem=dma((6,)), first_sem=dma((4,)),
        send=dma(both + (2, chunks, row_devices)), recv=dma(both + (2, chunks, row_devices)),
        red_send=dma(both + (2, chunks, row_devices)), red_recv=dma(both + (2, chunks, row_devices)),
        y_cross=dma((2, 2, chunks)), p_local=dma((chunks,)), p_cross=dma((2, 2, chunks)),
        b_local=dma((2, chunks)), b_cross=dma((2, 2, chunks)),
        s_local=dma(both), s_send=dma((2, members)), s_recv=dma((len(names), members)))
    done = run(functools.partial(stages_kernel, per_core, kinds, places, mixes), 1, ins, outs, scratch, cost=400)
    gathered = {name: getattr(done, f"shared{i}") for i, name in enumerate(names)}
    bound, calls = done.bound, 1

    grids = per_core * members * sections
    block = G
    blocks = channels // 2 // block
    in_buf = pltpu.VMEM((2, per_core, members, chunks, sections, count, lanes), F32)
    big, small = pltpu.VMEM((grids, channels, lanes), F32), pltpu.VMEM((grids, channels // 2, lanes), F32)
    grad_scratch = dict(fbuf=in_buf, gbuf=in_buf, in_sem=dma((2, 2)), f1=big, fs=small, d1=big, ds=big)
    row_dims = (2, channels // 2, channels, lanes)
    far_grad = run(functools.partial(far_grad_kernel, per_core), 1 + calls, gathered,
                   dict(far=jax.ShapeDtypeStruct((kx_half,) + row_dims, F32)),
                   dict(out=pltpu.VMEM((2, 2, block, channels, lanes), F32), send=dma((kx_half * blocks,)),
                        recv=dma((kx_half * blocks,)), **grad_scratch)).far
    bound_rows = bound.reshape(micro_count * rows_dev, channels, width)
    bound_block = pl.BlockSpec((bound_rows.shape[0] // (kx_half * blocks), channels, width),
                               lambda x, i, m: (x * blocks + i, 0, 0))
    grid_spec = pltpu.PrefetchScalarGridSpec(
        num_scalar_prefetch=1, grid=(kx_half, blocks),
        in_specs=[hbm] * len(gathered)
        + [pl.BlockSpec((None, 2, block, channels, lanes), lambda x, i, m: (x, 0, i, 0, 0)), bound_block],
        out_specs=[pl.BlockSpec((2, None, 2, block, channels, lanes), lambda x, i, m: (0, x, 0, i, 0, 0)), bound_block],
        scratch_shapes=list(grad_scratch.values()))
    spectral_grad, boundary = pl.pallas_call(
        functools.partial(own_grad_kernel, [*gathered, "far", "bound_in", "out", "bound_out", *grad_scratch], per_core),
        grid_spec=grid_spec, out_shape=[jax.ShapeDtypeStruct((2, kx_half) + row_dims, F32),
                                        jax.ShapeDtypeStruct(bound_rows.shape, F32)],
        cost_estimate=pl.CostEstimate(flops=0, bytes_accessed=150_000_000, transcendentals=0),
        compiler_params=params())(
            jnp.reshape(section, (1,)).astype(jnp.int32), *gathered.values(), far_grad, bound_rows)
    spectral_grad = spectral_grad.reshape(spectral_w.shape)
    boundary = boundary.reshape((1, micro_count, 1) + inputs.shape[2:])

    def lower(value):
        return (value[:channels, :channels] + value[channels:, channels:]
                + value[:channels, channels:] + value[channels:, :channels])

    pair = lambda value: jnp.sum(value.reshape((2, per_core) + value.shape[1:]), 1)
    conv_local = jnp.stack([lower(value) for value in pair(done.cg)[::-1]])
    bias_local = jnp.sum(pair(done.bg)[::-1], -1)
    stat_local = jnp.sum(pair(done.stat), -1)
    shapes = [v.shape for v in (conv_local, bias_local, stat_local)]
    flat_sums = jnp.concatenate([v.reshape(-1) for v in (conv_local, bias_local, stat_local)])
    length = flat_sums.shape[0]
    flat_sums = jnp.pad(flat_sums, (0, -length % 1024)).reshape(-1, 128)
    flat_sums = jnp.sum(lax.all_gather(flat_sums, ("section", "batch", "rows"), axis=0), 0).reshape(-1)
    ends = np.cumsum([0] + [math.prod(shape) for shape in shapes])
    conv_sum, bias_sum, stat_sum = [flat_sums[ends[i]:ends[i + 1]].reshape(shapes[i]) for i in range(3)]
    own_stat = lax.dynamic_index_in_dim(stat_sum, section, 0, False)
    layer_rms = jnp.sqrt(own_stat[:2] / (channels * own_stat[2])[None, :] + 1e-06)[None]
    own = lambda value: lax.dynamic_slice_in_dim(value, section, 1, 0)
    return boundary, spectral_grad, own(conv_sum), own(bias_sum), layer_rms


def solution(mesh):
    placed = (
        P(None, "batch", "rows", None, None),
        P(None, "batch", "rows", None, None),
        P(None, "batch", "rows", None),
        P("section", "rows", None, None, None),
        P("section", None, None),
        P("section", None),
    )
    return jax.shard_map(
        local,
        mesh=mesh,
        in_specs=placed,
        out_specs=(
            P("section", None, "batch", "rows", None, None),
            P("section", "rows", None, None, None),
            P("section", None, None),
            P("section", None),
            P("section", None, None),
        ),
        check_vma=False,
    )
```

```python
import functools
import math
import types

import jax
import jax.numpy as jnp
import numpy as np
from jax import lax
from jax.experimental import pallas as pl
from jax.experimental.pallas import tpu as pltpu
from jax.sharding import PartitionSpec as P

R = 8
G = 8
AHEAD = 2
F32 = jnp.float32
BF16 = jnp.bfloat16
VMEM_LIMIT = 62 * 1024 * 1024
MESH = pl.DeviceIdType.MESH


def split(value):
    high = value.astype(BF16)
    return high, (value - high.astype(F32)).astype(BF16)


def dot(left, right, dims=(((1,), (0,)), ((), ()))):
    return lax.dot_general(left, right, dims, preferred_element_type=F32)


def dot3(left, right):
    return dot(left[0], right[0]) + (dot(left[1], right[0]) + dot(left[0], right[1]))


def np_split(value):
    high = value.astype(np.float32).astype(BF16)
    return high, (value - high.astype(np.float64)).astype(np.float32).astype(BF16)


def col_tables(width, half):
    phase = 2.0 * math.pi / width * (np.outer(np.arange(width), np.arange(half)) % width)
    cosine, sine = np.cos(phase) / math.sqrt(width), np.sin(phase) / math.sqrt(width)
    plain = np.concatenate([cosine, -sine, -sine, -cosine], 1)
    doubled = plain * np.tile(np.where(np.arange(half) == 0, 1.0, 2.0), 4)[None, :]
    return plain, doubled


def row_tables(height, mode_rows, first_row, rows_dev):
    position = jnp.arange(mode_rows, dtype=jnp.int32)
    frequency = jnp.where(position < mode_rows // 2, position, height - mode_rows + position)
    row = first_row + jnp.arange(rows_dev, dtype=jnp.int32)
    phase = 2.0 * math.pi / height * (frequency[:, None] * row[None, :] % height).astype(F32)
    small = jnp.concatenate([jnp.cos(phase), jnp.sin(phase)], 1) / math.sqrt(height)
    rounded = lax.reduce_precision(small, 8, 7)
    high, low = rounded.astype(BF16), (small - rounded).astype(BF16)
    forward = jnp.concatenate([jnp.concatenate([high, high], 1), jnp.concatenate([low, jnp.zeros_like(low)], 1)], 0)
    inverse = jnp.concatenate([high.T, high.T, low.T], 1)
    return forward, inverse


def to_modes(value, table, kron, spread, p_ref):
    mode_rows, count, lanes = p_ref.shape
    rows = value.shape[0] // count
    high, low = split(value)
    spectra = dot(jnp.concatenate([high, low, high], 1), table)
    for i in range(2):
        spread[i] = spectra[:, i * lanes:(i + 1) * lanes]
    out = p_ref.reshape(mode_rows * count, lanes)
    for first in range(0, count, 2):
        sides = []
        for c in (first, first + 1):
            pick = pl.ds(c, rows, stride=count)
            sides.append(jnp.concatenate([spread[i, pick, :] for i in range(2)], 0))
        high, low = split(jnp.concatenate(sides, 1))
        both = dot(kron, jnp.concatenate([high, low], 0))
        result = both[:mode_rows] + both[mode_rows:]
        for i in range(2):
            out[pl.ds(first + i, mode_rows, stride=count), :] = result[:, i * lanes:(i + 1) * lanes]


def from_modes(y_ref, table, kron, spread):
    mode_rows, count, lanes = y_ref.shape
    rows, pieces = spread.shape[1] // count, spread.shape[0]
    modes = y_ref.reshape(mode_rows * count, lanes)
    sides = []
    for first in range(0, count, 2):
        pair = [modes[pl.ds(c, mode_rows, stride=count), :] for c in (first, first + 1)]
        high, low = split(jnp.concatenate(pair, 1))
        both = dot(kron, jnp.concatenate([high, low, high], 0))
        for i in range(2):
            side = both[:, i * lanes:(i + 1) * lanes]
            sides.append(jnp.concatenate([side[:rows], side[rows:]], 1))
    high, low = split(jnp.concatenate(sides, 0))
    out = dot(jnp.concatenate([high, low, high], 1), table)
    for c in range(count):
        for i in range(pieces):
            spread[i, pl.ds(c, rows, stride=count), :] = out[c * rows:(c + 1) * rows, i * 128:(i + 1) * 128]
    return jnp.concatenate([spread[i] for i in range(pieces)], 1)


def gelu_parts(z):
    size = jnp.abs(z)
    gauss = jnp.exp(-0.5 * z * z)
    base = 1.0 + (0.3275911 / math.sqrt(2.0)) * size
    t = pl.reciprocal(base, approx=True)
    t = t * (2.0 - base * t)
    poly = t * (0.254829592 + t * (-0.284496736 + t * (1.421413741 + t * (-1.453152027 + t * 1.061405429))))
    tail = 0.5 * poly * gauss
    phi = jnp.where(z >= 0, 1.0 - tail, tail)
    return z * phi, phi + z * (gauss * (1.0 / math.sqrt(2.0 * math.pi)))


def flat(ref):
    rows, count, width = ref.shape
    return ref[...].reshape(rows * count, width)


def put(ref, value):
    ref[...] = value.reshape(ref.shape)


def place_and_peers():
    section, z = lax.axis_index("section"), lax.axis_index("rows")
    return section, z, lax.axis_size("rows")


def greet(section, z, n, lines, members=0):
    barrier = pltpu.get_barrier_semaphore()
    pl.semaphore_signal(barrier, inc=1, device_id={"section": 1 - section}, device_id_type=MESH)
    if not lines:
        pl.semaphore_wait(barrier, 1)
        return

    @pl.when(z > 0)
    def _():
        pl.semaphore_signal(barrier, inc=1, device_id={"rows": z - 1}, device_id_type=MESH)

    @pl.when(z < n - 1)
    def _():
        pl.semaphore_signal(barrier, inc=1, device_id={"rows": z + 1}, device_id_type=MESH)

    for away in range(1, members):
        pl.semaphore_signal(barrier, inc=1, device_id={"batch": lax.rem(lax.axis_index("batch") + away, members)},
                            device_id_type=MESH)

    others = 1 + max(members - 1, 0)
    pl.semaphore_wait(barrier, others + (z > 0).astype(jnp.int32) + (z < n - 1).astype(jnp.int32))


def to_core(src, dst, sems, section):
    return pltpu.make_async_remote_copy(src_ref=src, dst_ref=dst, send_sem=sems[0], recv_sem=sems[1],
                                        device_id={"section": 1 - section}, device_id_type=MESH)


def guard(condition, body):
    if isinstance(condition, (bool, np.bool_)):
        if condition:
            body()
    else:
        pl.when(condition)(body)


class Line:
    def __init__(self, section, z, n, chunks, send, recv):
        self.section, self.z, self.n, self.chunks = section, z, n, chunks
        self.send, self.recv = send, recv

    def move(self, way, q, hop, src, dst):
        return pltpu.make_async_remote_copy(
            src_ref=src, dst_ref=dst, send_sem=self.send.at[way, q, hop], recv_sem=self.recv.at[way, q, hop],
            device_id={"rows": self.z + 1 if way == 0 else self.z - 1}, device_id_type=MESH)

    def sends(self, way):
        return self.z < self.n - 1 if way == 0 else self.z > 0

    def hears(self, way):
        return self.z > 0 if way == 0 else self.z < self.n - 1


def within(value, count):
    return jnp.logical_and(value >= 0, value < count)


class Gather(Line):
    def __init__(self, section, z, n, r, parity):
        super().__init__(section, z, n, r.full.shape[1], r.send.at[parity], r.recv.at[parity])
        self.full, self.give_from = r.full.at[parity], r.y_give.at[parity]
        self.cross = r.y_cross.at[parity]

    def swap(self, q):
        return to_core(self.give_from.at[q], self.full.at[q, self.z, self.section],
                       (self.cross.at[0, q], self.cross.at[1, q]), self.section)

    def give(self, q):
        self.swap(q).start()

    def hop(self, way, q, hop):
        piece = self.full.at[q, self.source(way, hop)]
        return self.move(way, q, hop, piece, piece)

    def source(self, way, hop):
        return self.z - hop if way == 0 else self.z + hop

    def known(self, way, hop):
        at = self.source(way, hop)
        return at >= 0 if way == 0 else at < self.n

    def own(self, q):
        self.swap(q).wait_recv()
        for way in range(2):
            @pl.when(self.sends(way))
            def _():
                self.hop(way, q, 0).start()

    def step(self, q, hop):
        for way in range(2):
            @pl.when(self.known(way, hop + 1))
            def _():
                piece = self.full.at[q, self.source(way, hop + 1)]
                self.move(way, q, hop, piece, piece).wait_recv()

                @pl.when(self.sends(way))
                def _():
                    self.hop(way, q, hop + 1).start()

    def begin(self):
        for q in range(min(AHEAD, self.chunks)):
            self.own(q)

    def tick(self, t):
        @pl.when(t + AHEAD < self.chunks)
        def _():
            self.own(t + AHEAD)

        for hop in range(self.n - 1):
            q = t - hop - 1
            pl.when(within(q, self.chunks))(functools.partial(self.step, q, hop))

    def finish(self):
        def body(q, carry):
            self.swap(q).wait_send()
            for way in range(2):
                for hop in range(self.n - 1):
                    @pl.when(jnp.logical_and(self.sends(way), self.known(way, hop)))
                    def _():
                        self.hop(way, q, hop).wait_send()
            return carry

        lax.fori_loop(0, self.chunks, body, 0)


class Sum(Line):
    def __init__(self, section, z, n, r, parity, admit):
        super().__init__(section, z, n, r.part.shape[2], r.red_send.at[parity], r.red_recv.at[parity])
        self.part, self.come, self.keep, self.admit = r.part.at[parity], r.come.at[parity], r.keep.at[parity], admit

    def owner(self, way, hop):
        return self.z + self.n - hop if way == 0 else self.z - self.n + hop

    def valid(self, way, hop):
        return self.z <= hop - 1 if way == 0 else self.z >= self.n - hop

    def sent(self, way, q, hop):
        return self.move(way, q, hop, self.part.at[self.owner(way, hop), q], self.come.at[way, q, hop - 1])

    def heard(self, way, q, hop):
        come = self.come.at[way, q, hop - 1]
        self.move(way, q, hop, come, come).wait_recv()

    def first(self, q):
        self.admit(q)
        for way in range(2):
            @pl.when(jnp.logical_not(self.hears(way)))
            def _():
                for hop in range(1, self.n):
                    @pl.when(self.valid(way, hop))
                    def _():
                        self.sent(way, q, hop).start()

    def step(self, q, hop):
        for way in range(2):
            @pl.when(jnp.logical_and(self.valid(way, hop), self.hears(way)))
            def _():
                self.heard(way, q, hop - 1)
                owner = self.owner(way, hop)
                self.part[owner, q] = self.part[owner, q] + self.come[way, q, hop - 2]
                self.sent(way, q, hop).start()

    def final(self, q):
        for way in range(2):
            @pl.when(self.hears(way))
            def _():
                self.heard(way, q, self.n - 1)
                self.part[self.z, q] = self.part[self.z, q] + self.come[way, q, self.n - 2]

        self.keep[q] = self.part[self.z, q]

    def tick(self, t):
        pl.when(within(t, self.chunks))(functools.partial(self.first, t))
        for hop in range(2, self.n + 1):
            q = t - hop + 1
            pl.when(within(q, self.chunks))(
                functools.partial(self.step, q, hop) if hop < self.n else functools.partial(self.final, q))

    def finish(self):
        def body(q, carry):
            for way in range(2):
                for hop in range(1, self.n):
                    @pl.when(self.valid(way, hop))
                    def _():
                        self.sent(way, q, hop).wait_send()
            return carry

        lax.fori_loop(0, self.chunks, body, 0)


class Reduce(Line):
    def __init__(self, section, z, n, part, come, f_out, f_sem, send, recv, ahead):
        super().__init__(section, z, n, part.shape[1], send, recv)
        self.ahead = ahead
        self.part, self.come, self.f_out, self.f_sem = part, come, f_out, f_sem

    def owner(self, way, hop):
        return self.z + self.n - hop if way == 0 else self.z - self.n + hop

    def valid(self, way, hop):
        return self.z <= hop - 1 if way == 0 else self.z >= self.n - hop

    def sent(self, way, q, hop):
        return self.move(way, q, hop, self.part.at[self.owner(way, hop), q], self.come.at[way, q, hop])

    def heard(self, way, q, hop):
        come = self.come.at[way, q, hop]
        self.move(way, q, hop, come, come).wait_recv()

    def first(self, t):
        for hop in range(1, self.n):
            q = t - hop + 1

            def send():
                for way in range(2):
                    @pl.when(jnp.logical_and(self.valid(way, hop), jnp.logical_not(self.hears(way))))
                    def _():
                        self.sent(way, q, hop).start()

            guard(0 <= q < self.chunks if isinstance(q, int) else q < self.chunks, send)

    def step(self, q, hop):
        for way in range(2):
            @pl.when(jnp.logical_and(self.valid(way, hop), self.hears(way)))
            def _():
                self.heard(way, q, hop - 1)
                owner = self.owner(way, hop)
                self.part[owner, q] = self.part[owner, q] + self.come[way, q, hop - 1]
                self.sent(way, q, hop).start()

    def result(self, q):
        return pltpu.make_async_copy(self.part.at[self.z, q], self.f_out.at[q], self.f_sem.at[q])

    def final(self, q):
        for way in range(2):
            @pl.when(self.hears(way))
            def _():
                self.heard(way, q, self.n - 1)
                self.part[self.z, q] = self.part[self.z, q] + self.come[way, q, self.n - 1]

        self.result(q).start()

    def tick(self, t):
        if isinstance(t, int) and t == 0:
            for early in range(self.ahead):
                self.first(early)
        self.first(t + self.ahead)
        for hop in range(2, self.n + 1):
            q = t - hop + 1
            if isinstance(q, int):
                valid = 0 <= q < self.chunks
            else:
                valid = q < self.chunks
            guard(valid, functools.partial(self.step, q, hop) if hop < self.n else functools.partial(self.final, q))

    def finish(self):
        def body(q, carry):
            self.result(q).wait()
            for way in range(2):
                for hop in range(1, self.n):
                    @pl.when(self.valid(way, hop))
                    def _():
                        self.sent(way, q, hop).wait_send()
            return carry

        lax.fori_loop(0, self.chunks, body, 0)


def fetch(src, dst, sem, parts=4):
    step = dst.shape[0] // parts
    for i in range(parts):
        pltpu.make_async_copy(src.at[pl.ds(i * step, step)], dst.at[pl.ds(i * step, step)], sem).start()


def arrived(dst, sem):
    pltpu.make_async_copy(dst, dst, sem).wait()


def portions(total, count):
    return [(i * total // count, (i + 1) * total // count) for i in range(count)]


def conv_rows(weight, bias, a, out, first, last):
    channels, width = a.shape[1:]
    block = weight.shape[0] // channels

    def body(i, carry):
        at = pl.ds(i * block, block)
        high, low = split(a[at].reshape(block * channels, width))
        result = dot(weight[...], jnp.concatenate([high, high, low], 0)).reshape(block, channels, width)
        out[at] = result + bias[...][None] if bias is not None else out[at] + result
        return carry

    lax.fori_loop(first, last, body, 0)


def grad_rows(a, gz, cg_ref, bg_ref, first, last):
    channels, width = a.shape[1:]

    def body(r, carry):
        grad, bias = carry
        g = gz[r]
        left = jnp.concatenate(split(a[r]), 0)
        right = jnp.concatenate(split(g), 0)
        return grad + dot(left, right, (((1,), (1,)), ((), ()))), bias + g

    grad, bias = lax.fori_loop(first, last, body, (cg_ref[...], bg_ref[...]))
    cg_ref[...] = grad
    bg_ref[...] = bias


def chunk_of(ref, q, count):
    rows, _, width = ref.shape
    return ref[:, pl.ds(pl.multiple_of(q * count, count), count), :].reshape(rows * count, width)


def chunk_at(ref, q, count):
    return ref.at[:, pl.ds(pl.multiple_of(q * count, count), count), :]


class Modes:
    def __init__(self, section, buffer, p_out, local, cross):
        self.section, self.buffer, self.p_out, self.local, self.cross = section, buffer, p_out, local, cross

    def view(self, q):
        n, halves, kx, count, lanes = self.buffer.shape[1:]
        return self.buffer.at[q].reshape(n * halves * kx, count, lanes)

    def copies(self, q):
        s = self.section
        return (pltpu.make_async_copy(self.buffer.at[q, :, s], self.p_out.at[:, q, 0], self.local.at[q]),
                to_core(self.buffer.at[q, :, 1 - s], self.p_out.at[:, q, 1],
                        (self.cross.at[0, q], self.cross.at[1, q]), s))

    def start(self, q):
        for copy in self.copies(q):
            copy.start()

    def wait(self, q):
        for copy in self.copies(q):
            copy.wait()


class Bound:
    def __init__(self, section, owner, micro, other, source, bound, local, cross):
        self.section, self.owner, self.micro, self.other = section, owner, micro, other
        self.source, self.bound, self.local, self.cross = source, bound, local, cross

    def copies(self, q, count, micro):
        src, dst = chunk_at(self.source, q, count), chunk_at(self.bound.at[micro], q, count)
        return (pltpu.make_async_copy(src, dst, self.local.at[q]),
                to_core(src, dst, (self.cross.at[0, q], self.cross.at[1, q]), self.section))

    def start(self, q, count):
        here, there = self.copies(q, count, self.micro)

        @pl.when(self.section == self.owner)
        def _():
            here.start()

        @pl.when(self.section != self.owner)
        def _():
            there.start()

    def wait(self, q, count):
        here, there = self.copies(q, count, self.micro)
        come = self.copies(q, count, self.other)[1]

        @pl.when(self.section == self.owner)
        def _():
            here.wait()
            come.wait_recv()

        @pl.when(self.section != self.owner)
        def _():
            there.wait_send()


def add_squares(value, total):
    rows, _, width = total.shape
    square = (value * value).reshape(rows, -1, width)
    for at in range(0, square.shape[1], G):
        total[...] += square[:, at:at + G]


def region_sums(rid_ref, eo, eb, stat_ref):
    rows, _, width = eo.shape
    rid = rid_ref[...]
    energies = (jnp.sum(eo[...], axis=1), jnp.sum(eb[...], axis=1), jnp.ones((rows, width), F32))
    for kind in range(3):
        for region in range(R):
            line = jnp.sum(jnp.where(rid == region + 1, energies[kind], 0.0), axis=0, keepdims=True)
            total = line[:, :128]
            for piece in range(1, width // 128):
                total = total + line[:, piece * 128:(piece + 1) * 128]
            stat_ref[kind, region:region + 1, :] = total


def start_kernel(per_core, r):
    section, z, n = place_and_peers()
    chunks, count, half = r.p_buf.shape[1], r.p_buf.shape[5], r.far.shape[0]
    blocks = [(j, q) for j in range(per_core) for q in range(chunks)]
    reduce = Reduce(section, z, n, r.part, r.come, r.f_out, r.f_sem, r.red_send, r.red_recv, 0)
    outs = [r.part] + [getattr(r, f"p{j}") for j in range(1, per_core)]
    modes = [Modes(section, r.p_buf.at[j], outs[j], r.p_local.at[j], r.p_cross.at[j]) for j in range(per_core)]

    def field(k):
        j, q = blocks[k]
        src = chunk_at(r.inputs.at[section * per_core + j, 0], q, count)
        return pltpu.make_async_copy(src, r.a_buf.at[k % 2], r.a_sem.at[k % 2])

    def weight_in(x):
        return pltpu.make_async_copy(r.weights.at[0, (1 - section) * half + x], r.w_buf.at[x % 2], r.w_sem.at[x % 2])

    def weight_out(x):
        return to_core(r.w_buf.at[x % 2], r.far.at[x], (r.w_cross.at[0, x], r.w_cross.at[1, x]), section)

    def lend(x):
        if x < half:
            weight_in(x).wait()
            weight_out(x).start()
        if 1 <= x <= half:
            weight_out(x - 1).wait_send()
            if x + 1 < half:
                weight_in(x + 1).start()

    field(0).start()
    for x in range(min(2, half)):
        weight_in(x).start()
    greet(section, z, n, True)
    for k, (j, q) in enumerate(blocks):
        if k + 1 < len(blocks):
            field(k + 1).start()
        field(k).wait()
        to_modes(flat(r.a_buf.at[k % 2]), r.table[...], r.kron[...], r.spread, modes[j].view(q))
        modes[j].start(q)
        lend(k)
        if k >= 1:
            if k <= chunks:
                modes[0].wait(k - 1)
            reduce.tick(k - 1)
    for k in range(len(blocks), half + 1):
        lend(k)
    for t in range(len(blocks) - 1, chunks + n - 1):
        reduce.tick(t)
    for x in range(half):
        weight_out(x).wait_recv()
    for j, q in blocks[chunks:]:
        modes[j].wait(q)
    reduce.finish()


class Share:
    def __init__(self, r, index, parity):
        self.r, self.index, self.parity = r, index, parity
        self.me, self.members = lax.axis_index("batch"), lax.axis_size("batch")

    def copies(self):
        source, target = self.r.keep.at[self.parity], getattr(self.r, f"shared{self.index}").at[self.me]
        yield pltpu.make_async_copy(source, target, self.r.s_local.at[self.parity])
        for away in range(1, self.members):
            yield pltpu.make_async_remote_copy(
                src_ref=source, dst_ref=target, send_sem=self.r.s_send.at[self.parity, away],
                recv_sem=self.r.s_recv.at[self.index, away],
                device_id={"batch": lax.rem(self.me + away, self.members)}, device_id_type=MESH)

    def start(self):
        for copy in self.copies():
            copy.start()

    def wait_send(self):
        for i, copy in enumerate(self.copies()):
            if i == 0:
                copy.wait()
            else:
                copy.wait_send()

    def wait_recv(self):
        for i, copy in enumerate(self.copies()):
            if i > 0:
                copy.wait_recv()


class Stage:
    def __init__(self, k, kind, j, per_core, places, section, z, n, r):
        self.k, self.kind, self.j, self.r, self.section, self.n = k, kind, j, r, section, n
        self.parity = k % 2
        self.micro, self.other = section * per_core + j, (1 - section) * per_core + j
        self.forward, self.last = kind in ("middle", "turn"), kind == "tail"
        self.buffers = {name: r.fields.at[i] for name, i in places.items()}
        self.sems = {name: r.field_sem.at[i] for name, i in places.items()}
        self.gather = Gather(section, z, n, r, self.parity)
        self.count, self.lanes = r.full.shape[5], r.full.shape[6]
        self.chunks = r.full.shape[1]
        plain = lambda name: getattr(r, f"{name}{j}")
        if kind == "middle":
            self.loads = dict(a=r.inputs.at[self.micro, 0])
            self.saves = dict(a=plain("a1_"), z=plain("dg0_"))
        elif kind == "turn":
            self.loads = dict(a=plain("a1_"), cot=r.cotangent.at[self.micro, 0])
            self.saves = dict(cot=plain("gz1_"))
        elif kind == "back":
            self.loads = dict(gz=plain("gz1_"), h=r.cotangent.at[self.micro, 0], a=plain("a1_"), dg=plain("dg0_"))
            self.saves = dict(h=plain("ga1_"), dg=plain("gz0_"))
        else:
            self.loads = dict(gz=plain("gz0_"), h=plain("ga1_"), a=r.inputs.at[self.micro, 0])
            self.saves = {}
        layer = 0 if kind in ("middle", "tail") else 1
        self.weight = getattr(r, f"conv_{'f' if self.forward else 'b'}{layer}")
        self.bias = getattr(r, f"bias{layer}")
        self.table = r.t_plain if kind == "middle" else r.t_doubled
        self.itable = r.it_doubled if self.forward else r.it_plain
        if not self.last:
            self.modes = Modes(section, r.p_buf, r.part.at[self.parity], r.p_local, r.p_cross.at[self.parity])
        if kind in ("turn", "tail"):
            self.bound = Bound(section, 1 if kind == "turn" else 0, self.micro, self.other,
                               self.buffers["a" if kind == "turn" else "h"], r.bound,
                               r.b_local.at[self.parity], r.b_cross.at[self.parity])

    def prefetch(self):
        for name, src in self.loads.items():
            fetch(src, self.buffers[name], self.sems[name])
        if self.forward:
            self.rid_copy().start()

    def rid_copy(self):
        return pltpu.make_async_copy(self.r.region.at[self.micro, 0], self.r.rid.at[self.parity],
                                     self.r.rid_sem.at[self.parity])

    def got(self, name):
        arrived(self.buffers[name], self.sems[name])

    def open(self):
        r, b = self.r, self.buffers
        if self.forward:
            r.eo[...] = jnp.zeros_like(r.eo)
            r.eb[...] = jnp.zeros_like(r.eb)
            self.got("a")
        else:
            for name in ("gz", "h", "a"):
                self.got(name)
            at = self.k - self.r.first_back
            r.cg[at] = jnp.zeros_like(r.cg[at])
            r.bg[at] = jnp.zeros_like(r.bg[at])

    def before(self, i):
        r, b = self.r, self.buffers
        a = b["a"]
        rows, channels = a.shape[:2]
        blocks, parts = rows // (self.weight.shape[0] // channels), self.n - 1
        span = (i * blocks // parts, (i + 1) * blocks // parts)
        if self.forward:
            conv_rows(self.weight, self.bias, a, b["z"], *span)
        else:
            conv_rows(self.weight, None, b["gz"], b["h"], *span)
            at = self.k - r.first_back
            grad_rows(a, b["gz"], r.cg.at[at], r.bg.at[at], i * rows // parts, (i + 1) * rows // parts)

    def outs(self, q):
        return [pltpu.make_async_copy(chunk_at(self.buffers[name], q, self.count), chunk_at(dst, q, self.count),
                                      self.r.out_sem.at[self.parity, i, q])
                for i, (name, dst) in enumerate(self.saves.items())]

    def late(self):
        for name in ("cot", "dg"):
            if name in self.loads:
                self.got(name)

    def chunk(self, q):
        r, b, count = self.r, self.buffers, self.count
        spectral = from_modes(self.gather.full.at[q].reshape(-1, count, self.lanes), self.itable[...], r.ikron[...],
                              r.spread)
        if self.forward:
            branch, slope = gelu_parts(spectral + chunk_of(b["z"], q, count))
            if self.kind == "turn":
                put(chunk_at(b["cot"], q, count), chunk_of(b["cot"], q, count) * slope)
            else:
                put(chunk_at(b["z"], q, count), slope)
            add_squares(branch, r.eb)
            out = chunk_of(b["a"], q, count) + branch
            put(chunk_at(b["a"], q, count), out)
            add_squares(out, r.eo)
            source = b["cot" if self.kind == "turn" else "a"]
        else:
            ga = spectral + chunk_of(b["h"], q, count)
            put(chunk_at(b["h"], q, count), ga)
            if not self.last:
                put(chunk_at(b["dg"], q, count), ga * chunk_of(b["dg"], q, count))
                source = b["dg"]
        for copy in self.outs(q):
            copy.start()
        if self.kind in ("turn", "tail"):
            self.bound.start(q, count)
        if not self.last:
            to_modes(chunk_of(source, q, count), self.table[...], r.kron[...], r.spread, self.modes.view(q))

            pl.when(q == self.chunks - 1)(self.gather.finish)
            self.modes.start(q)

    def end(self):
        if self.forward:
            self.rid_copy().wait()
            region_sums(self.r.rid.at[self.parity], self.r.eo, self.r.eb, self.r.stat.at[self.k])
        if self.last:
            self.gather.finish()

    def close(self):
        def body(q, carry):
            for copy in self.outs(q):
                copy.wait()
            if self.kind in ("turn", "tail"):
                self.bound.wait(q, self.count)
            return carry

        lax.fori_loop(0, self.chunks, body, 0)


def stages_kernel(per_core, kinds, places, mixes, r):
    section, z, n = place_and_peers()
    chunks = r.full.shape[1]
    r.first_back = 2 * per_core
    stages = [Stage(k, kind, j, per_core, places[k], section, z, n, r)
              for k, (kind, j) in enumerate((kind, j) for kind in kinds for j in range(per_core))]
    ticks = chunks + n - 1
    stages[0].prefetch()
    first = [pltpu.make_async_copy(r.p_in, r.part.at[1], r.first_sem.at[0]),
             pltpu.make_async_copy(r.y_in.at[0], r.full.at[0, :, z, section], r.first_sem.at[1]),
             pltpu.make_async_copy(r.y_in.at[1], r.y_give.at[0], r.first_sem.at[2]),
             pltpu.make_async_copy(r.f_in, r.keep.at[0], r.first_sem.at[3])]
    for copy in first:
        copy.start()
    greet(section, z, n, True, lax.axis_size("batch"))
    for copy in first:
        copy.wait()
    for q in range(chunks):
        stages[0].gather.give(q)
    shares = [Share(r, 0, 0)]
    shares[0].start()
    sums = Sum(section, z, n, r, 1, lambda q: None)
    for k, stage in enumerate(stages):
        gather = stage.gather
        now = None if stage.last else Sum(section, z, n, r, stage.parity, stage.modes.wait)
        mix = None
        if sums is not None:
            mix = Mix(section, z, *mixes[(k + 1) // per_core], sums, stages[k + 1].gather, r)
            share = Share(r, k + 1, 1 - stage.parity)
            if k >= 1:
                shares[k - 1].wait_send()
            shares.append(share)
            mix.prime()
        lead = 0 if k == 0 else chunks - 1
        ready = n - 1 - lead
        gather.begin()
        stage.open()

        def early(i, carry):
            if sums is not None:
                sums.tick(i + lead)
            gather.tick(i)
            stage.before(i)
            if mix is not None and not mix.flip:
                pl.when(within(i - ready, chunks))(lambda: mix.chunk(i - ready))
            return carry

        lax.fori_loop(0, n - 1, early, 0)
        if k > 0:
            stages[k - 1].close()
        if k + 1 < len(stages):
            stages[k + 1].prefetch()
        stage.late()

        def later(q, carry):
            i = q + n - 1
            if sums is not None:
                sums.tick(i + lead)
            if now is not None:
                now.tick(i - n)
            gather.tick(i)
            stage.chunk(q)
            if mix is not None:
                if mix.flip:
                    pl.when(q == 0)(sums.finish)
                    mix.chunk(q)
                else:
                    pl.when(within(i - ready, chunks))(lambda: mix.chunk(i - ready))
            return carry

        lax.fori_loop(0, chunks, later, 0)
        if mix is not None:
            if not mix.flip:
                sums.finish()
            mix.finish()
            share.start()
        stage.end()
        sums = now
    stages[-1].close()
    for share in shares[-2:]:
        share.wait_send()
    for share in shares:
        share.wait_recv()


def swap_halves(value):
    return pltpu.roll(value, value.shape[-1] // 2, value.ndim - 1)


def left_lanes(shape):
    return lax.broadcasted_iota(jnp.int32, shape, len(shape) - 1) < shape[-1] // 2


SLOTS = 4


def weight_stream(own, base, local_ref, far_ref, wbuf, sem):
    step, count = pl.program_id(0), pl.num_programs(0)

    def begin(at):
        slot = lax.rem(at, SLOTS)

        @pl.when(own)
        def _():
            fetch(local_ref.at[0, base + at], wbuf.at[slot], sem.at[slot])

        @pl.when(jnp.logical_not(own))
        def _():
            fetch(far_ref.at[at], wbuf.at[slot], sem.at[slot])

    @pl.when(step == 0)
    def _():
        for at in range(SLOTS - 1):
            @pl.when(at < count)
            def _():
                begin(at)

    @pl.when(step + SLOTS - 1 < count)
    def _():
        begin(step + SLOTS - 1)

    slot = lax.rem(step, SLOTS)
    arrived(wbuf.at[slot], sem.at[slot])
    return wbuf.at[slot]


def pieces(array):
    return [array[at:at + G] for at in range(0, array.shape[0], G)]


def spread_row(ref, row):
    return ref[pl.ds(row, G, stride=0), :]


def mix_kernel(m_ref, f_ref, local_ref, far_ref, y_ref, wbuf, f1, f2, sem):
    weight = weight_stream(m_ref[0] == 1, m_ref[1], local_ref, far_ref, wbuf, sem)
    grids, channels, lanes = f1.shape
    for g in range(grids):
        f1[g] = f_ref[:, g].reshape(channels, lanes)
    f2[...] = swap_halves(f1[...])
    groups = channels // G

    def body(block, acc):
        at = pl.multiple_of(block * G, G)
        acc = list(acc)
        for u in range(G):
            rows = [spread_row(f.at[g], at + u) for g in range(grids) for f in (f1, f2)]
            for o in range(groups):
                w = weight[at + u, o * G:(o + 1) * G, :]
                for k, row in enumerate(rows):
                    acc[k * groups + o] = acc[k * groups + o] + row * w
        return tuple(acc)

    acc = lax.fori_loop(0, groups, body, tuple(jnp.zeros((G, lanes), F32) for _ in range(2 * grids * groups)))
    left = left_lanes((channels, lanes))
    for g in range(grids):
        a, b = [jnp.concatenate(acc[k * groups:(k + 1) * groups], 0) for k in (2 * g, 2 * g + 1)]
        y_ref[g] = jnp.where(left, a - swap_halves(a), b + swap_halves(b)).reshape(y_ref.shape[1:])


def mix_t_kernel(m_ref, d_ref, local_ref, far_ref, y_ref, wbuf, a1, a2, sem):
    weight = weight_stream(m_ref[0] == 1, m_ref[1], local_ref, far_ref, wbuf, sem)
    grids, channels, lanes = a1.shape
    d = [d_ref[:, g].reshape(channels, lanes) for g in range(grids)]
    d1 = [pieces(d[g]) for g in range(grids)]
    d2 = [pieces(swap_halves(d[g])) for g in range(grids)]
    groups = channels // G

    def body(block, carry):
        at = pl.multiple_of(block * G, G)
        rows = [[] for _ in range(2 * grids)]
        for u in range(G):
            total = [None] * (2 * grids)
            for o in range(groups):
                w = weight[at + u, o * G:(o + 1) * G, :]
                for g in range(grids):
                    for side, source in enumerate((d1, d2)):
                        term = w * source[g][o]
                        k = 2 * g + side
                        total[k] = term if total[k] is None else total[k] + term
            for k in range(2 * grids):
                rows[k].append(jnp.sum(total[k], axis=0, keepdims=True))
        for g in range(grids):
            a1[g, pl.ds(at, G), :] = jnp.concatenate(rows[2 * g], 0)
            a2[g, pl.ds(at, G), :] = jnp.concatenate(rows[2 * g + 1], 0)
        return carry

    lax.fori_loop(0, groups, body, 0)
    left = left_lanes((channels, lanes))
    for g in range(grids):
        a, b = a1[g], a2[g]
        y_ref[g] = jnp.where(left, a + swap_halves(a), swap_halves(b) - b).reshape(y_ref.shape[1:])


class Mix:
    def __init__(self, section, z, layer, flip, sums, gather, r):
        self.section, self.z, self.layer, self.flip, self.r = section, z, layer, flip, r
        self.sums, self.gather = sums, gather
        self.chunks, self.grids, self.half, self.count, self.lanes = sums.part.shape[1:]
        self.channels, self.slots = r.weights.shape[2], r.wbuf.shape[0]
        self.blocks = self.chunks * self.half

    def begin(self, block):
        q, x = block // self.half, block % self.half
        slot = lax.rem(block, self.slots)
        rows = pl.ds(q * self.count, self.count)

        @pl.when(self.section == self.layer)
        def _():
            pltpu.make_async_copy(self.r.weights.at[0, self.section * self.half + x, rows], self.r.wbuf.at[slot],
                                  self.r.wsem.at[slot]).start()

        @pl.when(self.section != self.layer)
        def _():
            pltpu.make_async_copy(self.r.far.at[x, rows], self.r.wbuf.at[slot], self.r.wsem.at[slot]).start()

    def prime(self):
        for block in range(min(self.slots, self.blocks)):
            self.begin(jnp.int32(block))
        if not self.flip:
            self.r.macc[...] = jnp.zeros_like(self.r.macc)

    def chunk(self, q):
        def body(x, carry):
            block = q * self.half + x
            slot = lax.rem(block, self.slots)
            weight = self.r.wbuf.at[slot]
            arrived(weight, self.r.wsem.at[slot])
            (self.transposed if self.flip else self.forward)(q, x, weight)

            @pl.when(block + self.slots < self.blocks)
            def _():
                self.begin(block + self.slots)

            return carry

        lax.fori_loop(0, self.half, body, 0)
        if self.flip:
            self.gather.give(q)

    def forward(self, q, x, weight):
        sides, groups = 2 * self.grids, self.channels // G
        total, source = self.r.macc.at[x], self.r.msrc
        for g in range(self.grids):
            value = self.sums.part[self.z, q, g, x]
            source[2 * g, :self.count] = value
            source[2 * g + 1, :self.count] = swap_halves(value)
        keys = [(k, o) for k in range(sides) for o in range(groups)]

        def body(octet, acc):
            acc = dict(zip(keys, acc))
            for u in range(G):
                i = octet * G + u
                rows = [spread_row(source.at[k], i) for k in range(sides)]
                for o in range(groups):
                    w = weight[i, o * G:(o + 1) * G, :]
                    for k in range(sides):
                        acc[k, o] = acc[k, o] + rows[k] * w
            return tuple(acc[key] for key in keys)

        acc = lax.fori_loop(0, self.count // G, body, tuple(total[k, o * G:(o + 1) * G, :] for k, o in keys))
        for key, value in zip(keys, acc):
            total[key[0], key[1] * G:(key[1] + 1) * G, :] = value

    def transposed(self, q, x, weight):
        sides, groups = 2 * self.grids, self.channels // G
        source = self.r.msrc
        for g in range(self.grids):
            value = jnp.concatenate([self.sums.part[self.z, at, g, x] for at in range(self.chunks)], 0)
            source[2 * g] = value
            source[2 * g + 1] = swap_halves(value)
        rows = [pieces(source[k]) for k in range(sides)]
        out = [[] for _ in range(sides)]
        for i in range(self.count):
            total = [None] * sides
            for o in range(groups):
                w = weight[i, o * G:(o + 1) * G, :]
                for k in range(sides):
                    term = w * rows[k][o]
                    total[k] = term if total[k] is None else total[k] + term
            for k in range(sides):
                out[k].append(jnp.sum(total[k], axis=0, keepdims=True))
        left = left_lanes((self.count, self.lanes))
        for g in range(self.grids):
            a, b = [jnp.concatenate(out[2 * g + side], 0) for side in range(2)]
            self.put(g, q, x, jnp.where(left, a + swap_halves(a), swap_halves(b) - b))

    def put(self, g, q, x, value):
        if g == 0:
            self.gather.full[q, self.z, self.section, x] = value
        else:
            self.gather.give_from[q, x] = value

    def finish(self):
        if self.flip:
            return
        left = left_lanes((self.channels, self.lanes))

        def body(x, carry):
            for g in range(self.grids):
                a, b = [self.r.macc[x, 2 * g + side] for side in range(2)]
                result = jnp.where(left, a - swap_halves(a), b + swap_halves(b))
                for q in range(self.chunks):
                    self.put(g, q, x, result[q * self.count:(q + 1) * self.count])
            return carry

        lax.fori_loop(0, self.half, body, 0)
        for q in range(self.chunks):
            self.gather.give(q)


def gather_columns(f_ref, d_ref, left_of, right_of):
    channels = f_ref.shape[2] * f_ref.shape[5]
    lanes = f_ref.shape[6]
    left = left_lanes((channels, lanes))
    for stream in range(f_ref.shape[0]):
        for member in range(f_ref.shape[1]):
            for g in range(f_ref.shape[3]):
                at = (stream * f_ref.shape[1] + member) * f_ref.shape[3] + g
                both = []
                for x in range(2):
                    f = f_ref[stream, member, :, g, x].reshape(channels, lanes)
                    turned = swap_halves(f)
                    left_of[x, at] = jnp.concatenate([f, jnp.where(left, -turned, turned)], 0).T
                    both.append(d_ref[stream, member, :, g, x].reshape(channels, lanes))
                right_of[at] = jnp.concatenate(both, 0).T


def column_products(left_of, right_of, product):
    grids, double, lanes = right_of.shape
    half = double // 2
    left = left_lanes((2 * grids, lanes))
    rows = right_of.reshape(grids * double, lanes)
    sides = [left_of.at[x].reshape(grids * double, lanes) for x in range(2)]

    def body(k, carry):
        pick = pl.ds(k, 2 * grids, stride=half)
        d = rows[pick, :]
        f_high, f_low = split(jnp.concatenate([side[pick, :] for side in sides], 0))
        d_high, d_low = split(jnp.concatenate([jnp.where(left, d, 0.0), jnp.where(left, 0.0, d)], 0))
        product[k] = dot(jnp.concatenate([f_high, f_low, f_high], 0), jnp.concatenate([d_high, d_high, d_low], 0),
                         (((0,), (0,)), ((), ())))
        return carry

    lax.fori_loop(0, half, body, 0, unroll=4)


def product_rows(product, first, out):
    half, double, lanes = product.shape
    channels = double // 2
    rows = product.reshape(half * double, lanes)

    def body(i, carry):
        parts = [rows[pl.ds(part * channels + first + i, half, stride=double), :] for part in range(2)]
        tile = jnp.concatenate(parts, 0).T
        for x in range(2):
            out[x, i] = tile[x * channels:(x + 1) * channels]
        return carry

    lax.fori_loop(0, out.shape[1], body, 0, unroll=4)


class GradInput:
    def __init__(self, first, f, g, fbuf, gbuf, sem):
        self.first, self.f, self.g, self.fbuf, self.gbuf, self.sem = first, f, g, fbuf, gbuf, sem

    def load(self, x, slot):
        for layer, condition in enumerate((self.first, jnp.logical_not(self.first))):
            @pl.when(condition)
            def _():
                for j in range(len(self.f[layer])):
                    pltpu.make_async_copy(self.f[layer][j].at[:, :, :, pl.ds(2 * x, 2)], self.fbuf.at[slot, j],
                                          self.sem.at[0, slot]).start()
                    pltpu.make_async_copy(self.g[layer][j].at[:, :, :, pl.ds(2 * x, 2)], self.gbuf.at[slot, j],
                                          self.sem.at[1, slot]).start()

    def next(self, x, count):
        slot = lax.rem(x, 2)

        @pl.when(x + 1 < count)
        def _():
            self.load(x + 1, 1 - slot)

        arrived(self.fbuf.at[slot], self.sem.at[0, slot])
        arrived(self.gbuf.at[slot], self.sem.at[1, slot])
        return self.fbuf.at[slot], self.gbuf.at[slot]


def grad_input(r, first, per_core):
    f = [[getattr(r, f"f{layer}{j}") for j in range(per_core)] for layer in range(2)]
    g = [[getattr(r, f"g{layer}{j}") for j in range(per_core)] for layer in range(2)]
    return GradInput(first, f, g, r.fbuf, r.gbuf, r.in_sem)


def far_grad_kernel(per_core, r):
    section, z, n = place_and_peers()
    pairs, block = r.far.shape[0] // 2, r.out.shape[2]
    blocks = r.far.shape[1] // block
    source = grad_input(r, section != 0, per_core)

    def move(k, slot):
        p, i = k // blocks, k % blocks
        return to_core(r.out.at[slot], r.far.at[pl.ds(2 * p, 2), pl.ds(i * block, block)], (r.send.at[k], r.recv.at[k]),
                       section)

    source.load(0, 0)
    greet(section, z, n, False)

    def body(p, carry):
        gather_columns(*source.next(p, pairs), r.left_of, r.right_of)
        column_products(r.left_of, r.right_of, r.product)

        def inner(i, carry):
            k = p * blocks + i

            @pl.when(k >= 2)
            def _():
                move(k - 2, lax.rem(k, 2)).wait_send()

            product_rows(r.product, i * block, r.out.at[lax.rem(k, 2)])
            move(k, lax.rem(k, 2)).start()
            return carry

        return lax.fori_loop(0, blocks, inner, carry)

    lax.fori_loop(0, pairs, body, 0)
    total = pairs * blocks
    for k in (total - 2, total - 1):
        move(k, k % 2).wait_send()

    def close(k, carry):
        move(k, 0).wait_recv()
        return carry

    lax.fori_loop(0, total, close, 0)


def own_grad_kernel(names, per_core, m_ref, *refs):
    r = types.SimpleNamespace(**dict(zip(names, refs)))
    p, i = pl.program_id(0), pl.program_id(1)
    source = grad_input(r, m_ref[0] == 0, per_core)

    @pl.when(i == 0)
    def _():
        @pl.when(p == 0)
        def _():
            source.load(0, 0)

        gather_columns(*source.next(p, pl.num_programs(0)), r.left_of, r.right_of)
        column_products(r.left_of, r.right_of, r.product)

    r.bound_out[...] = r.bound_in[...]
    r.out[1 - m_ref[0]] = r.far[...]
    product_rows(r.product, i * r.out.shape[2], r.out.at[m_ref[0]])


def whole(array):
    return pl.BlockSpec(array.shape, lambda *_: (0,) * array.ndim)


def params(**kw):
    return pltpu.CompilerParams(vmem_limit_bytes=VMEM_LIMIT, **kw)


def local(inputs, cotangent, region_id, spectral_w, conv_w, bias_vector):
    micro_count, _, rows_dev, channels, width = inputs.shape
    lanes = spectral_w.shape[-1]
    half = lanes // 2
    kx_dev = spectral_w.shape[1]
    row_devices, sections = lax.axis_size("rows"), lax.axis_size("section")
    mode_rows, height = kx_dev * row_devices, rows_dev * row_devices
    section = lax.axis_index("section")
    per_core = micro_count // sections
    kx_half = kx_dev // sections

    plain, doubled = col_tables(width, half)

    def stacked(array):
        high, low = np_split(array)
        return np.concatenate([high, high, low], 0)

    t_plain, t_doubled, it_plain, it_doubled = [stacked(t) for t in (plain, doubled, plain.T, doubled.T)]
    kron, ikron = row_tables(height, mode_rows, lax.axis_index("rows") * rows_dev, rows_dev)

    count = 2 * G
    chunks = channels // count
    hbm, vmem = pl.BlockSpec(memory_space=pl.ANY), pl.BlockSpec(memory_space=pltpu.VMEM)
    field_shape = jax.ShapeDtypeStruct((rows_dev, channels, width), F32)
    part_dims = (row_devices, chunks, sections, kx_half, count, lanes)
    p_shape, f_shape = jax.ShapeDtypeStruct(part_dims, F32), jax.ShapeDtypeStruct(part_dims[1:], F32)
    y_shape = jax.ShapeDtypeStruct((sections, chunks, kx_half, count, lanes), F32)
    stat_shape = jax.ShapeDtypeStruct((3, R, 128), F32)
    cg_shape = jax.ShapeDtypeStruct((2 * channels, 2 * channels), F32)
    bg_shape = jax.ShapeDtypeStruct((channels, width), F32)
    bound_shape = jax.ShapeDtypeStruct((micro_count, rows_dev, channels, width), F32)
    dma = pltpu.SemaphoreType.DMA
    field_buf = pltpu.VMEM((rows_dev, channels, width), F32)
    full_dims = (chunks, row_devices, sections, kx_half, count, lanes)
    spread = pltpu.VMEM((width // 128, rows_dev * count, 128), F32)
    energy = pltpu.VMEM((rows_dev, G, width), F32)
    line_sems = dma((2, chunks, row_devices))
    start_scratch = dict(part=pltpu.VMEM(part_dims, F32), come=pltpu.VMEM((2, chunks, row_devices) + part_dims[2:], F32),
                         f_sem=dma((chunks,)), red_send=line_sems, red_recv=line_sems)

    def run(body, ident, ins, outs, scratch, cost=50, aliases=None):
        names = [*ins, *outs, *scratch]
        spec = lambda entry: vmem if isinstance(entry, tuple) else hbm
        plain = lambda entry: entry[0] if isinstance(entry, tuple) else entry
        kernel = lambda *refs: body(types.SimpleNamespace(**dict(zip(names, refs))))
        positions = {list(ins).index(k): list(outs).index(v) for k, v in (aliases or {}).items()}
        result = pl.pallas_call(
            kernel, in_specs=[spec(e) for e in ins.values()], out_specs=[spec(e) for e in outs.values()],
            out_shape=[plain(e) for e in outs.values()], scratch_shapes=list(scratch.values()),
            input_output_aliases=positions,
            cost_estimate=pl.CostEstimate(flops=0, bytes_accessed=cost * 3_000_000, transcendentals=0),
            compiler_params=params(collective_id=ident, has_side_effects=True))(*[plain(e) for e in ins.values()])
        return types.SimpleNamespace(**dict(zip(outs, result)))

    conv_rows_at_once = 256 // channels
    conv_both = lax.all_gather(conv_w, "section", axis=0, tiled=True)
    bias_both = lax.all_gather(bias_vector, "section", axis=0, tiled=True)

    def conv_parts(matrix):
        wide = jnp.kron(jnp.eye(conv_rows_at_once, dtype=F32), matrix)
        rounded = lax.reduce_precision(wide, 8, 7)
        high, low = rounded.astype(BF16), (wide - rounded).astype(BF16)
        return jnp.concatenate([high, low, high], 1)

    conv_fwd = [conv_parts(conv_both[l].T) for l in range(2)]
    conv_bwd = [conv_parts(conv_both[l]) for l in range(2)]
    bias_wide = [jnp.broadcast_to(bias_both[l][:, None], (channels, width)) for l in range(2)]

    def mixing(body, layer, pair):
        flag = jnp.stack([(section == layer).astype(jnp.int32), section * kx_half])
        f_block = pl.BlockSpec((chunks, sections, None, count, lanes), lambda x, m: (0, 0, x, 0, 0))
        y_block = pl.BlockSpec((sections, chunks, None, count, lanes), lambda x, m: (0, 0, x, 0, 0))
        small = pltpu.VMEM((sections, channels, lanes), F32)
        grid_spec = pltpu.PrefetchScalarGridSpec(
            num_scalar_prefetch=1, grid=(kx_half,), in_specs=[f_block, hbm, hbm], out_specs=y_block,
            scratch_shapes=[pltpu.VMEM((SLOTS, channels, channels, lanes), F32), small, small, dma((SLOTS,))])
        return pl.pallas_call(
            body, grid_spec=grid_spec, out_shape=y_shape, compiler_params=params(),
            cost_estimate=pl.CostEstimate(flops=0, bytes_accessed=30_000_000, transcendentals=0))(
                flag, pair, spectral_w, far_weights)

    streams = range(per_core)
    start = run(
        functools.partial(start_kernel, per_core), 0,
        dict(inputs=inputs, weights=spectral_w, table=(t_plain,), kron=(kron,)),
        dict(f_out=f_shape, far=jax.ShapeDtypeStruct((kx_half,) + spectral_w.shape[2:], F32),
             **{f"p{j}": p_shape for j in streams[1:]}),
        dict(a_buf=pltpu.VMEM((2, rows_dev, count, width), F32), w_buf=pltpu.VMEM((2,) + spectral_w.shape[2:], F32),
             p_buf=pltpu.VMEM((per_core,) + full_dims, F32), spread=spread, a_sem=dma((2,)), w_sem=dma((2,)),
             w_cross=dma((2, kx_half)), p_local=dma((per_core, chunks)), p_cross=dma((per_core, 2, chunks)),
             **start_scratch))
    far_weights = start.far

    members = lax.axis_size("batch")
    kinds = ["middle", "turn", "back", "tail"]
    mixes = [(0, False), (1, False), (1, True), (0, True)]
    names = ["f00", "f01", "f10", "f11", "g10", "g11", "g00", "g01"]
    places = [dict(a=0, z=1), dict(a=2, z=3), dict(a=4, z=5, cot=6), dict(a=0, z=1, cot=2),
              dict(gz=3, a=4, h=5, dg=6), dict(gz=0, a=1, h=2, dg=3), dict(gz=4, a=5, h=6), dict(gz=0, a=1, h=2)]
    y = mixing(mix_kernel, 0, start.f_out)
    both = (2,)
    ins = dict(inputs=inputs, cotangent=cotangent, region=region_id, weights=spectral_w, far=far_weights,
               p_in=start.p1, f_in=start.f_out, y_in=y, t_plain=(t_plain,), t_doubled=(t_doubled,), it_plain=(it_plain,),
               it_doubled=(it_doubled,), kron=(kron,), ikron=(ikron,),
               **{f"conv_f{l}": (conv_fwd[l],) for l in range(2)}, **{f"conv_b{l}": (conv_bwd[l],) for l in range(2)},
               **{f"bias{l}": (bias_wide[l],) for l in range(2)})
    outs = dict(bound=bound_shape, stat=(jax.ShapeDtypeStruct((2 * per_core,) + stat_shape.shape, F32),),
                cg=(jax.ShapeDtypeStruct((2 * per_core,) + cg_shape.shape, F32),),
                bg=(jax.ShapeDtypeStruct((2 * per_core,) + bg_shape.shape, F32),),
                **{f"{name}{j}": field_shape for name in ("a1_", "dg0_", "gz1_", "ga1_", "gz0_") for j in streams},
                **{f"shared{i}": jax.ShapeDtypeStruct((members,) + f_shape.shape, F32) for i in range(len(names))})
    scratch = dict(
        fields=pltpu.VMEM((7,) + field_shape.shape, F32), full=pltpu.VMEM(both + full_dims, F32),
        part=pltpu.VMEM(both + part_dims, F32),
        come=pltpu.VMEM(both + (2, chunks, row_devices - 1) + part_dims[2:], F32),
        keep=pltpu.VMEM(both + f_shape.shape, F32), y_give=pltpu.VMEM(both + y_shape.shape[1:], F32),
        p_buf=pltpu.VMEM(full_dims, F32), spread=spread, eo=energy, eb=energy,
        rid=pltpu.VMEM((2, rows_dev, width), jnp.int32),
        wbuf=pltpu.VMEM((6, count, channels, lanes), F32), macc=pltpu.VMEM((kx_half, 2 * sections, channels, lanes), F32),
        msrc=pltpu.VMEM((2 * sections, channels, lanes), F32),
        field_sem=dma((7,)), rid_sem=dma(both), out_sem=dma((2, 2, chunks)), wsem=dma((6,)), first_sem=dma((4,)),
        send=dma(both + (2, chunks, row_devices)), recv=dma(both + (2, chunks, row_devices)),
        red_send=dma(both + (2, chunks, row_devices)), red_recv=dma(both + (2, chunks, row_devices)),
        y_cross=dma((2, 2, chunks)), p_local=dma((chunks,)), p_cross=dma((2, 2, chunks)),
        b_local=dma((2, chunks)), b_cross=dma((2, 2, chunks)),
        s_local=dma(both), s_send=dma((2, members)), s_recv=dma((len(names), members)))
    done = run(functools.partial(stages_kernel, per_core, kinds, places, mixes), 1, ins, outs, scratch, cost=400)
    gathered = {name: getattr(done, f"shared{i}") for i, name in enumerate(names)}
    bound, calls = done.bound, 1

    grids = per_core * members * sections
    block = 2 * G
    pairs, blocks = kx_half // 2, channels // block
    in_buf = pltpu.VMEM((2, per_core, members, chunks, sections, 2, count, lanes), F32)
    grad_scratch = dict(fbuf=in_buf, gbuf=in_buf, in_sem=dma((2, 2)), left_of=pltpu.VMEM((2, grids, lanes, lanes), F32),
                        right_of=pltpu.VMEM((grids, lanes, lanes), F32), product=pltpu.VMEM((half, lanes, lanes), F32))
    far_grad = run(functools.partial(far_grad_kernel, per_core), 1 + calls, gathered,
                   dict(far=jax.ShapeDtypeStruct((kx_half, channels, channels, lanes), F32)),
                   dict(out=pltpu.VMEM((2, 2, block, channels, lanes), F32), send=dma((pairs * blocks,)),
                        recv=dma((pairs * blocks,)), **grad_scratch)).far
    bound_rows = bound.reshape(micro_count * rows_dev, channels, width)
    bound_block = pl.BlockSpec((bound_rows.shape[0] // (pairs * blocks), channels, width),
                               lambda p, i, m: (p * blocks + i, 0, 0))
    grid_spec = pltpu.PrefetchScalarGridSpec(
        num_scalar_prefetch=1, grid=(pairs, blocks),
        in_specs=[hbm] * len(gathered)
        + [pl.BlockSpec((2, block, channels, lanes), lambda p, i, m: (p, i, 0, 0)), bound_block],
        out_specs=[pl.BlockSpec((2, 2, block, channels, lanes), lambda p, i, m: (0, p, i, 0, 0)), bound_block],
        scratch_shapes=list(grad_scratch.values()))
    spectral_grad, boundary = pl.pallas_call(
        functools.partial(own_grad_kernel, [*gathered, "far", "bound_in", "out", "bound_out", *grad_scratch], per_core),
        grid_spec=grid_spec, out_shape=[jax.ShapeDtypeStruct((2, kx_half, channels, channels, lanes), F32),
                                        jax.ShapeDtypeStruct(bound_rows.shape, F32)],
        cost_estimate=pl.CostEstimate(flops=0, bytes_accessed=150_000_000, transcendentals=0),
        compiler_params=params())(
            jnp.reshape(section, (1,)).astype(jnp.int32), *gathered.values(), far_grad, bound_rows)
    spectral_grad = spectral_grad.reshape(spectral_w.shape)
    boundary = boundary.reshape((1, micro_count, 1) + inputs.shape[2:])

    def lower(value):
        return (value[:channels, :channels] + value[channels:, channels:]
                + value[:channels, channels:] + value[channels:, :channels])

    pair = lambda value: jnp.sum(value.reshape((2, per_core) + value.shape[1:]), 1)
    conv_local = jnp.stack([lower(value) for value in pair(done.cg)[::-1]])
    bias_local = jnp.sum(pair(done.bg)[::-1], -1)
    stat_local = jnp.sum(pair(done.stat), -1)
    shapes = [v.shape for v in (conv_local, bias_local, stat_local)]
    flat_sums = jnp.concatenate([v.reshape(-1) for v in (conv_local, bias_local, stat_local)])
    length = flat_sums.shape[0]
    flat_sums = jnp.pad(flat_sums, (0, -length % 1024)).reshape(-1, 128)
    flat_sums = jnp.sum(lax.all_gather(flat_sums, ("section", "batch", "rows"), axis=0), 0).reshape(-1)
    ends = np.cumsum([0] + [math.prod(shape) for shape in shapes])
    conv_sum, bias_sum, stat_sum = [flat_sums[ends[i]:ends[i + 1]].reshape(shapes[i]) for i in range(3)]
    own_stat = lax.dynamic_index_in_dim(stat_sum, section, 0, False)
    layer_rms = jnp.sqrt(own_stat[:2] / (channels * own_stat[2])[None, :] + 1e-06)[None]
    own = lambda value: lax.dynamic_slice_in_dim(value, section, 1, 0)
    return boundary, spectral_grad, own(conv_sum), own(bias_sum), layer_rms


def solution(mesh):
    placed = (
        P(None, "batch", "rows", None, None),
        P(None, "batch", "rows", None, None),
        P(None, "batch", "rows", None),
        P("section", "rows", None, None, None),
        P("section", None, None),
        P("section", None),
    )
    return jax.shard_map(
        local,
        mesh=mesh,
        in_specs=placed,
        out_specs=(
            P("section", None, "batch", "rows", None, None),
            P("section", "rows", None, None, None),
            P("section", None, None),
            P("section", None),
            P("section", None, None),
        ),
        check_vma=False,
    )
```

```python
import functools
import math
import types

import jax
import jax.numpy as jnp
import numpy as np
from jax import lax
from jax.experimental import pallas as pl
from jax.experimental.pallas import tpu as pltpu
from jax.sharding import PartitionSpec as P

R = 8
G = 8
AHEAD = 2
F32 = jnp.float32
BF16 = jnp.bfloat16
VMEM_LIMIT = 62 * 1024 * 1024
MESH = pl.DeviceIdType.MESH


def split(value):
    high = value.astype(BF16)
    return high, (value - high.astype(F32)).astype(BF16)


def dot(left, right, dims=(((1,), (0,)), ((), ()))):
    return lax.dot_general(left, right, dims, preferred_element_type=F32)


def dot3(left, right):
    return dot(left[0], right[0]) + (dot(left[1], right[0]) + dot(left[0], right[1]))


def np_split(value):
    high = value.astype(np.float32).astype(BF16)
    return high, (value - high.astype(np.float64)).astype(np.float32).astype(BF16)


def col_tables(width, half):
    phase = 2.0 * math.pi / width * (np.outer(np.arange(width), np.arange(half)) % width)
    cosine, sine = np.cos(phase) / math.sqrt(width), np.sin(phase) / math.sqrt(width)
    plain = np.concatenate([cosine, -sine, -sine, -cosine], 1)
    doubled = plain * np.tile(np.where(np.arange(half) == 0, 1.0, 2.0), 4)[None, :]
    return plain, doubled


def row_tables(height, mode_rows, first_row, rows_dev):
    position = jnp.arange(mode_rows, dtype=jnp.int32)
    frequency = jnp.where(position < mode_rows // 2, position, height - mode_rows + position)
    row = first_row + jnp.arange(rows_dev, dtype=jnp.int32)
    phase = 2.0 * math.pi / height * (frequency[:, None] * row[None, :] % height).astype(F32)
    small = jnp.concatenate([jnp.cos(phase), jnp.sin(phase)], 1) / math.sqrt(height)
    rounded = lax.reduce_precision(small, 8, 7)
    high, low = rounded.astype(BF16), (small - rounded).astype(BF16)
    forward = jnp.concatenate([jnp.concatenate([high, high], 1), jnp.concatenate([low, jnp.zeros_like(low)], 1)], 0)
    inverse = jnp.concatenate([high.T, high.T, low.T], 1)
    return forward, inverse


def to_modes(value, table, kron, spread, p_ref):
    mode_rows, count, lanes = p_ref.shape
    rows = value.shape[0] // count
    high, low = split(value)
    spectra = dot(jnp.concatenate([high, low, high], 1), table)
    for i in range(2):
        spread[i] = spectra[:, i * lanes:(i + 1) * lanes]
    out = p_ref.reshape(mode_rows * count, lanes)
    for first in range(0, count, 2):
        sides = []
        for c in (first, first + 1):
            pick = pl.ds(c, rows, stride=count)
            sides.append(jnp.concatenate([spread[i, pick, :] for i in range(2)], 0))
        high, low = split(jnp.concatenate(sides, 1))
        both = dot(kron, jnp.concatenate([high, low], 0))
        result = both[:mode_rows] + both[mode_rows:]
        for i in range(2):
            out[pl.ds(first + i, mode_rows, stride=count), :] = result[:, i * lanes:(i + 1) * lanes]


def from_modes(y_ref, table, kron, spread):
    mode_rows, count, lanes = y_ref.shape
    rows, pieces = spread.shape[1] // count, spread.shape[0]
    modes = y_ref.reshape(mode_rows * count, lanes)
    sides = []
    for first in range(0, count, 2):
        pair = [modes[pl.ds(c, mode_rows, stride=count), :] for c in (first, first + 1)]
        high, low = split(jnp.concatenate(pair, 1))
        both = dot(kron, jnp.concatenate([high, low, high], 0))
        for i in range(2):
            side = both[:, i * lanes:(i + 1) * lanes]
            sides.append(jnp.concatenate([side[:rows], side[rows:]], 1))
    high, low = split(jnp.concatenate(sides, 0))
    out = dot(jnp.concatenate([high, low, high], 1), table)
    for c in range(count):
        for i in range(pieces):
            spread[i, pl.ds(c, rows, stride=count), :] = out[c * rows:(c + 1) * rows, i * 128:(i + 1) * 128]
    return jnp.concatenate([spread[i] for i in range(pieces)], 1)


def gelu_parts(z):
    size = jnp.abs(z)
    gauss = jnp.exp(-0.5 * z * z)
    base = 1.0 + (0.3275911 / math.sqrt(2.0)) * size
    t = pl.reciprocal(base, approx=True)
    t = t * (2.0 - base * t)
    poly = t * (0.254829592 + t * (-0.284496736 + t * (1.421413741 + t * (-1.453152027 + t * 1.061405429))))
    tail = 0.5 * poly * gauss
    phi = jnp.where(z >= 0, 1.0 - tail, tail)
    return z * phi, phi + z * (gauss * (1.0 / math.sqrt(2.0 * math.pi)))


def flat(ref):
    rows, count, width = ref.shape
    return ref[...].reshape(rows * count, width)


def put(ref, value):
    ref[...] = value.reshape(ref.shape)


def place_and_peers():
    section, z = lax.axis_index("section"), lax.axis_index("rows")
    return section, z, lax.axis_size("rows")


def greet(section, z, n, lines, members=0):
    barrier = pltpu.get_barrier_semaphore()
    pl.semaphore_signal(barrier, inc=1, device_id={"section": 1 - section}, device_id_type=MESH)
    if not lines:
        pl.semaphore_wait(barrier, 1)
        return

    @pl.when(z > 0)
    def _():
        pl.semaphore_signal(barrier, inc=1, device_id={"rows": z - 1}, device_id_type=MESH)

    @pl.when(z < n - 1)
    def _():
        pl.semaphore_signal(barrier, inc=1, device_id={"rows": z + 1}, device_id_type=MESH)

    for away in range(1, members):
        pl.semaphore_signal(barrier, inc=1, device_id={"batch": lax.rem(lax.axis_index("batch") + away, members)},
                            device_id_type=MESH)

    others = 1 + max(members - 1, 0)
    pl.semaphore_wait(barrier, others + (z > 0).astype(jnp.int32) + (z < n - 1).astype(jnp.int32))


def to_core(src, dst, sems, section):
    return pltpu.make_async_remote_copy(src_ref=src, dst_ref=dst, send_sem=sems[0], recv_sem=sems[1],
                                        device_id={"section": 1 - section}, device_id_type=MESH)


def guard(condition, body):
    if isinstance(condition, (bool, np.bool_)):
        if condition:
            body()
    else:
        pl.when(condition)(body)


class Line:
    def __init__(self, section, z, n, chunks, send, recv):
        self.section, self.z, self.n, self.chunks = section, z, n, chunks
        self.send, self.recv = send, recv

    def move(self, way, q, hop, src, dst):
        return pltpu.make_async_remote_copy(
            src_ref=src, dst_ref=dst, send_sem=self.send.at[way, q, hop], recv_sem=self.recv.at[way, q, hop],
            device_id={"rows": self.z + 1 if way == 0 else self.z - 1}, device_id_type=MESH)

    def sends(self, way):
        return self.z < self.n - 1 if way == 0 else self.z > 0

    def hears(self, way):
        return self.z > 0 if way == 0 else self.z < self.n - 1


def within(value, count):
    if isinstance(value, int):
        return 0 <= value < count
    return jnp.logical_and(value >= 0, value < count)


class Gather(Line):
    def __init__(self, section, z, n, r, parity):
        super().__init__(section, z, n, r.full.shape[1], r.send.at[parity], r.recv.at[parity])
        self.full, self.give_from = r.full.at[parity], r.y_give.at[parity]
        self.cross = r.y_cross.at[parity]

    def swap(self, q):
        return to_core(self.give_from.at[q], self.full.at[q, self.z, self.section],
                       (self.cross.at[0, q], self.cross.at[1, q]), self.section)

    def give(self, q):
        self.swap(q).start()

    def hop(self, way, q, hop):
        piece = self.full.at[q, self.source(way, hop)]
        return self.move(way, q, hop, piece, piece)

    def source(self, way, hop):
        return self.z - hop if way == 0 else self.z + hop

    def known(self, way, hop):
        at = self.source(way, hop)
        return at >= 0 if way == 0 else at < self.n

    def own(self, q):
        self.swap(q).wait_recv()
        for way in range(2):
            @pl.when(self.sends(way))
            def _():
                self.hop(way, q, 0).start()

    def step(self, q, hop):
        for way in range(2):
            @pl.when(self.known(way, hop + 1))
            def _():
                piece = self.full.at[q, self.source(way, hop + 1)]
                self.move(way, q, hop, piece, piece).wait_recv()

                @pl.when(self.sends(way))
                def _():
                    self.hop(way, q, hop + 1).start()

    def poll(self, i, second):
        if second:
            def begin():
                for q in range(min(2, self.chunks)):
                    self.own(q)

            guard(i == 0, begin)
            guard(within(i - 1, self.chunks - 2), lambda: self.own(i + 1))
        for hop in range(self.n - 1):
            if hop % 2 == second:
                q = i - 1 + (second - hop) // 2
                guard(within(q, self.chunks), functools.partial(self.step, q, hop))

    def finish(self):
        def body(q, carry):
            self.swap(q).wait_send()
            for way in range(2):
                for hop in range(self.n - 1):
                    @pl.when(jnp.logical_and(self.sends(way), self.known(way, hop)))
                    def _():
                        self.hop(way, q, hop).wait_send()
            return carry

        lax.fori_loop(0, self.chunks, body, 0)


class Sum(Line):
    def __init__(self, section, z, n, r, parity, admit):
        super().__init__(section, z, n, r.part.shape[2], r.red_send.at[parity], r.red_recv.at[parity])
        self.part, self.come, self.keep, self.admit = r.part.at[parity], r.come.at[parity], r.keep.at[parity], admit

    def owner(self, way, hop):
        return self.z + self.n - hop if way == 0 else self.z - self.n + hop

    def valid(self, way, hop):
        return self.z <= hop - 1 if way == 0 else self.z >= self.n - hop

    def sent(self, way, q, hop):
        return self.move(way, q, hop, self.part.at[self.owner(way, hop), q], self.come.at[way, q, hop - 1])

    def heard(self, way, q, hop):
        come = self.come.at[way, q, hop - 1]
        self.move(way, q, hop, come, come).wait_recv()

    def first(self, q):
        self.admit(q)
        for way in range(2):
            @pl.when(jnp.logical_not(self.hears(way)))
            def _():
                for hop in range(1, self.n):
                    @pl.when(self.valid(way, hop))
                    def _():
                        self.sent(way, q, hop).start()

    def step(self, q, hop):
        for way in range(2):
            @pl.when(jnp.logical_and(self.valid(way, hop), self.hears(way)))
            def _():
                self.heard(way, q, hop - 1)
                owner = self.owner(way, hop)
                self.part[owner, q] = self.part[owner, q] + self.come[way, q, hop - 2]
                self.sent(way, q, hop).start()

    def final(self, q):
        for way in range(2):
            @pl.when(self.hears(way))
            def _():
                self.heard(way, q, self.n - 1)
                self.part[self.z, q] = self.part[self.z, q] + self.come[way, q, self.n - 2]

        self.keep[q] = self.part[self.z, q]

    def poll(self, i, second):
        if not second:
            guard(within(i, self.chunks), functools.partial(self.first, i))
        for hop in range(2, self.n + 1):
            if (hop + 1) % 2 == second:
                q = i + (second - hop + 1) // 2
                guard(within(q, self.chunks),
                      functools.partial(self.step, q, hop) if hop < self.n else functools.partial(self.final, q))

    def finish(self):
        def body(q, carry):
            for way in range(2):
                for hop in range(1, self.n):
                    @pl.when(self.valid(way, hop))
                    def _():
                        self.sent(way, q, hop).wait_send()
            return carry

        lax.fori_loop(0, self.chunks, body, 0)


class Reduce(Line):
    def __init__(self, section, z, n, part, come, f_out, f_sem, send, recv, ahead):
        super().__init__(section, z, n, part.shape[1], send, recv)
        self.ahead = ahead
        self.part, self.come, self.f_out, self.f_sem = part, come, f_out, f_sem

    def owner(self, way, hop):
        return self.z + self.n - hop if way == 0 else self.z - self.n + hop

    def valid(self, way, hop):
        return self.z <= hop - 1 if way == 0 else self.z >= self.n - hop

    def sent(self, way, q, hop):
        return self.move(way, q, hop, self.part.at[self.owner(way, hop), q], self.come.at[way, q, hop])

    def heard(self, way, q, hop):
        come = self.come.at[way, q, hop]
        self.move(way, q, hop, come, come).wait_recv()

    def first(self, t):
        for hop in range(1, self.n):
            q = t - hop + 1

            def send():
                for way in range(2):
                    @pl.when(jnp.logical_and(self.valid(way, hop), jnp.logical_not(self.hears(way))))
                    def _():
                        self.sent(way, q, hop).start()

            guard(0 <= q < self.chunks if isinstance(q, int) else q < self.chunks, send)

    def step(self, q, hop):
        for way in range(2):
            @pl.when(jnp.logical_and(self.valid(way, hop), self.hears(way)))
            def _():
                self.heard(way, q, hop - 1)
                owner = self.owner(way, hop)
                self.part[owner, q] = self.part[owner, q] + self.come[way, q, hop - 1]
                self.sent(way, q, hop).start()

    def result(self, q):
        return pltpu.make_async_copy(self.part.at[self.z, q], self.f_out.at[q], self.f_sem.at[q])

    def final(self, q):
        for way in range(2):
            @pl.when(self.hears(way))
            def _():
                self.heard(way, q, self.n - 1)
                self.part[self.z, q] = self.part[self.z, q] + self.come[way, q, self.n - 1]

        self.result(q).start()

    def tick(self, t):
        if isinstance(t, int) and t == 0:
            for early in range(self.ahead):
                self.first(early)
        self.first(t + self.ahead)
        for hop in range(2, self.n + 1):
            q = t - hop + 1
            if isinstance(q, int):
                valid = 0 <= q < self.chunks
            else:
                valid = q < self.chunks
            guard(valid, functools.partial(self.step, q, hop) if hop < self.n else functools.partial(self.final, q))

    def finish(self):
        def body(q, carry):
            self.result(q).wait()
            for way in range(2):
                for hop in range(1, self.n):
                    @pl.when(self.valid(way, hop))
                    def _():
                        self.sent(way, q, hop).wait_send()
            return carry

        lax.fori_loop(0, self.chunks, body, 0)


def fetch(src, dst, sem, parts=4):
    step = dst.shape[0] // parts
    for i in range(parts):
        pltpu.make_async_copy(src.at[pl.ds(i * step, step)], dst.at[pl.ds(i * step, step)], sem).start()


def arrived(dst, sem):
    pltpu.make_async_copy(dst, dst, sem).wait()


def portions(total, count):
    return [(i * total // count, (i + 1) * total // count) for i in range(count)]


def conv_rows(weight, bias, a, out, first, last):
    channels, width = a.shape[1:]
    block = weight.shape[0] // channels

    def body(i, carry):
        at = pl.ds(i * block, block)
        high, low = split(a[at].reshape(block * channels, width))
        result = dot(weight[...], jnp.concatenate([high, high, low], 0)).reshape(block, channels, width)
        out[at] = result + bias[...][None] if bias is not None else out[at] + result
        return carry

    lax.fori_loop(first, last, body, 0)


def grad_rows(a, gz, cg_ref, bg_ref, first, last):
    channels, width = a.shape[1:]

    def body(r, carry):
        grad, bias = carry
        g = gz[r]
        left = jnp.concatenate(split(a[r]), 0)
        right = jnp.concatenate(split(g), 0)
        return grad + dot(left, right, (((1,), (1,)), ((), ()))), bias + g

    grad, bias = lax.fori_loop(first, last, body, (cg_ref[...], bg_ref[...]))
    cg_ref[...] = grad
    bg_ref[...] = bias


def chunk_of(ref, q, count):
    rows, _, width = ref.shape
    return ref[:, pl.ds(pl.multiple_of(q * count, count), count), :].reshape(rows * count, width)


def chunk_at(ref, q, count):
    return ref.at[:, pl.ds(pl.multiple_of(q * count, count), count), :]


class Modes:
    def __init__(self, section, buffer, p_out, local, cross):
        self.section, self.buffer, self.p_out, self.local, self.cross = section, buffer, p_out, local, cross

    def view(self, q):
        n, halves, kx, count, lanes = self.buffer.shape[1:]
        return self.buffer.at[q].reshape(n * halves * kx, count, lanes)

    def copies(self, q):
        s = self.section
        return (pltpu.make_async_copy(self.buffer.at[q, :, s], self.p_out.at[:, q, 0], self.local.at[q]),
                to_core(self.buffer.at[q, :, 1 - s], self.p_out.at[:, q, 1],
                        (self.cross.at[0, q], self.cross.at[1, q]), s))

    def start(self, q):
        for copy in self.copies(q):
            copy.start()

    def wait(self, q):
        for copy in self.copies(q):
            copy.wait()


class Bound:
    def __init__(self, section, owner, micro, other, source, bound, local, cross):
        self.section, self.owner, self.micro, self.other = section, owner, micro, other
        self.source, self.bound, self.local, self.cross = source, bound, local, cross

    def copies(self, q, count, micro):
        src, dst = chunk_at(self.source, q, count), chunk_at(self.bound.at[micro], q, count)
        return (pltpu.make_async_copy(src, dst, self.local.at[q]),
                to_core(src, dst, (self.cross.at[0, q], self.cross.at[1, q]), self.section))

    def start(self, q, count):
        here, there = self.copies(q, count, self.micro)

        @pl.when(self.section == self.owner)
        def _():
            here.start()

        @pl.when(self.section != self.owner)
        def _():
            there.start()

    def wait(self, q, count):
        here, there = self.copies(q, count, self.micro)
        come = self.copies(q, count, self.other)[1]

        @pl.when(self.section == self.owner)
        def _():
            here.wait()
            come.wait_recv()

        @pl.when(self.section != self.owner)
        def _():
            there.wait_send()


def add_squares(value, total):
    rows, _, width = total.shape
    square = (value * value).reshape(rows, -1, width)
    for at in range(0, square.shape[1], G):
        total[...] += square[:, at:at + G]


def region_sums(rid_ref, eo, eb, stat_ref):
    rows, _, width = eo.shape
    rid = rid_ref[...]
    energies = (jnp.sum(eo[...], axis=1), jnp.sum(eb[...], axis=1), jnp.ones((rows, width), F32))
    for kind in range(3):
        for region in range(R):
            line = jnp.sum(jnp.where(rid == region + 1, energies[kind], 0.0), axis=0, keepdims=True)
            total = line[:, :128]
            for piece in range(1, width // 128):
                total = total + line[:, piece * 128:(piece + 1) * 128]
            stat_ref[kind, region:region + 1, :] = total


def start_kernel(per_core, r):
    section, z, n = place_and_peers()
    chunks, count, half = r.p_buf.shape[1], r.p_buf.shape[5], r.far.shape[0]
    blocks = [(j, q) for j in range(per_core) for q in range(chunks)]
    reduce = Reduce(section, z, n, r.part, r.come, r.f_out, r.f_sem, r.red_send, r.red_recv, 0)
    outs = [r.part] + [getattr(r, f"p{j}") for j in range(1, per_core)]
    modes = [Modes(section, r.p_buf.at[j], outs[j], r.p_local.at[j], r.p_cross.at[j]) for j in range(per_core)]

    def field(k):
        j, q = blocks[k]
        src = chunk_at(r.inputs.at[section * per_core + j, 0], q, count)
        return pltpu.make_async_copy(src, r.a_buf.at[k % 2], r.a_sem.at[k % 2])

    def weight_in(x):
        return pltpu.make_async_copy(r.weights.at[0, (1 - section) * half + x], r.w_buf.at[x % 2], r.w_sem.at[x % 2])

    def weight_out(x):
        return to_core(r.w_buf.at[x % 2], r.far.at[x], (r.w_cross.at[0, x], r.w_cross.at[1, x]), section)

    def lend(x):
        if x < half:
            weight_in(x).wait()
            weight_out(x).start()
        if 1 <= x <= half:
            weight_out(x - 1).wait_send()
            if x + 1 < half:
                weight_in(x + 1).start()

    field(0).start()
    for x in range(min(2, half)):
        weight_in(x).start()
    greet(section, z, n, True)
    for k, (j, q) in enumerate(blocks):
        if k + 1 < len(blocks):
            field(k + 1).start()
        field(k).wait()
        to_modes(flat(r.a_buf.at[k % 2]), r.table[...], r.kron[...], r.spread, modes[j].view(q))
        modes[j].start(q)
        lend(k)
        if k >= 1:
            if k <= chunks:
                modes[0].wait(k - 1)
            reduce.tick(k - 1)
    for k in range(len(blocks), half + 1):
        lend(k)
    for t in range(len(blocks) - 1, chunks + n - 1):
        reduce.tick(t)
    for x in range(half):
        weight_out(x).wait_recv()
    for j, q in blocks[chunks:]:
        modes[j].wait(q)
    reduce.finish()


class Share:
    def __init__(self, r, index, parity):
        self.r, self.index, self.parity = r, index, parity
        self.me, self.members = lax.axis_index("batch"), lax.axis_size("batch")

    def copies(self):
        source, target = self.r.keep.at[self.parity], getattr(self.r, f"shared{self.index}").at[self.me]
        yield pltpu.make_async_copy(source, target, self.r.s_local.at[self.parity])
        for away in range(1, self.members):
            yield pltpu.make_async_remote_copy(
                src_ref=source, dst_ref=target, send_sem=self.r.s_send.at[self.parity, away],
                recv_sem=self.r.s_recv.at[self.index, away],
                device_id={"batch": lax.rem(self.me + away, self.members)}, device_id_type=MESH)

    def start(self):
        for copy in self.copies():
            copy.start()

    def wait_send(self):
        for i, copy in enumerate(self.copies()):
            if i == 0:
                copy.wait()
            else:
                copy.wait_send()

    def wait_recv(self):
        for i, copy in enumerate(self.copies()):
            if i > 0:
                copy.wait_recv()


class Stage:
    def __init__(self, k, kind, j, per_core, places, section, z, n, r):
        self.k, self.kind, self.j, self.r, self.section, self.n = k, kind, j, r, section, n
        self.parity = k % 2
        self.micro, self.other = section * per_core + j, (1 - section) * per_core + j
        self.forward, self.last = kind in ("middle", "turn"), kind == "tail"
        self.buffers = {name: r.fields.at[i] for name, i in places.items()}
        self.sems = {name: r.field_sem.at[i] for name, i in places.items()}
        self.gather = Gather(section, z, n, r, self.parity)
        self.count, self.lanes = r.full.shape[5], r.full.shape[6]
        self.chunks = r.full.shape[1]
        plain = lambda name: getattr(r, f"{name}{j}")
        if kind == "middle":
            self.loads = dict(a=r.inputs.at[self.micro, 0])
            self.saves = dict(a=plain("a1_"), z=plain("dg0_"))
        elif kind == "turn":
            self.loads = dict(a=plain("a1_"), cot=r.cotangent.at[self.micro, 0])
            self.saves = dict(cot=plain("gz1_"))
        elif kind == "back":
            self.loads = dict(gz=plain("gz1_"), h=r.cotangent.at[self.micro, 0], a=plain("a1_"), dg=plain("dg0_"))
            self.saves = dict(h=plain("ga1_"), dg=plain("gz0_"))
        else:
            self.loads = dict(gz=plain("gz0_"), h=plain("ga1_"), a=r.inputs.at[self.micro, 0])
            self.saves = {}
        layer = 0 if kind in ("middle", "tail") else 1
        self.weight = getattr(r, f"conv_{'f' if self.forward else 'b'}{layer}")
        self.bias = getattr(r, f"bias{layer}")
        self.table = r.t_plain if kind == "middle" else r.t_doubled
        self.itable = r.it_doubled if self.forward else r.it_plain
        if not self.last:
            self.modes = Modes(section, r.p_buf, r.part.at[self.parity], r.p_local, r.p_cross.at[self.parity])
        if kind in ("turn", "tail"):
            self.bound = Bound(section, 1 if kind == "turn" else 0, self.micro, self.other,
                               self.buffers["a" if kind == "turn" else "h"], r.bound,
                               r.b_local.at[self.parity], r.b_cross.at[self.parity])

    def prefetch(self):
        for name, src in self.loads.items():
            fetch(src, self.buffers[name], self.sems[name])
        if self.forward:
            self.rid_copy().start()

    def rid_copy(self):
        return pltpu.make_async_copy(self.r.region.at[self.micro, 0], self.r.rid.at[self.parity],
                                     self.r.rid_sem.at[self.parity])

    def got(self, name):
        arrived(self.buffers[name], self.sems[name])

    def open(self):
        r, b = self.r, self.buffers
        if self.forward:
            r.eo[...] = jnp.zeros_like(r.eo)
            r.eb[...] = jnp.zeros_like(r.eb)
            self.got("a")
        else:
            for name in ("gz", "h"):
                self.got(name)
            at = self.k - self.r.first_back
            r.cg[at] = jnp.zeros_like(r.cg[at])
            r.bg[at] = jnp.zeros_like(r.bg[at])

    def before(self, i, parts):
        a = self.buffers["a"]
        blocks = a.shape[0] // (self.weight.shape[0] // a.shape[1])
        span = (i * blocks // parts, (i + 1) * blocks // parts)
        if self.forward:
            conv_rows(self.weight, self.bias, a, self.buffers["z"], *span)
        else:
            conv_rows(self.weight, None, self.buffers["gz"], self.buffers["h"], *span)

    def grads(self, part):
        if not self.forward:
            at, rows = self.k - self.r.first_back, self.buffers["a"].shape[0]
            grad_rows(self.buffers["a"], self.buffers["gz"], self.r.cg.at[at], self.r.bg.at[at],
                      part * rows // 2, (part + 1) * rows // 2)

    def outs(self, q):
        return [pltpu.make_async_copy(chunk_at(self.buffers[name], q, self.count), chunk_at(dst, q, self.count),
                                      self.r.out_sem.at[self.parity, i, q])
                for i, (name, dst) in enumerate(self.saves.items())]

    def late(self):
        for name in ("cot", "dg"):
            if name in self.loads:
                self.got(name)
        if not self.forward:
            self.got("a")

    def chunk(self, q):
        r, b, count = self.r, self.buffers, self.count
        spectral = from_modes(self.gather.full.at[q].reshape(-1, count, self.lanes), self.itable[...], r.ikron[...],
                              r.spread)
        if self.forward:
            branch, slope = gelu_parts(spectral + chunk_of(b["z"], q, count))
            if self.kind == "turn":
                put(chunk_at(b["cot"], q, count), chunk_of(b["cot"], q, count) * slope)
            else:
                put(chunk_at(b["z"], q, count), slope)
            add_squares(branch, r.eb)
            out = chunk_of(b["a"], q, count) + branch
            put(chunk_at(b["a"], q, count), out)
            add_squares(out, r.eo)
        else:
            ga = spectral + chunk_of(b["h"], q, count)
            put(chunk_at(b["h"], q, count), ga)
            if not self.last:
                put(chunk_at(b["dg"], q, count), ga * chunk_of(b["dg"], q, count))
        for copy in self.outs(q):
            copy.start()
        if self.kind in ("turn", "tail"):
            self.bound.start(q, count)

    def modes_of(self, q):
        if self.last:
            return
        r, source = self.r, self.buffers[dict(middle="a", turn="cot", back="dg")[self.kind]]
        to_modes(chunk_of(source, q, self.count), self.table[...], r.kron[...], r.spread, self.modes.view(q))

        pl.when(q == self.chunks - 1)(self.gather.finish)
        self.modes.start(q)

    def end(self):
        if self.forward:
            self.rid_copy().wait()
            region_sums(self.r.rid.at[self.parity], self.r.eo, self.r.eb, self.r.stat.at[self.k])
        if self.last:
            self.gather.finish()

    def close(self):
        def body(q, carry):
            for copy in self.outs(q):
                copy.wait()
            if self.kind in ("turn", "tail"):
                self.bound.wait(q, self.count)
            return carry

        lax.fori_loop(0, self.chunks, body, 0)


def stages_kernel(per_core, kinds, places, mixes, r):
    section, z, n = place_and_peers()
    chunks = r.full.shape[1]
    r.first_back = 2 * per_core
    stages = [Stage(k, kind, j, per_core, places[k], section, z, n, r)
              for k, (kind, j) in enumerate((kind, j) for kind in kinds for j in range(per_core))]
    lag = n // 2
    lead, shift = chunks - 2, max(1, lag + 2 - chunks)
    stages[0].prefetch()
    first = [pltpu.make_async_copy(r.p_in, r.part.at[1], r.first_sem.at[0]),
             pltpu.make_async_copy(r.y_in.at[0], r.full.at[0, :, z, section], r.first_sem.at[1]),
             pltpu.make_async_copy(r.y_in.at[1], r.y_give.at[0], r.first_sem.at[2]),
             pltpu.make_async_copy(r.f_in, r.keep.at[0], r.first_sem.at[3])]
    for copy in first:
        copy.start()
    greet(section, z, n, True, lax.axis_size("batch"))
    for copy in first:
        copy.wait()
    for q in range(chunks):
        stages[0].gather.give(q)
    sums = Sum(section, z, n, r, 1, lambda q: None)
    for i in range(lead + 1):
        for second in range(2):
            sums.poll(i, second)
            if i == lead:
                stages[0].gather.poll(0, second)
    shares = [Share(r, 0, 0)]
    shares[0].start()
    for k, stage in enumerate(stages):
        now = None if stage.last else Sum(section, z, n, r, stage.parity, stage.modes.wait)
        mix = share = None
        if sums is not None:
            mix = Mix(section, z, *mixes[(k + 1) // per_core], sums, stages[k + 1].gather, r)
            share = Share(r, k + 1, 1 - stage.parity)
            mix.prime()
        stage.open()
        stage.before(0, lag)

        def poll(i, second):
            if sums is not None:
                sums.poll(i + lead, second)
            stage.gather.poll(i, second)

        def early(i, carry):
            poll(i, 0)
            stage.before(i, lag)
            poll(i, 1)
            if mix is not None and not mix.flip:
                pl.when(within(i - shift, chunks))(lambda: mix.chunk(i - shift))
            return carry

        lax.fori_loop(1, lag, early, 0)
        stage.late()
        stage.grads(0)

        def turn_over():
            if k > 0:
                stages[k - 1].close()
            if now is not None:
                shares[k].wait_send()
            if k + 1 < len(stages):
                stages[k + 1].prefetch()

        def settle():
            sums.finish()
            mix.finish()

        def later(q, carry):
            i = q + lag
            poll(i, 0)
            if now is not None:
                now.poll(q - 1, 0)
            stage.chunk(q)
            poll(i, 1)
            if now is not None:
                now.poll(q - 1, 1)
            if k + 1 < len(stages):
                pl.when(q == chunks - 1)(lambda: stages[k + 1].gather.poll(0, 1))
            stage.modes_of(q)
            pl.when(q == 0)(lambda: stage.grads(1))
            pl.when(q == 1)(turn_over)
            if mix is not None and mix.flip:
                pl.when(q == 1)(sums.finish)
                for half in range(2):
                    at = 2 * (q - 1) + half
                    pl.when(within(at, chunks))(lambda: mix.chunk(at))
            elif mix is not None:
                at = i - shift
                pl.when(jnp.logical_and(within(at, chunks), q < chunks - 1))(lambda: mix.chunk(at))
                pl.when(q == chunks - 2)(settle)
            if share is not None:
                pl.when(q == chunks - 2)(share.start)
            return carry

        lax.fori_loop(0, chunks, later, 0)
        stage.end()
        if share is not None:
            shares.append(share)
        sums = now
    stages[-1].close()
    for share in shares[-2:]:
        share.wait_send()
    for share in shares:
        share.wait_recv()


def swap_halves(value):
    return pltpu.roll(value, value.shape[-1] // 2, value.ndim - 1)


def left_lanes(shape):
    return lax.broadcasted_iota(jnp.int32, shape, len(shape) - 1) < shape[-1] // 2


SLOTS = 4


def weight_stream(own, base, local_ref, far_ref, wbuf, sem):
    step, count = pl.program_id(0), pl.num_programs(0)

    def begin(at):
        slot = lax.rem(at, SLOTS)

        @pl.when(own)
        def _():
            fetch(local_ref.at[0, base + at], wbuf.at[slot], sem.at[slot])

        @pl.when(jnp.logical_not(own))
        def _():
            fetch(far_ref.at[at], wbuf.at[slot], sem.at[slot])

    @pl.when(step == 0)
    def _():
        for at in range(SLOTS - 1):
            @pl.when(at < count)
            def _():
                begin(at)

    @pl.when(step + SLOTS - 1 < count)
    def _():
        begin(step + SLOTS - 1)

    slot = lax.rem(step, SLOTS)
    arrived(wbuf.at[slot], sem.at[slot])
    return wbuf.at[slot]


def pieces(array):
    return [array[at:at + G] for at in range(0, array.shape[0], G)]


def spread_row(ref, row):
    return ref[pl.ds(row, G, stride=0), :]


def mix_kernel(m_ref, f_ref, local_ref, far_ref, y_ref, wbuf, f1, f2, sem):
    weight = weight_stream(m_ref[0] == 1, m_ref[1], local_ref, far_ref, wbuf, sem)
    grids, channels, lanes = f1.shape
    for g in range(grids):
        f1[g] = f_ref[:, g].reshape(channels, lanes)
    f2[...] = swap_halves(f1[...])
    groups = channels // G

    def body(block, acc):
        at = pl.multiple_of(block * G, G)
        acc = list(acc)
        for u in range(G):
            rows = [spread_row(f.at[g], at + u) for g in range(grids) for f in (f1, f2)]
            for o in range(groups):
                w = weight[at + u, o * G:(o + 1) * G, :]
                for k, row in enumerate(rows):
                    acc[k * groups + o] = acc[k * groups + o] + row * w
        return tuple(acc)

    acc = lax.fori_loop(0, groups, body, tuple(jnp.zeros((G, lanes), F32) for _ in range(2 * grids * groups)))
    left = left_lanes((channels, lanes))
    for g in range(grids):
        a, b = [jnp.concatenate(acc[k * groups:(k + 1) * groups], 0) for k in (2 * g, 2 * g + 1)]
        y_ref[g] = jnp.where(left, a - swap_halves(a), b + swap_halves(b)).reshape(y_ref.shape[1:])


def mix_t_kernel(m_ref, d_ref, local_ref, far_ref, y_ref, wbuf, a1, a2, sem):
    weight = weight_stream(m_ref[0] == 1, m_ref[1], local_ref, far_ref, wbuf, sem)
    grids, channels, lanes = a1.shape
    d = [d_ref[:, g].reshape(channels, lanes) for g in range(grids)]
    d1 = [pieces(d[g]) for g in range(grids)]
    d2 = [pieces(swap_halves(d[g])) for g in range(grids)]
    groups = channels // G

    def body(block, carry):
        at = pl.multiple_of(block * G, G)
        rows = [[] for _ in range(2 * grids)]
        for u in range(G):
            total = [None] * (2 * grids)
            for o in range(groups):
                w = weight[at + u, o * G:(o + 1) * G, :]
                for g in range(grids):
                    for side, source in enumerate((d1, d2)):
                        term = w * source[g][o]
                        k = 2 * g + side
                        total[k] = term if total[k] is None else total[k] + term
            for k in range(2 * grids):
                rows[k].append(jnp.sum(total[k], axis=0, keepdims=True))
        for g in range(grids):
            a1[g, pl.ds(at, G), :] = jnp.concatenate(rows[2 * g], 0)
            a2[g, pl.ds(at, G), :] = jnp.concatenate(rows[2 * g + 1], 0)
        return carry

    lax.fori_loop(0, groups, body, 0)
    left = left_lanes((channels, lanes))
    for g in range(grids):
        a, b = a1[g], a2[g]
        y_ref[g] = jnp.where(left, a + swap_halves(a), swap_halves(b) - b).reshape(y_ref.shape[1:])


class Mix:
    def __init__(self, section, z, layer, flip, sums, gather, r):
        self.section, self.z, self.layer, self.flip, self.r = section, z, layer, flip, r
        self.sums, self.gather = sums, gather
        self.chunks, self.grids, self.half, self.count, self.lanes = sums.part.shape[1:]
        self.channels, self.slots = r.weights.shape[2], r.wbuf.shape[0]
        self.blocks = self.chunks * self.half

    def begin(self, block):
        q, x = block // self.half, block % self.half
        slot = lax.rem(block, self.slots)
        rows = pl.ds(q * self.count, self.count)

        @pl.when(self.section == self.layer)
        def _():
            pltpu.make_async_copy(self.r.weights.at[0, self.section * self.half + x, rows], self.r.wbuf.at[slot],
                                  self.r.wsem.at[slot]).start()

        @pl.when(self.section != self.layer)
        def _():
            pltpu.make_async_copy(self.r.far.at[x, rows], self.r.wbuf.at[slot], self.r.wsem.at[slot]).start()

    def prime(self):
        for block in range(min(self.slots, self.blocks)):
            self.begin(jnp.int32(block))
        if not self.flip:
            self.r.macc[...] = jnp.zeros_like(self.r.macc)

    def chunk(self, q):
        def body(x, carry):
            block = q * self.half + x
            slot = lax.rem(block, self.slots)
            weight = self.r.wbuf.at[slot]
            arrived(weight, self.r.wsem.at[slot])
            (self.transposed if self.flip else self.forward)(q, x, weight)

            @pl.when(block + self.slots < self.blocks)
            def _():
                self.begin(block + self.slots)

            return carry

        lax.fori_loop(0, self.half, body, 0)
        if self.flip:
            self.gather.give(q)

    def forward(self, q, x, weight):
        sides, groups = 2 * self.grids, self.channels // G
        total, source = self.r.macc.at[x], self.r.msrc
        for g in range(self.grids):
            value = self.sums.part[self.z, q, g, x]
            source[2 * g, :self.count] = value
            source[2 * g + 1, :self.count] = swap_halves(value)
        keys = [(k, o) for k in range(sides) for o in range(groups)]

        def body(octet, acc):
            acc = dict(zip(keys, acc))
            for u in range(G):
                i = octet * G + u
                rows = [spread_row(source.at[k], i) for k in range(sides)]
                for o in range(groups):
                    w = weight[i, o * G:(o + 1) * G, :]
                    for k in range(sides):
                        acc[k, o] = acc[k, o] + rows[k] * w
            return tuple(acc[key] for key in keys)

        acc = lax.fori_loop(0, self.count // G, body, tuple(total[k, o * G:(o + 1) * G, :] for k, o in keys))
        for key, value in zip(keys, acc):
            total[key[0], key[1] * G:(key[1] + 1) * G, :] = value

    def transposed(self, q, x, weight):
        sides, groups = 2 * self.grids, self.channels // G
        source = self.r.msrc
        for g in range(self.grids):
            value = jnp.concatenate([self.sums.part[self.z, at, g, x] for at in range(self.chunks)], 0)
            source[2 * g] = value
            source[2 * g + 1] = swap_halves(value)
        rows = [pieces(source[k]) for k in range(sides)]
        out = [[] for _ in range(sides)]
        for i in range(self.count):
            total = [None] * sides
            for o in range(groups):
                w = weight[i, o * G:(o + 1) * G, :]
                for k in range(sides):
                    term = w * rows[k][o]
                    total[k] = term if total[k] is None else total[k] + term
            for k in range(sides):
                out[k].append(jnp.sum(total[k], axis=0, keepdims=True))
        left = left_lanes((self.count, self.lanes))
        for g in range(self.grids):
            a, b = [jnp.concatenate(out[2 * g + side], 0) for side in range(2)]
            self.put(g, q, x, jnp.where(left, a + swap_halves(a), swap_halves(b) - b))

    def put(self, g, q, x, value):
        if g == 0:
            self.gather.full[q, self.z, self.section, x] = value
        else:
            self.gather.give_from[q, x] = value

    def finish(self):
        if self.flip:
            return
        left = left_lanes((self.channels, self.lanes))

        def body(x, carry):
            for g in range(self.grids):
                a, b = [self.r.macc[x, 2 * g + side] for side in range(2)]
                result = jnp.where(left, a - swap_halves(a), b + swap_halves(b))
                for q in range(self.chunks):
                    self.put(g, q, x, result[q * self.count:(q + 1) * self.count])
            return carry

        lax.fori_loop(0, self.half, body, 0)
        for q in range(self.chunks):
            self.gather.give(q)


def gather_columns(f_ref, d_ref, left_of, right_of):
    channels = f_ref.shape[2] * f_ref.shape[5]
    lanes = f_ref.shape[6]
    left = left_lanes((channels, lanes))
    for stream in range(f_ref.shape[0]):
        for member in range(f_ref.shape[1]):
            for g in range(f_ref.shape[3]):
                at = (stream * f_ref.shape[1] + member) * f_ref.shape[3] + g
                both = []
                for x in range(2):
                    f = f_ref[stream, member, :, g, x].reshape(channels, lanes)
                    turned = swap_halves(f)
                    left_of[x, at] = jnp.concatenate([f, jnp.where(left, -turned, turned)], 0).T
                    both.append(d_ref[stream, member, :, g, x].reshape(channels, lanes))
                right_of[at] = jnp.concatenate(both, 0).T


def column_products(left_of, right_of, product):
    grids, double, lanes = right_of.shape
    half = double // 2
    left = left_lanes((2 * grids, lanes))
    rows = right_of.reshape(grids * double, lanes)
    sides = [left_of.at[x].reshape(grids * double, lanes) for x in range(2)]

    def body(k, carry):
        pick = pl.ds(k, 2 * grids, stride=half)
        d = rows[pick, :]
        f_high, f_low = split(jnp.concatenate([side[pick, :] for side in sides], 0))
        d_high, d_low = split(jnp.concatenate([jnp.where(left, d, 0.0), jnp.where(left, 0.0, d)], 0))
        product[k] = dot(jnp.concatenate([f_high, f_low, f_high], 0), jnp.concatenate([d_high, d_high, d_low], 0),
                         (((0,), (0,)), ((), ())))
        return carry

    lax.fori_loop(0, half, body, 0, unroll=4)


def product_rows(product, first, out):
    half, double, lanes = product.shape
    channels = double // 2
    rows = product.reshape(half * double, lanes)

    def body(i, carry):
        parts = [rows[pl.ds(part * channels + first + i, half, stride=double), :] for part in range(2)]
        tile = jnp.concatenate(parts, 0).T
        for x in range(2):
            out[x, i] = tile[x * channels:(x + 1) * channels]
        return carry

    lax.fori_loop(0, out.shape[1], body, 0, unroll=4)


class GradInput:
    def __init__(self, first, f, g, fbuf, gbuf, sem):
        self.first, self.f, self.g, self.fbuf, self.gbuf, self.sem = first, f, g, fbuf, gbuf, sem

    def load(self, x, slot):
        for layer, condition in enumerate((self.first, jnp.logical_not(self.first))):
            @pl.when(condition)
            def _():
                for j in range(len(self.f[layer])):
                    pltpu.make_async_copy(self.f[layer][j].at[:, :, :, pl.ds(2 * x, 2)], self.fbuf.at[slot, j],
                                          self.sem.at[0, slot]).start()
                    pltpu.make_async_copy(self.g[layer][j].at[:, :, :, pl.ds(2 * x, 2)], self.gbuf.at[slot, j],
                                          self.sem.at[1, slot]).start()

    def next(self, x, count):
        slot = lax.rem(x, 2)

        @pl.when(x + 1 < count)
        def _():
            self.load(x + 1, 1 - slot)

        arrived(self.fbuf.at[slot], self.sem.at[0, slot])
        arrived(self.gbuf.at[slot], self.sem.at[1, slot])
        return self.fbuf.at[slot], self.gbuf.at[slot]


def grad_input(r, first, per_core):
    f = [[getattr(r, f"f{layer}{j}") for j in range(per_core)] for layer in range(2)]
    g = [[getattr(r, f"g{layer}{j}") for j in range(per_core)] for layer in range(2)]
    return GradInput(first, f, g, r.fbuf, r.gbuf, r.in_sem)


def far_grad_kernel(per_core, r):
    section, z, n = place_and_peers()
    pairs, block = r.far.shape[0] // 2, r.out.shape[2]
    blocks = r.far.shape[1] // block
    source = grad_input(r, section != 0, per_core)

    def move(k, slot):
        p, i = k // blocks, k % blocks
        return to_core(r.out.at[slot], r.far.at[pl.ds(2 * p, 2), pl.ds(i * block, block)], (r.send.at[k], r.recv.at[k]),
                       section)

    source.load(0, 0)
    greet(section, z, n, False)

    def body(p, carry):
        gather_columns(*source.next(p, pairs), r.left_of, r.right_of)
        column_products(r.left_of, r.right_of, r.product)

        def inner(i, carry):
            k = p * blocks + i

            @pl.when(k >= 2)
            def _():
                move(k - 2, lax.rem(k, 2)).wait_send()

            product_rows(r.product, i * block, r.out.at[lax.rem(k, 2)])
            move(k, lax.rem(k, 2)).start()
            return carry

        return lax.fori_loop(0, blocks, inner, carry)

    lax.fori_loop(0, pairs, body, 0)
    total = pairs * blocks
    for k in (total - 2, total - 1):
        move(k, k % 2).wait_send()

    def close(k, carry):
        move(k, 0).wait_recv()
        return carry

    lax.fori_loop(0, total, close, 0)


def own_grad_kernel(names, per_core, m_ref, *refs):
    r = types.SimpleNamespace(**dict(zip(names, refs)))
    p, i = pl.program_id(0), pl.program_id(1)
    source = grad_input(r, m_ref[0] == 0, per_core)

    @pl.when(i == 0)
    def _():
        @pl.when(p == 0)
        def _():
            source.load(0, 0)

        gather_columns(*source.next(p, pl.num_programs(0)), r.left_of, r.right_of)
        column_products(r.left_of, r.right_of, r.product)

    r.bound_out[...] = r.bound_in[...]
    r.out[1 - m_ref[0]] = r.far[...]
    product_rows(r.product, i * r.out.shape[2], r.out.at[m_ref[0]])


def whole(array):
    return pl.BlockSpec(array.shape, lambda *_: (0,) * array.ndim)


def params(**kw):
    return pltpu.CompilerParams(vmem_limit_bytes=VMEM_LIMIT, **kw)


def local(inputs, cotangent, region_id, spectral_w, conv_w, bias_vector):
    micro_count, _, rows_dev, channels, width = inputs.shape
    lanes = spectral_w.shape[-1]
    half = lanes // 2
    kx_dev = spectral_w.shape[1]
    row_devices, sections = lax.axis_size("rows"), lax.axis_size("section")
    mode_rows, height = kx_dev * row_devices, rows_dev * row_devices
    section = lax.axis_index("section")
    per_core = micro_count // sections
    kx_half = kx_dev // sections

    plain, doubled = col_tables(width, half)

    def stacked(array):
        high, low = np_split(array)
        return np.concatenate([high, high, low], 0)

    t_plain, t_doubled, it_plain, it_doubled = [stacked(t) for t in (plain, doubled, plain.T, doubled.T)]
    kron, ikron = row_tables(height, mode_rows, lax.axis_index("rows") * rows_dev, rows_dev)

    count = 2 * G
    chunks = channels // count
    hbm, vmem = pl.BlockSpec(memory_space=pl.ANY), pl.BlockSpec(memory_space=pltpu.VMEM)
    field_shape = jax.ShapeDtypeStruct((rows_dev, channels, width), F32)
    part_dims = (row_devices, chunks, sections, kx_half, count, lanes)
    p_shape, f_shape = jax.ShapeDtypeStruct(part_dims, F32), jax.ShapeDtypeStruct(part_dims[1:], F32)
    y_shape = jax.ShapeDtypeStruct((sections, chunks, kx_half, count, lanes), F32)
    stat_shape = jax.ShapeDtypeStruct((3, R, 128), F32)
    cg_shape = jax.ShapeDtypeStruct((2 * channels, 2 * channels), F32)
    bg_shape = jax.ShapeDtypeStruct((channels, width), F32)
    bound_shape = jax.ShapeDtypeStruct((micro_count, rows_dev, channels, width), F32)
    dma = pltpu.SemaphoreType.DMA
    field_buf = pltpu.VMEM((rows_dev, channels, width), F32)
    full_dims = (chunks, row_devices, sections, kx_half, count, lanes)
    spread = pltpu.VMEM((width // 128, rows_dev * count, 128), F32)
    energy = pltpu.VMEM((rows_dev, G, width), F32)
    line_sems = dma((2, chunks, row_devices))
    start_scratch = dict(part=pltpu.VMEM(part_dims, F32), come=pltpu.VMEM((2, chunks, row_devices) + part_dims[2:], F32),
                         f_sem=dma((chunks,)), red_send=line_sems, red_recv=line_sems)

    def run(body, ident, ins, outs, scratch, cost=50, aliases=None):
        names = [*ins, *outs, *scratch]
        spec = lambda entry: vmem if isinstance(entry, tuple) else hbm
        plain = lambda entry: entry[0] if isinstance(entry, tuple) else entry
        kernel = lambda *refs: body(types.SimpleNamespace(**dict(zip(names, refs))))
        positions = {list(ins).index(k): list(outs).index(v) for k, v in (aliases or {}).items()}
        result = pl.pallas_call(
            kernel, in_specs=[spec(e) for e in ins.values()], out_specs=[spec(e) for e in outs.values()],
            out_shape=[plain(e) for e in outs.values()], scratch_shapes=list(scratch.values()),
            input_output_aliases=positions,
            cost_estimate=pl.CostEstimate(flops=0, bytes_accessed=cost * 3_000_000, transcendentals=0),
            compiler_params=params(collective_id=ident, has_side_effects=True))(*[plain(e) for e in ins.values()])
        return types.SimpleNamespace(**dict(zip(outs, result)))

    conv_rows_at_once = 256 // channels
    conv_both = lax.all_gather(conv_w, "section", axis=0, tiled=True)
    bias_both = lax.all_gather(bias_vector, "section", axis=0, tiled=True)

    def conv_parts(matrix):
        wide = jnp.kron(jnp.eye(conv_rows_at_once, dtype=F32), matrix)
        rounded = lax.reduce_precision(wide, 8, 7)
        high, low = rounded.astype(BF16), (wide - rounded).astype(BF16)
        return jnp.concatenate([high, low, high], 1)

    conv_fwd = [conv_parts(conv_both[l].T) for l in range(2)]
    conv_bwd = [conv_parts(conv_both[l]) for l in range(2)]
    bias_wide = [jnp.broadcast_to(bias_both[l][:, None], (channels, width)) for l in range(2)]

    def mixing(body, layer, pair):
        flag = jnp.stack([(section == layer).astype(jnp.int32), section * kx_half])
        f_block = pl.BlockSpec((chunks, sections, None, count, lanes), lambda x, m: (0, 0, x, 0, 0))
        y_block = pl.BlockSpec((sections, chunks, None, count, lanes), lambda x, m: (0, 0, x, 0, 0))
        small = pltpu.VMEM((sections, channels, lanes), F32)
        grid_spec = pltpu.PrefetchScalarGridSpec(
            num_scalar_prefetch=1, grid=(kx_half,), in_specs=[f_block, hbm, hbm], out_specs=y_block,
            scratch_shapes=[pltpu.VMEM((SLOTS, channels, channels, lanes), F32), small, small, dma((SLOTS,))])
        return pl.pallas_call(
            body, grid_spec=grid_spec, out_shape=y_shape, compiler_params=params(),
            cost_estimate=pl.CostEstimate(flops=0, bytes_accessed=30_000_000, transcendentals=0))(
                flag, pair, spectral_w, far_weights)

    streams = range(per_core)
    start = run(
        functools.partial(start_kernel, per_core), 0,
        dict(inputs=inputs, weights=spectral_w, table=(t_plain,), kron=(kron,)),
        dict(f_out=f_shape, far=jax.ShapeDtypeStruct((kx_half,) + spectral_w.shape[2:], F32),
             **{f"p{j}": p_shape for j in streams[1:]}),
        dict(a_buf=pltpu.VMEM((2, rows_dev, count, width), F32), w_buf=pltpu.VMEM((2,) + spectral_w.shape[2:], F32),
             p_buf=pltpu.VMEM((per_core,) + full_dims, F32), spread=spread, a_sem=dma((2,)), w_sem=dma((2,)),
             w_cross=dma((2, kx_half)), p_local=dma((per_core, chunks)), p_cross=dma((per_core, 2, chunks)),
             **start_scratch))
    far_weights = start.far

    members = lax.axis_size("batch")
    kinds = ["middle", "turn", "back", "tail"]
    mixes = [(0, False), (1, False), (1, True), (0, True)]
    names = ["f00", "f01", "f10", "f11", "g10", "g11", "g00", "g01"]
    places = [dict(a=0, z=1), dict(a=2, z=3), dict(a=4, z=5, cot=6), dict(a=0, z=1, cot=2),
              dict(gz=3, a=4, h=5, dg=6), dict(gz=0, a=1, h=2, dg=3), dict(gz=4, a=5, h=6), dict(gz=0, a=1, h=2)]
    y = mixing(mix_kernel, 0, start.f_out)
    both = (2,)
    ins = dict(inputs=inputs, cotangent=cotangent, region=region_id, weights=spectral_w, far=far_weights,
               p_in=start.p1, f_in=start.f_out, y_in=y, t_plain=(t_plain,), t_doubled=(t_doubled,), it_plain=(it_plain,),
               it_doubled=(it_doubled,), kron=(kron,), ikron=(ikron,),
               **{f"conv_f{l}": (conv_fwd[l],) for l in range(2)}, **{f"conv_b{l}": (conv_bwd[l],) for l in range(2)},
               **{f"bias{l}": (bias_wide[l],) for l in range(2)})
    outs = dict(bound=bound_shape, stat=(jax.ShapeDtypeStruct((2 * per_core,) + stat_shape.shape, F32),),
                cg=(jax.ShapeDtypeStruct((2 * per_core,) + cg_shape.shape, F32),),
                bg=(jax.ShapeDtypeStruct((2 * per_core,) + bg_shape.shape, F32),),
                **{f"{name}{j}": field_shape for name in ("a1_", "dg0_", "gz1_", "ga1_", "gz0_") for j in streams},
                **{f"shared{i}": jax.ShapeDtypeStruct((members,) + f_shape.shape, F32) for i in range(len(names))})
    scratch = dict(
        fields=pltpu.VMEM((7,) + field_shape.shape, F32), full=pltpu.VMEM(both + full_dims, F32),
        part=pltpu.VMEM(both + part_dims, F32),
        come=pltpu.VMEM(both + (2, chunks, row_devices - 1) + part_dims[2:], F32),
        keep=pltpu.VMEM(both + f_shape.shape, F32), y_give=pltpu.VMEM(both + y_shape.shape[1:], F32),
        p_buf=pltpu.VMEM(full_dims, F32), spread=spread, eo=energy, eb=energy,
        rid=pltpu.VMEM((2, rows_dev, width), jnp.int32),
        wbuf=pltpu.VMEM((6, count, channels, lanes), F32), macc=pltpu.VMEM((kx_half, 2 * sections, channels, lanes), F32),
        msrc=pltpu.VMEM((2 * sections, channels, lanes), F32),
        field_sem=dma((7,)), rid_sem=dma(both), out_sem=dma((2, 2, chunks)), wsem=dma((6,)), first_sem=dma((4,)),
        send=dma(both + (2, chunks, row_devices)), recv=dma(both + (2, chunks, row_devices)),
        red_send=dma(both + (2, chunks, row_devices)), red_recv=dma(both + (2, chunks, row_devices)),
        y_cross=dma((2, 2, chunks)), p_local=dma((chunks,)), p_cross=dma((2, 2, chunks)),
        b_local=dma((2, chunks)), b_cross=dma((2, 2, chunks)),
        s_local=dma(both), s_send=dma((2, members)), s_recv=dma((len(names), members)))
    done = run(functools.partial(stages_kernel, per_core, kinds, places, mixes), 1, ins, outs, scratch, cost=400)
    gathered = {name: getattr(done, f"shared{i}") for i, name in enumerate(names)}
    bound, calls = done.bound, 1

    grids = per_core * members * sections
    block = 2 * G
    pairs, blocks = kx_half // 2, channels // block
    in_buf = pltpu.VMEM((2, per_core, members, chunks, sections, 2, count, lanes), F32)
    grad_scratch = dict(fbuf=in_buf, gbuf=in_buf, in_sem=dma((2, 2)), left_of=pltpu.VMEM((2, grids, lanes, lanes), F32),
                        right_of=pltpu.VMEM((grids, lanes, lanes), F32), product=pltpu.VMEM((half, lanes, lanes), F32))
    far_grad = run(functools.partial(far_grad_kernel, per_core), 1 + calls, gathered,
                   dict(far=jax.ShapeDtypeStruct((kx_half, channels, channels, lanes), F32)),
                   dict(out=pltpu.VMEM((2, 2, block, channels, lanes), F32), send=dma((pairs * blocks,)),
                        recv=dma((pairs * blocks,)), **grad_scratch)).far
    bound_rows = bound.reshape(micro_count * rows_dev, channels, width)
    bound_block = pl.BlockSpec((bound_rows.shape[0] // (pairs * blocks), channels, width),
                               lambda p, i, m: (p * blocks + i, 0, 0))
    grid_spec = pltpu.PrefetchScalarGridSpec(
        num_scalar_prefetch=1, grid=(pairs, blocks),
        in_specs=[hbm] * len(gathered)
        + [pl.BlockSpec((2, block, channels, lanes), lambda p, i, m: (p, i, 0, 0)), bound_block],
        out_specs=[pl.BlockSpec((2, 2, block, channels, lanes), lambda p, i, m: (0, p, i, 0, 0)), bound_block],
        scratch_shapes=list(grad_scratch.values()))
    spectral_grad, boundary = pl.pallas_call(
        functools.partial(own_grad_kernel, [*gathered, "far", "bound_in", "out", "bound_out", *grad_scratch], per_core),
        grid_spec=grid_spec, out_shape=[jax.ShapeDtypeStruct((2, kx_half, channels, channels, lanes), F32),
                                        jax.ShapeDtypeStruct(bound_rows.shape, F32)],
        cost_estimate=pl.CostEstimate(flops=0, bytes_accessed=150_000_000, transcendentals=0),
        compiler_params=params())(
            jnp.reshape(section, (1,)).astype(jnp.int32), *gathered.values(), far_grad, bound_rows)
    spectral_grad = spectral_grad.reshape(spectral_w.shape)
    boundary = boundary.reshape((1, micro_count, 1) + inputs.shape[2:])

    def lower(value):
        return (value[:channels, :channels] + value[channels:, channels:]
                + value[:channels, channels:] + value[channels:, :channels])

    pair = lambda value: jnp.sum(value.reshape((2, per_core) + value.shape[1:]), 1)
    conv_local = jnp.stack([lower(value) for value in pair(done.cg)[::-1]])
    bias_local = jnp.sum(pair(done.bg)[::-1], -1)
    stat_local = jnp.sum(pair(done.stat), -1)
    shapes = [v.shape for v in (conv_local, bias_local, stat_local)]
    flat_sums = jnp.concatenate([v.reshape(-1) for v in (conv_local, bias_local, stat_local)])
    length = flat_sums.shape[0]
    flat_sums = jnp.pad(flat_sums, (0, -length % 1024)).reshape(-1, 128)
    flat_sums = jnp.sum(lax.all_gather(flat_sums, ("section", "batch", "rows"), axis=0), 0).reshape(-1)
    ends = np.cumsum([0] + [math.prod(shape) for shape in shapes])
    conv_sum, bias_sum, stat_sum = [flat_sums[ends[i]:ends[i + 1]].reshape(shapes[i]) for i in range(3)]
    own_stat = lax.dynamic_index_in_dim(stat_sum, section, 0, False)
    layer_rms = jnp.sqrt(own_stat[:2] / (channels * own_stat[2])[None, :] + 1e-06)[None]
    own = lambda value: lax.dynamic_slice_in_dim(value, section, 1, 0)
    return boundary, spectral_grad, own(conv_sum), own(bias_sum), layer_rms


def solution(mesh):
    placed = (
        P(None, "batch", "rows", None, None),
        P(None, "batch", "rows", None, None),
        P(None, "batch", "rows", None),
        P("section", "rows", None, None, None),
        P("section", None, None),
        P("section", None),
    )
    return jax.shard_map(
        local,
        mesh=mesh,
        in_specs=placed,
        out_specs=(
            P("section", None, "batch", "rows", None, None),
            P("section", "rows", None, None, None),
            P("section", None, None),
            P("section", None),
            P("section", None, None),
        ),
        check_vma=False,
    )
```

```python
import functools
import math
import types

import jax
import jax.numpy as jnp
import numpy as np
from jax import lax
from jax.experimental import pallas as pl
from jax.experimental.pallas import tpu as pltpu
from jax.sharding import PartitionSpec as P

R = 8
G = 8
AHEAD = 2
F32 = jnp.float32
BF16 = jnp.bfloat16
VMEM_LIMIT = 62 * 1024 * 1024
MESH = pl.DeviceIdType.MESH


def split(value):
    high = value.astype(BF16)
    return high, (value - high.astype(F32)).astype(BF16)


def dot(left, right, dims=(((1,), (0,)), ((), ()))):
    return lax.dot_general(left, right, dims, preferred_element_type=F32)


def dot3(left, right):
    return dot(left[0], right[0]) + (dot(left[1], right[0]) + dot(left[0], right[1]))


def np_split(value):
    high = value.astype(np.float32).astype(BF16)
    return high, (value - high.astype(np.float64)).astype(np.float32).astype(BF16)


def col_tables(width, half):
    phase = 2.0 * math.pi / width * (np.outer(np.arange(width), np.arange(half)) % width)
    cosine, sine = np.cos(phase) / math.sqrt(width), np.sin(phase) / math.sqrt(width)
    plain = np.concatenate([cosine, -sine, -sine, -cosine], 1)
    doubled = plain * np.tile(np.where(np.arange(half) == 0, 1.0, 2.0), 4)[None, :]
    return plain, doubled


def row_tables(height, mode_rows, first_row, rows_dev):
    position = jnp.arange(mode_rows, dtype=jnp.int32)
    frequency = jnp.where(position < mode_rows // 2, position, height - mode_rows + position)
    row = first_row + jnp.arange(rows_dev, dtype=jnp.int32)
    phase = 2.0 * math.pi / height * (frequency[:, None] * row[None, :] % height).astype(F32)
    small = jnp.concatenate([jnp.cos(phase), jnp.sin(phase)], 1) / math.sqrt(height)
    rounded = lax.reduce_precision(small, 8, 7)
    high, low = rounded.astype(BF16), (small - rounded).astype(BF16)
    forward = jnp.concatenate([jnp.concatenate([high, high], 1), jnp.concatenate([low, jnp.zeros_like(low)], 1)], 0)
    inverse = jnp.concatenate([high.T, high.T, low.T], 1)
    return forward, inverse


def to_modes(value, table, kron, spread, p_ref):
    mode_rows, count, lanes = p_ref.shape
    rows = value.shape[0] // count
    high, low = split(value)
    spectra = dot(jnp.concatenate([high, low, high], 1), table)
    for i in range(2):
        spread[i] = spectra[:, i * lanes:(i + 1) * lanes]
    out = p_ref.reshape(mode_rows * count, lanes)
    for first in range(0, count, 2):
        sides = []
        for c in (first, first + 1):
            pick = pl.ds(c, rows, stride=count)
            sides.append(jnp.concatenate([spread[i, pick, :] for i in range(2)], 0))
        high, low = split(jnp.concatenate(sides, 1))
        both = dot(kron, jnp.concatenate([high, low], 0))
        result = both[:mode_rows] + both[mode_rows:]
        for i in range(2):
            out[pl.ds(first + i, mode_rows, stride=count), :] = result[:, i * lanes:(i + 1) * lanes]


def from_modes(y_ref, table, kron, spread):
    mode_rows, count, lanes = y_ref.shape
    rows, pieces = spread.shape[1] // count, spread.shape[0]
    modes = y_ref.reshape(mode_rows * count, lanes)
    sides = []
    for first in range(0, count, 2):
        pair = [modes[pl.ds(c, mode_rows, stride=count), :] for c in (first, first + 1)]
        high, low = split(jnp.concatenate(pair, 1))
        both = dot(kron, jnp.concatenate([high, low, high], 0))
        for i in range(2):
            side = both[:, i * lanes:(i + 1) * lanes]
            sides.append(jnp.concatenate([side[:rows], side[rows:]], 1))
    high, low = split(jnp.concatenate(sides, 0))
    out = dot(jnp.concatenate([high, low, high], 1), table)
    for c in range(count):
        for i in range(pieces):
            spread[i, pl.ds(c, rows, stride=count), :] = out[c * rows:(c + 1) * rows, i * 128:(i + 1) * 128]
    return jnp.concatenate([spread[i] for i in range(pieces)], 1)


def gelu_parts(z):
    size = jnp.abs(z)
    gauss = jnp.exp(-0.5 * z * z)
    base = 1.0 + (0.3275911 / math.sqrt(2.0)) * size
    t = pl.reciprocal(base, approx=True)
    t = t * (2.0 - base * t)
    poly = t * (0.254829592 + t * (-0.284496736 + t * (1.421413741 + t * (-1.453152027 + t * 1.061405429))))
    tail = 0.5 * poly * gauss
    phi = jnp.where(z >= 0, 1.0 - tail, tail)
    return z * phi, phi + z * (gauss * (1.0 / math.sqrt(2.0 * math.pi)))


def flat(ref):
    rows, count, width = ref.shape
    return ref[...].reshape(rows * count, width)


def put(ref, value):
    ref[...] = value.reshape(ref.shape)


def place_and_peers():
    section, z = lax.axis_index("section"), lax.axis_index("rows")
    return section, z, lax.axis_size("rows")


def greet(section, z, n, lines, members=0):
    barrier = pltpu.get_barrier_semaphore()
    pl.semaphore_signal(barrier, inc=1, device_id={"section": 1 - section}, device_id_type=MESH)
    if not lines:
        pl.semaphore_wait(barrier, 1)
        return

    @pl.when(z > 0)
    def _():
        pl.semaphore_signal(barrier, inc=1, device_id={"rows": z - 1}, device_id_type=MESH)

    @pl.when(z < n - 1)
    def _():
        pl.semaphore_signal(barrier, inc=1, device_id={"rows": z + 1}, device_id_type=MESH)

    for away in range(1, members):
        pl.semaphore_signal(barrier, inc=1, device_id={"batch": lax.rem(lax.axis_index("batch") + away, members)},
                            device_id_type=MESH)

    others = 1 + max(members - 1, 0)
    pl.semaphore_wait(barrier, others + (z > 0).astype(jnp.int32) + (z < n - 1).astype(jnp.int32))


def to_core(src, dst, sems, section):
    return pltpu.make_async_remote_copy(src_ref=src, dst_ref=dst, send_sem=sems[0], recv_sem=sems[1],
                                        device_id={"section": 1 - section}, device_id_type=MESH)


def guard(condition, body):
    if isinstance(condition, (bool, np.bool_)):
        if condition:
            body()
    else:
        pl.when(condition)(body)


class Line:
    def __init__(self, section, z, n, chunks, send, recv):
        self.section, self.z, self.n, self.chunks = section, z, n, chunks
        self.send, self.recv = send, recv

    def move(self, way, q, hop, src, dst):
        return pltpu.make_async_remote_copy(
            src_ref=src, dst_ref=dst, send_sem=self.send.at[way, q, hop], recv_sem=self.recv.at[way, q, hop],
            device_id={"rows": self.z + 1 if way == 0 else self.z - 1}, device_id_type=MESH)

    def sends(self, way):
        return self.z < self.n - 1 if way == 0 else self.z > 0

    def hears(self, way):
        return self.z > 0 if way == 0 else self.z < self.n - 1


def within(value, count):
    return jnp.logical_and(value >= 0, value < count)


class Gather(Line):
    def __init__(self, section, z, n, r, parity):
        super().__init__(section, z, n, r.full.shape[1], r.send.at[parity], r.recv.at[parity])
        self.full, self.give_from = r.full.at[parity], r.y_give.at[parity]
        self.cross = r.y_cross.at[parity]

    def swap(self, q):
        return to_core(self.give_from.at[q], self.full.at[q, self.z, self.section],
                       (self.cross.at[0, q], self.cross.at[1, q]), self.section)

    def give(self, q):
        self.swap(q).start()

    def hop(self, way, q, hop):
        piece = self.full.at[q, self.source(way, hop)]
        return self.move(way, q, hop, piece, piece)

    def source(self, way, hop):
        return self.z - hop if way == 0 else self.z + hop

    def known(self, way, hop):
        at = self.source(way, hop)
        return at >= 0 if way == 0 else at < self.n

    def own(self, q):
        self.swap(q).wait_recv()
        for way in range(2):
            @pl.when(self.sends(way))
            def _():
                self.hop(way, q, 0).start()

    def step(self, q, hop):
        for way in range(2):
            @pl.when(self.known(way, hop + 1))
            def _():
                piece = self.full.at[q, self.source(way, hop + 1)]
                self.move(way, q, hop, piece, piece).wait_recv()

                @pl.when(self.sends(way))
                def _():
                    self.hop(way, q, hop + 1).start()

    def begin(self):
        for q in range(min(AHEAD, self.chunks)):
            self.own(q)

    def tick(self, t):
        @pl.when(t + AHEAD < self.chunks)
        def _():
            self.own(t + AHEAD)

        for hop in range(self.n - 1):
            q = t - hop - 1
            pl.when(within(q, self.chunks))(functools.partial(self.step, q, hop))

    def finish(self):
        def body(q, carry):
            self.swap(q).wait_send()
            for way in range(2):
                for hop in range(self.n - 1):
                    @pl.when(jnp.logical_and(self.sends(way), self.known(way, hop)))
                    def _():
                        self.hop(way, q, hop).wait_send()
            return carry

        lax.fori_loop(0, self.chunks, body, 0)


class Sum(Line):
    def __init__(self, section, z, n, r, parity, admit):
        super().__init__(section, z, n, r.part.shape[2], r.red_send.at[parity], r.red_recv.at[parity])
        self.part, self.come, self.keep, self.admit = r.part.at[parity], r.come.at[parity], r.keep.at[parity], admit

    def owner(self, way, hop):
        return self.z + self.n - hop if way == 0 else self.z - self.n + hop

    def valid(self, way, hop):
        return self.z <= hop - 1 if way == 0 else self.z >= self.n - hop

    def sent(self, way, q, hop):
        return self.move(way, q, hop, self.part.at[self.owner(way, hop), q], self.come.at[way, q, hop - 1])

    def heard(self, way, q, hop):
        come = self.come.at[way, q, hop - 1]
        self.move(way, q, hop, come, come).wait_recv()

    def first(self, q):
        self.admit(q)
        for way in range(2):
            @pl.when(jnp.logical_not(self.hears(way)))
            def _():
                for hop in range(1, self.n):
                    @pl.when(self.valid(way, hop))
                    def _():
                        self.sent(way, q, hop).start()

    def step(self, q, hop):
        for way in range(2):
            @pl.when(jnp.logical_and(self.valid(way, hop), self.hears(way)))
            def _():
                self.heard(way, q, hop - 1)
                owner = self.owner(way, hop)
                self.part[owner, q] = self.part[owner, q] + self.come[way, q, hop - 2]
                self.sent(way, q, hop).start()

    def final(self, q):
        for way in range(2):
            @pl.when(self.hears(way))
            def _():
                self.heard(way, q, self.n - 1)
                self.part[self.z, q] = self.part[self.z, q] + self.come[way, q, self.n - 2]

        self.keep[q] = self.part[self.z, q]

    def tick(self, t):
        pl.when(within(t, self.chunks))(functools.partial(self.first, t))
        for hop in range(2, self.n + 1):
            q = t - hop + 1
            pl.when(within(q, self.chunks))(
                functools.partial(self.step, q, hop) if hop < self.n else functools.partial(self.final, q))

    def finish(self):
        def body(q, carry):
            for way in range(2):
                for hop in range(1, self.n):
                    @pl.when(self.valid(way, hop))
                    def _():
                        self.sent(way, q, hop).wait_send()
            return carry

        lax.fori_loop(0, self.chunks, body, 0)


def fetch(src, dst, sem, parts=4):
    step = dst.shape[0] // parts
    for i in range(parts):
        pltpu.make_async_copy(src.at[pl.ds(i * step, step)], dst.at[pl.ds(i * step, step)], sem).start()


def arrived(dst, sem):
    pltpu.make_async_copy(dst, dst, sem).wait()


def portions(total, count):
    return [(i * total // count, (i + 1) * total // count) for i in range(count)]


def conv_rows(weight, bias, a, out, first, last):
    channels, width = a.shape[1:]
    block = weight.shape[0] // channels

    def body(i, carry):
        at = pl.ds(i * block, block)
        high, low = split(a[at].reshape(block * channels, width))
        result = dot(weight[...], jnp.concatenate([high, high, low], 0)).reshape(block, channels, width)
        out[at] = result + bias[...][None] if bias is not None else out[at] + result
        return carry

    lax.fori_loop(first, last, body, 0)


def grad_rows(a, gz, cg_ref, bg_ref, first, last):
    channels, width = a.shape[1:]

    def body(r, carry):
        grad, bias = carry
        g = gz[r]
        left = jnp.concatenate(split(a[r]), 0)
        right = jnp.concatenate(split(g), 0)
        return grad + dot(left, right, (((1,), (1,)), ((), ()))), bias + g

    grad, bias = lax.fori_loop(first, last, body, (cg_ref[...], bg_ref[...]))
    cg_ref[...] = grad
    bg_ref[...] = bias


def chunk_of(ref, q, count):
    rows, _, width = ref.shape
    return ref[:, pl.ds(pl.multiple_of(q * count, count), count), :].reshape(rows * count, width)


def chunk_at(ref, q, count):
    return ref.at[:, pl.ds(pl.multiple_of(q * count, count), count), :]


class Modes:
    def __init__(self, section, buffer, p_out, local, cross):
        self.section, self.buffer, self.p_out, self.local, self.cross = section, buffer, p_out, local, cross

    def view(self, q):
        n, halves, kx, count, lanes = self.buffer.shape[1:]
        return self.buffer.at[q].reshape(n * halves * kx, count, lanes)

    def copies(self, q):
        s = self.section
        return (pltpu.make_async_copy(self.buffer.at[q, :, s], self.p_out.at[:, q, 0], self.local.at[q]),
                to_core(self.buffer.at[q, :, 1 - s], self.p_out.at[:, q, 1],
                        (self.cross.at[0, q], self.cross.at[1, q]), s))

    def start(self, q):
        for copy in self.copies(q):
            copy.start()

    def wait(self, q):
        for copy in self.copies(q):
            copy.wait()


class Bound:
    def __init__(self, section, owner, micro, other, source, bound, local, cross):
        self.section, self.owner, self.micro, self.other = section, owner, micro, other
        self.source, self.bound, self.local, self.cross = source, bound, local, cross

    def copies(self, q, count, micro):
        src, dst = chunk_at(self.source, q, count), chunk_at(self.bound.at[micro], q, count)
        return (pltpu.make_async_copy(src, dst, self.local.at[q]),
                to_core(src, dst, (self.cross.at[0, q], self.cross.at[1, q]), self.section))

    def start(self, q, count):
        here, there = self.copies(q, count, self.micro)

        @pl.when(self.section == self.owner)
        def _():
            here.start()

        @pl.when(self.section != self.owner)
        def _():
            there.start()

    def wait(self, q, count):
        here, there = self.copies(q, count, self.micro)
        come = self.copies(q, count, self.other)[1]

        @pl.when(self.section == self.owner)
        def _():
            here.wait()
            come.wait_recv()

        @pl.when(self.section != self.owner)
        def _():
            there.wait_send()


def add_squares(value, total):
    rows, _, width = total.shape
    square = (value * value).reshape(rows, -1, width)
    for at in range(0, square.shape[1], G):
        total[...] += square[:, at:at + G]


def region_sums(rid_ref, eo, eb, stat_ref):
    rows, _, width = eo.shape
    rid = rid_ref[...]
    energies = (jnp.sum(eo[...], axis=1), jnp.sum(eb[...], axis=1), jnp.ones((rows, width), F32))
    for kind in range(3):
        for region in range(R):
            line = jnp.sum(jnp.where(rid == region + 1, energies[kind], 0.0), axis=0, keepdims=True)
            total = line[:, :128]
            for piece in range(1, width // 128):
                total = total + line[:, piece * 128:(piece + 1) * 128]
            stat_ref[kind, region:region + 1, :] = total


class Share:
    def __init__(self, r, index, parity):
        self.r, self.index, self.parity = r, index, parity
        self.me, self.members = lax.axis_index("batch"), lax.axis_size("batch")

    def copies(self):
        source, target = self.r.keep.at[self.parity], getattr(self.r, f"shared{self.index}").at[self.me]
        yield pltpu.make_async_copy(source, target, self.r.s_local.at[self.parity])
        for away in range(1, self.members):
            yield pltpu.make_async_remote_copy(
                src_ref=source, dst_ref=target, send_sem=self.r.s_send.at[self.parity, away],
                recv_sem=self.r.s_recv.at[self.index, away],
                device_id={"batch": lax.rem(self.me + away, self.members)}, device_id_type=MESH)

    def start(self):
        for copy in self.copies():
            copy.start()

    def wait_send(self):
        for i, copy in enumerate(self.copies()):
            if i == 0:
                copy.wait()
            else:
                copy.wait_send()

    def wait_recv(self):
        for i, copy in enumerate(self.copies()):
            if i > 0:
                copy.wait_recv()


class Head:
    def __init__(self, micro, place, parity, section, r):
        self.r, self.field, self.sem = r, r.fields.at[place], r.field_sem.at[place]
        self.source, self.count = r.inputs.at[micro, 0], r.full.shape[5]
        self.modes = Modes(section, r.p_buf, r.part.at[parity], r.p_local, r.p_cross.at[parity])

    def fetch(self):
        fetch(self.source, self.field, self.sem)

    def got(self):
        arrived(self.field, self.sem)

    def chunk(self, q):
        r = self.r
        to_modes(chunk_of(self.field, q, self.count), r.t_plain[...], r.kron[...], r.spread, self.modes.view(q))
        self.modes.start(q)


class Stage:
    def __init__(self, k, kind, j, per_core, places, section, z, n, r):
        self.k, self.kind, self.j, self.r, self.section, self.n = k, kind, j, r, section, n
        self.parity = k % 2
        self.micro, self.other = section * per_core + j, (1 - section) * per_core + j
        self.forward, self.last = kind in ("middle", "turn"), kind == "tail"
        self.buffers = {name: r.fields.at[i] for name, i in places.items()}
        self.sems = {name: r.field_sem.at[i] for name, i in places.items()}
        self.gather = Gather(section, z, n, r, self.parity)
        self.count, self.lanes = r.full.shape[5], r.full.shape[6]
        self.chunks = r.full.shape[1]
        plain = lambda name: getattr(r, f"{name}{j}")
        if kind == "middle":
            self.loads = dict(a=r.inputs.at[self.micro, 0])
            self.saves = dict(a=plain("a1_"), z=plain("dg0_"))
        elif kind == "turn":
            self.loads = dict(a=plain("a1_"), cot=r.cotangent.at[self.micro, 0])
            self.saves = dict(cot=plain("gz1_"))
        elif kind == "back":
            self.loads = dict(gz=plain("gz1_"), h=r.cotangent.at[self.micro, 0], a=plain("a1_"), dg=plain("dg0_"))
            self.saves = dict(h=plain("ga1_"), dg=plain("gz0_"))
        else:
            self.loads = dict(gz=plain("gz0_"), h=plain("ga1_"), a=r.inputs.at[self.micro, 0])
            self.saves = {}
        layer = 0 if kind in ("middle", "tail") else 1
        self.weight, self.bias = r.conv.at[layer if self.forward else 2 + layer], r.bias.at[layer]
        self.table = r.t_plain if kind == "middle" else r.t_doubled
        self.itable = r.it_doubled if self.forward else r.it_plain
        if not self.last:
            self.modes = Modes(section, r.p_buf, r.part.at[self.parity], r.p_local, r.p_cross.at[self.parity])
        if kind in ("turn", "tail"):
            self.bound = Bound(section, 1 if kind == "turn" else 0, self.micro, self.other,
                               self.buffers["a" if kind == "turn" else "h"], r.bound,
                               r.b_local.at[self.parity], r.b_cross.at[self.parity])

    def prefetch(self):
        for name, src in self.loads.items():
            if self.kind != "middle":
                fetch(src, self.buffers[name], self.sems[name])
        if self.forward:
            self.rid_copy().start()

    def rid_copy(self):
        return pltpu.make_async_copy(self.r.region.at[self.micro, 0], self.r.rid.at[self.parity],
                                     self.r.rid_sem.at[self.parity])

    def got(self, name):
        arrived(self.buffers[name], self.sems[name])

    def open(self):
        r, b = self.r, self.buffers
        if self.forward:
            r.eo[...] = jnp.zeros_like(r.eo)
            r.eb[...] = jnp.zeros_like(r.eb)
            if self.kind != "middle":
                self.got("a")
        else:
            for name in ("gz", "h", "a"):
                self.got(name)
            at = self.k - self.r.first_back
            r.cg[at] = jnp.zeros_like(r.cg[at])
            r.bg[at] = jnp.zeros_like(r.bg[at])

    def before(self, i):
        r, b = self.r, self.buffers
        a = b["a"]
        rows, channels = a.shape[:2]
        blocks, parts = rows // (self.weight.shape[0] // channels), self.n - 1
        span = (i * blocks // parts, (i + 1) * blocks // parts)
        if self.forward:
            conv_rows(self.weight, self.bias, a, b["z"], *span)
        else:
            conv_rows(self.weight, None, b["gz"], b["h"], *span)
            at = self.k - r.first_back
            grad_rows(a, b["gz"], r.cg.at[at], r.bg.at[at], i * rows // parts, (i + 1) * rows // parts)

    def outs(self, q):
        return [pltpu.make_async_copy(chunk_at(self.buffers[name], q, self.count), chunk_at(dst, q, self.count),
                                      self.r.out_sem.at[self.parity, i, q])
                for i, (name, dst) in enumerate(self.saves.items())]

    def late(self):
        for name in ("cot", "dg"):
            if name in self.loads:
                self.got(name)

    def chunk(self, q):
        r, b, count = self.r, self.buffers, self.count
        spectral = from_modes(self.gather.full.at[q].reshape(-1, count, self.lanes), self.itable[...], r.ikron[...],
                              r.spread)
        if self.forward:
            branch, slope = gelu_parts(spectral + chunk_of(b["z"], q, count))
            if self.kind == "turn":
                put(chunk_at(b["cot"], q, count), chunk_of(b["cot"], q, count) * slope)
            else:
                put(chunk_at(b["z"], q, count), slope)
            add_squares(branch, r.eb)
            out = chunk_of(b["a"], q, count) + branch
            put(chunk_at(b["a"], q, count), out)
            add_squares(out, r.eo)
            source = b["cot" if self.kind == "turn" else "a"]
        else:
            ga = spectral + chunk_of(b["h"], q, count)
            put(chunk_at(b["h"], q, count), ga)
            if not self.last:
                put(chunk_at(b["dg"], q, count), ga * chunk_of(b["dg"], q, count))
                source = b["dg"]
        for copy in self.outs(q):
            copy.start()
        if self.kind in ("turn", "tail"):
            self.bound.start(q, count)
        if not self.last:
            to_modes(chunk_of(source, q, count), self.table[...], r.kron[...], r.spread, self.modes.view(q))

            pl.when(q == self.chunks - 1)(self.gather.finish)
            self.modes.start(q)

    def end(self):
        if self.forward:
            self.rid_copy().wait()
            region_sums(self.r.rid.at[self.parity], self.r.eo, self.r.eb, self.r.stat.at[self.k])
        if self.last:
            self.gather.finish()

    def close(self):
        def body(q, carry):
            for copy in self.outs(q):
                copy.wait()
            if self.kind in ("turn", "tail"):
                self.bound.wait(q, self.count)
            return carry

        lax.fori_loop(0, self.chunks, body, 0)


def stages_kernel(per_core, kinds, places, mixes, r):
    section, z, n = place_and_peers()
    chunks, count = r.full.shape[1], r.full.shape[5]
    r.first_back = 2 * per_core
    stages = [Stage(k, kind, j, per_core, places[k], section, z, n, r)
              for k, (kind, j) in enumerate((kind, j) for kind in kinds for j in range(per_core))]
    heads = [Head(section * per_core + j, places[j]["a"], j, section, r) for j in range(per_core)]
    half = r.far.shape[0]

    def spare(q, x):
        groups = r.fields.shape[1] // count
        at = q * half + x
        place, at = 3 + at // (2 * groups), at % (2 * groups)
        side, group = at // groups, at % groups
        return r.fields.at[place, pl.ds(pl.multiple_of(group * count, count), count), :,
                           pl.ds(pl.multiple_of(side * 128, 128), 128)]

    def lend_in(q, x):
        rows = pl.ds(q * count, count)
        return pltpu.make_async_copy(r.weights.at[0, (1 - section) * half + x, rows], spare(q, x), r.w_load.at[q, x])

    def lent(q, x):
        return to_core(spare(q, x), r.far.at[x, pl.ds(q * count, count)],
                       (r.w_cross.at[0, q, x], r.w_cross.at[1, q, x]), section)

    blocks = [(q, x) for q in range(chunks) for x in range(half)]
    for head in heads:
        head.fetch()
    for block in blocks:
        lend_in(*block).start()
    greet(section, z, n, True, lax.axis_size("batch"))
    ahead, sums = [Sum(section, z, n, r, j, heads[j].modes.wait) for j in range(2)]
    mix = Mix(section, z, *mixes[0], ahead, stages[0].gather, r, lent)
    heads[0].got()

    def opening(q, carry):
        ahead.tick(q - 1)
        heads[0].chunk(q)

        @pl.when(q == 0)
        def _():
            for block in blocks:
                lend_in(*block).wait()
                lent(*block).start()

        return carry

    lax.fori_loop(0, chunks, opening, 0)
    heads[1].got()
    mix.prime()

    def second(q, carry):
        ahead.tick(q + chunks - 1)

        @pl.when(q < chunks)
        def _():
            heads[1].chunk(q)

        sums.tick(q - 1)
        pl.when(within(q + chunks - n, chunks))(lambda: mix.chunk(q + chunks - n))
        return carry

    lax.fori_loop(0, n, second, 0)
    ahead.finish()
    mix.finish()
    shares = [Share(r, 0, 0)]
    shares[0].start()
    for block in blocks:
        lent(*block).wait_send()
    stages[0].prefetch()
    for k, stage in enumerate(stages):
        gather = stage.gather
        now = None if stage.last else Sum(section, z, n, r, stage.parity, stage.modes.wait)
        mix = None
        if sums is not None:
            mix = Mix(section, z, *mixes[(k + 1) // per_core], sums, stages[k + 1].gather, r)
            share = Share(r, k + 1, 1 - stage.parity)
            if k >= 1:
                shares[k - 1].wait_send()
            shares.append(share)
            mix.prime()
        lead = n - 1 if k == 0 else chunks - 1
        ready = n - 1 - lead
        gather.begin()
        stage.open()

        def early(i, carry):
            if sums is not None:
                sums.tick(i + lead)
            gather.tick(i)
            stage.before(i)
            if mix is not None and not mix.flip:
                pl.when(within(i - ready, chunks))(lambda: mix.chunk(i - ready))
            return carry

        lax.fori_loop(0, n - 1, early, 0)
        if k > 0:
            stages[k - 1].close()
        if k + 1 < len(stages):
            stages[k + 1].prefetch()
        stage.late()

        def later(q, carry):
            i = q + n - 1
            if sums is not None:
                sums.tick(i + lead)
            if now is not None:
                now.tick(i - n)
            gather.tick(i)
            stage.chunk(q)
            if mix is not None:
                if mix.flip:
                    pl.when(q == 0)(sums.finish)
                    mix.chunk(q)
                else:
                    pl.when(within(i - ready, chunks))(lambda: mix.chunk(i - ready))
            return carry

        lax.fori_loop(0, chunks, later, 0)
        if mix is not None:
            if not mix.flip:
                sums.finish()
            mix.finish()
            share.start()
        stage.end()
        sums = now
    stages[-1].close()
    for share in shares[-2:]:
        share.wait_send()
    for share in shares:
        share.wait_recv()


def swap_halves(value):
    return pltpu.roll(value, value.shape[-1] // 2, value.ndim - 1)


def left_lanes(shape):
    return lax.broadcasted_iota(jnp.int32, shape, len(shape) - 1) < shape[-1] // 2


def pieces(array):
    return [array[at:at + G] for at in range(0, array.shape[0], G)]


def spread_row(ref, row):
    return ref[pl.ds(row, G, stride=0), :]


class Mix:
    def __init__(self, section, z, layer, flip, sums, gather, r, lent=None):
        self.lent = lent
        self.section, self.z, self.layer, self.flip, self.r = section, z, layer, flip, r
        self.sums, self.gather = sums, gather
        self.chunks, self.grids, self.half, self.count, self.lanes = sums.part.shape[1:]
        self.channels, self.slots = r.weights.shape[2], r.wbuf.shape[0]
        self.blocks = self.chunks * self.half

    def begin(self, block):
        q, x = block // self.half, block % self.half
        slot = lax.rem(block, self.slots)
        rows = pl.ds(q * self.count, self.count)
        if self.lent is not None:
            self.lent(q, x).wait_recv()

        @pl.when(self.section == self.layer)
        def _():
            pltpu.make_async_copy(self.r.weights.at[0, self.section * self.half + x, rows], self.r.wbuf.at[slot],
                                  self.r.wsem.at[slot]).start()

        @pl.when(self.section != self.layer)
        def _():
            pltpu.make_async_copy(self.r.far.at[x, rows], self.r.wbuf.at[slot], self.r.wsem.at[slot]).start()

    def prime(self):
        for block in range(min(self.slots, self.blocks)):
            self.begin(jnp.int32(block))
        if not self.flip:
            self.r.macc[...] = jnp.zeros_like(self.r.macc)

    def chunk(self, q):
        def body(x, carry):
            block = q * self.half + x
            slot = lax.rem(block, self.slots)
            weight = self.r.wbuf.at[slot]
            arrived(weight, self.r.wsem.at[slot])
            (self.transposed if self.flip else self.forward)(q, x, weight)

            @pl.when(block + self.slots < self.blocks)
            def _():
                self.begin(block + self.slots)

            return carry

        lax.fori_loop(0, self.half, body, 0)
        if self.flip:
            self.gather.give(q)

    def forward(self, q, x, weight):
        sides, groups = 2 * self.grids, self.channels // G
        total, source = self.r.macc.at[x], self.r.msrc
        for g in range(self.grids):
            value = self.sums.part[self.z, q, g, x]
            source[2 * g, :self.count] = value
            source[2 * g + 1, :self.count] = swap_halves(value)
        keys = [(k, o) for k in range(sides) for o in range(groups)]

        def body(octet, acc):
            acc = dict(zip(keys, acc))
            for u in range(G):
                i = octet * G + u
                rows = [spread_row(source.at[k], i) for k in range(sides)]
                for o in range(groups):
                    w = weight[i, o * G:(o + 1) * G, :]
                    for k in range(sides):
                        acc[k, o] = acc[k, o] + rows[k] * w
            return tuple(acc[key] for key in keys)

        acc = lax.fori_loop(0, self.count // G, body, tuple(total[k, o * G:(o + 1) * G, :] for k, o in keys))
        for key, value in zip(keys, acc):
            total[key[0], key[1] * G:(key[1] + 1) * G, :] = value

    def transposed(self, q, x, weight):
        sides, groups = 2 * self.grids, self.channels // G
        source = self.r.msrc
        for g in range(self.grids):
            value = jnp.concatenate([self.sums.part[self.z, at, g, x] for at in range(self.chunks)], 0)
            source[2 * g] = value
            source[2 * g + 1] = swap_halves(value)
        rows = [pieces(source[k]) for k in range(sides)]
        out = [[] for _ in range(sides)]
        for i in range(self.count):
            total = [None] * sides
            for o in range(groups):
                w = weight[i, o * G:(o + 1) * G, :]
                for k in range(sides):
                    term = w * rows[k][o]
                    total[k] = term if total[k] is None else total[k] + term
            for k in range(sides):
                out[k].append(jnp.sum(total[k], axis=0, keepdims=True))
        left = left_lanes((self.count, self.lanes))
        for g in range(self.grids):
            a, b = [jnp.concatenate(out[2 * g + side], 0) for side in range(2)]
            self.put(g, q, x, jnp.where(left, a + swap_halves(a), swap_halves(b) - b))

    def put(self, g, q, x, value):
        if g == 0:
            self.gather.full[q, self.z, self.section, x] = value
        else:
            self.gather.give_from[q, x] = value

    def finish(self):
        if self.flip:
            return
        left = left_lanes((self.channels, self.lanes))

        def body(x, carry):
            for g in range(self.grids):
                a, b = [self.r.macc[x, 2 * g + side] for side in range(2)]
                result = jnp.where(left, a - swap_halves(a), b + swap_halves(b))
                for q in range(self.chunks):
                    self.put(g, q, x, result[q * self.count:(q + 1) * self.count])
            return carry

        lax.fori_loop(0, self.half, body, 0)
        for q in range(self.chunks):
            self.gather.give(q)


def gather_columns(f_ref, d_ref, left_of, right_of):
    channels = f_ref.shape[2] * f_ref.shape[5]
    lanes = f_ref.shape[6]
    left = left_lanes((channels, lanes))
    for stream in range(f_ref.shape[0]):
        for member in range(f_ref.shape[1]):
            for g in range(f_ref.shape[3]):
                at = (stream * f_ref.shape[1] + member) * f_ref.shape[3] + g
                both = []
                for x in range(2):
                    f = f_ref[stream, member, :, g, x].reshape(channels, lanes)
                    turned = swap_halves(f)
                    left_of[x, at] = jnp.concatenate([f, jnp.where(left, -turned, turned)], 0).T
                    both.append(d_ref[stream, member, :, g, x].reshape(channels, lanes))
                right_of[at] = jnp.concatenate(both, 0).T


def column_products(left_of, right_of, product):
    grids, double, lanes = right_of.shape
    half = double // 2
    left = left_lanes((2 * grids, lanes))
    rows = right_of.reshape(grids * double, lanes)
    sides = [left_of.at[x].reshape(grids * double, lanes) for x in range(2)]

    def body(k, carry):
        pick = pl.ds(k, 2 * grids, stride=half)
        d = rows[pick, :]
        f_high, f_low = split(jnp.concatenate([side[pick, :] for side in sides], 0))
        d_high, d_low = split(jnp.concatenate([jnp.where(left, d, 0.0), jnp.where(left, 0.0, d)], 0))
        product[k] = dot(jnp.concatenate([f_high, f_low, f_high], 0), jnp.concatenate([d_high, d_high, d_low], 0),
                         (((0,), (0,)), ((), ())))
        return carry

    lax.fori_loop(0, half, body, 0, unroll=4)


def product_rows(product, first, out):
    half, double, lanes = product.shape
    channels = double // 2
    rows = product.reshape(half * double, lanes)

    def body(i, carry):
        parts = [rows[pl.ds(part * channels + first + i, half, stride=double), :] for part in range(2)]
        tile = jnp.concatenate(parts, 0).T
        for x in range(2):
            out[x, i] = tile[x * channels:(x + 1) * channels]
        return carry

    lax.fori_loop(0, out.shape[1], body, 0, unroll=4)


class GradInput:
    def __init__(self, first, f, g, fbuf, gbuf, sem):
        self.first, self.f, self.g, self.fbuf, self.gbuf, self.sem = first, f, g, fbuf, gbuf, sem

    def load(self, x, slot):
        for layer, condition in enumerate((self.first, jnp.logical_not(self.first))):
            @pl.when(condition)
            def _():
                for j in range(len(self.f[layer])):
                    pltpu.make_async_copy(self.f[layer][j].at[:, :, :, pl.ds(2 * x, 2)], self.fbuf.at[slot, j],
                                          self.sem.at[0, slot]).start()
                    pltpu.make_async_copy(self.g[layer][j].at[:, :, :, pl.ds(2 * x, 2)], self.gbuf.at[slot, j],
                                          self.sem.at[1, slot]).start()

    def next(self, x, count):
        slot = lax.rem(x, 2)

        @pl.when(x + 1 < count)
        def _():
            self.load(x + 1, 1 - slot)

        arrived(self.fbuf.at[slot], self.sem.at[0, slot])
        arrived(self.gbuf.at[slot], self.sem.at[1, slot])
        return self.fbuf.at[slot], self.gbuf.at[slot]


def grad_input(r, first, per_core):
    f = [[getattr(r, f"f{layer}{j}") for j in range(per_core)] for layer in range(2)]
    g = [[getattr(r, f"g{layer}{j}") for j in range(per_core)] for layer in range(2)]
    return GradInput(first, f, g, r.fbuf, r.gbuf, r.in_sem)


def far_grad_kernel(per_core, r):
    section, z, n = place_and_peers()
    pairs, block = r.far.shape[0] // 2, r.out.shape[2]
    blocks = r.far.shape[1] // block
    source = grad_input(r, section != 0, per_core)

    def move(k, slot):
        p, i = k // blocks, k % blocks
        return to_core(r.out.at[slot], r.far.at[pl.ds(2 * p, 2), pl.ds(i * block, block)], (r.send.at[k], r.recv.at[k]),
                       section)

    source.load(0, 0)
    greet(section, z, n, False)

    def body(p, carry):
        gather_columns(*source.next(p, pairs), r.left_of, r.right_of)
        column_products(r.left_of, r.right_of, r.product)

        def inner(i, carry):
            k = p * blocks + i

            @pl.when(k >= 2)
            def _():
                move(k - 2, lax.rem(k, 2)).wait_send()

            product_rows(r.product, i * block, r.out.at[lax.rem(k, 2)])
            move(k, lax.rem(k, 2)).start()
            return carry

        return lax.fori_loop(0, blocks, inner, carry)

    lax.fori_loop(0, pairs, body, 0)
    total = pairs * blocks
    for k in (total - 2, total - 1):
        move(k, k % 2).wait_send()

    def close(k, carry):
        move(k, 0).wait_recv()
        return carry

    lax.fori_loop(0, total, close, 0)


def own_grad_kernel(names, per_core, m_ref, *refs):
    r = types.SimpleNamespace(**dict(zip(names, refs)))
    p, i = pl.program_id(0), pl.program_id(1)
    source = grad_input(r, m_ref[0] == 0, per_core)

    @pl.when(i == 0)
    def _():
        @pl.when(p == 0)
        def _():
            source.load(0, 0)

        gather_columns(*source.next(p, pl.num_programs(0)), r.left_of, r.right_of)
        column_products(r.left_of, r.right_of, r.product)

    block = r.out.shape[2]

    @pl.when(i == pl.num_programs(1) - 1)
    def _():
        r.bound_out[...] = r.bound_in[...]

    r.out[1 - m_ref[0]] = r.far[:, pl.ds(pl.multiple_of(i * block, block), block)]
    product_rows(r.product, i * block, r.out.at[m_ref[0]])


def whole(array):
    return pl.BlockSpec(array.shape, lambda *_: (0,) * array.ndim)


def params(**kw):
    return pltpu.CompilerParams(vmem_limit_bytes=VMEM_LIMIT, **kw)


def local(inputs, cotangent, region_id, spectral_w, conv_w, bias_vector):
    micro_count, _, rows_dev, channels, width = inputs.shape
    lanes = spectral_w.shape[-1]
    half = lanes // 2
    kx_dev = spectral_w.shape[1]
    row_devices, sections = lax.axis_size("rows"), lax.axis_size("section")
    mode_rows, height = kx_dev * row_devices, rows_dev * row_devices
    section = lax.axis_index("section")
    per_core = micro_count // sections
    kx_half = kx_dev // sections

    plain, doubled = col_tables(width, half)

    def stacked(array):
        high, low = np_split(array)
        return np.concatenate([high, high, low], 0)

    t_plain, t_doubled, it_plain, it_doubled = [stacked(t) for t in (plain, doubled, plain.T, doubled.T)]
    kron, ikron = row_tables(height, mode_rows, lax.axis_index("rows") * rows_dev, rows_dev)

    count = 2 * G
    chunks = channels // count
    hbm, vmem = pl.BlockSpec(memory_space=pl.ANY), pl.BlockSpec(memory_space=pltpu.VMEM)
    field_shape = jax.ShapeDtypeStruct((rows_dev, channels, width), F32)
    part_dims = (row_devices, chunks, sections, kx_half, count, lanes)
    p_shape, f_shape = jax.ShapeDtypeStruct(part_dims, F32), jax.ShapeDtypeStruct(part_dims[1:], F32)
    y_shape = jax.ShapeDtypeStruct((sections, chunks, kx_half, count, lanes), F32)
    stat_shape = jax.ShapeDtypeStruct((3, R, 128), F32)
    cg_shape = jax.ShapeDtypeStruct((2 * channels, 2 * channels), F32)
    bg_shape = jax.ShapeDtypeStruct((channels, width), F32)
    bound_shape = jax.ShapeDtypeStruct((micro_count, rows_dev, channels, width), F32)
    dma = pltpu.SemaphoreType.DMA
    field_buf = pltpu.VMEM((rows_dev, channels, width), F32)
    full_dims = (chunks, row_devices, sections, kx_half, count, lanes)
    spread = pltpu.VMEM((width // 128, rows_dev * count, 128), F32)
    energy = pltpu.VMEM((rows_dev, G, width), F32)
    line_sems = dma((2, chunks, row_devices))
    def run(body, ident, ins, outs, scratch, cost=50, aliases=None):
        names = [*ins, *outs, *scratch]
        spec = lambda entry: vmem if isinstance(entry, tuple) else hbm
        plain = lambda entry: entry[0] if isinstance(entry, tuple) else entry
        kernel = lambda *refs: body(types.SimpleNamespace(**dict(zip(names, refs))))
        positions = {list(ins).index(k): list(outs).index(v) for k, v in (aliases or {}).items()}
        result = pl.pallas_call(
            kernel, in_specs=[spec(e) for e in ins.values()], out_specs=[spec(e) for e in outs.values()],
            out_shape=[plain(e) for e in outs.values()], scratch_shapes=list(scratch.values()),
            input_output_aliases=positions,
            cost_estimate=pl.CostEstimate(flops=0, bytes_accessed=cost * 3_000_000, transcendentals=0),
            compiler_params=params(collective_id=ident, has_side_effects=True))(*[plain(e) for e in ins.values()])
        return types.SimpleNamespace(**dict(zip(outs, result)))

    conv_rows_at_once = 256 // channels
    conv_both = lax.all_gather(conv_w, "section", axis=0, tiled=True)
    bias_both = lax.all_gather(bias_vector, "section", axis=0, tiled=True)

    maps = jnp.concatenate([jnp.swapaxes(conv_both, 1, 2), conv_both], 0)
    at = np.arange(conv_rows_at_once * channels) // channels
    wide = jnp.where(at[:, None] == at[None, :], jnp.tile(maps, (1, conv_rows_at_once, conv_rows_at_once)), 0.0)
    rounded = lax.reduce_precision(wide, 8, 7)
    high, low = rounded.astype(BF16), (wide - rounded).astype(BF16)
    conv_tables = jnp.concatenate([high, low, high], 2)
    bias_wide = jnp.broadcast_to(bias_both[:, :, None], (2, channels, width))

    streams = range(per_core)
    members = lax.axis_size("batch")
    kinds = ["middle", "turn", "back", "tail"]
    mixes = [(0, False), (1, False), (1, True), (0, True)]
    names = ["f00", "f01", "f10", "f11", "g10", "g11", "g00", "g01"]
    places = [dict(a=0, z=1), dict(a=2, z=3), dict(a=4, z=5, cot=6), dict(a=0, z=1, cot=2),
              dict(gz=3, a=4, h=5, dg=6), dict(gz=0, a=1, h=2, dg=3), dict(gz=4, a=5, h=6), dict(gz=0, a=1, h=2)]
    both = (2,)
    ins = dict(inputs=inputs, cotangent=cotangent, region=region_id, weights=spectral_w, t_plain=(t_plain,),
               t_doubled=(t_doubled,), it_plain=(it_plain,), it_doubled=(it_doubled,), kron=(kron,), ikron=(ikron,),
               conv=(conv_tables,), bias=(bias_wide,))
    outs = dict(far=jax.ShapeDtypeStruct((kx_half,) + spectral_w.shape[2:], F32), bound=bound_shape, stat=(jax.ShapeDtypeStruct((2 * per_core,) + stat_shape.shape, F32),),
                cg=(jax.ShapeDtypeStruct((2 * per_core,) + cg_shape.shape, F32),),
                bg=(jax.ShapeDtypeStruct((2 * per_core,) + bg_shape.shape, F32),),
                **{f"{name}{j}": field_shape for name in ("a1_", "dg0_", "gz1_", "ga1_", "gz0_") for j in streams},
                **{f"shared{i}": jax.ShapeDtypeStruct((members,) + f_shape.shape, F32) for i in range(len(names))})
    scratch = dict(
        fields=pltpu.VMEM((7,) + field_shape.shape, F32), full=pltpu.VMEM(both + full_dims, F32),
        part=pltpu.VMEM(both + part_dims, F32),
        come=pltpu.VMEM(both + (2, chunks, row_devices - 1) + part_dims[2:], F32),
        keep=pltpu.VMEM(both + f_shape.shape, F32), y_give=pltpu.VMEM(both + y_shape.shape[1:], F32),
        p_buf=pltpu.VMEM(full_dims, F32), spread=spread, eo=energy, eb=energy,
        rid=pltpu.VMEM((2, rows_dev, width), jnp.int32),
        wbuf=pltpu.VMEM((6, count, channels, lanes), F32), macc=pltpu.VMEM((kx_half, 2 * sections, channels, lanes), F32),
        msrc=pltpu.VMEM((2 * sections, channels, lanes), F32),
        field_sem=dma((7,)), rid_sem=dma(both), out_sem=dma((2, 2, chunks)), wsem=dma((6,)), w_load=dma((chunks, kx_half)), w_cross=dma((2, chunks, kx_half)),
        send=dma(both + (2, chunks, row_devices)), recv=dma(both + (2, chunks, row_devices)),
        red_send=dma(both + (2, chunks, row_devices)), red_recv=dma(both + (2, chunks, row_devices)),
        y_cross=dma((2, 2, chunks)), p_local=dma((chunks,)), p_cross=dma((2, 2, chunks)),
        b_local=dma((2, chunks)), b_cross=dma((2, 2, chunks)),
        s_local=dma(both), s_send=dma((2, members)), s_recv=dma((len(names), members)))
    done = run(functools.partial(stages_kernel, per_core, kinds, places, mixes), 0, ins, outs, scratch, cost=400)
    gathered = {name: getattr(done, f"shared{i}") for i, name in enumerate(names)}
    bound, calls = done.bound, 0

    grids = per_core * members * sections
    block = 2 * G
    pairs, blocks = kx_half // 2, channels // block
    in_buf = pltpu.VMEM((2, per_core, members, chunks, sections, 2, count, lanes), F32)
    grad_scratch = dict(fbuf=in_buf, gbuf=in_buf, in_sem=dma((2, 2)), left_of=pltpu.VMEM((2, grids, lanes, lanes), F32),
                        right_of=pltpu.VMEM((grids, lanes, lanes), F32), product=pltpu.VMEM((half, lanes, lanes), F32))
    far_grad = run(functools.partial(far_grad_kernel, per_core), 1 + calls, gathered,
                   dict(far=jax.ShapeDtypeStruct((kx_half, channels, channels, lanes), F32)),
                   dict(out=pltpu.VMEM((2, 2, block, channels, lanes), F32), send=dma((pairs * blocks,)),
                        recv=dma((pairs * blocks,)), **grad_scratch)).far
    bound_rows = bound.reshape(micro_count * rows_dev, channels, width)
    bound_block = pl.BlockSpec((bound_rows.shape[0] // pairs, channels, width), lambda p, i, m: (p, 0, 0))
    grid_spec = pltpu.PrefetchScalarGridSpec(
        num_scalar_prefetch=1, grid=(pairs, blocks),
        in_specs=[hbm] * len(gathered)
        + [pl.BlockSpec((2, channels, channels, lanes), lambda p, i, m: (p, 0, 0, 0)), bound_block],
        out_specs=[pl.BlockSpec((2, 2, block, channels, lanes), lambda p, i, m: (0, p, i, 0, 0)), bound_block],
        scratch_shapes=list(grad_scratch.values()))
    spectral_grad, boundary = pl.pallas_call(
        functools.partial(own_grad_kernel, [*gathered, "far", "bound_in", "out", "bound_out", *grad_scratch], per_core),
        grid_spec=grid_spec, out_shape=[jax.ShapeDtypeStruct((2, kx_half, channels, channels, lanes), F32),
                                        jax.ShapeDtypeStruct(bound_rows.shape, F32)],
        cost_estimate=pl.CostEstimate(flops=0, bytes_accessed=150_000_000, transcendentals=0),
        compiler_params=params())(
            jnp.reshape(section, (1,)).astype(jnp.int32), *gathered.values(), far_grad, bound_rows)
    spectral_grad = spectral_grad.reshape(spectral_w.shape)
    boundary = boundary.reshape((1, micro_count, 1) + inputs.shape[2:])

    def lower(value):
        return (value[:channels, :channels] + value[channels:, channels:]
                + value[:channels, channels:] + value[channels:, :channels])

    pair = lambda value: jnp.sum(value.reshape((2, per_core) + value.shape[1:]), 1)
    conv_local = jnp.stack([lower(value) for value in pair(done.cg)[::-1]])
    bias_local = jnp.sum(pair(done.bg)[::-1], -1)
    stat_local = jnp.sum(pair(done.stat), -1)
    shapes = [v.shape for v in (conv_local, bias_local, stat_local)]
    flat_sums = jnp.concatenate([v.reshape(-1) for v in (conv_local, bias_local, stat_local)])
    length = flat_sums.shape[0]
    flat_sums = jnp.pad(flat_sums, (0, -length % 1024)).reshape(-1, 128)
    flat_sums = jnp.sum(lax.all_gather(flat_sums, ("section", "batch", "rows"), axis=0), 0).reshape(-1)
    ends = np.cumsum([0] + [math.prod(shape) for shape in shapes])
    conv_sum, bias_sum, stat_sum = [flat_sums[ends[i]:ends[i + 1]].reshape(shapes[i]) for i in range(3)]
    own_stat = lax.dynamic_index_in_dim(stat_sum, section, 0, False)
    layer_rms = jnp.sqrt(own_stat[:2] / (channels * own_stat[2])[None, :] + 1e-06)[None]
    own = lambda value: lax.dynamic_slice_in_dim(value, section, 1, 0)
    return boundary, spectral_grad, own(conv_sum), own(bias_sum), layer_rms


def solution(mesh):
    placed = (
        P(None, "batch", "rows", None, None),
        P(None, "batch", "rows", None, None),
        P(None, "batch", "rows", None),
        P("section", "rows", None, None, None),
        P("section", None, None),
        P("section", None),
    )
    return jax.shard_map(
        local,
        mesh=mesh,
        in_specs=placed,
        out_specs=(
            P("section", None, "batch", "rows", None, None),
            P("section", "rows", None, None, None),
            P("section", None, None),
            P("section", None),
            P("section", None, None),
        ),
        check_vma=False,
    )
```

```python
import functools
import math
import types

import jax
import jax.numpy as jnp
import numpy as np
from jax import lax
from jax.experimental import pallas as pl
from jax.experimental.pallas import tpu as pltpu
from jax.sharding import PartitionSpec as P

R = 8
G = 8
AHEAD = 2
F32 = jnp.float32
BF16 = jnp.bfloat16
VMEM_LIMIT = 62 * 1024 * 1024
MESH = pl.DeviceIdType.MESH


def split(value):
    high = value.astype(BF16)
    return high, (value - high.astype(F32)).astype(BF16)


def dot(left, right, dims=(((1,), (0,)), ((), ()))):
    return lax.dot_general(left, right, dims, preferred_element_type=F32)


def dot3(left, right):
    return dot(left[0], right[0]) + (dot(left[1], right[0]) + dot(left[0], right[1]))


def np_split(value):
    high = value.astype(np.float32).astype(BF16)
    return high, (value - high.astype(np.float64)).astype(np.float32).astype(BF16)


def col_tables(width, half):
    phase = 2.0 * math.pi / width * (np.outer(np.arange(width), np.arange(half)) % width)
    cosine, sine = np.cos(phase) / math.sqrt(width), np.sin(phase) / math.sqrt(width)
    plain = np.concatenate([cosine, -sine, -sine, -cosine], 1)
    doubled = plain * np.tile(np.where(np.arange(half) == 0, 1.0, 2.0), 4)[None, :]
    return plain, doubled


def row_tables(height, mode_rows, first_row, rows_dev):
    position = jnp.arange(mode_rows, dtype=jnp.int32)
    frequency = jnp.where(position < mode_rows // 2, position, height - mode_rows + position)
    row = first_row + jnp.arange(rows_dev, dtype=jnp.int32)
    phase = 2.0 * math.pi / height * (frequency[:, None] * row[None, :] % height).astype(F32)
    small = jnp.concatenate([jnp.cos(phase), jnp.sin(phase)], 1) / math.sqrt(height)
    rounded = lax.reduce_precision(small, 8, 7)
    high, low = rounded.astype(BF16), (small - rounded).astype(BF16)
    forward = jnp.concatenate([jnp.concatenate([high, high], 1), jnp.concatenate([low, jnp.zeros_like(low)], 1)], 0)
    inverse = jnp.concatenate([high.T, high.T, low.T], 1)
    return forward, inverse


def to_modes(value, table, kron, spread, p_ref):
    mode_rows, count, lanes = p_ref.shape
    rows = value.shape[0] // count
    high, low = split(value)
    spectra = dot(jnp.concatenate([high, low, high], 1), table)
    for i in range(2):
        spread[i] = spectra[:, i * lanes:(i + 1) * lanes]
    out = p_ref.reshape(mode_rows * count, lanes)
    for first in range(0, count, 2):
        sides = []
        for c in (first, first + 1):
            pick = pl.ds(c, rows, stride=count)
            sides.append(jnp.concatenate([spread[i, pick, :] for i in range(2)], 0))
        high, low = split(jnp.concatenate(sides, 1))
        both = dot(kron, jnp.concatenate([high, low], 0))
        result = both[:mode_rows] + both[mode_rows:]
        for i in range(2):
            out[pl.ds(first + i, mode_rows, stride=count), :] = result[:, i * lanes:(i + 1) * lanes]


def from_modes(y_ref, table, kron, spread):
    mode_rows, count, lanes = y_ref.shape
    rows, pieces = spread.shape[1] // count, spread.shape[0]
    modes = y_ref.reshape(mode_rows * count, lanes)
    sides = []
    for first in range(0, count, 2):
        pair = [modes[pl.ds(c, mode_rows, stride=count), :] for c in (first, first + 1)]
        high, low = split(jnp.concatenate(pair, 1))
        both = dot(kron, jnp.concatenate([high, low, high], 0))
        for i in range(2):
            side = both[:, i * lanes:(i + 1) * lanes]
            sides.append(jnp.concatenate([side[:rows], side[rows:]], 1))
    high, low = split(jnp.concatenate(sides, 0))
    out = dot(jnp.concatenate([high, low, high], 1), table)
    for c in range(count):
        for i in range(pieces):
            spread[i, pl.ds(c, rows, stride=count), :] = out[c * rows:(c + 1) * rows, i * 128:(i + 1) * 128]
    return jnp.concatenate([spread[i] for i in range(pieces)], 1)


def gelu_parts(z):
    gauss = jnp.exp2((-0.5 / math.log(2.0)) * (z * z))
    base = 1.0 + (0.3275911 / math.sqrt(2.0)) * jnp.abs(z)
    t = pl.reciprocal(base, approx=True)
    t = t * (2.0 - base * t)
    poly = t * (0.127414796 + t * (-0.142248368 + t * (0.7107068705 + t * (-0.7265760135 + t * 0.5307027145))))
    tail = poly * gauss
    phi = jnp.where(z >= 0, 1.0 - tail, tail)
    return z * phi, phi + z * (gauss * (1.0 / math.sqrt(2.0 * math.pi)))


def flat(ref):
    rows, count, width = ref.shape
    return ref[...].reshape(rows * count, width)


def put(ref, value):
    ref[...] = value.reshape(ref.shape)


def place_and_peers():
    section, z = lax.axis_index("section"), lax.axis_index("rows")
    return section, z, lax.axis_size("rows")


def greet(section, z, n, lines, members=0):
    barrier = pltpu.get_barrier_semaphore()
    pl.semaphore_signal(barrier, inc=1, device_id={"section": 1 - section}, device_id_type=MESH)
    if not lines:
        pl.semaphore_wait(barrier, 1)
        return

    @pl.when(z > 0)
    def _():
        pl.semaphore_signal(barrier, inc=1, device_id={"rows": z - 1}, device_id_type=MESH)

    @pl.when(z < n - 1)
    def _():
        pl.semaphore_signal(barrier, inc=1, device_id={"rows": z + 1}, device_id_type=MESH)

    for away in range(1, members):
        pl.semaphore_signal(barrier, inc=1, device_id={"batch": lax.rem(lax.axis_index("batch") + away, members)},
                            device_id_type=MESH)

    others = 1 + max(members - 1, 0)
    pl.semaphore_wait(barrier, others + (z > 0).astype(jnp.int32) + (z < n - 1).astype(jnp.int32))


def to_core(src, dst, sems, section):
    return pltpu.make_async_remote_copy(src_ref=src, dst_ref=dst, send_sem=sems[0], recv_sem=sems[1],
                                        device_id={"section": 1 - section}, device_id_type=MESH)


def guard(condition, body):
    if isinstance(condition, (bool, np.bool_)):
        if condition:
            body()
    else:
        pl.when(condition)(body)


class Line:
    def __init__(self, section, z, n, chunks, send, recv):
        self.section, self.z, self.n, self.chunks = section, z, n, chunks
        self.send, self.recv = send, recv

    def move(self, way, q, hop, src, dst):
        return pltpu.make_async_remote_copy(
            src_ref=src, dst_ref=dst, send_sem=self.send.at[way, q, hop], recv_sem=self.recv.at[way, q, hop],
            device_id={"rows": self.z + 1 if way == 0 else self.z - 1}, device_id_type=MESH)

    def sends(self, way):
        return self.z < self.n - 1 if way == 0 else self.z > 0

    def hears(self, way):
        return self.z > 0 if way == 0 else self.z < self.n - 1


def within(value, count):
    return jnp.logical_and(value >= 0, value < count)


class Gather(Line):
    def __init__(self, section, z, n, r, parity):
        super().__init__(section, z, n, r.full.shape[1], r.send.at[parity], r.recv.at[parity])
        self.full, self.give_from = r.full.at[parity], r.y_give.at[parity]
        self.cross = r.y_cross.at[parity]

    def swap(self, q):
        return to_core(self.give_from.at[q], self.full.at[q, self.z, self.section],
                       (self.cross.at[0, q], self.cross.at[1, q]), self.section)

    def give(self, q):
        self.swap(q).start()

    def hop(self, way, q, hop):
        piece = self.full.at[q, self.source(way, hop)]
        return self.move(way, q, hop, piece, piece)

    def source(self, way, hop):
        return self.z - hop if way == 0 else self.z + hop

    def known(self, way, hop):
        at = self.source(way, hop)
        return at >= 0 if way == 0 else at < self.n

    def own(self, q):
        self.swap(q).wait_recv()
        for way in range(2):
            @pl.when(self.sends(way))
            def _():
                self.hop(way, q, 0).start()

    def step(self, q, hop):
        for way in range(2):
            @pl.when(self.known(way, hop + 1))
            def _():
                piece = self.full.at[q, self.source(way, hop + 1)]
                self.move(way, q, hop, piece, piece).wait_recv()

                @pl.when(self.sends(way))
                def _():
                    self.hop(way, q, hop + 1).start()

    def begin(self):
        for q in range(min(AHEAD, self.chunks)):
            self.own(q)

    def tick(self, t):
        @pl.when(t + AHEAD < self.chunks)
        def _():
            self.own(t + AHEAD)

        for hop in range(self.n - 1):
            q = t - hop - 1
            pl.when(within(q, self.chunks))(functools.partial(self.step, q, hop))

    def finish(self):
        def body(q, carry):
            self.swap(q).wait_send()
            for way in range(2):
                for hop in range(self.n - 1):
                    @pl.when(jnp.logical_and(self.sends(way), self.known(way, hop)))
                    def _():
                        self.hop(way, q, hop).wait_send()
            return carry

        lax.fori_loop(0, self.chunks, body, 0)


class Sum(Line):
    def __init__(self, section, z, n, r, parity, admit):
        super().__init__(section, z, n, r.part.shape[2], r.red_send.at[parity], r.red_recv.at[parity])
        self.part, self.come, self.keep, self.admit = r.part.at[parity], r.come.at[parity], r.keep.at[parity], admit

    def owner(self, way, hop):
        return self.z + self.n - hop if way == 0 else self.z - self.n + hop

    def valid(self, way, hop):
        return self.z <= hop - 1 if way == 0 else self.z >= self.n - hop

    def sent(self, way, q, hop):
        return self.move(way, q, hop, self.part.at[self.owner(way, hop), q], self.come.at[way, q, hop - 1])

    def heard(self, way, q, hop):
        come = self.come.at[way, q, hop - 1]
        self.move(way, q, hop, come, come).wait_recv()

    def first(self, q):
        self.admit(q)
        for way in range(2):
            @pl.when(jnp.logical_not(self.hears(way)))
            def _():
                for hop in range(1, self.n):
                    @pl.when(self.valid(way, hop))
                    def _():
                        self.sent(way, q, hop).start()

    def step(self, q, hop):
        for way in range(2):
            @pl.when(jnp.logical_and(self.valid(way, hop), self.hears(way)))
            def _():
                self.heard(way, q, hop - 1)
                owner = self.owner(way, hop)
                self.part[owner, q] = self.part[owner, q] + self.come[way, q, hop - 2]
                self.sent(way, q, hop).start()

    def final(self, q):
        for way in range(2):
            @pl.when(self.hears(way))
            def _():
                self.heard(way, q, self.n - 1)
                self.part[self.z, q] = self.part[self.z, q] + self.come[way, q, self.n - 2]

        self.keep[q] = self.part[self.z, q]

    def tick(self, t):
        pl.when(within(t, self.chunks))(functools.partial(self.first, t))
        for hop in range(2, self.n + 1):
            q = t - hop + 1
            pl.when(within(q, self.chunks))(
                functools.partial(self.step, q, hop) if hop < self.n else functools.partial(self.final, q))

    def finish(self):
        def body(q, carry):
            for way in range(2):
                for hop in range(1, self.n):
                    @pl.when(self.valid(way, hop))
                    def _():
                        self.sent(way, q, hop).wait_send()
            return carry

        lax.fori_loop(0, self.chunks, body, 0)


def fetch(src, dst, sem, parts=1):
    step = dst.shape[0] // parts
    for i in range(parts):
        pltpu.make_async_copy(src.at[pl.ds(i * step, step)], dst.at[pl.ds(i * step, step)], sem).start()


def arrived(dst, sem):
    pltpu.make_async_copy(dst, dst, sem).wait()


def portions(total, count):
    return [(i * total // count, (i + 1) * total // count) for i in range(count)]


def conv_rows(weight, bias, a, out, first, last):
    channels, width = a.shape[1:]
    block = weight.shape[0] // channels

    def body(i, carry):
        at = pl.ds(i * block, block)
        high, low = split(a[at].reshape(block * channels, width))
        result = dot(weight[...], jnp.concatenate([high, high, low], 0)).reshape(block, channels, width)
        out[at] = result + bias[...][None] if bias is not None else out[at] + result
        return carry

    lax.fori_loop(first, last, body, 0)


def grad_rows(a, gz, cg_ref, bg_ref, first, last):
    channels, width = a.shape[1:]

    def body(r, carry):
        grad, bias = carry
        g = gz[r]
        left = jnp.concatenate(split(a[r]), 0)
        right = jnp.concatenate(split(g), 0)
        return grad + dot(left, right, (((1,), (1,)), ((), ()))), bias + g

    grad, bias = lax.fori_loop(first, last, body, (cg_ref[...], bg_ref[...]))
    cg_ref[...] = grad
    bg_ref[...] = bias


def chunk_of(ref, q, count):
    rows, _, width = ref.shape
    return ref[:, pl.ds(pl.multiple_of(q * count, count), count), :].reshape(rows * count, width)


def chunk_at(ref, q, count):
    return ref.at[:, pl.ds(pl.multiple_of(q * count, count), count), :]


class Modes:
    def __init__(self, section, buffer, p_out, cross):
        self.section, self.buffer, self.p_out, self.cross = section, buffer, p_out, cross

    def view(self, q):
        n, halves, kx, count, lanes = self.buffer.shape[1:]
        return self.buffer.at[q].reshape(n * halves * kx, count, lanes)

    def cross_copy(self, q):
        return to_core(self.buffer.at[q, :, 1 - self.section], self.p_out.at[:, q, 1],
                       (self.cross.at[0, q], self.cross.at[1, q]), self.section)

    def start(self, q):
        self.cross_copy(q).start()
        self.p_out[:, q, 0] = self.buffer[q, :, self.section]

    def wait(self, q):
        self.cross_copy(q).wait()


class Bound:
    def __init__(self, section, owner, micro, other, source, bound, local, cross):
        self.section, self.owner, self.micro, self.other = section, owner, micro, other
        self.source, self.bound, self.local, self.cross = source, bound, local, cross

    def copies(self, q, count, micro):
        src, dst = chunk_at(self.source, q, count), chunk_at(self.bound.at[micro], q, count)
        return (pltpu.make_async_copy(src, dst, self.local.at[q]),
                to_core(src, dst, (self.cross.at[0, q], self.cross.at[1, q]), self.section))

    def start(self, q, count):
        here, there = self.copies(q, count, self.micro)

        @pl.when(self.section == self.owner)
        def _():
            here.start()

        @pl.when(self.section != self.owner)
        def _():
            there.start()

    def wait(self, q, count):
        here, there = self.copies(q, count, self.micro)
        come = self.copies(q, count, self.other)[1]

        @pl.when(self.section == self.owner)
        def _():
            here.wait()
            come.wait_recv()

        @pl.when(self.section != self.owner)
        def _():
            there.wait_send()


def add_squares(value, total):
    rows, _, width = total.shape
    square = (value * value).reshape(rows, -1, width)
    for at in range(0, square.shape[1], G):
        total[...] += square[:, at:at + G]


def region_sums(rid_ref, eo, eb, stat_ref):
    rows, _, width = eo.shape
    rid = rid_ref[...]
    energies = (jnp.sum(eo[...], axis=1), jnp.sum(eb[...], axis=1), jnp.ones((rows, width), F32))
    for kind in range(3):
        for region in range(R):
            line = jnp.sum(jnp.where(rid == region + 1, energies[kind], 0.0), axis=0, keepdims=True)
            total = line[:, :128]
            for piece in range(1, width // 128):
                total = total + line[:, piece * 128:(piece + 1) * 128]
            stat_ref[kind, region:region + 1, :] = total


class Share:
    def __init__(self, r, index, parity):
        self.r, self.index, self.parity = r, index, parity
        self.me, self.members = lax.axis_index("batch"), lax.axis_size("batch")

    def copies(self):
        source, target = self.r.keep.at[self.parity], getattr(self.r, f"shared{self.index}").at[self.me]
        yield pltpu.make_async_copy(source, target, self.r.s_local.at[self.parity])
        for away in range(1, self.members):
            yield pltpu.make_async_remote_copy(
                src_ref=source, dst_ref=target, send_sem=self.r.s_send.at[self.parity, away],
                recv_sem=self.r.s_recv.at[self.index, away],
                device_id={"batch": lax.rem(self.me + away, self.members)}, device_id_type=MESH)

    def start(self):
        for copy in self.copies():
            copy.start()

    def wait_send(self):
        for i, copy in enumerate(self.copies()):
            if i == 0:
                copy.wait()
            else:
                copy.wait_send()

    def wait_recv(self):
        for i, copy in enumerate(self.copies()):
            if i > 0:
                copy.wait_recv()


class Head:
    def __init__(self, micro, place, parity, section, r):
        self.r, self.field, self.sem = r, r.fields.at[place], r.field_sem.at[place]
        self.source, self.count = r.inputs.at[micro, 0], r.full.shape[5]
        self.modes = Modes(section, r.p_buf, r.part.at[parity], r.p_cross.at[parity])

    def fetch(self):
        fetch(self.source, self.field, self.sem, 4)

    def got(self):
        arrived(self.field, self.sem)

    def chunk(self, q):
        r = self.r
        to_modes(chunk_of(self.field, q, self.count), r.t_plain[...], r.kron[...], r.spread, self.modes.view(q))
        self.modes.start(q)


class Stage:
    def __init__(self, k, kind, j, per_core, places, section, z, n, r):
        self.k, self.kind, self.j, self.r, self.section, self.n = k, kind, j, r, section, n
        self.parity = k % 2
        self.micro, self.other = section * per_core + j, (1 - section) * per_core + j
        self.forward, self.last = kind in ("middle", "turn"), kind == "tail"
        self.buffers = {name: r.fields.at[i] for name, i in places.items()}
        self.sems = {name: r.field_sem.at[i] for name, i in places.items()}
        self.gather = Gather(section, z, n, r, self.parity)
        self.count, self.lanes = r.full.shape[5], r.full.shape[6]
        self.chunks = r.full.shape[1]
        plain = lambda name: getattr(r, f"{name}{j}")
        if kind == "middle":
            self.loads = dict(a=r.inputs.at[self.micro, 0])
            self.saves = dict(a=plain("a1_"), z=plain("dg0_"))
        elif kind == "turn":
            self.loads = dict(a=plain("a1_"), cot=r.cotangent.at[self.micro, 0])
            self.saves = dict(cot=plain("gz1_"))
        elif kind == "back":
            self.loads = dict(gz=plain("gz1_"), h=r.cotangent.at[self.micro, 0], a=plain("a1_"), dg=plain("dg0_"))
            self.saves = dict(h=plain("ga1_"), dg=plain("gz0_"))
        else:
            self.loads = dict(gz=plain("gz0_"), h=plain("ga1_"), a=r.inputs.at[self.micro, 0])
            self.saves = {}
        layer = 0 if kind in ("middle", "tail") else 1
        self.weight, self.bias = r.conv.at[layer if self.forward else 2 + layer], r.bias.at[layer]
        self.table = r.t_plain if kind == "middle" else r.t_doubled
        self.itable = r.it_doubled if self.forward else r.it_plain
        if not self.last:
            self.modes = Modes(section, r.p_buf, r.part.at[self.parity], r.p_cross.at[self.parity])
        if kind in ("turn", "tail"):
            self.bound = Bound(section, 1 if kind == "turn" else 0, self.micro, self.other,
                               self.buffers["a" if kind == "turn" else "h"], r.bound,
                               r.b_local.at[self.parity], r.b_cross.at[self.parity])

    def prefetch(self):
        for name, src in self.loads.items():
            if self.kind != "middle":
                fetch(src, self.buffers[name], self.sems[name])
        if self.forward:
            self.rid_copy().start()

    def rid_copy(self):
        return pltpu.make_async_copy(self.r.region.at[self.micro, 0], self.r.rid.at[self.parity],
                                     self.r.rid_sem.at[self.parity])

    def got(self, name):
        arrived(self.buffers[name], self.sems[name])

    def open(self):
        r, b = self.r, self.buffers
        if self.forward:
            r.eo[...] = jnp.zeros_like(r.eo)
            r.eb[...] = jnp.zeros_like(r.eb)
            if self.kind != "middle":
                self.got("a")
        else:
            for name in ("gz", "h", "a"):
                self.got(name)
            at = self.k - self.r.first_back
            r.cg[at] = jnp.zeros_like(r.cg[at])
            r.bg[at] = jnp.zeros_like(r.bg[at])

    def before(self, i):
        r, b = self.r, self.buffers
        a = b["a"]
        rows, channels = a.shape[:2]
        blocks, parts = rows // (self.weight.shape[0] // channels), self.n - 1
        span = (i * blocks // parts, (i + 1) * blocks // parts)
        if self.forward:
            conv_rows(self.weight, self.bias, a, b["z"], *span)
        else:
            conv_rows(self.weight, None, b["gz"], b["h"], *span)
            at = self.k - r.first_back
            grad_rows(a, b["gz"], r.cg.at[at], r.bg.at[at], i * rows // parts, (i + 1) * rows // parts)

    def outs(self, q):
        return [pltpu.make_async_copy(chunk_at(self.buffers[name], q, self.count), chunk_at(dst, q, self.count),
                                      self.r.out_sem.at[self.parity, i, q])
                for i, (name, dst) in enumerate(self.saves.items())]

    def late(self):
        for name in ("cot", "dg"):
            if name in self.loads:
                self.got(name)

    def chunk(self, q):
        r, b, count = self.r, self.buffers, self.count
        spectral = from_modes(self.gather.full.at[q].reshape(-1, count, self.lanes), self.itable[...], r.ikron[...],
                              r.spread)
        if self.forward:
            branch, slope = gelu_parts(spectral + chunk_of(b["z"], q, count))
            if self.kind == "turn":
                put(chunk_at(b["cot"], q, count), chunk_of(b["cot"], q, count) * slope)
            else:
                put(chunk_at(b["z"], q, count), slope)
            add_squares(branch, r.eb)
            out = chunk_of(b["a"], q, count) + branch
            put(chunk_at(b["a"], q, count), out)
            add_squares(out, r.eo)
            source = b["cot" if self.kind == "turn" else "a"]
        else:
            ga = spectral + chunk_of(b["h"], q, count)
            put(chunk_at(b["h"], q, count), ga)
            if not self.last:
                put(chunk_at(b["dg"], q, count), ga * chunk_of(b["dg"], q, count))
                source = b["dg"]
        for copy in self.outs(q):
            copy.start()
        if self.kind in ("turn", "tail"):
            self.bound.start(q, count)
        if not self.last:
            to_modes(chunk_of(source, q, count), self.table[...], r.kron[...], r.spread, self.modes.view(q))

            pl.when(q == self.chunks - 1)(self.gather.finish)
            self.modes.start(q)

    def end(self):
        if self.forward:
            self.rid_copy().wait()
            region_sums(self.r.rid.at[self.parity], self.r.eo, self.r.eb, self.r.stat.at[self.k])
        if self.last:
            self.gather.finish()

    def close(self):
        def body(q, carry):
            for copy in self.outs(q):
                copy.wait()
            if self.kind in ("turn", "tail"):
                self.bound.wait(q, self.count)
            return carry

        lax.fori_loop(0, self.chunks, body, 0)


def stages_kernel(per_core, kinds, places, mixes, r):
    section, z, n = place_and_peers()
    chunks, count = r.full.shape[1], r.full.shape[5]
    r.first_back = 2 * per_core
    stages = [Stage(k, kind, j, per_core, places[k], section, z, n, r)
              for k, (kind, j) in enumerate((kind, j) for kind in kinds for j in range(per_core))]
    heads = [Head(section * per_core + j, places[j]["a"], j, section, r) for j in range(per_core)]
    half = r.far.shape[0]

    def spare(q, x):
        groups = r.fields.shape[1] // count
        at = q * half + x
        place, at = 3 + at // (2 * groups), at % (2 * groups)
        side, group = at // groups, at % groups
        return r.fields.at[place, pl.ds(pl.multiple_of(group * count, count), count), :,
                           pl.ds(pl.multiple_of(side * 128, 128), 128)]

    def lend_in(q, x):
        rows = pl.ds(q * count, count)
        return pltpu.make_async_copy(r.weights.at[0, (1 - section) * half + x, rows], spare(q, x), r.w_load.at[q, x])

    def lent(q, x):
        return to_core(spare(q, x), r.far.at[x, pl.ds(q * count, count)],
                       (r.w_cross.at[0, q, x], r.w_cross.at[1, q, x]), section)

    blocks = [(q, x) for q in range(chunks) for x in range(half)]
    for head in heads:
        head.fetch()
    for block in blocks:
        lend_in(*block).start()
    greet(section, z, n, True, lax.axis_size("batch"))
    wide = r.full.at[1].reshape(-1, *r.wide_own.shape)
    small = [to_core(wide.at[section], wide.at[section], (r.m_cross.at[0, 0], r.m_cross.at[1, 0]), section),
             to_core(r.bias.at[section], r.bias.at[section], (r.m_cross.at[0, 1], r.m_cross.at[1, 1]), section)]
    wide[section] = r.wide_own[...]
    r.bias[section] = r.bias_own[...]
    for copy in small:
        copy.start()
    ahead, sums = [Sum(section, z, n, r, j, heads[j].modes.wait) for j in range(2)]
    mix = Mix(section, z, *mixes[0], ahead, stages[0].gather, r, lent)
    heads[0].got()

    def opening(q, carry):
        ahead.tick(q - 1)
        heads[0].chunk(q)

        @pl.when(q == 0)
        def _():
            for block in blocks:
                lend_in(*block).wait()
                lent(*block).start()

        return carry

    lax.fori_loop(0, chunks, opening, 0)
    for copy in small:
        copy.wait()
    for way in range(2):
        for layer in range(2):
            high, low = split(jnp.concatenate([wide[layer, way, side] for side in range(wide.shape[2])], 1))
            r.conv[2 * way + layer] = jnp.concatenate([high, low, high], 1)
    heads[1].got()
    mix.prime()

    def second(q, carry):
        ahead.tick(q + chunks - 1)

        @pl.when(q < chunks)
        def _():
            heads[1].chunk(q)

        sums.tick(q - 1)
        pl.when(within(q + chunks - n, chunks))(lambda: mix.chunk(q + chunks - n))
        return carry

    lax.fori_loop(0, n, second, 0)
    ahead.finish()
    mix.finish()
    shares = [Share(r, 0, 0)]
    shares[0].start()
    for block in blocks:
        lent(*block).wait_send()
    stages[0].prefetch()
    for k, stage in enumerate(stages):
        gather = stage.gather
        now = None if stage.last else Sum(section, z, n, r, stage.parity, stage.modes.wait)
        mix = None
        if sums is not None:
            mix = Mix(section, z, *mixes[(k + 1) // per_core], sums, stages[k + 1].gather, r)
            share = Share(r, k + 1, 1 - stage.parity)
            if k >= 1:
                shares[k - 1].wait_send()
            shares.append(share)
            mix.prime()
        lead = n - 1 if k == 0 else chunks - 1
        ready = n - 1 - lead
        gather.begin()
        stage.open()

        def early(i, carry):
            if sums is not None:
                sums.tick(i + lead)
            gather.tick(i)
            stage.before(i)
            if mix is not None and not mix.flip:
                pl.when(within(i - ready, chunks))(lambda: mix.chunk(i - ready))
            return carry

        lax.fori_loop(0, n - 1, early, 0)
        if k > 0:
            stages[k - 1].close()
        if k + 1 < len(stages):
            stages[k + 1].prefetch()
        stage.late()

        def later(q, carry):
            i = q + n - 1
            if sums is not None:
                sums.tick(i + lead)
            if now is not None:
                now.tick(i - n)
            gather.tick(i)
            stage.chunk(q)
            if mix is not None:
                if mix.flip:
                    pl.when(q == 0)(sums.finish)
                    mix.chunk(q)
                else:
                    pl.when(within(i - ready, chunks))(lambda: mix.chunk(i - ready))
            return carry

        lax.fori_loop(0, chunks, later, 0)
        if mix is not None:
            if not mix.flip:
                sums.finish()
            mix.finish()
            share.start()
        stage.end()
        sums = now
    stages[-1].close()
    for share in shares[-2:]:
        share.wait_send()
    for share in shares:
        share.wait_recv()


def swap_halves(value):
    return pltpu.roll(value, value.shape[-1] // 2, value.ndim - 1)


def left_lanes(shape):
    return lax.broadcasted_iota(jnp.int32, shape, len(shape) - 1) < shape[-1] // 2


def pieces(array):
    return [array[at:at + G] for at in range(0, array.shape[0], G)]


def spread_row(ref, row):
    return ref[pl.ds(row, G, stride=0), :]


class Mix:
    def __init__(self, section, z, layer, flip, sums, gather, r, lent=None):
        self.lent = lent
        self.section, self.z, self.layer, self.flip, self.r = section, z, layer, flip, r
        self.sums, self.gather = sums, gather
        self.chunks, self.grids, self.half, self.count, self.lanes = sums.part.shape[1:]
        self.channels, self.slots = r.weights.shape[2], r.wbuf.shape[0]
        self.blocks = self.chunks * self.half // 2

    def begin(self, block):
        per = self.half // 2
        q, x = block // per, 2 * (block % per)
        slot = lax.rem(block, self.slots)
        rows = pl.ds(q * self.count, self.count)
        if self.lent is not None:
            for at in range(2):
                self.lent(q, x + at).wait_recv()

        @pl.when(self.section == self.layer)
        def _():
            pltpu.make_async_copy(self.r.weights.at[0, pl.ds(self.section * self.half + x, 2), rows],
                                  self.r.wbuf.at[slot], self.r.wsem.at[slot]).start()

        @pl.when(self.section != self.layer)
        def _():
            pltpu.make_async_copy(self.r.far.at[pl.ds(x, 2), rows], self.r.wbuf.at[slot], self.r.wsem.at[slot]).start()

    def prime(self):
        for block in range(min(self.slots, self.blocks)):
            self.begin(jnp.int32(block))
        if not self.flip:
            self.r.macc[...] = jnp.zeros_like(self.r.macc)

    def chunk(self, q):
        def body(x, carry):
            block = q * (self.half // 2) + x // 2
            slot = lax.rem(block, self.slots)

            @pl.when(lax.rem(x, 2) == 0)
            def _():
                arrived(self.r.wbuf.at[slot], self.r.wsem.at[slot])

            (self.transposed if self.flip else self.forward)(q, x, self.r.wbuf.at[slot, lax.rem(x, 2)])

            @pl.when(jnp.logical_and(lax.rem(x, 2) == 1, block + self.slots < self.blocks))
            def _():
                self.begin(block + self.slots)

            return carry

        lax.fori_loop(0, self.half, body, 0)
        if self.flip:
            self.gather.give(q)

    def forward(self, q, x, weight):
        sides, groups = 2 * self.grids, self.channels // G
        total, source = self.r.macc.at[x], self.r.msrc
        for g in range(self.grids):
            value = self.sums.part[self.z, q, g, x]
            source[2 * g, :self.count] = value
            source[2 * g + 1, :self.count] = swap_halves(value)
        keys = [(k, o) for k in range(sides) for o in range(groups)]

        def body(octet, acc):
            acc = dict(zip(keys, acc))
            for u in range(G):
                i = octet * G + u
                rows = [spread_row(source.at[k], i) for k in range(sides)]
                for o in range(groups):
                    w = weight[i, o * G:(o + 1) * G, :]
                    for k in range(sides):
                        acc[k, o] = acc[k, o] + rows[k] * w
            return tuple(acc[key] for key in keys)

        acc = lax.fori_loop(0, self.count // G, body, tuple(total[k, o * G:(o + 1) * G, :] for k, o in keys))
        for key, value in zip(keys, acc):
            total[key[0], key[1] * G:(key[1] + 1) * G, :] = value

    def transposed(self, q, x, weight):
        sides, groups = 2 * self.grids, self.channels // G
        source = self.r.msrc
        for g in range(self.grids):
            value = jnp.concatenate([self.sums.part[self.z, at, g, x] for at in range(self.chunks)], 0)
            source[2 * g] = value
            source[2 * g + 1] = swap_halves(value)
        rows = [pieces(source[k]) for k in range(sides)]
        out = [[] for _ in range(sides)]
        for i in range(self.count):
            total = [None] * sides
            for o in range(groups):
                w = weight[i, o * G:(o + 1) * G, :]
                for k in range(sides):
                    term = w * rows[k][o]
                    total[k] = term if total[k] is None else total[k] + term
            for k in range(sides):
                out[k].append(jnp.sum(total[k], axis=0, keepdims=True))
        left = left_lanes((self.count, self.lanes))
        for g in range(self.grids):
            a, b = [jnp.concatenate(out[2 * g + side], 0) for side in range(2)]
            self.put(g, q, x, jnp.where(left, a + swap_halves(a), swap_halves(b) - b))

    def put(self, g, q, x, value):
        if g == 0:
            self.gather.full[q, self.z, self.section, x] = value
        else:
            self.gather.give_from[q, x] = value

    def finish(self):
        if self.flip:
            return
        left = left_lanes((self.channels, self.lanes))

        def body(x, carry):
            for g in range(self.grids):
                a, b = [self.r.macc[x, 2 * g + side] for side in range(2)]
                result = jnp.where(left, a - swap_halves(a), b + swap_halves(b))
                for q in range(self.chunks):
                    self.put(g, q, x, result[q * self.count:(q + 1) * self.count])
            return carry

        lax.fori_loop(0, self.half, body, 0)
        for q in range(self.chunks):
            self.gather.give(q)


def gather_columns(f_ref, d_ref, left_of, right_of):
    channels = f_ref.shape[2] * f_ref.shape[5]
    lanes = f_ref.shape[6]
    left = left_lanes((channels, lanes))
    for stream in range(f_ref.shape[0]):
        for member in range(f_ref.shape[1]):
            for g in range(f_ref.shape[3]):
                at = (stream * f_ref.shape[1] + member) * f_ref.shape[3] + g
                both = []
                for x in range(2):
                    f = f_ref[stream, member, :, g, x].reshape(channels, lanes)
                    turned = swap_halves(f)
                    left_of[x, at] = jnp.concatenate([f, jnp.where(left, -turned, turned)], 0).T
                    both.append(d_ref[stream, member, :, g, x].reshape(channels, lanes))
                right_of[at] = jnp.concatenate(both, 0).T


def column_products(left_of, right_of, product):
    grids, double, lanes = right_of.shape
    half = double // 2
    left = left_lanes((2 * grids, lanes))
    rows = right_of.reshape(grids * double, lanes)
    sides = [left_of.at[x].reshape(grids * double, lanes) for x in range(2)]

    def body(k, carry):
        pick = pl.ds(k, 2 * grids, stride=half)
        d = rows[pick, :]
        f_high, f_low = split(jnp.concatenate([side[pick, :] for side in sides], 0))
        d_high, d_low = split(jnp.concatenate([jnp.where(left, d, 0.0), jnp.where(left, 0.0, d)], 0))
        product[k] = dot(jnp.concatenate([f_high, f_low, f_high], 0), jnp.concatenate([d_high, d_high, d_low], 0),
                         (((0,), (0,)), ((), ())))
        return carry

    lax.fori_loop(0, half, body, 0, unroll=4)


def product_rows(product, first, out):
    half, double, lanes = product.shape
    channels = double // 2
    rows = product.reshape(half * double, lanes)

    def body(i, carry):
        parts = [rows[pl.ds(part * channels + first + i, half, stride=double), :] for part in range(2)]
        tile = jnp.concatenate(parts, 0).T
        for x in range(2):
            out[x, i] = tile[x * channels:(x + 1) * channels]
        return carry

    lax.fori_loop(0, out.shape[1], body, 0, unroll=4)


class GradInput:
    def __init__(self, first, f, g, fbuf, gbuf, sem):
        self.first, self.f, self.g, self.fbuf, self.gbuf, self.sem = first, f, g, fbuf, gbuf, sem

    def load(self, x, slot):
        for layer, condition in enumerate((self.first, jnp.logical_not(self.first))):
            @pl.when(condition)
            def _():
                for j in range(len(self.f[layer])):
                    pltpu.make_async_copy(self.f[layer][j].at[:, :, :, pl.ds(2 * x, 2)], self.fbuf.at[slot, j],
                                          self.sem.at[0, slot]).start()
                    pltpu.make_async_copy(self.g[layer][j].at[:, :, :, pl.ds(2 * x, 2)], self.gbuf.at[slot, j],
                                          self.sem.at[1, slot]).start()

    def next(self, x, count):
        slot = lax.rem(x, 2)

        @pl.when(x + 1 < count)
        def _():
            self.load(x + 1, 1 - slot)

        arrived(self.fbuf.at[slot], self.sem.at[0, slot])
        arrived(self.gbuf.at[slot], self.sem.at[1, slot])
        return self.fbuf.at[slot], self.gbuf.at[slot]


def grad_input(r, first, per_core):
    f = [[getattr(r, f"f{layer}{j}") for j in range(per_core)] for layer in range(2)]
    g = [[getattr(r, f"g{layer}{j}") for j in range(per_core)] for layer in range(2)]
    return GradInput(first, f, g, r.fbuf, r.gbuf, r.in_sem)


def far_grad_kernel(per_core, r):
    section, z, n = place_and_peers()
    pairs, block = r.far.shape[0] // 2, r.out.shape[2]
    blocks = r.far.shape[1] // block
    source = grad_input(r, section != 0, per_core)

    def move(k, slot):
        p, i = k // blocks, k % blocks
        return to_core(r.out.at[slot], r.far.at[pl.ds(2 * p, 2), pl.ds(i * block, block)], (r.send.at[k], r.recv.at[k]),
                       section)

    source.load(0, 0)
    greet(section, z, n, False)

    def body(p, carry):
        gather_columns(*source.next(p, pairs), r.left_of, r.right_of)
        column_products(r.left_of, r.right_of, r.product)

        def inner(i, carry):
            k = p * blocks + i

            @pl.when(k >= 2)
            def _():
                move(k - 2, lax.rem(k, 2)).wait_send()

            product_rows(r.product, i * block, r.out.at[lax.rem(k, 2)])
            move(k, lax.rem(k, 2)).start()
            return carry

        return lax.fori_loop(0, blocks, inner, carry)

    lax.fori_loop(0, pairs, body, 0)
    total = pairs * blocks
    for k in (total - 2, total - 1):
        move(k, k % 2).wait_send()

    def close(k, carry):
        move(k, 0).wait_recv()
        return carry

    lax.fori_loop(0, total, close, 0)


def own_grad_kernel(names, per_core, m_ref, *refs):
    r = types.SimpleNamespace(**dict(zip(names, refs)))
    p, i = pl.program_id(0), pl.program_id(1)
    source = grad_input(r, m_ref[0] == 0, per_core)

    @pl.when(i == 0)
    def _():
        @pl.when(p == 0)
        def _():
            source.load(0, 0)

        gather_columns(*source.next(p, pl.num_programs(0)), r.left_of, r.right_of)
        column_products(r.left_of, r.right_of, r.product)

    r.bound_out[...] = r.bound_in[...]
    r.out[1 - m_ref[0]] = r.far[...]
    product_rows(r.product, i * r.out.shape[2], r.out.at[m_ref[0]])


def whole(array):
    return pl.BlockSpec(array.shape, lambda *_: (0,) * array.ndim)


def params(**kw):
    return pltpu.CompilerParams(vmem_limit_bytes=VMEM_LIMIT, **kw)


def local(inputs, cotangent, region_id, spectral_w, conv_w, bias_vector):
    micro_count, _, rows_dev, channels, width = inputs.shape
    lanes = spectral_w.shape[-1]
    half = lanes // 2
    kx_dev = spectral_w.shape[1]
    row_devices, sections = lax.axis_size("rows"), lax.axis_size("section")
    mode_rows, height = kx_dev * row_devices, rows_dev * row_devices
    section = lax.axis_index("section")
    per_core = micro_count // sections
    kx_half = kx_dev // sections

    plain, doubled = col_tables(width, half)

    def stacked(array):
        high, low = np_split(array)
        return np.concatenate([high, high, low], 0)

    t_plain, t_doubled, it_plain, it_doubled = [stacked(t) for t in (plain, doubled, plain.T, doubled.T)]
    kron, ikron = row_tables(height, mode_rows, lax.axis_index("rows") * rows_dev, rows_dev)

    count = 2 * G
    chunks = channels // count
    hbm, vmem = pl.BlockSpec(memory_space=pl.ANY), pl.BlockSpec(memory_space=pltpu.VMEM)
    field_shape = jax.ShapeDtypeStruct((rows_dev, channels, width), F32)
    part_dims = (row_devices, chunks, sections, kx_half, count, lanes)
    p_shape, f_shape = jax.ShapeDtypeStruct(part_dims, F32), jax.ShapeDtypeStruct(part_dims[1:], F32)
    y_shape = jax.ShapeDtypeStruct((sections, chunks, kx_half, count, lanes), F32)
    stat_shape = jax.ShapeDtypeStruct((3, R, 128), F32)
    cg_shape = jax.ShapeDtypeStruct((2 * channels, 2 * channels), F32)
    bg_shape = jax.ShapeDtypeStruct((channels, width), F32)
    bound_shape = jax.ShapeDtypeStruct((micro_count, rows_dev, channels, width), F32)
    dma = pltpu.SemaphoreType.DMA
    field_buf = pltpu.VMEM((rows_dev, channels, width), F32)
    full_dims = (chunks, row_devices, sections, kx_half, count, lanes)
    spread = pltpu.VMEM((width // 128, rows_dev * count, 128), F32)
    energy = pltpu.VMEM((rows_dev, G, width), F32)
    line_sems = dma((2, chunks, row_devices))
    def run(body, ident, ins, outs, scratch, cost=50, aliases=None):
        names = [*ins, *outs, *scratch]
        spec = lambda entry: vmem if isinstance(entry, tuple) else hbm
        plain = lambda entry: entry[0] if isinstance(entry, tuple) else entry
        kernel = lambda *refs: body(types.SimpleNamespace(**dict(zip(names, refs))))
        positions = {list(ins).index(k): list(outs).index(v) for k, v in (aliases or {}).items()}
        result = pl.pallas_call(
            kernel, in_specs=[spec(e) for e in ins.values()], out_specs=[spec(e) for e in outs.values()],
            out_shape=[plain(e) for e in outs.values()], scratch_shapes=list(scratch.values()),
            input_output_aliases=positions,
            cost_estimate=pl.CostEstimate(flops=0, bytes_accessed=cost * 3_000_000, transcendentals=0),
            compiler_params=params(collective_id=ident, has_side_effects=True))(*[plain(e) for e in ins.values()])
        return types.SimpleNamespace(**dict(zip(outs, result)))

    conv_rows_at_once = 256 // channels
    maps = jnp.stack([conv_w[0].T, conv_w[0]])
    at = np.arange(conv_rows_at_once * channels) // channels
    wide_own = jnp.where(at[:, None] == at[None, :], jnp.tile(maps, (1, conv_rows_at_once, conv_rows_at_once)), 0.0)
    wide_own = jnp.stack(jnp.split(wide_own, wide_own.shape[2] // 128, 2), 1)
    bias_own = jnp.broadcast_to(bias_vector[0][:, None], (channels, width))

    streams = range(per_core)
    members = lax.axis_size("batch")
    kinds = ["middle", "turn", "back", "tail"]
    mixes = [(0, False), (1, False), (1, True), (0, True)]
    names = ["f00", "f01", "f10", "f11", "g10", "g11", "g00", "g01"]
    places = [dict(a=0, z=1), dict(a=2, z=3), dict(a=4, z=5, cot=6), dict(a=0, z=1, cot=2),
              dict(gz=3, a=4, h=5, dg=6), dict(gz=0, a=1, h=2, dg=3), dict(gz=4, a=5, h=6), dict(gz=0, a=1, h=2)]
    both = (2,)
    ins = dict(inputs=inputs, cotangent=cotangent, region=region_id, weights=spectral_w, t_plain=(t_plain,),
               t_doubled=(t_doubled,), it_plain=(it_plain,), it_doubled=(it_doubled,), kron=(kron,), ikron=(ikron,),
               wide_own=(wide_own,), bias_own=(bias_own,))
    outs = dict(far=jax.ShapeDtypeStruct((kx_half,) + spectral_w.shape[2:], F32), bound=bound_shape, stat=(jax.ShapeDtypeStruct((2 * per_core,) + stat_shape.shape, F32),),
                cg=(jax.ShapeDtypeStruct((2 * per_core,) + cg_shape.shape, F32),),
                bg=(jax.ShapeDtypeStruct((2 * per_core,) + bg_shape.shape, F32),),
                **{f"{name}{j}": field_shape for name in ("a1_", "dg0_", "gz1_", "ga1_", "gz0_") for j in streams},
                **{f"shared{i}": jax.ShapeDtypeStruct((members,) + f_shape.shape, F32) for i in range(len(names))})
    scratch = dict(
        fields=pltpu.VMEM((7,) + field_shape.shape, F32), full=pltpu.VMEM(both + full_dims, F32),
        part=pltpu.VMEM(both + part_dims, F32),
        come=pltpu.VMEM(both + (2, chunks, row_devices - 1) + part_dims[2:], F32),
        keep=pltpu.VMEM(both + f_shape.shape, F32), y_give=pltpu.VMEM(both + y_shape.shape[1:], F32),
        p_buf=pltpu.VMEM(full_dims, F32), spread=spread, eo=energy, eb=energy,
        rid=pltpu.VMEM((2, rows_dev, width), jnp.int32),
        wbuf=pltpu.VMEM((3, 2, count, channels, lanes), F32), macc=pltpu.VMEM((kx_half, 2 * sections, channels, lanes), F32),
        msrc=pltpu.VMEM((2 * sections, channels, lanes), F32),
        bias=pltpu.VMEM((2, channels, width), F32),
        conv=pltpu.VMEM((4, len(at), 3 * len(at)), BF16), m_cross=dma((2, 2)),
        field_sem=dma((7,)), rid_sem=dma(both), out_sem=dma((2, 2, chunks)), wsem=dma((3,)), w_load=dma((chunks, kx_half)), w_cross=dma((2, chunks, kx_half)),
        send=dma(both + (2, chunks, row_devices)), recv=dma(both + (2, chunks, row_devices)),
        red_send=dma(both + (2, chunks, row_devices)), red_recv=dma(both + (2, chunks, row_devices)),
        y_cross=dma((2, 2, chunks)), p_cross=dma((2, 2, chunks)),
        b_local=dma((2, chunks)), b_cross=dma((2, 2, chunks)),
        s_local=dma(both), s_send=dma((2, members)), s_recv=dma((len(names), members)))
    done = run(functools.partial(stages_kernel, per_core, kinds, places, mixes), 0, ins, outs, scratch, cost=400)
    gathered = {name: getattr(done, f"shared{i}") for i, name in enumerate(names)}
    bound, calls = done.bound, 0

    grids = per_core * members * sections
    block = 2 * G
    pairs, blocks = kx_half // 2, channels // block
    in_buf = pltpu.VMEM((2, per_core, members, chunks, sections, 2, count, lanes), F32)
    grad_scratch = dict(fbuf=in_buf, gbuf=in_buf, in_sem=dma((2, 2)), left_of=pltpu.VMEM((2, grids, lanes, lanes), F32),
                        right_of=pltpu.VMEM((grids, lanes, lanes), F32), product=pltpu.VMEM((half, lanes, lanes), F32))
    far_grad = run(functools.partial(far_grad_kernel, per_core), 1 + calls, gathered,
                   dict(far=jax.ShapeDtypeStruct((kx_half, channels, channels, lanes), F32)),
                   dict(out=pltpu.VMEM((2, 2, block, channels, lanes), F32), send=dma((pairs * blocks,)),
                        recv=dma((pairs * blocks,)), **grad_scratch)).far
    bound_rows = bound.reshape(micro_count * rows_dev, channels, width)
    bound_block = pl.BlockSpec((bound_rows.shape[0] // (pairs * blocks), channels, width),
                               lambda p, i, m: (p * blocks + i, 0, 0))
    grid_spec = pltpu.PrefetchScalarGridSpec(
        num_scalar_prefetch=1, grid=(pairs, blocks),
        in_specs=[hbm] * len(gathered)
        + [pl.BlockSpec((2, block, channels, lanes), lambda p, i, m: (p, i, 0, 0)), bound_block],
        out_specs=[pl.BlockSpec((2, 2, block, channels, lanes), lambda p, i, m: (0, p, i, 0, 0)), bound_block],
        scratch_shapes=list(grad_scratch.values()))
    spectral_grad, boundary = pl.pallas_call(
        functools.partial(own_grad_kernel, [*gathered, "far", "bound_in", "out", "bound_out", *grad_scratch], per_core),
        grid_spec=grid_spec, out_shape=[jax.ShapeDtypeStruct((2, kx_half, channels, channels, lanes), F32),
                                        jax.ShapeDtypeStruct(bound_rows.shape, F32)],
        cost_estimate=pl.CostEstimate(flops=0, bytes_accessed=150_000_000, transcendentals=0),
        compiler_params=params())(
            jnp.reshape(section, (1,)).astype(jnp.int32), *gathered.values(), far_grad, bound_rows)
    spectral_grad = spectral_grad.reshape(spectral_w.shape)
    boundary = boundary.reshape((1, micro_count, 1) + inputs.shape[2:])

    def lower(value):
        return (value[:channels, :channels] + value[channels:, channels:]
                + value[:channels, channels:] + value[channels:, :channels])

    pair = lambda value: jnp.sum(value.reshape((2, per_core) + value.shape[1:]), 1)
    conv_local = jnp.stack([lower(value) for value in pair(done.cg)[::-1]])
    bias_local = jnp.sum(pair(done.bg)[::-1], -1)
    stat_local = jnp.sum(pair(done.stat), -1)
    shapes = [v.shape for v in (conv_local, bias_local, stat_local)]
    flat_sums = jnp.concatenate([v.reshape(-1) for v in (conv_local, bias_local, stat_local)])
    length = flat_sums.shape[0]
    flat_sums = jnp.pad(flat_sums, (0, -length % 1024)).reshape(-1, 128)
    flat_sums = jnp.sum(lax.all_gather(flat_sums, ("section", "batch", "rows"), axis=0), 0).reshape(-1)
    ends = np.cumsum([0] + [math.prod(shape) for shape in shapes])
    conv_sum, bias_sum, stat_sum = [flat_sums[ends[i]:ends[i + 1]].reshape(shapes[i]) for i in range(3)]
    own_stat = lax.dynamic_index_in_dim(stat_sum, section, 0, False)
    layer_rms = jnp.sqrt(own_stat[:2] / (channels * own_stat[2])[None, :] + 1e-06)[None]
    own = lambda value: lax.dynamic_slice_in_dim(value, section, 1, 0)
    return boundary, spectral_grad, own(conv_sum), own(bias_sum), layer_rms


def solution(mesh):
    placed = (
        P(None, "batch", "rows", None, None),
        P(None, "batch", "rows", None, None),
        P(None, "batch", "rows", None),
        P("section", "rows", None, None, None),
        P("section", None, None),
        P("section", None),
    )
    return jax.shard_map(
        local,
        mesh=mesh,
        in_specs=placed,
        out_specs=(
            P("section", None, "batch", "rows", None, None),
            P("section", "rows", None, None, None),
            P("section", None, None),
            P("section", None),
            P("section", None, None),
        ),
        check_vma=False,
    )
```

```python
import functools
import math
import types

import jax
import jax.numpy as jnp
import numpy as np
from jax import lax
from jax.experimental import pallas as pl
from jax.experimental.pallas import tpu as pltpu
from jax.sharding import PartitionSpec as P

R = 8
G = 8
F32 = jnp.float32
BF16 = jnp.bfloat16
VMEM_LIMIT = 62 * 1024 * 1024
MESH = pl.DeviceIdType.MESH


def split(value):
    high = value.astype(BF16)
    return high, (value - high.astype(F32)).astype(BF16)


def dot(left, right, dims=(((1,), (0,)), ((), ()))):
    return lax.dot_general(left, right, dims, preferred_element_type=F32)


def dot3(left, right):
    return dot(left[0], right[0]) + (dot(left[1], right[0]) + dot(left[0], right[1]))


def np_split(value):
    high = value.astype(np.float32).astype(BF16)
    return high, (value - high.astype(np.float64)).astype(np.float32).astype(BF16)


def col_tables(width, half):
    phase = 2.0 * math.pi / width * (np.outer(np.arange(width), np.arange(half)) % width)
    cosine, sine = np.cos(phase) / math.sqrt(width), np.sin(phase) / math.sqrt(width)
    plain = np.concatenate([cosine, -sine, -sine, -cosine], 1)
    doubled = plain * np.tile(np.where(np.arange(half) == 0, 1.0, 2.0), 4)[None, :]
    return plain, doubled


def row_tables(height, mode_rows, first_row, rows_dev):
    position = jnp.arange(mode_rows, dtype=jnp.int32)
    frequency = jnp.where(position < mode_rows // 2, position, height - mode_rows + position)
    row = first_row + jnp.arange(rows_dev, dtype=jnp.int32)
    phase = 2.0 * math.pi / height * (frequency[:, None] * row[None, :] % height).astype(F32)
    small = jnp.concatenate([jnp.cos(phase), jnp.sin(phase)], 1) / math.sqrt(height)
    rounded = lax.reduce_precision(small, 8, 7)
    high, low = rounded.astype(BF16), (small - rounded).astype(BF16)
    forward = jnp.concatenate([jnp.concatenate([high, high], 1), jnp.concatenate([low, jnp.zeros_like(low)], 1)], 0)
    inverse = jnp.concatenate([high.T, high.T, low.T], 1)
    return forward, inverse


def to_modes(value, table, kron, spread, p_ref):
    mode_rows, count, lanes = p_ref.shape
    rows = value.shape[0] // count
    high, low = split(value)
    spectra = dot(jnp.concatenate([high, low, high], 1), table)
    for i in range(2):
        spread[i] = spectra[:, i * lanes:(i + 1) * lanes]
    out = p_ref.reshape(mode_rows * count, lanes)
    for first in range(0, count, 2):
        sides = []
        for c in (first, first + 1):
            pick = pl.ds(c, rows, stride=count)
            sides.append(jnp.concatenate([spread[i, pick, :] for i in range(2)], 0))
        high, low = split(jnp.concatenate(sides, 1))
        both = dot(kron, jnp.concatenate([high, low], 0))
        result = both[:mode_rows] + both[mode_rows:]
        for i in range(2):
            out[pl.ds(first + i, mode_rows, stride=count), :] = result[:, i * lanes:(i + 1) * lanes]


def from_modes(y_ref, table, kron, spread):
    mode_rows, count, lanes = y_ref.shape
    rows, pieces = spread.shape[1] // count, spread.shape[0]
    modes = y_ref.reshape(mode_rows * count, lanes)
    sides = []
    for first in range(0, count, 2):
        pair = [modes[pl.ds(c, mode_rows, stride=count), :] for c in (first, first + 1)]
        high, low = split(jnp.concatenate(pair, 1))
        both = dot(kron, jnp.concatenate([high, low, high], 0))
        for i in range(2):
            side = both[:, i * lanes:(i + 1) * lanes]
            sides.append(jnp.concatenate([side[:rows], side[rows:]], 1))
    high, low = split(jnp.concatenate(sides, 0))
    out = dot(jnp.concatenate([high, low, high], 1), table)
    for c in range(count):
        for i in range(pieces):
            spread[i, pl.ds(c, rows, stride=count), :] = out[c * rows:(c + 1) * rows, i * 128:(i + 1) * 128]
    return jnp.concatenate([spread[i] for i in range(pieces)], 1)


def gelu_parts(z):
    gauss = jnp.exp2((-0.5 / math.log(2.0)) * (z * z))
    base = 1.0 + (0.3275911 / math.sqrt(2.0)) * jnp.abs(z)
    t = pl.reciprocal(base, approx=True)
    t = t * (2.0 - base * t)
    poly = t * (0.127414796 + t * (-0.142248368 + t * (0.7107068705 + t * (-0.7265760135 + t * 0.5307027145))))
    tail = poly * gauss
    phi = jnp.where(z >= 0, 1.0 - tail, tail)
    return z * phi, phi + z * (gauss * (1.0 / math.sqrt(2.0 * math.pi)))


def flat(ref):
    rows, count, width = ref.shape
    return ref[...].reshape(rows * count, width)


def put(ref, value):
    ref[...] = value.reshape(ref.shape)


def place_and_peers():
    section, z = lax.axis_index("section"), lax.axis_index("rows")
    return section, z, lax.axis_size("rows")


def greet(section, z, n, lines, members=0):
    barrier = pltpu.get_barrier_semaphore()
    pl.semaphore_signal(barrier, inc=1, device_id={"section": 1 - section}, device_id_type=MESH)
    if not lines:
        pl.semaphore_wait(barrier, 1)
        return

    @pl.when(z > 0)
    def _():
        pl.semaphore_signal(barrier, inc=1, device_id={"rows": z - 1}, device_id_type=MESH)

    @pl.when(z < n - 1)
    def _():
        pl.semaphore_signal(barrier, inc=1, device_id={"rows": z + 1}, device_id_type=MESH)

    for away in range(1, members):
        pl.semaphore_signal(barrier, inc=1, device_id={"batch": lax.rem(lax.axis_index("batch") + away, members)},
                            device_id_type=MESH)

    others = 1 + max(members - 1, 0)
    pl.semaphore_wait(barrier, others + (z > 0).astype(jnp.int32) + (z < n - 1).astype(jnp.int32))


def to_core(src, dst, sems, section):
    return pltpu.make_async_remote_copy(src_ref=src, dst_ref=dst, send_sem=sems[0], recv_sem=sems[1],
                                        device_id={"section": 1 - section}, device_id_type=MESH)


def guard(condition, body):
    if isinstance(condition, (bool, np.bool_)):
        if condition:
            body()
    else:
        pl.when(condition)(body)


class Line:
    def __init__(self, section, z, n, chunks, send, recv):
        self.section, self.z, self.n, self.chunks = section, z, n, chunks
        self.send, self.recv = send, recv

    def move(self, way, q, hop, src, dst):
        return pltpu.make_async_remote_copy(
            src_ref=src, dst_ref=dst, send_sem=self.send.at[way, q, hop], recv_sem=self.recv.at[way, q, hop],
            device_id={"rows": self.z + 1 if way == 0 else self.z - 1}, device_id_type=MESH)

    def sends(self, way):
        return self.z < self.n - 1 if way == 0 else self.z > 0

    def hears(self, way):
        return self.z > 0 if way == 0 else self.z < self.n - 1


def within(value, count):
    return jnp.logical_and(value >= 0, value < count)


class Gather(Line):
    def __init__(self, section, z, n, r, parity):
        super().__init__(section, z, n, r.full.shape[1], r.send.at[parity], r.recv.at[parity])
        self.full, self.give_from = r.full.at[parity], r.y_give.at[parity]
        self.cross = r.y_cross.at[parity]

    def swap(self, q):
        return to_core(self.give_from.at[q], self.full.at[q, self.z, self.section],
                       (self.cross.at[0, q], self.cross.at[1, q]), self.section)

    def give(self, q):
        self.swap(q).start()

    def hop(self, way, q, hop):
        piece = self.full.at[q, self.source(way, hop)]
        return self.move(way, q, hop, piece, piece)

    def source(self, way, hop):
        return self.z - hop if way == 0 else self.z + hop

    def known(self, way, hop):
        at = self.source(way, hop)
        return at >= 0 if way == 0 else at < self.n

    def own(self, q):
        self.swap(q).wait_recv()
        for way in range(2):
            @pl.when(self.sends(way))
            def _():
                self.hop(way, q, 0).start()

    def step(self, q, hop):
        for way in range(2):
            @pl.when(self.known(way, hop + 1))
            def _():
                piece = self.full.at[q, self.source(way, hop + 1)]
                self.move(way, q, hop, piece, piece).wait_recv()

                @pl.when(self.sends(way))
                def _():
                    self.hop(way, q, hop + 1).start()

    def tick(self, t):
        pl.when(within(t, self.chunks))(functools.partial(self.own, t))
        for hop in range(self.n - 1):
            q = t - hop - 1
            pl.when(within(q, self.chunks))(functools.partial(self.step, q, hop))

    def finish(self):
        def body(q, carry):
            self.swap(q).wait_send()
            for way in range(2):
                for hop in range(self.n - 1):
                    @pl.when(jnp.logical_and(self.sends(way), self.known(way, hop)))
                    def _():
                        self.hop(way, q, hop).wait_send()
            return carry

        lax.fori_loop(0, self.chunks, body, 0)


class Sum(Line):
    def __init__(self, section, z, n, r, parity, admit):
        super().__init__(section, z, n, r.part.shape[2], r.red_send.at[parity], r.red_recv.at[parity])
        self.part, self.come, self.keep, self.admit = r.part.at[parity], r.come.at[parity], r.keep.at[parity], admit

    def owner(self, way, hop):
        return self.z + self.n - hop if way == 0 else self.z - self.n + hop

    def valid(self, way, hop):
        return self.z <= hop - 1 if way == 0 else self.z >= self.n - hop

    def sent(self, way, q, hop):
        return self.move(way, q, hop, self.part.at[self.owner(way, hop), q], self.come.at[way, q, hop - 1])

    def heard(self, way, q, hop):
        come = self.come.at[way, q, hop - 1]
        self.move(way, q, hop, come, come).wait_recv()

    def first(self, q):
        self.admit(q)
        self.step(q, 1)

    def step(self, q, hop):
        for way in range(2):
            @pl.when(self.valid(way, hop))
            def _():
                if hop > 1:
                    @pl.when(self.hears(way))
                    def _():
                        self.heard(way, q, hop - 1)
                        owner = self.owner(way, hop)
                        self.part[owner, q] = self.part[owner, q] + self.come[way, q, hop - 2]

                self.sent(way, q, hop).start()

    def final(self, q):
        for way in range(2):
            @pl.when(self.hears(way))
            def _():
                self.heard(way, q, self.n - 1)
                self.part[self.z, q] = self.part[self.z, q] + self.come[way, q, self.n - 2]

        self.keep[q] = self.part[self.z, q]

    def tick(self, t):
        pl.when(within(t, self.chunks))(functools.partial(self.first, t))
        for hop in range(2, self.n + 1):
            q = t - hop + 1
            pl.when(within(q, self.chunks))(
                functools.partial(self.step, q, hop) if hop < self.n else functools.partial(self.final, q))

    def finish(self):
        def body(q, carry):
            for way in range(2):
                for hop in range(1, self.n):
                    @pl.when(self.valid(way, hop))
                    def _():
                        self.sent(way, q, hop).wait_send()
            return carry

        lax.fori_loop(0, self.chunks, body, 0)


def fetch(src, dst, sem, parts=1):
    step = dst.shape[0] // parts
    for i in range(parts):
        pltpu.make_async_copy(src.at[pl.ds(i * step, step)], dst.at[pl.ds(i * step, step)], sem).start()


def arrived(dst, sem):
    pltpu.make_async_copy(dst, dst, sem).wait()


def portions(total, count):
    return [(i * total // count, (i + 1) * total // count) for i in range(count)]


def conv_rows(weight, bias, a, out, first, last):
    channels, width = a.shape[1:]
    block = weight.shape[0] // channels

    def body(i, carry):
        at = pl.ds(i * block, block)
        high, low = split(a[at].reshape(block * channels, width))
        result = dot(weight[...], jnp.concatenate([high, high, low], 0)).reshape(block, channels, width)
        out[at] = result + bias[...][None] if bias is not None else out[at] + result
        return carry

    lax.fori_loop(first, last, body, 0)


def grad_rows(a, gz, cg_ref, bg_ref, first, last):
    channels, width = a.shape[1:]

    def body(r, carry):
        grad, bias = carry
        g = gz[r]
        left = jnp.concatenate(split(a[r]), 0)
        right = jnp.concatenate(split(g), 0)
        return grad + dot(left, right, (((1,), (1,)), ((), ()))), bias + g

    grad, bias = lax.fori_loop(first, last, body, (cg_ref[...], bg_ref[...]))
    cg_ref[...] = grad
    bg_ref[...] = bias


def chunk_of(ref, q, count):
    rows, _, width = ref.shape
    return ref[:, pl.ds(pl.multiple_of(q * count, count), count), :].reshape(rows * count, width)


def chunk_at(ref, q, count):
    return ref.at[:, pl.ds(pl.multiple_of(q * count, count), count), :]


class Modes:
    def __init__(self, section, buffer, p_out, cross):
        self.section, self.buffer, self.p_out, self.cross = section, buffer, p_out, cross

    def view(self, q):
        n, halves, kx, count, lanes = self.buffer.shape[1:]
        return self.buffer.at[q].reshape(n * halves * kx, count, lanes)

    def cross_copy(self, q):
        return to_core(self.buffer.at[q, :, 1 - self.section], self.p_out.at[:, q, 1],
                       (self.cross.at[0, q], self.cross.at[1, q]), self.section)

    def start(self, q):
        self.cross_copy(q).start()
        self.p_out[:, q, 0] = self.buffer[q, :, self.section]

    def wait(self, q):
        self.cross_copy(q).wait()


class Bound:
    def __init__(self, section, owner, micro, other, source, bound, local, cross):
        self.section, self.owner, self.micro, self.other = section, owner, micro, other
        self.source, self.bound, self.local, self.cross = source, bound, local, cross

    def copies(self, q, count, micro):
        src, dst = chunk_at(self.source, q, count), chunk_at(self.bound.at[micro], q, count)
        return (pltpu.make_async_copy(src, dst, self.local.at[q]),
                to_core(src, dst, (self.cross.at[0, q], self.cross.at[1, q]), self.section))

    def start(self, q, count):
        here, there = self.copies(q, count, self.micro)

        @pl.when(self.section == self.owner)
        def _():
            here.start()

        @pl.when(self.section != self.owner)
        def _():
            there.start()

    def wait(self, q, count):
        here, there = self.copies(q, count, self.micro)
        come = self.copies(q, count, self.other)[1]

        @pl.when(self.section == self.owner)
        def _():
            here.wait()
            come.wait_recv()

        @pl.when(self.section != self.owner)
        def _():
            there.wait_send()


def add_squares(value, total):
    rows, _, width = total.shape
    square = (value * value).reshape(rows, -1, width)
    for at in range(0, square.shape[1], G):
        total[...] += square[:, at:at + G]


def region_sums(rid_ref, eo, eb, stat_ref):
    rows, _, width = eo.shape
    rid = rid_ref[...]
    energies = (jnp.sum(eo[...], axis=1), jnp.sum(eb[...], axis=1), jnp.ones((rows, width), F32))
    for kind in range(3):
        for region in range(R):
            line = jnp.sum(jnp.where(rid == region + 1, energies[kind], 0.0), axis=0, keepdims=True)
            total = line[:, :128]
            for piece in range(1, width // 128):
                total = total + line[:, piece * 128:(piece + 1) * 128]
            stat_ref[kind, region:region + 1, :] = total


class Share:
    def __init__(self, r, index, parity):
        self.r, self.index, self.parity = r, index, parity
        self.me, self.members = lax.axis_index("batch"), lax.axis_size("batch")

    def copies(self):
        source, target = self.r.keep.at[self.parity], getattr(self.r, f"shared{self.index}").at[self.me]
        yield pltpu.make_async_copy(source, target, self.r.s_local.at[self.parity])
        for away in range(1, self.members):
            yield pltpu.make_async_remote_copy(
                src_ref=source, dst_ref=target, send_sem=self.r.s_send.at[self.parity, away],
                recv_sem=self.r.s_recv.at[self.index, away],
                device_id={"batch": lax.rem(self.me + away, self.members)}, device_id_type=MESH)

    def start(self):
        for copy in self.copies():
            copy.start()

    def wait_send(self):
        for i, copy in enumerate(self.copies()):
            if i == 0:
                copy.wait()
            else:
                copy.wait_send()

    def wait_recv(self):
        for i, copy in enumerate(self.copies()):
            if i > 0:
                copy.wait_recv()


class Head:
    def __init__(self, micro, place, parity, section, r):
        self.r, self.field, self.sem = r, r.fields.at[place], r.field_sem.at[place]
        self.source, self.count = r.inputs.at[micro, 0], r.full.shape[5]
        self.modes = Modes(section, r.p_buf, r.part.at[parity], r.p_cross.at[parity])

    def fetch(self):
        fetch(self.source, self.field, self.sem, 4)

    def got(self):
        arrived(self.field, self.sem)

    def chunk(self, q):
        r = self.r
        to_modes(chunk_of(self.field, q, self.count), r.t_plain[...], r.kron[...], r.spread, self.modes.view(q))
        self.modes.start(q)


class Stage:
    def __init__(self, k, kind, j, per_core, places, section, z, n, r):
        self.k, self.kind, self.j, self.r, self.section, self.n = k, kind, j, r, section, n
        self.parity = k % 2
        self.micro, self.other = section * per_core + j, (1 - section) * per_core + j
        self.forward, self.last = kind in ("middle", "turn"), kind == "tail"
        self.buffers = {name: r.fields.at[i] for name, i in places.items()}
        self.sems = {name: r.field_sem.at[i] for name, i in places.items()}
        self.gather = Gather(section, z, n, r, self.parity)
        self.count, self.lanes = r.full.shape[5], r.full.shape[6]
        self.chunks = r.full.shape[1]
        plain = lambda name: getattr(r, f"{name}{j}")
        if kind == "middle":
            self.loads = dict(a=r.inputs.at[self.micro, 0])
            self.saves = dict(a=plain("a1_"), z=plain("dg0_"))
        elif kind == "turn":
            self.loads = dict(a=plain("a1_"), cot=r.cotangent.at[self.micro, 0])
            self.saves = dict(cot=plain("gz1_"))
        elif kind == "back":
            self.loads = dict(gz=plain("gz1_"), h=r.cotangent.at[self.micro, 0], a=plain("a1_"), dg=plain("dg0_"))
            self.saves = dict(h=plain("ga1_"), dg=plain("gz0_"))
        else:
            self.loads = dict(gz=plain("gz0_"), h=plain("ga1_"), a=r.inputs.at[self.micro, 0])
            self.saves = {}
        layer = 0 if kind in ("middle", "tail") else 1
        self.weight, self.bias = r.conv.at[layer if self.forward else 2 + layer], r.bias.at[layer]
        self.table = r.t_plain if kind == "middle" else r.t_doubled
        self.itable = r.it_doubled if self.forward else r.it_plain
        if not self.last:
            self.modes = Modes(section, r.p_buf, r.part.at[self.parity], r.p_cross.at[self.parity])
        if kind in ("turn", "tail"):
            self.bound = Bound(section, 1 if kind == "turn" else 0, self.micro, self.other,
                               self.buffers["a" if kind == "turn" else "h"], r.bound,
                               r.b_local.at[self.parity], r.b_cross.at[self.parity])

    def prefetch(self):
        for name, src in self.loads.items():
            if self.kind != "middle":
                fetch(src, self.buffers[name], self.sems[name])
        if self.forward:
            self.rid_copy().start()

    def rid_copy(self):
        return pltpu.make_async_copy(self.r.region.at[self.micro, 0], self.r.rid.at[self.parity],
                                     self.r.rid_sem.at[self.parity])

    def got(self, name):
        arrived(self.buffers[name], self.sems[name])

    def open(self):
        r, b = self.r, self.buffers
        if self.forward:
            r.eo[...] = jnp.zeros_like(r.eo)
            r.eb[...] = jnp.zeros_like(r.eb)
            if self.kind != "middle":
                self.got("a")
        else:
            for name in ("gz", "h", "a"):
                self.got(name)
            at = self.k - self.r.first_back
            r.cg[at] = jnp.zeros_like(r.cg[at])
            r.bg[at] = jnp.zeros_like(r.bg[at])

    def before(self, i):
        r, b = self.r, self.buffers
        a = b["a"]
        rows, channels = a.shape[:2]
        blocks, parts = rows // (self.weight.shape[0] // channels), self.n - 1
        span = (i * blocks // parts, (i + 1) * blocks // parts)
        if self.forward:
            conv_rows(self.weight, self.bias, a, b["z"], *span)
        else:
            conv_rows(self.weight, None, b["gz"], b["h"], *span)
            at = self.k - r.first_back
            grad_rows(a, b["gz"], r.cg.at[at], r.bg.at[at], i * rows // parts, (i + 1) * rows // parts)

    def outs(self, q):
        return [pltpu.make_async_copy(chunk_at(self.buffers[name], q, self.count), chunk_at(dst, q, self.count),
                                      self.r.out_sem.at[self.parity, i, q])
                for i, (name, dst) in enumerate(self.saves.items())]

    def late(self):
        for name in ("cot", "dg"):
            if name in self.loads:
                self.got(name)

    def chunk(self, q):
        r, b, count = self.r, self.buffers, self.count
        spectral = from_modes(self.gather.full.at[q].reshape(-1, count, self.lanes), self.itable[...], r.ikron[...],
                              r.spread)
        if self.forward:
            branch, slope = gelu_parts(spectral + chunk_of(b["z"], q, count))
            if self.kind == "turn":
                put(chunk_at(b["cot"], q, count), chunk_of(b["cot"], q, count) * slope)
            else:
                put(chunk_at(b["z"], q, count), slope)
            add_squares(branch, r.eb)
            out = chunk_of(b["a"], q, count) + branch
            put(chunk_at(b["a"], q, count), out)
            add_squares(out, r.eo)
            source = b["cot" if self.kind == "turn" else "a"]
        else:
            ga = spectral + chunk_of(b["h"], q, count)
            put(chunk_at(b["h"], q, count), ga)
            if not self.last:
                put(chunk_at(b["dg"], q, count), ga * chunk_of(b["dg"], q, count))
                source = b["dg"]
        for copy in self.outs(q):
            copy.start()
        if self.kind in ("turn", "tail"):
            self.bound.start(q, count)
        if not self.last:
            to_modes(chunk_of(source, q, count), self.table[...], r.kron[...], r.spread, self.modes.view(q))

            pl.when(q == self.chunks - 1)(self.gather.finish)
            self.modes.start(q)

    def end(self):
        if self.forward:
            self.rid_copy().wait()
            region_sums(self.r.rid.at[self.parity], self.r.eo, self.r.eb, self.r.stat.at[self.k])
        if self.last:
            self.gather.finish()

    def close(self):
        def body(q, carry):
            for copy in self.outs(q):
                copy.wait()
            if self.kind in ("turn", "tail"):
                self.bound.wait(q, self.count)
            return carry

        lax.fori_loop(0, self.chunks, body, 0)


def stages_kernel(per_core, kinds, places, mixes, r):
    section, z, n = place_and_peers()
    chunks, count = r.full.shape[1], r.full.shape[5]
    r.first_back = 2 * per_core
    stages = [Stage(k, kind, j, per_core, places[k], section, z, n, r)
              for k, (kind, j) in enumerate((kind, j) for kind in kinds for j in range(per_core))]
    heads = [Head(section * per_core + j, places[j]["a"], j, section, r) for j in range(per_core)]
    half = r.far.shape[0]

    def spare(q, x):
        groups = r.fields.shape[1] // count
        at = q * half + x
        place, at = 3 + at // (2 * groups), at % (2 * groups)
        side, group = at // groups, at % groups
        return r.fields.at[place, pl.ds(pl.multiple_of(group * count, count), count), :,
                           pl.ds(pl.multiple_of(side * 128, 128), 128)]

    def lend_in(q, x):
        rows = pl.ds(q * count, count)
        return pltpu.make_async_copy(r.weights.at[0, (1 - section) * half + x, rows], spare(q, x), r.w_load.at[q, x])

    def lent(q, x):
        return to_core(spare(q, x), r.far.at[x, pl.ds(q * count, count)],
                       (r.w_cross.at[0, q, x], r.w_cross.at[1, q, x]), section)

    blocks = [(q, x) for q in range(chunks) for x in range(half)]
    for head in heads:
        head.fetch()
    for block in blocks:
        lend_in(*block).start()
    greet(section, z, n, True, lax.axis_size("batch"))
    wide = r.full.at[1].reshape(-1, *r.wide_own.shape)
    small = [to_core(wide.at[section], wide.at[section], (r.m_cross.at[0, 0], r.m_cross.at[1, 0]), section),
             to_core(r.bias.at[section], r.bias.at[section], (r.m_cross.at[0, 1], r.m_cross.at[1, 1]), section)]
    wide[section] = r.wide_own[...]
    r.bias[section] = r.bias_own[...]
    for copy in small:
        copy.start()
    ahead, sums = [Sum(section, z, n, r, j, heads[j].modes.wait) for j in range(2)]
    mix = Mix(section, z, *mixes[0], ahead, stages[0].gather, r, lent)
    heads[0].got()

    def opening(q, carry):
        ahead.tick(q - 1)
        heads[0].chunk(q)

        @pl.when(q == 0)
        def _():
            for block in blocks:
                lend_in(*block).wait()
                lent(*block).start()

        return carry

    lax.fori_loop(0, chunks, opening, 0)
    for copy in small:
        copy.wait()
    for way in range(2):
        for layer in range(2):
            high, low = split(jnp.concatenate([wide[layer, way, side] for side in range(wide.shape[2])], 1))
            r.conv[2 * way + layer] = jnp.concatenate([high, low, high], 1)
    heads[1].got()
    mix.prime()

    def second(q, carry):
        ahead.tick(q + chunks - 1)

        @pl.when(q < chunks)
        def _():
            heads[1].chunk(q)

        sums.tick(q - 1)
        pl.when(within(q + chunks - n, chunks))(lambda: mix.chunk(q + chunks - n))
        return carry

    lax.fori_loop(0, n, second, 0)
    ahead.finish()
    mix.finish()
    shares = [Share(r, 0, 0)]
    shares[0].start()
    for block in blocks:
        lent(*block).wait_send()
    stages[0].prefetch()
    for k, stage in enumerate(stages):
        gather = stage.gather
        now = None if stage.last else Sum(section, z, n, r, stage.parity, stage.modes.wait)
        mix = None
        if sums is not None:
            mix = Mix(section, z, *mixes[(k + 1) // per_core], sums, stages[k + 1].gather, r)
            share = Share(r, k + 1, 1 - stage.parity)
            if k >= 1:
                shares[k - 1].wait_send()
            shares.append(share)
            mix.prime()
        lead = n - 1 if k == 0 else chunks - 1
        ready = n - 1 - lead
        stage.open()

        def early(i, carry):
            if sums is not None:
                sums.tick(i + lead)
            gather.tick(i)
            stage.before(i)
            if mix is not None and not mix.flip:
                pl.when(within(i - ready, chunks))(lambda: mix.chunk(i - ready))
            return carry

        lax.fori_loop(0, n - 1, early, 0)
        if k > 0:
            stages[k - 1].close()
        if k + 1 < len(stages):
            stages[k + 1].prefetch()
        stage.late()

        def later(q, carry):
            i = q + n - 1
            if sums is not None:
                sums.tick(i + lead)
            if now is not None:
                now.tick(i - n)
            gather.tick(i)
            stage.chunk(q)
            if mix is not None:
                if mix.flip:
                    pl.when(q == 0)(sums.finish)
                    mix.chunk(q)
                else:
                    pl.when(within(i - ready, chunks))(lambda: mix.chunk(i - ready))
            return carry

        lax.fori_loop(0, chunks, later, 0)
        if mix is not None:
            if not mix.flip:
                sums.finish()
            mix.finish()
            share.start()
        stage.end()
        sums = now
    stages[-1].close()
    for share in shares[-2:]:
        share.wait_send()
    for share in shares:
        share.wait_recv()


def swap_halves(value):
    return pltpu.roll(value, value.shape[-1] // 2, value.ndim - 1)


def left_lanes(shape):
    return lax.broadcasted_iota(jnp.int32, shape, len(shape) - 1) < shape[-1] // 2


def pieces(array):
    return [array[at:at + G] for at in range(0, array.shape[0], G)]


def spread_row(ref, row):
    return ref[pl.ds(row, G, stride=0), :]


class Mix:
    def __init__(self, section, z, layer, flip, sums, gather, r, lent=None):
        self.lent = lent
        self.section, self.z, self.layer, self.flip, self.r = section, z, layer, flip, r
        self.sums, self.gather = sums, gather
        self.chunks, self.grids, self.half, self.count, self.lanes = sums.part.shape[1:]
        self.channels, self.slots = r.weights.shape[2], r.wbuf.shape[0]
        self.blocks = self.chunks * self.half // 2

    def begin(self, block):
        per = self.half // 2
        q, x = block // per, 2 * (block % per)
        slot = lax.rem(block, self.slots)
        rows = pl.ds(q * self.count, self.count)
        if self.lent is not None:
            for at in range(2):
                self.lent(q, x + at).wait_recv()

        @pl.when(self.section == self.layer)
        def _():
            pltpu.make_async_copy(self.r.weights.at[0, pl.ds(self.section * self.half + x, 2), rows],
                                  self.r.wbuf.at[slot], self.r.wsem.at[slot]).start()

        @pl.when(self.section != self.layer)
        def _():
            pltpu.make_async_copy(self.r.far.at[pl.ds(x, 2), rows], self.r.wbuf.at[slot], self.r.wsem.at[slot]).start()

    def prime(self):
        for block in range(min(self.slots, self.blocks)):
            self.begin(jnp.int32(block))
        if not self.flip:
            self.r.macc[...] = jnp.zeros_like(self.r.macc)

    def chunk(self, q):
        def body(x, carry):
            block = q * (self.half // 2) + x // 2
            slot = lax.rem(block, self.slots)

            @pl.when(lax.rem(x, 2) == 0)
            def _():
                arrived(self.r.wbuf.at[slot], self.r.wsem.at[slot])

            (self.transposed if self.flip else self.forward)(q, x, self.r.wbuf.at[slot, lax.rem(x, 2)])

            @pl.when(jnp.logical_and(lax.rem(x, 2) == 1, block + self.slots < self.blocks))
            def _():
                self.begin(block + self.slots)

            return carry

        lax.fori_loop(0, self.half, body, 0)
        if self.flip:
            self.gather.give(q)

    def forward(self, q, x, weight):
        sides, groups = 2 * self.grids, self.channels // G
        total, source = self.r.macc.at[x], self.r.msrc
        for g in range(self.grids):
            value = self.sums.part[self.z, q, g, x]
            source[2 * g, :self.count] = value
            source[2 * g + 1, :self.count] = swap_halves(value)
        keys = [(k, o) for k in range(sides) for o in range(groups)]

        def body(octet, acc):
            acc = dict(zip(keys, acc))
            for u in range(G):
                i = octet * G + u
                rows = [spread_row(source.at[k], i) for k in range(sides)]
                for o in range(groups):
                    w = weight[i, o * G:(o + 1) * G, :]
                    for k in range(sides):
                        acc[k, o] = acc[k, o] + rows[k] * w
            return tuple(acc[key] for key in keys)

        acc = lax.fori_loop(0, self.count // G, body, tuple(total[k, o * G:(o + 1) * G, :] for k, o in keys))
        for key, value in zip(keys, acc):
            total[key[0], key[1] * G:(key[1] + 1) * G, :] = value

    def transposed(self, q, x, weight):
        sides, groups = 2 * self.grids, self.channels // G
        source = self.r.msrc
        for g in range(self.grids):
            value = jnp.concatenate([self.sums.part[self.z, at, g, x] for at in range(self.chunks)], 0)
            source[2 * g] = value
            source[2 * g + 1] = swap_halves(value)
        rows = [pieces(source[k]) for k in range(sides)]
        out = [[] for _ in range(sides)]
        for i in range(self.count):
            total = [None] * sides
            for o in range(groups):
                w = weight[i, o * G:(o + 1) * G, :]
                for k in range(sides):
                    term = w * rows[k][o]
                    total[k] = term if total[k] is None else total[k] + term
            for k in range(sides):
                out[k].append(jnp.sum(total[k], axis=0, keepdims=True))
        left = left_lanes((self.count, self.lanes))
        for g in range(self.grids):
            a, b = [jnp.concatenate(out[2 * g + side], 0) for side in range(2)]
            self.put(g, q, x, jnp.where(left, a + swap_halves(a), swap_halves(b) - b))

    def put(self, g, q, x, value):
        if g == 0:
            self.gather.full[q, self.z, self.section, x] = value
        else:
            self.gather.give_from[q, x] = value

    def finish(self):
        if self.flip:
            return
        left = left_lanes((self.channels, self.lanes))

        def body(x, carry):
            for g in range(self.grids):
                a, b = [self.r.macc[x, 2 * g + side] for side in range(2)]
                result = jnp.where(left, a - swap_halves(a), b + swap_halves(b))
                for q in range(self.chunks):
                    self.put(g, q, x, result[q * self.count:(q + 1) * self.count])
            return carry

        lax.fori_loop(0, self.half, body, 0)
        for q in range(self.chunks):
            self.gather.give(q)


def gather_columns(f_ref, d_ref, left_of, right_of):
    channels = f_ref.shape[2] * f_ref.shape[5]
    lanes = f_ref.shape[6]
    left = left_lanes((channels, lanes))
    for stream in range(f_ref.shape[0]):
        for member in range(f_ref.shape[1]):
            for g in range(f_ref.shape[3]):
                at = (stream * f_ref.shape[1] + member) * f_ref.shape[3] + g
                both = []
                for x in range(2):
                    f = f_ref[stream, member, :, g, x].reshape(channels, lanes)
                    turned = swap_halves(f)
                    left_of[x, at] = jnp.concatenate([f, jnp.where(left, -turned, turned)], 0).T
                    both.append(d_ref[stream, member, :, g, x].reshape(channels, lanes))
                right_of[at] = jnp.concatenate(both, 0).T


def column_products(left_of, right_of, product):
    grids, double, lanes = right_of.shape
    half = double // 2
    left = left_lanes((2 * grids, lanes))
    rows = right_of.reshape(grids * double, lanes)
    sides = [left_of.at[x].reshape(grids * double, lanes) for x in range(2)]

    def body(k, carry):
        pick = pl.ds(k, 2 * grids, stride=half)
        d = rows[pick, :]
        f_high, f_low = split(jnp.concatenate([side[pick, :] for side in sides], 0))
        d_high, d_low = split(jnp.concatenate([jnp.where(left, d, 0.0), jnp.where(left, 0.0, d)], 0))
        product[k] = dot(jnp.concatenate([f_high, f_low, f_high], 0), jnp.concatenate([d_high, d_high, d_low], 0),
                         (((0,), (0,)), ((), ())))
        return carry

    lax.fori_loop(0, half, body, 0, unroll=4)


def product_rows(product, first, out):
    half, double, lanes = product.shape
    channels = double // 2
    rows = product.reshape(half * double, lanes)

    def body(i, carry):
        parts = [rows[pl.ds(part * channels + first + i, half, stride=double), :] for part in range(2)]
        tile = jnp.concatenate(parts, 0).T
        for x in range(2):
            out[x, i] = tile[x * channels:(x + 1) * channels]
        return carry

    lax.fori_loop(0, out.shape[1], body, 0, unroll=4)


class GradInput:
    def __init__(self, first, f, g, fbuf, gbuf, sem):
        self.first, self.f, self.g, self.fbuf, self.gbuf, self.sem = first, f, g, fbuf, gbuf, sem

    def load(self, x, slot):
        for layer, condition in enumerate((self.first, jnp.logical_not(self.first))):
            @pl.when(condition)
            def _():
                for j in range(len(self.f[layer])):
                    pltpu.make_async_copy(self.f[layer][j].at[:, :, :, pl.ds(2 * x, 2)], self.fbuf.at[slot, j],
                                          self.sem.at[0, slot]).start()
                    pltpu.make_async_copy(self.g[layer][j].at[:, :, :, pl.ds(2 * x, 2)], self.gbuf.at[slot, j],
                                          self.sem.at[1, slot]).start()

    def next(self, x, count):
        slot = lax.rem(x, 2)

        @pl.when(x + 1 < count)
        def _():
            self.load(x + 1, 1 - slot)

        arrived(self.fbuf.at[slot], self.sem.at[0, slot])
        arrived(self.gbuf.at[slot], self.sem.at[1, slot])
        return self.fbuf.at[slot], self.gbuf.at[slot]


def grad_input(r, first, per_core):
    f = [[getattr(r, f"f{layer}{j}") for j in range(per_core)] for layer in range(2)]
    g = [[getattr(r, f"g{layer}{j}") for j in range(per_core)] for layer in range(2)]
    return GradInput(first, f, g, r.fbuf, r.gbuf, r.in_sem)


def far_grad_kernel(per_core, r):
    section, z, n = place_and_peers()
    pairs, block = r.far.shape[0] // 2, r.out.shape[2]
    blocks = r.far.shape[1] // block
    source = grad_input(r, section != 0, per_core)

    def move(k, slot):
        p, i = k // blocks, k % blocks
        return to_core(r.out.at[slot], r.far.at[pl.ds(2 * p, 2), pl.ds(i * block, block)], (r.send.at[k], r.recv.at[k]),
                       section)

    source.load(0, 0)
    greet(section, z, n, False)

    def body(p, carry):
        gather_columns(*source.next(p, pairs), r.left_of, r.right_of)
        column_products(r.left_of, r.right_of, r.product)

        def inner(i, carry):
            k = p * blocks + i

            @pl.when(k >= 2)
            def _():
                move(k - 2, lax.rem(k, 2)).wait_send()

            product_rows(r.product, i * block, r.out.at[lax.rem(k, 2)])
            move(k, lax.rem(k, 2)).start()
            return carry

        return lax.fori_loop(0, blocks, inner, carry)

    lax.fori_loop(0, pairs, body, 0)
    total = pairs * blocks
    for k in (total - 2, total - 1):
        move(k, k % 2).wait_send()

    def close(k, carry):
        move(k, 0).wait_recv()
        return carry

    lax.fori_loop(0, total, close, 0)


def own_grad_kernel(names, per_core, m_ref, *refs):
    r = types.SimpleNamespace(**dict(zip(names, refs)))
    p, i = pl.program_id(0), pl.program_id(1)
    source = grad_input(r, m_ref[0] == 0, per_core)

    @pl.when(i == 0)
    def _():
        @pl.when(p == 0)
        def _():
            source.load(0, 0)

        gather_columns(*source.next(p, pl.num_programs(0)), r.left_of, r.right_of)
        column_products(r.left_of, r.right_of, r.product)

    r.bound_out[...] = r.bound_in[...]
    r.out[1 - m_ref[0]] = r.far[...]
    product_rows(r.product, i * r.out.shape[2], r.out.at[m_ref[0]])


def whole(array):
    return pl.BlockSpec(array.shape, lambda *_: (0,) * array.ndim)


def params(**kw):
    return pltpu.CompilerParams(vmem_limit_bytes=VMEM_LIMIT, **kw)


def local(inputs, cotangent, region_id, spectral_w, conv_w, bias_vector):
    micro_count, _, rows_dev, channels, width = inputs.shape
    lanes = spectral_w.shape[-1]
    half = lanes // 2
    kx_dev = spectral_w.shape[1]
    row_devices, sections = lax.axis_size("rows"), lax.axis_size("section")
    mode_rows, height = kx_dev * row_devices, rows_dev * row_devices
    section = lax.axis_index("section")
    per_core = micro_count // sections
    kx_half = kx_dev // sections

    plain, doubled = col_tables(width, half)

    def stacked(array):
        high, low = np_split(array)
        return np.concatenate([high, high, low], 0)

    t_plain, t_doubled, it_plain, it_doubled = [stacked(t) for t in (plain, doubled, plain.T, doubled.T)]
    kron, ikron = row_tables(height, mode_rows, lax.axis_index("rows") * rows_dev, rows_dev)

    count = 2 * G
    chunks = channels // count
    hbm, vmem = pl.BlockSpec(memory_space=pl.ANY), pl.BlockSpec(memory_space=pltpu.VMEM)
    field_shape = jax.ShapeDtypeStruct((rows_dev, channels, width), F32)
    part_dims = (row_devices, chunks, sections, kx_half, count, lanes)
    p_shape, f_shape = jax.ShapeDtypeStruct(part_dims, F32), jax.ShapeDtypeStruct(part_dims[1:], F32)
    y_shape = jax.ShapeDtypeStruct((sections, chunks, kx_half, count, lanes), F32)
    stat_shape = jax.ShapeDtypeStruct((3, R, 128), F32)
    cg_shape = jax.ShapeDtypeStruct((2 * channels, 2 * channels), F32)
    bg_shape = jax.ShapeDtypeStruct((channels, width), F32)
    bound_shape = jax.ShapeDtypeStruct((micro_count, rows_dev, channels, width), F32)
    dma = pltpu.SemaphoreType.DMA
    field_buf = pltpu.VMEM((rows_dev, channels, width), F32)
    full_dims = (chunks, row_devices, sections, kx_half, count, lanes)
    spread = pltpu.VMEM((width // 128, rows_dev * count, 128), F32)
    energy = pltpu.VMEM((rows_dev, G, width), F32)
    line_sems = dma((2, chunks, row_devices))
    def run(body, ident, ins, outs, scratch, cost=50, aliases=None):
        names = [*ins, *outs, *scratch]
        spec = lambda entry: vmem if isinstance(entry, tuple) else hbm
        plain = lambda entry: entry[0] if isinstance(entry, tuple) else entry
        kernel = lambda *refs: body(types.SimpleNamespace(**dict(zip(names, refs))))
        positions = {list(ins).index(k): list(outs).index(v) for k, v in (aliases or {}).items()}
        result = pl.pallas_call(
            kernel, in_specs=[spec(e) for e in ins.values()], out_specs=[spec(e) for e in outs.values()],
            out_shape=[plain(e) for e in outs.values()], scratch_shapes=list(scratch.values()),
            input_output_aliases=positions,
            cost_estimate=pl.CostEstimate(flops=0, bytes_accessed=cost * 3_000_000, transcendentals=0),
            compiler_params=params(collective_id=ident, has_side_effects=True))(*[plain(e) for e in ins.values()])
        return types.SimpleNamespace(**dict(zip(outs, result)))

    conv_rows_at_once = 256 // channels
    maps = jnp.stack([conv_w[0].T, conv_w[0]])
    at = np.arange(conv_rows_at_once * channels) // channels
    wide_own = jnp.where(at[:, None] == at[None, :], jnp.tile(maps, (1, conv_rows_at_once, conv_rows_at_once)), 0.0)
    wide_own = jnp.stack(jnp.split(wide_own, wide_own.shape[2] // 128, 2), 1)
    bias_own = jnp.broadcast_to(bias_vector[0][:, None], (channels, width))

    streams = range(per_core)
    members = lax.axis_size("batch")
    kinds = ["middle", "turn", "back", "tail"]
    mixes = [(0, False), (1, False), (1, True), (0, True)]
    names = ["f00", "f01", "f10", "f11", "g10", "g11", "g00", "g01"]
    places = [dict(a=0, z=1), dict(a=2, z=3), dict(a=4, z=5, cot=6), dict(a=0, z=1, cot=2),
              dict(gz=3, a=4, h=5, dg=6), dict(gz=0, a=1, h=2, dg=3), dict(gz=4, a=5, h=6), dict(gz=0, a=1, h=2)]
    both = (2,)
    ins = dict(inputs=inputs, cotangent=cotangent, region=region_id, weights=spectral_w, t_plain=(t_plain,),
               t_doubled=(t_doubled,), it_plain=(it_plain,), it_doubled=(it_doubled,), kron=(kron,), ikron=(ikron,),
               wide_own=(wide_own,), bias_own=(bias_own,))
    outs = dict(far=jax.ShapeDtypeStruct((kx_half,) + spectral_w.shape[2:], F32), bound=bound_shape, stat=(jax.ShapeDtypeStruct((2 * per_core,) + stat_shape.shape, F32),),
                cg=(jax.ShapeDtypeStruct((2 * per_core,) + cg_shape.shape, F32),),
                bg=(jax.ShapeDtypeStruct((2 * per_core,) + bg_shape.shape, F32),),
                **{f"{name}{j}": field_shape for name in ("a1_", "dg0_", "gz1_", "ga1_", "gz0_") for j in streams},
                **{f"shared{i}": jax.ShapeDtypeStruct((members,) + f_shape.shape, F32) for i in range(len(names))})
    scratch = dict(
        fields=pltpu.VMEM((7,) + field_shape.shape, F32), full=pltpu.VMEM(both + full_dims, F32),
        part=pltpu.VMEM(both + part_dims, F32),
        come=pltpu.VMEM(both + (2, chunks, row_devices - 1) + part_dims[2:], F32),
        keep=pltpu.VMEM(both + f_shape.shape, F32), y_give=pltpu.VMEM(both + y_shape.shape[1:], F32),
        p_buf=pltpu.VMEM(full_dims, F32), spread=spread, eo=energy, eb=energy,
        rid=pltpu.VMEM((2, rows_dev, width), jnp.int32),
        wbuf=pltpu.VMEM((3, 2, count, channels, lanes), F32), macc=pltpu.VMEM((kx_half, 2 * sections, channels, lanes), F32),
        msrc=pltpu.VMEM((2 * sections, channels, lanes), F32),
        bias=pltpu.VMEM((2, channels, width), F32),
        conv=pltpu.VMEM((4, len(at), 3 * len(at)), BF16), m_cross=dma((2, 2)),
        field_sem=dma((7,)), rid_sem=dma(both), out_sem=dma((2, 2, chunks)), wsem=dma((3,)), w_load=dma((chunks, kx_half)), w_cross=dma((2, chunks, kx_half)),
        send=dma(both + (2, chunks, row_devices)), recv=dma(both + (2, chunks, row_devices)),
        red_send=dma(both + (2, chunks, row_devices)), red_recv=dma(both + (2, chunks, row_devices)),
        y_cross=dma((2, 2, chunks)), p_cross=dma((2, 2, chunks)),
        b_local=dma((2, chunks)), b_cross=dma((2, 2, chunks)),
        s_local=dma(both), s_send=dma((2, members)), s_recv=dma((len(names), members)))
    done = run(functools.partial(stages_kernel, per_core, kinds, places, mixes), 0, ins, outs, scratch, cost=400)
    gathered = {name: getattr(done, f"shared{i}") for i, name in enumerate(names)}
    bound, calls = done.bound, 0

    grids = per_core * members * sections
    block = 2 * G
    pairs, blocks = kx_half // 2, channels // block
    in_buf = pltpu.VMEM((2, per_core, members, chunks, sections, 2, count, lanes), F32)
    grad_scratch = dict(fbuf=in_buf, gbuf=in_buf, in_sem=dma((2, 2)), left_of=pltpu.VMEM((2, grids, lanes, lanes), F32),
                        right_of=pltpu.VMEM((grids, lanes, lanes), F32), product=pltpu.VMEM((half, lanes, lanes), F32))
    far_grad = run(functools.partial(far_grad_kernel, per_core), 1 + calls, gathered,
                   dict(far=jax.ShapeDtypeStruct((kx_half, channels, channels, lanes), F32)),
                   dict(out=pltpu.VMEM((2, 2, block, channels, lanes), F32), send=dma((pairs * blocks,)),
                        recv=dma((pairs * blocks,)), **grad_scratch)).far
    bound_rows = bound.reshape(micro_count * rows_dev, channels, width)
    bound_block = pl.BlockSpec((bound_rows.shape[0] // (pairs * blocks), channels, width),
                               lambda p, i, m: (p * blocks + i, 0, 0))
    grid_spec = pltpu.PrefetchScalarGridSpec(
        num_scalar_prefetch=1, grid=(pairs, blocks),
        in_specs=[hbm] * len(gathered)
        + [pl.BlockSpec((2, block, channels, lanes), lambda p, i, m: (p, i, 0, 0)), bound_block],
        out_specs=[pl.BlockSpec((2, 2, block, channels, lanes), lambda p, i, m: (0, p, i, 0, 0)), bound_block],
        scratch_shapes=list(grad_scratch.values()))
    spectral_grad, boundary = pl.pallas_call(
        functools.partial(own_grad_kernel, [*gathered, "far", "bound_in", "out", "bound_out", *grad_scratch], per_core),
        grid_spec=grid_spec, out_shape=[jax.ShapeDtypeStruct((2, kx_half, channels, channels, lanes), F32),
                                        jax.ShapeDtypeStruct(bound_rows.shape, F32)],
        cost_estimate=pl.CostEstimate(flops=0, bytes_accessed=150_000_000, transcendentals=0),
        compiler_params=params())(
            jnp.reshape(section, (1,)).astype(jnp.int32), *gathered.values(), far_grad, bound_rows)
    spectral_grad = spectral_grad.reshape(spectral_w.shape)
    boundary = boundary.reshape((1, micro_count, 1) + inputs.shape[2:])

    def lower(value):
        return (value[:channels, :channels] + value[channels:, channels:]
                + value[:channels, channels:] + value[channels:, :channels])

    pair = lambda value: jnp.sum(value.reshape((2, per_core) + value.shape[1:]), 1)
    conv_local = jnp.stack([lower(value) for value in pair(done.cg)[::-1]])
    bias_local = jnp.sum(pair(done.bg)[::-1], -1)
    stat_local = jnp.sum(pair(done.stat), -1)
    shapes = [v.shape for v in (conv_local, bias_local, stat_local)]
    flat_sums = jnp.concatenate([v.reshape(-1) for v in (conv_local, bias_local, stat_local)])
    length = flat_sums.shape[0]
    flat_sums = jnp.pad(flat_sums, (0, -length % 1024)).reshape(-1, 128)
    flat_sums = jnp.sum(lax.all_gather(flat_sums, ("section", "batch", "rows"), axis=0), 0).reshape(-1)
    ends = np.cumsum([0] + [math.prod(shape) for shape in shapes])
    conv_sum, bias_sum, stat_sum = [flat_sums[ends[i]:ends[i + 1]].reshape(shapes[i]) for i in range(3)]
    own_stat = lax.dynamic_index_in_dim(stat_sum, section, 0, False)
    layer_rms = jnp.sqrt(own_stat[:2] / (channels * own_stat[2])[None, :] + 1e-06)[None]
    own = lambda value: lax.dynamic_slice_in_dim(value, section, 1, 0)
    return boundary, spectral_grad, own(conv_sum), own(bias_sum), layer_rms


def solution(mesh):
    placed = (
        P(None, "batch", "rows", None, None),
        P(None, "batch", "rows", None, None),
        P(None, "batch", "rows", None),
        P("section", "rows", None, None, None),
        P("section", None, None),
        P("section", None),
    )
    return jax.shard_map(
        local,
        mesh=mesh,
        in_specs=placed,
        out_specs=(
            P("section", None, "batch", "rows", None, None),
            P("section", "rows", None, None, None),
            P("section", None, None),
            P("section", None),
            P("section", None, None),
        ),
        check_vma=False,
    )
```

```python
import functools
import math
import types

import jax
import jax.numpy as jnp
import numpy as np
from jax import lax
from jax.experimental import pallas as pl
from jax.experimental.pallas import tpu as pltpu
from jax.sharding import PartitionSpec as P

R = 8
G = 8
F32 = jnp.float32
BF16 = jnp.bfloat16
VMEM_LIMIT = 62 * 1024 * 1024
MESH = pl.DeviceIdType.MESH


def split(value):
    high = value.astype(BF16)
    return high, (value - high.astype(F32)).astype(BF16)


def dot(left, right, dims=(((1,), (0,)), ((), ()))):
    return lax.dot_general(left, right, dims, preferred_element_type=F32)


def dot3(left, right):
    return dot(left[0], right[0]) + (dot(left[1], right[0]) + dot(left[0], right[1]))


def np_split(value):
    high = value.astype(np.float32).astype(BF16)
    return high, (value - high.astype(np.float64)).astype(np.float32).astype(BF16)


def col_tables(width, half):
    phase = 2.0 * math.pi / width * (np.outer(np.arange(width), np.arange(half)) % width)
    cosine, sine = np.cos(phase) / math.sqrt(width), np.sin(phase) / math.sqrt(width)
    plain = np.concatenate([cosine, -sine, -sine, -cosine], 1)
    doubled = plain * np.tile(np.where(np.arange(half) == 0, 1.0, 2.0), 4)[None, :]
    return plain, doubled


def row_tables(height, mode_rows, first_row, rows_dev):
    position = jnp.arange(mode_rows, dtype=jnp.int32)
    frequency = jnp.where(position < mode_rows // 2, position, height - mode_rows + position)
    row = first_row + jnp.arange(rows_dev, dtype=jnp.int32)
    phase = 2.0 * math.pi / height * (frequency[:, None] * row[None, :] % height).astype(F32)
    small = jnp.concatenate([jnp.cos(phase), jnp.sin(phase)], 1) / math.sqrt(height)
    rounded = lax.reduce_precision(small, 8, 7)
    high, low = rounded.astype(BF16), (small - rounded).astype(BF16)
    forward = jnp.concatenate([jnp.concatenate([high, high], 1), jnp.concatenate([low, jnp.zeros_like(low)], 1)], 0)
    inverse = jnp.concatenate([high.T, high.T, low.T], 1)
    return forward, inverse


def to_modes(value, table, kron, spread, p_ref):
    mode_rows, count, lanes = p_ref.shape
    rows = value.shape[0] // count
    high, low = split(value)
    spectra = dot(jnp.concatenate([high, low, high], 1), table)
    for i in range(2):
        spread[i] = spectra[:, i * lanes:(i + 1) * lanes]
    out = p_ref.reshape(mode_rows * count, lanes)
    for first in range(0, count, 2):
        sides = []
        for c in (first, first + 1):
            pick = pl.ds(c, rows, stride=count)
            sides.append(jnp.concatenate([spread[i, pick, :] for i in range(2)], 0))
        high, low = split(jnp.concatenate(sides, 1))
        both = dot(kron, jnp.concatenate([high, low], 0))
        result = both[:mode_rows] + both[mode_rows:]
        for i in range(2):
            out[pl.ds(first + i, mode_rows, stride=count), :] = result[:, i * lanes:(i + 1) * lanes]


def from_modes(y_ref, table, kron, spread):
    mode_rows, count, lanes = y_ref.shape
    rows, pieces = spread.shape[1] // count, spread.shape[0]
    modes = y_ref.reshape(mode_rows * count, lanes)
    sides = []
    for first in range(0, count, 2):
        pair = [modes[pl.ds(c, mode_rows, stride=count), :] for c in (first, first + 1)]
        high, low = split(jnp.concatenate(pair, 1))
        both = dot(kron, jnp.concatenate([high, low, high], 0))
        for i in range(2):
            side = both[:, i * lanes:(i + 1) * lanes]
            sides.append(jnp.concatenate([side[:rows], side[rows:]], 1))
    high, low = split(jnp.concatenate(sides, 0))
    out = dot(jnp.concatenate([high, low, high], 1), table)
    for c in range(count):
        for i in range(pieces):
            spread[i, pl.ds(c, rows, stride=count), :] = out[c * rows:(c + 1) * rows, i * 128:(i + 1) * 128]
    return jnp.concatenate([spread[i] for i in range(pieces)], 1)


def gelu_parts(z):
    gauss = jnp.exp2((-0.5 / math.log(2.0)) * (z * z))
    base = 1.0 + (0.3275911 / math.sqrt(2.0)) * jnp.abs(z)
    t = pl.reciprocal(base, approx=True)
    t = t * (2.0 - base * t)
    poly = t * (0.127414796 + t * (-0.142248368 + t * (0.7107068705 + t * (-0.7265760135 + t * 0.5307027145))))
    tail = poly * gauss
    phi = jnp.where(z >= 0, 1.0 - tail, tail)
    return z * phi, phi + z * (gauss * (1.0 / math.sqrt(2.0 * math.pi)))


def flat(ref):
    rows, count, width = ref.shape
    return ref[...].reshape(rows * count, width)


def put(ref, value):
    ref[...] = value.reshape(ref.shape)


def place_and_peers():
    section, z = lax.axis_index("section"), lax.axis_index("rows")
    return section, z, lax.axis_size("rows")


def greet(section, z, n, lines, members=0):
    barrier = pltpu.get_barrier_semaphore()
    pl.semaphore_signal(barrier, inc=1, device_id={"section": 1 - section}, device_id_type=MESH)
    if not lines:
        pl.semaphore_wait(barrier, 1)
        return

    @pl.when(z > 0)
    def _():
        pl.semaphore_signal(barrier, inc=1, device_id={"rows": z - 1}, device_id_type=MESH)

    @pl.when(z < n - 1)
    def _():
        pl.semaphore_signal(barrier, inc=1, device_id={"rows": z + 1}, device_id_type=MESH)

    for away in range(1, members):
        pl.semaphore_signal(barrier, inc=1, device_id={"batch": lax.rem(lax.axis_index("batch") + away, members)},
                            device_id_type=MESH)

    others = 1 + max(members - 1, 0)
    pl.semaphore_wait(barrier, others + (z > 0).astype(jnp.int32) + (z < n - 1).astype(jnp.int32))


def to_core(src, dst, sems, section):
    return pltpu.make_async_remote_copy(src_ref=src, dst_ref=dst, send_sem=sems[0], recv_sem=sems[1],
                                        device_id={"section": 1 - section}, device_id_type=MESH)


def guard(condition, body):
    if isinstance(condition, (bool, np.bool_)):
        if condition:
            body()
    else:
        pl.when(condition)(body)


class Line:
    def __init__(self, section, z, n, chunks, send, recv):
        self.section, self.z, self.n, self.chunks = section, z, n, chunks
        self.send, self.recv = send, recv

    def move(self, way, q, hop, src, dst):
        return pltpu.make_async_remote_copy(
            src_ref=src, dst_ref=dst, send_sem=self.send.at[way, q, hop], recv_sem=self.recv.at[way, q, hop],
            device_id={"rows": self.z + 1 if way == 0 else self.z - 1}, device_id_type=MESH)

    def sends(self, way):
        return self.z < self.n - 1 if way == 0 else self.z > 0

    def hears(self, way):
        return self.z > 0 if way == 0 else self.z < self.n - 1


def within(value, count):
    return jnp.logical_and(value >= 0, value < count)


class Gather(Line):
    def __init__(self, section, z, n, r, parity):
        super().__init__(section, z, n, r.full.shape[1], r.send.at[parity], r.recv.at[parity])
        self.full, self.give_from = r.full.at[parity], r.y_give.at[parity]
        self.cross = r.y_cross.at[parity]

    def swap(self, q):
        return to_core(self.give_from.at[q], self.full.at[q, self.z, self.section],
                       (self.cross.at[0, q], self.cross.at[1, q]), self.section)

    def give(self, q):
        self.swap(q).start()

    def hop(self, way, q, hop):
        piece = self.full.at[q, self.source(way, hop)]
        return self.move(way, q, hop, piece, piece)

    def source(self, way, hop):
        return self.z - hop if way == 0 else self.z + hop

    def known(self, way, hop):
        at = self.source(way, hop)
        return at >= 0 if way == 0 else at < self.n

    def own(self, q):
        self.swap(q).wait_recv()
        for way in range(2):
            @pl.when(self.sends(way))
            def _():
                self.hop(way, q, 0).start()

    def step(self, q, hop):
        for way in range(2):
            @pl.when(self.known(way, hop + 1))
            def _():
                piece = self.full.at[q, self.source(way, hop + 1)]
                self.move(way, q, hop, piece, piece).wait_recv()

                @pl.when(self.sends(way))
                def _():
                    self.hop(way, q, hop + 1).start()

    def tick(self, t):
        pl.when(within(t, self.chunks))(functools.partial(self.own, t))
        for hop in range(self.n - 1):
            q = t - hop - 1
            pl.when(within(q, self.chunks))(functools.partial(self.step, q, hop))

    def finish(self):
        def body(q, carry):
            self.swap(q).wait_send()
            for way in range(2):
                for hop in range(self.n - 1):
                    @pl.when(jnp.logical_and(self.sends(way), self.known(way, hop)))
                    def _():
                        self.hop(way, q, hop).wait_send()
            return carry

        lax.fori_loop(0, self.chunks, body, 0)


class Sum(Line):
    def __init__(self, section, z, n, r, parity, admit):
        super().__init__(section, z, n, r.part.shape[2], r.red_send.at[parity], r.red_recv.at[parity])
        self.part, self.come, self.keep, self.admit = r.part.at[parity], r.come.at[parity], r.keep.at[parity], admit

    def owner(self, way, hop):
        return self.z + self.n - hop if way == 0 else self.z - self.n + hop

    def valid(self, way, hop):
        return self.z <= hop - 1 if way == 0 else self.z >= self.n - hop

    def sent(self, way, q, hop):
        return self.move(way, q, hop, self.part.at[self.owner(way, hop), q], self.come.at[way, q, hop - 1])

    def heard(self, way, q, hop):
        come = self.come.at[way, q, hop - 1]
        self.move(way, q, hop, come, come).wait_recv()

    def first(self, q):
        self.admit(q)
        self.step(q, 1)

    def step(self, q, hop):
        for way in range(2):
            @pl.when(self.valid(way, hop))
            def _():
                if hop > 1:
                    @pl.when(self.hears(way))
                    def _():
                        self.heard(way, q, hop - 1)
                        owner = self.owner(way, hop)
                        self.part[owner, q] = self.part[owner, q] + self.come[way, q, hop - 2]

                self.sent(way, q, hop).start()

    def final(self, q):
        for way in range(2):
            @pl.when(self.hears(way))
            def _():
                self.heard(way, q, self.n - 1)
                self.part[self.z, q] = self.part[self.z, q] + self.come[way, q, self.n - 2]

        self.keep[q] = self.part[self.z, q]

    def tick(self, t):
        pl.when(within(t, self.chunks))(functools.partial(self.first, t))
        for hop in range(2, self.n + 1):
            q = t - hop + 1
            pl.when(within(q, self.chunks))(
                functools.partial(self.step, q, hop) if hop < self.n else functools.partial(self.final, q))

    def finish(self):
        def body(q, carry):
            for way in range(2):
                for hop in range(1, self.n):
                    @pl.when(self.valid(way, hop))
                    def _():
                        self.sent(way, q, hop).wait_send()
            return carry

        lax.fori_loop(0, self.chunks, body, 0)


def fetch(src, dst, sem, parts=1):
    step = dst.shape[0] // parts
    for i in range(parts):
        pltpu.make_async_copy(src.at[pl.ds(i * step, step)], dst.at[pl.ds(i * step, step)], sem).start()


def arrived(dst, sem):
    pltpu.make_async_copy(dst, dst, sem).wait()


def portions(total, count):
    return [(i * total // count, (i + 1) * total // count) for i in range(count)]


def conv_rows(weight, bias, a, out, first, last):
    channels, width = a.shape[1:]
    block = weight.shape[0] // channels

    def body(i, carry):
        at = pl.ds(i * block, block)
        high, low = split(a[at].reshape(block * channels, width))
        result = dot(weight[...], jnp.concatenate([high, high, low], 0)).reshape(block, channels, width)
        out[at] = result + bias[...][None] if bias is not None else out[at] + result
        return carry

    lax.fori_loop(first, last, body, 0)


def grad_rows(a, gz, cg_ref, bg_ref, first, last):
    channels, width = a.shape[1:]

    def body(r, carry):
        grad, bias = carry
        g = gz[r]
        left = jnp.concatenate(split(a[r]), 0)
        right = jnp.concatenate(split(g), 0)
        return grad + dot(left, right, (((1,), (1,)), ((), ()))), bias + g

    grad, bias = lax.fori_loop(first, last, body, (cg_ref[...], bg_ref[...]))
    cg_ref[...] = grad
    bg_ref[...] = bias


def chunk_of(ref, q, count):
    rows, _, width = ref.shape
    return ref[:, pl.ds(pl.multiple_of(q * count, count), count), :].reshape(rows * count, width)


def chunk_at(ref, q, count):
    return ref.at[:, pl.ds(pl.multiple_of(q * count, count), count), :]


class Modes:
    def __init__(self, section, buffer, p_out, cross):
        self.section, self.buffer, self.p_out, self.cross = section, buffer, p_out, cross

    def view(self, q):
        n, halves, kx, count, lanes = self.buffer.shape[1:]
        return self.buffer.at[q].reshape(n * halves * kx, count, lanes)

    def cross_copy(self, q):
        return to_core(self.buffer.at[q, :, 1 - self.section], self.p_out.at[:, q, 1],
                       (self.cross.at[0, q], self.cross.at[1, q]), self.section)

    def start(self, q):
        self.cross_copy(q).start()
        self.p_out[:, q, 0] = self.buffer[q, :, self.section]

    def wait(self, q):
        self.cross_copy(q).wait()


class Bound:
    def __init__(self, section, owner, micro, other, source, bound, local, cross):
        self.section, self.owner, self.micro, self.other = section, owner, micro, other
        self.source, self.bound, self.local, self.cross = source, bound, local, cross

    def copies(self, q, count, micro):
        src, dst = chunk_at(self.source, q, count), chunk_at(self.bound.at[micro], q, count)
        return (pltpu.make_async_copy(src, dst, self.local.at[q]),
                to_core(src, dst, (self.cross.at[0, q], self.cross.at[1, q]), self.section))

    def start(self, q, count):
        here, there = self.copies(q, count, self.micro)

        @pl.when(self.section == self.owner)
        def _():
            here.start()

        @pl.when(self.section != self.owner)
        def _():
            there.start()

    def wait(self, q, count):
        here, there = self.copies(q, count, self.micro)
        come = self.copies(q, count, self.other)[1]

        @pl.when(self.section == self.owner)
        def _():
            here.wait()
            come.wait_recv()

        @pl.when(self.section != self.owner)
        def _():
            there.wait_send()


def add_squares(value, total):
    rows, _, width = total.shape
    square = (value * value).reshape(rows, -1, width)
    for at in range(0, square.shape[1], G):
        total[...] += square[:, at:at + G]


def region_sums(rid_ref, eo, eb, stat_ref):
    rows, _, width = eo.shape
    rid = rid_ref[...]
    energies = (jnp.sum(eo[...], axis=1), jnp.sum(eb[...], axis=1), jnp.ones((rows, width), F32))
    for kind in range(3):
        for region in range(R):
            line = jnp.sum(jnp.where(rid == region + 1, energies[kind], 0.0), axis=0, keepdims=True)
            total = line[:, :128]
            for piece in range(1, width // 128):
                total = total + line[:, piece * 128:(piece + 1) * 128]
            stat_ref[kind, region:region + 1, :] = total


class Share:
    def __init__(self, r, index, parity):
        self.r, self.index, self.parity = r, index, parity
        self.me, self.members = lax.axis_index("batch"), lax.axis_size("batch")

    def copies(self):
        source, target = self.r.keep.at[self.parity], getattr(self.r, f"shared{self.index}").at[self.me]
        yield pltpu.make_async_copy(source, target, self.r.s_local.at[self.parity])
        for away in range(1, self.members):
            yield pltpu.make_async_remote_copy(
                src_ref=source, dst_ref=target, send_sem=self.r.s_send.at[self.parity, away],
                recv_sem=self.r.s_recv.at[self.index, away],
                device_id={"batch": lax.rem(self.me + away, self.members)}, device_id_type=MESH)

    def start(self):
        for copy in self.copies():
            copy.start()

    def wait_send(self):
        for i, copy in enumerate(self.copies()):
            if i == 0:
                copy.wait()
            else:
                copy.wait_send()

    def wait_recv(self):
        for i, copy in enumerate(self.copies()):
            if i > 0:
                copy.wait_recv()


class Head:
    def __init__(self, micro, place, parity, section, r):
        self.r, self.field, self.sem = r, r.fields.at[place], r.field_sem.at[place]
        self.source, self.count = r.inputs.at[micro, 0], r.full.shape[5]
        self.modes = Modes(section, r.p_buf, r.part.at[parity], r.p_cross.at[parity])

    def fetch(self):
        fetch(self.source, self.field, self.sem, 4)

    def got(self):
        arrived(self.field, self.sem)

    def chunk(self, q):
        r = self.r
        to_modes(chunk_of(self.field, q, self.count), r.t_plain[...], r.kron[...], r.spread, self.modes.view(q))
        self.modes.start(q)


class Stage:
    def __init__(self, k, kind, j, per_core, places, section, z, n, r):
        self.k, self.kind, self.j, self.r, self.section, self.n = k, kind, j, r, section, n
        self.parity = k % 2
        self.micro, self.other = section * per_core + j, (1 - section) * per_core + j
        self.forward, self.last = kind in ("middle", "turn"), kind == "tail"
        self.buffers = {name: r.fields.at[i] for name, i in places.items()}
        self.sems = {name: r.field_sem.at[i] for name, i in places.items()}
        self.gather = Gather(section, z, n, r, self.parity)
        self.count, self.lanes = r.full.shape[5], r.full.shape[6]
        self.chunks = r.full.shape[1]
        plain = lambda name: getattr(r, f"{name}{j}")
        if kind == "middle":
            self.loads = dict(a=r.inputs.at[self.micro, 0])
            self.saves = dict(a=plain("a1_"), z=plain("dg0_"))
        elif kind == "turn":
            self.loads = dict(a=plain("a1_"), cot=r.cotangent.at[self.micro, 0])
            self.saves = dict(cot=plain("gz1_"))
        elif kind == "back":
            self.loads = dict(gz=plain("gz1_"), h=r.cotangent.at[self.micro, 0], a=plain("a1_"), dg=plain("dg0_"))
            self.saves = dict(h=plain("ga1_"), dg=plain("gz0_"))
        else:
            self.loads = dict(gz=plain("gz0_"), h=plain("ga1_"), a=r.inputs.at[self.micro, 0])
            self.saves = {}
        layer = 0 if kind in ("middle", "tail") else 1
        self.weight, self.bias = r.conv.at[layer if self.forward else 2 + layer], r.bias.at[layer]
        self.table = r.t_plain if kind == "middle" else r.t_doubled
        self.itable = r.it_doubled if self.forward else r.it_plain
        if not self.last:
            self.modes = Modes(section, r.p_buf, r.part.at[self.parity], r.p_cross.at[self.parity])
        if kind in ("turn", "tail"):
            self.bound = Bound(section, 1 if kind == "turn" else 0, self.micro, self.other,
                               self.buffers["a" if kind == "turn" else "h"], r.bound,
                               r.b_local.at[self.parity], r.b_cross.at[self.parity])

    def prefetch(self):
        for name, src in self.loads.items():
            if self.kind != "middle":
                fetch(src, self.buffers[name], self.sems[name])
        if self.forward:
            self.rid_copy().start()

    def rid_copy(self):
        return pltpu.make_async_copy(self.r.region.at[self.micro, 0], self.r.rid.at[self.parity],
                                     self.r.rid_sem.at[self.parity])

    def got(self, name):
        arrived(self.buffers[name], self.sems[name])

    def open(self):
        r, b = self.r, self.buffers
        if self.forward:
            r.eo[...] = jnp.zeros_like(r.eo)
            r.eb[...] = jnp.zeros_like(r.eb)
            if self.kind != "middle":
                self.got("a")
        else:
            for name in ("gz", "h", "a"):
                self.got(name)
            at = self.k - self.r.first_back
            r.cg[at] = jnp.zeros_like(r.cg[at])
            r.bg[at] = jnp.zeros_like(r.bg[at])

    def before(self, i):
        r, b = self.r, self.buffers
        a = b["a"]
        rows, channels = a.shape[:2]
        blocks, parts = rows // (self.weight.shape[0] // channels), self.n - 1
        span = (i * blocks // parts, (i + 1) * blocks // parts)
        if self.forward:
            conv_rows(self.weight, self.bias, a, b["z"], *span)
        else:
            conv_rows(self.weight, None, b["gz"], b["h"], *span)
            at = self.k - r.first_back
            grad_rows(a, b["gz"], r.cg.at[at], r.bg.at[at], i * rows // parts, (i + 1) * rows // parts)

    def outs(self, q):
        return [pltpu.make_async_copy(chunk_at(self.buffers[name], q, self.count), chunk_at(dst, q, self.count),
                                      self.r.out_sem.at[self.parity, i, q])
                for i, (name, dst) in enumerate(self.saves.items())]

    def late(self):
        for name in ("cot", "dg"):
            if name in self.loads:
                self.got(name)

    def chunk(self, q):
        r, b, count = self.r, self.buffers, self.count
        spectral = from_modes(self.gather.full.at[q].reshape(-1, count, self.lanes), self.itable[...], r.ikron[...],
                              r.spread)
        if self.forward:
            branch, slope = gelu_parts(spectral + chunk_of(b["z"], q, count))
            if self.kind == "turn":
                put(chunk_at(b["cot"], q, count), chunk_of(b["cot"], q, count) * slope)
            else:
                put(chunk_at(b["z"], q, count), slope)
            add_squares(branch, r.eb)
            out = chunk_of(b["a"], q, count) + branch
            put(chunk_at(b["a"], q, count), out)
            add_squares(out, r.eo)
            source = b["cot" if self.kind == "turn" else "a"]
        else:
            ga = spectral + chunk_of(b["h"], q, count)
            put(chunk_at(b["h"], q, count), ga)
            if not self.last:
                put(chunk_at(b["dg"], q, count), ga * chunk_of(b["dg"], q, count))
                source = b["dg"]
        for copy in self.outs(q):
            copy.start()
        if self.kind in ("turn", "tail"):
            self.bound.start(q, count)
        if not self.last:
            to_modes(chunk_of(source, q, count), self.table[...], r.kron[...], r.spread, self.modes.view(q))

            pl.when(q == self.chunks - 1)(self.gather.finish)
            self.modes.start(q)

    def end(self):
        if self.forward:
            self.rid_copy().wait()
            region_sums(self.r.rid.at[self.parity], self.r.eo, self.r.eb, self.r.stat.at[self.k])
        if self.last:
            self.gather.finish()

    def close(self):
        def body(q, carry):
            for copy in self.outs(q):
                copy.wait()
            if self.kind in ("turn", "tail"):
                self.bound.wait(q, self.count)
            return carry

        lax.fori_loop(0, self.chunks, body, 0)


def stages_kernel(per_core, kinds, places, mixes, r):
    section, z, n = place_and_peers()
    chunks, count = r.full.shape[1], r.full.shape[5]
    r.first_back = 2 * per_core
    stages = [Stage(k, kind, j, per_core, places[k], section, z, n, r)
              for k, (kind, j) in enumerate((kind, j) for kind in kinds for j in range(per_core))]
    heads = [Head(section * per_core + j, places[j]["a"], j, section, r) for j in range(per_core)]
    half = r.far.shape[0]

    def spare(q, x):
        groups = r.fields.shape[1] // count
        at = q * half + x
        place, at = 3 + at // (2 * groups), at % (2 * groups)
        side, group = at // groups, at % groups
        return r.fields.at[place, pl.ds(pl.multiple_of(group * count, count), count), :,
                           pl.ds(pl.multiple_of(side * 128, 128), 128)]

    def lend_in(q, x):
        rows = pl.ds(q * count, count)
        return pltpu.make_async_copy(r.weights.at[0, (1 - section) * half + x, rows], spare(q, x), r.w_load.at[q, x])

    def lent(q, x):
        return to_core(spare(q, x), r.far.at[x, pl.ds(q * count, count)],
                       (r.w_cross.at[0, q, x], r.w_cross.at[1, q, x]), section)

    blocks = [(q, x) for q in range(chunks) for x in range(half)]
    for head in heads:
        head.fetch()
    for block in blocks:
        lend_in(*block).start()
    greet(section, z, n, True, lax.axis_size("batch"))
    wide = r.full.at[1].reshape(-1, *r.wide_own.shape)
    small = [to_core(wide.at[section], wide.at[section], (r.m_cross.at[0, 0], r.m_cross.at[1, 0]), section),
             to_core(r.bias.at[section], r.bias.at[section], (r.m_cross.at[0, 1], r.m_cross.at[1, 1]), section)]
    wide[section] = r.wide_own[...]
    r.bias[section] = r.bias_own[...]
    for copy in small:
        copy.start()
    ahead, sums = [Sum(section, z, n, r, j, heads[j].modes.wait) for j in range(2)]
    mix = Mix(section, z, *mixes[0], ahead, stages[0].gather, r, lent)
    heads[0].got()

    def opening(q, carry):
        ahead.tick(q - 1)
        heads[0].chunk(q)

        @pl.when(q == 0)
        def _():
            for block in blocks:
                lend_in(*block).wait()
                lent(*block).start()

        return carry

    lax.fori_loop(0, chunks, opening, 0)
    for copy in small:
        copy.wait()
    for way in range(2):
        for layer in range(2):
            high, low = split(jnp.concatenate([wide[layer, way, side] for side in range(wide.shape[2])], 1))
            r.conv[2 * way + layer] = jnp.concatenate([high, low, high], 1)
    heads[1].got()
    mix.prime()

    def second(q, carry):
        ahead.tick(q + chunks - 1)

        @pl.when(q < chunks)
        def _():
            heads[1].chunk(q)

        sums.tick(q - 1)
        at = q + min(chunks - n, 0)
        pl.when(within(at, chunks))(lambda: mix.chunk(at))
        return carry

    lax.fori_loop(0, max(n, chunks), second, 0)
    ahead.finish()
    mix.finish()
    shares = [Share(r, 0, 0)]
    shares[0].start()
    for block in blocks:
        lent(*block).wait_send()
    stages[0].prefetch()
    for k, stage in enumerate(stages):
        gather = stage.gather
        now = None if stage.last else Sum(section, z, n, r, stage.parity, stage.modes.wait)
        mix = None
        if sums is not None:
            mix = Mix(section, z, *mixes[(k + 1) // per_core], sums, stages[k + 1].gather, r)
            share = Share(r, k + 1, 1 - stage.parity)
            shares.append(share)
            mix.prime()
        lead = (max(n, chunks) if k == 0 else chunks) - 1
        ready = max(0, n - 1 - lead)
        stage.open()

        def early(i, carry):
            if sums is not None:
                sums.tick(i + lead)
            gather.tick(i)
            stage.before(i)
            if mix is not None and not mix.flip:
                pl.when(within(i - ready, chunks))(lambda: mix.chunk(i - ready))
            return carry

        lax.fori_loop(0, n - 1, early, 0)
        if k > 0:
            stages[k - 1].close()
        if now is not None:
            shares[k].wait_send()
        if k + 1 < len(stages):
            stages[k + 1].prefetch()
        stage.late()

        def later(q, carry):
            i = q + n - 1
            if sums is not None:
                sums.tick(i + lead)
            if now is not None:
                now.tick(i - n)
            gather.tick(i)
            stage.chunk(q)
            if mix is not None:
                if mix.flip:
                    pl.when(q == 0)(sums.finish)
                    mix.chunk(q)
                else:
                    pl.when(within(i - ready, chunks))(lambda: mix.chunk(i - ready))
            return carry

        lax.fori_loop(0, chunks, later, 0)
        if mix is not None:
            if not mix.flip:
                sums.finish()
            mix.finish()
            share.start()
        stage.end()
        sums = now
    stages[-1].close()
    for share in shares[-2:]:
        share.wait_send()
    for share in shares:
        share.wait_recv()


def swap_halves(value):
    return pltpu.roll(value, value.shape[-1] // 2, value.ndim - 1)


def left_lanes(shape):
    return lax.broadcasted_iota(jnp.int32, shape, len(shape) - 1) < shape[-1] // 2


def pieces(array):
    return [array[at:at + G] for at in range(0, array.shape[0], G)]


def spread_row(ref, row):
    return ref[pl.ds(row, G, stride=0), :]


class Mix:
    def __init__(self, section, z, layer, flip, sums, gather, r, lent=None):
        self.lent = lent
        self.section, self.z, self.layer, self.flip, self.r = section, z, layer, flip, r
        self.sums, self.gather = sums, gather
        self.chunks, self.grids, self.half, self.count, self.lanes = sums.part.shape[1:]
        self.channels, self.slots = r.weights.shape[2], r.wbuf.shape[0]
        self.blocks = self.chunks * self.half // 2

    def begin(self, block):
        per = self.half // 2
        q, x = block // per, 2 * (block % per)
        slot = lax.rem(block, self.slots)
        rows = pl.ds(q * self.count, self.count)
        if self.lent is not None:
            for at in range(2):
                self.lent(q, x + at).wait_recv()

        @pl.when(self.section == self.layer)
        def _():
            pltpu.make_async_copy(self.r.weights.at[0, pl.ds(self.section * self.half + x, 2), rows],
                                  self.r.wbuf.at[slot], self.r.wsem.at[slot]).start()

        @pl.when(self.section != self.layer)
        def _():
            pltpu.make_async_copy(self.r.far.at[pl.ds(x, 2), rows], self.r.wbuf.at[slot], self.r.wsem.at[slot]).start()

    def prime(self):
        for block in range(min(self.slots, self.blocks)):
            self.begin(jnp.int32(block))
        if not self.flip:
            self.r.macc[...] = jnp.zeros_like(self.r.macc)

    def chunk(self, q):
        def body(x, carry):
            block = q * (self.half // 2) + x // 2
            slot = lax.rem(block, self.slots)

            @pl.when(lax.rem(x, 2) == 0)
            def _():
                arrived(self.r.wbuf.at[slot], self.r.wsem.at[slot])

            (self.transposed if self.flip else self.forward)(q, x, self.r.wbuf.at[slot, lax.rem(x, 2)])

            @pl.when(jnp.logical_and(lax.rem(x, 2) == 1, block + self.slots < self.blocks))
            def _():
                self.begin(block + self.slots)

            return carry

        if self.flip:
            pl.when(q == 0)(self.sources)
        lax.fori_loop(0, self.half, body, 0)
        if self.flip:
            self.gather.give(q)

    def sources(self):
        def body(x, carry):
            for g in range(self.grids):
                value = jnp.concatenate([self.sums.part[self.z, at, g, x] for at in range(self.chunks)], 0)
                self.r.macc[x, 2 * g] = value
                self.r.macc[x, 2 * g + 1] = swap_halves(value)
            return carry

        lax.fori_loop(0, self.half, body, 0)

    def forward(self, q, x, weight):
        sides, groups = 2 * self.grids, self.channels // G
        total, source = self.r.macc.at[x], self.r.msrc
        for g in range(self.grids):
            value = self.sums.part[self.z, q, g, x]
            source[2 * g, :self.count] = value
            source[2 * g + 1, :self.count] = swap_halves(value)
        keys = [(k, o) for k in range(sides) for o in range(groups)]

        def body(octet, acc):
            acc = dict(zip(keys, acc))
            for u in range(G):
                i = octet * G + u
                rows = [spread_row(source.at[k], i) for k in range(sides)]
                for o in range(groups):
                    w = weight[i, o * G:(o + 1) * G, :]
                    for k in range(sides):
                        acc[k, o] = acc[k, o] + rows[k] * w
            return tuple(acc[key] for key in keys)

        acc = lax.fori_loop(0, self.count // G, body, tuple(total[k, o * G:(o + 1) * G, :] for k, o in keys))
        for key, value in zip(keys, acc):
            total[key[0], key[1] * G:(key[1] + 1) * G, :] = value

    def transposed(self, q, x, weight):
        sides, groups = 2 * self.grids, self.channels // G
        rows = [pieces(self.r.macc[x, k]) for k in range(sides)]
        out = [[] for _ in range(sides)]
        for i in range(self.count):
            total = [None] * sides
            for o in range(groups):
                w = weight[i, o * G:(o + 1) * G, :]
                for k in range(sides):
                    term = w * rows[k][o]
                    total[k] = term if total[k] is None else total[k] + term
            for k in range(sides):
                out[k].append(jnp.sum(total[k], axis=0, keepdims=True))
        left = left_lanes((self.count, self.lanes))
        for g in range(self.grids):
            a, b = [jnp.concatenate(out[2 * g + side], 0) for side in range(2)]
            self.put(g, q, x, jnp.where(left, a + swap_halves(a), swap_halves(b) - b))

    def put(self, g, q, x, value):
        if g == 0:
            self.gather.full[q, self.z, self.section, x] = value
        else:
            self.gather.give_from[q, x] = value

    def finish(self):
        if self.flip:
            return
        left = left_lanes((self.channels, self.lanes))

        def body(x, carry):
            for g in range(self.grids):
                a, b = [self.r.macc[x, 2 * g + side] for side in range(2)]
                result = jnp.where(left, a - swap_halves(a), b + swap_halves(b))
                for q in range(self.chunks):
                    self.put(g, q, x, result[q * self.count:(q + 1) * self.count])
            return carry

        lax.fori_loop(0, self.half, body, 0)
        for q in range(self.chunks):
            self.gather.give(q)


def gather_columns(f_ref, d_ref, left_of, right_of):
    channels = f_ref.shape[2] * f_ref.shape[5]
    lanes = f_ref.shape[6]
    left = left_lanes((channels, lanes))
    for stream in range(f_ref.shape[0]):
        for member in range(f_ref.shape[1]):
            for g in range(f_ref.shape[3]):
                at = (stream * f_ref.shape[1] + member) * f_ref.shape[3] + g
                both = []
                for x in range(2):
                    f = f_ref[stream, member, :, g, x].reshape(channels, lanes)
                    turned = swap_halves(f)
                    left_of[x, at] = jnp.concatenate([f, jnp.where(left, -turned, turned)], 0).T
                    both.append(d_ref[stream, member, :, g, x].reshape(channels, lanes))
                right_of[at] = jnp.concatenate(both, 0).T


def column_products(left_of, right_of, product):
    grids, double, lanes = right_of.shape
    half = double // 2
    left = left_lanes((2 * grids, lanes))
    rows = right_of.reshape(grids * double, lanes)
    sides = [left_of.at[x].reshape(grids * double, lanes) for x in range(2)]

    def body(k, carry):
        pick = pl.ds(k, 2 * grids, stride=half)
        d = rows[pick, :]
        f_high, f_low = split(jnp.concatenate([side[pick, :] for side in sides], 0))
        d_high, d_low = split(jnp.concatenate([jnp.where(left, d, 0.0), jnp.where(left, 0.0, d)], 0))
        product[k] = dot(jnp.concatenate([f_high, f_low, f_high], 0), jnp.concatenate([d_high, d_high, d_low], 0),
                         (((0,), (0,)), ((), ())))
        return carry

    lax.fori_loop(0, half, body, 0, unroll=4)


def product_rows(product, first, out):
    half, double, lanes = product.shape
    channels = double // 2
    rows = product.reshape(half * double, lanes)

    def body(i, carry):
        parts = [rows[pl.ds(part * channels + first + i, half, stride=double), :] for part in range(2)]
        tile = jnp.concatenate(parts, 0).T
        for x in range(2):
            out[x, i] = tile[x * channels:(x + 1) * channels]
        return carry

    lax.fori_loop(0, out.shape[1], body, 0, unroll=4)


class GradInput:
    def __init__(self, first, f, g, fbuf, gbuf, sem):
        self.first, self.f, self.g, self.fbuf, self.gbuf, self.sem = first, f, g, fbuf, gbuf, sem

    def load(self, x, slot):
        for layer, condition in enumerate((self.first, jnp.logical_not(self.first))):
            @pl.when(condition)
            def _():
                for j in range(len(self.f[layer])):
                    pltpu.make_async_copy(self.f[layer][j].at[:, :, :, pl.ds(2 * x, 2)], self.fbuf.at[slot, j],
                                          self.sem.at[0, slot]).start()
                    pltpu.make_async_copy(self.g[layer][j].at[:, :, :, pl.ds(2 * x, 2)], self.gbuf.at[slot, j],
                                          self.sem.at[1, slot]).start()

    def next(self, x, count):
        slot = lax.rem(x, 2)

        @pl.when(x + 1 < count)
        def _():
            self.load(x + 1, 1 - slot)

        arrived(self.fbuf.at[slot], self.sem.at[0, slot])
        arrived(self.gbuf.at[slot], self.sem.at[1, slot])
        return self.fbuf.at[slot], self.gbuf.at[slot]


def grad_input(r, first, per_core):
    f = [[getattr(r, f"f{layer}{j}") for j in range(per_core)] for layer in range(2)]
    g = [[getattr(r, f"g{layer}{j}") for j in range(per_core)] for layer in range(2)]
    return GradInput(first, f, g, r.fbuf, r.gbuf, r.in_sem)


def far_grad_kernel(per_core, r):
    section, z, n = place_and_peers()
    pairs, block = r.far.shape[0] // 2, r.out.shape[2]
    blocks = r.far.shape[1] // block
    source = grad_input(r, section != 0, per_core)

    def move(k, slot):
        p, i = k // blocks, k % blocks
        return to_core(r.out.at[slot], r.far.at[pl.ds(2 * p, 2), pl.ds(i * block, block)], (r.send.at[k], r.recv.at[k]),
                       section)

    source.load(0, 0)
    greet(section, z, n, False)

    def body(p, carry):
        gather_columns(*source.next(p, pairs), r.left_of, r.right_of)
        column_products(r.left_of, r.right_of, r.product)

        def inner(i, carry):
            k = p * blocks + i

            @pl.when(k >= 2)
            def _():
                move(k - 2, lax.rem(k, 2)).wait_send()

            product_rows(r.product, i * block, r.out.at[lax.rem(k, 2)])
            move(k, lax.rem(k, 2)).start()
            return carry

        return lax.fori_loop(0, blocks, inner, carry)

    lax.fori_loop(0, pairs, body, 0)
    total = pairs * blocks
    for k in (total - 2, total - 1):
        move(k, k % 2).wait_send()

    def close(k, carry):
        move(k, 0).wait_recv()
        return carry

    lax.fori_loop(0, total, close, 0)


def own_grad_kernel(names, per_core, m_ref, *refs):
    r = types.SimpleNamespace(**dict(zip(names, refs)))
    p, i = pl.program_id(0), pl.program_id(1)
    source = grad_input(r, m_ref[0] == 0, per_core)

    @pl.when(i == 0)
    def _():
        @pl.when(p == 0)
        def _():
            source.load(0, 0)

        gather_columns(*source.next(p, pl.num_programs(0)), r.left_of, r.right_of)
        column_products(r.left_of, r.right_of, r.product)

    r.bound_out[...] = r.bound_in[...]
    r.out[1 - m_ref[0]] = r.far[...]
    product_rows(r.product, i * r.out.shape[2], r.out.at[m_ref[0]])


def whole(array):
    return pl.BlockSpec(array.shape, lambda *_: (0,) * array.ndim)


def params(**kw):
    return pltpu.CompilerParams(vmem_limit_bytes=VMEM_LIMIT, **kw)


def local(inputs, cotangent, region_id, spectral_w, conv_w, bias_vector):
    micro_count, _, rows_dev, channels, width = inputs.shape
    lanes = spectral_w.shape[-1]
    half = lanes // 2
    kx_dev = spectral_w.shape[1]
    row_devices, sections = lax.axis_size("rows"), lax.axis_size("section")
    mode_rows, height = kx_dev * row_devices, rows_dev * row_devices
    section = lax.axis_index("section")
    per_core = micro_count // sections
    kx_half = kx_dev // sections

    plain, doubled = col_tables(width, half)

    def stacked(array):
        high, low = np_split(array)
        return np.concatenate([high, high, low], 0)

    t_plain, t_doubled, it_plain, it_doubled = [stacked(t) for t in (plain, doubled, plain.T, doubled.T)]
    kron, ikron = row_tables(height, mode_rows, lax.axis_index("rows") * rows_dev, rows_dev)

    count = G
    chunks = channels // count
    hbm, vmem = pl.BlockSpec(memory_space=pl.ANY), pl.BlockSpec(memory_space=pltpu.VMEM)
    field_shape = jax.ShapeDtypeStruct((rows_dev, channels, width), F32)
    part_dims = (row_devices, chunks, sections, kx_half, count, lanes)
    p_shape, f_shape = jax.ShapeDtypeStruct(part_dims, F32), jax.ShapeDtypeStruct(part_dims[1:], F32)
    y_shape = jax.ShapeDtypeStruct((sections, chunks, kx_half, count, lanes), F32)
    stat_shape = jax.ShapeDtypeStruct((3, R, 128), F32)
    cg_shape = jax.ShapeDtypeStruct((2 * channels, 2 * channels), F32)
    bg_shape = jax.ShapeDtypeStruct((channels, width), F32)
    bound_shape = jax.ShapeDtypeStruct((micro_count, rows_dev, channels, width), F32)
    dma = pltpu.SemaphoreType.DMA
    field_buf = pltpu.VMEM((rows_dev, channels, width), F32)
    full_dims = (chunks, row_devices, sections, kx_half, count, lanes)
    spread = pltpu.VMEM((width // 128, rows_dev * count, 128), F32)
    energy = pltpu.VMEM((rows_dev, G, width), F32)
    line_sems = dma((2, chunks, row_devices))
    def run(body, ident, ins, outs, scratch, cost=50, aliases=None):
        names = [*ins, *outs, *scratch]
        spec = lambda entry: vmem if isinstance(entry, tuple) else hbm
        plain = lambda entry: entry[0] if isinstance(entry, tuple) else entry
        kernel = lambda *refs: body(types.SimpleNamespace(**dict(zip(names, refs))))
        positions = {list(ins).index(k): list(outs).index(v) for k, v in (aliases or {}).items()}
        result = pl.pallas_call(
            kernel, in_specs=[spec(e) for e in ins.values()], out_specs=[spec(e) for e in outs.values()],
            out_shape=[plain(e) for e in outs.values()], scratch_shapes=list(scratch.values()),
            input_output_aliases=positions,
            cost_estimate=pl.CostEstimate(flops=0, bytes_accessed=cost * 3_000_000, transcendentals=0),
            compiler_params=params(collective_id=ident, has_side_effects=True))(*[plain(e) for e in ins.values()])
        return types.SimpleNamespace(**dict(zip(outs, result)))

    conv_rows_at_once = 256 // channels
    maps = jnp.stack([conv_w[0].T, conv_w[0]])
    at = np.arange(conv_rows_at_once * channels) // channels
    wide_own = jnp.where(at[:, None] == at[None, :], jnp.tile(maps, (1, conv_rows_at_once, conv_rows_at_once)), 0.0)
    wide_own = jnp.stack(jnp.split(wide_own, wide_own.shape[2] // 128, 2), 1)
    bias_own = jnp.broadcast_to(bias_vector[0][:, None], (channels, width))

    streams = range(per_core)
    members = lax.axis_size("batch")
    kinds = ["middle", "turn", "back", "tail"]
    mixes = [(0, False), (1, False), (1, True), (0, True)]
    names = ["f00", "f01", "f10", "f11", "g10", "g11", "g00", "g01"]
    places = [dict(a=0, z=1), dict(a=2, z=3), dict(a=4, z=5, cot=6), dict(a=0, z=1, cot=2),
              dict(gz=3, a=4, h=5, dg=6), dict(gz=0, a=1, h=2, dg=3), dict(gz=4, a=5, h=6), dict(gz=0, a=1, h=2)]
    both = (2,)
    ins = dict(inputs=inputs, cotangent=cotangent, region=region_id, weights=spectral_w, t_plain=(t_plain,),
               t_doubled=(t_doubled,), it_plain=(it_plain,), it_doubled=(it_doubled,), kron=(kron,), ikron=(ikron,),
               wide_own=(wide_own,), bias_own=(bias_own,))
    outs = dict(far=jax.ShapeDtypeStruct((kx_half,) + spectral_w.shape[2:], F32), bound=bound_shape, stat=(jax.ShapeDtypeStruct((2 * per_core,) + stat_shape.shape, F32),),
                cg=(jax.ShapeDtypeStruct((2 * per_core,) + cg_shape.shape, F32),),
                bg=(jax.ShapeDtypeStruct((2 * per_core,) + bg_shape.shape, F32),),
                **{f"{name}{j}": field_shape for name in ("a1_", "dg0_", "gz1_", "ga1_", "gz0_") for j in streams},
                **{f"shared{i}": jax.ShapeDtypeStruct((members,) + f_shape.shape, F32) for i in range(len(names))})
    scratch = dict(
        fields=pltpu.VMEM((7,) + field_shape.shape, F32), full=pltpu.VMEM(both + full_dims, F32),
        part=pltpu.VMEM(both + part_dims, F32),
        come=pltpu.VMEM(both + (2, chunks, row_devices - 1) + part_dims[2:], F32),
        keep=pltpu.VMEM(both + f_shape.shape, F32), y_give=pltpu.VMEM(both + y_shape.shape[1:], F32),
        p_buf=pltpu.VMEM(full_dims, F32), spread=spread, eo=energy, eb=energy,
        rid=pltpu.VMEM((2, rows_dev, width), jnp.int32),
        wbuf=pltpu.VMEM((6, 2, count, channels, lanes), F32), macc=pltpu.VMEM((kx_half, 2 * sections, channels, lanes), F32),
        msrc=pltpu.VMEM((2 * sections, channels, lanes), F32),
        bias=pltpu.VMEM((2, channels, width), F32),
        conv=pltpu.VMEM((4, len(at), 3 * len(at)), BF16), m_cross=dma((2, 2)),
        field_sem=dma((7,)), rid_sem=dma(both), out_sem=dma((2, 2, chunks)), wsem=dma((6,)), w_load=dma((chunks, kx_half)), w_cross=dma((2, chunks, kx_half)),
        send=dma(both + (2, chunks, row_devices)), recv=dma(both + (2, chunks, row_devices)),
        red_send=dma(both + (2, chunks, row_devices)), red_recv=dma(both + (2, chunks, row_devices)),
        y_cross=dma((2, 2, chunks)), p_cross=dma((2, 2, chunks)),
        b_local=dma((2, chunks)), b_cross=dma((2, 2, chunks)),
        s_local=dma(both), s_send=dma((2, members)), s_recv=dma((len(names), members)))
    done = run(functools.partial(stages_kernel, per_core, kinds, places, mixes), 0, ins, outs, scratch, cost=400)
    gathered = {name: getattr(done, f"shared{i}") for i, name in enumerate(names)}
    bound, calls = done.bound, 0

    grids = per_core * members * sections
    block = 2 * G
    pairs, blocks = kx_half // 2, channels // block
    in_buf = pltpu.VMEM((2, per_core, members, chunks, sections, 2, count, lanes), F32)
    grad_scratch = dict(fbuf=in_buf, gbuf=in_buf, in_sem=dma((2, 2)), left_of=pltpu.VMEM((2, grids, lanes, lanes), F32),
                        right_of=pltpu.VMEM((grids, lanes, lanes), F32), product=pltpu.VMEM((half, lanes, lanes), F32))
    far_grad = run(functools.partial(far_grad_kernel, per_core), 1 + calls, gathered,
                   dict(far=jax.ShapeDtypeStruct((kx_half, channels, channels, lanes), F32)),
                   dict(out=pltpu.VMEM((2, 2, block, channels, lanes), F32), send=dma((pairs * blocks,)),
                        recv=dma((pairs * blocks,)), **grad_scratch)).far
    bound_rows = bound.reshape(micro_count * rows_dev, channels, width)
    bound_block = pl.BlockSpec((bound_rows.shape[0] // (pairs * blocks), channels, width),
                               lambda p, i, m: (p * blocks + i, 0, 0))
    grid_spec = pltpu.PrefetchScalarGridSpec(
        num_scalar_prefetch=1, grid=(pairs, blocks),
        in_specs=[hbm] * len(gathered)
        + [pl.BlockSpec((2, block, channels, lanes), lambda p, i, m: (p, i, 0, 0)), bound_block],
        out_specs=[pl.BlockSpec((2, 2, block, channels, lanes), lambda p, i, m: (0, p, i, 0, 0)), bound_block],
        scratch_shapes=list(grad_scratch.values()))
    spectral_grad, boundary = pl.pallas_call(
        functools.partial(own_grad_kernel, [*gathered, "far", "bound_in", "out", "bound_out", *grad_scratch], per_core),
        grid_spec=grid_spec, out_shape=[jax.ShapeDtypeStruct((2, kx_half, channels, channels, lanes), F32),
                                        jax.ShapeDtypeStruct(bound_rows.shape, F32)],
        cost_estimate=pl.CostEstimate(flops=0, bytes_accessed=150_000_000, transcendentals=0),
        compiler_params=params())(
            jnp.reshape(section, (1,)).astype(jnp.int32), *gathered.values(), far_grad, bound_rows)
    spectral_grad = spectral_grad.reshape(spectral_w.shape)
    boundary = boundary.reshape((1, micro_count, 1) + inputs.shape[2:])

    def lower(value):
        return (value[:channels, :channels] + value[channels:, channels:]
                + value[:channels, channels:] + value[channels:, :channels])

    pair = lambda value: jnp.sum(value.reshape((2, per_core) + value.shape[1:]), 1)
    conv_local = jnp.stack([lower(value) for value in pair(done.cg)[::-1]])
    bias_local = jnp.sum(pair(done.bg)[::-1], -1)
    stat_local = jnp.sum(pair(done.stat), -1)
    shapes = [v.shape for v in (conv_local, bias_local, stat_local)]
    flat_sums = jnp.concatenate([v.reshape(-1) for v in (conv_local, bias_local, stat_local)])
    length = flat_sums.shape[0]
    flat_sums = jnp.pad(flat_sums, (0, -length % 1024)).reshape(-1, 128)
    flat_sums = jnp.sum(lax.all_gather(flat_sums, ("section", "batch", "rows"), axis=0), 0).reshape(-1)
    ends = np.cumsum([0] + [math.prod(shape) for shape in shapes])
    conv_sum, bias_sum, stat_sum = [flat_sums[ends[i]:ends[i + 1]].reshape(shapes[i]) for i in range(3)]
    own_stat = lax.dynamic_index_in_dim(stat_sum, section, 0, False)
    layer_rms = jnp.sqrt(own_stat[:2] / (channels * own_stat[2])[None, :] + 1e-06)[None]
    own = lambda value: lax.dynamic_slice_in_dim(value, section, 1, 0)
    return boundary, spectral_grad, own(conv_sum), own(bias_sum), layer_rms


def solution(mesh):
    placed = (
        P(None, "batch", "rows", None, None),
        P(None, "batch", "rows", None, None),
        P(None, "batch", "rows", None),
        P("section", "rows", None, None, None),
        P("section", None, None),
        P("section", None),
    )
    return jax.shard_map(
        local,
        mesh=mesh,
        in_specs=placed,
        out_specs=(
            P("section", None, "batch", "rows", None, None),
            P("section", "rows", None, None, None),
            P("section", None, None),
            P("section", None),
            P("section", None, None),
        ),
        check_vma=False,
    )
```

```python
import functools
import math
import types

import jax
import jax.numpy as jnp
import numpy as np
from jax import lax
from jax.experimental import pallas as pl
from jax.experimental.pallas import tpu as pltpu
from jax.sharding import PartitionSpec as P

R = 8
G = 8
F32 = jnp.float32
BF16 = jnp.bfloat16
VMEM_LIMIT = 62 * 1024 * 1024
MESH = pl.DeviceIdType.MESH


def split(value):
    high = value.astype(BF16)
    return high, (value - high.astype(F32)).astype(BF16)


def dot(left, right, dims=(((1,), (0,)), ((), ()))):
    return lax.dot_general(left, right, dims, preferred_element_type=F32)


def dot3(left, right):
    return dot(left[0], right[0]) + (dot(left[1], right[0]) + dot(left[0], right[1]))


def np_split(value):
    high = value.astype(np.float32).astype(BF16)
    return high, (value - high.astype(np.float64)).astype(np.float32).astype(BF16)


def col_tables(width, half):
    phase = 2.0 * math.pi / width * (np.outer(np.arange(width), np.arange(half)) % width)
    cosine, sine = np.cos(phase) / math.sqrt(width), np.sin(phase) / math.sqrt(width)
    plain = np.concatenate([cosine, -sine, -sine, -cosine], 1)
    doubled = plain * np.tile(np.where(np.arange(half) == 0, 1.0, 2.0), 4)[None, :]
    return plain, doubled


def row_tables(height, mode_rows, first_row, rows_dev):
    position = jnp.arange(mode_rows, dtype=jnp.int32)
    frequency = jnp.where(position < mode_rows // 2, position, height - mode_rows + position)
    row = first_row + jnp.arange(rows_dev, dtype=jnp.int32)
    phase = 2.0 * math.pi / height * (frequency[:, None] * row[None, :] % height).astype(F32)
    small = jnp.concatenate([jnp.cos(phase), jnp.sin(phase)], 1) / math.sqrt(height)
    rounded = lax.reduce_precision(small, 8, 7)
    high, low = rounded.astype(BF16), (small - rounded).astype(BF16)
    forward = jnp.concatenate([jnp.concatenate([high, high], 1), jnp.concatenate([low, jnp.zeros_like(low)], 1)], 0)
    inverse = jnp.concatenate([high.T, high.T, low.T], 1)
    return forward, inverse


def to_modes(value, table, kron, spread, p_ref):
    mode_rows, count, lanes = p_ref.shape
    rows = value.shape[0] // count
    high, low = split(value)
    spectra = dot(jnp.concatenate([high, low, high], 1), table)
    for i in range(2):
        spread[i] = spectra[:, i * lanes:(i + 1) * lanes]
    out = p_ref.reshape(mode_rows * count, lanes)
    for first in range(0, count, 2):
        sides = []
        for c in (first, first + 1):
            pick = pl.ds(c, rows, stride=count)
            sides.append(jnp.concatenate([spread[i, pick, :] for i in range(2)], 0))
        high, low = split(jnp.concatenate(sides, 1))
        both = dot(kron, jnp.concatenate([high, low], 0))
        result = both[:mode_rows] + both[mode_rows:]
        for i in range(2):
            out[pl.ds(first + i, mode_rows, stride=count), :] = result[:, i * lanes:(i + 1) * lanes]


def from_modes(y_ref, table, kron, spread):
    mode_rows, count, lanes = y_ref.shape
    rows, pieces = spread.shape[1] // count, spread.shape[0]
    modes = y_ref.reshape(mode_rows * count, lanes)
    sides = []
    for first in range(0, count, 2):
        pair = [modes[pl.ds(c, mode_rows, stride=count), :] for c in (first, first + 1)]
        high, low = split(jnp.concatenate(pair, 1))
        both = dot(kron, jnp.concatenate([high, low, high], 0))
        for i in range(2):
            side = both[:, i * lanes:(i + 1) * lanes]
            sides.append(jnp.concatenate([side[:rows], side[rows:]], 1))
    high, low = split(jnp.concatenate(sides, 0))
    out = dot(jnp.concatenate([high, low, high], 1), table)
    for c in range(count):
        for i in range(pieces):
            spread[i, pl.ds(c, rows, stride=count), :] = out[c * rows:(c + 1) * rows, i * 128:(i + 1) * 128]
    return jnp.concatenate([spread[i] for i in range(pieces)], 1)


def gelu_parts(z):
    gauss = jnp.exp2((-0.5 / math.log(2.0)) * (z * z))
    base = 1.0 + (0.3275911 / math.sqrt(2.0)) * jnp.abs(z)
    t = pl.reciprocal(base, approx=True)
    t = t * (2.0 - base * t)
    poly = t * (0.127414796 + t * (-0.142248368 + t * (0.7107068705 + t * (-0.7265760135 + t * 0.5307027145))))
    tail = poly * gauss
    phi = jnp.where(z >= 0, 1.0 - tail, tail)
    return z * phi, phi + z * (gauss * (1.0 / math.sqrt(2.0 * math.pi)))


def flat(ref):
    rows, count, width = ref.shape
    return ref[...].reshape(rows * count, width)


def put(ref, value):
    ref[...] = value.reshape(ref.shape)


def place_and_peers():
    section, z = lax.axis_index("section"), lax.axis_index("rows")
    return section, z, lax.axis_size("rows")


def greet(section, z, n, lines, members=0):
    barrier = pltpu.get_barrier_semaphore()
    pl.semaphore_signal(barrier, inc=1, device_id={"section": 1 - section}, device_id_type=MESH)
    if not lines:
        pl.semaphore_wait(barrier, 1)
        return

    @pl.when(z > 0)
    def _():
        pl.semaphore_signal(barrier, inc=1, device_id={"rows": z - 1}, device_id_type=MESH)

    @pl.when(z < n - 1)
    def _():
        pl.semaphore_signal(barrier, inc=1, device_id={"rows": z + 1}, device_id_type=MESH)

    for away in range(1, members):
        pl.semaphore_signal(barrier, inc=1, device_id={"batch": lax.rem(lax.axis_index("batch") + away, members)},
                            device_id_type=MESH)

    others = 1 + max(members - 1, 0)
    pl.semaphore_wait(barrier, others + (z > 0).astype(jnp.int32) + (z < n - 1).astype(jnp.int32))


def to_core(src, dst, sems, section):
    return pltpu.make_async_remote_copy(src_ref=src, dst_ref=dst, send_sem=sems[0], recv_sem=sems[1],
                                        device_id={"section": 1 - section}, device_id_type=MESH)


def guard(condition, body):
    if isinstance(condition, (bool, np.bool_)):
        if condition:
            body()
    else:
        pl.when(condition)(body)


class Line:
    def __init__(self, section, z, n, chunks, send, recv):
        self.section, self.z, self.n, self.chunks = section, z, n, chunks
        self.send, self.recv = send, recv

    def move(self, way, q, hop, src, dst):
        return pltpu.make_async_remote_copy(
            src_ref=src, dst_ref=dst, send_sem=self.send.at[way, q, hop], recv_sem=self.recv.at[way, q, hop],
            device_id={"rows": self.z + 1 if way == 0 else self.z - 1}, device_id_type=MESH)

    def sends(self, way):
        return self.z < self.n - 1 if way == 0 else self.z > 0

    def hears(self, way):
        return self.z > 0 if way == 0 else self.z < self.n - 1


def within(value, count):
    return jnp.logical_and(value >= 0, value < count)


class Gather(Line):
    def __init__(self, section, z, n, r, parity):
        super().__init__(section, z, n, r.full.shape[1], r.send.at[parity], r.recv.at[parity])
        self.full, self.give_from = r.full.at[parity], r.y_give.at[parity]
        self.cross = r.y_cross.at[parity]

    def swap(self, q):
        return to_core(self.give_from.at[q], self.full.at[q, self.z, self.section],
                       (self.cross.at[0, q], self.cross.at[1, q]), self.section)

    def give(self, q):
        self.swap(q).start()

    def hop(self, way, q, hop):
        piece = self.full.at[q, self.source(way, hop)]
        return self.move(way, q, hop, piece, piece)

    def source(self, way, hop):
        return self.z - hop if way == 0 else self.z + hop

    def known(self, way, hop):
        at = self.source(way, hop)
        return at >= 0 if way == 0 else at < self.n

    def own(self, q):
        self.swap(q).wait_recv()
        for way in range(2):
            @pl.when(self.sends(way))
            def _():
                self.hop(way, q, 0).start()

    def step(self, q, hop):
        for way in range(2):
            @pl.when(self.known(way, hop + 1))
            def _():
                piece = self.full.at[q, self.source(way, hop + 1)]
                self.move(way, q, hop, piece, piece).wait_recv()

                @pl.when(self.sends(way))
                def _():
                    self.hop(way, q, hop + 1).start()

    def tick(self, t):
        pl.when(within(t, self.chunks))(functools.partial(self.own, t))
        for hop in range(self.n - 1):
            q = t - hop - 1
            pl.when(within(q, self.chunks))(functools.partial(self.step, q, hop))

    def finish(self):
        def body(q, carry):
            self.swap(q).wait_send()
            for way in range(2):
                for hop in range(self.n - 1):
                    @pl.when(jnp.logical_and(self.sends(way), self.known(way, hop)))
                    def _():
                        self.hop(way, q, hop).wait_send()
            return carry

        lax.fori_loop(0, self.chunks, body, 0)


class Sum(Line):
    def __init__(self, section, z, n, r, parity, admit):
        super().__init__(section, z, n, r.part.shape[2], r.red_send.at[parity], r.red_recv.at[parity])
        self.part, self.come, self.keep, self.admit = r.part.at[parity], r.come.at[parity], r.keep.at[parity], admit

    def owner(self, way, hop):
        return self.z + self.n - hop if way == 0 else self.z - self.n + hop

    def valid(self, way, hop):
        return self.z <= hop - 1 if way == 0 else self.z >= self.n - hop

    def sent(self, way, q, hop):
        return self.move(way, q, hop, self.part.at[self.owner(way, hop), q], self.come.at[way, q, hop - 1])

    def heard(self, way, q, hop):
        come = self.come.at[way, q, hop - 1]
        self.move(way, q, hop, come, come).wait_recv()

    def first(self, q):
        self.admit(q)
        self.step(q, 1)

    def step(self, q, hop):
        for way in range(2):
            @pl.when(self.valid(way, hop))
            def _():
                if hop > 1:
                    @pl.when(self.hears(way))
                    def _():
                        self.heard(way, q, hop - 1)
                        owner = self.owner(way, hop)
                        self.part[owner, q] = self.part[owner, q] + self.come[way, q, hop - 2]

                self.sent(way, q, hop).start()

    def final(self, q):
        for way in range(2):
            @pl.when(self.hears(way))
            def _():
                self.heard(way, q, self.n - 1)
                self.part[self.z, q] = self.part[self.z, q] + self.come[way, q, self.n - 2]

        self.keep[q] = self.part[self.z, q]

    def tick(self, t):
        pl.when(within(t, self.chunks))(functools.partial(self.first, t))
        for hop in range(2, self.n + 1):
            q = t - hop + 1
            pl.when(within(q, self.chunks))(
                functools.partial(self.step, q, hop) if hop < self.n else functools.partial(self.final, q))

    def finish(self):
        def body(q, carry):
            for way in range(2):
                for hop in range(1, self.n):
                    @pl.when(self.valid(way, hop))
                    def _():
                        self.sent(way, q, hop).wait_send()
            return carry

        lax.fori_loop(0, self.chunks, body, 0)


def fetch(src, dst, sem, parts=1):
    step = dst.shape[0] // parts
    for i in range(parts):
        pltpu.make_async_copy(src.at[pl.ds(i * step, step)], dst.at[pl.ds(i * step, step)], sem).start()


def arrived(dst, sem):
    pltpu.make_async_copy(dst, dst, sem).wait()


def portions(total, count):
    return [(i * total // count, (i + 1) * total // count) for i in range(count)]


def conv_rows(weight, bias, a, out, first, last):
    channels, width = a.shape[1:]
    block = weight.shape[0] // channels

    def body(i, carry):
        at = pl.ds(i * block, block)
        high, low = split(a[at].reshape(block * channels, width))
        result = dot(weight[...], jnp.concatenate([high, high, low], 0)).reshape(block, channels, width)
        out[at] = result + bias[...][None] if bias is not None else out[at] + result
        return carry

    lax.fori_loop(first, last, body, 0)


def grad_rows(a, gz, cg_ref, bg_ref, first, last):
    channels, width = a.shape[1:]

    def body(r, carry):
        grad, bias = carry
        g = gz[r]
        left = jnp.concatenate(split(a[r]), 0)
        right = jnp.concatenate(split(g), 0)
        return grad + dot(left, right, (((1,), (1,)), ((), ()))), bias + g

    grad, bias = lax.fori_loop(first, last, body, (cg_ref[...], bg_ref[...]))
    cg_ref[...] = grad
    bg_ref[...] = bias


def chunk_of(ref, q, count):
    rows, _, width = ref.shape
    return ref[:, pl.ds(pl.multiple_of(q * count, count), count), :].reshape(rows * count, width)


def chunk_at(ref, q, count):
    return ref.at[:, pl.ds(pl.multiple_of(q * count, count), count), :]


class Modes:
    def __init__(self, section, buffer, p_out, cross):
        self.section, self.buffer, self.p_out, self.cross = section, buffer, p_out, cross

    def view(self, q):
        n, halves, kx, count, lanes = self.buffer.shape[1:]
        return self.buffer.at[q].reshape(n * halves * kx, count, lanes)

    def cross_copy(self, q):
        return to_core(self.buffer.at[q, :, 1 - self.section], self.p_out.at[:, q, 1],
                       (self.cross.at[0, q], self.cross.at[1, q]), self.section)

    def start(self, q):
        self.cross_copy(q).start()
        self.p_out[:, q, 0] = self.buffer[q, :, self.section]

    def wait(self, q):
        self.cross_copy(q).wait()


class Bound:
    def __init__(self, section, owner, micro, other, source, bound, local, cross):
        self.section, self.owner, self.micro, self.other = section, owner, micro, other
        self.source, self.bound, self.local, self.cross = source, bound, local, cross

    def copies(self, q, count, micro):
        src, dst = chunk_at(self.source, q, count), chunk_at(self.bound.at[micro], q, count)
        return (pltpu.make_async_copy(src, dst, self.local.at[q]),
                to_core(src, dst, (self.cross.at[0, q], self.cross.at[1, q]), self.section))

    def start(self, q, count):
        here, there = self.copies(q, count, self.micro)

        @pl.when(self.section == self.owner)
        def _():
            here.start()

        @pl.when(self.section != self.owner)
        def _():
            there.start()

    def wait(self, q, count):
        here, there = self.copies(q, count, self.micro)
        come = self.copies(q, count, self.other)[1]

        @pl.when(self.section == self.owner)
        def _():
            here.wait()
            come.wait_recv()

        @pl.when(self.section != self.owner)
        def _():
            there.wait_send()


def add_squares(value, total):
    rows, _, width = total.shape
    square = (value * value).reshape(rows, -1, width)
    for at in range(0, square.shape[1], G):
        total[...] += square[:, at:at + G]


def region_sums(rid_ref, eo, eb, stat_ref):
    rows, _, width = eo.shape
    rid = rid_ref[...]
    energies = (jnp.sum(eo[...], axis=1), jnp.sum(eb[...], axis=1), jnp.ones((rows, width), F32))
    for kind in range(3):
        for region in range(R):
            line = jnp.sum(jnp.where(rid == region + 1, energies[kind], 0.0), axis=0, keepdims=True)
            total = line[:, :128]
            for piece in range(1, width // 128):
                total = total + line[:, piece * 128:(piece + 1) * 128]
            stat_ref[kind, region:region + 1, :] = total


class Share:
    def __init__(self, r, index, parity):
        self.r, self.index, self.parity = r, index, parity
        self.me, self.members = lax.axis_index("batch"), lax.axis_size("batch")

    def copies(self):
        source, target = self.r.keep.at[self.parity], getattr(self.r, f"shared{self.index}").at[self.me]
        yield pltpu.make_async_copy(source, target, self.r.s_local.at[self.parity])
        for away in range(1, self.members):
            yield pltpu.make_async_remote_copy(
                src_ref=source, dst_ref=target, send_sem=self.r.s_send.at[self.parity, away],
                recv_sem=self.r.s_recv.at[self.index, away],
                device_id={"batch": lax.rem(self.me + away, self.members)}, device_id_type=MESH)

    def start(self):
        for copy in self.copies():
            copy.start()

    def wait_send(self):
        for i, copy in enumerate(self.copies()):
            if i == 0:
                copy.wait()
            else:
                copy.wait_send()

    def wait_recv(self):
        for i, copy in enumerate(self.copies()):
            if i > 0:
                copy.wait_recv()


class Head:
    def __init__(self, micro, place, parity, section, r):
        self.r, self.field, self.sem = r, r.fields.at[place], r.field_sem.at[place]
        self.source, self.count = r.inputs.at[micro, 0], r.full.shape[5]
        self.modes = Modes(section, r.p_buf, r.part.at[parity], r.p_cross.at[parity])

    def fetch(self):
        fetch(self.source, self.field, self.sem, 4)

    def got(self):
        arrived(self.field, self.sem)

    def chunk(self, q):
        r = self.r
        to_modes(chunk_of(self.field, q, self.count), r.t_plain[...], r.kron[...], r.spread, self.modes.view(q))
        self.modes.start(q)


class Stage:
    def __init__(self, k, kind, j, per_core, places, section, z, n, r):
        self.k, self.kind, self.j, self.r, self.section, self.n = k, kind, j, r, section, n
        self.parity = k % 2
        self.micro, self.other = section * per_core + j, (1 - section) * per_core + j
        self.forward, self.last = kind in ("middle", "turn"), kind == "tail"
        self.buffers = {name: r.fields.at[i] for name, i in places.items()}
        self.sems = {name: r.field_sem.at[i] for name, i in places.items()}
        self.gather = Gather(section, z, n, r, self.parity)
        self.count, self.lanes = r.full.shape[5], r.full.shape[6]
        self.chunks = r.full.shape[1]
        plain = lambda name: getattr(r, f"{name}{j}")
        if kind == "middle":
            self.loads = dict(a=r.inputs.at[self.micro, 0])
            self.saves = dict(a=plain("a1_"), z=plain("dg0_"))
        elif kind == "turn":
            self.loads = dict(a=plain("a1_"), cot=r.cotangent.at[self.micro, 0])
            self.saves = dict(cot=plain("gz1_"))
        elif kind == "back":
            self.loads = dict(gz=plain("gz1_"), h=r.cotangent.at[self.micro, 0], a=plain("a1_"), dg=plain("dg0_"))
            self.saves = dict(h=plain("ga1_"), dg=plain("gz0_"))
        else:
            self.loads = dict(gz=plain("gz0_"), h=plain("ga1_"), a=r.inputs.at[self.micro, 0])
            self.saves = {}
        layer = 0 if kind in ("middle", "tail") else 1
        self.weight, self.bias = r.conv.at[layer if self.forward else 2 + layer], r.bias.at[layer]
        self.table = r.t_plain if kind == "middle" else r.t_doubled
        self.itable = r.it_doubled if self.forward else r.it_plain
        if not self.last:
            self.modes = Modes(section, r.p_buf, r.part.at[self.parity], r.p_cross.at[self.parity])
        if kind in ("turn", "tail"):
            self.bound = Bound(section, 1 if kind == "turn" else 0, self.micro, self.other,
                               self.buffers["a" if kind == "turn" else "h"], r.bound,
                               r.b_local.at[self.parity], r.b_cross.at[self.parity])

    def prefetch(self):
        for name, src in self.loads.items():
            if self.kind != "middle":
                fetch(src, self.buffers[name], self.sems[name])
        if self.forward:
            self.rid_copy().start()

    def rid_copy(self):
        return pltpu.make_async_copy(self.r.region.at[self.micro, 0], self.r.rid.at[self.parity],
                                     self.r.rid_sem.at[self.parity])

    def got(self, name):
        arrived(self.buffers[name], self.sems[name])

    def open(self):
        r, b = self.r, self.buffers
        if self.forward:
            r.eo[...] = jnp.zeros_like(r.eo)
            r.eb[...] = jnp.zeros_like(r.eb)
            if self.kind != "middle":
                self.got("a")
        else:
            for name in ("gz", "h"):
                self.got(name)
            at = self.k - self.r.first_back
            r.cg[at] = jnp.zeros_like(r.cg[at])
            r.bg[at] = jnp.zeros_like(r.bg[at])

    def before(self, i, parts):
        a = self.buffers["a"]
        blocks = a.shape[0] // (self.weight.shape[0] // a.shape[1])
        span = (i * blocks // parts, (i + 1) * blocks // parts)
        if self.forward:
            conv_rows(self.weight, self.bias, a, self.buffers["z"], *span)
        else:
            conv_rows(self.weight, None, self.buffers["gz"], self.buffers["h"], *span)

    def grads(self, part):
        if not self.forward:
            at, rows = self.k - self.r.first_back, self.buffers["a"].shape[0]
            grad_rows(self.buffers["a"], self.buffers["gz"], self.r.cg.at[at], self.r.bg.at[at],
                      part * rows // 2, (part + 1) * rows // 2)

    def outs(self, q):
        return [pltpu.make_async_copy(chunk_at(self.buffers[name], q, self.count), chunk_at(dst, q, self.count),
                                      self.r.out_sem.at[self.parity, i, q])
                for i, (name, dst) in enumerate(self.saves.items())]

    def late(self):
        for name in ("cot", "dg"):
            if name in self.loads:
                self.got(name)
        if not self.forward:
            self.got("a")

    def chunk(self, q):
        r, b, count = self.r, self.buffers, self.count
        spectral = from_modes(self.gather.full.at[q].reshape(-1, count, self.lanes), self.itable[...], r.ikron[...],
                              r.spread)
        if self.forward:
            branch, slope = gelu_parts(spectral + chunk_of(b["z"], q, count))
            if self.kind == "turn":
                put(chunk_at(b["cot"], q, count), chunk_of(b["cot"], q, count) * slope)
            else:
                put(chunk_at(b["z"], q, count), slope)
            add_squares(branch, r.eb)
            out = chunk_of(b["a"], q, count) + branch
            put(chunk_at(b["a"], q, count), out)
            add_squares(out, r.eo)
        else:
            ga = spectral + chunk_of(b["h"], q, count)
            put(chunk_at(b["h"], q, count), ga)
            if not self.last:
                put(chunk_at(b["dg"], q, count), ga * chunk_of(b["dg"], q, count))
        for copy in self.outs(q):
            copy.start()
        if self.kind in ("turn", "tail"):
            self.bound.start(q, count)

    def modes_of(self, q):
        if self.last:
            return
        r, source = self.r, self.buffers[dict(middle="a", turn="cot", back="dg")[self.kind]]
        to_modes(chunk_of(source, q, self.count), self.table[...], r.kron[...], r.spread, self.modes.view(q))

        pl.when(q == self.chunks - 1)(self.gather.finish)
        self.modes.start(q)

    def end(self):
        if self.forward:
            self.rid_copy().wait()
            region_sums(self.r.rid.at[self.parity], self.r.eo, self.r.eb, self.r.stat.at[self.k])
        if self.last:
            self.gather.finish()

    def close(self):
        def body(q, carry):
            for copy in self.outs(q):
                copy.wait()
            if self.kind in ("turn", "tail"):
                self.bound.wait(q, self.count)
            return carry

        lax.fori_loop(0, self.chunks, body, 0)


def stages_kernel(per_core, kinds, places, mixes, r):
    section, z, n = place_and_peers()
    chunks, count = r.full.shape[1], r.full.shape[5]
    r.first_back = 2 * per_core
    stages = [Stage(k, kind, j, per_core, places[k], section, z, n, r)
              for k, (kind, j) in enumerate((kind, j) for kind in kinds for j in range(per_core))]
    heads = [Head(section * per_core + j, places[j]["a"], j, section, r) for j in range(per_core)]
    half = r.far.shape[0]

    def spare(q, x):
        groups = r.fields.shape[1] // count
        at = q * half + x
        place, at = 3 + at // (2 * groups), at % (2 * groups)
        side, group = at // groups, at % groups
        return r.fields.at[place, pl.ds(pl.multiple_of(group * count, count), count), :,
                           pl.ds(pl.multiple_of(side * 128, 128), 128)]

    def lend_in(q, x):
        rows = pl.ds(q * count, count)
        return pltpu.make_async_copy(r.weights.at[0, (1 - section) * half + x, rows], spare(q, x), r.w_load.at[q, x])

    def lent(q, x):
        return to_core(spare(q, x), r.far.at[x, pl.ds(q * count, count)],
                       (r.w_cross.at[0, q, x], r.w_cross.at[1, q, x]), section)

    blocks = [(q, x) for q in range(chunks) for x in range(half)]
    for head in heads:
        head.fetch()
    for block in blocks:
        lend_in(*block).start()
    greet(section, z, n, True, lax.axis_size("batch"))
    wide = r.full.at[1].reshape(-1, *r.wide_own.shape)
    small = [to_core(wide.at[section], wide.at[section], (r.m_cross.at[0, 0], r.m_cross.at[1, 0]), section),
             to_core(r.bias.at[section], r.bias.at[section], (r.m_cross.at[0, 1], r.m_cross.at[1, 1]), section)]
    wide[section] = r.wide_own[...]
    r.bias[section] = r.bias_own[...]
    for copy in small:
        copy.start()
    ahead, sums = [Sum(section, z, n, r, j, heads[j].modes.wait) for j in range(2)]
    mix = Mix(section, z, *mixes[0], ahead, stages[0].gather, r, lent)
    heads[0].got()

    def opening(q, carry):
        ahead.tick(q - 1)
        heads[0].chunk(q)

        @pl.when(q == 0)
        def _():
            for block in blocks:
                lend_in(*block).wait()
                lent(*block).start()

        return carry

    lax.fori_loop(0, chunks, opening, 0)
    for copy in small:
        copy.wait()
    for way in range(2):
        for layer in range(2):
            high, low = split(jnp.concatenate([wide[layer, way, side] for side in range(wide.shape[2])], 1))
            r.conv[2 * way + layer] = jnp.concatenate([high, low, high], 1)
    heads[1].got()
    mix.prime()

    def second(q, carry):
        ahead.tick(q + chunks - 1)

        @pl.when(q < chunks)
        def _():
            heads[1].chunk(q)

        sums.tick(q - 1)
        pl.when(within(q + chunks - n, chunks))(lambda: mix.chunk(q + chunks - n))
        return carry

    lax.fori_loop(0, n, second, 0)
    ahead.finish()
    mix.finish()
    shares = [Share(r, 0, 0)]
    shares[0].start()
    for block in blocks:
        lent(*block).wait_send()
    stages[0].prefetch()
    lag = n - 1
    stages[0].gather.tick(0)
    for k, stage in enumerate(stages):
        now = None if stage.last else Sum(section, z, n, r, stage.parity, stage.modes.wait)
        mix = share = None
        if sums is not None:
            mix = Mix(section, z, *mixes[(k + 1) // per_core], sums, stages[k + 1].gather, r)
            share = Share(r, k + 1, 1 - stage.parity)
            if k >= 1:
                shares[k - 1].wait_send()
            shares.append(share)
            mix.prime()
        lead = n - 2 if k == 0 else chunks - 2
        shift = n - 1 - lead
        stage.open()
        stage.before(0, lag)

        def tick(i):
            if sums is not None:
                sums.tick(i + lead)
            stage.gather.tick(i)

        def absorb(at):
            mix.chunk(at)

            @pl.when(at == chunks - 1)
            def _():
                sums.finish()
                mix.finish()

        def early(i, carry):
            tick(i)
            stage.before(i, lag)
            if mix is not None and not mix.flip:
                pl.when(within(i - shift, chunks))(lambda: absorb(i - shift))
            return carry

        lax.fori_loop(1, lag, early, 0)
        stage.late()
        stage.grads(0)

        def turn_over():
            if k > 0:
                stages[k - 1].close()
            if k + 1 < len(stages):
                stages[k + 1].prefetch()

        def later(q, carry):
            tick(q + lag)
            if now is not None:
                now.tick(q - 1)
            if k + 1 < len(stages):
                pl.when(q == chunks - 1)(lambda: stages[k + 1].gather.tick(0))
            stage.chunk(q)
            stage.modes_of(q)
            pl.when(q == 0)(lambda: stage.grads(1))
            pl.when(q == 1)(turn_over)
            if mix is not None and mix.flip:
                pl.when(q == 1)(sums.finish)
                for half_of in range(2):
                    at = 2 * (q - 1) + half_of
                    pl.when(within(at, chunks))(functools.partial(mix.chunk, at))
            elif mix is not None:
                at = q + lag - shift
                pl.when(jnp.logical_and(within(at, chunks), q < chunks - 1))(lambda: absorb(at))
            if share is not None:
                pl.when(q == chunks - 2)(share.start)
            return carry

        lax.fori_loop(0, chunks, later, 0)
        stage.end()
        sums = now
    stages[-1].close()
    for share in shares[-2:]:
        share.wait_send()
    for share in shares:
        share.wait_recv()


def swap_halves(value):
    return pltpu.roll(value, value.shape[-1] // 2, value.ndim - 1)


def left_lanes(shape):
    return lax.broadcasted_iota(jnp.int32, shape, len(shape) - 1) < shape[-1] // 2


def pieces(array):
    return [array[at:at + G] for at in range(0, array.shape[0], G)]


def spread_row(ref, row):
    return ref[pl.ds(row, G, stride=0), :]


class Mix:
    def __init__(self, section, z, layer, flip, sums, gather, r, lent=None):
        self.lent = lent
        self.section, self.z, self.layer, self.flip, self.r = section, z, layer, flip, r
        self.sums, self.gather = sums, gather
        self.chunks, self.grids, self.half, self.count, self.lanes = sums.part.shape[1:]
        self.channels, self.slots = r.weights.shape[2], r.wbuf.shape[0]
        self.blocks = self.chunks * self.half // 2

    def begin(self, block):
        per = self.half // 2
        q, x = block // per, 2 * (block % per)
        slot = lax.rem(block, self.slots)
        rows = pl.ds(q * self.count, self.count)
        if self.lent is not None:
            for at in range(2):
                self.lent(q, x + at).wait_recv()

        @pl.when(self.section == self.layer)
        def _():
            pltpu.make_async_copy(self.r.weights.at[0, pl.ds(self.section * self.half + x, 2), rows],
                                  self.r.wbuf.at[slot], self.r.wsem.at[slot]).start()

        @pl.when(self.section != self.layer)
        def _():
            pltpu.make_async_copy(self.r.far.at[pl.ds(x, 2), rows], self.r.wbuf.at[slot], self.r.wsem.at[slot]).start()

    def prime(self):
        for block in range(min(self.slots, self.blocks)):
            self.begin(jnp.int32(block))
        if not self.flip:
            self.r.macc[...] = jnp.zeros_like(self.r.macc)

    def chunk(self, q):
        def body(x, carry):
            block = q * (self.half // 2) + x // 2
            slot = lax.rem(block, self.slots)

            @pl.when(lax.rem(x, 2) == 0)
            def _():
                arrived(self.r.wbuf.at[slot], self.r.wsem.at[slot])

            (self.transposed if self.flip else self.forward)(q, x, self.r.wbuf.at[slot, lax.rem(x, 2)])

            @pl.when(jnp.logical_and(lax.rem(x, 2) == 1, block + self.slots < self.blocks))
            def _():
                self.begin(block + self.slots)

            return carry

        if self.flip:
            pl.when(q == 0)(self.sources)
        lax.fori_loop(0, self.half, body, 0)
        if self.flip:
            self.gather.give(q)

    def sources(self):
        def body(x, carry):
            for g in range(self.grids):
                value = jnp.concatenate([self.sums.part[self.z, at, g, x] for at in range(self.chunks)], 0)
                self.r.macc[x, 2 * g] = value
                self.r.macc[x, 2 * g + 1] = swap_halves(value)
            return carry

        lax.fori_loop(0, self.half, body, 0)

    def forward(self, q, x, weight):
        sides, groups = 2 * self.grids, self.channels // G
        total, source = self.r.macc.at[x], self.r.msrc
        for g in range(self.grids):
            value = self.sums.part[self.z, q, g, x]
            source[2 * g, :self.count] = value
            source[2 * g + 1, :self.count] = swap_halves(value)
        keys = [(k, o) for k in range(sides) for o in range(groups)]

        def body(octet, acc):
            acc = dict(zip(keys, acc))
            for u in range(G):
                i = octet * G + u
                rows = [spread_row(source.at[k], i) for k in range(sides)]
                for o in range(groups):
                    w = weight[i, o * G:(o + 1) * G, :]
                    for k in range(sides):
                        acc[k, o] = acc[k, o] + rows[k] * w
            return tuple(acc[key] for key in keys)

        acc = lax.fori_loop(0, self.count // G, body, tuple(total[k, o * G:(o + 1) * G, :] for k, o in keys))
        for key, value in zip(keys, acc):
            total[key[0], key[1] * G:(key[1] + 1) * G, :] = value

    def transposed(self, q, x, weight):
        sides, groups = 2 * self.grids, self.channels // G
        rows = [pieces(self.r.macc[x, k]) for k in range(sides)]
        out = [[] for _ in range(sides)]
        for i in range(self.count):
            total = [None] * sides
            for o in range(groups):
                w = weight[i, o * G:(o + 1) * G, :]
                for k in range(sides):
                    term = w * rows[k][o]
                    total[k] = term if total[k] is None else total[k] + term
            for k in range(sides):
                out[k].append(jnp.sum(total[k], axis=0, keepdims=True))
        left = left_lanes((self.count, self.lanes))
        for g in range(self.grids):
            a, b = [jnp.concatenate(out[2 * g + side], 0) for side in range(2)]
            self.put(g, q, x, jnp.where(left, a + swap_halves(a), swap_halves(b) - b))

    def put(self, g, q, x, value):
        if g == 0:
            self.gather.full[q, self.z, self.section, x] = value
        else:
            self.gather.give_from[q, x] = value

    def finish(self):
        if self.flip:
            return
        left = left_lanes((self.channels, self.lanes))

        def body(x, carry):
            for g in range(self.grids):
                a, b = [self.r.macc[x, 2 * g + side] for side in range(2)]
                result = jnp.where(left, a - swap_halves(a), b + swap_halves(b))
                for q in range(self.chunks):
                    self.put(g, q, x, result[q * self.count:(q + 1) * self.count])
            return carry

        lax.fori_loop(0, self.half, body, 0)
        for q in range(self.chunks):
            self.gather.give(q)


def gather_columns(f_ref, d_ref, left_of, right_of):
    channels = f_ref.shape[2] * f_ref.shape[5]
    lanes = f_ref.shape[6]
    left = left_lanes((channels, lanes))
    for stream in range(f_ref.shape[0]):
        for member in range(f_ref.shape[1]):
            for g in range(f_ref.shape[3]):
                at = (stream * f_ref.shape[1] + member) * f_ref.shape[3] + g
                both = []
                for x in range(2):
                    f = f_ref[stream, member, :, g, x].reshape(channels, lanes)
                    turned = swap_halves(f)
                    left_of[x, at] = jnp.concatenate([f, jnp.where(left, -turned, turned)], 0).T
                    both.append(d_ref[stream, member, :, g, x].reshape(channels, lanes))
                right_of[at] = jnp.concatenate(both, 0).T


def column_products(left_of, right_of, product):
    grids, double, lanes = right_of.shape
    half = double // 2
    left = left_lanes((2 * grids, lanes))
    rows = right_of.reshape(grids * double, lanes)
    sides = [left_of.at[x].reshape(grids * double, lanes) for x in range(2)]

    def body(k, carry):
        pick = pl.ds(k, 2 * grids, stride=half)
        d = rows[pick, :]
        f_high, f_low = split(jnp.concatenate([side[pick, :] for side in sides], 0))
        d_high, d_low = split(jnp.concatenate([jnp.where(left, d, 0.0), jnp.where(left, 0.0, d)], 0))
        product[k] = dot(jnp.concatenate([f_high, f_low, f_high], 0), jnp.concatenate([d_high, d_high, d_low], 0),
                         (((0,), (0,)), ((), ())))
        return carry

    lax.fori_loop(0, half, body, 0, unroll=4)


def product_rows(product, first, out):
    half, double, lanes = product.shape
    channels = double // 2
    rows = product.reshape(half * double, lanes)

    def body(i, carry):
        parts = [rows[pl.ds(part * channels + first + i, half, stride=double), :] for part in range(2)]
        tile = jnp.concatenate(parts, 0).T
        for x in range(2):
            out[x, i] = tile[x * channels:(x + 1) * channels]
        return carry

    lax.fori_loop(0, out.shape[1], body, 0, unroll=4)


class GradInput:
    def __init__(self, first, f, g, fbuf, gbuf, sem):
        self.first, self.f, self.g, self.fbuf, self.gbuf, self.sem = first, f, g, fbuf, gbuf, sem

    def load(self, x, slot):
        for layer, condition in enumerate((self.first, jnp.logical_not(self.first))):
            @pl.when(condition)
            def _():
                for j in range(len(self.f[layer])):
                    pltpu.make_async_copy(self.f[layer][j].at[:, :, :, pl.ds(2 * x, 2)], self.fbuf.at[slot, j],
                                          self.sem.at[0, slot]).start()
                    pltpu.make_async_copy(self.g[layer][j].at[:, :, :, pl.ds(2 * x, 2)], self.gbuf.at[slot, j],
                                          self.sem.at[1, slot]).start()

    def next(self, x, count):
        slot = lax.rem(x, 2)

        @pl.when(x + 1 < count)
        def _():
            self.load(x + 1, 1 - slot)

        arrived(self.fbuf.at[slot], self.sem.at[0, slot])
        arrived(self.gbuf.at[slot], self.sem.at[1, slot])
        return self.fbuf.at[slot], self.gbuf.at[slot]


def grad_input(r, first, per_core):
    f = [[getattr(r, f"f{layer}{j}") for j in range(per_core)] for layer in range(2)]
    g = [[getattr(r, f"g{layer}{j}") for j in range(per_core)] for layer in range(2)]
    return GradInput(first, f, g, r.fbuf, r.gbuf, r.in_sem)


def far_grad_kernel(per_core, r):
    section, z, n = place_and_peers()
    pairs, block = r.far.shape[0] // 2, r.out.shape[2]
    blocks = r.far.shape[1] // block
    source = grad_input(r, section != 0, per_core)

    def move(k, slot):
        p, i = k // blocks, k % blocks
        return to_core(r.out.at[slot], r.far.at[pl.ds(2 * p, 2), pl.ds(i * block, block)], (r.send.at[k], r.recv.at[k]),
                       section)

    source.load(0, 0)
    greet(section, z, n, False)

    def body(p, carry):
        gather_columns(*source.next(p, pairs), r.left_of, r.right_of)
        column_products(r.left_of, r.right_of, r.product)

        def inner(i, carry):
            k = p * blocks + i

            @pl.when(k >= 2)
            def _():
                move(k - 2, lax.rem(k, 2)).wait_send()

            product_rows(r.product, i * block, r.out.at[lax.rem(k, 2)])
            move(k, lax.rem(k, 2)).start()
            return carry

        return lax.fori_loop(0, blocks, inner, carry)

    lax.fori_loop(0, pairs, body, 0)
    total = pairs * blocks
    for k in (total - 2, total - 1):
        move(k, k % 2).wait_send()

    def close(k, carry):
        move(k, 0).wait_recv()
        return carry

    lax.fori_loop(0, total, close, 0)


def own_grad_kernel(names, per_core, m_ref, *refs):
    r = types.SimpleNamespace(**dict(zip(names, refs)))
    p, i = pl.program_id(0), pl.program_id(1)
    source = grad_input(r, m_ref[0] == 0, per_core)

    @pl.when(i == 0)
    def _():
        @pl.when(p == 0)
        def _():
            source.load(0, 0)

        gather_columns(*source.next(p, pl.num_programs(0)), r.left_of, r.right_of)
        column_products(r.left_of, r.right_of, r.product)

    r.bound_out[...] = r.bound_in[...]
    r.out[1 - m_ref[0]] = r.far[...]
    product_rows(r.product, i * r.out.shape[2], r.out.at[m_ref[0]])


def whole(array):
    return pl.BlockSpec(array.shape, lambda *_: (0,) * array.ndim)


def params(**kw):
    return pltpu.CompilerParams(vmem_limit_bytes=VMEM_LIMIT, **kw)


def local(inputs, cotangent, region_id, spectral_w, conv_w, bias_vector):
    micro_count, _, rows_dev, channels, width = inputs.shape
    lanes = spectral_w.shape[-1]
    half = lanes // 2
    kx_dev = spectral_w.shape[1]
    row_devices, sections = lax.axis_size("rows"), lax.axis_size("section")
    mode_rows, height = kx_dev * row_devices, rows_dev * row_devices
    section = lax.axis_index("section")
    per_core = micro_count // sections
    kx_half = kx_dev // sections

    plain, doubled = col_tables(width, half)

    def stacked(array):
        high, low = np_split(array)
        return np.concatenate([high, high, low], 0)

    t_plain, t_doubled, it_plain, it_doubled = [stacked(t) for t in (plain, doubled, plain.T, doubled.T)]
    kron, ikron = row_tables(height, mode_rows, lax.axis_index("rows") * rows_dev, rows_dev)

    count = 2 * G
    chunks = channels // count
    hbm, vmem = pl.BlockSpec(memory_space=pl.ANY), pl.BlockSpec(memory_space=pltpu.VMEM)
    field_shape = jax.ShapeDtypeStruct((rows_dev, channels, width), F32)
    part_dims = (row_devices, chunks, sections, kx_half, count, lanes)
    p_shape, f_shape = jax.ShapeDtypeStruct(part_dims, F32), jax.ShapeDtypeStruct(part_dims[1:], F32)
    y_shape = jax.ShapeDtypeStruct((sections, chunks, kx_half, count, lanes), F32)
    stat_shape = jax.ShapeDtypeStruct((3, R, 128), F32)
    cg_shape = jax.ShapeDtypeStruct((2 * channels, 2 * channels), F32)
    bg_shape = jax.ShapeDtypeStruct((channels, width), F32)
    bound_shape = jax.ShapeDtypeStruct((micro_count, rows_dev, channels, width), F32)
    dma = pltpu.SemaphoreType.DMA
    field_buf = pltpu.VMEM((rows_dev, channels, width), F32)
    full_dims = (chunks, row_devices, sections, kx_half, count, lanes)
    spread = pltpu.VMEM((width // 128, rows_dev * count, 128), F32)
    energy = pltpu.VMEM((rows_dev, G, width), F32)
    line_sems = dma((2, chunks, row_devices))
    def run(body, ident, ins, outs, scratch, cost=50, aliases=None):
        names = [*ins, *outs, *scratch]
        spec = lambda entry: vmem if isinstance(entry, tuple) else hbm
        plain = lambda entry: entry[0] if isinstance(entry, tuple) else entry
        kernel = lambda *refs: body(types.SimpleNamespace(**dict(zip(names, refs))))
        positions = {list(ins).index(k): list(outs).index(v) for k, v in (aliases or {}).items()}
        result = pl.pallas_call(
            kernel, in_specs=[spec(e) for e in ins.values()], out_specs=[spec(e) for e in outs.values()],
            out_shape=[plain(e) for e in outs.values()], scratch_shapes=list(scratch.values()),
            input_output_aliases=positions,
            cost_estimate=pl.CostEstimate(flops=0, bytes_accessed=cost * 3_000_000, transcendentals=0),
            compiler_params=params(collective_id=ident, has_side_effects=True))(*[plain(e) for e in ins.values()])
        return types.SimpleNamespace(**dict(zip(outs, result)))

    conv_rows_at_once = 256 // channels
    maps = jnp.stack([conv_w[0].T, conv_w[0]])
    at = np.arange(conv_rows_at_once * channels) // channels
    wide_own = jnp.where(at[:, None] == at[None, :], jnp.tile(maps, (1, conv_rows_at_once, conv_rows_at_once)), 0.0)
    wide_own = jnp.stack(jnp.split(wide_own, wide_own.shape[2] // 128, 2), 1)
    bias_own = jnp.broadcast_to(bias_vector[0][:, None], (channels, width))

    streams = range(per_core)
    members = lax.axis_size("batch")
    kinds = ["middle", "turn", "back", "tail"]
    mixes = [(0, False), (1, False), (1, True), (0, True)]
    names = ["f00", "f01", "f10", "f11", "g10", "g11", "g00", "g01"]
    places = [dict(a=0, z=1), dict(a=2, z=3), dict(a=4, z=5, cot=6), dict(a=0, z=1, cot=2),
              dict(gz=3, a=4, h=5, dg=6), dict(gz=0, a=1, h=2, dg=3), dict(gz=4, a=5, h=6), dict(gz=0, a=1, h=2)]
    both = (2,)
    ins = dict(inputs=inputs, cotangent=cotangent, region=region_id, weights=spectral_w, t_plain=(t_plain,),
               t_doubled=(t_doubled,), it_plain=(it_plain,), it_doubled=(it_doubled,), kron=(kron,), ikron=(ikron,),
               wide_own=(wide_own,), bias_own=(bias_own,))
    outs = dict(far=jax.ShapeDtypeStruct((kx_half,) + spectral_w.shape[2:], F32), bound=bound_shape, stat=(jax.ShapeDtypeStruct((2 * per_core,) + stat_shape.shape, F32),),
                cg=(jax.ShapeDtypeStruct((2 * per_core,) + cg_shape.shape, F32),),
                bg=(jax.ShapeDtypeStruct((2 * per_core,) + bg_shape.shape, F32),),
                **{f"{name}{j}": field_shape for name in ("a1_", "dg0_", "gz1_", "ga1_", "gz0_") for j in streams},
                **{f"shared{i}": jax.ShapeDtypeStruct((members,) + f_shape.shape, F32) for i in range(len(names))})
    scratch = dict(
        fields=pltpu.VMEM((7,) + field_shape.shape, F32), full=pltpu.VMEM(both + full_dims, F32),
        part=pltpu.VMEM(both + part_dims, F32),
        come=pltpu.VMEM(both + (2, chunks, row_devices - 1) + part_dims[2:], F32),
        keep=pltpu.VMEM(both + f_shape.shape, F32), y_give=pltpu.VMEM(both + y_shape.shape[1:], F32),
        p_buf=pltpu.VMEM(full_dims, F32), spread=spread, eo=energy, eb=energy,
        rid=pltpu.VMEM((2, rows_dev, width), jnp.int32),
        wbuf=pltpu.VMEM((3, 2, count, channels, lanes), F32), macc=pltpu.VMEM((kx_half, 2 * sections, channels, lanes), F32),
        msrc=pltpu.VMEM((2 * sections, channels, lanes), F32),
        bias=pltpu.VMEM((2, channels, width), F32),
        conv=pltpu.VMEM((4, len(at), 3 * len(at)), BF16), m_cross=dma((2, 2)),
        field_sem=dma((7,)), rid_sem=dma(both), out_sem=dma((2, 2, chunks)), wsem=dma((3,)), w_load=dma((chunks, kx_half)), w_cross=dma((2, chunks, kx_half)),
        send=dma(both + (2, chunks, row_devices)), recv=dma(both + (2, chunks, row_devices)),
        red_send=dma(both + (2, chunks, row_devices)), red_recv=dma(both + (2, chunks, row_devices)),
        y_cross=dma((2, 2, chunks)), p_cross=dma((2, 2, chunks)),
        b_local=dma((2, chunks)), b_cross=dma((2, 2, chunks)),
        s_local=dma(both), s_send=dma((2, members)), s_recv=dma((len(names), members)))
    done = run(functools.partial(stages_kernel, per_core, kinds, places, mixes), 0, ins, outs, scratch, cost=400)
    gathered = {name: getattr(done, f"shared{i}") for i, name in enumerate(names)}
    bound, calls = done.bound, 0

    grids = per_core * members * sections
    block = 2 * G
    pairs, blocks = kx_half // 2, channels // block
    in_buf = pltpu.VMEM((2, per_core, members, chunks, sections, 2, count, lanes), F32)
    grad_scratch = dict(fbuf=in_buf, gbuf=in_buf, in_sem=dma((2, 2)), left_of=pltpu.VMEM((2, grids, lanes, lanes), F32),
                        right_of=pltpu.VMEM((grids, lanes, lanes), F32), product=pltpu.VMEM((half, lanes, lanes), F32))
    far_grad = run(functools.partial(far_grad_kernel, per_core), 1 + calls, gathered,
                   dict(far=jax.ShapeDtypeStruct((kx_half, channels, channels, lanes), F32)),
                   dict(out=pltpu.VMEM((2, 2, block, channels, lanes), F32), send=dma((pairs * blocks,)),
                        recv=dma((pairs * blocks,)), **grad_scratch)).far
    bound_rows = bound.reshape(micro_count * rows_dev, channels, width)
    bound_block = pl.BlockSpec((bound_rows.shape[0] // (pairs * blocks), channels, width),
                               lambda p, i, m: (p * blocks + i, 0, 0))
    grid_spec = pltpu.PrefetchScalarGridSpec(
        num_scalar_prefetch=1, grid=(pairs, blocks),
        in_specs=[hbm] * len(gathered)
        + [pl.BlockSpec((2, block, channels, lanes), lambda p, i, m: (p, i, 0, 0)), bound_block],
        out_specs=[pl.BlockSpec((2, 2, block, channels, lanes), lambda p, i, m: (0, p, i, 0, 0)), bound_block],
        scratch_shapes=list(grad_scratch.values()))
    spectral_grad, boundary = pl.pallas_call(
        functools.partial(own_grad_kernel, [*gathered, "far", "bound_in", "out", "bound_out", *grad_scratch], per_core),
        grid_spec=grid_spec, out_shape=[jax.ShapeDtypeStruct((2, kx_half, channels, channels, lanes), F32),
                                        jax.ShapeDtypeStruct(bound_rows.shape, F32)],
        cost_estimate=pl.CostEstimate(flops=0, bytes_accessed=150_000_000, transcendentals=0),
        compiler_params=params())(
            jnp.reshape(section, (1,)).astype(jnp.int32), *gathered.values(), far_grad, bound_rows)
    spectral_grad = spectral_grad.reshape(spectral_w.shape)
    boundary = boundary.reshape((1, micro_count, 1) + inputs.shape[2:])

    def lower(value):
        return (value[:channels, :channels] + value[channels:, channels:]
                + value[:channels, channels:] + value[channels:, :channels])

    pair = lambda value: jnp.sum(value.reshape((2, per_core) + value.shape[1:]), 1)
    conv_local = jnp.stack([lower(value) for value in pair(done.cg)[::-1]])
    bias_local = jnp.sum(pair(done.bg)[::-1], -1)
    stat_local = jnp.sum(pair(done.stat), -1)
    shapes = [v.shape for v in (conv_local, bias_local, stat_local)]
    flat_sums = jnp.concatenate([v.reshape(-1) for v in (conv_local, bias_local, stat_local)])
    length = flat_sums.shape[0]
    flat_sums = jnp.pad(flat_sums, (0, -length % 1024)).reshape(-1, 128)
    flat_sums = jnp.sum(lax.all_gather(flat_sums, ("section", "batch", "rows"), axis=0), 0).reshape(-1)
    ends = np.cumsum([0] + [math.prod(shape) for shape in shapes])
    conv_sum, bias_sum, stat_sum = [flat_sums[ends[i]:ends[i + 1]].reshape(shapes[i]) for i in range(3)]
    own_stat = lax.dynamic_index_in_dim(stat_sum, section, 0, False)
    layer_rms = jnp.sqrt(own_stat[:2] / (channels * own_stat[2])[None, :] + 1e-06)[None]
    own = lambda value: lax.dynamic_slice_in_dim(value, section, 1, 0)
    return boundary, spectral_grad, own(conv_sum), own(bias_sum), layer_rms


def solution(mesh):
    placed = (
        P(None, "batch", "rows", None, None),
        P(None, "batch", "rows", None, None),
        P(None, "batch", "rows", None),
        P("section", "rows", None, None, None),
        P("section", None, None),
        P("section", None),
    )
    return jax.shard_map(
        local,
        mesh=mesh,
        in_specs=placed,
        out_specs=(
            P("section", None, "batch", "rows", None, None),
            P("section", "rows", None, None, None),
            P("section", None, None),
            P("section", None),
            P("section", None, None),
        ),
        check_vma=False,
    )
```

```python
import functools
import math
import types

import jax
import jax.numpy as jnp
import numpy as np
from jax import lax
from jax.experimental import pallas as pl
from jax.experimental.pallas import tpu as pltpu
from jax.sharding import PartitionSpec as P

R = 8
G = 8
F32 = jnp.float32
BF16 = jnp.bfloat16
VMEM_LIMIT = 62 * 1024 * 1024
MESH = pl.DeviceIdType.MESH


def split(value):
    high = value.astype(BF16)
    return high, (value - high.astype(F32)).astype(BF16)


def dot(left, right, dims=(((1,), (0,)), ((), ()))):
    return lax.dot_general(left, right, dims, preferred_element_type=F32)


def dot3(left, right):
    return dot(left[0], right[0]) + (dot(left[1], right[0]) + dot(left[0], right[1]))


def np_split(value):
    high = value.astype(np.float32).astype(BF16)
    return high, (value - high.astype(np.float64)).astype(np.float32).astype(BF16)


def col_tables(width, half):
    phase = 2.0 * math.pi / width * (np.outer(np.arange(width), np.arange(half)) % width)
    cosine, sine = np.cos(phase) / math.sqrt(width), np.sin(phase) / math.sqrt(width)
    plain = np.concatenate([cosine, -sine, -sine, -cosine], 1)
    doubled = plain * np.tile(np.where(np.arange(half) == 0, 1.0, 2.0), 4)[None, :]
    return plain, doubled


def row_tables(height, mode_rows, first_row, rows_dev):
    position = jnp.arange(mode_rows, dtype=jnp.int32)
    frequency = jnp.where(position < mode_rows // 2, position, height - mode_rows + position)
    row = first_row + jnp.arange(rows_dev, dtype=jnp.int32)
    phase = 2.0 * math.pi / height * (frequency[:, None] * row[None, :] % height).astype(F32)
    small = jnp.concatenate([jnp.cos(phase), jnp.sin(phase)], 1) / math.sqrt(height)
    rounded = lax.reduce_precision(small, 8, 7)
    high, low = rounded.astype(BF16), (small - rounded).astype(BF16)
    forward = jnp.concatenate([jnp.concatenate([high, high], 1), jnp.concatenate([low, jnp.zeros_like(low)], 1)], 0)
    inverse = jnp.concatenate([high.T, high.T, low.T], 1)
    return forward, inverse


def to_modes(value, table, kron, spread, p_ref):
    mode_rows, count, lanes = p_ref.shape
    rows = value.shape[0] // count
    high, low = split(value)
    spectra = dot(jnp.concatenate([high, low, high], 1), table)
    for i in range(2):
        spread[i] = spectra[:, i * lanes:(i + 1) * lanes]
    out = p_ref.reshape(mode_rows * count, lanes)
    for first in range(0, count, 2):
        sides = []
        for c in (first, first + 1):
            pick = pl.ds(c, rows, stride=count)
            sides.append(jnp.concatenate([spread[i, pick, :] for i in range(2)], 0))
        high, low = split(jnp.concatenate(sides, 1))
        both = dot(kron, jnp.concatenate([high, low], 0))
        result = both[:mode_rows] + both[mode_rows:]
        for i in range(2):
            out[pl.ds(first + i, mode_rows, stride=count), :] = result[:, i * lanes:(i + 1) * lanes]


def from_modes(y_ref, table, kron, spread):
    mode_rows, count, lanes = y_ref.shape
    rows, pieces = spread.shape[1] // count, spread.shape[0]
    modes = y_ref.reshape(mode_rows * count, lanes)
    sides = []
    for first in range(0, count, 2):
        pair = [modes[pl.ds(c, mode_rows, stride=count), :] for c in (first, first + 1)]
        high, low = split(jnp.concatenate(pair, 1))
        both = dot(kron, jnp.concatenate([high, low, high], 0))
        for i in range(2):
            side = both[:, i * lanes:(i + 1) * lanes]
            sides.append(jnp.concatenate([side[:rows], side[rows:]], 1))
    high, low = split(jnp.concatenate(sides, 0))
    out = dot(jnp.concatenate([high, low, high], 1), table)
    for c in range(count):
        for i in range(pieces):
            spread[i, pl.ds(c, rows, stride=count), :] = out[c * rows:(c + 1) * rows, i * 128:(i + 1) * 128]
    return jnp.concatenate([spread[i] for i in range(pieces)], 1)


def gelu_parts(z):
    gauss = jnp.exp2((-0.5 / math.log(2.0)) * (z * z))
    base = 1.0 + (0.3275911 / math.sqrt(2.0)) * jnp.abs(z)
    t = pl.reciprocal(base, approx=True)
    t = t * (2.0 - base * t)
    poly = t * (0.127414796 + t * (-0.142248368 + t * (0.7107068705 + t * (-0.7265760135 + t * 0.5307027145))))
    tail = poly * gauss
    phi = jnp.where(z >= 0, 1.0 - tail, tail)
    return z * phi, phi + z * (gauss * (1.0 / math.sqrt(2.0 * math.pi)))


def flat(ref):
    rows, count, width = ref.shape
    return ref[...].reshape(rows * count, width)


def put(ref, value):
    ref[...] = value.reshape(ref.shape)


def place_and_peers():
    section, z = lax.axis_index("section"), lax.axis_index("rows")
    return section, z, lax.axis_size("rows")


def greet(section, z, n, lines, members=0):
    barrier = pltpu.get_barrier_semaphore()
    pl.semaphore_signal(barrier, inc=1, device_id={"section": 1 - section}, device_id_type=MESH)
    if not lines:
        pl.semaphore_wait(barrier, 1)
        return

    @pl.when(z > 0)
    def _():
        pl.semaphore_signal(barrier, inc=1, device_id={"rows": z - 1}, device_id_type=MESH)

    @pl.when(z < n - 1)
    def _():
        pl.semaphore_signal(barrier, inc=1, device_id={"rows": z + 1}, device_id_type=MESH)

    for away in range(1, members):
        pl.semaphore_signal(barrier, inc=1, device_id={"batch": lax.rem(lax.axis_index("batch") + away, members)},
                            device_id_type=MESH)

    others = 1 + max(members - 1, 0)
    pl.semaphore_wait(barrier, others + (z > 0).astype(jnp.int32) + (z < n - 1).astype(jnp.int32))


def to_core(src, dst, sems, section):
    return pltpu.make_async_remote_copy(src_ref=src, dst_ref=dst, send_sem=sems[0], recv_sem=sems[1],
                                        device_id={"section": 1 - section}, device_id_type=MESH)


def guard(condition, body):
    if isinstance(condition, (bool, np.bool_)):
        if condition:
            body()
    else:
        pl.when(condition)(body)


class Line:
    def __init__(self, section, z, n, chunks, send, recv):
        self.section, self.z, self.n, self.chunks = section, z, n, chunks
        self.send, self.recv = send, recv

    def move(self, way, q, hop, src, dst):
        return pltpu.make_async_remote_copy(
            src_ref=src, dst_ref=dst, send_sem=self.send.at[way, q, hop], recv_sem=self.recv.at[way, q, hop],
            device_id={"rows": self.z + 1 if way == 0 else self.z - 1}, device_id_type=MESH)

    def sends(self, way):
        return self.z < self.n - 1 if way == 0 else self.z > 0

    def hears(self, way):
        return self.z > 0 if way == 0 else self.z < self.n - 1


def within(value, count):
    return jnp.logical_and(value >= 0, value < count)


class Gather(Line):
    def __init__(self, section, z, n, r, parity):
        super().__init__(section, z, n, r.full.shape[1], r.send.at[parity], r.recv.at[parity])
        self.full, self.give_from = r.full.at[parity], r.y_give.at[parity]
        self.cross = r.y_cross.at[parity]

    def swap(self, q):
        return to_core(self.give_from.at[q], self.full.at[q, self.z, self.section],
                       (self.cross.at[0, q], self.cross.at[1, q]), self.section)

    def give(self, q):
        self.swap(q).start()

    def hop(self, way, q, hop):
        piece = self.full.at[q, self.source(way, hop)]
        return self.move(way, q, hop, piece, piece)

    def source(self, way, hop):
        return self.z - hop if way == 0 else self.z + hop

    def known(self, way, hop):
        at = self.source(way, hop)
        return at >= 0 if way == 0 else at < self.n

    def own(self, q):
        self.swap(q).wait_recv()
        for way in range(2):
            @pl.when(self.sends(way))
            def _():
                self.hop(way, q, 0).start()

    def step(self, q, hop):
        for way in range(2):
            @pl.when(self.known(way, hop + 1))
            def _():
                piece = self.full.at[q, self.source(way, hop + 1)]
                self.move(way, q, hop, piece, piece).wait_recv()

                @pl.when(self.sends(way))
                def _():
                    self.hop(way, q, hop + 1).start()

    def free(self, t):
        pl.when(within(t, self.chunks))(functools.partial(self.own, t))

    def rest(self, t):
        for hop in range(self.n - 1):
            q = t - hop - 1
            pl.when(within(q, self.chunks))(functools.partial(self.step, q, hop))

    def finish(self):
        def body(q, carry):
            self.swap(q).wait_send()
            for way in range(2):
                for hop in range(self.n - 1):
                    @pl.when(jnp.logical_and(self.sends(way), self.known(way, hop)))
                    def _():
                        self.hop(way, q, hop).wait_send()
            return carry

        lax.fori_loop(0, self.chunks, body, 0)


class Sum(Line):
    def __init__(self, section, z, n, r, parity, admit):
        super().__init__(section, z, n, r.part.shape[2], r.red_send.at[parity], r.red_recv.at[parity])
        self.part, self.come, self.keep, self.admit = r.part.at[parity], r.come.at[parity], r.keep.at[parity], admit

    def owner(self, way, hop):
        return self.z + self.n - hop if way == 0 else self.z - self.n + hop

    def valid(self, way, hop):
        return self.z <= hop - 1 if way == 0 else self.z >= self.n - hop

    def sent(self, way, q, hop):
        return self.move(way, q, hop, self.part.at[self.owner(way, hop), q], self.come.at[way, q, hop - 1])

    def heard(self, way, q, hop):
        come = self.come.at[way, q, hop - 1]
        self.move(way, q, hop, come, come).wait_recv()

    def first(self, q):
        self.admit(q)
        self.launch(q, 1)

    def launch(self, q, hop):
        for way in range(2):
            @pl.when(jnp.logical_and(self.valid(way, hop), jnp.logical_not(self.hears(way))))
            def _():
                self.sent(way, q, hop).start()

    def step(self, q, hop):
        for way in range(2):
            @pl.when(jnp.logical_and(self.valid(way, hop), self.hears(way)))
            def _():
                self.heard(way, q, hop - 1)
                owner = self.owner(way, hop)
                self.part[owner, q] = self.part[owner, q] + self.come[way, q, hop - 2]
                self.sent(way, q, hop).start()

    def final(self, q):
        for way in range(2):
            @pl.when(self.hears(way))
            def _():
                self.heard(way, q, self.n - 1)
                self.part[self.z, q] = self.part[self.z, q] + self.come[way, q, self.n - 2]

        self.keep[q] = self.part[self.z, q]

    def free(self, t):
        pl.when(within(t, self.chunks))(functools.partial(self.first, t))
        for hop in range(2, self.n):
            q = t - hop + 1
            pl.when(within(q, self.chunks))(functools.partial(self.launch, q, hop))

    def rest(self, t):
        for hop in range(2, self.n + 1):
            q = t - hop + 1
            pl.when(within(q, self.chunks))(
                functools.partial(self.step, q, hop) if hop < self.n else functools.partial(self.final, q))

    def tick(self, t):
        self.free(t)
        self.rest(t)

    def finish(self):
        def body(q, carry):
            for way in range(2):
                for hop in range(1, self.n):
                    @pl.when(self.valid(way, hop))
                    def _():
                        self.sent(way, q, hop).wait_send()
            return carry

        lax.fori_loop(0, self.chunks, body, 0)


def fetch(src, dst, sem, parts=1):
    step = dst.shape[0] // parts
    for i in range(parts):
        pltpu.make_async_copy(src.at[pl.ds(i * step, step)], dst.at[pl.ds(i * step, step)], sem).start()


def arrived(dst, sem):
    pltpu.make_async_copy(dst, dst, sem).wait()


def portions(total, count):
    return [(i * total // count, (i + 1) * total // count) for i in range(count)]


def conv_rows(weight, bias, a, out, first, last):
    channels, width = a.shape[1:]
    block = weight.shape[0] // channels

    def body(i, carry):
        at = pl.ds(i * block, block)
        high, low = split(a[at].reshape(block * channels, width))
        result = dot(weight[...], jnp.concatenate([high, high, low], 0)).reshape(block, channels, width)
        out[at] = result + bias[...][None] if bias is not None else out[at] + result
        return carry

    lax.fori_loop(first, last, body, 0)


def grad_rows(a, gz, cg_ref, bg_ref, first, last):
    channels, width = a.shape[1:]

    def body(r, carry):
        grad, bias = carry
        g = gz[r]
        left = jnp.concatenate(split(a[r]), 0)
        right = jnp.concatenate(split(g), 0)
        return grad + dot(left, right, (((1,), (1,)), ((), ()))), bias + g

    grad, bias = lax.fori_loop(first, last, body, (cg_ref[...], bg_ref[...]))
    cg_ref[...] = grad
    bg_ref[...] = bias


def chunk_of(ref, q, count):
    rows, _, width = ref.shape
    return ref[:, pl.ds(pl.multiple_of(q * count, count), count), :].reshape(rows * count, width)


def chunk_at(ref, q, count):
    return ref.at[:, pl.ds(pl.multiple_of(q * count, count), count), :]


class Modes:
    def __init__(self, section, buffer, p_out, cross):
        self.section, self.buffer, self.p_out, self.cross = section, buffer, p_out, cross

    def view(self, q):
        n, halves, kx, count, lanes = self.buffer.shape[1:]
        return self.buffer.at[q].reshape(n * halves * kx, count, lanes)

    def cross_copy(self, q):
        return to_core(self.buffer.at[q, :, 1 - self.section], self.p_out.at[:, q, 1],
                       (self.cross.at[0, q], self.cross.at[1, q]), self.section)

    def start(self, q):
        self.cross_copy(q).start()
        self.p_out[:, q, 0] = self.buffer[q, :, self.section]

    def wait(self, q):
        self.cross_copy(q).wait()


class Bound:
    def __init__(self, section, owner, micro, other, source, bound, local, cross):
        self.section, self.owner, self.micro, self.other = section, owner, micro, other
        self.source, self.bound, self.local, self.cross = source, bound, local, cross

    def copies(self, q, count, micro):
        src, dst = chunk_at(self.source, q, count), chunk_at(self.bound.at[micro], q, count)
        return (pltpu.make_async_copy(src, dst, self.local.at[q]),
                to_core(src, dst, (self.cross.at[0, q], self.cross.at[1, q]), self.section))

    def start(self, q, count):
        here, there = self.copies(q, count, self.micro)

        @pl.when(self.section == self.owner)
        def _():
            here.start()

        @pl.when(self.section != self.owner)
        def _():
            there.start()

    def wait(self, q, count):
        here, there = self.copies(q, count, self.micro)
        come = self.copies(q, count, self.other)[1]

        @pl.when(self.section == self.owner)
        def _():
            here.wait()
            come.wait_recv()

        @pl.when(self.section != self.owner)
        def _():
            there.wait_send()


def add_squares(value, total):
    rows, _, width = total.shape
    square = (value * value).reshape(rows, -1, width)
    for at in range(0, square.shape[1], G):
        total[...] += square[:, at:at + G]


def region_sums(rid_ref, eo, eb, stat_ref):
    rows, _, width = eo.shape
    rid = rid_ref[...]
    energies = (jnp.sum(eo[...], axis=1), jnp.sum(eb[...], axis=1), jnp.ones((rows, width), F32))
    for kind in range(3):
        for region in range(R):
            line = jnp.sum(jnp.where(rid == region + 1, energies[kind], 0.0), axis=0, keepdims=True)
            total = line[:, :128]
            for piece in range(1, width // 128):
                total = total + line[:, piece * 128:(piece + 1) * 128]
            stat_ref[kind, region:region + 1, :] = total


class Share:
    def __init__(self, r, index, parity):
        self.r, self.index, self.parity = r, index, parity
        self.me, self.members = lax.axis_index("batch"), lax.axis_size("batch")

    def copies(self):
        source, target = self.r.keep.at[self.parity], getattr(self.r, f"shared{self.index}").at[self.me]
        yield pltpu.make_async_copy(source, target, self.r.s_local.at[self.parity])
        for away in range(1, self.members):
            yield pltpu.make_async_remote_copy(
                src_ref=source, dst_ref=target, send_sem=self.r.s_send.at[self.parity, away],
                recv_sem=self.r.s_recv.at[self.index, away],
                device_id={"batch": lax.rem(self.me + away, self.members)}, device_id_type=MESH)

    def start(self):
        for copy in self.copies():
            copy.start()

    def wait_send(self):
        for i, copy in enumerate(self.copies()):
            if i == 0:
                copy.wait()
            else:
                copy.wait_send()

    def wait_recv(self):
        for i, copy in enumerate(self.copies()):
            if i > 0:
                copy.wait_recv()


class Head:
    def __init__(self, micro, place, parity, section, r):
        self.r, self.field, self.sem = r, r.fields.at[place], r.field_sem.at[place]
        self.source, self.count = r.inputs.at[micro, 0], r.full.shape[5]
        self.modes = Modes(section, r.p_buf, r.part.at[parity], r.p_cross.at[parity])

    def fetch(self):
        fetch(self.source, self.field, self.sem, 4)

    def got(self):
        arrived(self.field, self.sem)

    def chunk(self, q):
        r = self.r
        to_modes(chunk_of(self.field, q, self.count), r.t_plain[...], r.kron[...], r.spread, self.modes.view(q))
        self.modes.start(q)


class Stage:
    def __init__(self, k, kind, j, per_core, places, section, z, n, r):
        self.k, self.kind, self.j, self.r, self.section, self.n = k, kind, j, r, section, n
        self.parity = k % 2
        self.micro, self.other = section * per_core + j, (1 - section) * per_core + j
        self.forward, self.last = kind in ("middle", "turn"), kind == "tail"
        self.buffers = {name: r.fields.at[i] for name, i in places.items()}
        self.sems = {name: r.field_sem.at[i] for name, i in places.items()}
        self.gather = Gather(section, z, n, r, self.parity)
        self.count, self.lanes = r.full.shape[5], r.full.shape[6]
        self.chunks = r.full.shape[1]
        plain = lambda name: getattr(r, f"{name}{j}")
        if kind == "middle":
            self.loads = dict(a=r.inputs.at[self.micro, 0])
            self.saves = dict(a=plain("a1_"), z=plain("dg0_"))
        elif kind == "turn":
            self.loads = dict(a=plain("a1_"), cot=r.cotangent.at[self.micro, 0])
            self.saves = dict(cot=plain("gz1_"))
        elif kind == "back":
            self.loads = dict(gz=plain("gz1_"), h=r.cotangent.at[self.micro, 0], a=plain("a1_"), dg=plain("dg0_"))
            self.saves = dict(h=plain("ga1_"), dg=plain("gz0_"))
        else:
            self.loads = dict(gz=plain("gz0_"), h=plain("ga1_"), a=r.inputs.at[self.micro, 0])
            self.saves = {}
        layer = 0 if kind in ("middle", "tail") else 1
        self.weight, self.bias = r.conv.at[layer if self.forward else 2 + layer], r.bias.at[layer]
        self.table = r.t_plain if kind == "middle" else r.t_doubled
        self.itable = r.it_doubled if self.forward else r.it_plain
        if not self.last:
            self.modes = Modes(section, r.p_buf, r.part.at[self.parity], r.p_cross.at[self.parity])
        if kind in ("turn", "tail"):
            self.bound = Bound(section, 1 if kind == "turn" else 0, self.micro, self.other,
                               self.buffers["a" if kind == "turn" else "h"], r.bound,
                               r.b_local.at[self.parity], r.b_cross.at[self.parity])

    def prefetch(self):
        for name, src in self.loads.items():
            if self.kind != "middle":
                fetch(src, self.buffers[name], self.sems[name])
        if self.forward:
            self.rid_copy().start()

    def rid_copy(self):
        return pltpu.make_async_copy(self.r.region.at[self.micro, 0], self.r.rid.at[self.parity],
                                     self.r.rid_sem.at[self.parity])

    def got(self, name):
        arrived(self.buffers[name], self.sems[name])

    def open(self):
        r, b = self.r, self.buffers
        if self.forward:
            r.eo[...] = jnp.zeros_like(r.eo)
            r.eb[...] = jnp.zeros_like(r.eb)
            if self.kind != "middle":
                self.got("a")
        else:
            for name in ("gz", "h", "a"):
                self.got(name)
            at = self.k - self.r.first_back
            r.cg[at] = jnp.zeros_like(r.cg[at])
            r.bg[at] = jnp.zeros_like(r.bg[at])

    def before(self, i):
        r, b = self.r, self.buffers
        a = b["a"]
        rows, channels = a.shape[:2]
        blocks, parts = rows // (self.weight.shape[0] // channels), self.n - 1
        span = (i * blocks // parts, (i + 1) * blocks // parts)
        if self.forward:
            conv_rows(self.weight, self.bias, a, b["z"], *span)
        else:
            conv_rows(self.weight, None, b["gz"], b["h"], *span)
            at = self.k - r.first_back
            grad_rows(a, b["gz"], r.cg.at[at], r.bg.at[at], i * rows // parts, (i + 1) * rows // parts)

    def outs(self, q):
        return [pltpu.make_async_copy(chunk_at(self.buffers[name], q, self.count), chunk_at(dst, q, self.count),
                                      self.r.out_sem.at[self.parity, i, q])
                for i, (name, dst) in enumerate(self.saves.items())]

    def late(self):
        for name in ("cot", "dg"):
            if name in self.loads:
                self.got(name)

    def chunk(self, q):
        r, b, count = self.r, self.buffers, self.count
        spectral = from_modes(self.gather.full.at[q].reshape(-1, count, self.lanes), self.itable[...], r.ikron[...],
                              r.spread)
        if self.forward:
            branch, slope = gelu_parts(spectral + chunk_of(b["z"], q, count))
            if self.kind == "turn":
                put(chunk_at(b["cot"], q, count), chunk_of(b["cot"], q, count) * slope)
            else:
                put(chunk_at(b["z"], q, count), slope)
            add_squares(branch, r.eb)
            out = chunk_of(b["a"], q, count) + branch
            put(chunk_at(b["a"], q, count), out)
            add_squares(out, r.eo)
            source = b["cot" if self.kind == "turn" else "a"]
        else:
            ga = spectral + chunk_of(b["h"], q, count)
            put(chunk_at(b["h"], q, count), ga)
            if not self.last:
                put(chunk_at(b["dg"], q, count), ga * chunk_of(b["dg"], q, count))
                source = b["dg"]
        for copy in self.outs(q):
            copy.start()
        if self.kind in ("turn", "tail"):
            self.bound.start(q, count)
        if not self.last:
            to_modes(chunk_of(source, q, count), self.table[...], r.kron[...], r.spread, self.modes.view(q))

            pl.when(q == self.chunks - 1)(self.gather.finish)
            self.modes.start(q)

    def end(self):
        if self.forward:
            self.rid_copy().wait()
            region_sums(self.r.rid.at[self.parity], self.r.eo, self.r.eb, self.r.stat.at[self.k])
        if self.last:
            self.gather.finish()

    def close(self):
        def body(q, carry):
            for copy in self.outs(q):
                copy.wait()
            if self.kind in ("turn", "tail"):
                self.bound.wait(q, self.count)
            return carry

        lax.fori_loop(0, self.chunks, body, 0)


def stages_kernel(per_core, kinds, places, mixes, r):
    section, z, n = place_and_peers()
    chunks, count = r.full.shape[1], r.full.shape[5]
    r.first_back = 2 * per_core
    stages = [Stage(k, kind, j, per_core, places[k], section, z, n, r)
              for k, (kind, j) in enumerate((kind, j) for kind in kinds for j in range(per_core))]
    heads = [Head(section * per_core + j, places[j]["a"], j, section, r) for j in range(per_core)]
    half = r.far.shape[0]

    def spare(q, x):
        groups = r.fields.shape[1] // count
        at = q * half + x
        place, at = 3 + at // (2 * groups), at % (2 * groups)
        side, group = at // groups, at % groups
        return r.fields.at[place, pl.ds(pl.multiple_of(group * count, count), count), :,
                           pl.ds(pl.multiple_of(side * 128, 128), 128)]

    def lend_in(q, x):
        rows = pl.ds(q * count, count)
        return pltpu.make_async_copy(r.weights.at[0, (1 - section) * half + x, rows], spare(q, x), r.w_load.at[q, x])

    def lent(q, x):
        return to_core(spare(q, x), r.far.at[x, pl.ds(q * count, count)],
                       (r.w_cross.at[0, q, x], r.w_cross.at[1, q, x]), section)

    blocks = [(q, x) for q in range(chunks) for x in range(half)]
    for head in heads:
        head.fetch()
    for block in blocks:
        lend_in(*block).start()
    greet(section, z, n, True, lax.axis_size("batch"))
    wide = r.full.at[1].reshape(-1, *r.wide_own.shape)
    small = [to_core(wide.at[section], wide.at[section], (r.m_cross.at[0, 0], r.m_cross.at[1, 0]), section),
             to_core(r.bias.at[section], r.bias.at[section], (r.m_cross.at[0, 1], r.m_cross.at[1, 1]), section)]
    wide[section] = r.wide_own[...]
    r.bias[section] = r.bias_own[...]
    for copy in small:
        copy.start()
    ahead, sums = [Sum(section, z, n, r, j, heads[j].modes.wait) for j in range(2)]
    mix = Mix(section, z, *mixes[0], ahead, stages[0].gather, r, lent)
    heads[0].got()

    def opening(q, carry):
        ahead.tick(q - 1)
        heads[0].chunk(q)

        @pl.when(q == 0)
        def _():
            for block in blocks:
                lend_in(*block).wait()
                lent(*block).start()

        return carry

    lax.fori_loop(0, chunks, opening, 0)
    for copy in small:
        copy.wait()
    for way in range(2):
        for layer in range(2):
            high, low = split(jnp.concatenate([wide[layer, way, side] for side in range(wide.shape[2])], 1))
            r.conv[2 * way + layer] = jnp.concatenate([high, low, high], 1)
    heads[1].got()
    mix.prime()

    def second(q, carry):
        ahead.tick(q + chunks - 1)

        @pl.when(q < chunks)
        def _():
            heads[1].chunk(q)

        sums.tick(q - 1)
        pl.when(within(q + chunks - n, chunks))(lambda: mix.chunk(q + chunks - n))
        return carry

    lax.fori_loop(0, n, second, 0)
    ahead.finish()
    mix.finish()
    shares = [Share(r, 0, 0)]
    shares[0].start()
    for block in blocks:
        lent(*block).wait_send()
    stages[0].prefetch()
    for k, stage in enumerate(stages):
        gather = stage.gather
        now = None if stage.last else Sum(section, z, n, r, stage.parity, stage.modes.wait)
        mix = None
        if sums is not None:
            mix = Mix(section, z, *mixes[(k + 1) // per_core], sums, stages[k + 1].gather, r)
            share = Share(r, k + 1, 1 - stage.parity)
            if k >= 1:
                shares[k - 1].wait_send()
            shares.append(share)
            mix.prime()
        lead = n - 1 if k == 0 else chunks - 1
        ready = n - 1 - lead
        stage.open()

        def early(i, carry):
            gather.free(i)
            if sums is not None:
                sums.tick(i + lead)
            gather.rest(i)
            stage.before(i)
            if mix is not None and not mix.flip:
                pl.when(within(i - ready, chunks))(lambda: mix.chunk(i - ready))
            return carry

        lax.fori_loop(0, n - 1, early, 0)
        if k > 0:
            stages[k - 1].close()
        if k + 1 < len(stages):
            stages[k + 1].prefetch()
        stage.late()

        def later(q, carry):
            i = q + n - 1
            gather.free(i)
            if now is not None:
                now.free(i - n)
            if sums is not None:
                sums.tick(i + lead)
            if now is not None:
                now.rest(i - n)
            gather.rest(i)
            stage.chunk(q)
            if mix is not None:
                if mix.flip:
                    pl.when(q == 0)(sums.finish)
                    mix.chunk(q)
                else:
                    pl.when(within(i - ready, chunks))(lambda: mix.chunk(i - ready))
            return carry

        lax.fori_loop(0, chunks, later, 0)
        if mix is not None:
            if not mix.flip:
                sums.finish()
            mix.finish()
            share.start()
        stage.end()
        sums = now
    stages[-1].close()
    for share in shares[-2:]:
        share.wait_send()
    for share in shares:
        share.wait_recv()


def swap_halves(value):
    return pltpu.roll(value, value.shape[-1] // 2, value.ndim - 1)


def left_lanes(shape):
    return lax.broadcasted_iota(jnp.int32, shape, len(shape) - 1) < shape[-1] // 2


def pieces(array):
    return [array[at:at + G] for at in range(0, array.shape[0], G)]


def spread_row(ref, row):
    return ref[pl.ds(row, G, stride=0), :]


class Mix:
    def __init__(self, section, z, layer, flip, sums, gather, r, lent=None):
        self.lent = lent
        self.section, self.z, self.layer, self.flip, self.r = section, z, layer, flip, r
        self.sums, self.gather = sums, gather
        self.chunks, self.grids, self.half, self.count, self.lanes = sums.part.shape[1:]
        self.channels, self.slots = r.weights.shape[2], r.wbuf.shape[0]
        self.blocks = self.chunks * self.half // 2

    def begin(self, block):
        per = self.half // 2
        q, x = block // per, 2 * (block % per)
        slot = lax.rem(block, self.slots)
        rows = pl.ds(q * self.count, self.count)
        if self.lent is not None:
            for at in range(2):
                self.lent(q, x + at).wait_recv()

        @pl.when(self.section == self.layer)
        def _():
            pltpu.make_async_copy(self.r.weights.at[0, pl.ds(self.section * self.half + x, 2), rows],
                                  self.r.wbuf.at[slot], self.r.wsem.at[slot]).start()

        @pl.when(self.section != self.layer)
        def _():
            pltpu.make_async_copy(self.r.far.at[pl.ds(x, 2), rows], self.r.wbuf.at[slot], self.r.wsem.at[slot]).start()

    def prime(self):
        for block in range(min(self.slots, self.blocks)):
            self.begin(jnp.int32(block))
        if not self.flip:
            self.r.macc[...] = jnp.zeros_like(self.r.macc)

    def chunk(self, q):
        def body(x, carry):
            block = q * (self.half // 2) + x // 2
            slot = lax.rem(block, self.slots)

            @pl.when(lax.rem(x, 2) == 0)
            def _():
                arrived(self.r.wbuf.at[slot], self.r.wsem.at[slot])

            (self.transposed if self.flip else self.forward)(q, x, self.r.wbuf.at[slot, lax.rem(x, 2)])

            @pl.when(jnp.logical_and(lax.rem(x, 2) == 1, block + self.slots < self.blocks))
            def _():
                self.begin(block + self.slots)

            return carry

        if self.flip:
            pl.when(q == 0)(self.sources)
        lax.fori_loop(0, self.half, body, 0)
        if self.flip:
            self.gather.give(q)

    def sources(self):
        def body(x, carry):
            for g in range(self.grids):
                value = jnp.concatenate([self.sums.part[self.z, at, g, x] for at in range(self.chunks)], 0)
                self.r.macc[x, 2 * g] = value
                self.r.macc[x, 2 * g + 1] = swap_halves(value)
            return carry

        lax.fori_loop(0, self.half, body, 0)

    def forward(self, q, x, weight):
        sides, groups = 2 * self.grids, self.channels // G
        total, source = self.r.macc.at[x], self.r.msrc
        for g in range(self.grids):
            value = self.sums.part[self.z, q, g, x]
            source[2 * g, :self.count] = value
            source[2 * g + 1, :self.count] = swap_halves(value)
        keys = [(k, o) for k in range(sides) for o in range(groups)]

        def body(octet, acc):
            acc = dict(zip(keys, acc))
            for u in range(G):
                i = octet * G + u
                rows = [spread_row(source.at[k], i) for k in range(sides)]
                for o in range(groups):
                    w = weight[i, o * G:(o + 1) * G, :]
                    for k in range(sides):
                        acc[k, o] = acc[k, o] + rows[k] * w
            return tuple(acc[key] for key in keys)

        acc = lax.fori_loop(0, self.count // G, body, tuple(total[k, o * G:(o + 1) * G, :] for k, o in keys))
        for key, value in zip(keys, acc):
            total[key[0], key[1] * G:(key[1] + 1) * G, :] = value

    def transposed(self, q, x, weight):
        sides, groups = 2 * self.grids, self.channels // G
        rows = [pieces(self.r.macc[x, k]) for k in range(sides)]
        out = [[] for _ in range(sides)]
        for i in range(self.count):
            total = [None] * sides
            for o in range(groups):
                w = weight[i, o * G:(o + 1) * G, :]
                for k in range(sides):
                    term = w * rows[k][o]
                    total[k] = term if total[k] is None else total[k] + term
            for k in range(sides):
                out[k].append(jnp.sum(total[k], axis=0, keepdims=True))
        left = left_lanes((self.count, self.lanes))
        for g in range(self.grids):
            a, b = [jnp.concatenate(out[2 * g + side], 0) for side in range(2)]
            self.put(g, q, x, jnp.where(left, a + swap_halves(a), swap_halves(b) - b))

    def put(self, g, q, x, value):
        if g == 0:
            self.gather.full[q, self.z, self.section, x] = value
        else:
            self.gather.give_from[q, x] = value

    def finish(self):
        if self.flip:
            return
        left = left_lanes((self.channels, self.lanes))

        def body(x, carry):
            for g in range(self.grids):
                a, b = [self.r.macc[x, 2 * g + side] for side in range(2)]
                result = jnp.where(left, a - swap_halves(a), b + swap_halves(b))
                for q in range(self.chunks):
                    self.put(g, q, x, result[q * self.count:(q + 1) * self.count])
            return carry

        lax.fori_loop(0, self.half, body, 0)
        for q in range(self.chunks):
            self.gather.give(q)


def gather_columns(f_ref, d_ref, left_of, right_of):
    channels = f_ref.shape[2] * f_ref.shape[5]
    lanes = f_ref.shape[6]
    left = left_lanes((channels, lanes))
    for stream in range(f_ref.shape[0]):
        for member in range(f_ref.shape[1]):
            for g in range(f_ref.shape[3]):
                at = (stream * f_ref.shape[1] + member) * f_ref.shape[3] + g
                both = []
                for x in range(2):
                    f = f_ref[stream, member, :, g, x].reshape(channels, lanes)
                    turned = swap_halves(f)
                    left_of[x, at] = jnp.concatenate([f, jnp.where(left, -turned, turned)], 0).T
                    both.append(d_ref[stream, member, :, g, x].reshape(channels, lanes))
                right_of[at] = jnp.concatenate(both, 0).T


def column_products(left_of, right_of, product):
    grids, double, lanes = right_of.shape
    half = double // 2
    left = left_lanes((2 * grids, lanes))
    rows = right_of.reshape(grids * double, lanes)
    sides = [left_of.at[x].reshape(grids * double, lanes) for x in range(2)]

    def body(k, carry):
        pick = pl.ds(k, 2 * grids, stride=half)
        d = rows[pick, :]
        f_high, f_low = split(jnp.concatenate([side[pick, :] for side in sides], 0))
        d_high, d_low = split(jnp.concatenate([jnp.where(left, d, 0.0), jnp.where(left, 0.0, d)], 0))
        product[k] = dot(jnp.concatenate([f_high, f_low, f_high], 0), jnp.concatenate([d_high, d_high, d_low], 0),
                         (((0,), (0,)), ((), ())))
        return carry

    lax.fori_loop(0, half, body, 0, unroll=4)


def product_rows(product, first, out):
    half, double, lanes = product.shape
    channels = double // 2
    rows = product.reshape(half * double, lanes)

    def body(i, carry):
        parts = [rows[pl.ds(part * channels + first + i, half, stride=double), :] for part in range(2)]
        tile = jnp.concatenate(parts, 0).T
        for x in range(2):
            out[x, i] = tile[x * channels:(x + 1) * channels]
        return carry

    lax.fori_loop(0, out.shape[1], body, 0, unroll=4)


class GradInput:
    def __init__(self, first, f, g, fbuf, gbuf, sem):
        self.first, self.f, self.g, self.fbuf, self.gbuf, self.sem = first, f, g, fbuf, gbuf, sem

    def load(self, x, slot):
        for layer, condition in enumerate((self.first, jnp.logical_not(self.first))):
            @pl.when(condition)
            def _():
                for j in range(len(self.f[layer])):
                    pltpu.make_async_copy(self.f[layer][j].at[:, :, :, pl.ds(2 * x, 2)], self.fbuf.at[slot, j],
                                          self.sem.at[0, slot]).start()
                    pltpu.make_async_copy(self.g[layer][j].at[:, :, :, pl.ds(2 * x, 2)], self.gbuf.at[slot, j],
                                          self.sem.at[1, slot]).start()

    def next(self, x, count):
        slot = lax.rem(x, 2)

        @pl.when(x + 1 < count)
        def _():
            self.load(x + 1, 1 - slot)

        arrived(self.fbuf.at[slot], self.sem.at[0, slot])
        arrived(self.gbuf.at[slot], self.sem.at[1, slot])
        return self.fbuf.at[slot], self.gbuf.at[slot]


def grad_input(r, first, per_core):
    f = [[getattr(r, f"f{layer}{j}") for j in range(per_core)] for layer in range(2)]
    g = [[getattr(r, f"g{layer}{j}") for j in range(per_core)] for layer in range(2)]
    return GradInput(first, f, g, r.fbuf, r.gbuf, r.in_sem)


def far_grad_kernel(per_core, r):
    section, z, n = place_and_peers()
    pairs, block = r.far.shape[0] // 2, r.out.shape[2]
    blocks = r.far.shape[1] // block
    source = grad_input(r, section != 0, per_core)

    def move(k, slot):
        p, i = k // blocks, k % blocks
        return to_core(r.out.at[slot], r.far.at[pl.ds(2 * p, 2), pl.ds(i * block, block)], (r.send.at[k], r.recv.at[k]),
                       section)

    source.load(0, 0)
    greet(section, z, n, False)

    def body(p, carry):
        gather_columns(*source.next(p, pairs), r.left_of, r.right_of)
        column_products(r.left_of, r.right_of, r.product)

        def inner(i, carry):
            k = p * blocks + i

            @pl.when(k >= 2)
            def _():
                move(k - 2, lax.rem(k, 2)).wait_send()

            product_rows(r.product, i * block, r.out.at[lax.rem(k, 2)])
            move(k, lax.rem(k, 2)).start()
            return carry

        return lax.fori_loop(0, blocks, inner, carry)

    lax.fori_loop(0, pairs, body, 0)
    total = pairs * blocks
    for k in (total - 2, total - 1):
        move(k, k % 2).wait_send()

    def close(k, carry):
        move(k, 0).wait_recv()
        return carry

    lax.fori_loop(0, total, close, 0)


def own_grad_kernel(names, per_core, m_ref, *refs):
    r = types.SimpleNamespace(**dict(zip(names, refs)))
    p, i = pl.program_id(0), pl.program_id(1)
    source = grad_input(r, m_ref[0] == 0, per_core)

    @pl.when(i == 0)
    def _():
        @pl.when(p == 0)
        def _():
            source.load(0, 0)

        gather_columns(*source.next(p, pl.num_programs(0)), r.left_of, r.right_of)
        column_products(r.left_of, r.right_of, r.product)

    r.bound_out[...] = r.bound_in[...]
    r.out[1 - m_ref[0]] = r.far[...]
    product_rows(r.product, i * r.out.shape[2], r.out.at[m_ref[0]])


def whole(array):
    return pl.BlockSpec(array.shape, lambda *_: (0,) * array.ndim)


def params(**kw):
    return pltpu.CompilerParams(vmem_limit_bytes=VMEM_LIMIT, **kw)


def local(inputs, cotangent, region_id, spectral_w, conv_w, bias_vector):
    micro_count, _, rows_dev, channels, width = inputs.shape
    lanes = spectral_w.shape[-1]
    half = lanes // 2
    kx_dev = spectral_w.shape[1]
    row_devices, sections = lax.axis_size("rows"), lax.axis_size("section")
    mode_rows, height = kx_dev * row_devices, rows_dev * row_devices
    section = lax.axis_index("section")
    per_core = micro_count // sections
    kx_half = kx_dev // sections

    plain, doubled = col_tables(width, half)

    def stacked(array):
        high, low = np_split(array)
        return np.concatenate([high, high, low], 0)

    t_plain, t_doubled, it_plain, it_doubled = [stacked(t) for t in (plain, doubled, plain.T, doubled.T)]
    kron, ikron = row_tables(height, mode_rows, lax.axis_index("rows") * rows_dev, rows_dev)

    count = 2 * G
    chunks = channels // count
    hbm, vmem = pl.BlockSpec(memory_space=pl.ANY), pl.BlockSpec(memory_space=pltpu.VMEM)
    field_shape = jax.ShapeDtypeStruct((rows_dev, channels, width), F32)
    part_dims = (row_devices, chunks, sections, kx_half, count, lanes)
    p_shape, f_shape = jax.ShapeDtypeStruct(part_dims, F32), jax.ShapeDtypeStruct(part_dims[1:], F32)
    y_shape = jax.ShapeDtypeStruct((sections, chunks, kx_half, count, lanes), F32)
    stat_shape = jax.ShapeDtypeStruct((3, R, 128), F32)
    cg_shape = jax.ShapeDtypeStruct((2 * channels, 2 * channels), F32)
    bg_shape = jax.ShapeDtypeStruct((channels, width), F32)
    bound_shape = jax.ShapeDtypeStruct((micro_count, rows_dev, channels, width), F32)
    dma = pltpu.SemaphoreType.DMA
    field_buf = pltpu.VMEM((rows_dev, channels, width), F32)
    full_dims = (chunks, row_devices, sections, kx_half, count, lanes)
    spread = pltpu.VMEM((width // 128, rows_dev * count, 128), F32)
    energy = pltpu.VMEM((rows_dev, G, width), F32)
    line_sems = dma((2, chunks, row_devices))
    def run(body, ident, ins, outs, scratch, cost=50, aliases=None):
        names = [*ins, *outs, *scratch]
        spec = lambda entry: vmem if isinstance(entry, tuple) else hbm
        plain = lambda entry: entry[0] if isinstance(entry, tuple) else entry
        kernel = lambda *refs: body(types.SimpleNamespace(**dict(zip(names, refs))))
        positions = {list(ins).index(k): list(outs).index(v) for k, v in (aliases or {}).items()}
        result = pl.pallas_call(
            kernel, in_specs=[spec(e) for e in ins.values()], out_specs=[spec(e) for e in outs.values()],
            out_shape=[plain(e) for e in outs.values()], scratch_shapes=list(scratch.values()),
            input_output_aliases=positions,
            cost_estimate=pl.CostEstimate(flops=0, bytes_accessed=cost * 3_000_000, transcendentals=0),
            compiler_params=params(collective_id=ident, has_side_effects=True))(*[plain(e) for e in ins.values()])
        return types.SimpleNamespace(**dict(zip(outs, result)))

    conv_rows_at_once = 256 // channels
    maps = jnp.stack([conv_w[0].T, conv_w[0]])
    at = np.arange(conv_rows_at_once * channels) // channels
    wide_own = jnp.where(at[:, None] == at[None, :], jnp.tile(maps, (1, conv_rows_at_once, conv_rows_at_once)), 0.0)
    wide_own = jnp.stack(jnp.split(wide_own, wide_own.shape[2] // 128, 2), 1)
    bias_own = jnp.broadcast_to(bias_vector[0][:, None], (channels, width))

    streams = range(per_core)
    members = lax.axis_size("batch")
    kinds = ["middle", "turn", "back", "tail"]
    mixes = [(0, False), (1, False), (1, True), (0, True)]
    names = ["f00", "f01", "f10", "f11", "g10", "g11", "g00", "g01"]
    places = [dict(a=0, z=1), dict(a=2, z=3), dict(a=4, z=5, cot=6), dict(a=0, z=1, cot=2),
              dict(gz=3, a=4, h=5, dg=6), dict(gz=0, a=1, h=2, dg=3), dict(gz=4, a=5, h=6), dict(gz=0, a=1, h=2)]
    both = (2,)
    ins = dict(inputs=inputs, cotangent=cotangent, region=region_id, weights=spectral_w, t_plain=(t_plain,),
               t_doubled=(t_doubled,), it_plain=(it_plain,), it_doubled=(it_doubled,), kron=(kron,), ikron=(ikron,),
               wide_own=(wide_own,), bias_own=(bias_own,))
    outs = dict(far=jax.ShapeDtypeStruct((kx_half,) + spectral_w.shape[2:], F32), bound=bound_shape, stat=(jax.ShapeDtypeStruct((2 * per_core,) + stat_shape.shape, F32),),
                cg=(jax.ShapeDtypeStruct((2 * per_core,) + cg_shape.shape, F32),),
                bg=(jax.ShapeDtypeStruct((2 * per_core,) + bg_shape.shape, F32),),
                **{f"{name}{j}": field_shape for name in ("a1_", "dg0_", "gz1_", "ga1_", "gz0_") for j in streams},
                **{f"shared{i}": jax.ShapeDtypeStruct((members,) + f_shape.shape, F32) for i in range(len(names))})
    scratch = dict(
        fields=pltpu.VMEM((7,) + field_shape.shape, F32), full=pltpu.VMEM(both + full_dims, F32),
        part=pltpu.VMEM(both + part_dims, F32),
        come=pltpu.VMEM(both + (2, chunks, row_devices - 1) + part_dims[2:], F32),
        keep=pltpu.VMEM(both + f_shape.shape, F32), y_give=pltpu.VMEM(both + y_shape.shape[1:], F32),
        p_buf=pltpu.VMEM(full_dims, F32), spread=spread, eo=energy, eb=energy,
        rid=pltpu.VMEM((2, rows_dev, width), jnp.int32),
        wbuf=pltpu.VMEM((3, 2, count, channels, lanes), F32), macc=pltpu.VMEM((kx_half, 2 * sections, channels, lanes), F32),
        msrc=pltpu.VMEM((2 * sections, channels, lanes), F32),
        bias=pltpu.VMEM((2, channels, width), F32),
        conv=pltpu.VMEM((4, len(at), 3 * len(at)), BF16), m_cross=dma((2, 2)),
        field_sem=dma((7,)), rid_sem=dma(both), out_sem=dma((2, 2, chunks)), wsem=dma((3,)), w_load=dma((chunks, kx_half)), w_cross=dma((2, chunks, kx_half)),
        send=dma(both + (2, chunks, row_devices)), recv=dma(both + (2, chunks, row_devices)),
        red_send=dma(both + (2, chunks, row_devices)), red_recv=dma(both + (2, chunks, row_devices)),
        y_cross=dma((2, 2, chunks)), p_cross=dma((2, 2, chunks)),
        b_local=dma((2, chunks)), b_cross=dma((2, 2, chunks)),
        s_local=dma(both), s_send=dma((2, members)), s_recv=dma((len(names), members)))
    done = run(functools.partial(stages_kernel, per_core, kinds, places, mixes), 0, ins, outs, scratch, cost=400)
    gathered = {name: getattr(done, f"shared{i}") for i, name in enumerate(names)}
    bound, calls = done.bound, 0

    grids = per_core * members * sections
    block = 2 * G
    pairs, blocks = kx_half // 2, channels // block
    in_buf = pltpu.VMEM((2, per_core, members, chunks, sections, 2, count, lanes), F32)
    grad_scratch = dict(fbuf=in_buf, gbuf=in_buf, in_sem=dma((2, 2)), left_of=pltpu.VMEM((2, grids, lanes, lanes), F32),
                        right_of=pltpu.VMEM((grids, lanes, lanes), F32), product=pltpu.VMEM((half, lanes, lanes), F32))
    far_grad = run(functools.partial(far_grad_kernel, per_core), 1 + calls, gathered,
                   dict(far=jax.ShapeDtypeStruct((kx_half, channels, channels, lanes), F32)),
                   dict(out=pltpu.VMEM((2, 2, block, channels, lanes), F32), send=dma((pairs * blocks,)),
                        recv=dma((pairs * blocks,)), **grad_scratch)).far
    bound_rows = bound.reshape(micro_count * rows_dev, channels, width)
    bound_block = pl.BlockSpec((bound_rows.shape[0] // (pairs * blocks), channels, width),
                               lambda p, i, m: (p * blocks + i, 0, 0))
    grid_spec = pltpu.PrefetchScalarGridSpec(
        num_scalar_prefetch=1, grid=(pairs, blocks),
        in_specs=[hbm] * len(gathered)
        + [pl.BlockSpec((2, block, channels, lanes), lambda p, i, m: (p, i, 0, 0)), bound_block],
        out_specs=[pl.BlockSpec((2, 2, block, channels, lanes), lambda p, i, m: (0, p, i, 0, 0)), bound_block],
        scratch_shapes=list(grad_scratch.values()))
    spectral_grad, boundary = pl.pallas_call(
        functools.partial(own_grad_kernel, [*gathered, "far", "bound_in", "out", "bound_out", *grad_scratch], per_core),
        grid_spec=grid_spec, out_shape=[jax.ShapeDtypeStruct((2, kx_half, channels, channels, lanes), F32),
                                        jax.ShapeDtypeStruct(bound_rows.shape, F32)],
        cost_estimate=pl.CostEstimate(flops=0, bytes_accessed=150_000_000, transcendentals=0),
        compiler_params=params())(
            jnp.reshape(section, (1,)).astype(jnp.int32), *gathered.values(), far_grad, bound_rows)
    spectral_grad = spectral_grad.reshape(spectral_w.shape)
    boundary = boundary.reshape((1, micro_count, 1) + inputs.shape[2:])

    def lower(value):
        return (value[:channels, :channels] + value[channels:, channels:]
                + value[:channels, channels:] + value[channels:, :channels])

    pair = lambda value: jnp.sum(value.reshape((2, per_core) + value.shape[1:]), 1)
    conv_local = jnp.stack([lower(value) for value in pair(done.cg)[::-1]])
    bias_local = jnp.sum(pair(done.bg)[::-1], -1)
    stat_local = jnp.sum(pair(done.stat), -1)
    shapes = [v.shape for v in (conv_local, bias_local, stat_local)]
    flat_sums = jnp.concatenate([v.reshape(-1) for v in (conv_local, bias_local, stat_local)])
    length = flat_sums.shape[0]
    flat_sums = jnp.pad(flat_sums, (0, -length % 1024)).reshape(-1, 128)
    flat_sums = jnp.sum(lax.all_gather(flat_sums, ("section", "batch", "rows"), axis=0), 0).reshape(-1)
    ends = np.cumsum([0] + [math.prod(shape) for shape in shapes])
    conv_sum, bias_sum, stat_sum = [flat_sums[ends[i]:ends[i + 1]].reshape(shapes[i]) for i in range(3)]
    own_stat = lax.dynamic_index_in_dim(stat_sum, section, 0, False)
    layer_rms = jnp.sqrt(own_stat[:2] / (channels * own_stat[2])[None, :] + 1e-06)[None]
    own = lambda value: lax.dynamic_slice_in_dim(value, section, 1, 0)
    return boundary, spectral_grad, own(conv_sum), own(bias_sum), layer_rms


def solution(mesh):
    placed = (
        P(None, "batch", "rows", None, None),
        P(None, "batch", "rows", None, None),
        P(None, "batch", "rows", None),
        P("section", "rows", None, None, None),
        P("section", None, None),
        P("section", None),
    )
    return jax.shard_map(
        local,
        mesh=mesh,
        in_specs=placed,
        out_specs=(
            P("section", None, "batch", "rows", None, None),
            P("section", "rows", None, None, None),
            P("section", None, None),
            P("section", None),
            P("section", None, None),
        ),
        check_vma=False,
    )
```
